32 devices in a mesh: shot: 2 (over y), gx: 4 (over z), gy: 2 (over x), gz: 2 (over core).
Axes of the slice: x: 2, y: 2, z: 4, core: 2. Of those that a mesh axis runs over, the one named last changes fastest.
Arguments:
- stored: float32 [8, 16, 64, 256], P('shot', 'gx', 'gy', 'gz'), parts along dimension 0, may hold values from -6 to 6
- adjoint_end: float32 [8, 16, 64, 256], P('shot', 'gx', 'gy', 'gz'), parts along dimension 0, may hold values from -6 to 6
- labels: int32 [16, 64, 256], P('gx', 'gy', 'gz'), may hold values from 0 to 7
- tissue: float32 [3, 8], replicated, may hold values from 0 to 2, as said below
- source_cells: int32 [128, 3], P('shot'), parts along dimension 0, may hold values from 0 to 255, as said below
- source_wave: float32 [4, 128], P(None, 'shot'), parts along dimension 1, may hold values from -6 to 6
- receiver_cells: int32 [1024, 3], replicated, may hold values from 0 to 255, as said below
- receiver_wave: float32 [4, 2048], P(None, 'shot'), parts along dimension 1, may hold values from -6 to 6
Outputs:
- gradient: float32 [4, 16, 64, 256], P('shot', 'gx', 'gy', 'gz'), parts along dimension 0
- adjoint_start: float32 [8, 16, 64, 256], P('shot', 'gx', 'gy', 'gz'), parts along dimension 0
The draws below stay inside these ranges and needn't reach their ends.
There are 2 independent parts, one for each index of `shot`. The reference program is written for one: setup_inputs(seed, part) draws one part's arguments, and reference() takes and returns one part's arrays. A program takes and returns all parts, laid end to end along the dimension named above; an argument that names none is the same for every part. Nothing has to cross between parts.
Inputs may be any that keep to these rules, and one draw needn't show every extreme that they name: `tissue`: row 0 is the Courant number, row 1 the relative density, row 2 the absorption per step. `source_cells`: each row is a cell (x, y, z) of the grid; cells may repeat. `receiver_cells`: each row is a cell (x, y, z) of the grid; cells may repeat.
All inputs are finite; a program needn't handle non-finite values.
Results may differ from the reference program's by a relative error of at most 0.00002.
Values sent between devices are 32-bit elements; how exact they have to be, the bound alone decides.
No kernel may reach another device: no remote copies, remote signals or barrier semaphores. Data moves between devices by JAX's collectives and lax.ppermute only.
A program may use at most 64 MiB of HBM per device.

```python
import jax
import jax.numpy as jnp
from jax import lax

STEPS = 4
LABELS = 8
SOURCES = 64
RECEIVERS = 1024
NX = 16
NY = 64
NZ = 256


def cell_draw(key, number):
    subkeys = jax.random.split(key, 3)
    column_x = jax.random.randint(subkeys[0], (number,), 0, NX)
    column_y = jax.random.randint(subkeys[1], (number,), 0, NY)
    column_z = jax.random.randint(subkeys[2], (number,), 0, NZ)
    chosen = jnp.stack([column_x, column_y, column_z], 1).astype(jnp.int32)
    chosen = chosen.at[0].set(jnp.array([0, NY - 1, NZ - 1], jnp.int32))
    chosen = chosen.at[1].set(jnp.array([NX - 1, 0, 0], jnp.int32))
    return chosen


def draw_source_cells(key, part):
    key = jax.random.fold_in(key, 1)
    return cell_draw(key, SOURCES)


def draw_receiver_cells(key, part):
    key = jax.random.fold_in(key, 2)
    return cell_draw(key, RECEIVERS)


def draw_tissue(key, part):
    key = jax.random.fold_in(key, 3)
    subkeys = jax.random.split(key, 3)
    sound_speed = jax.random.uniform(subkeys[0], (LABELS,), jnp.float32, 0.15, 0.35)
    density = jax.random.uniform(subkeys[1], (LABELS,), jnp.float32, 1.0, 1.9)
    absorb = jax.random.uniform(subkeys[2], (LABELS,), jnp.float32, 0.0, 0.08)
    return jnp.stack([sound_speed, density, absorb], 0).astype(jnp.float32)


def plant(values, key, low, largest):
    longest = values.shape.index(max(values.shape))
    spots = []
    for shift in (0, 1):
        where = [jax.random.randint(jax.random.fold_in(key, axis), (), 0, length) for axis, length in enumerate(values.shape)]
        where[longest] = (where[longest] + shift) % values.shape[longest]
        spots.append(tuple(where))
    return values.at[spots[0]].set(low).at[spots[1]].set(largest)


def levels(stream_key, dims, cuts, smallest, top_value):
    def one(position, parts):
        draws = jax.random.uniform(jax.random.fold_in(jax.random.fold_in(stream_key, 6), position), (parts,), jnp.float32, smallest / len(cuts), top_value / len(cuts))
        return jnp.repeat(jnp.exp(draws), dims[position] // parts).reshape((-1,) + (1,) * (len(dims) - position - 1))

    gain = one(*cuts[0])
    for cut in cuts[1:]:
        gain = gain * one(*cut)
    return gain


def scatter_about(key, extent, scale, reach, pieces=(), held_as=jnp.bfloat16):
    values = jax.random.normal(key, extent, jnp.float32) * scale
    if len(pieces) > 0:
        values = levels(key, extent, pieces, -0.22, 0.18) * values
    return jnp.clip(values, min=-reach, max=reach).astype(held_as)


def setup_inputs(seed: int = 0, part: int = 0) -> dict:
    seeds = jax.random.split(jax.random.key(seed), 9)
    part_keys = jax.random.split(jax.random.fold_in(seeds[8], part), 9)
    return {
        "stored": scatter_about(part_keys[0], (4, NX, NY, NZ), 1.0, 6.0, ((1, 4), (2, 2), (3, 2)), jnp.float32),
        "adjoint_end": scatter_about(part_keys[1], (4, NX, NY, NZ), 1.0, 6.0, ((1, 4), (2, 2), (3, 2)), jnp.float32),
        "labels": plant(jax.random.randint(seeds[2], (NX, NY, NZ), 0, LABELS), jax.random.fold_in(seeds[2], 1), 0, LABELS - 1).astype(jnp.int32),
        "tissue": draw_tissue(jax.random.fold_in(seeds[8], 71), part),
        "source_cells": draw_source_cells(jax.random.fold_in(jax.random.fold_in(seeds[8], part), 71), part),
        "source_wave": scatter_about(part_keys[5], (STEPS, SOURCES), 1.0, 6.0, (), jnp.float32),
        "receiver_cells": draw_receiver_cells(jax.random.fold_in(seeds[8], 71), part),
        "receiver_wave": scatter_about(part_keys[7], (STEPS, RECEIVERS), 1.0, 6.0, (), jnp.float32),
    }


def shifted(values, along, offset):
    length = values.shape[along]
    pad_width = [(0, 0)] * values.ndim
    if offset > 0:
        pad_width[along] = (0, offset)
        padded = jnp.pad(values, pad_width)
        return lax.slice_in_dim(padded, offset, offset + length, axis=along)
    pad_width[along] = (-offset, 0)
    padded = jnp.pad(values, pad_width)
    return lax.slice_in_dim(padded, 0, length, axis=along)


def grad_up(values):
    return jnp.stack([shifted(values, along, 1) - values for along in range(3)], 0)


def div_down(velocity):
    result = velocity[0] - shifted(velocity[0], 0, -1)
    result = result + (velocity[1] - shifted(velocity[1], 1, -1))
    return result + (velocity[2] - shifted(velocity[2], 2, -1))


def coefficients(labels, tissue):
    sound_speed = jnp.zeros(labels.shape, jnp.float32)
    density = jnp.zeros(labels.shape, jnp.float32)
    absorb = jnp.zeros(labels.shape, jnp.float32)
    for label_id in range(tissue.shape[1]):
        picked = (labels == label_id).astype(jnp.float32)
        sound_speed = sound_speed + picked * tissue[0, label_id]
        density = density + picked * tissue[1, label_id]
        absorb = absorb + picked * tissue[2, label_id]
    return jnp.stack([density * sound_speed, sound_speed / density, 1.0 - absorb], 0)


def inject(grid_shape, cell_list, amounts, anchor):
    relative = cell_list - anchor[None, :]
    inside = jnp.ones(relative.shape[0], bool)
    for along in range(3):
        inside = inside & (relative[:, along] >= 0) & (relative[:, along] < grid_shape[along])
    total_cells = grid_shape[0] * grid_shape[1] * grid_shape[2]
    flat_index = (relative[:, 0] * grid_shape[1] + relative[:, 1]) * grid_shape[2] + relative[:, 2]
    flat_index = jnp.where(inside, flat_index, total_cells).astype(jnp.int32)
    result = jnp.zeros((total_cells,), jnp.float32).at[flat_index].add(amounts, mode="drop")
    return result.reshape(grid_shape)


def forward_step(pressure, velocity, tissue_grid, source_add):
    slopes_now = grad_up(pressure)
    velocity = velocity - tissue_grid[1] * slopes_now
    spread = div_down(velocity)
    pressure = tissue_grid[2] * (pressure - tissue_grid[0] * spread) + source_add
    return pressure, velocity, slopes_now, spread


def adjoint_step(pressure_adj, velocity_adj, tissue_grid, receiver_add):
    pressure_adj = pressure_adj + receiver_add
    scaled = (tissue_grid[0] * tissue_grid[2]) * pressure_adj
    velocity_adj = velocity_adj + grad_up(scaled)
    return pressure_adj, velocity_adj


def reference(stored, adjoint_end, labels, tissue, source_cells, source_wave, receiver_cells, receiver_wave):
    tissue_grid = coefficients(labels, tissue)
    wave_state = jnp.roll(stored, NX // 2, axis=1)
    pressure, velocity = wave_state[0], wave_state[1:]
    anchor = jnp.zeros((3,), jnp.int32)
    grid_shape = pressure.shape
    slope_list = []
    spread_list = []
    for counter in range(STEPS):
        source_add = inject(grid_shape, source_cells, source_wave[counter], anchor)
        pressure, velocity, slopes_now, spread = forward_step(pressure, velocity, tissue_grid, source_add)
        slope_list.append(slopes_now)
        spread_list.append(spread)
    pressure_adj, velocity_adj = adjoint_end[0], adjoint_end[1:]
    grad_stiff = jnp.zeros(grid_shape, jnp.float32)
    grad_buoy = jnp.zeros(grid_shape, jnp.float32)
    for counter in range(STEPS - 1, -1, -1):
        receiver_add = inject(grid_shape, receiver_cells, receiver_wave[counter], anchor)
        pressure_adj, velocity_adj = adjoint_step(pressure_adj, velocity_adj, tissue_grid, receiver_add)
        grad_stiff = grad_stiff - tissue_grid[2] * pressure_adj * spread_list[counter]
        slopes_now = slope_list[counter]
        grad_buoy = grad_buoy - ((velocity_adj[0] * slopes_now[0] + velocity_adj[1] * slopes_now[1]) + velocity_adj[2] * slopes_now[2])
        pressure_adj = tissue_grid[2] * pressure_adj + div_down(tissue_grid[1] * velocity_adj)
    gradient = jnp.stack([grad_stiff, grad_buoy], 0)
    adjoint_start = jnp.concatenate([pressure_adj[None], velocity_adj], 0)
    return gradient, adjoint_start
```

```python
import jax
import jax.numpy as jnp
from jax import lax
from jax.experimental import pallas as pl
from jax.experimental.pallas import tpu as pltpu
from jax.sharding import PartitionSpec as P

STEPS = 4
MARGIN = 4
BX, BY, BZ = 4, 32, 128
EX, EY = BX + 2 * MARGIN, BY + 2 * MARGIN
STRIP = 2 * MARGIN
F32 = jnp.float32
BF16 = jnp.bfloat16
VMEM_LIMIT = 48 * 1024 * 1024


def lanes(shape):
    return lax.broadcasted_iota(jnp.int32, shape, len(shape) - 1)


def rows(shape):
    return lax.broadcasted_iota(jnp.int32, shape, len(shape) - 2)


def pack_kernel(stored_ref, adj_ref, lab_ref, al_ref, ep_ref, strip_ref):
    gz = lax.axis_index("gz")
    lane = lanes((BY, BZ))
    row = rows((8, BZ))

    def plane(field, x):
        if field < 4:
            return stored_ref[field, x]
        if field < 8:
            return adj_ref[field - 4, x]
        return lab_ref[x].astype(F32) + 1.0

    for group in range(3):
        strip = jnp.zeros((BY, BZ), F32)
        for slot in range(4 if group < 2 else 1):
            field = group * 4 + slot
            for x in range(BX):
                block = plane(field, x)
                if field >= 4:
                    al_ref[field - 4, x] = block
                ep_ref[field * BX + x] = jnp.where(row < MARGIN, block[0:8], block[BY - 8 : BY])
                base = slot * BX * STRIP + x * STRIP
                rolled = pltpu.roll(block, (base + MARGIN) % BZ, 1)
                first = base + MARGIN * gz
                strip = jnp.where((lane >= first) & (lane < first + MARGIN), rolled, strip)
        strip_ref[group] = strip
        ep_ref[9 * BX + group] = jnp.where(row < MARGIN, strip[0:8], strip[BY - 8 : BY])


def merge_kernel(up_ref, down_ref, strip_ref, other_ref, dup_ref, ddown_ref, xw_ref, xa_ref):
    row = rows((8, BZ))

    def halo(index):
        return jnp.where(row < MARGIN, up_ref[index], down_ref[index])

    for index in range(4 * BX):
        xw_ref[index] = halo(index)
    for index in range(5 * BX):
        xa_ref[index] = halo(4 * BX + index)
    for group in range(3):
        target, first = ((xw_ref, 4 * BX), (xa_ref, 5 * BX), (xa_ref, 5 * BX + 5))[group]
        for tile in range(4):
            sl = slice(tile * 8, tile * 8 + 8)
            target[first + tile] = strip_ref[group, sl] + other_ref[group, sl]
        diagonal = jnp.where(row < MARGIN, dup_ref[group], ddown_ref[group])
        target[first + 4] = halo(9 * BX + group) + diagonal


def split(values):
    high = values.astype(BF16)
    rest = values - high.astype(F32)
    middle = rest.astype(BF16)
    low = (rest - middle.astype(F32)).astype(BF16)
    return high, middle, low


def inject_points(table_ref, count, width, out_ref, strip_out_ref, waves):
    gx, gy, gz = (lax.axis_index(name) for name in ("gx", "gy", "gz"))
    cut = BZ * lax.axis_size("gz") // 2 - MARGIN
    for start in range(0, count, width):
        sl = slice(start, start + width)
        cell_x = table_ref[0:1, sl].astype(jnp.int32) - (gx * BX - MARGIN)
        cell_y = table_ref[1:2, sl].astype(jnp.int32) - gy * BY
        cell_z = table_ref[2:3, sl].astype(jnp.int32)
        in_x = (cell_x >= 0) & (cell_x < EX)
        in_y = (cell_y >= -MARGIN) & (cell_y < BY + MARGIN)
        row = jnp.where(cell_y < 0, cell_y + EY, cell_y)
        flat = jnp.where(in_x & in_y, cell_x * EY + row, -1)
        row = jnp.where(in_y, row, -1)
        zz = cell_z - cut
        in_strip = in_x & (zz >= 0) & (zz < STRIP)
        strip_lane = jnp.where(in_strip, cell_x * STRIP + zz, -1)
        here = (rows((EX * EY, width)) == flat).astype(F32).astype(BF16)
        at_z = rows((BZ, width)) == (cell_z - gz * BZ)
        at_strip = (rows((BZ, width)) == strip_lane).astype(F32).astype(BF16)
        at_row = rows((EY, width)) == row
        for wave in range(waves):
            total = None
            strip_total = None
            for part in split(table_ref[4 + wave : 5 + wave, sl]):
                part = part.astype(F32)
                term = lax.dot_general(
                    here,
                    jnp.where(at_z, part, 0.0).astype(BF16),
                    (((1,), (1,)), ((), ())),
                    preferred_element_type=F32,
                )
                total = term if total is None else total + term
                term = lax.dot_general(
                    jnp.where(at_row, part, 0.0).astype(BF16),
                    at_strip,
                    (((1,), (1,)), ((), ())),
                    preferred_element_type=F32,
                )
                strip_total = term if strip_total is None else strip_total + term
            if start > 0:
                total = total + out_ref[wave]
                strip_total = strip_total + strip_out_ref[wave]
            out_ref[wave] = total
            strip_out_ref[wave] = strip_total


def inject_kernel(receivers_ref, sources_ref, r_ref, rs_ref, s_ref, ss_ref):
    inject_points(receivers_ref, receivers_ref.shape[1], 256, r_ref, rs_ref, STEPS)
    inject_points(sources_ref, sources_ref.shape[1], 128, s_ref, ss_ref, STEPS - 1)


def strip_of(packed, block, slot):
    lane = lanes(packed.shape)
    width = BX * STRIP
    shift = (block * width - slot * width) % BZ
    moved = pltpu.roll(packed, shift, 1) if shift else packed
    return jnp.where((lane >= block * width) & (lane < (block + 1) * width), moved, 0.0)


def y_up(v):
    return pltpu.roll(v, EY - 1, 0)


def y_down(v):
    return pltpu.roll(v, 1, 0)


def z_up(v, strip, x):
    edge = pltpu.roll(strip, (BZ - 1 - (x * STRIP + MARGIN)) % BZ, 1)
    return jnp.where(lanes(v.shape) == BZ - 1, edge, pltpu.roll(v, BZ - 1, 1))


def z_down(v, strip, x):
    edge = pltpu.roll(strip, (BZ - (x * STRIP + MARGIN - 1)) % BZ, 1)
    return jnp.where(lanes(v.shape) == 0, edge, pltpu.roll(v, 1, 1))


def coefficient_values(labels, tissue_ref):
    stiffness = jnp.zeros(labels.shape, F32)
    buoyancy = jnp.zeros(labels.shape, F32)
    damping = jnp.zeros(labels.shape, F32)
    for index in range(tissue_ref.shape[1]):
        picked = labels == float(index + 1)
        speed = tissue_ref[0, index]
        density = tissue_ref[1, index]
        ratio = (jnp.full((8, BZ), speed, F32) / jnp.full((8, BZ), density, F32))[0:1, :]
        stiffness = jnp.where(picked, density * speed, stiffness)
        buoyancy = jnp.where(picked, ratio, buoyancy)
        damping = jnp.where(picked, 1.0 - tissue_ref[2, index], damping)
    return stiffness, buoyancy, damping


def adjoint_kernel(
    al, al_low, al_high, xa, xa_low, xa_high, r_ref, rs_ref, tissue_ref,
    out_ref, hist_ref, coef_ref, coef_strip_ref,
    field, strip, sem,
):
    gz = lax.axis_index("gz")
    cut_up = jnp.where(gz == lax.axis_size("gz") // 2 - 1, 1.0, 0.0)
    cut_down = jnp.where(gz == lax.axis_size("gz") // 2, 1.0, 0.0)
    copies = []
    for block, (own, extra) in enumerate(((al_low, xa_low), (al, xa), (al_high, xa_high))):
        planes = pl.ds(block * BX, BX)
        copies.append(pltpu.make_async_copy(own, field.at[:, planes, pl.ds(0, BY), :], sem))
        for index in range(5):
            copies.append(
                pltpu.make_async_copy(
                    extra.at[pl.ds(index * BX, BX)],
                    field.at[index, planes, pl.ds(BY, 8), :],
                    sem,
                )
            )
        for group in range(2):
            copies.append(
                pltpu.make_async_copy(
                    extra.at[pl.ds(5 * BX + 5 * group, 5)], strip.at[block, group], sem
                )
            )
    for copy in copies:
        copy.start()
    for copy in copies:
        copy.wait()

    for x in range(EX):
        for index, values in enumerate(coefficient_values(field[4, x], tissue_ref)):
            coef_ref[index, x] = values
    packed = [[strip[b, g].reshape(EY, BZ) for g in range(2)] for b in range(3)]
    label_strip = sum(strip_of(packed[b][1], b, 0) for b in range(3))
    stiff_s, buoy_s, damp_s = coefficient_values(label_strip, tissue_ref)
    coef_strip_ref[0], coef_strip_ref[1], coef_strip_ref[2] = stiff_s, buoy_s, damp_s
    q_s, wx_s, wy_s, wz_s = (
        sum(strip_of(packed[b][0], b, slot) for b in range(3)) for slot in range(4)
    )

    for step in range(1, STEPS + 1):
        k = STEPS - step
        q_s = q_s + rs_ref[k]
        u_s = stiff_s * damp_s * q_s
        wx_s = wx_s + (pltpu.roll(u_s, BZ - STRIP, 1) - u_s)
        wy_s = wy_s + (y_up(u_s) - u_s)
        wz_s = wz_s + (pltpu.roll(u_s, BZ - 1, 1) - u_s)
        bx_s, by_s, bz_s = buoy_s * wx_s, buoy_s * wy_s, buoy_s * wz_s
        spread = (bx_s - pltpu.roll(bx_s, STRIP, 1)) + (by_s - y_down(by_s))
        spread = spread + (bz_s - pltpu.roll(bz_s, 1, 1))
        q_s = damp_s * q_s + spread
        edge_up = u_s * cut_up
        edge_down = bz_s * cut_down

        def injected(x):
            value = field[0, x] + r_ref[k, x]
            return value, coef_ref[0, x] * coef_ref[2, x] * value

        bx_below = None
        q_now, u_now = injected(step - 1)
        for x in range(step - 1, EX - step):
            q_next, u_next = injected(x + 1)
            wx = field[1, x] + (u_next - u_now)
            field[1, x] = wx
            bx = coef_ref[1, x] * wx
            if x >= step:
                wy = field[2, x] + (y_up(u_now) - u_now)
                wz = field[3, x] + (z_up(u_now, edge_up, x) - u_now)
                field[2, x] = wy
                field[3, x] = wz
                damped = coef_ref[2, x] * q_now
                if BX <= x < 2 * BX:
                    hist_ref[k, 0, x - BX] = damped[0:BY]
                    hist_ref[k, 1, x - BX] = wx[0:BY]
                    hist_ref[k, 2, x - BX] = wy[0:BY]
                    hist_ref[k, 3, x - BX] = wz[0:BY]
                by = coef_ref[1, x] * wy
                bz = coef_ref[1, x] * wz
                spread = (bx - bx_below) + (by - y_down(by))
                spread = spread + (bz - z_down(bz, edge_down, x))
                field[0, x] = damped + spread
            bx_below = bx
            q_now, u_now = q_next, u_next

    for index in range(4):
        for x in range(BX):
            out_ref[index, x] = field[index, BX + x, 0:BY]


def forward_kernel(
    ag, agx, coef_ref, coef_strip_ref, s_ref, ss_ref, hist_ref, grad_ref, field, strip, sem
):
    gx = lax.axis_index("gx")
    gz = lax.axis_index("gz")
    count = ag.shape[0]
    cut_up = jnp.where(gz == lax.axis_size("gz") // 2 - 1, 1.0, 0.0)
    cut_down = jnp.where(gz == lax.axis_size("gz") // 2, 1.0, 0.0)

    def copies(block):
        source = lax.rem(gx - 1 + block + count + count // 2, count)
        planes = pl.ds(block * BX, BX)
        result = [
            pltpu.make_async_copy(ag.at[source], field.at[:, planes, pl.ds(0, BY), :], sem)
        ]
        for index in range(4):
            result.append(
                pltpu.make_async_copy(
                    agx.at[source, pl.ds(index * BX, BX)],
                    field.at[index, planes, pl.ds(BY, 8), :],
                    sem,
                )
            )
        result.append(
            pltpu.make_async_copy(agx.at[source, pl.ds(4 * BX, 5)], strip.at[block], sem)
        )
        return result

    inside = (gx > 0, None, gx < count - 1)

    def start(block):
        for copy in copies(block):
            copy.start()

    def clear(block):
        planes = slice(block * BX, block * BX + BX)
        field[:, planes] = jnp.zeros((4, BX, EY, BZ), F32)
        strip[block] = jnp.zeros((5, 8, BZ), F32)

    def finish(block):
        for copy in copies(block):
            copy.wait()

    start(1)
    for block in (0, 2):
        pl.when(inside[block])(lambda block=block: start(block))
        pl.when(jnp.logical_not(inside[block]))(lambda block=block: clear(block))
    finish(1)
    for block in (0, 2):
        pl.when(inside[block])(lambda block=block: finish(block))

    packed = [strip[b].reshape(EY, BZ) for b in range(3)]
    stiff_s, buoy_s, damp_s = coef_strip_ref[0], coef_strip_ref[1], coef_strip_ref[2]
    p_s, vx_s, vy_s, vz_s = (
        sum(strip_of(packed[b], b, slot) for b in range(3)) for slot in range(4)
    )

    for step in range(1, STEPS + 1):
        k = step - 1
        edge_up = p_s * cut_up
        vx_s = vx_s - buoy_s * (pltpu.roll(p_s, BZ - STRIP, 1) - p_s)
        vy_s = vy_s - buoy_s * (y_up(p_s) - p_s)
        vz_s = vz_s - buoy_s * (pltpu.roll(p_s, BZ - 1, 1) - p_s)
        edge_down = vz_s * cut_down
        if step < STEPS:
            spread = (vx_s - pltpu.roll(vx_s, STRIP, 1)) + (vy_s - y_down(vy_s))
            spread = spread + (vz_s - pltpu.roll(vz_s, 1, 1))
            p_s = damp_s * (p_s - stiff_s * spread) + ss_ref[k]

        vx_below = None
        p_now = field[0, step - 1]
        for x in range(step - 1, EX - step):
            p_next = field[0, x + 1]
            buoyancy = coef_ref[1, x]
            slope_x = p_next - p_now
            vx = field[1, x] - buoyancy * slope_x
            field[1, x] = vx
            if x >= step:
                slope_y = y_up(p_now) - p_now
                slope_z = z_up(p_now, edge_up, x) - p_now
                vy = field[2, x] - buoyancy * slope_y
                vz = field[3, x] - buoyancy * slope_z
                field[2, x] = vy
                field[3, x] = vz
                spread = (vx - vx_below) + (vy - y_down(vy))
                spread = spread + (vz - z_down(vz, edge_down, x))
                if step < STEPS:
                    field[0, x] = (
                        coef_ref[2, x] * (p_now - coef_ref[0, x] * spread) + s_ref[k, x]
                    )
                if BX <= x < 2 * BX:
                    own = x - BX
                    term = hist_ref[k, 0, own] * spread[0:BY]
                    grad_s = -term if k == 0 else grad_ref[0, own] - term
                    grad_ref[0, own] = grad_s
                    term = hist_ref[k, 1, own] * slope_x[0:BY]
                    term = term + hist_ref[k, 2, own] * slope_y[0:BY]
                    term = term + hist_ref[k, 3, own] * slope_z[0:BY]
                    grad_ref[1, own] = -term if k == 0 else grad_ref[1, own] - term
            vx_below = vx
            p_now = p_next


def shape(*dims):
    return jax.ShapeDtypeStruct(dims, F32)


def call(kernel, outs, operands, scratch=(), any_operands=(), smem_operands=(), bytes_moved=1 << 20):
    def spec(index):
        if index in any_operands:
            return pl.BlockSpec(memory_space=pl.ANY)
        if index in smem_operands:
            return pl.BlockSpec(memory_space=pltpu.SMEM)
        return pl.BlockSpec(memory_space=pltpu.VMEM)

    return pl.pallas_call(
        kernel,
        out_shape=outs,
        in_specs=[spec(index) for index in range(len(operands))],
        out_specs=[pl.BlockSpec(memory_space=pltpu.VMEM)] * len(outs),
        scratch_shapes=list(scratch),
        compiler_params=pltpu.CompilerParams(vmem_limit_bytes=VMEM_LIMIT),
        cost_estimate=pl.CostEstimate(flops=1 << 24, bytes_accessed=bytes_moved, transcendentals=0),
    )(*operands)


def from_sides(array, axes):
    count = lax.axis_size("gy")

    def route(offset):
        pairs = []
        for target in range(count):
            source = target + offset
            if 0 <= source < count:
                if "gz" in axes:
                    pairs += [(2 * source + z, 2 * target + 1 - z) for z in range(2)]
                else:
                    pairs.append((source, target))
        return pairs

    if count == 2:
        both = lax.ppermute(array, axes, route(1) + route(-1))
        me = lax.axis_index("gy")
        return both * (me == 0).astype(F32), both * (me == 1).astype(F32)
    return lax.ppermute(array, axes, route(1)), lax.ppermute(array, axes, route(-1))


def along_x(array):
    count = lax.axis_size("gx")
    forward = [(i, i + 1) for i in range(count - 1)]
    backward = [(i + 1, i) for i in range(count - 1)]
    return lax.ppermute(array, "gx", forward), lax.ppermute(array, "gx", backward)


def table(cells, wave, width):
    short = width - cells.shape[0]
    places = jnp.pad(cells.T.astype(F32), ((0, 1), (0, short)), constant_values=-1000.0)
    return jnp.concatenate([places, jnp.pad(wave, ((0, 0), (0, short)))], 0)


def local(
    stored, adjoint_end, labels, tissue, source_cells, source_wave, receiver_cells, receiver_wave
):
    assert lax.axis_size("gz") == 2 and labels.shape == (BX, BY, BZ)
    gathered = lax.all_gather(stored, "gx")
    al, edges, strips = call(
        pack_kernel,
        [shape(5, BX, BY, BZ), shape(9 * BX + 3, 8, BZ), shape(3, BY, BZ)],
        [stored, adjoint_end, labels],
    )
    al_low, al_high = along_x(al)
    other = lax.ppermute(strips, "gz", [(0, 1), (1, 0)])
    up, down = from_sides(edges, "gy")
    diagonal_up, diagonal_down = from_sides(edges[9 * BX :], ("gy", "gz"))
    xw, xa = call(
        merge_kernel,
        [shape(4 * BX + 5, 8, BZ), shape(5 * BX + 10, 8, BZ)],
        [up, down, strips, other, diagonal_up, diagonal_down],
    )
    gathered_x = lax.all_gather(xw, "gx")
    xa_low, xa_high = along_x(xa)
    receivers = table(receiver_cells, receiver_wave, -(-receiver_cells.shape[0] // 256) * 256)
    sources = table(source_cells, source_wave, -(-source_cells.shape[0] // 128) * 128)
    r, rs, s, ss = call(
        inject_kernel,
        [
            shape(STEPS, EX * EY, BZ),
            shape(STEPS, EY, BZ),
            shape(STEPS - 1, EX * EY, BZ),
            shape(STEPS - 1, EY, BZ),
        ],
        [receivers, sources],
    )
    r = r.reshape(STEPS, EX, EY, BZ)
    s = s.reshape(STEPS - 1, EX, EY, BZ)
    adjoint_start, hist, coef, coef_strip = call(
        adjoint_kernel,
        [
            shape(4, BX, BY, BZ),
            shape(STEPS, 4, BX, BY, BZ),
            shape(3, EX, EY, BZ),
            shape(3, EY, BZ),
        ],
        [al, al_low, al_high, xa, xa_low, xa_high, r, rs, tissue],
        scratch=[
            pltpu.VMEM((5, EX, EY, BZ), F32),
            pltpu.VMEM((3, 2, 5, 8, BZ), F32),
            pltpu.SemaphoreType.DMA,
        ],
        any_operands=range(6),
        smem_operands=(8,),
    )
    (gradient,) = call(
        forward_kernel,
        [shape(2, BX, BY, BZ)],
        [gathered, gathered_x, coef, coef_strip, s, ss, hist],
        scratch=[
            pltpu.VMEM((4, EX, EY, BZ), F32),
            pltpu.VMEM((3, 5, 8, BZ), F32),
            pltpu.SemaphoreType.DMA,
        ],
        any_operands=range(2),
    )
    return gradient, adjoint_start


def solution(mesh):
    return jax.shard_map(
        local,
        mesh=mesh,
        in_specs=(
            P("shot", "gx", "gy", "gz"),
            P("shot", "gx", "gy", "gz"),
            P("gx", "gy", "gz"),
            P(),
            P("shot", None),
            P(None, "shot"),
            P(),
            P(None, "shot"),
        ),
        out_specs=(P("shot", "gx", "gy", "gz"), P("shot", "gx", "gy", "gz")),
        check_vma=False,
    )
```

```python
import jax
import jax.numpy as jnp
from jax import lax
from jax.experimental import pallas as pl
from jax.experimental.pallas import tpu as pltpu
from jax.sharding import PartitionSpec as P

STEPS = 4
MARGIN = 4
BX, BY, BZ = 4, 32, 128
EX, EY = BX + 2 * MARGIN, BY + 2 * MARGIN
STRIP = 2 * MARGIN
F32 = jnp.float32
BF16 = jnp.bfloat16
VMEM_LIMIT = 16 * 1024 * 1024
OWN_ROWS = BX * BY + 2 * BX * 8 + EY
ADJ_ROWS_OWN = BX * BY + 3 * BX * 8 + EY
WAVE_ROWS = 3 * BY + 5 * 8 + EY
ADJ_ROWS = 3 * BY + 8 * 8 + EY


def lanes(shape):
    return lax.broadcasted_iota(jnp.int32, shape, len(shape) - 1)


def rows(shape):
    return lax.broadcasted_iota(jnp.int32, shape, len(shape) - 2)


def run(copies):
    for copy in copies:
        copy.start()
    for copy in copies:
        copy.wait()


def class_values(tissue_ref, index):
    speed = jnp.full((1, BZ), tissue_ref[0, index], F32)
    density = jnp.full((1, BZ), tissue_ref[1, index], F32)
    damping = 1.0 - jnp.full((1, BZ), tissue_ref[2, index], F32)
    return density * speed, speed / density, damping


def buoyancy_of(labels, tissue_ref):
    result = jnp.zeros(labels.shape, F32)
    for index in range(tissue_ref.shape[1]):
        result = jnp.where(labels == float(index + 1), class_values(tissue_ref, index)[1], result)
    return result


def coefficients(labels, tissue_ref):
    stiffness = jnp.zeros(labels.shape, F32)
    buoyancy = jnp.zeros(labels.shape, F32)
    damping = jnp.zeros(labels.shape, F32)
    for index in range(tissue_ref.shape[1]):
        picked = labels == float(index + 1)
        values = class_values(tissue_ref, index)
        stiffness = jnp.where(picked, values[0], stiffness)
        buoyancy = jnp.where(picked, values[1], buoyancy)
        damping = jnp.where(picked, values[2], damping)
    return stiffness, buoyancy, damping


def face_kernel(
    stored_hbm, adj_hbm, lab_hbm, tissue_hbm,
    p_ref, ql_ref, face_x_ref, face_y_ref, face_z_ref,
    stored, adj, lab, tissue, sem,
):
    run([
        pltpu.make_async_copy(stored_hbm, stored, sem),
        pltpu.make_async_copy(adj_hbm, adj, sem),
        pltpu.make_async_copy(lab_hbm, lab, sem),
        pltpu.make_async_copy(tissue_hbm, tissue, sem),
    ])
    lane = lanes((BY, BZ))
    row = rows((8, BZ))
    face_y = jnp.zeros((8, BZ), F32)
    face_z = jnp.zeros((BY, BZ), F32)
    for x in range(BX):
        labels = lab[x].astype(F32) + 1.0
        buoyancy = buoyancy_of(labels, tissue)
        plane = slice(x * BY, x * BY + BY)
        p_ref[plane] = stored[0, x]
        ql_ref[plane] = adj[0, x]
        ql_ref[x * BY + BX * BY : (x + 1) * BY + BX * BY] = labels
        for kind, (v, factor) in enumerate(((stored, None), (adj, buoyancy))):
            vx, vy, vz = v[1, x], v[2, x, BY - 8 : BY], v[3, x]
            if factor is not None:
                vx, vy, vz = factor * vx, factor[BY - 8 : BY] * vy, factor * vz
            if x == BX - 1:
                face_x_ref[kind * BY : kind * BY + BY] = vx
            index = kind * BX + x
            face_y = jnp.where(row == index, pltpu.roll(vy, (index + 1) % 8, 0), face_y)
            face_z = jnp.where(lane == index, pltpu.roll(vz, index + 1, 1), face_z)
    face_y_ref[...] = face_y
    face_z_ref[...] = face_z


def pack_kernel(
    stored_hbm, adj_hbm, lab_hbm, tissue_hbm, face_x, face_y, face_z,
    s_ref, t_ref, edge_ref, corner_ref, strip_ref,
    stored, adj, lab, tissue, sem,
):
    run([
        pltpu.make_async_copy(stored_hbm, stored, sem),
        pltpu.make_async_copy(adj_hbm, adj, sem),
        pltpu.make_async_copy(lab_hbm, lab, sem),
        pltpu.make_async_copy(tissue_hbm, tissue, sem),
    ])
    gx, gy, gz = (lax.axis_index(name) for name in ("gx", "gy", "gz"))
    count = lax.axis_size("gx")
    lane = lanes((BY, BZ))
    row = rows((BY, BZ))
    tile_row = rows((8, BZ))
    below = (
        jnp.where(gx == count // 2, 0.0, 1.0),
        jnp.where(gx == 0, 0.0, 1.0),
    )
    has_y = jnp.where(gy == 0, 0.0, 1.0)
    has_z = jnp.where(gz == 0, 0.0, 1.0)
    planes = [[None] * BX for _ in range(5)]
    previous = [face_x[kind * BY : kind * BY + BY] * below[kind] for kind in range(2)]
    tile_y = face_y[...] * has_y
    tile_z = face_z[...] * has_z
    for x in range(BX):
        labels = lab[x].astype(F32) + 1.0
        buoyancy = buoyancy_of(labels, tissue)
        planes[0][x] = stored[0, x]
        planes[2][x] = adj[0, x]
        planes[4][x] = labels
        for kind, v in enumerate((stored, adj)):
            vx, vy, vz = v[1, x], v[2, x], v[3, x]
            if kind == 1:
                vx, vy, vz = buoyancy * vx, buoyancy * vy, buoyancy * vz
            index = kind * BX + x
            row_below = tile_y[index : index + 1]
            lane_below = pltpu.roll(tile_z, (BZ - index) % BZ, 1) if index else tile_z
            y_below = jnp.where(row == 0, row_below, pltpu.roll(vy, 1, 0))
            z_below = jnp.where(lane == 0, lane_below, pltpu.roll(vz, 1, 1))
            spread = ((vx - previous[kind]) + (vy - y_below)) + (vz - z_below)
            previous[kind] = vx
            (s_ref, t_ref)[kind][x * BY : x * BY + BY] = spread
            planes[1 + 2 * kind][x] = spread

    strips = [jnp.zeros((BY, BZ), F32) for _ in range(2)]
    for field in range(5):
        group, slot = (0, field) if field < 2 else (1, field - 2)
        for x in range(BX):
            block = planes[field][x]
            tile = jnp.where(tile_row < MARGIN, block[0:8], block[BY - 8 : BY])
            index = field * BX + x
            edge_ref[index * 8 : index * 8 + 8] = tile
            base = slot * BX * STRIP + x * STRIP
            rolled = pltpu.roll(block, base + MARGIN, 1)
            first = base + MARGIN * gz
            strips[group] = jnp.where(
                (lane >= first) & (lane < first + MARGIN), rolled, strips[group]
            )
    for group in range(2):
        strip = strips[group]
        strip_ref[group * BY : group * BY + BY] = strip
        tile = jnp.where(tile_row < MARGIN, strip[0:8], strip[BY - 8 : BY])
        index = 5 * BX + group
        edge_ref[index * 8 : index * 8 + 8] = tile
        corner_ref[group * 8 : group * 8 + 8] = tile


def merge_kernel(
    up_ref, down_ref, strip_ref, other_ref, corner_up_ref, corner_down_ref, s_ref, t_ref,
    own_ref, high_ref, low_ref, adj_own_ref, even_ref, odd_ref,
    halo_ref,
):
    gx, gy = lax.axis_index("gx"), lax.axis_index("gy")
    row = rows((8, BZ))
    take_up = (row < MARGIN) & (gy < lax.axis_size("gy") - 1)
    take_down = (row >= MARGIN) & (gy > 0)

    def halo(up, down, index):
        sl = slice(index * 8, index * 8 + 8)
        return jnp.where(take_up, up[sl], jnp.where(take_down, down[sl], 0.0))

    for index in range(5 * BX):
        halo_ref[index] = halo(up_ref, down_ref, index)
    own_ref[0 : BX * BY] = s_ref[...]
    for index in range(2 * BX):
        start = BX * BY + index * 8
        own_ref[start : start + 8] = halo_ref[index]
    high_ref[0 : 3 * BY] = s_ref[0 : 3 * BY]
    low_ref[0 : 3 * BY] = s_ref[BY : 4 * BY]
    for place, (high, low) in enumerate(((0, 1), (1, 2), (2, 3), (4, 6), (5, 7))):
        start = 3 * BY + place * 8
        high_ref[start : start + 8] = halo_ref[high]
        low_ref[start : start + 8] = halo_ref[low]
    adj_own_ref[0 : BX * BY] = t_ref[...]
    for index in range(3 * BX):
        start = BX * BY + index * 8
        adj_own_ref[start : start + 8] = halo_ref[2 * BX + index]
    parity = lax.rem(gx, 2)
    for first, target in ((1 - parity, even_ref), (parity, odd_ref)):
        for place in range(3):
            target[place * BY : place * BY + BY] = t_ref[
                pl.ds(pl.multiple_of((first + place) * BY, BY), BY)
            ]
        indices = [2 * BX + first, 2 * BX + first + 1, 2 * BX + first + 2]
        indices += [3 * BX + 2 * first, 3 * BX + 2 * first + 1]
        indices += [4 * BX + first, 4 * BX + first + 1, 4 * BX + first + 2]
        for place, index in enumerate(indices):
            start = 3 * BY + place * 8
            target[start : start + 8] = halo_ref[index]
    for group, targets in enumerate(((own_ref, high_ref, low_ref), (adj_own_ref, even_ref, odd_ref))):
        strip = strip_ref[group * BY : group * BY + BY] + other_ref[group * BY : group * BY + BY]
        tile = halo(up_ref, down_ref, 5 * BX + group) + halo(corner_up_ref, corner_down_ref, group)
        for target in targets:
            start = target.shape[0] - EY
            target[start : start + BY] = strip
            target[start + BY : start + EY] = tile


def split(values):
    high = values.astype(BF16)
    rest = values - high.astype(F32)
    middle = rest.astype(BF16)
    low = (rest - middle.astype(F32)).astype(BF16)
    return high, middle, low


def inject_points(cells, wave_ref, width, out_ref, strip_out_ref, waves):
    gx, gy, gz = (lax.axis_index(name) for name in ("gx", "gy", "gz"))
    cut = BZ * lax.axis_size("gz") // 2 - MARGIN
    for start in range(0, cells.shape[1], width):
        sl = slice(start, start + width)
        cell_x = cells[0:1, sl] - (gx * BX - MARGIN)
        cell_y = cells[1:2, sl] - gy * BY
        cell_z = cells[2:3, sl]
        in_x = (cell_x >= 0) & (cell_x < EX)
        in_y = (cell_y >= -MARGIN) & (cell_y < BY + MARGIN)
        row = jnp.where(cell_y < 0, cell_y + EY, cell_y)
        flat = jnp.where(in_x & in_y, cell_x * EY + row, -1)
        row = jnp.where(in_y, row, -1)
        zz = cell_z - cut
        in_strip = in_x & (zz >= 0) & (zz < STRIP)
        strip_lane = jnp.where(in_strip, cell_x * STRIP + zz, -1)
        here = (rows((EX * EY, width)) == flat).astype(F32).astype(BF16)
        at_z = rows((BZ, width)) == (cell_z - gz * BZ)
        at_strip = (rows((BZ, width)) == strip_lane).astype(F32).astype(BF16)
        at_row = rows((EY, width)) == row
        for wave in range(waves):
            total = None
            strip_total = None
            for part in split(wave_ref[wave : wave + 1, sl]):
                part = part.astype(F32)
                term = lax.dot_general(
                    here,
                    jnp.where(at_z, part, 0.0).astype(BF16),
                    (((1,), (1,)), ((), ())),
                    preferred_element_type=F32,
                )
                total = term if total is None else total + term
                term = lax.dot_general(
                    jnp.where(at_row, part, 0.0).astype(BF16),
                    at_strip,
                    (((1,), (1,)), ((), ())),
                    preferred_element_type=F32,
                )
                strip_total = term if strip_total is None else strip_total + term
            if start > 0:
                total = total + out_ref[wave]
                strip_total = strip_total + strip_out_ref[wave]
            out_ref[wave] = total
            strip_out_ref[wave] = strip_total


def inject_kernel(
    receiver_hbm, receiver_wave_hbm, source_hbm, source_wave_hbm,
    r_ref, rs_ref, s_ref, ss_ref,
    receivers, receiver_wave, sources, source_wave, sem,
):
    run([
        pltpu.make_async_copy(receiver_hbm, receivers, sem),
        pltpu.make_async_copy(receiver_wave_hbm, receiver_wave, sem),
        pltpu.make_async_copy(source_hbm, sources, sem),
        pltpu.make_async_copy(source_wave_hbm, source_wave, sem),
    ])
    inject_points(receivers, receiver_wave, 256, r_ref, rs_ref, STEPS)
    inject_points(sources, source_wave, sources.shape[1], s_ref, ss_ref, STEPS - 1)


def strip_of(packed, block, slot):
    lane = lanes(packed.shape)
    width = BX * STRIP
    shift = (block * width - slot * width) % BZ
    moved = pltpu.roll(packed, shift, 1) if shift else packed
    return jnp.where((lane >= block * width) & (lane < (block + 1) * width), moved, 0.0)


def y_up(v):
    return pltpu.roll(v, EY - 1, 0)


def y_down(v):
    return pltpu.roll(v, 1, 0)


def z_up(v, strip, x):
    edge = pltpu.roll(strip, (BZ - 1 - (x * STRIP + MARGIN)) % BZ, 1)
    return jnp.where(lanes(v.shape) == BZ - 1, edge, pltpu.roll(v, BZ - 1, 1))


def z_down(v, strip, x):
    edge = pltpu.roll(strip, (BZ - (x * STRIP + MARGIN - 1)) % BZ, 1)
    return jnp.where(lanes(v.shape) == 0, edge, pltpu.roll(v, 1, 1))


def strip_flux(values, buoyancy):
    flux_x = buoyancy * (pltpu.roll(values, BZ - STRIP, 1) - values)
    flux_y = buoyancy * (y_up(values) - values)
    flux_z = buoyancy * (pltpu.roll(values, BZ - 1, 1) - values)
    spread = (flux_x - pltpu.roll(flux_x, STRIP, 1)) + (flux_y - y_down(flux_y))
    return flux_z, spread + (flux_z - pltpu.roll(flux_z, 1, 1))


def cut_flags():
    gz, half = lax.axis_index("gz"), lax.axis_size("gz") // 2
    return jnp.where(gz == half - 1, 1.0, 0.0), jnp.where(gz == half, 1.0, 0.0)


def adjoint_kernel(
    ql, ql_even, ql_odd, late, late_even, late_odd, adj_hbm, r_ref, rs_ref, tissue_hbm,
    out_ref, hist_ref, coef_ref, coef_strip_ref,
    field, strip, tissue, sem,
):
    gx, count = lax.axis_index("gx"), lax.axis_size("gx")
    cut_up, cut_down = cut_flags()

    def plane_copies(source, first, rows_of, index, planes):
        return [
            pltpu.make_async_copy(
                source.at[pl.ds(first + i * rows_of, rows_of)],
                field.at[index, plane, pl.ds(0 if rows_of == BY else BY, rows_of), :],
                sem,
            )
            for i, plane in enumerate(planes)
        ]

    def own_copies():
        planes = range(BX, 2 * BX)
        copies = [
            pltpu.make_async_copy(adj_hbm.at[pl.ds(1, 3)], out_ref.at[pl.ds(1, 3)], sem),
            pltpu.make_async_copy(tissue_hbm, tissue, sem),
            pltpu.make_async_copy(late.at[pl.ds(ADJ_ROWS_OWN - EY, EY)], strip.at[1], sem),
        ]
        copies += plane_copies(ql, 0, BY, 0, planes) + plane_copies(ql, BX * BY, BY, 2, planes)
        copies += plane_copies(late, 0, BY, 1, planes)
        for index in range(3):
            copies += plane_copies(late, BX * BY + index * BX * 8, 8, index, planes)
        return copies

    def side_copies(raw, extra, block):
        first = 1 if block == 0 else 2 * BX
        planes = range(block * BX, block * BX + BX)
        copies = [pltpu.make_async_copy(extra.at[pl.ds(ADJ_ROWS - EY, EY)], strip.at[block], sem)]
        copies += plane_copies(raw, 0, BY, 0, planes) + plane_copies(raw, BX * BY, BY, 2, planes)
        copies += plane_copies(extra, 0, BY, 1, range(first, first + 3))
        copies += plane_copies(extra, 3 * BY, 8, 0, range(first, first + 3))
        near = first + 1 if block == 0 else first
        copies += plane_copies(extra, 3 * BY + 24, 8, 1, range(near, near + 2))
        copies += plane_copies(extra, 3 * BY + 40, 8, 2, range(first, first + 3))
        return copies

    def clear(block):
        planes = slice(block * BX, block * BX + BX)
        field[:, planes] = jnp.zeros((3, BX, EY, BZ), F32)
        strip[block] = jnp.zeros((EY, BZ), F32)

    def both(even, act):
        for raw, extra, block in (
            (ql_even, late_even, 2 if even else 0),
            (ql_odd, late_odd, 0 if even else 2),
        ):
            inside = gx > 0 if block == 0 else gx < count - 1
            act(side_copies(raw, extra, block), inside, block)

    def start(copies, inside, block):
        @pl.when(inside)
        def _():
            for copy in copies:
                copy.start()

        @pl.when(jnp.logical_not(inside))
        def _():
            clear(block)

    def finish(copies, inside, block):
        @pl.when(inside)
        def _():
            for copy in copies:
                copy.wait()

    is_even = lax.rem(gx, 2) == 0
    for copy in own_copies():
        copy.start()
    for act in (start, finish):
        pl.when(is_even)(lambda: both(True, act))
        pl.when(jnp.logical_not(is_even))(lambda: both(False, act))
    for copy in own_copies():
        copy.wait()

    for x in range(EX):
        for index, values in enumerate(coefficients(field[2, x], tissue)):
            coef_ref[index, x] = values
    packed = [strip[block] for block in range(3)]
    q_s, t_s, label_s = (
        sum(strip_of(packed[block], block, slot) for block in range(3)) for slot in range(3)
    )
    stiff_s, buoy_s, damp_s = coefficients(label_s, tissue)
    coef_strip_ref[0], coef_strip_ref[1], coef_strip_ref[2] = stiff_s, buoy_s, damp_s

    for step in range(1, STEPS + 1):
        k = STEPS - step
        q_s = q_s + rs_ref[k]
        u_s = stiff_s * damp_s * q_s
        flux_s, spread = strip_flux(u_s, buoy_s)
        t_s = t_s + spread
        q_s = damp_s * q_s + t_s
        edge_up = u_s * cut_up
        edge_down = flux_s * cut_down

        def injected(x):
            value = field[0, x] + r_ref[k, x]
            return value, coef_ref[0, x] * coef_ref[2, x] * value

        flux_below = None
        q_now, u_now = injected(step - 1)
        for x in range(step - 1, EX - step):
            q_next, u_next = injected(x + 1)
            buoyancy = coef_ref[1, x]
            slope_x = u_next - u_now
            flux_x = buoyancy * slope_x
            if x >= step:
                slope_y = y_up(u_now) - u_now
                slope_z = z_up(u_now, edge_up, x) - u_now
                flux_y = buoyancy * slope_y
                flux_z = buoyancy * slope_z
                spread = (flux_x - flux_below) + (flux_y - y_down(flux_y))
                spread = spread + (flux_z - z_down(flux_z, edge_down, x))
                damped = coef_ref[2, x] * q_now
                if BX <= x < 2 * BX:
                    own = x - BX
                    hist_ref[k, 0, own] = damped[0:BY]
                    for index, slope in enumerate((slope_x, slope_y, slope_z)):
                        w = out_ref[1 + index, own] + slope[0:BY]
                        out_ref[1 + index, own] = w
                        hist_ref[k, 1 + index, own] = w
                t = field[1, x] + spread
                field[1, x] = t
                field[0, x] = damped + t
            flux_below = flux_x
            q_now, u_now = q_next, u_next

    for x in range(BX):
        out_ref[0, x] = field[0, BX + x, 0:BY]


def forward_kernel(
    p, p_high, p_low, late, late_high, late_low,
    coef_ref, coef_strip_ref, s_ref, ss_ref, hist_ref,
    grad_ref,
    field, strip, sem,
):
    gx, count = lax.axis_index("gx"), lax.axis_size("gx")
    cut_up, cut_down = cut_flags()

    def plane_copies(source, first, rows_of, index, planes):
        return [
            pltpu.make_async_copy(
                source.at[pl.ds(first + i * rows_of, rows_of)],
                field.at[index, plane, pl.ds(0 if rows_of == BY else BY, rows_of), :],
                sem,
            )
            for i, plane in enumerate(planes)
        ]

    def own_copies():
        planes = range(BX, 2 * BX)
        copies = [pltpu.make_async_copy(late.at[pl.ds(OWN_ROWS - EY, EY)], strip.at[1], sem)]
        copies += plane_copies(p, 0, BY, 0, planes) + plane_copies(late, 0, BY, 1, planes)
        for index in range(2):
            copies += plane_copies(late, BX * BY + index * BX * 8, 8, index, planes)
        return copies

    def side_copies(raw, extra, block):
        first = 1 if block == 0 else 2 * BX
        near = first + 1 if block == 0 else first
        copies = [pltpu.make_async_copy(extra.at[pl.ds(WAVE_ROWS - EY, EY)], strip.at[block], sem)]
        copies += plane_copies(raw, 0, BY, 0, range(block * BX, block * BX + BX))
        copies += plane_copies(extra, 0, BY, 1, range(first, first + 3))
        copies += plane_copies(extra, 3 * BY, 8, 0, range(first, first + 3))
        copies += plane_copies(extra, 3 * BY + 24, 8, 1, range(near, near + 2))
        return copies

    def clear(block):
        planes = slice(block * BX, block * BX + BX)
        field[:, planes] = jnp.zeros((2, BX, EY, BZ), F32)
        strip[block] = jnp.zeros((EY, BZ), F32)

    sides = ((p_low, late_low, 0, gx > 0), (p_high, late_high, 2, gx < count - 1))
    for copy in own_copies():
        copy.start()
    for raw, extra, block, inside in sides:

        @pl.when(inside)
        def _(raw=raw, extra=extra, block=block):
            for copy in side_copies(raw, extra, block):
                copy.start()

        @pl.when(jnp.logical_not(inside))
        def _(block=block):
            clear(block)

    for copy in own_copies():
        copy.wait()
    for raw, extra, block, inside in sides:

        @pl.when(inside)
        def _(raw=raw, extra=extra, block=block):
            for copy in side_copies(raw, extra, block):
                copy.wait()

    packed = [strip[block] for block in range(3)]
    p_s, s_s = (
        sum(strip_of(packed[block], block, slot) for block in range(3)) for slot in range(2)
    )
    stiff_s, buoy_s, damp_s = coef_strip_ref[0], coef_strip_ref[1], coef_strip_ref[2]

    for step in range(1, STEPS + 1):
        k = step - 1
        edge_up = p_s * cut_up
        flux_s, spread = strip_flux(p_s, buoy_s)
        edge_down = flux_s * cut_down
        if step < STEPS:
            s_s = s_s - spread
            p_s = damp_s * (p_s - stiff_s * s_s) + ss_ref[k]

        flux_below = None
        p_now = field[0, step - 1]
        for x in range(step - 1, EX - step):
            p_next = field[0, x + 1]
            buoyancy = coef_ref[1, x]
            slope_x = p_next - p_now
            flux_x = buoyancy * slope_x
            if x >= step:
                slope_y = y_up(p_now) - p_now
                slope_z = z_up(p_now, edge_up, x) - p_now
                flux_y = buoyancy * slope_y
                flux_z = buoyancy * slope_z
                spread = (flux_x - flux_below) + (flux_y - y_down(flux_y))
                spread = spread + (flux_z - z_down(flux_z, edge_down, x))
                spread = field[1, x] - spread
                if step < STEPS:
                    field[1, x] = spread
                    field[0, x] = (
                        coef_ref[2, x] * (p_now - coef_ref[0, x] * spread) + s_ref[k, x]
                    )
                if BX <= x < 2 * BX:
                    own = x - BX
                    term = hist_ref[k, 0, own] * spread[0:BY]
                    grad_ref[0, own] = -term if k == 0 else grad_ref[0, own] - term
                    term = hist_ref[k, 1, own] * slope_x[0:BY]
                    term = term + hist_ref[k, 2, own] * slope_y[0:BY]
                    term = term + hist_ref[k, 3, own] * slope_z[0:BY]
                    grad_ref[1, own] = -term if k == 0 else grad_ref[1, own] - term
            flux_below = flux_x
            p_now = p_next


def shape(*dims):
    return jax.ShapeDtypeStruct(dims, F32)


def call(kernel, outs, operands, scratch, places=""):
    spaces = {"h": pltpu.HBM, "a": pl.ANY, "v": pltpu.VMEM}
    return pl.pallas_call(
        kernel,
        out_shape=outs,
        in_specs=[pl.BlockSpec(memory_space=spaces[place]) for place in places],
        out_specs=[pl.BlockSpec(memory_space=pltpu.VMEM)] * len(outs),
        scratch_shapes=scratch,
        compiler_params=pltpu.CompilerParams(vmem_limit_bytes=VMEM_LIMIT),
        cost_estimate=pl.CostEstimate(flops=1 << 24, bytes_accessed=1 << 20, transcendentals=0),
    )(*operands)


def from_sides(array, axes):
    count = lax.axis_size("gy")

    def route(offset):
        pairs = []
        for target in range(count):
            source = target + offset
            if 0 <= source < count:
                if "gz" in axes:
                    pairs += [(2 * source + z, 2 * target + 1 - z) for z in range(2)]
                else:
                    pairs.append((source, target))
        return pairs

    if count == 2:
        both = lax.ppermute(array, axes, route(1) + route(-1))
        return both, both
    return lax.ppermute(array, axes, route(1)), lax.ppermute(array, axes, route(-1))


def rotated(array, axis, offset):
    count = lax.axis_size(axis)
    return lax.ppermute(array, axis, [((i + offset) % count, i) for i in range(count)])


def paired(array, odd):
    count = lax.axis_size("gx")
    pairs = []
    for i in range(count):
        partner = i ^ 1 if not odd else ((i - 1) ^ 1) + 1
        pairs.append((partner if 0 <= partner < count else i, i))
    return lax.ppermute(array, "gx", pairs)


def local(
    stored, adjoint_end, labels, tissue, source_cells, source_wave, receiver_cells, receiver_wave
):
    assert lax.axis_size("gz") == 2 and labels.shape == (BX, BY, BZ)
    half = lax.axis_size("gx") // 2
    block_scratch = [
        pltpu.VMEM((4, BX, BY, BZ), F32),
        pltpu.VMEM((4, BX, BY, BZ), F32),
        pltpu.VMEM((BX, BY, BZ), jnp.int32),
        pltpu.SMEM(tissue.shape, F32),
        pltpu.SemaphoreType.DMA,
    ]
    arguments = [stored, adjoint_end, labels, tissue]
    p, ql, face_x, face_y, face_z = call(
        face_kernel,
        [shape(BX * BY, BZ), shape(2 * BX * BY, BZ), shape(2 * BY, BZ), shape(8, BZ), shape(BY, BZ)],
        arguments,
        block_scratch,
        "hhhh",
    )
    face_x = rotated(face_x, "gx", -1)
    face_y = rotated(face_y, "gy", -1)
    face_z = rotated(face_z, "gz", -1)
    p_own, p_high, p_low = (rotated(p, "gx", half + offset) for offset in (0, 1, -1))
    ql_even, ql_odd = paired(ql, False), paired(ql, True)
    receivers, sources = receiver_cells.T, source_cells.T
    r, rs, src, src_strip = call(
        inject_kernel,
        [
            shape(STEPS, EX * EY, BZ),
            shape(STEPS, EY, BZ),
            shape(STEPS - 1, EX * EY, BZ),
            shape(STEPS - 1, EY, BZ),
        ],
        [receivers, receiver_wave, sources, source_wave],
        [
            pltpu.VMEM(receivers.shape, jnp.int32),
            pltpu.VMEM(receiver_wave.shape, F32),
            pltpu.VMEM(sources.shape, jnp.int32),
            pltpu.VMEM(source_wave.shape, F32),
            pltpu.SemaphoreType.DMA,
        ],
        "hhhh",
    )
    r = r.reshape(STEPS, EX, EY, BZ)
    src = src.reshape(STEPS - 1, EX, EY, BZ)
    s, t, edges, corners, strips = call(
        pack_kernel,
        [
            shape(BX * BY, BZ),
            shape(BX * BY, BZ),
            shape((5 * BX + 2) * 8, BZ),
            shape(16, BZ),
            shape(2 * BY, BZ),
        ],
        arguments + [face_x, face_y, face_z],
        block_scratch,
        "hhhhvvv",
    )
    other = rotated(strips, "gz", 1)
    up, down = from_sides(edges, "gy")
    corner_up, corner_down = from_sides(corners, ("gy", "gz"))
    late, late_for_low, late_for_high, adj_late, adj_even, adj_odd = call(
        merge_kernel,
        [
            shape(OWN_ROWS, BZ),
            shape(WAVE_ROWS, BZ),
            shape(WAVE_ROWS, BZ),
            shape(ADJ_ROWS_OWN, BZ),
            shape(ADJ_ROWS, BZ),
            shape(ADJ_ROWS, BZ),
        ],
        [up, down, strips, other, corner_up, corner_down, s, t],
        [pltpu.VMEM((5 * BX, 8, BZ), F32)],
        "vvvvvvvv",
    )
    late_own = rotated(late, "gx", half)
    late_high = rotated(late_for_low, "gx", half + 1)
    late_low = rotated(late_for_high, "gx", half - 1)
    adj_even, adj_odd = paired(adj_even, False), paired(adj_odd, True)
    adjoint_start, hist, coef, coef_strip = call(
        adjoint_kernel,
        [
            shape(4, BX, BY, BZ),
            shape(STEPS, 4, BX, BY, BZ),
            shape(3, EX, EY, BZ),
            shape(3, EY, BZ),
        ],
        [ql, ql_even, ql_odd, adj_late, adj_even, adj_odd, adjoint_end, r, rs, tissue],
        [
            pltpu.VMEM((3, EX, EY, BZ), F32),
            pltpu.VMEM((3, EY, BZ), F32),
            pltpu.SMEM(tissue.shape, F32),
            pltpu.SemaphoreType.DMA,
        ],
        "aaaaaahvvh",
    )
    (gradient,) = call(
        forward_kernel,
        [shape(2, BX, BY, BZ)],
        [p_own, p_high, p_low, late_own, late_high, late_low, coef, coef_strip, src, src_strip, hist],
        [
            pltpu.VMEM((2, EX, EY, BZ), F32),
            pltpu.VMEM((3, EY, BZ), F32),
            pltpu.SemaphoreType.DMA,
        ],
        "aaaaaavvvvv",
    )
    return gradient, adjoint_start


def solution(mesh):
    return jax.shard_map(
        local,
        mesh=mesh,
        in_specs=(
            P("shot", "gx", "gy", "gz"),
            P("shot", "gx", "gy", "gz"),
            P("gx", "gy", "gz"),
            P(),
            P("shot", None),
            P(None, "shot"),
            P(),
            P(None, "shot"),
        ),
        out_specs=(P("shot", "gx", "gy", "gz"), P("shot", "gx", "gy", "gz")),
        check_vma=False,
    )
```

```python
import jax
import jax.numpy as jnp
from jax import lax
from jax.experimental import pallas as pl
from jax.experimental.pallas import tpu as pltpu
from jax.sharding import PartitionSpec as P

STEPS = 4
MARGIN = 4
BX, BY, BZ = 4, 32, 128
EX, EY = BX + 2 * MARGIN, BY + 2 * MARGIN
STRIP = 2 * MARGIN
F32 = jnp.float32
BF16 = jnp.bfloat16
VMEM_LIMIT = 16 * 1024 * 1024
PLANES = BX * BY
OWN_ROWS = PLANES + 2 * BX * 8 + EY
ADJ_OWN_ROWS = PLANES + 3 * BX * 8 + EY
WAVE_ROWS = 3 * BY + 5 * 8 + EY
ADJ_ROWS = 3 * BY + 8 * 8 + EY


def lanes(shape):
    return lax.broadcasted_iota(jnp.int32, shape, len(shape) - 1)


def rows(shape):
    return lax.broadcasted_iota(jnp.int32, shape, len(shape) - 2)


def run(copies):
    for copy in copies:
        copy.start()
    for copy in copies:
        copy.wait()


def class_values(tissue_ref, index):
    speed = jnp.full((1, BZ), tissue_ref[0, index], F32)
    density = jnp.full((1, BZ), tissue_ref[1, index], F32)
    damping = 1.0 - jnp.full((1, BZ), tissue_ref[2, index], F32)
    return density * speed, speed / density, damping


def buoyancy_of(labels, tissue_ref):
    result = jnp.zeros(labels.shape, F32)
    for index in range(tissue_ref.shape[1]):
        result = jnp.where(labels == float(index + 1), class_values(tissue_ref, index)[1], result)
    return result


def coefficients(labels, tissue_ref):
    stiffness = jnp.zeros(labels.shape, F32)
    buoyancy = jnp.zeros(labels.shape, F32)
    damping = jnp.zeros(labels.shape, F32)
    for index in range(tissue_ref.shape[1]):
        picked = labels == float(index + 1)
        values = class_values(tissue_ref, index)
        stiffness = jnp.where(picked, values[0], stiffness)
        buoyancy = jnp.where(picked, values[1], buoyancy)
        damping = jnp.where(picked, values[2], damping)
    return stiffness, buoyancy, damping


def face_kernel(
    stored_hbm, adj_hbm, lab_hbm, tissue_hbm,
    p_ref, raw_ref, s_ref, t_ref, face_x_ref, face_y_ref, face_z_ref,
    stored, adj, lab, tissue, sem,
):
    run([
        pltpu.make_async_copy(stored_hbm, stored, sem),
        pltpu.make_async_copy(adj_hbm, adj, sem),
        pltpu.make_async_copy(lab_hbm, lab, sem),
        pltpu.make_async_copy(tissue_hbm, tissue, sem),
    ])
    lane = lanes((BY, BZ))
    row = rows((BY, BZ))
    tile_row = rows((8, BZ))
    face_y = jnp.zeros((8, BZ), F32)
    face_z = jnp.zeros((BY, BZ), F32)
    previous = [None, None]
    for x in range(BX):
        labels = lab[x].astype(F32) + 1.0
        buoyancy = buoyancy_of(labels, tissue)
        plane = slice(x * BY, x * BY + BY)
        p_ref[plane] = stored[0, x]
        for index, values in enumerate((stored[0, x], adj[0, x], labels)):
            raw_ref[index * PLANES + x * BY : index * PLANES + x * BY + BY] = values
        for kind, v in enumerate((stored, adj)):
            vx, vy, vz = v[1, x], v[2, x], v[3, x]
            if kind == 1:
                vx, vy, vz = buoyancy * vx, buoyancy * vy, buoyancy * vz
            y_below = pltpu.roll(vy, 1, 0)
            z_below = pltpu.roll(vz, 1, 1)
            index = kind * BX + x
            last = pltpu.roll(vy[BY - 8 : BY], (index + 1) % 8, 0)
            face_y = jnp.where(tile_row == index, last, face_y)
            face_z = jnp.where(lane == index, pltpu.roll(vz, index + 1, 1), face_z)
            spread = vx if x == 0 else vx - previous[kind]
            spread = spread + (vy - jnp.where(row == 0, 0.0, y_below))
            spread = spread + (vz - jnp.where(lane == 0, 0.0, z_below))
            (s_ref, t_ref)[kind][plane] = spread
            previous[kind] = vx
    for kind in range(2):
        face_x_ref[kind * BY : kind * BY + BY] = previous[kind]
    face_y_ref[...] = face_y
    face_z_ref[...] = face_z


def pack_kernel(
    raw_ref, s_in, t_in, face_x, face_y, face_z, _,
    s_ref, t_ref, edge_ref, corner_ref, strip_ref,
):
    gx, gy, gz = (lax.axis_index(name) for name in ("gx", "gy", "gz"))
    count = lax.axis_size("gx")
    lane = lanes((BY, BZ))
    row = rows((BY, BZ))
    tile_row = rows((8, BZ))
    below = (
        jnp.where(gx == count // 2, 0.0, 1.0),
        jnp.where(gx == 0, 0.0, 1.0),
    )
    tile_y = face_y[...] * jnp.where(gy == 0, 0.0, 1.0)
    tile_z = face_z[...] * jnp.where(gz == 0, 0.0, 1.0)
    strips = [jnp.zeros((BY, BZ), F32) for _ in range(2)]
    for field in range(5):
        group, slot = (0, field) if field < 2 else (1, field - 2)
        for x in range(BX):
            plane = slice(x * BY, x * BY + BY)
            if field in (1, 3):
                kind = field // 2
                block = (s_in, t_in)[kind][plane]
                if x == 0:
                    block = block - face_x[kind * BY : kind * BY + BY] * below[kind]
                index = kind * BX + x
                lane_below = pltpu.roll(tile_z, (BZ - index) % BZ, 1) if index else tile_z
                block = block - jnp.where(row == 0, tile_y[index : index + 1], 0.0)
                block = block - jnp.where(lane == 0, lane_below, 0.0)
                (s_ref, t_ref)[kind][plane] = block
            else:
                first = field // 2 * PLANES + x * BY
                block = raw_ref[first : first + BY]
            tile = jnp.where(tile_row < MARGIN, block[0:8], block[BY - 8 : BY])
            index = field * BX + x
            edge_ref[index * 8 : index * 8 + 8] = tile
            base = slot * BX * STRIP + x * STRIP
            rolled = pltpu.roll(block, base + MARGIN, 1)
            first = base + MARGIN * gz
            strips[group] = jnp.where(
                (lane >= first) & (lane < first + MARGIN), rolled, strips[group]
            )
    for group in range(2):
        strip = strips[group]
        strip_ref[group * BY : group * BY + BY] = strip
        tile = jnp.where(tile_row < MARGIN, strip[0:8], strip[BY - 8 : BY])
        index = 5 * BX + group
        edge_ref[index * 8 : index * 8 + 8] = tile
        corner_ref[group * 8 : group * 8 + 8] = tile


def merge_kernel(
    up_ref, down_ref, strip_ref, other_ref, corner_up_ref, corner_down_ref, s_ref, t_ref,
    _a, _b, _c, _d,
    own_ref, adj_own_ref, to_next_ref, to_last_ref,
):
    gy = lax.axis_index("gy")
    row = rows((8, BZ))
    take_up = (row < MARGIN) & (gy < lax.axis_size("gy") - 1)
    take_down = (row >= MARGIN) & (gy > 0)

    def halo(up, down, index):
        sl = slice(index * 8, index * 8 + 8)
        return jnp.where(take_up, up[sl], jnp.where(take_down, down[sl], 0.0))

    tiles = [halo(up_ref, down_ref, index) for index in range(5 * BX)]
    strips = []
    for group in range(2):
        sl = slice(group * BY, group * BY + BY)
        tile = halo(up_ref, down_ref, 5 * BX + group) + halo(corner_up_ref, corner_down_ref, group)
        strips.append((strip_ref[sl] + other_ref[sl], tile))

    def put(target, base, planes, chosen, strip):
        target[base : base + planes.shape[0]] = planes
        base += planes.shape[0]
        for index in chosen:
            target[base : base + 8] = tiles[index]
            base += 8
        target[base : base + BY] = strip[0]
        target[base + BY : base + EY] = strip[1]

    put(own_ref, 0, s_ref[...], range(2 * BX), strips[0])
    put(adj_own_ref, 0, t_ref[...], range(2 * BX, 5 * BX), strips[1])
    above, below = s_ref[0 : 3 * BY], s_ref[BY:PLANES]
    put(to_next_ref, 0, above, (0, 1, 2, 4, 5), strips[0])
    put(to_last_ref, 0, below, (1, 2, 3, 6, 7), strips[0])
    above, below = t_ref[0 : 3 * BY], t_ref[BY:PLANES]
    put(to_next_ref, WAVE_ROWS, below, (9, 10, 11, 14, 15, 17, 18, 19), strips[1])
    put(to_last_ref, WAVE_ROWS, above, (8, 9, 10, 12, 13, 16, 17, 18), strips[1])


def split(values):
    high = values.astype(BF16)
    rest = values - high.astype(F32)
    middle = rest.astype(BF16)
    low = (rest - middle.astype(F32)).astype(BF16)
    return high, middle, low


def places(cells, sl):
    gx, gy, gz = (lax.axis_index(name) for name in ("gx", "gy", "gz"))
    cut = BZ * lax.axis_size("gz") // 2 - MARGIN
    cell_x = cells[0:1, sl] - (gx * BX - MARGIN)
    cell_y = cells[1:2, sl] - gy * BY
    cell_z = cells[2:3, sl]
    in_x = (cell_x >= 0) & (cell_x < EX)
    in_y = (cell_y >= -MARGIN) & (cell_y < BY + MARGIN)
    row = jnp.where(cell_y < 0, cell_y + EY, cell_y)
    flat = jnp.where(in_x & in_y, cell_x * EY + row, -1)
    row = jnp.where(in_y, row, -1)
    zz = cell_z - cut
    in_strip = in_x & (zz >= 0) & (zz < STRIP)
    strip_lane = jnp.where(in_strip, cell_x * STRIP + zz, -1)
    return flat, cell_z - gz * BZ, row, strip_lane


def hits(count, index):
    return rows((count, index.shape[1])) == index


def product(left, right):
    return lax.dot_general(
        left, right, (((1,), (1,)), ((), ())), preferred_element_type=F32
    )


def inject_points(cells, wave_ref, width, waves, out_ref, strip_out_ref):
    count = len(waves)
    for start in range(0, cells.shape[1], width):
        sl = slice(start, start + width)
        flat, z, row, strip_lane = places(cells, sl)
        here = hits(EX * EY, flat).astype(F32).astype(BF16)
        at_strip = hits(BZ, strip_lane).astype(F32).astype(BF16)
        at_z, at_row = hits(BZ, z), hits(EY, row)
        total = strip_total = None
        parts = [split(wave_ref[wave : wave + 1, sl]) for wave in waves]
        for part in range(3):
            amounts = [parts[wave][part].astype(F32) for wave in range(count)]
            right = jnp.concatenate([jnp.where(at_z, a, 0.0) for a in amounts], 0).astype(BF16)
            left = jnp.concatenate([jnp.where(at_row, a, 0.0) for a in amounts], 0).astype(BF16)
            term, strip_term = product(here, right), product(left, at_strip)
            total = term if part == 0 else total + term
            strip_total = strip_term if part == 0 else strip_total + strip_term
        for wave in range(count):
            value = total[:, wave * BZ : wave * BZ + BZ]
            strip_value = strip_total[wave * EY : wave * EY + EY]
            if start > 0:
                value = value + out_ref[wave]
                strip_value = strip_value + strip_out_ref[wave]
            out_ref[wave] = value
            strip_out_ref[wave] = strip_value


def late_kernel(
    receiver_hbm, receiver_wave_hbm, _, r_ref, rs_ref, receivers, receiver_wave, sem
):
    run([
        pltpu.make_async_copy(receiver_hbm, receivers, sem),
        pltpu.make_async_copy(receiver_wave_hbm, receiver_wave, sem),
    ])
    inject_points(receivers, receiver_wave, 256, (2, 3), r_ref, rs_ref)


def early_kernel(
    receiver_hbm, receiver_wave_hbm, source_hbm, source_wave_hbm, _,
    r_ref, rs_ref, s_ref, ss_ref,
    receivers, receiver_wave, sources, source_wave, sem,
):
    run([
        pltpu.make_async_copy(receiver_hbm, receivers, sem),
        pltpu.make_async_copy(receiver_wave_hbm, receiver_wave, sem),
        pltpu.make_async_copy(source_hbm, sources, sem),
        pltpu.make_async_copy(source_wave_hbm, source_wave, sem),
    ])
    inject_points(receivers, receiver_wave, 256, (0, 1), r_ref, rs_ref)
    inject_points(sources, source_wave, sources.shape[1], (0, 1, 2), s_ref, ss_ref)


def strip_of(packed, block, slot):
    lane = lanes(packed.shape)
    width = BX * STRIP
    shift = (block * width - slot * width) % BZ
    moved = pltpu.roll(packed, shift, 1) if shift else packed
    return jnp.where((lane >= block * width) & (lane < (block + 1) * width), moved, 0.0)


def y_up(v):
    return pltpu.roll(v, EY - 1, 0)


def y_down(v):
    return pltpu.roll(v, 1, 0)


def z_up(v, strip, x):
    edge = pltpu.roll(strip, (BZ - 1 - (x * STRIP + MARGIN)) % BZ, 1)
    return jnp.where(lanes(v.shape) == BZ - 1, edge, pltpu.roll(v, BZ - 1, 1))


def z_down(v, strip, x):
    edge = pltpu.roll(strip, (BZ - (x * STRIP + MARGIN - 1)) % BZ, 1)
    return jnp.where(lanes(v.shape) == 0, edge, pltpu.roll(v, 1, 1))


def strip_flux(values, buoyancy):
    flux_x = buoyancy * (pltpu.roll(values, BZ - STRIP, 1) - values)
    flux_y = buoyancy * (y_up(values) - values)
    flux_z = buoyancy * (pltpu.roll(values, BZ - 1, 1) - values)
    spread = (flux_x - pltpu.roll(flux_x, STRIP, 1)) + (flux_y - y_down(flux_y))
    return flux_z, spread + (flux_z - pltpu.roll(flux_z, 1, 1))


def cut_flags():
    gz, half = lax.axis_index("gz"), lax.axis_size("gz") // 2
    return jnp.where(gz == half - 1, 1.0, 0.0), jnp.where(gz == half, 1.0, 0.0)


def widened(blocks, flags, x, raw_first, tile_firsts):
    block, plane = divmod(x, BX)
    main, tiles = blocks[block]
    tile_first = tile_firsts[block][plane]
    if tile_first is None:
        tile = jnp.zeros((8, BZ), F32)
    else:
        tile = tiles[tile_first : tile_first + 8]
    first = raw_first[block][plane]
    if first is None:
        return jnp.zeros((EY, BZ), F32)
    value = jnp.concatenate([main[first : first + BY], tile], 0)
    return value if block == 1 else value * flags[block]


def series(base, wanted, step):
    result = [None] * BX
    for place, plane in enumerate(wanted):
        result[plane] = base + place * step
    return result


def side_flags():
    gx = lax.axis_index("gx")
    low = jnp.where(gx > 0, 1.0, 0.0)
    high = jnp.where(gx < lax.axis_size("gx") - 1, 1.0, 0.0)
    return low, None, high


def whole_strip(packed, flags, slot):
    parts = [strip_of(packed[block], block, slot) for block in range(3)]
    return parts[1] + parts[0] * flags[0] + parts[2] * flags[2]


def adjoint_kernel(
    raw_low, raw_own, raw_high, low, own, high, adj_hbm, ra_ref, rsa_ref, rb_ref, rsb_ref,
    tissue_hbm,
    out_ref, hist_ref, coef_ref, coef_strip_ref,
    field, tissue, sem, w_sem,
):
    w_copy = pltpu.make_async_copy(adj_hbm.at[pl.ds(1, 3)], out_ref.at[pl.ds(1, 3)], w_sem)
    w_copy.start()
    run([pltpu.make_async_copy(tissue_hbm, tissue, sem)])
    cut_up, cut_down = cut_flags()
    flags = side_flags()
    r_refs = ((ra_ref, 0), (ra_ref, 1), (rb_ref, 0), (rb_ref, 1))
    rs_refs = ((rsa_ref, 0), (rsa_ref, 1), (rsb_ref, 0), (rsb_ref, 1))
    every, lows, highs = range(BX), range(1, BX), range(BX - 1)
    base = WAVE_ROWS
    raws = (raw_low, raw_own, raw_high)
    lates = (low, own, high)

    def initial(index, x):
        tile = 3 * BY + base
        tiles = {
            0: (series(tile, lows, 8), series(PLANES, every, 8), series(tile, highs, 8)),
            1: (
                series(tile + 24, lows[1:], 8),
                series(PLANES + 32, every, 8),
                series(tile + 24, highs[:2], 8),
            ),
            2: (series(tile + 40, lows, 8), series(PLANES + 64, every, 8), series(tile + 40, highs, 8)),
        }[index]
        if index == 1:
            mains = lates
            firsts = (series(base, lows, BY), series(0, every, BY), series(base, highs, BY))
        else:
            mains = raws
            firsts = [series(PLANES * (1 if index == 0 else 2), every, BY)] * 3
        return widened(list(zip(mains, lates)), flags, x, firsts, tiles)

    for x in range(EX):
        for index, values in enumerate(coefficients(initial(2, x), tissue)):
            coef_ref[index, x] = values
    packed = [
        low[base + ADJ_ROWS - EY : base + ADJ_ROWS],
        own[ADJ_OWN_ROWS - EY : ADJ_OWN_ROWS],
        high[base + ADJ_ROWS - EY : base + ADJ_ROWS],
    ]
    q_s, t_s, label_s = (whole_strip(packed, flags, slot) for slot in range(3))
    stiff_s, buoy_s, damp_s = coefficients(label_s, tissue)
    coef_strip_ref[0], coef_strip_ref[1], coef_strip_ref[2] = stiff_s, buoy_s, damp_s
    w_copy.wait()

    for step in range(1, STEPS + 1):
        k = STEPS - step
        rs_ref, place = rs_refs[k]
        q_s = q_s + rs_ref[place]
        u_s = stiff_s * damp_s * q_s
        flux_s, spread = strip_flux(u_s, buoy_s)
        t_s = t_s + spread
        q_s = damp_s * q_s + t_s
        edge_up = u_s * cut_up
        edge_down = flux_s * cut_down

        def injected(x):
            r_ref, place = r_refs[k]
            value = initial(0, x) if step == 1 else field[0, x]
            value = value + r_ref[place, x]
            return value, coef_ref[0, x] * coef_ref[2, x] * value

        flux_below = None
        q_now, u_now = injected(step - 1)
        for x in range(step - 1, EX - step):
            q_next, u_next = injected(x + 1)
            buoyancy = coef_ref[1, x]
            slope_x = u_next - u_now
            flux_x = buoyancy * slope_x
            if x >= step:
                slope_y = y_up(u_now) - u_now
                slope_z = z_up(u_now, edge_up, x) - u_now
                flux_y = buoyancy * slope_y
                flux_z = buoyancy * slope_z
                spread = (flux_x - flux_below) + (flux_y - y_down(flux_y))
                spread = spread + (flux_z - z_down(flux_z, edge_down, x))
                damped = coef_ref[2, x] * q_now
                if BX <= x < 2 * BX:
                    place = x - BX
                    hist_ref[k, 0, place] = damped[0:BY]
                    for index, slope in enumerate((slope_x, slope_y, slope_z)):
                        w = out_ref[1 + index, place] + slope[0:BY]
                        out_ref[1 + index, place] = w
                        hist_ref[k, 1 + index, place] = w
                t = (initial(1, x) if step == 1 else field[1, x]) + spread
                if step < STEPS:
                    field[1, x] = t
                    field[0, x] = damped + t
                else:
                    out_ref[0, x - BX] = (damped + t)[0:BY]
            flux_below = flux_x
            q_now, u_now = q_next, u_next


def forward_kernel(
    raw_low, p_own, raw_high, low, own, high,
    coef_ref, coef_strip_ref, s_ref, ss_ref, hist_ref,
    grad_ref,
    field,
):
    cut_up, cut_down = cut_flags()
    flags = side_flags()
    every, lows, highs = range(BX), range(1, BX), range(BX - 1)
    raws = (raw_low, p_own, raw_high)
    lates = (low, own, high)

    def initial(index, x):
        tile = 3 * BY
        if index == 0:
            tiles = (series(tile, lows, 8), series(PLANES, every, 8), series(tile, highs, 8))
            return widened(list(zip(raws, lates)), flags, x, [series(0, every, BY)] * 3, tiles)
        tiles = (
            series(tile + 24, lows[1:], 8),
            series(PLANES + 32, every, 8),
            series(tile + 24, highs[:2], 8),
        )
        firsts = (series(0, lows, BY), series(0, every, BY), series(0, highs, BY))
        return widened(list(zip(lates, lates)), flags, x, firsts, tiles)

    packed = [
        low[WAVE_ROWS - EY : WAVE_ROWS],
        own[OWN_ROWS - EY : OWN_ROWS],
        high[WAVE_ROWS - EY : WAVE_ROWS],
    ]
    p_s, s_s = (whole_strip(packed, flags, slot) for slot in range(2))
    stiff_s, buoy_s, damp_s = coef_strip_ref[0], coef_strip_ref[1], coef_strip_ref[2]

    for step in range(1, STEPS + 1):
        k = step - 1
        edge_up = p_s * cut_up
        flux_s, spread = strip_flux(p_s, buoy_s)
        edge_down = flux_s * cut_down
        if step < STEPS:
            s_s = s_s - spread
            p_s = damp_s * (p_s - stiff_s * s_s) + ss_ref[k]

        def pressure(x):
            return initial(0, x) if step == 1 else field[0, x]

        flux_below = None
        p_now = pressure(step - 1)
        for x in range(step - 1, EX - step):
            p_next = pressure(x + 1)
            buoyancy = coef_ref[1, x]
            slope_x = p_next - p_now
            flux_x = buoyancy * slope_x
            if x >= step:
                slope_y = y_up(p_now) - p_now
                slope_z = z_up(p_now, edge_up, x) - p_now
                flux_y = buoyancy * slope_y
                flux_z = buoyancy * slope_z
                spread = (flux_x - flux_below) + (flux_y - y_down(flux_y))
                spread = spread + (flux_z - z_down(flux_z, edge_down, x))
                spread = (initial(1, x) if step == 1 else field[1, x]) - spread
                if step < STEPS:
                    field[1, x] = spread
                    field[0, x] = (
                        coef_ref[2, x] * (p_now - coef_ref[0, x] * spread) + s_ref[k, x]
                    )
                if BX <= x < 2 * BX:
                    place = x - BX
                    term = hist_ref[k, 0, place] * spread[0:BY]
                    grad_ref[0, place] = -term if k == 0 else grad_ref[0, place] - term
                    term = hist_ref[k, 1, place] * slope_x[0:BY]
                    term = term + hist_ref[k, 2, place] * slope_y[0:BY]
                    term = term + hist_ref[k, 3, place] * slope_z[0:BY]
                    grad_ref[1, place] = -term if k == 0 else grad_ref[1, place] - term
            flux_below = flux_x
            p_now = p_next


def shape(*dims):
    return jax.ShapeDtypeStruct(dims, F32)


def call(kernel, outs, operands, scratch, places):
    spaces = {"h": pltpu.HBM, "a": pl.ANY, "v": pltpu.VMEM}
    operands = [
        pltpu.with_memory_space_constraint(operand, pltpu.HBM) if place == "h" else operand
        for operand, place in zip(operands, places)
    ]
    return pl.pallas_call(
        kernel,
        out_shape=outs,
        in_specs=[pl.BlockSpec(memory_space=spaces[place]) for place in places],
        out_specs=[pl.BlockSpec(memory_space=pltpu.VMEM)] * len(outs),
        scratch_shapes=scratch,
        compiler_params=pltpu.CompilerParams(vmem_limit_bytes=VMEM_LIMIT),
        cost_estimate=pl.CostEstimate(flops=1 << 24, bytes_accessed=1 << 20, transcendentals=0),
    )(*operands)


def from_sides(array, axes):
    count = lax.axis_size("gy")

    def route(offset):
        pairs = []
        for target in range(count):
            source = target + offset
            if 0 <= source < count:
                if "gz" in axes:
                    pairs += [(2 * source + z, 2 * target + 1 - z) for z in range(2)]
                else:
                    pairs.append((source, target))
        return pairs

    if count == 2:
        both = lax.ppermute(array, axes, route(1) + route(-1))
        return both, both
    return lax.ppermute(array, axes, route(1)), lax.ppermute(array, axes, route(-1))


def rotated(array, axis, offset):
    count = lax.axis_size(axis)
    return lax.ppermute(array, axis, [((i + offset) % count, i) for i in range(count)])


def neighbours(to_next, to_last, cut):
    count = lax.axis_size("gx")
    if count == 4:
        return rotated(to_next, "gx", -1), rotated(to_last, "gx", 1)
    half = count // 2
    return (
        jnp.concatenate(
            [rotated(to_next[:cut], "gx", half + 1), rotated(to_next[cut:], "gx", -1)], 0
        ),
        jnp.concatenate(
            [rotated(to_last[:cut], "gx", half - 1), rotated(to_last[cut:], "gx", 1)], 0
        ),
    )


def local(
    stored, adjoint_end, labels, tissue, source_cells, source_wave, receiver_cells, receiver_wave
):
    assert lax.axis_size("gz") == 2 and labels.shape == (BX, BY, BZ)
    half = lax.axis_size("gx") // 2
    p, raw, s, t, face_x, face_y, face_z = call(
        face_kernel,
        [
            shape(PLANES, BZ),
            shape(3 * PLANES, BZ),
            shape(PLANES, BZ),
            shape(PLANES, BZ),
            shape(2 * BY, BZ),
            shape(8, BZ),
            shape(BY, BZ),
        ],
        [stored, adjoint_end, labels, tissue],
        [
            pltpu.VMEM(stored.shape, F32),
            pltpu.VMEM(adjoint_end.shape, F32),
            pltpu.VMEM(labels.shape, jnp.int32),
            pltpu.SMEM(tissue.shape, F32),
            pltpu.SemaphoreType.DMA,
        ],
        "hhhh",
    )
    receivers, sources = receiver_cells.T, source_cells.T
    point_scratch = [
        pltpu.VMEM(receivers.shape, jnp.int32),
        pltpu.VMEM(receiver_wave.shape, F32),
        pltpu.VMEM(sources.shape, jnp.int32),
        pltpu.VMEM(source_wave.shape, F32),
    ]
    rb, rsb = call(
        late_kernel,
        [shape(2, EX * EY, BZ), shape(2, EY, BZ)],
        [receivers, receiver_wave, face_y],
        point_scratch[:2] + [pltpu.SemaphoreType.DMA],
        "hha",
    )
    face_x = rotated(face_x, "gx", -1)
    face_y = rotated(face_y, "gy", -1)
    face_z = rotated(face_z, "gz", -1)
    p_own = rotated(p, "gx", half)
    raw_prev, raw_next = neighbours(raw, raw, PLANES)
    s, t, edges, corners, strips = call(
        pack_kernel,
        [
            shape(PLANES, BZ),
            shape(PLANES, BZ),
            shape((5 * BX + 2) * 8, BZ),
            shape(16, BZ),
            shape(2 * BY, BZ),
        ],
        [raw, s, t, face_x, face_y, face_z, rsb],
        [],
        "vvvvvva",
    )
    ra, rsa, src, src_strip = call(
        early_kernel,
        [
            shape(2, EX * EY, BZ),
            shape(2, EY, BZ),
            shape(STEPS - 1, EX * EY, BZ),
            shape(STEPS - 1, EY, BZ),
        ],
        [receivers, receiver_wave, sources, source_wave, corners],
        point_scratch + [pltpu.SemaphoreType.DMA],
        "hhhha",
    )
    ra, rb = ra.reshape(2, EX, EY, BZ), rb.reshape(2, EX, EY, BZ)
    src = src.reshape(STEPS - 1, EX, EY, BZ)
    other = rotated(strips, "gz", 1)
    up, down = from_sides(edges, "gy")
    corner_up, corner_down = from_sides(corners, ("gy", "gz"))
    late, adj_own, to_next, to_last = call(
        merge_kernel,
        [
            shape(OWN_ROWS, BZ),
            shape(ADJ_OWN_ROWS, BZ),
            shape(WAVE_ROWS + ADJ_ROWS, BZ),
            shape(WAVE_ROWS + ADJ_ROWS, BZ),
        ],
        [up, down, strips, other, corner_up, corner_down, s, t, rsa, p_own, raw_prev, raw_next],
        [],
        "vvvvvvvvaaaa",
    )
    late_prev, late_next = neighbours(to_next, to_last, WAVE_ROWS)
    late_own = rotated(late, "gx", half)
    adjoint_start, hist, coef, coef_strip = call(
        adjoint_kernel,
        [
            shape(4, BX, BY, BZ),
            shape(STEPS, 4, BX, BY, BZ),
            shape(3, EX, EY, BZ),
            shape(3, EY, BZ),
        ],
        [
            raw_prev, raw, raw_next, late_prev, adj_own, late_next,
            adjoint_end, ra, rsa, rb, rsb, tissue,
        ],
        [
            pltpu.VMEM((2, EX, EY, BZ), F32),
            pltpu.SMEM(tissue.shape, F32),
            pltpu.SemaphoreType.DMA,
            pltpu.SemaphoreType.DMA,
        ],
        "vvvvvvhvvvvh",
    )
    (gradient,) = call(
        forward_kernel,
        [shape(2, BX, BY, BZ)],
        [
            raw_next, p_own, raw_prev, late_next, late_own, late_prev,
            coef, coef_strip, src, src_strip, hist,
        ],
        [pltpu.VMEM((2, EX, EY, BZ), F32)],
        "vvvvvvvvvvv",
    )
    return gradient, adjoint_start


def solution(mesh):
    return jax.shard_map(
        local,
        mesh=mesh,
        in_specs=(
            P("shot", "gx", "gy", "gz"),
            P("shot", "gx", "gy", "gz"),
            P("gx", "gy", "gz"),
            P(),
            P("shot", None),
            P(None, "shot"),
            P(),
            P(None, "shot"),
        ),
        out_specs=(P("shot", "gx", "gy", "gz"), P("shot", "gx", "gy", "gz")),
        check_vma=False,
    )
```

```python
import jax
import jax.numpy as jnp
from jax import lax
from jax.experimental import pallas as pl
from jax.experimental.pallas import tpu as pltpu
from jax.sharding import PartitionSpec as P

STEPS = 4
MARGIN = 4
BX, BY, BZ = 4, 32, 128
EX, EY = BX + 2 * MARGIN, BY + 2 * MARGIN
STRIP = 2 * MARGIN
F32 = jnp.float32
BF16 = jnp.bfloat16
VMEM_LIMIT = 16 * 1024 * 1024
PLANES = BX * BY
WAVE_EDGE_ROWS = 2 * BX * 8 + EY
ADJ_EDGE_ROWS = 3 * BX * 8 + EY
WAVE_ROWS = PLANES + 3 * BY + 5 * 8 + EY
ADJ_ROWS = 2 * PLANES + 3 * BY + 8 * 8 + EY


def lanes(shape):
    return lax.broadcasted_iota(jnp.int32, shape, len(shape) - 1)


def rows(shape):
    return lax.broadcasted_iota(jnp.int32, shape, len(shape) - 2)


def run(copies):
    for copy in copies:
        copy.start()
    for copy in copies:
        copy.wait()


def coefficients(labels, table_ref):
    result = [jnp.zeros(labels.shape, F32) for _ in range(3)]
    for index in range(8):
        picked = labels == float(index + 1)
        for kind in range(3):
            row = kind * 8 + index
            result[kind] = jnp.where(picked, table_ref[row : row + 1], result[kind])
    return result


def buoyancy_of(labels, table_ref):
    result = jnp.zeros(labels.shape, F32)
    for index in range(8):
        result = jnp.where(labels == float(index + 1), table_ref[8 + index : 9 + index], result)
    return result


def face_kernel(
    stored_hbm, adj_hbm, lab_hbm, tissue_hbm, rc_hbm, rw_hbm, sc_hbm, sw_hbm,
    raw_ref, s_ref, t_ref, face_x_ref, face_y_ref, face_z_ref, table_ref,
    rc_ref, rw_ref, sc_ref, sw_ref,
    stored, adj, lab, tissue, sem,
):
    run([
        pltpu.make_async_copy(source, target, sem)
        for source, target in (
            (stored_hbm, stored), (adj_hbm, adj), (lab_hbm, lab), (tissue_hbm, tissue),
            (rc_hbm, rc_ref), (rw_hbm, rw_ref), (sc_hbm, sc_ref), (sw_hbm, sw_ref),
        )
    ])
    for index in range(tissue.shape[1]):
        speed = jnp.full((1, BZ), tissue[0, index], F32)
        density = jnp.full((1, BZ), tissue[1, index], F32)
        table_ref[index : index + 1] = density * speed
        table_ref[8 + index : 9 + index] = speed / density
        table_ref[16 + index : 17 + index] = 1.0 - jnp.full((1, BZ), tissue[2, index], F32)
    lane = lanes((BY, BZ))
    row = rows((BY, BZ))
    tile_row = rows((8, BZ))
    face_y = jnp.zeros((8, BZ), F32)
    face_z = jnp.zeros((BY, BZ), F32)
    previous = [None, None]
    for x in range(BX):
        labels = lab[x].astype(F32) + 1.0
        buoyancy = buoyancy_of(labels, table_ref)
        plane = slice(x * BY, x * BY + BY)
        for index, values in enumerate((stored[0, x], adj[0, x], labels)):
            raw_ref[index * PLANES + x * BY : index * PLANES + x * BY + BY] = values
        for kind, v in enumerate((stored, adj)):
            vx, vy, vz = v[1, x], v[2, x], v[3, x]
            if kind == 1:
                vx, vy, vz = buoyancy * vx, buoyancy * vy, buoyancy * vz
            y_below = pltpu.roll(vy, 1, 0)
            z_below = pltpu.roll(vz, 1, 1)
            index = kind * BX + x
            last = pltpu.roll(vy[BY - 8 : BY], (index + 1) % 8, 0)
            face_y = jnp.where(tile_row == index, last, face_y)
            face_z = jnp.where(lane == index, pltpu.roll(vz, index + 1, 1), face_z)
            spread = vx if x == 0 else vx - previous[kind]
            spread = spread + (vy - jnp.where(row == 0, 0.0, y_below))
            spread = spread + (vz - jnp.where(lane == 0, 0.0, z_below))
            (s_ref, t_ref)[kind][plane] = spread
            previous[kind] = vx
    for kind in range(2):
        face_x_ref[kind * BY : kind * BY + BY] = previous[kind]
    face_y_ref[...] = face_y
    face_z_ref[...] = face_z


def pack_kernel(
    raw_ref, s_in, t_in, face_x, face_y, face_z, _,
    wave_ref, t_ref, edge_ref, corner_ref, strip_ref,
):
    gx, gy, gz = (lax.axis_index(name) for name in ("gx", "gy", "gz"))
    count = lax.axis_size("gx")
    lane = lanes((BY, BZ))
    row = rows((BY, BZ))
    tile_row = rows((8, BZ))
    below = (
        jnp.where(gx == count // 2, 0.0, 1.0),
        jnp.where(gx == 0, 0.0, 1.0),
    )
    tile_y = face_y[...] * jnp.where(gy == 0, 0.0, 1.0)
    tile_z = face_z[...] * jnp.where(gz == 0, 0.0, 1.0)
    strips = [jnp.zeros((BY, BZ), F32) for _ in range(2)]
    for field in range(5):
        group, slot = (0, field) if field < 2 else (1, field - 2)
        for x in range(BX):
            plane = slice(x * BY, x * BY + BY)
            if field in (1, 3):
                kind = field // 2
                block = (s_in, t_in)[kind][plane]
                if x == 0:
                    block = block - face_x[kind * BY : kind * BY + BY] * below[kind]
                index = kind * BX + x
                lane_below = pltpu.roll(tile_z, (BZ - index) % BZ, 1) if index else tile_z
                block = block - jnp.where(row == 0, tile_y[index : index + 1], 0.0)
                block = block - jnp.where(lane == 0, lane_below, 0.0)
                if kind == 0:
                    wave_ref[PLANES + x * BY : PLANES + x * BY + BY] = block
                else:
                    t_ref[plane] = block
            else:
                first = field // 2 * PLANES + x * BY
                block = raw_ref[first : first + BY]
                if field == 0:
                    wave_ref[plane] = block
            tile = jnp.where(tile_row < MARGIN, block[0:8], block[BY - 8 : BY])
            index = field * BX + x
            edge_ref[index * 8 : index * 8 + 8] = tile
            base = slot * BX * STRIP + x * STRIP
            rolled = pltpu.roll(block, base + MARGIN, 1)
            first = base + MARGIN * gz
            strips[group] = jnp.where(
                (lane >= first) & (lane < first + MARGIN), rolled, strips[group]
            )
    for group in range(2):
        strip = strips[group]
        strip_ref[group * BY : group * BY + BY] = strip
        tile = jnp.where(tile_row < MARGIN, strip[0:8], strip[BY - 8 : BY])
        index = 5 * BX + group
        edge_ref[index * 8 : index * 8 + 8] = tile
        corner_ref[group * 8 : group * 8 + 8] = tile


def copy_rows(target, base, source, first, count):
    target[base : base + count] = source[pl.ds(pl.multiple_of(first, 8), count)]
    return base + count


def pair_planes():
    parity = lax.rem(lax.axis_index("gx"), 2)
    return 1 - parity, parity


def merge_kernel(
    up_ref, down_ref, strip_ref, other_ref, corner_up_ref, corner_down_ref, raw_ref, t_ref, _,
    wave_edge_ref, adj_edge_ref, even_ref, odd_ref,
):
    gy = lax.axis_index("gy")
    row = rows((8, BZ))
    take_up = (row < MARGIN) & (gy < lax.axis_size("gy") - 1)
    take_down = (row >= MARGIN) & (gy > 0)

    def halo(up, down, index):
        sl = slice(index * 8, index * 8 + 8)
        return jnp.where(take_up, up[sl], jnp.where(take_down, down[sl], 0.0))

    for index in range(5 * BX):
        target, place = (wave_edge_ref, index) if index < 8 else (adj_edge_ref, index - 8)
        target[place * 8 : place * 8 + 8] = halo(up_ref, down_ref, index)
    for group, target in enumerate((wave_edge_ref, adj_edge_ref)):
        base = target.shape[0] - EY
        sl = slice(group * BY, group * BY + BY)
        target[base : base + BY] = strip_ref[sl] + other_ref[sl]
        tile = halo(up_ref, down_ref, 5 * BX + group) + halo(corner_up_ref, corner_down_ref, group)
        target[base + BY : base + EY] = tile
    for target, first in zip((even_ref, odd_ref), pair_planes()):
        base = copy_rows(target, 0, raw_ref, PLANES, 2 * PLANES)
        base = copy_rows(target, base, t_ref, first * BY, 3 * BY)
        base = copy_rows(target, base, adj_edge_ref, first * 8, 24)
        base = copy_rows(target, base, adj_edge_ref, 32 + first * 16, 16)
        base = copy_rows(target, base, adj_edge_ref, 64 + first * 8, 24)
        copy_rows(target, base, adj_edge_ref, ADJ_EDGE_ROWS - EY, EY)


def join_kernel(wave_ref, edge_ref, even_ref, odd_ref):
    for target, first in zip((even_ref, odd_ref), pair_planes()):
        base = copy_rows(target, 0, wave_ref, 0, PLANES)
        base = copy_rows(target, base, wave_ref, PLANES + first * BY, 3 * BY)
        base = copy_rows(target, base, edge_ref, first * 8, 24)
        base = copy_rows(target, base, edge_ref, 32 + first * 16, 16)
        copy_rows(target, base, edge_ref, WAVE_EDGE_ROWS - EY, EY)


def split(values):
    high = values.astype(BF16)
    rest = values - high.astype(F32)
    middle = rest.astype(BF16)
    low = (rest - middle.astype(F32)).astype(BF16)
    return high, middle, low


def places(cells, sl):
    gx, gy, gz = (lax.axis_index(name) for name in ("gx", "gy", "gz"))
    cut = BZ * lax.axis_size("gz") // 2 - MARGIN
    cell_x = cells[0:1, sl] - (gx * BX - MARGIN)
    cell_y = cells[1:2, sl] - gy * BY
    cell_z = cells[2:3, sl]
    in_x = (cell_x >= 0) & (cell_x < EX)
    in_y = (cell_y >= -MARGIN) & (cell_y < BY + MARGIN)
    row = jnp.where(cell_y < 0, cell_y + EY, cell_y)
    flat = jnp.where(in_x & in_y, cell_x * EY + row, -1)
    row = jnp.where(in_y, row, -1)
    zz = cell_z - cut
    in_strip = in_x & (zz >= 0) & (zz < STRIP)
    strip_lane = jnp.where(in_strip, cell_x * STRIP + zz, -1)
    return flat, cell_z - gz * BZ, row, strip_lane


def hits(count, index):
    return rows((count, index.shape[1])) == index


def product(left, right):
    return lax.dot_general(
        left, right, (((1,), (1,)), ((), ())), preferred_element_type=F32
    )


def inject_points(cells, wave_ref, width, waves, planes, out_ref, strip_out_ref):
    count, low, total_rows = len(waves), planes[0] * EY, (planes[1] - planes[0]) * EY
    for start in range(0, cells.shape[1], width):
        sl = slice(start, start + width)
        flat, z, row, strip_lane = places(cells, sl)
        here = hits(total_rows, flat - low).astype(F32).astype(BF16)
        at_strip = hits(BZ, strip_lane).astype(F32).astype(BF16)
        at_z, at_row = hits(BZ, z), hits(EY, row)
        total = strip_total = None
        parts = [split(wave_ref[wave : wave + 1, sl]) for wave in waves]
        for part in range(3):
            amounts = [parts[wave][part].astype(F32) for wave in range(count)]
            right = jnp.concatenate([jnp.where(at_z, a, 0.0) for a in amounts], 0).astype(BF16)
            left = jnp.concatenate([jnp.where(at_row, a, 0.0) for a in amounts], 0).astype(BF16)
            term, strip_term = product(here, right), product(left, at_strip)
            total = term if part == 0 else total + term
            strip_total = strip_term if part == 0 else strip_total + strip_term
        for wave in range(count):
            value = total[:, wave * BZ : wave * BZ + BZ]
            strip_value = strip_total[wave * EY : wave * EY + EY]
            if start > 0:
                value = value + out_ref[wave]
                strip_value = strip_value + strip_out_ref[wave]
            out_ref[wave] = value
            strip_out_ref[wave] = strip_value


LATE_PLANES, EARLY_PLANES, SOURCE_PLANES = (0, EX), (2, EX - 2), (1, EX - 1)


def late_kernel(receivers, receiver_wave, r_ref, rs_ref):
    inject_points(receivers, receiver_wave, 256, (2, 3), LATE_PLANES, r_ref, rs_ref)


def early_kernel(
    receivers, receiver_wave, sources, source_wave, _, r_ref, rs_ref, s_ref, ss_ref
):
    inject_points(receivers, receiver_wave, 256, (0, 1), EARLY_PLANES, r_ref, rs_ref)
    width = sources.shape[1]
    inject_points(sources, source_wave, width, (0, 1, 2), SOURCE_PLANES, s_ref, ss_ref)


def strip_of(packed, block, slot):
    lane = lanes(packed.shape)
    width = BX * STRIP
    shift = (block * width - slot * width) % BZ
    moved = pltpu.roll(packed, shift, 1) if shift else packed
    return jnp.where((lane >= block * width) & (lane < (block + 1) * width), moved, 0.0)


def y_up(v):
    return pltpu.roll(v, EY - 1, 0)


def y_down(v):
    return pltpu.roll(v, 1, 0)


def z_up(v, strip, x):
    edge = pltpu.roll(strip, (BZ - 1 - (x * STRIP + MARGIN)) % BZ, 1)
    return jnp.where(lanes(v.shape) == BZ - 1, edge, pltpu.roll(v, BZ - 1, 1))


def z_down(v, strip, x):
    edge = pltpu.roll(strip, (BZ - (x * STRIP + MARGIN - 1)) % BZ, 1)
    return jnp.where(lanes(v.shape) == 0, edge, pltpu.roll(v, 1, 1))


def strip_flux(values, buoyancy):
    flux_x = buoyancy * (pltpu.roll(values, BZ - STRIP, 1) - values)
    flux_y = buoyancy * (y_up(values) - values)
    flux_z = buoyancy * (pltpu.roll(values, BZ - 1, 1) - values)
    spread = (flux_x - pltpu.roll(flux_x, STRIP, 1)) + (flux_y - y_down(flux_y))
    return flux_z, spread + (flux_z - pltpu.roll(flux_z, 1, 1))


def cut_flags():
    gz, half = lax.axis_index("gz"), lax.axis_size("gz") // 2
    return jnp.where(gz == half - 1, 1.0, 0.0), jnp.where(gz == half, 1.0, 0.0)


def sides():
    gx = lax.axis_index("gx")
    low = jnp.where(gx > 0, 1.0, 0.0)
    high = jnp.where(gx < lax.axis_size("gx") - 1, 1.0, 0.0)
    return low, high, lax.rem(gx, 2) == 0


def from_side(messages, first, count, block, side):
    even, odd = (message[first : first + count] for message in messages)
    low, high, even_above = side
    if block == 0:
        return jnp.where(even_above, odd, even) * low
    return jnp.where(even_above, even, odd) * high


def side_rows(base, wanted, step, block):
    planes = range(BX - wanted, BX) if block == 0 else range(wanted)
    return {plane: base + place * step for place, plane in enumerate(planes)}


def widened(own, own_tiles, messages, x, layout, side):
    block, plane = divmod(x, BX)
    if block == 1:
        main = own[0][own[1] + plane * BY : own[1] + plane * BY + BY]
        tile = own_tiles[0][own_tiles[1] + plane * 8 : own_tiles[1] + plane * 8 + 8]
        return jnp.concatenate([main, tile], 0)
    parts = []
    for (base, wanted), count in zip(layout, (BY, 8)):
        first = side_rows(base, wanted, count, block).get(plane)
        if first is None:
            parts.append(jnp.zeros((count, BZ), F32))
        else:
            parts.append(from_side(messages, first, count, block, side))
    return jnp.concatenate(parts, 0)


def whole_strip(own, messages, first, slot, side):
    low = from_side(messages, first, EY, 0, side)
    high = from_side(messages, first, EY, 2, side)
    return strip_of(low, 0, slot) + strip_of(own, 1, slot) + strip_of(high, 2, slot)


def adjoint_kernel(
    raw_ref, t_ref, edge_ref, even, odd, adj_hbm, ra_ref, rsa_ref, rb_ref, rsb_ref, table_ref,
    out_ref, hist_ref, coef_ref, coef_strip_ref,
    field, w_sem,
):
    w_copy = pltpu.make_async_copy(adj_hbm.at[pl.ds(1, 3)], out_ref.at[pl.ds(1, 3)], w_sem)
    w_copy.start()
    cut_up, cut_down = cut_flags()
    side = sides()
    messages = (even, odd)
    r_refs = ((ra_ref, 0), (ra_ref, 1), (rb_ref, 0), (rb_ref, 1))
    rs_refs = ((rsa_ref, 0), (rsa_ref, 1), (rsb_ref, 0), (rsb_ref, 1))
    tiles = 2 * PLANES + 3 * BY

    def initial(index, x):
        own = ((raw_ref, PLANES), (t_ref, 0), (raw_ref, 2 * PLANES))[index]
        layout = (
            ((0, 4), (tiles, 3)),
            ((2 * PLANES, 3), (tiles + 24, 2)),
            ((PLANES, 4), (tiles + 40, 3)),
        )[index]
        return widened(own, (edge_ref, 32 * index), messages, x, layout, side)

    for x in range(EX):
        stiff, buoy, damp = coefficients(initial(2, x), table_ref)
        coef_ref[0, x], coef_ref[1, x], coef_ref[2, x] = stiff, buoy, damp
    own_strip = edge_ref[ADJ_EDGE_ROWS - EY : ADJ_EDGE_ROWS]
    q_s, t_s, label_s = (
        whole_strip(own_strip, messages, ADJ_ROWS - EY, slot, side) for slot in range(3)
    )
    stiff_s, buoy_s, damp_s = coefficients(label_s, table_ref)
    coef_strip_ref[0], coef_strip_ref[1], coef_strip_ref[2] = stiff_s, buoy_s, damp_s
    w_copy.wait()

    for step in range(1, STEPS + 1):
        k = STEPS - step
        rs_ref, place = rs_refs[k]
        q_s = q_s + rs_ref[place]
        u_s = stiff_s * damp_s * q_s
        flux_s, spread = strip_flux(u_s, buoy_s)
        t_s = t_s + spread
        q_s = damp_s * q_s + t_s
        edge_up = u_s * cut_up
        edge_down = flux_s * cut_down

        def injected(x):
            r_ref, place = r_refs[k]
            value = initial(0, x) if step == 1 else field[0, x]
            value = value + r_ref[place, x - (EARLY_PLANES if k < 2 else LATE_PLANES)[0]]
            return value, coef_ref[0, x] * coef_ref[2, x] * value

        flux_below = None
        q_now, u_now = injected(step - 1)
        for x in range(step - 1, EX - step):
            q_next, u_next = injected(x + 1)
            buoyancy = coef_ref[1, x]
            slope_x = u_next - u_now
            flux_x = buoyancy * slope_x
            if x >= step:
                slope_y = y_up(u_now) - u_now
                slope_z = z_up(u_now, edge_up, x) - u_now
                flux_y = buoyancy * slope_y
                flux_z = buoyancy * slope_z
                spread = (flux_x - flux_below) + (flux_y - y_down(flux_y))
                spread = spread + (flux_z - z_down(flux_z, edge_down, x))
                damped = coef_ref[2, x] * q_now
                if BX <= x < 2 * BX:
                    place = x - BX
                    hist_ref[k, 0, place] = damped[0:BY]
                    for index, slope in enumerate((slope_x, slope_y, slope_z)):
                        w = out_ref[1 + index, place] + slope[0:BY]
                        out_ref[1 + index, place] = w
                        hist_ref[k, 1 + index, place] = w
                t = (initial(1, x) if step == 1 else field[1, x]) + spread
                if step < STEPS:
                    field[1, x] = t
                    field[0, x] = damped + t
                else:
                    out_ref[0, x - BX] = (damped + t)[0:BY]
            flux_below = flux_x
            q_now, u_now = q_next, u_next


def forward_kernel(
    wave_ref, edge_ref, even, odd, coef_ref, coef_strip_ref, s_ref, ss_ref, hist_ref,
    grad_ref,
    field,
):
    cut_up, cut_down = cut_flags()
    side = sides()
    messages = (even, odd)
    tiles = PLANES + 3 * BY

    def initial(index, x):
        layout = (((0, 4), (tiles, 3)), ((PLANES, 3), (tiles + 24, 2)))[index]
        own = (wave_ref, PLANES * index)
        return widened(own, (edge_ref, 32 * index), messages, x, layout, side)

    own_strip = edge_ref[WAVE_EDGE_ROWS - EY : WAVE_EDGE_ROWS]
    p_s, s_s = (
        whole_strip(own_strip, messages, WAVE_ROWS - EY, slot, side) for slot in range(2)
    )
    stiff_s, buoy_s, damp_s = coef_strip_ref[0], coef_strip_ref[1], coef_strip_ref[2]

    for step in range(1, STEPS + 1):
        k = step - 1
        edge_up = p_s * cut_up
        flux_s, spread = strip_flux(p_s, buoy_s)
        edge_down = flux_s * cut_down
        if step < STEPS:
            s_s = s_s - spread
            p_s = damp_s * (p_s - stiff_s * s_s) + ss_ref[k]

        def pressure(x):
            return initial(0, x) if step == 1 else field[0, x]

        flux_below = None
        p_now = pressure(step - 1)
        for x in range(step - 1, EX - step):
            p_next = pressure(x + 1)
            buoyancy = coef_ref[1, x]
            slope_x = p_next - p_now
            flux_x = buoyancy * slope_x
            if x >= step:
                slope_y = y_up(p_now) - p_now
                slope_z = z_up(p_now, edge_up, x) - p_now
                flux_y = buoyancy * slope_y
                flux_z = buoyancy * slope_z
                spread = (flux_x - flux_below) + (flux_y - y_down(flux_y))
                spread = spread + (flux_z - z_down(flux_z, edge_down, x))
                spread = (initial(1, x) if step == 1 else field[1, x]) - spread
                if step < STEPS:
                    field[1, x] = spread
                    field[0, x] = (
                        coef_ref[2, x] * (p_now - coef_ref[0, x] * spread)
                        + s_ref[k, x - SOURCE_PLANES[0]]
                    )
                if BX <= x < 2 * BX:
                    place = x - BX
                    term = hist_ref[k, 0, place] * spread[0:BY]
                    grad_ref[0, place] = -term if k == 0 else grad_ref[0, place] - term
                    term = hist_ref[k, 1, place] * slope_x[0:BY]
                    term = term + hist_ref[k, 2, place] * slope_y[0:BY]
                    term = term + hist_ref[k, 3, place] * slope_z[0:BY]
                    grad_ref[1, place] = -term if k == 0 else grad_ref[1, place] - term
            flux_below = flux_x
            p_now = p_next


def shape(*dims):
    return jax.ShapeDtypeStruct(dims, F32)


def call(kernel, outs, operands, scratch, places):
    spaces = {"h": pltpu.HBM, "a": pl.ANY, "v": pltpu.VMEM}
    operands = [
        pltpu.with_memory_space_constraint(operand, pltpu.HBM) if place == "h" else operand
        for operand, place in zip(operands, places)
    ]
    return pl.pallas_call(
        kernel,
        out_shape=outs,
        in_specs=[pl.BlockSpec(memory_space=spaces[place]) for place in places],
        out_specs=[pl.BlockSpec(memory_space=pltpu.VMEM)] * len(outs),
        scratch_shapes=scratch,
        compiler_params=pltpu.CompilerParams(vmem_limit_bytes=VMEM_LIMIT),
        cost_estimate=pl.CostEstimate(flops=1 << 24, bytes_accessed=1 << 20, transcendentals=0),
    )(*operands)


def from_sides(array, axes):
    count = lax.axis_size("gy")

    def route(offset):
        pairs = []
        for target in range(count):
            source = target + offset
            if 0 <= source < count:
                if "gz" in axes:
                    pairs += [(2 * source + z, 2 * target + 1 - z) for z in range(2)]
                else:
                    pairs.append((source, target))
        return pairs

    if count == 2:
        both = lax.ppermute(array, axes, route(1) + route(-1))
        return both, both
    return lax.ppermute(array, axes, route(1)), lax.ppermute(array, axes, route(-1))


def rotated(array, axis, offset):
    count = lax.axis_size(axis)
    return lax.ppermute(array, axis, [((i + offset) % count, i) for i in range(count)])


def paired(array, odd):
    count = lax.axis_size("gx")
    pairs = []
    for i in range(count):
        partner = ((i - 1) ^ 1) + 1 if odd else i ^ 1
        pairs.append((partner if 0 <= partner < count else i, i))
    return lax.ppermute(array, "gx", pairs)


def local(
    stored, adjoint_end, labels, tissue, source_cells, source_wave, receiver_cells, receiver_wave
):
    assert lax.axis_size("gz") == 2 and labels.shape == (BX, BY, BZ) and tissue.shape[1] == 8
    half = lax.axis_size("gx") // 2
    arguments = [
        stored, adjoint_end, labels, tissue,
        receiver_cells.T, receiver_wave, source_cells.T, source_wave,
    ]
    raw, s, t, face_x, face_y, face_z, table, receivers, receiver_wave, sources, source_wave = call(
        face_kernel,
        [
            shape(3 * PLANES, BZ),
            shape(PLANES, BZ),
            shape(PLANES, BZ),
            shape(2 * BY, BZ),
            shape(8, BZ),
            shape(BY, BZ),
            shape(24, BZ),
        ]
        + [jax.ShapeDtypeStruct(array.shape, array.dtype) for array in arguments[4:]],
        arguments,
        [
            pltpu.VMEM(stored.shape, F32),
            pltpu.VMEM(adjoint_end.shape, F32),
            pltpu.VMEM(labels.shape, jnp.int32),
            pltpu.SMEM(tissue.shape, F32),
            pltpu.SemaphoreType.DMA,
        ],
        "hhhhhhhh",
    )
    rb, rsb = call(
        late_kernel,
        [shape(2, EX * EY, BZ), shape(2, EY, BZ)],
        [receivers, receiver_wave],
        [],
        "vv",
    )
    face_x = rotated(face_x, "gx", -1)
    face_y = rotated(face_y, "gy", -1)
    face_z = rotated(face_z, "gz", -1)
    wave, t, edges, corners, strips = call(
        pack_kernel,
        [
            shape(2 * PLANES, BZ),
            shape(PLANES, BZ),
            shape((5 * BX + 2) * 8, BZ),
            shape(16, BZ),
            shape(2 * BY, BZ),
        ],
        [raw, s, t, face_x, face_y, face_z, rsb],
        [],
        "vvvvvva",
    )
    wave = rotated(wave, "gx", half)
    early_planes, source_planes = (last - first for first, last in (EARLY_PLANES, SOURCE_PLANES))
    ra, rsa, src, src_strip = call(
        early_kernel,
        [
            shape(2, early_planes * EY, BZ),
            shape(2, EY, BZ),
            shape(STEPS - 1, source_planes * EY, BZ),
            shape(STEPS - 1, EY, BZ),
        ],
        [receivers, receiver_wave, sources, source_wave, corners],
        [],
        "vvvva",
    )
    ra, rb = ra.reshape(2, early_planes, EY, BZ), rb.reshape(2, EX, EY, BZ)
    src = src.reshape(STEPS - 1, source_planes, EY, BZ)
    other = rotated(strips, "gz", 1)
    up, down = from_sides(edges, "gy")
    corner_up, corner_down = from_sides(corners, ("gy", "gz"))
    wave_edge, adj_edge, even, odd = call(
        merge_kernel,
        [
            shape(WAVE_EDGE_ROWS, BZ),
            shape(ADJ_EDGE_ROWS, BZ),
            shape(ADJ_ROWS, BZ),
            shape(ADJ_ROWS, BZ),
        ],
        [up, down, strips, other, corner_up, corner_down, raw, t, rsa],
        [],
        "vvvvvvvva",
    )
    wave_edge = rotated(wave_edge, "gx", half)
    even, odd = paired(even, False), paired(odd, True)
    wave_even, wave_odd = call(
        join_kernel,
        [shape(WAVE_ROWS, BZ), shape(WAVE_ROWS, BZ)],
        [wave, wave_edge],
        [],
        "vv",
    )
    wave_even, wave_odd = paired(wave_even, False), paired(wave_odd, True)
    adjoint_start, hist, coef, coef_strip = call(
        adjoint_kernel,
        [
            shape(4, BX, BY, BZ),
            shape(STEPS, 4, BX, BY, BZ),
            shape(3, EX, EY, BZ),
            shape(3, EY, BZ),
        ],
        [raw, t, adj_edge, even, odd, adjoint_end, ra, rsa, rb, rsb, table],
        [pltpu.VMEM((2, EX, EY, BZ), F32), pltpu.SemaphoreType.DMA],
        "vvvvvhvvvvv",
    )
    (gradient,) = call(
        forward_kernel,
        [shape(2, BX, BY, BZ)],
        [wave, wave_edge, wave_even, wave_odd, coef, coef_strip, src, src_strip, hist],
        [pltpu.VMEM((2, EX, EY, BZ), F32)],
        "vvvvvvvvv",
    )
    return gradient, adjoint_start


def solution(mesh):
    return jax.shard_map(
        local,
        mesh=mesh,
        in_specs=(
            P("shot", "gx", "gy", "gz"),
            P("shot", "gx", "gy", "gz"),
            P("gx", "gy", "gz"),
            P(),
            P("shot", None),
            P(None, "shot"),
            P(),
            P(None, "shot"),
        ),
        out_specs=(P("shot", "gx", "gy", "gz"), P("shot", "gx", "gy", "gz")),
        check_vma=False,
    )
```

```python
import jax
import jax.numpy as jnp
from jax import lax
from jax.experimental import pallas as pl
from jax.experimental.pallas import tpu as pltpu
from jax.sharding import PartitionSpec as P

STEPS = 4
MARGIN = 4
BX, BY, BZ = 4, 32, 128
EX, EY = BX + 2 * MARGIN, BY + 2 * MARGIN
STRIP = 2 * MARGIN
F32 = jnp.float32
BF16 = jnp.bfloat16
VMEM_LIMIT = 16 * 1024 * 1024
PLANES = BX * BY
WAVE_EDGE_ROWS = 2 * BX * 8 + EY
ADJ_EDGE_ROWS = 3 * BX * 8 + EY
WAVE_ROWS = PLANES + 3 * BY + 5 * 8 + EY
ADJ_ROWS = 2 * PLANES + 3 * BY + 8 * 8 + EY


def lanes(shape):
    return lax.broadcasted_iota(jnp.int32, shape, len(shape) - 1)


def rows(shape):
    return lax.broadcasted_iota(jnp.int32, shape, len(shape) - 2)


def run(copies):
    for copy in copies:
        copy.start()
    for copy in copies:
        copy.wait()


def coefficients(labels, table_ref):
    result = [jnp.zeros(labels.shape, F32) for _ in range(3)]
    for index in range(8):
        picked = labels == float(index + 1)
        for kind in range(3):
            row = kind * 8 + index
            result[kind] = jnp.where(picked, table_ref[row : row + 1], result[kind])
    return result


def buoyancy_of(labels, table_ref):
    result = jnp.zeros(labels.shape, F32)
    for index in range(8):
        result = jnp.where(labels == float(index + 1), table_ref[8 + index : 9 + index], result)
    return result


def face_kernel(
    stored_hbm, adj_hbm, lab_hbm, tissue_hbm, rc_hbm, rw_hbm, sc_hbm, sw_hbm,
    raw_ref, s_ref, t_ref, face_x_ref, face_y_ref, face_z_ref, table_ref,
    rc_ref, rw_ref, sc_ref, sw_ref,
    stored, adj, lab, tissue, sem,
):
    run([
        pltpu.make_async_copy(source, target, sem)
        for source, target in (
            (stored_hbm, stored), (adj_hbm, adj), (lab_hbm, lab), (tissue_hbm, tissue),
            (rc_hbm, rc_ref), (rw_hbm, rw_ref), (sc_hbm, sc_ref), (sw_hbm, sw_ref),
        )
    ])
    for index in range(tissue.shape[1]):
        speed = jnp.full((1, BZ), tissue[0, index], F32)
        density = jnp.full((1, BZ), tissue[1, index], F32)
        table_ref[index : index + 1] = density * speed
        table_ref[8 + index : 9 + index] = speed / density
        table_ref[16 + index : 17 + index] = 1.0 - jnp.full((1, BZ), tissue[2, index], F32)
    lane = lanes((BY, BZ))
    row = rows((BY, BZ))
    tile_row = rows((8, BZ))
    face_y = jnp.zeros((8, BZ), F32)
    face_z = jnp.zeros((BY, BZ), F32)
    previous = [None, None]
    for x in range(BX):
        labels = lab[x].astype(F32) + 1.0
        buoyancy = buoyancy_of(labels, table_ref)
        plane = slice(x * BY, x * BY + BY)
        for index, values in enumerate((stored[0, x], adj[0, x], labels)):
            raw_ref[index * PLANES + x * BY : index * PLANES + x * BY + BY] = values
        for kind, v in enumerate((stored, adj)):
            vx, vy, vz = v[1, x], v[2, x], v[3, x]
            if kind == 1:
                vx, vy, vz = buoyancy * vx, buoyancy * vy, buoyancy * vz
            y_below = pltpu.roll(vy, 1, 0)
            z_below = pltpu.roll(vz, 1, 1)
            index = kind * BX + x
            last = pltpu.roll(vy[BY - 8 : BY], (index + 1) % 8, 0)
            face_y = jnp.where(tile_row == index, last, face_y)
            face_z = jnp.where(lane == index, pltpu.roll(vz, index + 1, 1), face_z)
            spread = vx if x == 0 else vx - previous[kind]
            spread = spread + (vy - jnp.where(row == 0, 0.0, y_below))
            spread = spread + (vz - jnp.where(lane == 0, 0.0, z_below))
            (s_ref, t_ref)[kind][plane] = spread
            previous[kind] = vx
    for kind in range(2):
        face_x_ref[kind * BY : kind * BY + BY] = previous[kind]
    face_y_ref[...] = face_y
    face_z_ref[...] = face_z


def fix_kernel(raw_ref, s_in, t_in, face_x, face_y, face_z, _, wave_ref, t_ref):
    gx, gy, gz = (lax.axis_index(name) for name in ("gx", "gy", "gz"))
    lane = lanes((BY, BZ))
    row = rows((BY, BZ))
    below = (
        jnp.where(gx == lax.axis_size("gx") // 2, 0.0, 1.0),
        jnp.where(gx == 0, 0.0, 1.0),
    )
    tile_y = face_y[...] * jnp.where(gy == 0, 0.0, 1.0)
    tile_z = face_z[...] * jnp.where(gz == 0, 0.0, 1.0)
    wave_ref[0:PLANES] = raw_ref[0:PLANES]
    for kind, (source, target, base) in enumerate(((s_in, wave_ref, PLANES), (t_in, t_ref, 0))):
        for x in range(BX):
            block = source[x * BY : x * BY + BY]
            if x == 0:
                block = block - face_x[kind * BY : kind * BY + BY] * below[kind]
            index = kind * BX + x
            lane_below = pltpu.roll(tile_z, (BZ - index) % BZ, 1) if index else tile_z
            block = block - jnp.where(row == 0, tile_y[index : index + 1], 0.0)
            block = block - jnp.where(lane == 0, lane_below, 0.0)
            target[base + x * BY : base + x * BY + BY] = block


def edge_kernel(raw_ref, wave_ref, t_ref, edge_ref, corner_ref, strip_ref):
    gz = lax.axis_index("gz")
    lane = lanes((BY, BZ))
    tile_row = rows((8, BZ))
    strips = [jnp.zeros((BY, BZ), F32) for _ in range(2)]
    sources = (
        (wave_ref, 0), (wave_ref, PLANES), (raw_ref, PLANES), (t_ref, 0), (raw_ref, 2 * PLANES)
    )
    for field, (source, first_row) in enumerate(sources):
        group, slot = (0, field) if field < 2 else (1, field - 2)
        for x in range(BX):
            block = source[first_row + x * BY : first_row + x * BY + BY]
            tile = jnp.where(tile_row < MARGIN, block[0:8], block[BY - 8 : BY])
            index = field * BX + x
            edge_ref[index * 8 : index * 8 + 8] = tile
            base = slot * BX * STRIP + x * STRIP
            rolled = pltpu.roll(block, base + MARGIN, 1)
            first = base + MARGIN * gz
            strips[group] = jnp.where(
                (lane >= first) & (lane < first + MARGIN), rolled, strips[group]
            )
    for group in range(2):
        strip = strips[group]
        strip_ref[group * BY : group * BY + BY] = strip
        tile = jnp.where(tile_row < MARGIN, strip[0:8], strip[BY - 8 : BY])
        index = 5 * BX + group
        edge_ref[index * 8 : index * 8 + 8] = tile
        corner_ref[group * 8 : group * 8 + 8] = tile


def copy_rows(target, base, source, first, count):
    target[base : base + count] = source[pl.ds(pl.multiple_of(first, 8), count)]
    return base + count


def pair_planes():
    parity = lax.rem(lax.axis_index("gx"), 2)
    return 1 - parity, parity


def merge_kernel(
    up_ref, down_ref, strip_ref, other_ref, corner_up_ref, corner_down_ref, _a, _b,
    wave_edge_ref, adj_edge_ref,
):
    gy = lax.axis_index("gy")
    row = rows((8, BZ))
    take_up = (row < MARGIN) & (gy < lax.axis_size("gy") - 1)
    take_down = (row >= MARGIN) & (gy > 0)

    def halo(up, down, index):
        sl = slice(index * 8, index * 8 + 8)
        return jnp.where(take_up, up[sl], jnp.where(take_down, down[sl], 0.0))

    for index in range(5 * BX):
        target, place = (wave_edge_ref, index) if index < 8 else (adj_edge_ref, index - 8)
        target[place * 8 : place * 8 + 8] = halo(up_ref, down_ref, index)
    for group, target in enumerate((wave_edge_ref, adj_edge_ref)):
        base = target.shape[0] - EY
        sl = slice(group * BY, group * BY + BY)
        target[base : base + BY] = strip_ref[sl] + other_ref[sl]
        tile = halo(up_ref, down_ref, 5 * BX + group) + halo(corner_up_ref, corner_down_ref, group)
        target[base + BY : base + EY] = tile


def adjoint_join_kernel(raw_ref, t_ref, adj_edge_ref, _, even_ref, odd_ref):
    for target, first in zip((even_ref, odd_ref), pair_planes()):
        base = copy_rows(target, 0, raw_ref, PLANES, 2 * PLANES)
        base = copy_rows(target, base, t_ref, first * BY, 3 * BY)
        base = copy_rows(target, base, adj_edge_ref, first * 8, 24)
        base = copy_rows(target, base, adj_edge_ref, 32 + first * 16, 16)
        base = copy_rows(target, base, adj_edge_ref, 64 + first * 8, 24)
        copy_rows(target, base, adj_edge_ref, ADJ_EDGE_ROWS - EY, EY)


def join_kernel(wave_ref, edge_ref, even_ref, odd_ref):
    for target, first in zip((even_ref, odd_ref), pair_planes()):
        base = copy_rows(target, 0, wave_ref, 0, PLANES)
        base = copy_rows(target, base, wave_ref, PLANES + first * BY, 3 * BY)
        base = copy_rows(target, base, edge_ref, first * 8, 24)
        base = copy_rows(target, base, edge_ref, 32 + first * 16, 16)
        copy_rows(target, base, edge_ref, WAVE_EDGE_ROWS - EY, EY)


def split(values):
    high = values.astype(BF16)
    rest = values - high.astype(F32)
    middle = rest.astype(BF16)
    low = (rest - middle.astype(F32)).astype(BF16)
    return high, middle, low


def places(cells, sl):
    gx, gy, gz = (lax.axis_index(name) for name in ("gx", "gy", "gz"))
    cut = BZ * lax.axis_size("gz") // 2 - MARGIN
    cell_x = cells[0:1, sl] - (gx * BX - MARGIN)
    cell_y = cells[1:2, sl] - gy * BY
    cell_z = cells[2:3, sl]
    in_x = (cell_x >= 0) & (cell_x < EX)
    in_y = (cell_y >= -MARGIN) & (cell_y < BY + MARGIN)
    row = jnp.where(cell_y < 0, cell_y + EY, cell_y)
    flat = jnp.where(in_x & in_y, cell_x * EY + row, -1)
    row = jnp.where(in_y, row, -1)
    zz = cell_z - cut
    in_strip = in_x & (zz >= 0) & (zz < STRIP)
    strip_lane = jnp.where(in_strip, cell_x * STRIP + zz, -1)
    return flat, cell_z - gz * BZ, row, strip_lane


def hits(count, index):
    return rows((count, index.shape[1])) == index


def product(left, right):
    return lax.dot_general(
        left, right, (((1,), (1,)), ((), ())), preferred_element_type=F32
    )


def inject_points(cells, wave_ref, width, waves, planes, out_ref, strip_out_ref):
    count, low, total_rows = len(waves), planes[0] * EY, (planes[1] - planes[0]) * EY
    for start in range(0, cells.shape[1], width):
        sl = slice(start, start + width)
        flat, z, row, strip_lane = places(cells, sl)
        here = hits(total_rows, flat - low).astype(F32).astype(BF16)
        at_strip = hits(BZ, strip_lane).astype(F32).astype(BF16)
        at_z, at_row = hits(BZ, z), hits(EY, row)
        total = strip_total = None
        parts = [split(wave_ref[wave : wave + 1, sl]) for wave in waves]
        for part in range(3):
            amounts = [parts[wave][part].astype(F32) for wave in range(count)]
            right = jnp.concatenate([jnp.where(at_z, a, 0.0) for a in amounts], 0).astype(BF16)
            left = jnp.concatenate([jnp.where(at_row, a, 0.0) for a in amounts], 0).astype(BF16)
            term, strip_term = product(here, right), product(left, at_strip)
            total = term if part == 0 else total + term
            strip_total = strip_term if part == 0 else strip_total + strip_term
        for wave in range(count):
            value = total[:, wave * BZ : wave * BZ + BZ]
            strip_value = strip_total[wave * EY : wave * EY + EY]
            if start > 0:
                value = value + out_ref[wave]
                strip_value = strip_value + strip_out_ref[wave]
            out_ref[wave] = value
            strip_out_ref[wave] = strip_value


LATE_PLANES, EARLY_PLANES, SOURCE_PLANES = (0, EX), (2, EX - 2), (1, EX - 1)


def late_kernel(receivers, receiver_wave, r_ref, rs_ref):
    inject_points(receivers, receiver_wave, 256, (2, 3), LATE_PLANES, r_ref, rs_ref)


def early_kernel(receivers, receiver_wave, _, r_ref, rs_ref):
    inject_points(receivers, receiver_wave, 256, (0, 1), EARLY_PLANES, r_ref, rs_ref)


def source_kernel(sources, source_wave, _, s_ref, ss_ref):
    width = sources.shape[1]
    inject_points(sources, source_wave, width, (0, 1, 2), SOURCE_PLANES, s_ref, ss_ref)


def strip_of(packed, block, slot):
    lane = lanes(packed.shape)
    width = BX * STRIP
    shift = (block * width - slot * width) % BZ
    moved = pltpu.roll(packed, shift, 1) if shift else packed
    return jnp.where((lane >= block * width) & (lane < (block + 1) * width), moved, 0.0)


def y_up(v):
    return pltpu.roll(v, EY - 1, 0)


def y_down(v):
    return pltpu.roll(v, 1, 0)


def z_up(v, strip, x):
    edge = pltpu.roll(strip, (BZ - 1 - (x * STRIP + MARGIN)) % BZ, 1)
    return jnp.where(lanes(v.shape) == BZ - 1, edge, pltpu.roll(v, BZ - 1, 1))


def z_down(v, strip, x):
    edge = pltpu.roll(strip, (BZ - (x * STRIP + MARGIN - 1)) % BZ, 1)
    return jnp.where(lanes(v.shape) == 0, edge, pltpu.roll(v, 1, 1))


def strip_flux(values, buoyancy):
    flux_x = buoyancy * (pltpu.roll(values, BZ - STRIP, 1) - values)
    flux_y = buoyancy * (y_up(values) - values)
    flux_z = buoyancy * (pltpu.roll(values, BZ - 1, 1) - values)
    spread = (flux_x - pltpu.roll(flux_x, STRIP, 1)) + (flux_y - y_down(flux_y))
    return flux_z, spread + (flux_z - pltpu.roll(flux_z, 1, 1))


def cut_flags():
    gz, half = lax.axis_index("gz"), lax.axis_size("gz") // 2
    return jnp.where(gz == half - 1, 1.0, 0.0), jnp.where(gz == half, 1.0, 0.0)


def sides():
    gx = lax.axis_index("gx")
    low = jnp.where(gx > 0, 1.0, 0.0)
    high = jnp.where(gx < lax.axis_size("gx") - 1, 1.0, 0.0)
    return low, high, lax.rem(gx, 2) == 0


def from_side(messages, first, count, block, side):
    even, odd = (message[first : first + count] for message in messages)
    low, high, even_above = side
    if block == 0:
        return jnp.where(even_above, odd, even) * low
    return jnp.where(even_above, even, odd) * high


def side_rows(base, wanted, step, block):
    planes = range(BX - wanted, BX) if block == 0 else range(wanted)
    return {plane: base + place * step for place, plane in enumerate(planes)}


def widened(own, own_tiles, messages, x, layout, side):
    block, plane = divmod(x, BX)
    if block == 1:
        main = own[0][own[1] + plane * BY : own[1] + plane * BY + BY]
        tile = own_tiles[0][own_tiles[1] + plane * 8 : own_tiles[1] + plane * 8 + 8]
        return jnp.concatenate([main, tile], 0)
    parts = []
    for (base, wanted), count in zip(layout, (BY, 8)):
        first = side_rows(base, wanted, count, block).get(plane)
        if first is None:
            parts.append(jnp.zeros((count, BZ), F32))
        else:
            parts.append(from_side(messages, first, count, block, side))
    return jnp.concatenate(parts, 0)


def whole_strip(own, messages, first, slot, side):
    low = from_side(messages, first, EY, 0, side)
    high = from_side(messages, first, EY, 2, side)
    return strip_of(low, 0, slot) + strip_of(own, 1, slot) + strip_of(high, 2, slot)


def adjoint_kernel(
    raw_ref, t_ref, edge_ref, even, odd, adj_hbm, ra_ref, rsa_ref, rb_ref, rsb_ref, table_ref,
    out_ref, hist_ref, coef_ref, coef_strip_ref,
    field, w_sem,
):
    w_copy = pltpu.make_async_copy(adj_hbm.at[pl.ds(1, 3)], out_ref.at[pl.ds(1, 3)], w_sem)
    w_copy.start()
    cut_up, cut_down = cut_flags()
    side = sides()
    messages = (even, odd)
    r_refs = ((ra_ref, 0), (ra_ref, 1), (rb_ref, 0), (rb_ref, 1))
    rs_refs = ((rsa_ref, 0), (rsa_ref, 1), (rsb_ref, 0), (rsb_ref, 1))
    tiles = 2 * PLANES + 3 * BY

    def initial(index, x):
        own = ((raw_ref, PLANES), (t_ref, 0), (raw_ref, 2 * PLANES))[index]
        layout = (
            ((0, 4), (tiles, 3)),
            ((2 * PLANES, 3), (tiles + 24, 2)),
            ((PLANES, 4), (tiles + 40, 3)),
        )[index]
        return widened(own, (edge_ref, 32 * index), messages, x, layout, side)

    for x in range(EX):
        stiff, buoy, damp = coefficients(initial(2, x), table_ref)
        coef_ref[0, x], coef_ref[1, x], coef_ref[2, x] = stiff, buoy, damp
    own_strip = edge_ref[ADJ_EDGE_ROWS - EY : ADJ_EDGE_ROWS]
    q_s, t_s, label_s = (
        whole_strip(own_strip, messages, ADJ_ROWS - EY, slot, side) for slot in range(3)
    )
    stiff_s, buoy_s, damp_s = coefficients(label_s, table_ref)
    coef_strip_ref[0], coef_strip_ref[1], coef_strip_ref[2] = stiff_s, buoy_s, damp_s
    w_copy.wait()

    for step in range(1, STEPS + 1):
        k = STEPS - step
        rs_ref, place = rs_refs[k]
        q_s = q_s + rs_ref[place]
        u_s = stiff_s * damp_s * q_s
        flux_s, spread = strip_flux(u_s, buoy_s)
        t_s = t_s + spread
        q_s = damp_s * q_s + t_s
        edge_up = u_s * cut_up
        edge_down = flux_s * cut_down

        def injected(x):
            r_ref, place = r_refs[k]
            value = initial(0, x) if step == 1 else field[0, x]
            value = value + r_ref[place, x - (EARLY_PLANES if k < 2 else LATE_PLANES)[0]]
            return value, coef_ref[0, x] * coef_ref[2, x] * value

        flux_below = None
        q_now, u_now = injected(step - 1)
        for x in range(step - 1, EX - step):
            q_next, u_next = injected(x + 1)
            buoyancy = coef_ref[1, x]
            slope_x = u_next - u_now
            flux_x = buoyancy * slope_x
            if x >= step:
                slope_y = y_up(u_now) - u_now
                slope_z = z_up(u_now, edge_up, x) - u_now
                flux_y = buoyancy * slope_y
                flux_z = buoyancy * slope_z
                spread = (flux_x - flux_below) + (flux_y - y_down(flux_y))
                spread = spread + (flux_z - z_down(flux_z, edge_down, x))
                damped = coef_ref[2, x] * q_now
                if BX <= x < 2 * BX:
                    place = x - BX
                    hist_ref[k, 0, place] = damped[0:BY]
                    for index, slope in enumerate((slope_x, slope_y, slope_z)):
                        w = out_ref[1 + index, place] + slope[0:BY]
                        out_ref[1 + index, place] = w
                        hist_ref[k, 1 + index, place] = w
                t = (initial(1, x) if step == 1 else field[1, x]) + spread
                if step < STEPS:
                    field[1, x] = t
                    field[0, x] = damped + t
                else:
                    out_ref[0, x - BX] = (damped + t)[0:BY]
            flux_below = flux_x
            q_now, u_now = q_next, u_next


def forward_kernel(
    wave_ref, edge_ref, even, odd, coef_ref, coef_strip_ref, s_ref, ss_ref, hist_ref,
    grad_ref,
    field,
):
    cut_up, cut_down = cut_flags()
    side = sides()
    messages = (even, odd)
    tiles = PLANES + 3 * BY

    def initial(index, x):
        layout = (((0, 4), (tiles, 3)), ((PLANES, 3), (tiles + 24, 2)))[index]
        own = (wave_ref, PLANES * index)
        return widened(own, (edge_ref, 32 * index), messages, x, layout, side)

    own_strip = edge_ref[WAVE_EDGE_ROWS - EY : WAVE_EDGE_ROWS]
    p_s, s_s = (
        whole_strip(own_strip, messages, WAVE_ROWS - EY, slot, side) for slot in range(2)
    )
    stiff_s, buoy_s, damp_s = coef_strip_ref[0], coef_strip_ref[1], coef_strip_ref[2]

    for step in range(1, STEPS + 1):
        k = step - 1
        edge_up = p_s * cut_up
        flux_s, spread = strip_flux(p_s, buoy_s)
        edge_down = flux_s * cut_down
        if step < STEPS:
            s_s = s_s - spread
            p_s = damp_s * (p_s - stiff_s * s_s) + ss_ref[k]

        def pressure(x):
            return initial(0, x) if step == 1 else field[0, x]

        flux_below = None
        p_now = pressure(step - 1)
        for x in range(step - 1, EX - step):
            p_next = pressure(x + 1)
            buoyancy = coef_ref[1, x]
            slope_x = p_next - p_now
            flux_x = buoyancy * slope_x
            if x >= step:
                slope_y = y_up(p_now) - p_now
                slope_z = z_up(p_now, edge_up, x) - p_now
                flux_y = buoyancy * slope_y
                flux_z = buoyancy * slope_z
                spread = (flux_x - flux_below) + (flux_y - y_down(flux_y))
                spread = spread + (flux_z - z_down(flux_z, edge_down, x))
                spread = (initial(1, x) if step == 1 else field[1, x]) - spread
                if step < STEPS:
                    field[1, x] = spread
                    field[0, x] = (
                        coef_ref[2, x] * (p_now - coef_ref[0, x] * spread)
                        + s_ref[k, x - SOURCE_PLANES[0]]
                    )
                if BX <= x < 2 * BX:
                    place = x - BX
                    term = hist_ref[k, 0, place] * spread[0:BY]
                    grad_ref[0, place] = -term if k == 0 else grad_ref[0, place] - term
                    term = hist_ref[k, 1, place] * slope_x[0:BY]
                    term = term + hist_ref[k, 2, place] * slope_y[0:BY]
                    term = term + hist_ref[k, 3, place] * slope_z[0:BY]
                    grad_ref[1, place] = -term if k == 0 else grad_ref[1, place] - term
            flux_below = flux_x
            p_now = p_next


def shape(*dims):
    return jax.ShapeDtypeStruct(dims, F32)


def call(kernel, outs, operands, scratch, places):
    spaces = {"h": pltpu.HBM, "a": pl.ANY, "v": pltpu.VMEM}
    operands = [
        pltpu.with_memory_space_constraint(operand, pltpu.HBM) if place == "h" else operand
        for operand, place in zip(operands, places)
    ]
    return pl.pallas_call(
        kernel,
        out_shape=outs,
        in_specs=[pl.BlockSpec(memory_space=spaces[place]) for place in places],
        out_specs=[pl.BlockSpec(memory_space=pltpu.VMEM)] * len(outs),
        scratch_shapes=scratch,
        compiler_params=pltpu.CompilerParams(vmem_limit_bytes=VMEM_LIMIT),
        cost_estimate=pl.CostEstimate(flops=1 << 24, bytes_accessed=1 << 20, transcendentals=0),
    )(*operands)


def from_sides(array, axes):
    count = lax.axis_size("gy")

    def route(offset):
        pairs = []
        for target in range(count):
            source = target + offset
            if 0 <= source < count:
                if "gz" in axes:
                    pairs += [(2 * source + z, 2 * target + 1 - z) for z in range(2)]
                else:
                    pairs.append((source, target))
        return pairs

    if count == 2:
        both = lax.ppermute(array, axes, route(1) + route(-1))
        return both, both
    return lax.ppermute(array, axes, route(1)), lax.ppermute(array, axes, route(-1))


def rotated(array, axis, offset):
    count = lax.axis_size(axis)
    return lax.ppermute(array, axis, [((i + offset) % count, i) for i in range(count)])


def paired(array, odd):
    count = lax.axis_size("gx")
    pairs = []
    for i in range(count):
        partner = ((i - 1) ^ 1) + 1 if odd else i ^ 1
        pairs.append((partner if 0 <= partner < count else i, i))
    return lax.ppermute(array, "gx", pairs)


def local(
    stored, adjoint_end, labels, tissue, source_cells, source_wave, receiver_cells, receiver_wave
):
    assert lax.axis_size("gz") == 2 and labels.shape == (BX, BY, BZ) and tissue.shape[1] == 8
    half = lax.axis_size("gx") // 2
    arguments = [
        stored, adjoint_end, labels, tissue,
        receiver_cells.T, receiver_wave, source_cells.T, source_wave,
    ]
    raw, s, t, face_x, face_y, face_z, table, receivers, receiver_wave, sources, source_wave = call(
        face_kernel,
        [
            shape(3 * PLANES, BZ),
            shape(PLANES, BZ),
            shape(PLANES, BZ),
            shape(2 * BY, BZ),
            shape(8, BZ),
            shape(BY, BZ),
            shape(24, BZ),
        ]
        + [jax.ShapeDtypeStruct(array.shape, array.dtype) for array in arguments[4:]],
        arguments,
        [
            pltpu.VMEM(stored.shape, F32),
            pltpu.VMEM(adjoint_end.shape, F32),
            pltpu.VMEM(labels.shape, jnp.int32),
            pltpu.SMEM(tissue.shape, F32),
            pltpu.SemaphoreType.DMA,
        ],
        "hhhhhhhh",
    )
    rb, rsb = call(
        late_kernel,
        [shape(2, EX * EY, BZ), shape(2, EY, BZ)],
        [receivers, receiver_wave],
        [],
        "vv",
    )
    face_x = rotated(face_x, "gx", -1)
    face_y = rotated(face_y, "gy", -1)
    face_z = rotated(face_z, "gz", -1)
    wave, t = call(
        fix_kernel,
        [shape(2 * PLANES, BZ), shape(PLANES, BZ)],
        [raw, s, t, face_x, face_y, face_z, rsb],
        [],
        "vvvvvva",
    )
    edges, corners, strips = call(
        edge_kernel,
        [shape((5 * BX + 2) * 8, BZ), shape(16, BZ), shape(2 * BY, BZ)],
        [raw, wave, t],
        [],
        "vvv",
    )
    wave = rotated(wave, "gx", half)
    early_planes, source_planes = (last - first for first, last in (EARLY_PLANES, SOURCE_PLANES))
    ra, rsa = call(
        early_kernel,
        [shape(2, early_planes * EY, BZ), shape(2, EY, BZ)],
        [receivers, receiver_wave, corners],
        [],
        "vva",
    )
    ra, rb = ra.reshape(2, early_planes, EY, BZ), rb.reshape(2, EX, EY, BZ)
    other = rotated(strips, "gz", 1)
    up, down = from_sides(edges, "gy")
    corner_up, corner_down = from_sides(corners, ("gy", "gz"))
    wave_edge, adj_edge = call(
        merge_kernel,
        [shape(WAVE_EDGE_ROWS, BZ), shape(ADJ_EDGE_ROWS, BZ)],
        [up, down, strips, other, corner_up, corner_down, rsa, wave],
        [],
        "vvvvvvaa",
    )
    wave_edge = rotated(wave_edge, "gx", half)
    src, src_strip = call(
        source_kernel,
        [shape(STEPS - 1, source_planes * EY, BZ), shape(STEPS - 1, EY, BZ)],
        [sources, source_wave, adj_edge],
        [],
        "vva",
    )
    src = src.reshape(STEPS - 1, source_planes, EY, BZ)
    even, odd = call(
        adjoint_join_kernel,
        [shape(ADJ_ROWS, BZ), shape(ADJ_ROWS, BZ)],
        [raw, t, adj_edge, wave_edge],
        [],
        "vvva",
    )
    even, odd = paired(even, False), paired(odd, True)
    wave_even, wave_odd = call(
        join_kernel,
        [shape(WAVE_ROWS, BZ), shape(WAVE_ROWS, BZ)],
        [wave, wave_edge],
        [],
        "vv",
    )
    wave_even, wave_odd = paired(wave_even, False), paired(wave_odd, True)
    adjoint_start, hist, coef, coef_strip = call(
        adjoint_kernel,
        [
            shape(4, BX, BY, BZ),
            shape(STEPS, 4, BX, BY, BZ),
            shape(3, EX, EY, BZ),
            shape(3, EY, BZ),
        ],
        [raw, t, adj_edge, even, odd, adjoint_end, ra, rsa, rb, rsb, table],
        [pltpu.VMEM((2, EX, EY, BZ), F32), pltpu.SemaphoreType.DMA],
        "vvvvvhvvvvv",
    )
    (gradient,) = call(
        forward_kernel,
        [shape(2, BX, BY, BZ)],
        [wave, wave_edge, wave_even, wave_odd, coef, coef_strip, src, src_strip, hist],
        [pltpu.VMEM((2, EX, EY, BZ), F32)],
        "vvvvvvvvv",
    )
    return gradient, adjoint_start


def solution(mesh):
    return jax.shard_map(
        local,
        mesh=mesh,
        in_specs=(
            P("shot", "gx", "gy", "gz"),
            P("shot", "gx", "gy", "gz"),
            P("gx", "gy", "gz"),
            P(),
            P("shot", None),
            P(None, "shot"),
            P(),
            P(None, "shot"),
        ),
        out_specs=(P("shot", "gx", "gy", "gz"), P("shot", "gx", "gy", "gz")),
        check_vma=False,
    )
```

```python
import jax
import jax.numpy as jnp
from jax import lax
from jax.experimental import pallas as pl
from jax.experimental.pallas import tpu as pltpu
from jax.sharding import PartitionSpec as P

STEPS = 4
MARGIN = 4
BX, BY, BZ = 4, 32, 128
EX, EY = BX + 2 * MARGIN, BY + 2 * MARGIN
STRIP = 2 * MARGIN
F32 = jnp.float32
BF16 = jnp.bfloat16
VMEM_LIMIT = 16 * 1024 * 1024
PLANES = BX * BY
WAVE_OWN = (PLANES, PLANES + BY, PLANES + BY + 9 * 8)
ADJ_OWN = (PLANES, PLANES + BY, PLANES + BY + 13 * 8)
WAVE_SIDE = (PLANES + 3 * BY, PLANES + 4 * BY, PLANES + 4 * BY + 6 * 8)
ADJ_SIDE = (3 * BY, 4 * BY, 4 * BY + 9 * 8)


def lanes(shape):
    return lax.broadcasted_iota(jnp.int32, shape, len(shape) - 1)


def rows(shape):
    return lax.broadcasted_iota(jnp.int32, shape, len(shape) - 2)


def run(copies):
    for copy in copies:
        copy.start()
    for copy in copies:
        copy.wait()


def coefficients(labels, table_ref):
    result = [jnp.zeros(labels.shape, F32) for _ in range(3)]
    for index in range(8):
        picked = labels == float(index + 1)
        for kind in range(3):
            row = kind * 8 + index
            result[kind] = jnp.where(picked, table_ref[row : row + 1], result[kind])
    return result


def buoyancy_of(labels, table_ref):
    result = jnp.zeros(labels.shape, F32)
    for index in range(8):
        result = jnp.where(labels == float(index + 1), table_ref[8 + index : 9 + index], result)
    return result


def half_turn(tile):
    return pltpu.roll(tile, MARGIN, 0)


def load_kernel(
    stored_hbm, adj_hbm, lab_hbm, tissue_hbm, rc_hbm, rw_hbm, sc_hbm, sw_hbm,
    p_ref, ql_ref, s_ref, t_ref, last_x_ref, last_y_ref, strip_ref, table_ref,
    rc_ref, rw_ref, sc_ref, sw_ref, *rest,
):
    *sends, stored, adj, lab, tissue, sem = rest
    run([
        pltpu.make_async_copy(source, target, sem)
        for source, target in (
            (stored_hbm, stored), (adj_hbm, adj), (lab_hbm, lab), (tissue_hbm, tissue),
            (rc_hbm, rc_ref), (rw_hbm, rw_ref), (sc_hbm, sc_ref), (sw_hbm, sw_ref),
        )
    ])
    for index in range(tissue.shape[1]):
        speed = jnp.full((1, BZ), tissue[0, index], F32)
        density = jnp.full((1, BZ), tissue[1, index], F32)
        table_ref[index : index + 1] = density * speed
        table_ref[8 + index : 9 + index] = speed / density
        table_ref[16 + index : 17 + index] = 1.0 - jnp.full((1, BZ), tissue[2, index], F32)
    gy, gz = lax.axis_index("gy"), lax.axis_index("gz")
    lane = lanes((BY, BZ))
    row = rows((BY, BZ))
    tile_row = rows((8, BZ))
    strips = [jnp.zeros((BY, BZ), F32) for _ in range(3)]
    tiles = [None] * 39
    previous = [None, None]

    def edge_tile(block):
        return jnp.where(tile_row < MARGIN, block[0:8], block[BY - 8 : BY])

    for x in range(BX):
        labels = lab[x].astype(F32) + 1.0
        buoyancy = buoyancy_of(labels, table_ref)
        plane = slice(x * BY, x * BY + BY)
        fields = [stored[index, x] for index in range(4)] + [adj[0, x]]
        fields += [buoyancy * adj[index, x] for index in range(1, 4)] + [labels]
        p_ref[plane] = fields[0]
        ql_ref[plane] = fields[4]
        ql_ref[PLANES + x * BY : PLANES + x * BY + BY] = labels
        for index, block in enumerate(fields):
            tiles[index * BX + x] = edge_tile(block)
            group, slot = divmod(index, 4)
            base = slot * BX * STRIP + x * STRIP
            rolled = pltpu.roll(block, base + MARGIN, 1)
            first = base + MARGIN * gz
            strips[group] = jnp.where(
                (lane >= first) & (lane < first + MARGIN), rolled, strips[group]
            )
        for kind, target in enumerate((s_ref, t_ref)):
            vx, vy, vz = fields[4 * kind + 1 : 4 * kind + 4]
            spread = vx if x == 0 else vx - previous[kind]
            spread = spread + (vy - jnp.where(row == 0, 0.0, pltpu.roll(vy, 1, 0)))
            spread = spread + (vz - jnp.where(lane == 0, 0.0, pltpu.roll(vz, 1, 1)))
            target[plane] = spread
            previous[kind] = vx
            index = (kind * BX + x) * 8
            last_y_ref[index : index + 8] = vy[BY - 8 : BY]
    for kind in range(2):
        last_x_ref[kind * BY : kind * BY + BY] = previous[kind]
    for group in range(3):
        strip_ref[group * BY : group * BY + BY] = strips[group]
        tiles[9 * BX + group] = edge_tile(strips[group])

    def joined(first, second):
        second = first if second is None else second
        upward = jnp.where(tile_row < MARGIN, half_turn(first), second)
        downward = jnp.where(tile_row < MARGIN, first, half_turn(second))
        if len(sends) == 2:
            return (jnp.where(gy == 0, upward, downward),)
        return upward, downward

    tiles.append(None)
    half = len(sends) // 2
    for place in range(20):
        for target, tile in zip(sends[:half], joined(tiles[2 * place], tiles[2 * place + 1])):
            target[place * 8 : place * 8 + 8] = tile
    for place in range(2):
        first = tiles[9 * BX + 2 * place]
        for target, tile in zip(sends[half:], joined(first, tiles[9 * BX + 2 * place + 1])):
            target[place * 8 : place * 8 + 8] = tile


def copy_rows(target, base, source, first, count):
    target[base : base + count] = source[pl.ds(pl.multiple_of(first, 8), count)]
    return base + count


def pair_planes():
    parity = lax.rem(lax.axis_index("gx"), 2)
    return 1 - parity, parity


def merge_kernel(
    from_up, from_down, corner_up, corner_down, strip_ref, other_ref,
    s_ref, t_ref, last_x_ref, last_y_ref, _a, _b,
    wave_ref, adj_ref, token_ref,
):
    token_ref[...] = jnp.zeros((8, BZ), F32)
    gy = lax.axis_index("gy")
    tile_row = rows((8, BZ))
    row, lane = rows((BY, BZ)), lanes((BY, BZ))
    take_up = (tile_row < MARGIN) & (gy < lax.axis_size("gy") - 1)
    take_down = (tile_row >= MARGIN) & (gy > 0)
    _, cut_down = cut_flags()

    def halo(up, down, index):
        place, second = divmod(index, 2)
        sl = slice(place * 8, place * 8 + 8)
        above = half_turn(up[sl]) if second else up[sl]
        below = down[sl] if second else half_turn(down[sl])
        return jnp.where(take_up, above, jnp.where(take_down, below, 0.0))

    wide = []
    for group in range(3):
        sl = slice(group * BY, group * BY + BY)
        tile = halo(from_up, from_down, 9 * BX + group) + halo(corner_up, corner_down, group)
        wide.append(jnp.concatenate([strip_ref[sl] + other_ref[sl], tile], 0))
    strip_lane = lanes((EY, BZ))

    def strip_field(index):
        group, slot = divmod(index, 4)
        moved = pltpu.roll(wide[group], (BZ - slot * BX * STRIP) % BZ, 1) if slot else wide[group]
        return jnp.where(strip_lane < BX * STRIP, moved, 0.0)

    last_lanes = (BX - 1) * STRIP
    for kind, (source, target) in enumerate(((s_ref, wave_ref), (t_ref, adj_ref))):
        first = 4 * kind
        planes_end, x_end, tiles_end = (WAVE_OWN, ADJ_OWN)[kind]
        vx, vy, vz = (strip_field(first + 1 + axis) for axis in range(3))
        spread = vx - jnp.where(strip_lane < STRIP, 0.0, pltpu.roll(vx, STRIP, 1))
        spread = (spread + (vy - y_down(vy))) + (vz - pltpu.roll(vz, 1, 1))
        strip = strip_field(first)
        strip = strip + pltpu.roll(jnp.where(strip_lane < BX * STRIP, spread, 0.0), BX * STRIP, 1)
        last_slot = 2
        if kind == 1:
            strip = strip + pltpu.roll(strip_field(8), 2 * BX * STRIP, 1)
            last_slot = 3
        last = jnp.where(strip_lane >= last_lanes, vx, 0.0)
        strip = strip + pltpu.roll(last, last_slot * BX * STRIP - last_lanes, 1)
        target[tiles_end : tiles_end + EY] = strip
        target[planes_end:x_end] = last_x_ref[kind * BY : kind * BY + BY]

        vx_before = None
        for x in range(BX):
            vx_t, vy_t, vz_t = (
                halo(from_up, from_down, (first + 1 + axis) * BX + x) for axis in range(3)
            )
            below_z = pltpu.roll(vz, (BZ - (x * STRIP + MARGIN - 1)) % BZ, 1) * cut_down
            last_y = last_y_ref[(kind * BX + x) * 8 : (kind * BX + x) * 8 + 8]
            y_before = jnp.where(
                tile_row == 0, pltpu.roll(last_y, 1, 0), pltpu.roll(vy_t, 1, 0)
            )
            z_before = jnp.where(lane[0:8] == 0, below_z[BY:EY], pltpu.roll(vz_t, 1, 1))
            spread = vx_t if x == 0 else vx_t - vx_before
            spread = (spread + (vy_t - y_before)) + (vz_t - z_before)
            vx_before = vx_t
            block = source[x * BY : x * BY + BY]
            block = block - jnp.where(row == 0, vy_t[7:8], 0.0)
            block = block - jnp.where(lane == 0, below_z[0:BY], 0.0)
            target[x * BY : x * BY + BY] = block
            base = x_end + x * 8
            target[base : base + 8] = halo(from_up, from_down, first * BX + x)
            target[base + 32 : base + 40] = spread
            if kind == 1:
                target[base + 64 : base + 72] = halo(from_up, from_down, 8 * BX + x)
        target[tiles_end - 8 : tiles_end] = vx_before


def adjoint_join_kernel(ql_ref, adj_ref, _, even_ref, odd_ref, token_ref):
    token_ref[...] = jnp.zeros((8, BZ), F32)
    planes_end, x_end, tiles_end = ADJ_OWN
    for target, first in zip((even_ref, odd_ref), pair_planes()):
        base = copy_rows(target, 0, adj_ref, first * BY, 3 * BY)
        base = copy_rows(target, base, adj_ref, planes_end, BY)
        base = copy_rows(target, base, adj_ref, x_end + first * 8, 24)
        base = copy_rows(target, base, adj_ref, x_end + 32 + first * 16, 16)
        base = copy_rows(target, base, adj_ref, x_end + 64 + first * 8, 24)
        base = copy_rows(target, base, adj_ref, tiles_end - 8, 8 + EY)
        copy_rows(target, base, ql_ref, 0, 2 * PLANES)


def join_kernel(p_ref, wave_ref, _, even_ref, odd_ref):
    planes_end, x_end, tiles_end = WAVE_OWN
    for target, first in zip((even_ref, odd_ref), pair_planes()):
        base = copy_rows(target, 0, p_ref, 0, PLANES)
        base = copy_rows(target, base, wave_ref, first * BY, 3 * BY)
        base = copy_rows(target, base, wave_ref, planes_end, BY)
        base = copy_rows(target, base, wave_ref, x_end + first * 8, 24)
        base = copy_rows(target, base, wave_ref, x_end + 32 + first * 16, 16)
        copy_rows(target, base, wave_ref, tiles_end - 8, 8 + EY)


def split(values):
    high = values.astype(BF16)
    rest = values - high.astype(F32)
    middle = rest.astype(BF16)
    low = (rest - middle.astype(F32)).astype(BF16)
    return high, middle, low


def places(cells, sl):
    gx, gy, gz = (lax.axis_index(name) for name in ("gx", "gy", "gz"))
    cut = BZ * lax.axis_size("gz") // 2 - MARGIN
    cell_x = cells[0:1, sl] - (gx * BX - MARGIN)
    cell_y = cells[1:2, sl] - gy * BY
    cell_z = cells[2:3, sl]
    in_x = (cell_x >= 0) & (cell_x < EX)
    in_y = (cell_y >= -MARGIN) & (cell_y < BY + MARGIN)
    row = jnp.where(cell_y < 0, cell_y + EY, cell_y)
    flat = jnp.where(in_x & in_y, cell_x * EY + row, -1)
    row = jnp.where(in_y, row, -1)
    zz = cell_z - cut
    in_strip = in_x & (zz >= 0) & (zz < STRIP)
    strip_lane = jnp.where(in_strip, cell_x * STRIP + zz, -1)
    return flat, cell_z - gz * BZ, row, strip_lane


def hits(count, index):
    return rows((count, index.shape[1])) == index


def product(left, right):
    return lax.dot_general(
        left, right, (((1,), (1,)), ((), ())), preferred_element_type=F32
    )


def inject_points(cells, wave_ref, width, waves, planes, out_ref, strip_out_ref):
    count, low, total_rows = len(waves), planes[0] * EY, (planes[1] - planes[0]) * EY
    for start in range(0, cells.shape[1], width):
        sl = slice(start, start + width)
        flat, z, row, strip_lane = places(cells, sl)
        here = hits(total_rows, flat - low).astype(F32).astype(BF16)
        at_strip = hits(BZ, strip_lane).astype(F32).astype(BF16)
        at_z, at_row = hits(BZ, z), hits(EY, row)
        total = strip_total = None
        parts = [split(wave_ref[wave : wave + 1, sl]) for wave in waves]
        for part in range(3):
            amounts = [parts[wave][part].astype(F32) for wave in range(count)]
            right = jnp.concatenate([jnp.where(at_z, a, 0.0) for a in amounts], 0).astype(BF16)
            left = jnp.concatenate([jnp.where(at_row, a, 0.0) for a in amounts], 0).astype(BF16)
            term, strip_term = product(here, right), product(left, at_strip)
            total = term if part == 0 else total + term
            strip_total = strip_term if part == 0 else strip_total + strip_term
        for wave in range(count):
            value = total[:, wave * BZ : wave * BZ + BZ]
            strip_value = strip_total[wave * EY : wave * EY + EY]
            if start > 0:
                value = value + out_ref[wave]
                strip_value = strip_value + strip_out_ref[wave]
            out_ref[wave] = value
            strip_out_ref[wave] = strip_value


LATE_PLANES, EARLY_PLANES, SOURCE_PLANES = (0, EX), (2, EX - 2), (1, EX - 1)


def late_kernel(receivers, receiver_wave, r_ref, rs_ref):
    inject_points(receivers, receiver_wave, 256, (2, 3), LATE_PLANES, r_ref, rs_ref)


def early_kernel(receivers, receiver_wave, _, r_ref, rs_ref):
    inject_points(receivers, receiver_wave, 256, (0, 1), EARLY_PLANES, r_ref, rs_ref)


def source_kernel(sources, source_wave, _, s_ref, ss_ref):
    width = sources.shape[1]
    inject_points(sources, source_wave, width, (0, 1, 2), SOURCE_PLANES, s_ref, ss_ref)


def strip_of(packed, block, slot):
    lane = lanes(packed.shape)
    width = BX * STRIP
    shift = (block * width - slot * width) % BZ
    moved = pltpu.roll(packed, shift, 1) if shift else packed
    return jnp.where((lane >= block * width) & (lane < (block + 1) * width), moved, 0.0)


def y_up(v):
    return pltpu.roll(v, EY - 1, 0)


def y_down(v):
    return pltpu.roll(v, 1, 0)


def z_up(v, strip, x):
    edge = pltpu.roll(strip, (BZ - 1 - (x * STRIP + MARGIN)) % BZ, 1)
    return jnp.where(lanes(v.shape) == BZ - 1, edge, pltpu.roll(v, BZ - 1, 1))


def z_down(v, strip, x):
    edge = pltpu.roll(strip, (BZ - (x * STRIP + MARGIN - 1)) % BZ, 1)
    return jnp.where(lanes(v.shape) == 0, edge, pltpu.roll(v, 1, 1))


def strip_flux(values, buoyancy):
    flux_x = buoyancy * (pltpu.roll(values, BZ - STRIP, 1) - values)
    flux_y = buoyancy * (y_up(values) - values)
    flux_z = buoyancy * (pltpu.roll(values, BZ - 1, 1) - values)
    spread = (flux_x - pltpu.roll(flux_x, STRIP, 1)) + (flux_y - y_down(flux_y))
    return flux_z, spread + (flux_z - pltpu.roll(flux_z, 1, 1))


def cut_flags():
    gz, half = lax.axis_index("gz"), lax.axis_size("gz") // 2
    return jnp.where(gz == half - 1, 1.0, 0.0), jnp.where(gz == half, 1.0, 0.0)


def sides():
    gx = lax.axis_index("gx")
    low = jnp.where(gx > 0, 1.0, 0.0)
    high = jnp.where(gx < lax.axis_size("gx") - 1, 1.0, 0.0)
    return low, high, lax.rem(gx, 2) == 0


def from_side(messages, first, count, block, side):
    even, odd = (message[first : first + count] for message in messages)
    low, high, even_above = side
    if block == 0:
        return jnp.where(even_above, odd, even) * low
    return jnp.where(even_above, even, odd) * high


def side_rows(base, wanted, step, block):
    planes = range(BX - wanted, BX) if block == 0 else range(wanted)
    return {plane: base + place * step for place, plane in enumerate(planes)}


def widened(own, own_tiles, x, layout, side):
    block, plane = divmod(x, BX)
    if block == 1:
        main = own[0][own[1] + plane * BY : own[1] + plane * BY + BY]
        tile = own_tiles[0][own_tiles[1] + plane * 8 : own_tiles[1] + plane * 8 + 8]
        return jnp.concatenate([main, tile], 0)
    parts = []
    for (messages, base, wanted), count in zip(layout, (BY, 8)):
        first = side_rows(base, wanted, count, block).get(plane)
        if first is None:
            parts.append(jnp.zeros((count, BZ), F32))
        else:
            parts.append(from_side(messages, first, count, block, side))
    return jnp.concatenate(parts, 0)


def less_plane_below(value, x, own_ref, own_rows, messages, side_rows_of, side):
    if x == BX:
        planes_end, _, tiles_end = side_rows_of
        main = from_side(messages, planes_end, BY, 0, side)
        tile = from_side(messages, tiles_end - 8, 8, 0, side)
    elif x == 2 * BX:
        planes_end, _, tiles_end = own_rows
        high = side[1]
        main = own_ref[planes_end : planes_end + BY] * high
        tile = own_ref[tiles_end - 8 : tiles_end] * high
    else:
        return value
    return value - jnp.concatenate([main, tile], 0)


def strip_below(own, messages, first, slot, side):
    lane = lanes(own.shape)
    width = BX * STRIP
    low = from_side(messages, first, EY, 0, side)
    low = pltpu.roll(low, (width - slot * width) % BZ, 1)
    own = pltpu.roll(own * side[1], (2 * width - slot * width) % BZ, 1)
    in_own = (lane >= width) & (lane < width + STRIP)
    in_high = (lane >= 2 * width) & (lane < 2 * width + STRIP)
    return jnp.where(in_own, low, jnp.where(in_high, own, 0.0))


def whole_strip(own, messages, first, slot, side):
    low = from_side(messages, first, EY, 0, side)
    high = from_side(messages, first, EY, 2, side)
    return strip_of(low, 0, slot) + strip_of(own, 1, slot) + strip_of(high, 2, slot)


def adjoint_kernel(
    ql_ref, late_ref, even, odd, adj_hbm, ra_ref, rsa_ref, rb_ref, rsb_ref,
    table_ref,
    out_ref, hist_ref, coef_ref, coef_strip_ref,
    field, w_sem,
):
    w_copy = pltpu.make_async_copy(adj_hbm.at[pl.ds(1, 3)], out_ref.at[pl.ds(1, 3)], w_sem)
    w_copy.start()
    cut_up, cut_down = cut_flags()
    side = sides()
    messages = (even, odd)
    r_refs = ((ra_ref, 0), (ra_ref, 1), (rb_ref, 0), (rb_ref, 1))
    rs_refs = ((rsa_ref, 0), (rsa_ref, 1), (rsb_ref, 0), (rsb_ref, 1))
    tiles, own_tiles, raws = ADJ_SIDE[1], ADJ_OWN[1], ADJ_SIDE[2] + EY

    def initial(index, x):
        own = ((ql_ref, 0), (late_ref, 0), (ql_ref, PLANES))[index]
        layout = (
            ((messages, raws, 4), (messages, tiles, 3)),
            ((messages, 0, 3), (messages, tiles + 24, 2)),
            ((messages, raws + PLANES, 4), (messages, tiles + 40, 3)),
        )[index]
        value = widened(own, (late_ref, own_tiles + 32 * index), x, layout, side)
        if index == 1:
            value = less_plane_below(value, x, late_ref, ADJ_OWN, messages, ADJ_SIDE, side)
        return value

    for x in range(EX):
        stiff, buoy, damp = coefficients(initial(2, x), table_ref)
        coef_ref[0, x], coef_ref[1, x], coef_ref[2, x] = stiff, buoy, damp
    own_strip = late_ref[ADJ_OWN[2] : ADJ_OWN[2] + EY]
    q_s, t_s, label_s = (
        whole_strip(own_strip, messages, ADJ_SIDE[2], slot, side) for slot in range(3)
    )
    t_s = t_s - strip_below(own_strip, messages, ADJ_SIDE[2], 3, side)
    stiff_s, buoy_s, damp_s = coefficients(label_s, table_ref)
    coef_strip_ref[0], coef_strip_ref[1], coef_strip_ref[2] = stiff_s, buoy_s, damp_s
    w_copy.wait()

    for step in range(1, STEPS + 1):
        k = STEPS - step
        rs_ref, place = rs_refs[k]
        q_s = q_s + rs_ref[place]
        u_s = stiff_s * damp_s * q_s
        flux_s, spread = strip_flux(u_s, buoy_s)
        t_s = t_s + spread
        q_s = damp_s * q_s + t_s
        edge_up = u_s * cut_up
        edge_down = flux_s * cut_down

        def injected(x):
            r_ref, place = r_refs[k]
            value = initial(0, x) if step == 1 else field[0, x]
            value = value + r_ref[place, x - (EARLY_PLANES if k < 2 else LATE_PLANES)[0]]
            return value, coef_ref[0, x] * coef_ref[2, x] * value

        flux_below = None
        q_now, u_now = injected(step - 1)
        for x in range(step - 1, EX - step):
            q_next, u_next = injected(x + 1)
            buoyancy = coef_ref[1, x]
            slope_x = u_next - u_now
            flux_x = buoyancy * slope_x
            if x >= step:
                slope_y = y_up(u_now) - u_now
                slope_z = z_up(u_now, edge_up, x) - u_now
                flux_y = buoyancy * slope_y
                flux_z = buoyancy * slope_z
                spread = (flux_x - flux_below) + (flux_y - y_down(flux_y))
                spread = spread + (flux_z - z_down(flux_z, edge_down, x))
                damped = coef_ref[2, x] * q_now
                if BX <= x < 2 * BX:
                    place = x - BX
                    hist_ref[k, 0, place] = damped[0:BY]
                    for index, slope in enumerate((slope_x, slope_y, slope_z)):
                        w = out_ref[1 + index, place] + slope[0:BY]
                        out_ref[1 + index, place] = w
                        hist_ref[k, 1 + index, place] = w
                t = (initial(1, x) if step == 1 else field[1, x]) + spread
                if step < STEPS:
                    field[1, x] = t
                    field[0, x] = damped + t
                else:
                    out_ref[0, x - BX] = (damped + t)[0:BY]
            flux_below = flux_x
            q_now, u_now = q_next, u_next


def forward_kernel(
    p_ref, late_ref, even, odd, coef_ref, coef_strip_ref, s_ref, ss_ref, hist_ref,
    grad_ref,
    field,
):
    cut_up, cut_down = cut_flags()
    side = sides()
    messages = (even, odd)
    tiles, own_tiles = WAVE_SIDE[1], WAVE_OWN[1]

    def initial(index, x):
        layout = (
            ((messages, 0, 4), (messages, tiles, 3)),
            ((messages, PLANES, 3), (messages, tiles + 24, 2)),
        )[index]
        own = ((p_ref, 0), (late_ref, 0))[index]
        value = widened(own, (late_ref, own_tiles + 32 * index), x, layout, side)
        if index == 1:
            value = less_plane_below(value, x, late_ref, WAVE_OWN, messages, WAVE_SIDE, side)
        return value

    own_strip = late_ref[WAVE_OWN[2] : WAVE_OWN[2] + EY]
    p_s, s_s = (
        whole_strip(own_strip, messages, WAVE_SIDE[2], slot, side) for slot in range(2)
    )
    s_s = s_s - strip_below(own_strip, messages, WAVE_SIDE[2], 2, side)
    stiff_s, buoy_s, damp_s = coef_strip_ref[0], coef_strip_ref[1], coef_strip_ref[2]

    for step in range(1, STEPS + 1):
        k = step - 1
        edge_up = p_s * cut_up
        flux_s, spread = strip_flux(p_s, buoy_s)
        edge_down = flux_s * cut_down
        if step < STEPS:
            s_s = s_s - spread
            p_s = damp_s * (p_s - stiff_s * s_s) + ss_ref[k]

        def pressure(x):
            return initial(0, x) if step == 1 else field[0, x]

        flux_below = None
        p_now = pressure(step - 1)
        for x in range(step - 1, EX - step):
            p_next = pressure(x + 1)
            buoyancy = coef_ref[1, x]
            slope_x = p_next - p_now
            flux_x = buoyancy * slope_x
            if x >= step:
                slope_y = y_up(p_now) - p_now
                slope_z = z_up(p_now, edge_up, x) - p_now
                flux_y = buoyancy * slope_y
                flux_z = buoyancy * slope_z
                spread = (flux_x - flux_below) + (flux_y - y_down(flux_y))
                spread = spread + (flux_z - z_down(flux_z, edge_down, x))
                spread = (initial(1, x) if step == 1 else field[1, x]) - spread
                if step < STEPS:
                    field[1, x] = spread
                    field[0, x] = (
                        coef_ref[2, x] * (p_now - coef_ref[0, x] * spread)
                        + s_ref[k, x - SOURCE_PLANES[0]]
                    )
                if BX <= x < 2 * BX:
                    place = x - BX
                    term = hist_ref[k, 0, place] * spread[0:BY]
                    grad_ref[0, place] = -term if k == 0 else grad_ref[0, place] - term
                    term = hist_ref[k, 1, place] * slope_x[0:BY]
                    term = term + hist_ref[k, 2, place] * slope_y[0:BY]
                    term = term + hist_ref[k, 3, place] * slope_z[0:BY]
                    grad_ref[1, place] = -term if k == 0 else grad_ref[1, place] - term
            flux_below = flux_x
            p_now = p_next


def shape(*dims):
    return jax.ShapeDtypeStruct(dims, F32)


def call(kernel, outs, operands, scratch, places, micros=0.1):
    spaces = {"h": pltpu.HBM, "a": pl.ANY, "v": pltpu.VMEM}
    operands = [
        pltpu.with_memory_space_constraint(operand, pltpu.HBM) if place == "h" else operand
        for operand, place in zip(operands, places)
    ]
    return pl.pallas_call(
        kernel,
        out_shape=outs,
        in_specs=[pl.BlockSpec(memory_space=spaces[place]) for place in places],
        out_specs=[pl.BlockSpec(memory_space=pltpu.VMEM)] * len(outs),
        scratch_shapes=scratch,
        compiler_params=pltpu.CompilerParams(vmem_limit_bytes=VMEM_LIMIT),
        cost_estimate=pl.CostEstimate(
            flops=0, bytes_accessed=int(3.69e6 * micros), transcendentals=0
        ),
    )(*operands)


def from_sides(sends, axes):
    count = lax.axis_size("gy")

    def route(offset):
        pairs = []
        for target in range(count):
            source = target + offset
            if 0 <= source < count:
                if "gz" in axes:
                    pairs += [(2 * source + z, 2 * target + 1 - z) for z in range(2)]
                else:
                    pairs.append((source, target))
        return pairs

    if count == 2:
        both = lax.ppermute(sends[0], axes, route(1) + route(-1))
        return both, both
    upward, downward = sends
    return lax.ppermute(downward, axes, route(1)), lax.ppermute(upward, axes, route(-1))


def rotated(array, axis, offset):
    count = lax.axis_size(axis)
    return lax.ppermute(array, axis, [((i + offset) % count, i) for i in range(count)])


def paired(array, odd):
    count = lax.axis_size("gx")
    pairs = []
    for i in range(count):
        partner = ((i - 1) ^ 1) + 1 if odd else i ^ 1
        pairs.append((partner if 0 <= partner < count else i, i))
    return lax.ppermute(array, "gx", pairs)


def local(
    stored, adjoint_end, labels, tissue, source_cells, source_wave, receiver_cells, receiver_wave
):
    assert lax.axis_size("gz") == 2 and labels.shape == (BX, BY, BZ) and tissue.shape[1] == 8
    half = lax.axis_size("gx") // 2
    arguments = [
        stored, adjoint_end, labels, tissue,
        receiver_cells.T, receiver_wave, source_cells.T, source_wave,
    ]
    ways = 1 if lax.axis_size("gy") == 2 else 2
    p, ql, s, t, last_x, last_y, strips, table, receivers, receiver_wave, sources, source_wave, *sends = call(
        load_kernel,
        [
            shape(PLANES, BZ),
            shape(2 * PLANES, BZ),
            shape(PLANES, BZ),
            shape(PLANES, BZ),
            shape(2 * BY, BZ),
            shape(2 * BX * 8, BZ),
            shape(3 * BY, BZ),
            shape(24, BZ),
        ]
        + [jax.ShapeDtypeStruct(array.shape, array.dtype) for array in arguments[4:]]
        + [shape(20 * 8, BZ)] * ways
        + [shape(2 * 8, BZ)] * ways,
        arguments,
        [
            pltpu.VMEM(stored.shape, F32),
            pltpu.VMEM(adjoint_end.shape, F32),
            pltpu.VMEM(labels.shape, jnp.int32),
            pltpu.SMEM(tissue.shape, F32),
            pltpu.SemaphoreType.DMA,
        ],
        "hhhhhhhh",
        1.4,
    )
    from_up, from_down = from_sides(sends[:ways], "gy")
    other = rotated(strips, "gz", 1)
    corner_up, corner_down = from_sides(sends[ways:], ("gy", "gz"))
    p = rotated(p, "gx", half)
    rb, rsb = call(
        late_kernel,
        [shape(2, EX * EY, BZ), shape(2, EY, BZ)],
        [receivers, receiver_wave],
        [],
        "vv",
        1.2,
    )
    early_planes, source_planes = (last - first for first, last in (EARLY_PLANES, SOURCE_PLANES))
    late, adj_late, token = call(
        merge_kernel,
        [shape(WAVE_OWN[2] + EY, BZ), shape(ADJ_OWN[2] + EY, BZ), shape(8, BZ)],
        [from_up, from_down, corner_up, corner_down, strips, other, s, t, last_x, last_y, rsb, p],
        [],
        "vvvvvvvvvvaa",
    )
    late = rotated(late, "gx", half)
    token = rotated(token, "gz", 1)
    ra, rsa = call(
        early_kernel,
        [shape(2, early_planes * EY, BZ), shape(2, EY, BZ)],
        [receivers, receiver_wave, adj_late],
        [],
        "vva",
        1.0,
    )
    ra, rb = ra.reshape(2, early_planes, EY, BZ), rb.reshape(2, EX, EY, BZ)
    even, odd, second = call(
        adjoint_join_kernel,
        [shape(ADJ_SIDE[2] + EY + 2 * PLANES, BZ)] * 2 + [shape(8, BZ)],
        [ql, adj_late, token],
        [],
        "vva",
    )
    even, odd = paired(even, False), paired(odd, True)
    second = rotated(second, "gz", 1)
    src, src_strip = call(
        source_kernel,
        [shape(STEPS - 1, source_planes * EY, BZ), shape(STEPS - 1, EY, BZ)],
        [sources, source_wave, second],
        [],
        "vva",
        0.5,
    )
    src = src.reshape(STEPS - 1, source_planes, EY, BZ)
    wave_even, wave_odd = call(
        join_kernel,
        [shape(WAVE_SIDE[2] + EY, BZ)] * 2,
        [p, late, second],
        [],
        "vva",
    )
    wave_even, wave_odd = paired(wave_even, False), paired(wave_odd, True)
    adjoint_start, hist, coef, coef_strip = call(
        adjoint_kernel,
        [
            shape(4, BX, BY, BZ),
            shape(STEPS, 4, BX, BY, BZ),
            shape(3, EX, EY, BZ),
            shape(3, EY, BZ),
        ],
        [ql, adj_late, even, odd, adjoint_end, ra, rsa, rb, rsb, table],
        [pltpu.VMEM((2, EX, EY, BZ), F32), pltpu.SemaphoreType.DMA],
        "vvvvhvvvvv",
        3.9,
    )
    (gradient,) = call(
        forward_kernel,
        [shape(2, BX, BY, BZ)],
        [p, late, wave_even, wave_odd, coef, coef_strip, src, src_strip, hist],
        [pltpu.VMEM((2, EX, EY, BZ), F32)],
        "vvvvvvvvv",
        2.5,
    )
    return gradient, adjoint_start


def solution(mesh):
    return jax.shard_map(
        local,
        mesh=mesh,
        in_specs=(
            P("shot", "gx", "gy", "gz"),
            P("shot", "gx", "gy", "gz"),
            P("gx", "gy", "gz"),
            P(),
            P("shot", None),
            P(None, "shot"),
            P(),
            P(None, "shot"),
        ),
        out_specs=(P("shot", "gx", "gy", "gz"), P("shot", "gx", "gy", "gz")),
        check_vma=False,
    )
```

```python
import jax
import jax.numpy as jnp
from jax import lax
from jax.experimental import pallas as pl
from jax.experimental.pallas import tpu as pltpu
from jax.sharding import PartitionSpec as P

STEPS = 4
MARGIN = 4
BX, BY, BZ = 4, 32, 128
EX, EY = BX + 2 * MARGIN, BY + 2 * MARGIN
STRIP = 2 * MARGIN
F32 = jnp.float32
BF16 = jnp.bfloat16
VMEM_LIMIT = 16 * 1024 * 1024
PLANES = BX * BY
WAVE_OWN = (PLANES, PLANES + BY, PLANES + BY + 9 * 8)
ADJ_OWN = (PLANES, PLANES + BY, PLANES + BY + 13 * 8)
WAVE_SIDE = (PLANES + 3 * BY, PLANES + 4 * BY, PLANES + 4 * BY + 6 * 8)
ADJ_SIDE = (3 * BY, 4 * BY, 4 * BY + 9 * 8)


def lanes(shape):
    return lax.broadcasted_iota(jnp.int32, shape, len(shape) - 1)


def rows(shape):
    return lax.broadcasted_iota(jnp.int32, shape, len(shape) - 2)


def run(copies):
    for copy in copies:
        copy.start()
    for copy in copies:
        copy.wait()


def coefficients(labels, table_ref):
    result = [jnp.zeros(labels.shape, F32) for _ in range(3)]
    for index in range(8):
        picked = labels == float(index + 1)
        for kind in range(3):
            row = kind * 8 + index
            result[kind] = jnp.where(picked, table_ref[row : row + 1], result[kind])
    return result


def buoyancy_of(labels, table_ref):
    result = jnp.zeros(labels.shape, F32)
    for index in range(8):
        result = jnp.where(labels == float(index + 1), table_ref[8 + index : 9 + index], result)
    return result


def half_turn(tile):
    return pltpu.roll(tile, MARGIN, 0)


def load_kernel(
    stored_hbm, adj_hbm, lab_hbm, tissue_hbm, rc_hbm, rw_hbm, sc_hbm, sw_hbm,
    p_ref, ql_ref, s_ref, t_ref, last_x_ref, last_y_ref, strip_ref, table_ref,
    rc_ref, rw_ref, sc_ref, sw_ref, *rest,
):
    *sends, stored, adj, lab, tissue, sem = rest
    run([
        pltpu.make_async_copy(source, target, sem)
        for source, target in (
            (stored_hbm, stored), (adj_hbm, adj), (lab_hbm, lab), (tissue_hbm, tissue),
            (rc_hbm, rc_ref), (rw_hbm, rw_ref), (sc_hbm, sc_ref), (sw_hbm, sw_ref),
        )
    ])
    for index in range(tissue.shape[1]):
        speed = jnp.full((1, BZ), tissue[0, index], F32)
        density = jnp.full((1, BZ), tissue[1, index], F32)
        table_ref[index : index + 1] = density * speed
        table_ref[8 + index : 9 + index] = speed / density
        table_ref[16 + index : 17 + index] = 1.0 - jnp.full((1, BZ), tissue[2, index], F32)
    gy, gz = lax.axis_index("gy"), lax.axis_index("gz")
    lane = lanes((BY, BZ))
    row = rows((BY, BZ))
    tile_row = rows((8, BZ))
    strips = [jnp.zeros((BY, BZ), F32) for _ in range(3)]
    tiles = [None] * 39
    previous = [None, None]

    def edge_tile(block):
        return jnp.where(tile_row < MARGIN, block[0:8], block[BY - 8 : BY])

    for x in range(BX):
        labels = lab[x].astype(F32) + 1.0
        buoyancy = buoyancy_of(labels, table_ref)
        plane = slice(x * BY, x * BY + BY)
        fields = [stored[index, x] for index in range(4)] + [adj[0, x]]
        fields += [buoyancy * adj[index, x] for index in range(1, 4)] + [labels]
        p_ref[plane] = fields[0]
        ql_ref[plane] = fields[4]
        ql_ref[PLANES + x * BY : PLANES + x * BY + BY] = labels
        for index, block in enumerate(fields):
            tiles[index * BX + x] = edge_tile(block)
            group, slot = divmod(index, 4)
            base = slot * BX * STRIP + x * STRIP
            rolled = pltpu.roll(block, base + MARGIN, 1)
            first = base + MARGIN * gz
            strips[group] = jnp.where(
                (lane >= first) & (lane < first + MARGIN), rolled, strips[group]
            )
        for kind, target in enumerate((s_ref, t_ref)):
            vx, vy, vz = fields[4 * kind + 1 : 4 * kind + 4]
            spread = vx if x == 0 else vx - previous[kind]
            spread = spread + (vy - jnp.where(row == 0, 0.0, pltpu.roll(vy, 1, 0)))
            spread = spread + (vz - jnp.where(lane == 0, 0.0, pltpu.roll(vz, 1, 1)))
            target[plane] = spread
            previous[kind] = vx
            index = (kind * BX + x) * 8
            last_y_ref[index : index + 8] = vy[BY - 8 : BY]
    for kind in range(2):
        last_x_ref[kind * BY : kind * BY + BY] = previous[kind]
    for group in range(3):
        strip_ref[group * BY : group * BY + BY] = strips[group]
        tiles[9 * BX + group] = edge_tile(strips[group])

    def joined(first, second):
        second = first if second is None else second
        upward = jnp.where(tile_row < MARGIN, half_turn(first), second)
        downward = jnp.where(tile_row < MARGIN, first, half_turn(second))
        if len(sends) == 2:
            return (jnp.where(gy == 0, upward, downward),)
        return upward, downward

    tiles.append(None)
    half = len(sends) // 2
    for place in range(20):
        for target, tile in zip(sends[:half], joined(tiles[2 * place], tiles[2 * place + 1])):
            target[place * 8 : place * 8 + 8] = tile
    for place in range(2):
        first = tiles[9 * BX + 2 * place]
        for target, tile in zip(sends[half:], joined(first, tiles[9 * BX + 2 * place + 1])):
            target[place * 8 : place * 8 + 8] = tile


def copy_rows(target, base, source, first, count):
    target[base : base + count] = source[pl.ds(pl.multiple_of(first, 8), count)]
    return base + count


def pair_planes():
    parity = lax.rem(lax.axis_index("gx"), 2)
    return 1 - parity, parity


def merge_kernel(
    from_up, from_down, corner_up, corner_down, strip_ref, other_ref,
    s_ref, t_ref, last_x_ref, last_y_ref, _,
    wave_ref, adj_ref, token_ref,
):
    token_ref[...] = jnp.zeros((8, BZ), F32)
    gy = lax.axis_index("gy")
    tile_row = rows((8, BZ))
    row, lane = rows((BY, BZ)), lanes((BY, BZ))
    take_up = (tile_row < MARGIN) & (gy < lax.axis_size("gy") - 1)
    take_down = (tile_row >= MARGIN) & (gy > 0)
    _, cut_down = cut_flags()

    def halo(up, down, index):
        place, second = divmod(index, 2)
        sl = slice(place * 8, place * 8 + 8)
        above = half_turn(up[sl]) if second else up[sl]
        below = down[sl] if second else half_turn(down[sl])
        return jnp.where(take_up, above, jnp.where(take_down, below, 0.0))

    wide = []
    for group in range(3):
        sl = slice(group * BY, group * BY + BY)
        tile = halo(from_up, from_down, 9 * BX + group) + halo(corner_up, corner_down, group)
        wide.append(jnp.concatenate([strip_ref[sl] + other_ref[sl], tile], 0))
    strip_lane = lanes((EY, BZ))

    def strip_field(index):
        group, slot = divmod(index, 4)
        moved = pltpu.roll(wide[group], (BZ - slot * BX * STRIP) % BZ, 1) if slot else wide[group]
        return jnp.where(strip_lane < BX * STRIP, moved, 0.0)

    last_lanes = (BX - 1) * STRIP
    for kind, (source, target) in enumerate(((s_ref, wave_ref), (t_ref, adj_ref))):
        first = 4 * kind
        planes_end, x_end, tiles_end = (WAVE_OWN, ADJ_OWN)[kind]
        vx, vy, vz = (strip_field(first + 1 + axis) for axis in range(3))
        spread = vx - jnp.where(strip_lane < STRIP, 0.0, pltpu.roll(vx, STRIP, 1))
        spread = (spread + (vy - y_down(vy))) + (vz - pltpu.roll(vz, 1, 1))
        strip = strip_field(first)
        strip = strip + pltpu.roll(jnp.where(strip_lane < BX * STRIP, spread, 0.0), BX * STRIP, 1)
        last_slot = 2
        if kind == 1:
            strip = strip + pltpu.roll(strip_field(8), 2 * BX * STRIP, 1)
            last_slot = 3
        last = jnp.where(strip_lane >= last_lanes, vx, 0.0)
        strip = strip + pltpu.roll(last, last_slot * BX * STRIP - last_lanes, 1)
        target[tiles_end : tiles_end + EY] = strip
        target[planes_end:x_end] = last_x_ref[kind * BY : kind * BY + BY]

        vx_before = None
        for x in range(BX):
            vx_t, vy_t, vz_t = (
                halo(from_up, from_down, (first + 1 + axis) * BX + x) for axis in range(3)
            )
            below_z = pltpu.roll(vz, (BZ - (x * STRIP + MARGIN - 1)) % BZ, 1) * cut_down
            last_y = last_y_ref[(kind * BX + x) * 8 : (kind * BX + x) * 8 + 8]
            y_before = jnp.where(
                tile_row == 0, pltpu.roll(last_y, 1, 0), pltpu.roll(vy_t, 1, 0)
            )
            z_before = jnp.where(lane[0:8] == 0, below_z[BY:EY], pltpu.roll(vz_t, 1, 1))
            spread = vx_t if x == 0 else vx_t - vx_before
            spread = (spread + (vy_t - y_before)) + (vz_t - z_before)
            vx_before = vx_t
            block = source[x * BY : x * BY + BY]
            block = block - jnp.where(row == 0, vy_t[7:8], 0.0)
            block = block - jnp.where(lane == 0, below_z[0:BY], 0.0)
            target[x * BY : x * BY + BY] = block
            base = x_end + x * 8
            target[base : base + 8] = halo(from_up, from_down, first * BX + x)
            target[base + 32 : base + 40] = spread
            if kind == 1:
                target[base + 64 : base + 72] = halo(from_up, from_down, 8 * BX + x)
        target[tiles_end - 8 : tiles_end] = vx_before


def adjoint_join_kernel(ql_ref, adj_ref, _a, _b, even_ref, odd_ref, token_ref):
    token_ref[...] = jnp.zeros((8, BZ), F32)
    planes_end, x_end, tiles_end = ADJ_OWN
    for target, first in zip((even_ref, odd_ref), pair_planes()):
        base = copy_rows(target, 0, adj_ref, first * BY, 3 * BY)
        base = copy_rows(target, base, adj_ref, planes_end, BY)
        base = copy_rows(target, base, adj_ref, x_end + first * 8, 24)
        base = copy_rows(target, base, adj_ref, x_end + 32 + first * 16, 16)
        base = copy_rows(target, base, adj_ref, x_end + 64 + first * 8, 24)
        base = copy_rows(target, base, adj_ref, tiles_end - 8, 8 + EY)
        copy_rows(target, base, ql_ref, 0, 2 * PLANES)


def join_kernel(p_ref, wave_ref, _, even_ref, odd_ref):
    planes_end, x_end, tiles_end = WAVE_OWN
    for target, first in zip((even_ref, odd_ref), pair_planes()):
        base = copy_rows(target, 0, p_ref, 0, PLANES)
        base = copy_rows(target, base, wave_ref, first * BY, 3 * BY)
        base = copy_rows(target, base, wave_ref, planes_end, BY)
        base = copy_rows(target, base, wave_ref, x_end + first * 8, 24)
        base = copy_rows(target, base, wave_ref, x_end + 32 + first * 16, 16)
        copy_rows(target, base, wave_ref, tiles_end - 8, 8 + EY)


def split(values):
    high = values.astype(BF16)
    rest = values - high.astype(F32)
    middle = rest.astype(BF16)
    low = (rest - middle.astype(F32)).astype(BF16)
    return high, middle, low


def places(cells, sl):
    gx, gy, gz = (lax.axis_index(name) for name in ("gx", "gy", "gz"))
    cut = BZ * lax.axis_size("gz") // 2 - MARGIN
    cell_x = cells[0:1, sl] - (gx * BX - MARGIN)
    cell_y = cells[1:2, sl] - gy * BY
    cell_z = cells[2:3, sl]
    in_x = (cell_x >= 0) & (cell_x < EX)
    in_y = (cell_y >= -MARGIN) & (cell_y < BY + MARGIN)
    row = jnp.where(cell_y < 0, cell_y + EY, cell_y)
    flat = jnp.where(in_x & in_y, cell_x * EY + row, -1)
    row = jnp.where(in_y, row, -1)
    zz = cell_z - cut
    in_strip = in_x & (zz >= 0) & (zz < STRIP)
    strip_lane = jnp.where(in_strip, cell_x * STRIP + zz, -1)
    return flat, cell_z - gz * BZ, row, strip_lane


def hits(count, index):
    return rows((count, index.shape[1])) == index


def product(left, right):
    return lax.dot_general(
        left, right, (((1,), (1,)), ((), ())), preferred_element_type=F32
    )


def inject_points(cells, wave_ref, width, waves, planes, out_ref, strip_out_ref):
    count, low, total_rows = len(waves), planes[0] * EY, (planes[1] - planes[0]) * EY
    for start in range(0, cells.shape[1], width):
        sl = slice(start, start + width)
        flat, z, row, strip_lane = places(cells, sl)
        here = hits(total_rows, flat - low).astype(F32).astype(BF16)
        at_strip = hits(BZ, strip_lane).astype(F32).astype(BF16)
        at_z, at_row = hits(BZ, z), hits(EY, row)
        total = strip_total = None
        parts = [split(wave_ref[wave : wave + 1, sl]) for wave in waves]
        for part in range(3):
            amounts = [parts[wave][part].astype(F32) for wave in range(count)]
            right = jnp.concatenate([jnp.where(at_z, a, 0.0) for a in amounts], 0).astype(BF16)
            left = jnp.concatenate([jnp.where(at_row, a, 0.0) for a in amounts], 0).astype(BF16)
            term, strip_term = product(here, right), product(left, at_strip)
            total = term if part == 0 else total + term
            strip_total = strip_term if part == 0 else strip_total + strip_term
        for wave in range(count):
            value = total[:, wave * BZ : wave * BZ + BZ]
            strip_value = strip_total[wave * EY : wave * EY + EY]
            if start > 0:
                value = value + out_ref[wave]
                strip_value = strip_value + strip_out_ref[wave]
            out_ref[wave] = value
            strip_out_ref[wave] = strip_value


LATE_PLANES, EARLY_PLANES, SOURCE_PLANES = (0, EX), (2, EX - 2), (1, EX - 1)


def late_kernel(receivers, receiver_wave, r_ref, rs_ref):
    inject_points(receivers, receiver_wave, 256, (2, 3), LATE_PLANES, r_ref, rs_ref)


def early_kernel(receivers, receiver_wave, _, r_ref, rs_ref):
    inject_points(receivers, receiver_wave, 256, (0, 1), EARLY_PLANES, r_ref, rs_ref)


def source_kernel(sources, source_wave, _, s_ref, ss_ref):
    width = sources.shape[1]
    inject_points(sources, source_wave, width, (0, 1, 2), SOURCE_PLANES, s_ref, ss_ref)


def strip_of(packed, block, slot):
    lane = lanes(packed.shape)
    width = BX * STRIP
    shift = (block * width - slot * width) % BZ
    moved = pltpu.roll(packed, shift, 1) if shift else packed
    return jnp.where((lane >= block * width) & (lane < (block + 1) * width), moved, 0.0)


def y_up(v):
    return pltpu.roll(v, EY - 1, 0)


def y_down(v):
    return pltpu.roll(v, 1, 0)


def z_up(v, edge):
    return jnp.where(lanes(v.shape) == BZ - 1, edge, pltpu.roll(v, BZ - 1, 1))


def z_down(v, edge):
    return jnp.where(lanes(v.shape) == 0, edge, pltpu.roll(v, 1, 1))


def cut_edges(values, flux_z, cut_up, cut_down):
    place = lax.rem(lanes(values.shape), STRIP)
    above = jnp.where(place == MARGIN, values * cut_up, 0.0)
    below = jnp.where(place == MARGIN - 1, flux_z * cut_down, 0.0)
    return pltpu.roll(above, BZ - 2, 1) + below


def plane_edge(edges, x):
    return pltpu.roll(edges, (BZ - (x * STRIP + MARGIN - 1)) % BZ, 1)


def strip_flux(values, buoyancy):
    flux_x = buoyancy * (pltpu.roll(values, BZ - STRIP, 1) - values)
    flux_y = buoyancy * (y_up(values) - values)
    flux_z = buoyancy * (pltpu.roll(values, BZ - 1, 1) - values)
    spread = (flux_x - pltpu.roll(flux_x, STRIP, 1)) + (flux_y - y_down(flux_y))
    return flux_z, spread + (flux_z - pltpu.roll(flux_z, 1, 1))


def cut_flags():
    gz, half = lax.axis_index("gz"), lax.axis_size("gz") // 2
    return jnp.where(gz == half - 1, 1.0, 0.0), jnp.where(gz == half, 1.0, 0.0)


def sides():
    gx = lax.axis_index("gx")
    low = jnp.where(gx > 0, 1.0, 0.0)
    high = jnp.where(gx < lax.axis_size("gx") - 1, 1.0, 0.0)
    return low, high, lax.rem(gx, 2) == 0


def from_side(messages, first, count, block, side):
    even, odd = (message[first : first + count] for message in messages)
    low, high, even_above = side
    if block == 0:
        return jnp.where(even_above, odd, even) * low
    return jnp.where(even_above, even, odd) * high


def side_rows(base, wanted, step, block):
    planes = range(BX - wanted, BX) if block == 0 else range(wanted)
    return {plane: base + place * step for place, plane in enumerate(planes)}


def widened(own, own_tiles, x, layout, side):
    block, plane = divmod(x, BX)
    if block == 1:
        main = own[0][own[1] + plane * BY : own[1] + plane * BY + BY]
        tile = own_tiles[0][own_tiles[1] + plane * 8 : own_tiles[1] + plane * 8 + 8]
        return jnp.concatenate([main, tile], 0)
    parts = []
    for (messages, base, wanted), count in zip(layout, (BY, 8)):
        first = side_rows(base, wanted, count, block).get(plane)
        if first is None:
            parts.append(jnp.zeros((count, BZ), F32))
        else:
            parts.append(from_side(messages, first, count, block, side))
    return jnp.concatenate(parts, 0)


def less_plane_below(value, x, own_ref, own_rows, messages, side_rows_of, side):
    if x == BX:
        planes_end, _, tiles_end = side_rows_of
        main = from_side(messages, planes_end, BY, 0, side)
        tile = from_side(messages, tiles_end - 8, 8, 0, side)
    elif x == 2 * BX:
        planes_end, _, tiles_end = own_rows
        high = side[1]
        main = own_ref[planes_end : planes_end + BY] * high
        tile = own_ref[tiles_end - 8 : tiles_end] * high
    else:
        return value
    return value - jnp.concatenate([main, tile], 0)


def strip_below(own, messages, first, slot, side):
    lane = lanes(own.shape)
    width = BX * STRIP
    low = from_side(messages, first, EY, 0, side)
    low = pltpu.roll(low, (width - slot * width) % BZ, 1)
    own = pltpu.roll(own * side[1], (2 * width - slot * width) % BZ, 1)
    in_own = (lane >= width) & (lane < width + STRIP)
    in_high = (lane >= 2 * width) & (lane < 2 * width + STRIP)
    return jnp.where(in_own, low, jnp.where(in_high, own, 0.0))


def whole_strip(own, messages, first, slot, side):
    low = from_side(messages, first, EY, 0, side)
    high = from_side(messages, first, EY, 2, side)
    return strip_of(low, 0, slot) + strip_of(own, 1, slot) + strip_of(high, 2, slot)


def adjoint_kernel(
    ql_ref, late_ref, even, odd, adj_hbm, ra_ref, rsa_ref, rb_ref, rsb_ref,
    table_ref,
    out_ref, hist_ref, coef_ref, coef_strip_ref,
    q_ref, t_ref, u_ref, scale_ref, edge_ref, flux_ref, w_sem,
):
    w_copy = pltpu.make_async_copy(adj_hbm.at[pl.ds(1, 3)], out_ref.at[pl.ds(1, 3)], w_sem)
    w_copy.start()
    cut_up, cut_down = cut_flags()
    side = sides()
    messages = (even, odd)
    r_refs = ((ra_ref, 0), (ra_ref, 1), (rb_ref, 0), (rb_ref, 1))
    rs_refs = ((rsa_ref, 0), (rsa_ref, 1), (rsb_ref, 0), (rsb_ref, 1))
    tiles, own_tiles, raws = ADJ_SIDE[1], ADJ_OWN[1], ADJ_SIDE[2] + EY

    def initial(index, x):
        own = ((ql_ref, 0), (late_ref, 0), (ql_ref, PLANES))[index]
        layout = (
            ((messages, raws, 4), (messages, tiles, 3)),
            ((messages, 0, 3), (messages, tiles + 24, 2)),
            ((messages, raws + PLANES, 4), (messages, tiles + 40, 3)),
        )[index]
        value = widened(own, (late_ref, own_tiles + 32 * index), x, layout, side)
        if index == 1:
            value = less_plane_below(value, x, late_ref, ADJ_OWN, messages, ADJ_SIDE, side)
        return value

    for x in range(EX):
        stiff, buoy, damp = coefficients(initial(2, x), table_ref)
        coef_ref[0, x], coef_ref[1, x], coef_ref[2, x] = stiff, buoy, damp
        scale_ref[x] = stiff * damp
    own_strip = late_ref[ADJ_OWN[2] : ADJ_OWN[2] + EY]
    q_s, t_s, label_s = (
        whole_strip(own_strip, messages, ADJ_SIDE[2], slot, side) for slot in range(3)
    )
    t_s = t_s - strip_below(own_strip, messages, ADJ_SIDE[2], 3, side)
    stiff_s, buoy_s, damp_s = coefficients(label_s, table_ref)
    coef_strip_ref[0], coef_strip_ref[1], coef_strip_ref[2] = stiff_s, buoy_s, damp_s
    w_copy.wait()

    for step in range(1, STEPS + 1):
        k = STEPS - step
        rs_ref, place = rs_refs[k]
        q_s = q_s + rs_ref[place]
        u_s = stiff_s * damp_s * q_s
        flux_s, spread = strip_flux(u_s, buoy_s)
        t_s = t_s + spread
        q_s = damp_s * q_s + t_s
        edges = cut_edges(u_s, flux_s, cut_up, cut_down)
        r_ref, place = r_refs[k]
        r_first = (EARLY_PLANES if k < 2 else LATE_PLANES)[0]

        for x in range(step - 1, EX - step + 1):
            q = (initial(0, x) if step == 1 else q_ref[x]) + r_ref[place, x - r_first]
            q_ref[x] = q
            u_ref[x] = scale_ref[x] * q
            if step <= x < EX - step:
                edge_ref[x] = plane_edge(edges, x)

        for x in range(step - 1, EX - step):
            u, buoyancy = u_ref[x], coef_ref[1, x]
            slopes = [u_ref[x + 1] - u]
            if x >= step:
                slopes += [y_up(u) - u, z_up(u, edge_ref[x]) - u]
            for axis, slope in enumerate(slopes):
                flux_ref[axis, x] = buoyancy * slope
            if BX <= x < 2 * BX:
                for axis, slope in enumerate(slopes):
                    w = out_ref[1 + axis, x - BX] + slope[0:BY]
                    out_ref[1 + axis, x - BX] = w
                    hist_ref[k, 1 + axis, x - BX] = w

        for x in range(step, EX - step):
            flux_y, flux_z = flux_ref[1, x], flux_ref[2, x]
            spread = (flux_ref[0, x] - flux_ref[0, x - 1]) + (flux_y - y_down(flux_y))
            spread = spread + (flux_z - z_down(flux_z, edge_ref[x]))
            damped = coef_ref[2, x] * q_ref[x]
            t = (initial(1, x) if step == 1 else t_ref[x]) + spread
            if BX <= x < 2 * BX:
                hist_ref[k, 0, x - BX] = damped[0:BY]
            if step < STEPS:
                t_ref[x] = t
                q_ref[x] = damped + t
            else:
                out_ref[0, x - BX] = (damped + t)[0:BY]


def forward_kernel(
    own_p_ref, late_ref, even, odd, coef_ref, coef_strip_ref, s_ref, ss_ref, hist_ref,
    grad_ref,
    p_ref, spread_ref, edge_ref, flux_ref,
):
    cut_up, cut_down = cut_flags()
    side = sides()
    messages = (even, odd)
    tiles, own_tiles = WAVE_SIDE[1], WAVE_OWN[1]

    def initial(index, x):
        layout = (
            ((messages, 0, 4), (messages, tiles, 3)),
            ((messages, PLANES, 3), (messages, tiles + 24, 2)),
        )[index]
        own = ((own_p_ref, 0), (late_ref, 0))[index]
        value = widened(own, (late_ref, own_tiles + 32 * index), x, layout, side)
        if index == 1:
            value = less_plane_below(value, x, late_ref, WAVE_OWN, messages, WAVE_SIDE, side)
        return value

    own_strip = late_ref[WAVE_OWN[2] : WAVE_OWN[2] + EY]
    p_s, s_s = (
        whole_strip(own_strip, messages, WAVE_SIDE[2], slot, side) for slot in range(2)
    )
    s_s = s_s - strip_below(own_strip, messages, WAVE_SIDE[2], 2, side)
    stiff_s, buoy_s, damp_s = coef_strip_ref[0], coef_strip_ref[1], coef_strip_ref[2]

    for step in range(1, STEPS + 1):
        k = step - 1
        flux_s, spread = strip_flux(p_s, buoy_s)
        edges = cut_edges(p_s, flux_s, cut_up, cut_down)
        if step < STEPS:
            s_s = s_s - spread
            p_s = damp_s * (p_s - stiff_s * s_s) + ss_ref[k]

        for x in range(step - 1, EX - step + 1):
            if step == 1:
                p_ref[x] = initial(0, x)
            if step <= x < EX - step:
                edge_ref[x] = plane_edge(edges, x)

        for x in range(step - 1, EX - step):
            p, buoyancy = p_ref[x], coef_ref[1, x]
            slopes = [p_ref[x + 1] - p]
            if x >= step:
                slopes += [y_up(p) - p, z_up(p, edge_ref[x]) - p]
            for axis, slope in enumerate(slopes):
                flux_ref[axis, x] = buoyancy * slope
            if BX <= x < 2 * BX:
                place = x - BX
                term = hist_ref[k, 1, place] * slopes[0][0:BY]
                term = term + hist_ref[k, 2, place] * slopes[1][0:BY]
                term = term + hist_ref[k, 3, place] * slopes[2][0:BY]
                grad_ref[1, place] = -term if k == 0 else grad_ref[1, place] - term

        for x in range(step, EX - step):
            flux_y, flux_z = flux_ref[1, x], flux_ref[2, x]
            spread = (flux_ref[0, x] - flux_ref[0, x - 1]) + (flux_y - y_down(flux_y))
            spread = spread + (flux_z - z_down(flux_z, edge_ref[x]))
            spread = (initial(1, x) if step == 1 else spread_ref[x]) - spread
            if step < STEPS:
                spread_ref[x] = spread
                p_ref[x] = (
                    coef_ref[2, x] * (p_ref[x] - coef_ref[0, x] * spread)
                    + s_ref[k, x - SOURCE_PLANES[0]]
                )
            if BX <= x < 2 * BX:
                place = x - BX
                term = hist_ref[k, 0, place] * spread[0:BY]
                grad_ref[0, place] = -term if k == 0 else grad_ref[0, place] - term


def shape(*dims):
    return jax.ShapeDtypeStruct(dims, F32)


def call(kernel, outs, operands, scratch, places, micros=0.1):
    spaces = {"h": pltpu.HBM, "a": pl.ANY, "v": pltpu.VMEM}
    operands = [
        pltpu.with_memory_space_constraint(operand, pltpu.HBM) if place == "h" else operand
        for operand, place in zip(operands, places)
    ]
    return pl.pallas_call(
        kernel,
        out_shape=outs,
        in_specs=[pl.BlockSpec(memory_space=spaces[place]) for place in places],
        out_specs=[pl.BlockSpec(memory_space=pltpu.VMEM)] * len(outs),
        scratch_shapes=scratch,
        compiler_params=pltpu.CompilerParams(vmem_limit_bytes=VMEM_LIMIT),
        cost_estimate=pl.CostEstimate(
            flops=0, bytes_accessed=int(3.69e6 * micros), transcendentals=0
        ),
    )(*operands)


def from_sides(sends, axes):
    count = lax.axis_size("gy")

    def route(offset):
        pairs = []
        for target in range(count):
            source = target + offset
            if 0 <= source < count:
                if "gz" in axes:
                    pairs += [(2 * source + z, 2 * target + 1 - z) for z in range(2)]
                else:
                    pairs.append((source, target))
        return pairs

    if count == 2:
        both = lax.ppermute(sends[0], axes, route(1) + route(-1))
        return both, both
    upward, downward = sends
    return lax.ppermute(downward, axes, route(1)), lax.ppermute(upward, axes, route(-1))


def rotated(array, axis, offset):
    count = lax.axis_size(axis)
    return lax.ppermute(array, axis, [((i + offset) % count, i) for i in range(count)])


def paired(array, odd):
    count = lax.axis_size("gx")
    pairs = []
    for i in range(count):
        partner = ((i - 1) ^ 1) + 1 if odd else i ^ 1
        pairs.append((partner if 0 <= partner < count else i, i))
    return lax.ppermute(array, "gx", pairs)


def local(
    stored, adjoint_end, labels, tissue, source_cells, source_wave, receiver_cells, receiver_wave
):
    assert lax.axis_size("gz") == 2 and labels.shape == (BX, BY, BZ) and tissue.shape[1] == 8
    half = lax.axis_size("gx") // 2
    arguments = [
        stored, adjoint_end, labels, tissue,
        receiver_cells.T, receiver_wave, source_cells.T, source_wave,
    ]
    ways = 1 if lax.axis_size("gy") == 2 else 2
    p, ql, s, t, last_x, last_y, strips, table, receivers, receiver_wave, sources, source_wave, *sends = call(
        load_kernel,
        [
            shape(PLANES, BZ),
            shape(2 * PLANES, BZ),
            shape(PLANES, BZ),
            shape(PLANES, BZ),
            shape(2 * BY, BZ),
            shape(2 * BX * 8, BZ),
            shape(3 * BY, BZ),
            shape(24, BZ),
        ]
        + [jax.ShapeDtypeStruct(array.shape, array.dtype) for array in arguments[4:]]
        + [shape(20 * 8, BZ)] * ways
        + [shape(2 * 8, BZ)] * ways,
        arguments,
        [
            pltpu.VMEM(stored.shape, F32),
            pltpu.VMEM(adjoint_end.shape, F32),
            pltpu.VMEM(labels.shape, jnp.int32),
            pltpu.SMEM(tissue.shape, F32),
            pltpu.SemaphoreType.DMA,
        ],
        "hhhhhhhh",
        1.4,
    )
    from_up, from_down = from_sides(sends[:ways], "gy")
    other = rotated(strips, "gz", 1)
    corner_up, corner_down = from_sides(sends[ways:], ("gy", "gz"))
    p = rotated(p, "gx", half)
    rb, rsb = call(
        late_kernel,
        [shape(2, EX * EY, BZ), shape(2, EY, BZ)],
        [receivers, receiver_wave],
        [],
        "vv",
        1.2,
    )
    early_planes, source_planes = (last - first for first, last in (EARLY_PLANES, SOURCE_PLANES))
    late, adj_late, token = call(
        merge_kernel,
        [shape(WAVE_OWN[2] + EY, BZ), shape(ADJ_OWN[2] + EY, BZ), shape(8, BZ)],
        [from_up, from_down, corner_up, corner_down, strips, other, s, t, last_x, last_y, rsb],
        [],
        "vvvvvvvvvva",
    )
    late = rotated(late, "gx", half)
    token = rotated(token, "gz", 1)
    ra, rsa = call(
        early_kernel,
        [shape(2, early_planes * EY, BZ), shape(2, EY, BZ)],
        [receivers, receiver_wave, adj_late],
        [],
        "vva",
        1.0,
    )
    ra, rb = ra.reshape(2, early_planes, EY, BZ), rb.reshape(2, EX, EY, BZ)
    even, odd, second = call(
        adjoint_join_kernel,
        [shape(ADJ_SIDE[2] + EY + 2 * PLANES, BZ)] * 2 + [shape(8, BZ)],
        [ql, adj_late, token, p],
        [],
        "vvaa",
    )
    even, odd = paired(even, False), paired(odd, True)
    second = rotated(second, "gz", 1)
    src, src_strip = call(
        source_kernel,
        [shape(STEPS - 1, source_planes * EY, BZ), shape(STEPS - 1, EY, BZ)],
        [sources, source_wave, second],
        [],
        "vva",
        0.5,
    )
    src = src.reshape(STEPS - 1, source_planes, EY, BZ)
    wave_even, wave_odd = call(
        join_kernel,
        [shape(WAVE_SIDE[2] + EY, BZ)] * 2,
        [p, late, second],
        [],
        "vva",
    )
    wave_even, wave_odd = paired(wave_even, False), paired(wave_odd, True)
    adjoint_start, hist, coef, coef_strip = call(
        adjoint_kernel,
        [
            shape(4, BX, BY, BZ),
            shape(STEPS, 4, BX, BY, BZ),
            shape(3, EX, EY, BZ),
            shape(3, EY, BZ),
        ],
        [ql, adj_late, even, odd, adjoint_end, ra, rsa, rb, rsb, table],
        [pltpu.VMEM((EX, EY, BZ), F32)] * 5
        + [pltpu.VMEM((3, EX, EY, BZ), F32), pltpu.SemaphoreType.DMA],
        "vvvvhvvvvv",
        3.9,
    )
    (gradient,) = call(
        forward_kernel,
        [shape(2, BX, BY, BZ)],
        [p, late, wave_even, wave_odd, coef, coef_strip, src, src_strip, hist],
        [pltpu.VMEM((EX, EY, BZ), F32)] * 3 + [pltpu.VMEM((3, EX, EY, BZ), F32)],
        "vvvvvvvvv",
        2.5,
    )
    return gradient, adjoint_start


def solution(mesh):
    return jax.shard_map(
        local,
        mesh=mesh,
        in_specs=(
            P("shot", "gx", "gy", "gz"),
            P("shot", "gx", "gy", "gz"),
            P("gx", "gy", "gz"),
            P(),
            P("shot", None),
            P(None, "shot"),
            P(),
            P(None, "shot"),
        ),
        out_specs=(P("shot", "gx", "gy", "gz"), P("shot", "gx", "gy", "gz")),
        check_vma=False,
    )
```

```python
import jax
import jax.numpy as jnp
from jax import lax
from jax.experimental import pallas as pl
from jax.experimental.pallas import tpu as pltpu
from jax.sharding import PartitionSpec as P

STEPS = 4
MARGIN = 4
BX, BY, BZ = 4, 32, 128
EX, EY = BX + 2 * MARGIN, BY + 2 * MARGIN
STRIP = 2 * MARGIN
F32 = jnp.float32
BF16 = jnp.bfloat16
VMEM_LIMIT = 16 * 1024 * 1024
PLANES = BX * BY
WAVE_OWN = (0, BY, BY + 9 * 8)
WAVE_FIX = WAVE_OWN[2] + EY
FIX_LANE = 3 * BX * STRIP
ADJ_OWN = (PLANES, PLANES + BY, PLANES + BY + 13 * 8)
WAVE_SIDE = (PLANES + 3 * BY, PLANES + 4 * BY, PLANES + 4 * BY + 6 * 8)
ADJ_SIDE = (3 * BY, 4 * BY, 4 * BY + 9 * 8)


def lanes(shape):
    return lax.broadcasted_iota(jnp.int32, shape, len(shape) - 1)


def rows(shape):
    return lax.broadcasted_iota(jnp.int32, shape, len(shape) - 2)


def run(copies):
    for copy in copies:
        copy.start()
    for copy in copies:
        copy.wait()


def coefficients(labels, table_ref):
    result = [jnp.zeros(labels.shape, F32) for _ in range(3)]
    for index in range(8):
        picked = labels == float(index + 1)
        for kind in range(3):
            row = kind * 8 + index
            result[kind] = jnp.where(picked, table_ref[row : row + 1], result[kind])
    return result


def buoyancy_of(labels, table_ref):
    result = jnp.zeros(labels.shape, F32)
    for index in range(8):
        result = jnp.where(labels == float(index + 1), table_ref[8 + index : 9 + index], result)
    return result


def half_turn(tile):
    return pltpu.roll(tile, MARGIN, 0)


def load_kernel(
    stored_hbm, adj_hbm, lab_hbm, tissue_hbm, rc_hbm, rw_hbm, sc_hbm, sw_hbm,
    wave_ref, ql_ref, t_ref, last_x_ref, last_y_ref, strip_ref, table_ref,
    rc_ref, rw_ref, sc_ref, sw_ref, *rest,
):
    *sends, stored, adj, lab, tissue, sem = rest
    run([
        pltpu.make_async_copy(source, target, sem)
        for source, target in (
            (stored_hbm, stored), (adj_hbm, adj), (lab_hbm, lab), (tissue_hbm, tissue),
            (rc_hbm, rc_ref), (rw_hbm, rw_ref), (sc_hbm, sc_ref), (sw_hbm, sw_ref),
        )
    ])
    for index in range(tissue.shape[1]):
        speed = jnp.full((1, BZ), tissue[0, index], F32)
        density = jnp.full((1, BZ), tissue[1, index], F32)
        table_ref[index : index + 1] = density * speed
        table_ref[8 + index : 9 + index] = speed / density
        table_ref[16 + index : 17 + index] = 1.0 - jnp.full((1, BZ), tissue[2, index], F32)
    gy, gz = lax.axis_index("gy"), lax.axis_index("gz")
    lane = lanes((BY, BZ))
    row = rows((BY, BZ))
    tile_row = rows((8, BZ))
    strips = [jnp.zeros((BY, BZ), F32) for _ in range(3)]
    tiles = [None] * 39
    previous = [None, None]

    def edge_tile(block):
        return jnp.where(tile_row < MARGIN, block[0:8], block[BY - 8 : BY])

    for x in range(BX):
        labels = lab[x].astype(F32) + 1.0
        buoyancy = buoyancy_of(labels, table_ref)
        plane = slice(x * BY, x * BY + BY)
        fields = [stored[index, x] for index in range(4)] + [adj[0, x]]
        fields += [buoyancy * adj[index, x] for index in range(1, 4)] + [labels]
        wave_ref[plane] = fields[0]
        ql_ref[plane] = fields[4]
        ql_ref[PLANES + x * BY : PLANES + x * BY + BY] = labels
        for index, block in enumerate(fields):
            tiles[index * BX + x] = edge_tile(block)
            group, slot = divmod(index, 4)
            base = slot * BX * STRIP + x * STRIP
            rolled = pltpu.roll(block, base + MARGIN, 1)
            first = base + MARGIN * gz
            strips[group] = jnp.where(
                (lane >= first) & (lane < first + MARGIN), rolled, strips[group]
            )
        for kind, (target, base) in enumerate(((wave_ref, PLANES), (t_ref, 0))):
            vx, vy, vz = fields[4 * kind + 1 : 4 * kind + 4]
            spread = vx if x == 0 else vx - previous[kind]
            spread = spread + (vy - jnp.where(row == 0, 0.0, pltpu.roll(vy, 1, 0)))
            spread = spread + (vz - jnp.where(lane == 0, 0.0, pltpu.roll(vz, 1, 1)))
            target[base + x * BY : base + x * BY + BY] = spread
            previous[kind] = vx
            index = (kind * BX + x) * 8
            last_y_ref[index : index + 8] = vy[BY - 8 : BY]
    for kind in range(2):
        last_x_ref[kind * BY : kind * BY + BY] = previous[kind]
    for group in range(3):
        strip_ref[group * BY : group * BY + BY] = strips[group]
        tiles[9 * BX + group] = edge_tile(strips[group])

    def joined(first, second):
        second = first if second is None else second
        upward = jnp.where(tile_row < MARGIN, half_turn(first), second)
        downward = jnp.where(tile_row < MARGIN, first, half_turn(second))
        if len(sends) == 2:
            return (jnp.where(gy == 0, upward, downward),)
        return upward, downward

    tiles.append(None)
    half = len(sends) // 2
    for place in range(20):
        for target, tile in zip(sends[:half], joined(tiles[2 * place], tiles[2 * place + 1])):
            target[place * 8 : place * 8 + 8] = tile
    for place in range(2):
        first = tiles[9 * BX + 2 * place]
        for target, tile in zip(sends[half:], joined(first, tiles[9 * BX + 2 * place + 1])):
            target[place * 8 : place * 8 + 8] = tile


def copy_rows(target, base, source, first, count):
    target[base : base + count] = source[pl.ds(pl.multiple_of(first, 8), count)]
    return base + count


def pair_planes():
    parity = lax.rem(lax.axis_index("gx"), 2)
    return 1 - parity, parity


def merge_kernel(
    from_up, from_down, corner_up, corner_down, strip_ref, other_ref,
    t_ref, last_x_ref, last_y_ref, _,
    wave_ref, adj_ref, token_ref,
):
    token_ref[...] = jnp.zeros((8, BZ), F32)
    gy = lax.axis_index("gy")
    tile_row = rows((8, BZ))
    row, lane = rows((BY, BZ)), lanes((BY, BZ))
    take_up = (tile_row < MARGIN) & (gy < lax.axis_size("gy") - 1)
    take_down = (tile_row >= MARGIN) & (gy > 0)
    _, cut_down = cut_flags()

    def halo(up, down, index):
        place, second = divmod(index, 2)
        sl = slice(place * 8, place * 8 + 8)
        above = half_turn(up[sl]) if second else up[sl]
        below = down[sl] if second else half_turn(down[sl])
        return jnp.where(take_up, above, jnp.where(take_down, below, 0.0))

    wide = []
    for group in range(3):
        sl = slice(group * BY, group * BY + BY)
        tile = halo(from_up, from_down, 9 * BX + group) + halo(corner_up, corner_down, group)
        wide.append(jnp.concatenate([strip_ref[sl] + other_ref[sl], tile], 0))
    strip_lane = lanes((EY, BZ))

    def strip_field(index):
        group, slot = divmod(index, 4)
        moved = pltpu.roll(wide[group], (BZ - slot * BX * STRIP) % BZ, 1) if slot else wide[group]
        return jnp.where(strip_lane < BX * STRIP, moved, 0.0)

    last_lanes = (BX - 1) * STRIP
    fix_row = jnp.zeros((8, BZ), F32)
    fix_lane = jnp.zeros((BY, BZ), F32)
    for kind, target in enumerate((wave_ref, adj_ref)):
        first = 4 * kind
        planes_end, x_end, tiles_end = (WAVE_OWN, ADJ_OWN)[kind]
        vx, vy, vz = (strip_field(first + 1 + axis) for axis in range(3))
        spread = vx - jnp.where(strip_lane < STRIP, 0.0, pltpu.roll(vx, STRIP, 1))
        spread = (spread + (vy - y_down(vy))) + (vz - pltpu.roll(vz, 1, 1))
        strip = strip_field(first)
        strip = strip + pltpu.roll(jnp.where(strip_lane < BX * STRIP, spread, 0.0), BX * STRIP, 1)
        last_slot = 2
        if kind == 1:
            strip = strip + pltpu.roll(strip_field(8), 2 * BX * STRIP, 1)
            last_slot = 3
        last = jnp.where(strip_lane >= last_lanes, vx, 0.0)
        strip = strip + pltpu.roll(last, last_slot * BX * STRIP - last_lanes, 1)
        target[planes_end:x_end] = last_x_ref[kind * BY : kind * BY + BY]

        vx_before = None
        for x in range(BX):
            vx_t, vy_t, vz_t = (
                halo(from_up, from_down, (first + 1 + axis) * BX + x) for axis in range(3)
            )
            below_z = pltpu.roll(vz, (BZ - (x * STRIP + MARGIN - 1)) % BZ, 1) * cut_down
            last_y = last_y_ref[(kind * BX + x) * 8 : (kind * BX + x) * 8 + 8]
            y_before = jnp.where(
                tile_row == 0, pltpu.roll(last_y, 1, 0), pltpu.roll(vy_t, 1, 0)
            )
            z_before = jnp.where(lane[0:8] == 0, below_z[BY:EY], pltpu.roll(vz_t, 1, 1))
            spread = vx_t if x == 0 else vx_t - vx_before
            spread = (spread + (vy_t - y_before)) + (vz_t - z_before)
            vx_before = vx_t
            if kind == 0:
                fix_row = jnp.where(tile_row == x, vy_t[7:8], fix_row)
                moved = pltpu.roll(below_z[0:BY], FIX_LANE + x, 1)
                fix_lane = jnp.where(lane == FIX_LANE + x, moved, fix_lane)
            else:
                block = t_ref[x * BY : x * BY + BY]
                block = block - jnp.where(row == 0, vy_t[7:8], 0.0)
                block = block - jnp.where(lane == 0, below_z[0:BY], 0.0)
                target[x * BY : x * BY + BY] = block
            base = x_end + x * 8
            target[base : base + 8] = halo(from_up, from_down, first * BX + x)
            target[base + 32 : base + 40] = spread
            if kind == 1:
                target[base + 64 : base + 72] = halo(from_up, from_down, 8 * BX + x)
        target[tiles_end - 8 : tiles_end] = vx_before
        if kind == 0:
            target[tiles_end : tiles_end + BY] = strip[0:BY] + fix_lane
            target[tiles_end + BY : tiles_end + EY] = strip[BY:EY]
            target[WAVE_FIX : WAVE_FIX + 8] = fix_row
        else:
            target[tiles_end : tiles_end + EY] = strip


def adjoint_join_kernel(ql_ref, adj_ref, _a, _b, even_ref, odd_ref, token_ref):
    token_ref[...] = jnp.zeros((8, BZ), F32)
    planes_end, x_end, tiles_end = ADJ_OWN
    for target, first in zip((even_ref, odd_ref), pair_planes()):
        base = copy_rows(target, 0, adj_ref, first * BY, 3 * BY)
        base = copy_rows(target, base, adj_ref, planes_end, BY)
        base = copy_rows(target, base, adj_ref, x_end + first * 8, 24)
        base = copy_rows(target, base, adj_ref, x_end + 32 + first * 16, 16)
        base = copy_rows(target, base, adj_ref, x_end + 64 + first * 8, 24)
        base = copy_rows(target, base, adj_ref, tiles_end - 8, 8 + EY)
        copy_rows(target, base, ql_ref, 0, 2 * PLANES)


def join_kernel(wave_ref, late_ref, _, s_ref, even_ref, odd_ref):
    planes_end, x_end, tiles_end = WAVE_OWN
    row, lane = rows((BY, BZ)), lanes((BY, BZ))
    fix_lane = late_ref[tiles_end : tiles_end + BY]
    for x in range(BX):
        block = wave_ref[PLANES + x * BY : PLANES + x * BY + BY]
        fix_row = late_ref[WAVE_FIX + x : WAVE_FIX + x + 1]
        block = block - jnp.where(row == 0, fix_row, 0.0)
        block = block - jnp.where(lane == 0, pltpu.roll(fix_lane, BZ - FIX_LANE - x, 1), 0.0)
        s_ref[x * BY : x * BY + BY] = block
    for target, first in zip((even_ref, odd_ref), pair_planes()):
        base = copy_rows(target, 0, wave_ref, 0, PLANES)
        base = copy_rows(target, base, s_ref, first * BY, 3 * BY)
        base = copy_rows(target, base, late_ref, planes_end, BY)
        base = copy_rows(target, base, late_ref, x_end + first * 8, 24)
        base = copy_rows(target, base, late_ref, x_end + 32 + first * 16, 16)
        copy_rows(target, base, late_ref, tiles_end - 8, 8 + EY)


def split(values):
    high = values.astype(BF16)
    rest = values - high.astype(F32)
    middle = rest.astype(BF16)
    low = (rest - middle.astype(F32)).astype(BF16)
    return high, middle, low


def places(cells, sl):
    gx, gy, gz = (lax.axis_index(name) for name in ("gx", "gy", "gz"))
    cut = BZ * lax.axis_size("gz") // 2 - MARGIN
    cell_x = cells[0:1, sl] - (gx * BX - MARGIN)
    cell_y = cells[1:2, sl] - gy * BY
    cell_z = cells[2:3, sl]
    in_x = (cell_x >= 0) & (cell_x < EX)
    in_y = (cell_y >= -MARGIN) & (cell_y < BY + MARGIN)
    row = jnp.where(cell_y < 0, cell_y + EY, cell_y)
    flat = jnp.where(in_x & in_y, cell_x * EY + row, -1)
    row = jnp.where(in_y, row, -1)
    zz = cell_z - cut
    in_strip = in_x & (zz >= 0) & (zz < STRIP)
    strip_lane = jnp.where(in_strip, cell_x * STRIP + zz, -1)
    return flat, cell_z - gz * BZ, row, strip_lane


def hits(count, index):
    return rows((count, index.shape[1])) == index


def product(left, right):
    return lax.dot_general(
        left, right, (((1,), (1,)), ((), ())), preferred_element_type=F32
    )


def inject_points(cells, wave_ref, width, waves, planes, out_ref, strip_out_ref):
    count, low, total_rows = len(waves), planes[0] * EY, (planes[1] - planes[0]) * EY
    for start in range(0, cells.shape[1], width):
        sl = slice(start, start + width)
        flat, z, row, strip_lane = places(cells, sl)
        here = hits(total_rows, flat - low).astype(F32).astype(BF16)
        at_strip = hits(BZ, strip_lane).astype(F32).astype(BF16)
        at_z, at_row = hits(BZ, z), hits(EY, row)
        total = strip_total = None
        parts = [split(wave_ref[wave : wave + 1, sl]) for wave in waves]
        for part in range(3):
            amounts = [parts[wave][part].astype(F32) for wave in range(count)]
            right = jnp.concatenate([jnp.where(at_z, a, 0.0) for a in amounts], 0).astype(BF16)
            left = jnp.concatenate([jnp.where(at_row, a, 0.0) for a in amounts], 0).astype(BF16)
            term, strip_term = product(here, right), product(left, at_strip)
            total = term if part == 0 else total + term
            strip_total = strip_term if part == 0 else strip_total + strip_term
        for wave in range(count):
            value = total[:, wave * BZ : wave * BZ + BZ]
            strip_value = strip_total[wave * EY : wave * EY + EY]
            if start > 0:
                value = value + out_ref[wave]
                strip_value = strip_value + strip_out_ref[wave]
            out_ref[wave] = value
            strip_out_ref[wave] = strip_value


LATE_PLANES, EARLY_PLANES, SOURCE_PLANES = (0, EX), (2, EX - 2), (1, EX - 1)


def late_kernel(receivers, receiver_wave, r_ref, rs_ref):
    inject_points(receivers, receiver_wave, 256, (2, 3), LATE_PLANES, r_ref, rs_ref)


def early_kernel(receivers, receiver_wave, _, r_ref, rs_ref):
    inject_points(receivers, receiver_wave, 256, (0, 1), EARLY_PLANES, r_ref, rs_ref)


def source_kernel(sources, source_wave, _, s_ref, ss_ref):
    width = sources.shape[1]
    inject_points(sources, source_wave, width, (0, 1, 2), SOURCE_PLANES, s_ref, ss_ref)


def strip_of(packed, block, slot):
    lane = lanes(packed.shape)
    width = BX * STRIP
    shift = (block * width - slot * width) % BZ
    moved = pltpu.roll(packed, shift, 1) if shift else packed
    return jnp.where((lane >= block * width) & (lane < (block + 1) * width), moved, 0.0)


def y_up(v):
    return pltpu.roll(v, EY - 1, 0)


def y_down(v):
    return pltpu.roll(v, 1, 0)


def z_up(v, edge):
    return jnp.where(lanes(v.shape) == BZ - 1, edge, pltpu.roll(v, BZ - 1, 1))


def z_down(v, edge):
    return jnp.where(lanes(v.shape) == 0, edge, pltpu.roll(v, 1, 1))


def cut_edges(values, flux_z, cut_up, cut_down):
    place = lax.rem(lanes(values.shape), STRIP)
    above = jnp.where(place == MARGIN, values * cut_up, 0.0)
    below = jnp.where(place == MARGIN - 1, flux_z * cut_down, 0.0)
    return pltpu.roll(above, BZ - 2, 1) + below


def plane_edge(edges, x):
    return pltpu.roll(edges, (BZ - (x * STRIP + MARGIN - 1)) % BZ, 1)


def strip_flux(values, buoyancy):
    flux_x = buoyancy * (pltpu.roll(values, BZ - STRIP, 1) - values)
    flux_y = buoyancy * (y_up(values) - values)
    flux_z = buoyancy * (pltpu.roll(values, BZ - 1, 1) - values)
    spread = (flux_x - pltpu.roll(flux_x, STRIP, 1)) + (flux_y - y_down(flux_y))
    return flux_z, spread + (flux_z - pltpu.roll(flux_z, 1, 1))


def cut_flags():
    gz, half = lax.axis_index("gz"), lax.axis_size("gz") // 2
    return jnp.where(gz == half - 1, 1.0, 0.0), jnp.where(gz == half, 1.0, 0.0)


def sides():
    gx = lax.axis_index("gx")
    low = jnp.where(gx > 0, 1.0, 0.0)
    high = jnp.where(gx < lax.axis_size("gx") - 1, 1.0, 0.0)
    return low, high, lax.rem(gx, 2) == 0


def from_side(messages, first, count, block, side):
    even, odd = (message[first : first + count] for message in messages)
    low, high, even_above = side
    if block == 0:
        return jnp.where(even_above, odd, even) * low
    return jnp.where(even_above, even, odd) * high


def side_rows(base, wanted, step, block):
    planes = range(BX - wanted, BX) if block == 0 else range(wanted)
    return {plane: base + place * step for place, plane in enumerate(planes)}


def widened(own, own_tiles, x, layout, side):
    block, plane = divmod(x, BX)
    if block == 1:
        main = own[0][own[1] + plane * BY : own[1] + plane * BY + BY]
        tile = own_tiles[0][own_tiles[1] + plane * 8 : own_tiles[1] + plane * 8 + 8]
        return jnp.concatenate([main, tile], 0)
    parts = []
    for (messages, base, wanted), count in zip(layout, (BY, 8)):
        first = side_rows(base, wanted, count, block).get(plane)
        if first is None:
            parts.append(jnp.zeros((count, BZ), F32))
        else:
            parts.append(from_side(messages, first, count, block, side))
    return jnp.concatenate(parts, 0)


def less_plane_below(value, x, own_ref, own_rows, messages, side_rows_of, side):
    if x == BX:
        planes_end, _, tiles_end = side_rows_of
        main = from_side(messages, planes_end, BY, 0, side)
        tile = from_side(messages, tiles_end - 8, 8, 0, side)
    elif x == 2 * BX:
        planes_end, _, tiles_end = own_rows
        high = side[1]
        main = own_ref[planes_end : planes_end + BY] * high
        tile = own_ref[tiles_end - 8 : tiles_end] * high
    else:
        return value
    return value - jnp.concatenate([main, tile], 0)


def strip_below(own, messages, first, slot, side):
    lane = lanes(own.shape)
    width = BX * STRIP
    low = from_side(messages, first, EY, 0, side)
    low = pltpu.roll(low, (width - slot * width) % BZ, 1)
    own = pltpu.roll(own * side[1], (2 * width - slot * width) % BZ, 1)
    in_own = (lane >= width) & (lane < width + STRIP)
    in_high = (lane >= 2 * width) & (lane < 2 * width + STRIP)
    return jnp.where(in_own, low, jnp.where(in_high, own, 0.0))


def whole_strip(own, messages, first, slot, side):
    low = from_side(messages, first, EY, 0, side)
    high = from_side(messages, first, EY, 2, side)
    return strip_of(low, 0, slot) + strip_of(own, 1, slot) + strip_of(high, 2, slot)


def adjoint_kernel(
    ql_ref, late_ref, even, odd, adj_hbm, ra_ref, rsa_ref, rb_ref, rsb_ref,
    table_ref,
    out_ref, hist_ref, coef_ref, coef_strip_ref,
    q_ref, t_ref, u_ref, scale_ref, edge_ref, flux_ref, w_sem,
):
    w_copy = pltpu.make_async_copy(adj_hbm.at[pl.ds(1, 3)], out_ref.at[pl.ds(1, 3)], w_sem)
    w_copy.start()
    cut_up, cut_down = cut_flags()
    side = sides()
    messages = (even, odd)
    r_refs = ((ra_ref, 0), (ra_ref, 1), (rb_ref, 0), (rb_ref, 1))
    rs_refs = ((rsa_ref, 0), (rsa_ref, 1), (rsb_ref, 0), (rsb_ref, 1))
    tiles, own_tiles, raws = ADJ_SIDE[1], ADJ_OWN[1], ADJ_SIDE[2] + EY

    def initial(index, x):
        own = ((ql_ref, 0), (late_ref, 0), (ql_ref, PLANES))[index]
        layout = (
            ((messages, raws, 4), (messages, tiles, 3)),
            ((messages, 0, 3), (messages, tiles + 24, 2)),
            ((messages, raws + PLANES, 4), (messages, tiles + 40, 3)),
        )[index]
        value = widened(own, (late_ref, own_tiles + 32 * index), x, layout, side)
        if index == 1:
            value = less_plane_below(value, x, late_ref, ADJ_OWN, messages, ADJ_SIDE, side)
        return value

    for x in range(EX):
        stiff, buoy, damp = coefficients(initial(2, x), table_ref)
        coef_ref[0, x], coef_ref[1, x], coef_ref[2, x] = stiff, buoy, damp
        scale_ref[x] = stiff * damp
    own_strip = late_ref[ADJ_OWN[2] : ADJ_OWN[2] + EY]
    q_s, t_s, label_s = (
        whole_strip(own_strip, messages, ADJ_SIDE[2], slot, side) for slot in range(3)
    )
    t_s = t_s - strip_below(own_strip, messages, ADJ_SIDE[2], 3, side)
    stiff_s, buoy_s, damp_s = coefficients(label_s, table_ref)
    coef_strip_ref[0], coef_strip_ref[1], coef_strip_ref[2] = stiff_s, buoy_s, damp_s
    w_copy.wait()

    for step in range(1, STEPS + 1):
        k = STEPS - step
        rs_ref, place = rs_refs[k]
        q_s = q_s + rs_ref[place]
        u_s = stiff_s * damp_s * q_s
        flux_s, spread = strip_flux(u_s, buoy_s)
        t_s = t_s + spread
        q_s = damp_s * q_s + t_s
        edges = cut_edges(u_s, flux_s, cut_up, cut_down)
        r_ref, place = r_refs[k]
        r_first = (EARLY_PLANES if k < 2 else LATE_PLANES)[0]

        for x in range(step - 1, EX - step + 1):
            q = (initial(0, x) if step == 1 else q_ref[x]) + r_ref[place, x - r_first]
            q_ref[x] = q
            u_ref[x] = scale_ref[x] * q
            if step <= x < EX - step:
                edge_ref[x] = plane_edge(edges, x)

        for x in range(step - 1, EX - step):
            u, buoyancy = u_ref[x], coef_ref[1, x]
            slopes = [u_ref[x + 1] - u]
            if x >= step:
                slopes += [y_up(u) - u, z_up(u, edge_ref[x]) - u]
            for axis, slope in enumerate(slopes):
                flux_ref[axis, x] = buoyancy * slope
            if BX <= x < 2 * BX:
                for axis, slope in enumerate(slopes):
                    w = out_ref[1 + axis, x - BX] + slope[0:BY]
                    out_ref[1 + axis, x - BX] = w
                    hist_ref[k, 1 + axis, x - BX] = w

        for x in range(step, EX - step):
            flux_y, flux_z = flux_ref[1, x], flux_ref[2, x]
            spread = (flux_ref[0, x] - flux_ref[0, x - 1]) + (flux_y - y_down(flux_y))
            spread = spread + (flux_z - z_down(flux_z, edge_ref[x]))
            damped = coef_ref[2, x] * q_ref[x]
            t = (initial(1, x) if step == 1 else t_ref[x]) + spread
            if BX <= x < 2 * BX:
                hist_ref[k, 0, x - BX] = damped[0:BY]
            if step < STEPS:
                t_ref[x] = t
                q_ref[x] = damped + t
            else:
                out_ref[0, x - BX] = (damped + t)[0:BY]


def forward_kernel(
    wave_ref, own_s_ref, late_ref, even, odd, coef_ref, coef_strip_ref, s_ref, ss_ref, hist_ref,
    grad_ref,
    p_ref, spread_ref, edge_ref, flux_ref,
):
    cut_up, cut_down = cut_flags()
    side = sides()
    messages = (even, odd)
    tiles, own_tiles = WAVE_SIDE[1], WAVE_OWN[1]

    def initial(index, x):
        layout = (
            ((messages, 0, 4), (messages, tiles, 3)),
            ((messages, PLANES, 3), (messages, tiles + 24, 2)),
        )[index]
        own = ((wave_ref, 0), (own_s_ref, 0))[index]
        value = widened(own, (late_ref, own_tiles + 32 * index), x, layout, side)
        if index == 1:
            value = less_plane_below(value, x, late_ref, WAVE_OWN, messages, WAVE_SIDE, side)
        return value

    own_strip = late_ref[WAVE_OWN[2] : WAVE_OWN[2] + EY]
    p_s, s_s = (
        whole_strip(own_strip, messages, WAVE_SIDE[2], slot, side) for slot in range(2)
    )
    s_s = s_s - strip_below(own_strip, messages, WAVE_SIDE[2], 2, side)
    stiff_s, buoy_s, damp_s = coef_strip_ref[0], coef_strip_ref[1], coef_strip_ref[2]

    for step in range(1, STEPS + 1):
        k = step - 1
        flux_s, spread = strip_flux(p_s, buoy_s)
        edges = cut_edges(p_s, flux_s, cut_up, cut_down)
        if step < STEPS:
            s_s = s_s - spread
            p_s = damp_s * (p_s - stiff_s * s_s) + ss_ref[k]

        for x in range(step - 1, EX - step + 1):
            if step == 1:
                p_ref[x] = initial(0, x)
            if step <= x < EX - step:
                edge_ref[x] = plane_edge(edges, x)

        for x in range(step - 1, EX - step):
            p, buoyancy = p_ref[x], coef_ref[1, x]
            slopes = [p_ref[x + 1] - p]
            if x >= step:
                slopes += [y_up(p) - p, z_up(p, edge_ref[x]) - p]
            for axis, slope in enumerate(slopes):
                flux_ref[axis, x] = buoyancy * slope
            if BX <= x < 2 * BX:
                place = x - BX
                term = hist_ref[k, 1, place] * slopes[0][0:BY]
                term = term + hist_ref[k, 2, place] * slopes[1][0:BY]
                term = term + hist_ref[k, 3, place] * slopes[2][0:BY]
                grad_ref[1, place] = -term if k == 0 else grad_ref[1, place] - term

        for x in range(step, EX - step):
            flux_y, flux_z = flux_ref[1, x], flux_ref[2, x]
            spread = (flux_ref[0, x] - flux_ref[0, x - 1]) + (flux_y - y_down(flux_y))
            spread = spread + (flux_z - z_down(flux_z, edge_ref[x]))
            spread = (initial(1, x) if step == 1 else spread_ref[x]) - spread
            if step < STEPS:
                spread_ref[x] = spread
                p_ref[x] = (
                    coef_ref[2, x] * (p_ref[x] - coef_ref[0, x] * spread)
                    + s_ref[k, x - SOURCE_PLANES[0]]
                )
            if BX <= x < 2 * BX:
                place = x - BX
                term = hist_ref[k, 0, place] * spread[0:BY]
                grad_ref[0, place] = -term if k == 0 else grad_ref[0, place] - term


def shape(*dims):
    return jax.ShapeDtypeStruct(dims, F32)


def call(kernel, outs, operands, scratch, places, micros=0.1):
    spaces = {"h": pltpu.HBM, "a": pl.ANY, "v": pltpu.VMEM}
    operands = [
        pltpu.with_memory_space_constraint(operand, pltpu.HBM) if place == "h" else operand
        for operand, place in zip(operands, places)
    ]
    return pl.pallas_call(
        kernel,
        out_shape=outs,
        in_specs=[pl.BlockSpec(memory_space=spaces[place]) for place in places],
        out_specs=[pl.BlockSpec(memory_space=pltpu.VMEM)] * len(outs),
        scratch_shapes=scratch,
        compiler_params=pltpu.CompilerParams(vmem_limit_bytes=VMEM_LIMIT),
        cost_estimate=pl.CostEstimate(
            flops=0, bytes_accessed=int(3.69e6 * micros), transcendentals=0
        ),
    )(*operands)


def from_sides(sends, axes):
    count = lax.axis_size("gy")

    def route(offset):
        pairs = []
        for target in range(count):
            source = target + offset
            if 0 <= source < count:
                if "gz" in axes:
                    pairs += [(2 * source + z, 2 * target + 1 - z) for z in range(2)]
                else:
                    pairs.append((source, target))
        return pairs

    if count == 2:
        both = lax.ppermute(sends[0], axes, route(1) + route(-1))
        return both, both
    upward, downward = sends
    return lax.ppermute(downward, axes, route(1)), lax.ppermute(upward, axes, route(-1))


def rotated(array, axis, offset):
    count = lax.axis_size(axis)
    return lax.ppermute(array, axis, [((i + offset) % count, i) for i in range(count)])


def paired(array, odd):
    count = lax.axis_size("gx")
    pairs = []
    for i in range(count):
        partner = ((i - 1) ^ 1) + 1 if odd else i ^ 1
        pairs.append((partner if 0 <= partner < count else i, i))
    return lax.ppermute(array, "gx", pairs)


def local(
    stored, adjoint_end, labels, tissue, source_cells, source_wave, receiver_cells, receiver_wave
):
    assert lax.axis_size("gz") == 2 and labels.shape == (BX, BY, BZ) and tissue.shape[1] == 8
    half = lax.axis_size("gx") // 2
    arguments = [
        stored, adjoint_end, labels, tissue,
        receiver_cells.T, receiver_wave, source_cells.T, source_wave,
    ]
    ways = 1 if lax.axis_size("gy") == 2 else 2
    wave, ql, t, last_x, last_y, strips, table, receivers, receiver_wave, sources, source_wave, *sends = call(
        load_kernel,
        [
            shape(2 * PLANES, BZ),
            shape(2 * PLANES, BZ),
            shape(PLANES, BZ),
            shape(2 * BY, BZ),
            shape(2 * BX * 8, BZ),
            shape(3 * BY, BZ),
            shape(24, BZ),
        ]
        + [jax.ShapeDtypeStruct(array.shape, array.dtype) for array in arguments[4:]]
        + [shape(20 * 8, BZ)] * ways
        + [shape(2 * 8, BZ)] * ways,
        arguments,
        [
            pltpu.VMEM(stored.shape, F32),
            pltpu.VMEM(adjoint_end.shape, F32),
            pltpu.VMEM(labels.shape, jnp.int32),
            pltpu.SMEM(tissue.shape, F32),
            pltpu.SemaphoreType.DMA,
        ],
        "hhhhhhhh",
        1.4,
    )
    from_up, from_down = from_sides(sends[:ways], "gy")
    other = rotated(strips, "gz", 1)
    corner_up, corner_down = from_sides(sends[ways:], ("gy", "gz"))
    wave = rotated(wave, "gx", half)
    rb, rsb = call(
        late_kernel,
        [shape(2, EX * EY, BZ), shape(2, EY, BZ)],
        [receivers, receiver_wave],
        [],
        "vv",
        1.2,
    )
    early_planes, source_planes = (last - first for first, last in (EARLY_PLANES, SOURCE_PLANES))
    late, adj_late, token = call(
        merge_kernel,
        [shape(WAVE_FIX + 8, BZ), shape(ADJ_OWN[2] + EY, BZ), shape(8, BZ)],
        [from_up, from_down, corner_up, corner_down, strips, other, t, last_x, last_y, rsb],
        [],
        "vvvvvvvvva",
    )
    late = rotated(late, "gx", half)
    token = rotated(token, "gz", 1)
    ra, rsa = call(
        early_kernel,
        [shape(2, early_planes * EY, BZ), shape(2, EY, BZ)],
        [receivers, receiver_wave, adj_late],
        [],
        "vva",
        1.0,
    )
    ra, rb = ra.reshape(2, early_planes, EY, BZ), rb.reshape(2, EX, EY, BZ)
    even, odd, second = call(
        adjoint_join_kernel,
        [shape(ADJ_SIDE[2] + EY + 2 * PLANES, BZ)] * 2 + [shape(8, BZ)],
        [ql, adj_late, token, wave],
        [],
        "vvaa",
    )
    even, odd = paired(even, False), paired(odd, True)
    second = rotated(second, "gz", 1)
    src, src_strip = call(
        source_kernel,
        [shape(STEPS - 1, source_planes * EY, BZ), shape(STEPS - 1, EY, BZ)],
        [sources, source_wave, second],
        [],
        "vva",
        0.5,
    )
    src = src.reshape(STEPS - 1, source_planes, EY, BZ)
    own_s, wave_even, wave_odd = call(
        join_kernel,
        [shape(PLANES, BZ)] + [shape(WAVE_SIDE[2] + EY, BZ)] * 2,
        [wave, late, second],
        [],
        "vva",
    )
    wave_even, wave_odd = paired(wave_even, False), paired(wave_odd, True)
    adjoint_start, hist, coef, coef_strip = call(
        adjoint_kernel,
        [
            shape(4, BX, BY, BZ),
            shape(STEPS, 4, BX, BY, BZ),
            shape(3, EX, EY, BZ),
            shape(3, EY, BZ),
        ],
        [ql, adj_late, even, odd, adjoint_end, ra, rsa, rb, rsb, table],
        [pltpu.VMEM((EX, EY, BZ), F32)] * 5
        + [pltpu.VMEM((3, EX, EY, BZ), F32), pltpu.SemaphoreType.DMA],
        "vvvvhvvvvv",
        3.9,
    )
    (gradient,) = call(
        forward_kernel,
        [shape(2, BX, BY, BZ)],
        [wave, own_s, late, wave_even, wave_odd, coef, coef_strip, src, src_strip, hist],
        [pltpu.VMEM((EX, EY, BZ), F32)] * 3 + [pltpu.VMEM((3, EX, EY, BZ), F32)],
        "vvvvvvvvvv",
        2.5,
    )
    return gradient, adjoint_start


def solution(mesh):
    return jax.shard_map(
        local,
        mesh=mesh,
        in_specs=(
            P("shot", "gx", "gy", "gz"),
            P("shot", "gx", "gy", "gz"),
            P("gx", "gy", "gz"),
            P(),
            P("shot", None),
            P(None, "shot"),
            P(),
            P(None, "shot"),
        ),
        out_specs=(P("shot", "gx", "gy", "gz"), P("shot", "gx", "gy", "gz")),
        check_vma=False,
    )
```

```python
import jax
import jax.numpy as jnp
from jax import lax
from jax.experimental import pallas as pl
from jax.experimental.pallas import tpu as pltpu
from jax.sharding import PartitionSpec as P

STEPS = 4
MARGIN = 4
BX, BY, BZ = 4, 32, 128
EX, EY = BX + 2 * MARGIN, BY + 2 * MARGIN
STRIP = 2 * MARGIN
F32 = jnp.float32
BF16 = jnp.bfloat16
VMEM_LIMIT = 16 * 1024 * 1024
PLANES = BX * BY
WAVE_OWN = (0, BY, BY + 9 * 8)
WAVE_FIX = WAVE_OWN[2] + EY
FIX_LANE = 3 * BX * STRIP
ADJ_OWN = (PLANES, PLANES + BY, PLANES + BY + 13 * 8)
WAVE_SIDE = (PLANES + 3 * BY, PLANES + 4 * BY, PLANES + 4 * BY + 6 * 8)
ADJ_SIDE = (3 * BY, 4 * BY, 4 * BY + 9 * 8)


def lanes(shape):
    return lax.broadcasted_iota(jnp.int32, shape, len(shape) - 1)


def rows(shape):
    return lax.broadcasted_iota(jnp.int32, shape, len(shape) - 2)


def run(copies):
    for copy in copies:
        copy.start()
    for copy in copies:
        copy.wait()


def coefficients(labels, table_ref):
    result = [jnp.zeros(labels.shape, F32) for _ in range(3)]
    for index in range(8):
        picked = labels == float(index + 1)
        for kind in range(3):
            row = kind * 8 + index
            result[kind] = jnp.where(picked, table_ref[row : row + 1], result[kind])
    return result


def buoyancy_of(labels, table_ref):
    result = jnp.zeros(labels.shape, F32)
    for index in range(8):
        result = jnp.where(labels == float(index + 1), table_ref[8 + index : 9 + index], result)
    return result


def half_turn(tile):
    return pltpu.roll(tile, MARGIN, 0)


def load_kernel(
    stored_hbm, adj_hbm, lab_hbm, tissue_hbm, rc_hbm, rw_hbm, sc_hbm, sw_hbm,
    wave_ref, ql_ref, t_ref, last_x_ref, last_y_ref, strip_ref, table_ref,
    rc_ref, rw_ref, sc_ref, sw_ref, *rest,
):
    *sends, stored, adj, lab, tissue, sem = rest
    run([
        pltpu.make_async_copy(source, target, sem)
        for source, target in (
            (stored_hbm, stored), (adj_hbm, adj), (lab_hbm, lab), (tissue_hbm, tissue),
            (rc_hbm, rc_ref), (rw_hbm, rw_ref), (sc_hbm, sc_ref), (sw_hbm, sw_ref),
        )
    ])
    for index in range(tissue.shape[1]):
        speed = jnp.full((1, BZ), tissue[0, index], F32)
        density = jnp.full((1, BZ), tissue[1, index], F32)
        table_ref[index : index + 1] = density * speed
        table_ref[8 + index : 9 + index] = speed / density
        table_ref[16 + index : 17 + index] = 1.0 - jnp.full((1, BZ), tissue[2, index], F32)
    gy, gz = lax.axis_index("gy"), lax.axis_index("gz")
    lane = lanes((BY, BZ))
    row = rows((BY, BZ))
    tile_row = rows((8, BZ))
    strips = [jnp.zeros((BY, BZ), F32) for _ in range(3)]
    tiles = [None] * 39
    previous = [None, None]

    def edge_tile(block):
        return jnp.where(tile_row < MARGIN, block[0:8], block[BY - 8 : BY])

    for x in range(BX):
        labels = lab[x].astype(F32) + 1.0
        buoyancy = buoyancy_of(labels, table_ref)
        plane = slice(x * BY, x * BY + BY)
        fields = [stored[index, x] for index in range(4)] + [adj[0, x]]
        fields += [buoyancy * adj[index, x] for index in range(1, 4)] + [labels]
        wave_ref[plane] = fields[0]
        ql_ref[plane] = fields[4]
        ql_ref[PLANES + x * BY : PLANES + x * BY + BY] = labels
        for index, block in enumerate(fields):
            tiles[index * BX + x] = edge_tile(block)
            group, slot = divmod(index, 4)
            base = slot * BX * STRIP + x * STRIP
            rolled = pltpu.roll(block, base + MARGIN, 1)
            first = base + MARGIN * gz
            strips[group] = jnp.where(
                (lane >= first) & (lane < first + MARGIN), rolled, strips[group]
            )
        for kind, (target, base) in enumerate(((wave_ref, PLANES), (t_ref, 0))):
            vx, vy, vz = fields[4 * kind + 1 : 4 * kind + 4]
            spread = vx if x == 0 else vx - previous[kind]
            spread = spread + (vy - jnp.where(row == 0, 0.0, pltpu.roll(vy, 1, 0)))
            spread = spread + (vz - jnp.where(lane == 0, 0.0, pltpu.roll(vz, 1, 1)))
            target[base + x * BY : base + x * BY + BY] = spread
            previous[kind] = vx
            index = (kind * BX + x) * 8
            last_y_ref[index : index + 8] = vy[BY - 8 : BY]
    for kind in range(2):
        last_x_ref[kind * BY : kind * BY + BY] = previous[kind]
    for group in range(3):
        strip_ref[group * BY : group * BY + BY] = strips[group]
        tiles[9 * BX + group] = edge_tile(strips[group])

    def joined(first, second):
        second = first if second is None else second
        upward = jnp.where(tile_row < MARGIN, half_turn(first), second)
        downward = jnp.where(tile_row < MARGIN, first, half_turn(second))
        if len(sends) == 2:
            return (jnp.where(gy == 0, upward, downward),)
        return upward, downward

    tiles.append(None)
    half = len(sends) // 2
    for place in range(20):
        for target, tile in zip(sends[:half], joined(tiles[2 * place], tiles[2 * place + 1])):
            target[place * 8 : place * 8 + 8] = tile
    for place in range(2):
        first = tiles[9 * BX + 2 * place]
        for target, tile in zip(sends[half:], joined(first, tiles[9 * BX + 2 * place + 1])):
            target[place * 8 : place * 8 + 8] = tile


def copy_rows(target, base, source, first, count):
    target[base : base + count] = source[pl.ds(pl.multiple_of(first, 8), count)]
    return base + count


def pair_planes():
    parity = lax.rem(lax.axis_index("gx"), 2)
    return 1 - parity, parity


def merge_kernel(
    from_up, from_down, corner_up, corner_down, strip_ref, other_ref,
    t_ref, last_x_ref, last_y_ref, _,
    wave_ref, adj_ref, token_ref,
):
    token_ref[...] = jnp.zeros((8, BZ), F32)
    gy = lax.axis_index("gy")
    tile_row = rows((8, BZ))
    row, lane = rows((BY, BZ)), lanes((BY, BZ))
    take_up = (tile_row < MARGIN) & (gy < lax.axis_size("gy") - 1)
    take_down = (tile_row >= MARGIN) & (gy > 0)
    _, cut_down = cut_flags()

    def halo(up, down, index):
        place, second = divmod(index, 2)
        sl = slice(place * 8, place * 8 + 8)
        above = half_turn(up[sl]) if second else up[sl]
        below = down[sl] if second else half_turn(down[sl])
        return jnp.where(take_up, above, jnp.where(take_down, below, 0.0))

    wide = []
    for group in range(3):
        sl = slice(group * BY, group * BY + BY)
        tile = halo(from_up, from_down, 9 * BX + group) + halo(corner_up, corner_down, group)
        wide.append(jnp.concatenate([strip_ref[sl] + other_ref[sl], tile], 0))
    strip_lane = lanes((EY, BZ))

    def strip_field(index):
        group, slot = divmod(index, 4)
        moved = pltpu.roll(wide[group], (BZ - slot * BX * STRIP) % BZ, 1) if slot else wide[group]
        return jnp.where(strip_lane < BX * STRIP, moved, 0.0)

    last_lanes = (BX - 1) * STRIP
    fix_row = jnp.zeros((8, BZ), F32)
    fix_lane = jnp.zeros((BY, BZ), F32)
    for kind, target in enumerate((wave_ref, adj_ref)):
        first = 4 * kind
        planes_end, x_end, tiles_end = (WAVE_OWN, ADJ_OWN)[kind]
        vx, vy, vz = (strip_field(first + 1 + axis) for axis in range(3))
        spread = vx - jnp.where(strip_lane < STRIP, 0.0, pltpu.roll(vx, STRIP, 1))
        spread = (spread + (vy - y_down(vy))) + (vz - pltpu.roll(vz, 1, 1))
        strip = strip_field(first)
        strip = strip + pltpu.roll(jnp.where(strip_lane < BX * STRIP, spread, 0.0), BX * STRIP, 1)
        last_slot = 2
        if kind == 1:
            strip = strip + pltpu.roll(strip_field(8), 2 * BX * STRIP, 1)
            last_slot = 3
        last = jnp.where(strip_lane >= last_lanes, vx, 0.0)
        strip = strip + pltpu.roll(last, last_slot * BX * STRIP - last_lanes, 1)
        target[planes_end:x_end] = last_x_ref[kind * BY : kind * BY + BY]

        vx_before = None
        for x in range(BX):
            vx_t, vy_t, vz_t = (
                halo(from_up, from_down, (first + 1 + axis) * BX + x) for axis in range(3)
            )
            below_z = pltpu.roll(vz, (BZ - (x * STRIP + MARGIN - 1)) % BZ, 1) * cut_down
            last_y = last_y_ref[(kind * BX + x) * 8 : (kind * BX + x) * 8 + 8]
            y_before = jnp.where(
                tile_row == 0, pltpu.roll(last_y, 1, 0), pltpu.roll(vy_t, 1, 0)
            )
            z_before = jnp.where(lane[0:8] == 0, below_z[BY:EY], pltpu.roll(vz_t, 1, 1))
            spread = vx_t if x == 0 else vx_t - vx_before
            spread = (spread + (vy_t - y_before)) + (vz_t - z_before)
            vx_before = vx_t
            if kind == 0:
                fix_row = jnp.where(tile_row == x, vy_t[7:8], fix_row)
                moved = pltpu.roll(below_z[0:BY], FIX_LANE + x, 1)
                fix_lane = jnp.where(lane == FIX_LANE + x, moved, fix_lane)
            else:
                block = t_ref[x * BY : x * BY + BY]
                block = block - jnp.where(row == 0, vy_t[7:8], 0.0)
                block = block - jnp.where(lane == 0, below_z[0:BY], 0.0)
                target[x * BY : x * BY + BY] = block
            base = x_end + x * 8
            target[base : base + 8] = halo(from_up, from_down, first * BX + x)
            target[base + 32 : base + 40] = spread
            if kind == 1:
                target[base + 64 : base + 72] = halo(from_up, from_down, 8 * BX + x)
        target[tiles_end - 8 : tiles_end] = vx_before
        if kind == 0:
            target[tiles_end : tiles_end + BY] = strip[0:BY] + fix_lane
            target[tiles_end + BY : tiles_end + EY] = strip[BY:EY]
            target[WAVE_FIX : WAVE_FIX + 8] = fix_row
            target[WAVE_FIX + 8 : WAVE_FIX + 24] = jnp.zeros((16, BZ), F32)
        else:
            target[tiles_end : tiles_end + EY] = strip


def adjoint_join_kernel(ql_ref, adj_ref, _a, _b, even_ref, odd_ref, token_ref):
    token_ref[...] = jnp.zeros((8, BZ), F32)
    planes_end, x_end, tiles_end = ADJ_OWN
    for target, first in zip((even_ref, odd_ref), pair_planes()):
        base = copy_rows(target, 0, adj_ref, first * BY, 3 * BY)
        base = copy_rows(target, base, adj_ref, planes_end, BY)
        base = copy_rows(target, base, adj_ref, x_end + first * 8, 24)
        base = copy_rows(target, base, adj_ref, x_end + 32 + first * 16, 16)
        base = copy_rows(target, base, adj_ref, x_end + 64 + first * 8, 24)
        base = copy_rows(target, base, adj_ref, tiles_end - 8, 8 + EY)
        copy_rows(target, base, ql_ref, 0, 2 * PLANES)


def join_kernel(wave_ref, late_ref, _, s_ref, even_ref, odd_ref):
    planes_end, x_end, tiles_end = WAVE_OWN
    row, lane = rows((BY, BZ)), lanes((BY, BZ))
    fix_lane = late_ref[tiles_end : tiles_end + BY]
    for x in range(BX):
        block = wave_ref[PLANES + x * BY : PLANES + x * BY + BY]
        fix_row = late_ref[WAVE_FIX + x : WAVE_FIX + x + 1]
        block = block - jnp.where(row == 0, fix_row, 0.0)
        block = block - jnp.where(lane == 0, pltpu.roll(fix_lane, BZ - FIX_LANE - x, 1), 0.0)
        s_ref[x * BY : x * BY + BY] = block
    for target, first in zip((even_ref, odd_ref), pair_planes()):
        base = copy_rows(target, 0, wave_ref, 0, PLANES)
        base = copy_rows(target, base, s_ref, first * BY, 3 * BY)
        base = copy_rows(target, base, late_ref, planes_end, BY)
        base = copy_rows(target, base, late_ref, x_end + first * 8, 24)
        base = copy_rows(target, base, late_ref, x_end + 32 + first * 16, 16)
        copy_rows(target, base, late_ref, tiles_end - 8, 8 + EY)


def split(values):
    high = values.astype(BF16)
    rest = values - high.astype(F32)
    middle = rest.astype(BF16)
    low = (rest - middle.astype(F32)).astype(BF16)
    return high, middle, low


def places(cells, sl):
    gx, gy, gz = (lax.axis_index(name) for name in ("gx", "gy", "gz"))
    cut = BZ * lax.axis_size("gz") // 2 - MARGIN
    cell_x = cells[0:1, sl] - (gx * BX - MARGIN)
    cell_y = cells[1:2, sl] - gy * BY
    cell_z = cells[2:3, sl]
    in_x = (cell_x >= 0) & (cell_x < EX)
    in_y = (cell_y >= -MARGIN) & (cell_y < BY + MARGIN)
    row = jnp.where(cell_y < 0, cell_y + EY, cell_y)
    flat = jnp.where(in_x & in_y, cell_x * EY + row, -1)
    row = jnp.where(in_y, row, -1)
    zz = cell_z - cut
    in_strip = in_x & (zz >= 0) & (zz < STRIP)
    strip_lane = jnp.where(in_strip, cell_x * STRIP + zz, -1)
    return flat, cell_z - gz * BZ, row, strip_lane


def hits(count, index):
    return rows((count, index.shape[1])) == index


def product(left, right):
    return lax.dot_general(
        left, right, (((1,), (1,)), ((), ())), preferred_element_type=F32
    )


def inject_points(cells, wave_ref, width, waves, planes, out_ref, strip_out_ref):
    count, low, total_rows = len(waves), planes[0] * EY, (planes[1] - planes[0]) * EY
    for start in range(0, cells.shape[1], width):
        sl = slice(start, start + width)
        flat, z, row, strip_lane = places(cells, sl)
        here = hits(total_rows, flat - low).astype(F32).astype(BF16)
        at_strip = hits(BZ, strip_lane).astype(F32).astype(BF16)
        at_z, at_row = hits(BZ, z), hits(EY, row)
        total = strip_total = None
        parts = [split(wave_ref[wave : wave + 1, sl]) for wave in waves]
        for part in range(3):
            amounts = [parts[wave][part].astype(F32) for wave in range(count)]
            right = jnp.concatenate([jnp.where(at_z, a, 0.0) for a in amounts], 0).astype(BF16)
            left = jnp.concatenate([jnp.where(at_row, a, 0.0) for a in amounts], 0).astype(BF16)
            term, strip_term = product(here, right), product(left, at_strip)
            total = term if part == 0 else total + term
            strip_total = strip_term if part == 0 else strip_total + strip_term
        for wave in range(count):
            value = total[:, wave * BZ : wave * BZ + BZ]
            strip_value = strip_total[wave * EY : wave * EY + EY]
            if start > 0:
                value = value + out_ref[wave]
                strip_value = strip_value + strip_out_ref[wave]
            out_ref[wave] = value
            strip_out_ref[wave] = strip_value


LATE_PLANES, EARLY_PLANES, SOURCE_PLANES = (0, EX), (2, EX - 2), (1, EX - 1)


def late_kernel(receivers, receiver_wave, r_ref, rs_ref):
    inject_points(receivers, receiver_wave, 256, (2, 3), LATE_PLANES, r_ref, rs_ref)


def early_kernel(receivers, receiver_wave, _, r_ref, rs_ref):
    inject_points(receivers, receiver_wave, 256, (0, 1), EARLY_PLANES, r_ref, rs_ref)


def source_kernel(sources, source_wave, _, s_ref, ss_ref):
    width = sources.shape[1]
    inject_points(sources, source_wave, width, (0, 1, 2), SOURCE_PLANES, s_ref, ss_ref)


def strip_of(packed, block, slot):
    lane = lanes(packed.shape)
    width = BX * STRIP
    shift = (block * width - slot * width) % BZ
    moved = pltpu.roll(packed, shift, 1) if shift else packed
    return jnp.where((lane >= block * width) & (lane < (block + 1) * width), moved, 0.0)


def y_up(v):
    return pltpu.roll(v, EY - 1, 0)


def y_down(v):
    return pltpu.roll(v, 1, 0)


def z_up(v, edge):
    return jnp.where(lanes(v.shape) == BZ - 1, edge, pltpu.roll(v, BZ - 1, 1))


def z_down(v, edge):
    return jnp.where(lanes(v.shape) == 0, edge, pltpu.roll(v, 1, 1))


def cut_edges(values, flux_z, cut_up, cut_down):
    place = lax.rem(lanes(values.shape), STRIP)
    above = jnp.where(place == MARGIN, values * cut_up, 0.0)
    below = jnp.where(place == MARGIN - 1, flux_z * cut_down, 0.0)
    return pltpu.roll(above, BZ - 2, 1) + below


def plane_edge(edges, x):
    return pltpu.roll(edges, (BZ - (x * STRIP + MARGIN - 1)) % BZ, 1)


def strip_flux(values, buoyancy):
    flux_x = buoyancy * (pltpu.roll(values, BZ - STRIP, 1) - values)
    flux_y = buoyancy * (y_up(values) - values)
    flux_z = buoyancy * (pltpu.roll(values, BZ - 1, 1) - values)
    spread = (flux_x - pltpu.roll(flux_x, STRIP, 1)) + (flux_y - y_down(flux_y))
    return flux_z, spread + (flux_z - pltpu.roll(flux_z, 1, 1))


def cut_flags():
    gz, half = lax.axis_index("gz"), lax.axis_size("gz") // 2
    return jnp.where(gz == half - 1, 1.0, 0.0), jnp.where(gz == half, 1.0, 0.0)


def sides():
    gx = lax.axis_index("gx")
    low = jnp.where(gx > 0, 1.0, 0.0)
    high = jnp.where(gx < lax.axis_size("gx") - 1, 1.0, 0.0)
    return low, high, lax.rem(gx, 2) == 0


def from_side(messages, first, count, block, side):
    even, odd = (message[first : first + count] for message in messages)
    low, high, even_above = side
    if block == 0:
        return jnp.where(even_above, odd, even) * low
    return jnp.where(even_above, even, odd) * high


def side_rows(base, wanted, step, block):
    planes = range(BX - wanted, BX) if block == 0 else range(wanted)
    return {plane: base + place * step for place, plane in enumerate(planes)}


def widened(own, own_tiles, x, layout, side):
    block, plane = divmod(x, BX)
    if block == 1:
        main = own[0][own[1] + plane * BY : own[1] + plane * BY + BY]
        tile = own_tiles[0][own_tiles[1] + plane * 8 : own_tiles[1] + plane * 8 + 8]
        return jnp.concatenate([main, tile], 0)
    parts = []
    for (messages, base, wanted), count in zip(layout, (BY, 8)):
        first = side_rows(base, wanted, count, block).get(plane)
        if first is None:
            parts.append(jnp.zeros((count, BZ), F32))
        else:
            parts.append(from_side(messages, first, count, block, side))
    return jnp.concatenate(parts, 0)


def less_plane_below(value, x, own_ref, own_rows, messages, side_rows_of, side):
    if x == BX:
        planes_end, _, tiles_end = side_rows_of
        main = from_side(messages, planes_end, BY, 0, side)
        tile = from_side(messages, tiles_end - 8, 8, 0, side)
    elif x == 2 * BX:
        planes_end, _, tiles_end = own_rows
        high = side[1]
        main = own_ref[planes_end : planes_end + BY] * high
        tile = own_ref[tiles_end - 8 : tiles_end] * high
    else:
        return value
    return value - jnp.concatenate([main, tile], 0)


def strip_below(own, messages, first, slot, side):
    lane = lanes(own.shape)
    width = BX * STRIP
    low = from_side(messages, first, EY, 0, side)
    low = pltpu.roll(low, (width - slot * width) % BZ, 1)
    own = pltpu.roll(own * side[1], (2 * width - slot * width) % BZ, 1)
    in_own = (lane >= width) & (lane < width + STRIP)
    in_high = (lane >= 2 * width) & (lane < 2 * width + STRIP)
    return jnp.where(in_own, low, jnp.where(in_high, own, 0.0))


def whole_strip(own, messages, first, slot, side):
    low = from_side(messages, first, EY, 0, side)
    high = from_side(messages, first, EY, 2, side)
    return strip_of(low, 0, slot) + strip_of(own, 1, slot) + strip_of(high, 2, slot)


def adjoint_kernel(
    ql_ref, late_ref, even, odd, adj_hbm, ra_ref, rsa_ref, rb_ref, rsb_ref,
    table_ref,
    out_ref, hist_ref, coef_ref, coef_strip_ref,
    q_ref, t_ref, u_ref, scale_ref, edge_ref, flux_ref, w_sem,
):
    w_copy = pltpu.make_async_copy(adj_hbm.at[pl.ds(1, 3)], out_ref.at[pl.ds(1, 3)], w_sem)
    w_copy.start()
    cut_up, cut_down = cut_flags()
    side = sides()
    messages = (even, odd)
    r_refs = ((ra_ref, 0), (ra_ref, 1), (rb_ref, 0), (rb_ref, 1))
    rs_refs = ((rsa_ref, 0), (rsa_ref, 1), (rsb_ref, 0), (rsb_ref, 1))
    tiles, own_tiles, raws = ADJ_SIDE[1], ADJ_OWN[1], ADJ_SIDE[2] + EY

    def initial(index, x):
        own = ((ql_ref, 0), (late_ref, 0), (ql_ref, PLANES))[index]
        layout = (
            ((messages, raws, 4), (messages, tiles, 3)),
            ((messages, 0, 3), (messages, tiles + 24, 2)),
            ((messages, raws + PLANES, 4), (messages, tiles + 40, 3)),
        )[index]
        value = widened(own, (late_ref, own_tiles + 32 * index), x, layout, side)
        if index == 1:
            value = less_plane_below(value, x, late_ref, ADJ_OWN, messages, ADJ_SIDE, side)
        return value

    for x in range(EX):
        stiff, buoy, damp = coefficients(initial(2, x), table_ref)
        coef_ref[0, x], coef_ref[1, x], coef_ref[2, x] = stiff, buoy, damp
        scale_ref[x] = stiff * damp
    own_strip = late_ref[ADJ_OWN[2] : ADJ_OWN[2] + EY]
    q_s, t_s, label_s = (
        whole_strip(own_strip, messages, ADJ_SIDE[2], slot, side) for slot in range(3)
    )
    t_s = t_s - strip_below(own_strip, messages, ADJ_SIDE[2], 3, side)
    stiff_s, buoy_s, damp_s = coefficients(label_s, table_ref)
    coef_strip_ref[0], coef_strip_ref[1], coef_strip_ref[2] = stiff_s, buoy_s, damp_s
    w_copy.wait()

    for step in range(1, STEPS + 1):
        k = STEPS - step
        rs_ref, place = rs_refs[k]
        q_s = q_s + rs_ref[place]
        u_s = stiff_s * damp_s * q_s
        flux_s, spread = strip_flux(u_s, buoy_s)
        t_s = t_s + spread
        q_s = damp_s * q_s + t_s
        edges = cut_edges(u_s, flux_s, cut_up, cut_down)
        r_ref, place = r_refs[k]
        r_first = (EARLY_PLANES if k < 2 else LATE_PLANES)[0]

        for x in range(step - 1, EX - step + 1):
            q = (initial(0, x) if step == 1 else q_ref[x]) + r_ref[place, x - r_first]
            q_ref[x] = q
            u_ref[x] = scale_ref[x] * q
            if step <= x < EX - step:
                edge_ref[x] = plane_edge(edges, x)

        for x in range(step - 1, EX - step):
            u, buoyancy = u_ref[x], coef_ref[1, x]
            slopes = [u_ref[x + 1] - u]
            if x >= step:
                slopes += [y_up(u) - u, z_up(u, edge_ref[x]) - u]
            for axis, slope in enumerate(slopes):
                flux_ref[axis, x] = buoyancy * slope
            if BX <= x < 2 * BX:
                for axis, slope in enumerate(slopes):
                    w = out_ref[1 + axis, x - BX] + slope[0:BY]
                    out_ref[1 + axis, x - BX] = w
                    hist_ref[k, 1 + axis, x - BX] = w

        for x in range(step, EX - step):
            flux_y, flux_z = flux_ref[1, x], flux_ref[2, x]
            spread = (flux_ref[0, x] - flux_ref[0, x - 1]) + (flux_y - y_down(flux_y))
            spread = spread + (flux_z - z_down(flux_z, edge_ref[x]))
            damped = coef_ref[2, x] * q_ref[x]
            t = (initial(1, x) if step == 1 else t_ref[x]) + spread
            if BX <= x < 2 * BX:
                hist_ref[k, 0, x - BX] = damped[0:BY]
            if step < STEPS:
                t_ref[x] = t
                q_ref[x] = damped + t
            else:
                out_ref[0, x - BX] = (damped + t)[0:BY]


def forward_kernel(
    wave_ref, own_s_ref, late_ref, even, odd, coef_ref, coef_strip_ref, s_ref, ss_ref, hist_ref,
    grad_ref,
    p_ref, spread_ref, edge_ref, flux_ref,
):
    cut_up, cut_down = cut_flags()
    side = sides()
    messages = (even, odd)
    tiles, own_tiles = WAVE_SIDE[1], WAVE_OWN[1]

    def initial(index, x):
        layout = (
            ((messages, 0, 4), (messages, tiles, 3)),
            ((messages, PLANES, 3), (messages, tiles + 24, 2)),
        )[index]
        own = ((wave_ref, 0), (own_s_ref, 0))[index]
        value = widened(own, (late_ref, own_tiles + 32 * index), x, layout, side)
        if index == 1:
            value = less_plane_below(value, x, late_ref, WAVE_OWN, messages, WAVE_SIDE, side)
        return value

    own_strip = late_ref[WAVE_OWN[2] : WAVE_OWN[2] + EY]
    p_s, s_s = (
        whole_strip(own_strip, messages, WAVE_SIDE[2], slot, side) for slot in range(2)
    )
    s_s = s_s - strip_below(own_strip, messages, WAVE_SIDE[2], 2, side)
    stiff_s, buoy_s, damp_s = coef_strip_ref[0], coef_strip_ref[1], coef_strip_ref[2]

    for step in range(1, STEPS + 1):
        k = step - 1
        flux_s, spread = strip_flux(p_s, buoy_s)
        edges = cut_edges(p_s, flux_s, cut_up, cut_down)
        if step < STEPS:
            s_s = s_s - spread
            p_s = damp_s * (p_s - stiff_s * s_s) + ss_ref[k]

        for x in range(step - 1, EX - step + 1):
            if step == 1:
                p_ref[x] = initial(0, x)
            if step <= x < EX - step:
                edge_ref[x] = plane_edge(edges, x)

        for x in range(step - 1, EX - step):
            p, buoyancy = p_ref[x], coef_ref[1, x]
            slopes = [p_ref[x + 1] - p]
            if x >= step:
                slopes += [y_up(p) - p, z_up(p, edge_ref[x]) - p]
            for axis, slope in enumerate(slopes):
                flux_ref[axis, x] = buoyancy * slope
            if BX <= x < 2 * BX:
                place = x - BX
                term = hist_ref[k, 1, place] * slopes[0][0:BY]
                term = term + hist_ref[k, 2, place] * slopes[1][0:BY]
                term = term + hist_ref[k, 3, place] * slopes[2][0:BY]
                grad_ref[1, place] = -term if k == 0 else grad_ref[1, place] - term

        for x in range(step, EX - step):
            flux_y, flux_z = flux_ref[1, x], flux_ref[2, x]
            spread = (flux_ref[0, x] - flux_ref[0, x - 1]) + (flux_y - y_down(flux_y))
            spread = spread + (flux_z - z_down(flux_z, edge_ref[x]))
            spread = (initial(1, x) if step == 1 else spread_ref[x]) - spread
            if step < STEPS:
                spread_ref[x] = spread
                p_ref[x] = (
                    coef_ref[2, x] * (p_ref[x] - coef_ref[0, x] * spread)
                    + s_ref[k, x - SOURCE_PLANES[0]]
                )
            if BX <= x < 2 * BX:
                place = x - BX
                term = hist_ref[k, 0, place] * spread[0:BY]
                grad_ref[0, place] = -term if k == 0 else grad_ref[0, place] - term


def shape(*dims):
    return jax.ShapeDtypeStruct(dims, F32)


def call(kernel, outs, operands, scratch, places, micros=0.1):
    spaces = {"h": pltpu.HBM, "a": pl.ANY, "v": pltpu.VMEM}
    operands = [
        pltpu.with_memory_space_constraint(operand, pltpu.HBM) if place == "h" else operand
        for operand, place in zip(operands, places)
    ]
    return pl.pallas_call(
        kernel,
        out_shape=outs,
        in_specs=[pl.BlockSpec(memory_space=spaces[place]) for place in places],
        out_specs=[pl.BlockSpec(memory_space=pltpu.VMEM)] * len(outs),
        scratch_shapes=scratch,
        compiler_params=pltpu.CompilerParams(vmem_limit_bytes=VMEM_LIMIT),
        cost_estimate=pl.CostEstimate(
            flops=0, bytes_accessed=int(3.69e6 * micros), transcendentals=0
        ),
    )(*operands)


def from_sides(sends, axes):
    count = lax.axis_size("gy")

    def route(offset):
        pairs = []
        for target in range(count):
            source = target + offset
            if 0 <= source < count:
                if "gz" in axes:
                    pairs += [(2 * source + z, 2 * target + 1 - z) for z in range(2)]
                else:
                    pairs.append((source, target))
        return pairs

    if count == 2:
        both = lax.ppermute(sends[0], axes, route(1) + route(-1))
        return both, both
    upward, downward = sends
    return lax.ppermute(downward, axes, route(1)), lax.ppermute(upward, axes, route(-1))


def rotated(array, axis, offset):
    count = lax.axis_size(axis)
    return lax.ppermute(array, axis, [((i + offset) % count, i) for i in range(count)])


def paired(array, odd):
    count = lax.axis_size("gx")
    pairs = []
    for i in range(count):
        partner = ((i - 1) ^ 1) + 1 if odd else i ^ 1
        pairs.append((partner if 0 <= partner < count else i, i))
    return lax.ppermute(array, "gx", pairs)


def local(
    stored, adjoint_end, labels, tissue, source_cells, source_wave, receiver_cells, receiver_wave
):
    assert lax.axis_size("gz") == 2 and labels.shape == (BX, BY, BZ) and tissue.shape[1] == 8
    half = lax.axis_size("gx") // 2
    arguments = [
        stored, adjoint_end, labels, tissue,
        receiver_cells.T, receiver_wave, source_cells.T, source_wave,
    ]
    ways = 1 if lax.axis_size("gy") == 2 else 2
    wave, ql, t, last_x, last_y, strips, table, receivers, receiver_wave, sources, source_wave, *sends = call(
        load_kernel,
        [
            shape(2 * PLANES, BZ),
            shape(2 * PLANES, BZ),
            shape(PLANES, BZ),
            shape(2 * BY, BZ),
            shape(2 * BX * 8, BZ),
            shape(3 * BY, BZ),
            shape(24, BZ),
        ]
        + [jax.ShapeDtypeStruct(array.shape, array.dtype) for array in arguments[4:]]
        + [shape(20 * 8, BZ)] * ways
        + [shape(2 * 8, BZ)] * ways,
        arguments,
        [
            pltpu.VMEM(stored.shape, F32),
            pltpu.VMEM(adjoint_end.shape, F32),
            pltpu.VMEM(labels.shape, jnp.int32),
            pltpu.SMEM(tissue.shape, F32),
            pltpu.SemaphoreType.DMA,
        ],
        "hhhhhhhh",
        1.4,
    )
    from_up, from_down = from_sides(sends[:ways], "gy")
    other = rotated(strips, "gz", 1)
    corner_up, corner_down = from_sides(sends[ways:], ("gy", "gz"))
    wave = rotated(wave, "gx", half)
    rb, rsb = call(
        late_kernel,
        [shape(2, EX * EY, BZ), shape(2, EY, BZ)],
        [receivers, receiver_wave],
        [],
        "vv",
        1.2,
    )
    early_planes, source_planes = (last - first for first, last in (EARLY_PLANES, SOURCE_PLANES))
    late, adj_late, token = call(
        merge_kernel,
        [shape(WAVE_FIX + 24, BZ), shape(ADJ_OWN[2] + EY, BZ), shape(8, BZ)],
        [from_up, from_down, corner_up, corner_down, strips, other, t, last_x, last_y, rsb],
        [],
        "vvvvvvvvva",
    )
    late = rotated(late, "gx", half)
    token = rotated(token, "gz", 1)
    ra, rsa = call(
        early_kernel,
        [shape(2, early_planes * EY, BZ), shape(2, EY, BZ)],
        [receivers, receiver_wave, adj_late],
        [],
        "vva",
        1.0,
    )
    ra, rb = ra.reshape(2, early_planes, EY, BZ), rb.reshape(2, EX, EY, BZ)
    even, odd, second = call(
        adjoint_join_kernel,
        [shape(ADJ_SIDE[2] + EY + 2 * PLANES, BZ)] * 2 + [shape(8, BZ)],
        [ql, adj_late, token, wave],
        [],
        "vvaa",
    )
    even, odd = paired(even, False), paired(odd, True)
    second = rotated(second, "gz", 1)
    src, src_strip = call(
        source_kernel,
        [shape(STEPS - 1, source_planes * EY, BZ), shape(STEPS - 1, EY, BZ)],
        [sources, source_wave, second],
        [],
        "vva",
        0.5,
    )
    src = src.reshape(STEPS - 1, source_planes, EY, BZ)
    own_s, wave_even, wave_odd = call(
        join_kernel,
        [shape(PLANES, BZ)] + [shape(WAVE_SIDE[2] + EY, BZ)] * 2,
        [wave, late, second],
        [],
        "vva",
    )
    wave_even, wave_odd = paired(wave_even, False), paired(wave_odd, True)
    adjoint_start, hist, coef, coef_strip = call(
        adjoint_kernel,
        [
            shape(4, BX, BY, BZ),
            shape(STEPS, 4, BX, BY, BZ),
            shape(3, EX, EY, BZ),
            shape(3, EY, BZ),
        ],
        [ql, adj_late, even, odd, adjoint_end, ra, rsa, rb, rsb, table],
        [pltpu.VMEM((EX, EY, BZ), F32)] * 5
        + [pltpu.VMEM((3, EX, EY, BZ), F32), pltpu.SemaphoreType.DMA],
        "vvvvhvvvvv",
        3.9,
    )
    (gradient,) = call(
        forward_kernel,
        [shape(2, BX, BY, BZ)],
        [wave, own_s, late, wave_even, wave_odd, coef, coef_strip, src, src_strip, hist],
        [pltpu.VMEM((EX, EY, BZ), F32)] * 3 + [pltpu.VMEM((3, EX, EY, BZ), F32)],
        "vvvvvvvvvv",
        2.5,
    )
    return gradient, adjoint_start


def solution(mesh):
    return jax.shard_map(
        local,
        mesh=mesh,
        in_specs=(
            P("shot", "gx", "gy", "gz"),
            P("shot", "gx", "gy", "gz"),
            P("gx", "gy", "gz"),
            P(),
            P("shot", None),
            P(None, "shot"),
            P(),
            P(None, "shot"),
        ),
        out_specs=(P("shot", "gx", "gy", "gz"), P("shot", "gx", "gy", "gz")),
        check_vma=False,
    )
```

```python
import jax
import jax.numpy as jnp
from jax import lax
from jax.experimental import pallas as pl
from jax.experimental.pallas import tpu as pltpu
from jax.sharding import PartitionSpec as P

STEPS = 4
MARGIN = 4
BX, BY, BZ = 4, 32, 128
EX, EY = BX + 2 * MARGIN, BY + 2 * MARGIN
STRIP = 2 * MARGIN
F32 = jnp.float32
BF16 = jnp.bfloat16
VMEM_LIMIT = 16 * 1024 * 1024
PLANES = BX * BY
WAVE_OWN = (0, BY, BY + 9 * 8)
WAVE_FIX = WAVE_OWN[2] + EY
FIX_LANE = 3 * BX * STRIP
ADJ_OWN = (PLANES, PLANES + BY, PLANES + BY + 13 * 8)
WAVE_SIDE = (PLANES + 3 * BY, PLANES + 4 * BY, PLANES + 4 * BY + 6 * 8)
ADJ_SIDE = (3 * BY, 4 * BY, 4 * BY + 9 * 8)


def lanes(shape):
    return lax.broadcasted_iota(jnp.int32, shape, len(shape) - 1)


def rows(shape):
    return lax.broadcasted_iota(jnp.int32, shape, len(shape) - 2)


def run(copies):
    for copy in copies:
        copy.start()
    for copy in copies:
        copy.wait()


def coefficients(labels, table_ref):
    result = [jnp.zeros(labels.shape, F32) for _ in range(3)]
    for index in range(8):
        picked = labels == float(index + 1)
        for kind in range(3):
            row = kind * 8 + index
            result[kind] = jnp.where(picked, table_ref[row : row + 1], result[kind])
    return result


def buoyancy_of(labels, table_ref):
    result = jnp.zeros(labels.shape, F32)
    for index in range(8):
        result = jnp.where(labels == float(index + 1), table_ref[8 + index : 9 + index], result)
    return result


def half_turn(tile):
    return pltpu.roll(tile, MARGIN, 0)


def load_kernel(
    stored_hbm, adj_hbm, lab_hbm, tissue_hbm, rc_hbm, rw_hbm, sc_hbm, sw_hbm,
    wave_ref, ql_ref, t_ref, last_x_ref, last_y_ref, strip_ref, table_ref,
    rc_ref, rw_ref, sc_ref, sw_ref, *rest,
):
    *sends, stored, adj, lab, tissue, sem = rest
    run([
        pltpu.make_async_copy(source, target, sem)
        for source, target in (
            (stored_hbm, stored), (adj_hbm, adj), (lab_hbm, lab), (tissue_hbm, tissue),
            (rc_hbm, rc_ref), (rw_hbm, rw_ref), (sc_hbm, sc_ref), (sw_hbm, sw_ref),
        )
    ])
    for index in range(tissue.shape[1]):
        speed = jnp.full((1, BZ), tissue[0, index], F32)
        density = jnp.full((1, BZ), tissue[1, index], F32)
        table_ref[index : index + 1] = density * speed
        table_ref[8 + index : 9 + index] = speed / density
        table_ref[16 + index : 17 + index] = 1.0 - jnp.full((1, BZ), tissue[2, index], F32)
    gy, gz = lax.axis_index("gy"), lax.axis_index("gz")
    lane = lanes((BY, BZ))
    row = rows((BY, BZ))
    tile_row = rows((8, BZ))
    strips = [jnp.zeros((BY, BZ), F32) for _ in range(3)]
    tiles = [None] * 39
    previous = [None, None]

    def edge_tile(block):
        return jnp.where(tile_row < MARGIN, block[0:8], block[BY - 8 : BY])

    for x in range(BX):
        labels = lab[x].astype(F32) + 1.0
        buoyancy = buoyancy_of(labels, table_ref)
        plane = slice(x * BY, x * BY + BY)
        fields = [stored[index, x] for index in range(4)] + [adj[0, x]]
        fields += [buoyancy * adj[index, x] for index in range(1, 4)] + [labels]
        wave_ref[plane] = fields[0]
        ql_ref[plane] = fields[4]
        ql_ref[PLANES + x * BY : PLANES + x * BY + BY] = labels
        for index, block in enumerate(fields):
            tiles[index * BX + x] = edge_tile(block)
            group, slot = divmod(index, 4)
            base = slot * BX * STRIP + x * STRIP
            rolled = pltpu.roll(block, base + MARGIN, 1)
            first = base + MARGIN * gz
            strips[group] = jnp.where(
                (lane >= first) & (lane < first + MARGIN), rolled, strips[group]
            )
        for kind, (target, base) in enumerate(((wave_ref, PLANES), (t_ref, 0))):
            vx, vy, vz = fields[4 * kind + 1 : 4 * kind + 4]
            spread = vx if x == 0 else vx - previous[kind]
            spread = spread + (vy - jnp.where(row == 0, 0.0, pltpu.roll(vy, 1, 0)))
            spread = spread + (vz - jnp.where(lane == 0, 0.0, pltpu.roll(vz, 1, 1)))
            target[base + x * BY : base + x * BY + BY] = spread
            previous[kind] = vx
            index = (kind * BX + x) * 8
            last_y_ref[index : index + 8] = vy[BY - 8 : BY]
    for kind in range(2):
        last_x_ref[kind * BY : kind * BY + BY] = previous[kind]
    for group in range(3):
        strip_ref[group * BY : group * BY + BY] = strips[group]
        tiles[9 * BX + group] = edge_tile(strips[group])

    def joined(first, second):
        second = first if second is None else second
        upward = jnp.where(tile_row < MARGIN, half_turn(first), second)
        downward = jnp.where(tile_row < MARGIN, first, half_turn(second))
        if len(sends) == 2:
            return (jnp.where(gy == 0, upward, downward),)
        return upward, downward

    tiles.append(None)
    half = len(sends) // 2
    for place in range(20):
        for target, tile in zip(sends[:half], joined(tiles[2 * place], tiles[2 * place + 1])):
            target[place * 8 : place * 8 + 8] = tile
    for place in range(2):
        first = tiles[9 * BX + 2 * place]
        for target, tile in zip(sends[half:], joined(first, tiles[9 * BX + 2 * place + 1])):
            target[place * 8 : place * 8 + 8] = tile


def copy_rows(target, base, source, first, count):
    target[base : base + count] = source[pl.ds(pl.multiple_of(first, 8), count)]
    return base + count


def pair_planes():
    parity = lax.rem(lax.axis_index("gx"), 2)
    return 1 - parity, parity


def merge_kernel(
    from_up, from_down, corner_up, corner_down, strip_ref, other_ref,
    t_ref, last_x_ref, last_y_ref, _,
    wave_ref, adj_ref, token_ref,
):
    token_ref[...] = jnp.zeros((8, BZ), F32)
    gy = lax.axis_index("gy")
    tile_row = rows((8, BZ))
    row, lane = rows((BY, BZ)), lanes((BY, BZ))
    take_up = (tile_row < MARGIN) & (gy < lax.axis_size("gy") - 1)
    take_down = (tile_row >= MARGIN) & (gy > 0)
    _, cut_down = cut_flags()

    def halo(up, down, index):
        place, second = divmod(index, 2)
        sl = slice(place * 8, place * 8 + 8)
        above = half_turn(up[sl]) if second else up[sl]
        below = down[sl] if second else half_turn(down[sl])
        return jnp.where(take_up, above, jnp.where(take_down, below, 0.0))

    wide = []
    for group in range(3):
        sl = slice(group * BY, group * BY + BY)
        tile = halo(from_up, from_down, 9 * BX + group) + halo(corner_up, corner_down, group)
        wide.append(jnp.concatenate([strip_ref[sl] + other_ref[sl], tile], 0))
    strip_lane = lanes((EY, BZ))

    def strip_field(index):
        group, slot = divmod(index, 4)
        moved = pltpu.roll(wide[group], (BZ - slot * BX * STRIP) % BZ, 1) if slot else wide[group]
        return jnp.where(strip_lane < BX * STRIP, moved, 0.0)

    last_lanes = (BX - 1) * STRIP
    fix_row = jnp.zeros((8, BZ), F32)
    fix_lane = jnp.zeros((BY, BZ), F32)
    for kind, target in enumerate((wave_ref, adj_ref)):
        first = 4 * kind
        planes_end, x_end, tiles_end = (WAVE_OWN, ADJ_OWN)[kind]
        vx, vy, vz = (strip_field(first + 1 + axis) for axis in range(3))
        spread = vx - jnp.where(strip_lane < STRIP, 0.0, pltpu.roll(vx, STRIP, 1))
        spread = (spread + (vy - y_down(vy))) + (vz - pltpu.roll(vz, 1, 1))
        strip = strip_field(first)
        strip = strip + pltpu.roll(jnp.where(strip_lane < BX * STRIP, spread, 0.0), BX * STRIP, 1)
        last_slot = 2
        if kind == 1:
            strip = strip + pltpu.roll(strip_field(8), 2 * BX * STRIP, 1)
            last_slot = 3
        last = jnp.where(strip_lane >= last_lanes, vx, 0.0)
        strip = strip + pltpu.roll(last, last_slot * BX * STRIP - last_lanes, 1)
        target[planes_end:x_end] = last_x_ref[kind * BY : kind * BY + BY]

        vx_before = None
        for x in range(BX):
            vx_t, vy_t, vz_t = (
                halo(from_up, from_down, (first + 1 + axis) * BX + x) for axis in range(3)
            )
            below_z = pltpu.roll(vz, (BZ - (x * STRIP + MARGIN - 1)) % BZ, 1) * cut_down
            last_y = last_y_ref[(kind * BX + x) * 8 : (kind * BX + x) * 8 + 8]
            y_before = jnp.where(
                tile_row == 0, pltpu.roll(last_y, 1, 0), pltpu.roll(vy_t, 1, 0)
            )
            z_before = jnp.where(lane[0:8] == 0, below_z[BY:EY], pltpu.roll(vz_t, 1, 1))
            spread = vx_t if x == 0 else vx_t - vx_before
            spread = (spread + (vy_t - y_before)) + (vz_t - z_before)
            vx_before = vx_t
            if kind == 0:
                fix_row = jnp.where(tile_row == x, vy_t[7:8], fix_row)
                moved = pltpu.roll(below_z[0:BY], FIX_LANE + x, 1)
                fix_lane = jnp.where(lane == FIX_LANE + x, moved, fix_lane)
            else:
                block = t_ref[x * BY : x * BY + BY]
                block = block - jnp.where(row == 0, vy_t[7:8], 0.0)
                block = block - jnp.where(lane == 0, below_z[0:BY], 0.0)
                target[x * BY : x * BY + BY] = block
            base = x_end + x * 8
            target[base : base + 8] = halo(from_up, from_down, first * BX + x)
            target[base + 32 : base + 40] = spread
            if kind == 1:
                target[base + 64 : base + 72] = halo(from_up, from_down, 8 * BX + x)
        target[tiles_end - 8 : tiles_end] = vx_before
        if kind == 0:
            target[tiles_end : tiles_end + BY] = strip[0:BY] + fix_lane
            target[tiles_end + BY : tiles_end + EY] = strip[BY:EY]
            target[WAVE_FIX : WAVE_FIX + 8] = fix_row
            target[WAVE_FIX + 8 : WAVE_FIX + 24] = jnp.zeros((16, BZ), F32)
        else:
            target[tiles_end : tiles_end + EY] = strip


def adjoint_join_kernel(ql_ref, adj_ref, _a, _b, even_ref, odd_ref, token_ref):
    token_ref[...] = jnp.zeros((8, BZ), F32)
    planes_end, x_end, tiles_end = ADJ_OWN
    for target, first in zip((even_ref, odd_ref), pair_planes()):
        base = copy_rows(target, 0, adj_ref, first * BY, 3 * BY)
        base = copy_rows(target, base, adj_ref, planes_end, BY)
        base = copy_rows(target, base, adj_ref, x_end + first * 8, 24)
        base = copy_rows(target, base, adj_ref, x_end + 32 + first * 16, 16)
        base = copy_rows(target, base, adj_ref, x_end + 64 + first * 8, 24)
        base = copy_rows(target, base, adj_ref, tiles_end - 8, 8 + EY)
        copy_rows(target, base, ql_ref, 0, 2 * PLANES)


def join_kernel(wave_ref, late_ref, _, s_ref, even_ref, odd_ref):
    planes_end, x_end, tiles_end = WAVE_OWN
    row, lane = rows((BY, BZ)), lanes((BY, BZ))
    fix_lane = late_ref[tiles_end : tiles_end + BY]
    for x in range(BX):
        block = wave_ref[PLANES + x * BY : PLANES + x * BY + BY]
        fix_row = late_ref[WAVE_FIX + x : WAVE_FIX + x + 1]
        block = block - jnp.where(row == 0, fix_row, 0.0)
        block = block - jnp.where(lane == 0, pltpu.roll(fix_lane, BZ - FIX_LANE - x, 1), 0.0)
        s_ref[x * BY : x * BY + BY] = block
    for target, first in zip((even_ref, odd_ref), pair_planes()):
        base = copy_rows(target, 0, wave_ref, 0, PLANES)
        base = copy_rows(target, base, s_ref, first * BY, 3 * BY)
        base = copy_rows(target, base, late_ref, planes_end, BY)
        base = copy_rows(target, base, late_ref, x_end + first * 8, 24)
        base = copy_rows(target, base, late_ref, x_end + 32 + first * 16, 16)
        copy_rows(target, base, late_ref, tiles_end - 8, 8 + EY)


def split(values):
    high = values.astype(BF16)
    rest = values - high.astype(F32)
    middle = rest.astype(BF16)
    low = (rest - middle.astype(F32)).astype(BF16)
    return high, middle, low


def places(cells, sl):
    gx, gy, gz = (lax.axis_index(name) for name in ("gx", "gy", "gz"))
    cut = BZ * lax.axis_size("gz") // 2 - MARGIN
    cell_x = cells[0:1, sl] - (gx * BX - MARGIN)
    cell_y = cells[1:2, sl] - gy * BY
    cell_z = cells[2:3, sl]
    in_x = (cell_x >= 0) & (cell_x < EX)
    in_y = (cell_y >= -MARGIN) & (cell_y < BY + MARGIN)
    row = jnp.where(cell_y < 0, cell_y + EY, cell_y)
    flat = jnp.where(in_x & in_y, cell_x * EY + row, -1)
    row = jnp.where(in_y, row, -1)
    zz = cell_z - cut
    in_strip = in_x & (zz >= 0) & (zz < STRIP)
    strip_lane = jnp.where(in_strip, cell_x * STRIP + zz, -1)
    return flat, cell_z - gz * BZ, row, strip_lane


def hits(count, index):
    return rows((count, index.shape[1])) == index


def product(left, right):
    return lax.dot_general(
        left, right, (((1,), (1,)), ((), ())), preferred_element_type=F32
    )


def inject_points(cells, wave_ref, width, waves, planes, out_ref, strip_out_ref):
    count, low, total_rows = len(waves), planes[0] * EY, (planes[1] - planes[0]) * EY
    for start in range(0, cells.shape[1], width):
        sl = slice(start, start + width)
        flat, z, row, strip_lane = places(cells, sl)
        here = hits(total_rows, flat - low).astype(F32).astype(BF16)
        at_strip = hits(BZ, strip_lane).astype(F32).astype(BF16)
        at_z, at_row = hits(BZ, z), hits(EY, row)
        total = strip_total = None
        parts = [split(wave_ref[wave : wave + 1, sl]) for wave in waves]
        for part in range(3):
            amounts = [parts[wave][part].astype(F32) for wave in range(count)]
            right = jnp.concatenate([jnp.where(at_z, a, 0.0) for a in amounts], 0).astype(BF16)
            left = jnp.concatenate([jnp.where(at_row, a, 0.0) for a in amounts], 0).astype(BF16)
            term, strip_term = product(here, right), product(left, at_strip)
            total = term if part == 0 else total + term
            strip_total = strip_term if part == 0 else strip_total + strip_term
        for wave in range(count):
            value = total[:, wave * BZ : wave * BZ + BZ]
            strip_value = strip_total[wave * EY : wave * EY + EY]
            if start > 0:
                value = value + out_ref[wave]
                strip_value = strip_value + strip_out_ref[wave]
            out_ref[wave] = value
            strip_out_ref[wave] = strip_value


LATE_PLANES, EARLY_PLANES, SOURCE_PLANES = (0, EX), (2, EX - 2), (1, EX - 1)


def late_kernel(receivers, receiver_wave, r_ref, rs_ref):
    inject_points(receivers, receiver_wave, 256, (2, 3), LATE_PLANES, r_ref, rs_ref)


def early_kernel(receivers, receiver_wave, _, r_ref, rs_ref):
    inject_points(receivers, receiver_wave, 256, (0, 1), EARLY_PLANES, r_ref, rs_ref)


def source_kernel(sources, source_wave, _, s_ref, ss_ref):
    width = sources.shape[1]
    inject_points(sources, source_wave, width, (0, 1, 2), SOURCE_PLANES, s_ref, ss_ref)


def strip_of(packed, block, slot):
    lane = lanes(packed.shape)
    width = BX * STRIP
    shift = (block * width - slot * width) % BZ
    moved = pltpu.roll(packed, shift, 1) if shift else packed
    return jnp.where((lane >= block * width) & (lane < (block + 1) * width), moved, 0.0)


def y_up(v):
    return pltpu.roll(v, EY - 1, 0)


def y_down(v):
    return pltpu.roll(v, 1, 0)


def z_up(v, edge):
    return jnp.where(lanes(v.shape) == BZ - 1, edge, pltpu.roll(v, BZ - 1, 1))


def z_down(v, edge):
    return jnp.where(lanes(v.shape) == 0, edge, pltpu.roll(v, 1, 1))


def cut_edges(values, flux_z, cut_up, cut_down):
    place = lax.rem(lanes(values.shape), STRIP)
    above = jnp.where(place == MARGIN, values * cut_up, 0.0)
    below = jnp.where(place == MARGIN - 1, flux_z * cut_down, 0.0)
    return pltpu.roll(above, BZ - 2, 1) + below


def plane_edge(edges, x):
    return pltpu.roll(edges, (BZ - (x * STRIP + MARGIN - 1)) % BZ, 1)


def strip_flux(values, buoyancy):
    flux_x = buoyancy * (pltpu.roll(values, BZ - STRIP, 1) - values)
    flux_y = buoyancy * (y_up(values) - values)
    flux_z = buoyancy * (pltpu.roll(values, BZ - 1, 1) - values)
    spread = (flux_x - pltpu.roll(flux_x, STRIP, 1)) + (flux_y - y_down(flux_y))
    return flux_z, spread + (flux_z - pltpu.roll(flux_z, 1, 1))


def cut_flags():
    gz, half = lax.axis_index("gz"), lax.axis_size("gz") // 2
    return jnp.where(gz == half - 1, 1.0, 0.0), jnp.where(gz == half, 1.0, 0.0)


def sides():
    gx = lax.axis_index("gx")
    low = jnp.where(gx > 0, 1.0, 0.0)
    high = jnp.where(gx < lax.axis_size("gx") - 1, 1.0, 0.0)
    return low, high, lax.rem(gx, 2) == 0


def from_side(messages, first, count, block, side):
    even, odd = (message[first : first + count] for message in messages)
    low, high, even_above = side
    if block == 0:
        return jnp.where(even_above, odd, even) * low
    return jnp.where(even_above, even, odd) * high


def side_rows(base, wanted, step, block):
    planes = range(BX - wanted, BX) if block == 0 else range(wanted)
    return {plane: base + place * step for place, plane in enumerate(planes)}


def widened(own, own_tiles, x, layout, side):
    block, plane = divmod(x, BX)
    if block == 1:
        main = own[0][own[1] + plane * BY : own[1] + plane * BY + BY]
        tile = own_tiles[0][own_tiles[1] + plane * 8 : own_tiles[1] + plane * 8 + 8]
        return jnp.concatenate([main, tile], 0)
    parts = []
    for (messages, base, wanted), count in zip(layout, (BY, 8)):
        first = side_rows(base, wanted, count, block).get(plane)
        if first is None:
            parts.append(jnp.zeros((count, BZ), F32))
        else:
            parts.append(from_side(messages, first, count, block, side))
    return jnp.concatenate(parts, 0)


def less_plane_below(value, x, own_ref, own_rows, messages, side_rows_of, side):
    if x == BX:
        planes_end, _, tiles_end = side_rows_of
        main = from_side(messages, planes_end, BY, 0, side)
        tile = from_side(messages, tiles_end - 8, 8, 0, side)
    elif x == 2 * BX:
        planes_end, _, tiles_end = own_rows
        high = side[1]
        main = own_ref[planes_end : planes_end + BY] * high
        tile = own_ref[tiles_end - 8 : tiles_end] * high
    else:
        return value
    return value - jnp.concatenate([main, tile], 0)


def strip_below(own, messages, first, slot, side):
    lane = lanes(own.shape)
    width = BX * STRIP
    low = from_side(messages, first, EY, 0, side)
    low = pltpu.roll(low, (width - slot * width) % BZ, 1)
    own = pltpu.roll(own * side[1], (2 * width - slot * width) % BZ, 1)
    in_own = (lane >= width) & (lane < width + STRIP)
    in_high = (lane >= 2 * width) & (lane < 2 * width + STRIP)
    return jnp.where(in_own, low, jnp.where(in_high, own, 0.0))


def whole_strip(own, messages, first, slot, side):
    low = from_side(messages, first, EY, 0, side)
    high = from_side(messages, first, EY, 2, side)
    return strip_of(low, 0, slot) + strip_of(own, 1, slot) + strip_of(high, 2, slot)


def adjoint_kernel(
    ql_ref, late_ref, even, odd, adj_hbm, ra_ref, rsa_ref, rb_ref, rsb_ref,
    table_ref,
    out_ref, hist_ref, coef_ref, coef_strip_ref,
    q_ref, t_ref, u_ref, scale_ref, edge_ref, flux_ref, w_sem,
):
    w_copy = pltpu.make_async_copy(adj_hbm.at[pl.ds(1, 3)], out_ref.at[pl.ds(1, 3)], w_sem)
    w_copy.start()
    cut_up, cut_down = cut_flags()
    side = sides()
    messages = (even, odd)
    r_refs = ((ra_ref, 0), (ra_ref, 1), (rb_ref, 0), (rb_ref, 1))
    rs_refs = ((rsa_ref, 0), (rsa_ref, 1), (rsb_ref, 0), (rsb_ref, 1))
    tiles, own_tiles, raws = ADJ_SIDE[1], ADJ_OWN[1], ADJ_SIDE[2] + EY

    def initial(index, x):
        own = ((ql_ref, 0), (late_ref, 0), (ql_ref, PLANES))[index]
        layout = (
            ((messages, raws, 4), (messages, tiles, 3)),
            ((messages, 0, 3), (messages, tiles + 24, 2)),
            ((messages, raws + PLANES, 4), (messages, tiles + 40, 3)),
        )[index]
        value = widened(own, (late_ref, own_tiles + 32 * index), x, layout, side)
        if index == 1:
            value = less_plane_below(value, x, late_ref, ADJ_OWN, messages, ADJ_SIDE, side)
        return value

    for x in range(EX):
        stiff, buoy, damp = coefficients(initial(2, x), table_ref)
        coef_ref[0, x], coef_ref[1, x], coef_ref[2, x] = stiff, buoy, damp
        scale_ref[x] = stiff * damp
    own_strip = late_ref[ADJ_OWN[2] : ADJ_OWN[2] + EY]
    q_s, t_s, label_s = (
        whole_strip(own_strip, messages, ADJ_SIDE[2], slot, side) for slot in range(3)
    )
    t_s = t_s - strip_below(own_strip, messages, ADJ_SIDE[2], 3, side)
    stiff_s, buoy_s, damp_s = coefficients(label_s, table_ref)
    coef_strip_ref[0], coef_strip_ref[1], coef_strip_ref[2] = stiff_s, buoy_s, damp_s
    w_copy.wait()

    for step in range(1, STEPS + 1):
        k = STEPS - step
        rs_ref, place = rs_refs[k]
        q_s = q_s + rs_ref[place]
        u_s = stiff_s * damp_s * q_s
        flux_s, spread = strip_flux(u_s, buoy_s)
        t_s = t_s + spread
        q_s = damp_s * q_s + t_s
        edges = cut_edges(u_s, flux_s, cut_up, cut_down)
        r_ref, place = r_refs[k]
        r_first = (EARLY_PLANES if k < 2 else LATE_PLANES)[0]

        for x in range(step - 1, EX - step + 1):
            q = (initial(0, x) if step == 1 else q_ref[x]) + r_ref[place, x - r_first]
            q_ref[x] = q
            u_ref[x] = scale_ref[x] * q
            if step <= x < EX - step:
                edge_ref[x] = plane_edge(edges, x)

        for x in range(step - 1, EX - step):
            u, buoyancy = u_ref[x], coef_ref[1, x]
            slopes = [u_ref[x + 1] - u]
            if x >= step:
                slopes += [y_up(u) - u, z_up(u, edge_ref[x]) - u]
            for axis, slope in enumerate(slopes):
                flux_ref[axis, x] = buoyancy * slope
            if BX <= x < 2 * BX:
                for axis, slope in enumerate(slopes):
                    w = out_ref[1 + axis, x - BX] + slope[0:BY]
                    out_ref[1 + axis, x - BX] = w
                    hist_ref[k, 1 + axis, x - BX] = w

        for x in range(step, EX - step):
            flux_y, flux_z = flux_ref[1, x], flux_ref[2, x]
            spread = (flux_ref[0, x] - flux_ref[0, x - 1]) + (flux_y - y_down(flux_y))
            spread = spread + (flux_z - z_down(flux_z, edge_ref[x]))
            damped = coef_ref[2, x] * q_ref[x]
            t = (initial(1, x) if step == 1 else t_ref[x]) + spread
            if BX <= x < 2 * BX:
                hist_ref[k, 0, x - BX] = damped[0:BY]
            if step < STEPS:
                t_ref[x] = t
                q_ref[x] = damped + t
            else:
                out_ref[0, x - BX] = (damped + t)[0:BY]


def forward_kernel(
    wave_ref, own_s_ref, late_ref, even, odd, coef_ref, coef_strip_ref, s_ref, ss_ref, hist_ref,
    adjoint_ref, grad_hbm, adjoint_hbm,
    p_ref, spread_ref, edge_ref, flux_ref, grad_ref, sems,
):
    copies = [pltpu.make_async_copy(adjoint_ref, adjoint_hbm, sems.at[0])]
    copies[0].start()

    def send(index, kind, first, count):
        planes = pl.ds(first, count)
        copy = pltpu.make_async_copy(
            grad_ref.at[kind, planes], grad_hbm.at[kind, planes], sems.at[index]
        )
        copy.start()
        copies.append(copy)

    cut_up, cut_down = cut_flags()
    side = sides()
    messages = (even, odd)
    tiles, own_tiles = WAVE_SIDE[1], WAVE_OWN[1]

    def initial(index, x):
        layout = (
            ((messages, 0, 4), (messages, tiles, 3)),
            ((messages, PLANES, 3), (messages, tiles + 24, 2)),
        )[index]
        own = ((wave_ref, 0), (own_s_ref, 0))[index]
        value = widened(own, (late_ref, own_tiles + 32 * index), x, layout, side)
        if index == 1:
            value = less_plane_below(value, x, late_ref, WAVE_OWN, messages, WAVE_SIDE, side)
        return value

    own_strip = late_ref[WAVE_OWN[2] : WAVE_OWN[2] + EY]
    p_s, s_s = (
        whole_strip(own_strip, messages, WAVE_SIDE[2], slot, side) for slot in range(2)
    )
    s_s = s_s - strip_below(own_strip, messages, WAVE_SIDE[2], 2, side)
    stiff_s, buoy_s, damp_s = coef_strip_ref[0], coef_strip_ref[1], coef_strip_ref[2]

    for step in range(1, STEPS + 1):
        k = step - 1
        flux_s, spread = strip_flux(p_s, buoy_s)
        edges = cut_edges(p_s, flux_s, cut_up, cut_down)
        if step < STEPS:
            s_s = s_s - spread
            p_s = damp_s * (p_s - stiff_s * s_s) + ss_ref[k]

        for x in range(step - 1, EX - step + 1):
            if step == 1:
                p_ref[x] = initial(0, x)
            if step <= x < EX - step:
                edge_ref[x] = plane_edge(edges, x)

        for x in range(step - 1, EX - step):
            p, buoyancy = p_ref[x], coef_ref[1, x]
            slopes = [p_ref[x + 1] - p]
            if x >= step:
                slopes += [y_up(p) - p, z_up(p, edge_ref[x]) - p]
            for axis, slope in enumerate(slopes):
                flux_ref[axis, x] = buoyancy * slope
            if BX <= x < 2 * BX:
                place = x - BX
                term = hist_ref[k, 1, place] * slopes[0][0:BY]
                term = term + hist_ref[k, 2, place] * slopes[1][0:BY]
                term = term + hist_ref[k, 3, place] * slopes[2][0:BY]
                grad_ref[1, place] = -term if k == 0 else grad_ref[1, place] - term
        if step == STEPS:
            send(1, 1, 0, BX)

        for x in range(step, EX - step):
            flux_y, flux_z = flux_ref[1, x], flux_ref[2, x]
            spread = (flux_ref[0, x] - flux_ref[0, x - 1]) + (flux_y - y_down(flux_y))
            spread = spread + (flux_z - z_down(flux_z, edge_ref[x]))
            spread = (initial(1, x) if step == 1 else spread_ref[x]) - spread
            if step < STEPS:
                spread_ref[x] = spread
                p_ref[x] = (
                    coef_ref[2, x] * (p_ref[x] - coef_ref[0, x] * spread)
                    + s_ref[k, x - SOURCE_PLANES[0]]
                )
            if BX <= x < 2 * BX:
                place = x - BX
                term = hist_ref[k, 0, place] * spread[0:BY]
                grad_ref[0, place] = -term if k == 0 else grad_ref[0, place] - term
                if step == STEPS:
                    send(2 + place, 0, place, 1)
    for copy in copies:
        copy.wait()


def shape(*dims):
    return jax.ShapeDtypeStruct(dims, F32)


def call(kernel, outs, operands, scratch, places, micros=0.1, out_place="v"):
    spaces = {"h": pltpu.HBM, "a": pl.ANY, "v": pltpu.VMEM}
    operands = [
        pltpu.with_memory_space_constraint(operand, pltpu.HBM) if place == "h" else operand
        for operand, place in zip(operands, places)
    ]
    return pl.pallas_call(
        kernel,
        out_shape=outs,
        in_specs=[pl.BlockSpec(memory_space=spaces[place]) for place in places],
        out_specs=[pl.BlockSpec(memory_space=spaces[out_place])] * len(outs),
        scratch_shapes=scratch,
        compiler_params=pltpu.CompilerParams(vmem_limit_bytes=VMEM_LIMIT),
        cost_estimate=pl.CostEstimate(
            flops=0, bytes_accessed=int(3.69e6 * micros), transcendentals=0
        ),
    )(*operands)


def from_sides(sends, axes):
    count = lax.axis_size("gy")

    def route(offset):
        pairs = []
        for target in range(count):
            source = target + offset
            if 0 <= source < count:
                if "gz" in axes:
                    pairs += [(2 * source + z, 2 * target + 1 - z) for z in range(2)]
                else:
                    pairs.append((source, target))
        return pairs

    if count == 2:
        both = lax.ppermute(sends[0], axes, route(1) + route(-1))
        return both, both
    upward, downward = sends
    return lax.ppermute(downward, axes, route(1)), lax.ppermute(upward, axes, route(-1))


def rotated(array, axis, offset):
    count = lax.axis_size(axis)
    return lax.ppermute(array, axis, [((i + offset) % count, i) for i in range(count)])


def paired(array, odd):
    count = lax.axis_size("gx")
    pairs = []
    for i in range(count):
        partner = ((i - 1) ^ 1) + 1 if odd else i ^ 1
        pairs.append((partner if 0 <= partner < count else i, i))
    return lax.ppermute(array, "gx", pairs)


def local(
    stored, adjoint_end, labels, tissue, source_cells, source_wave, receiver_cells, receiver_wave
):
    assert lax.axis_size("gz") == 2 and labels.shape == (BX, BY, BZ) and tissue.shape[1] == 8
    half = lax.axis_size("gx") // 2
    arguments = [
        stored, adjoint_end, labels, tissue,
        receiver_cells.T, receiver_wave, source_cells.T, source_wave,
    ]
    ways = 1 if lax.axis_size("gy") == 2 else 2
    wave, ql, t, last_x, last_y, strips, table, receivers, receiver_wave, sources, source_wave, *sends = call(
        load_kernel,
        [
            shape(2 * PLANES, BZ),
            shape(2 * PLANES, BZ),
            shape(PLANES, BZ),
            shape(2 * BY, BZ),
            shape(2 * BX * 8, BZ),
            shape(3 * BY, BZ),
            shape(24, BZ),
        ]
        + [jax.ShapeDtypeStruct(array.shape, array.dtype) for array in arguments[4:]]
        + [shape(20 * 8, BZ)] * ways
        + [shape(2 * 8, BZ)] * ways,
        arguments,
        [
            pltpu.VMEM(stored.shape, F32),
            pltpu.VMEM(adjoint_end.shape, F32),
            pltpu.VMEM(labels.shape, jnp.int32),
            pltpu.SMEM(tissue.shape, F32),
            pltpu.SemaphoreType.DMA,
        ],
        "hhhhhhhh",
        1.4,
    )
    from_up, from_down = from_sides(sends[:ways], "gy")
    other = rotated(strips, "gz", 1)
    corner_up, corner_down = from_sides(sends[ways:], ("gy", "gz"))
    wave = rotated(wave, "gx", half)
    rb, rsb = call(
        late_kernel,
        [shape(2, EX * EY, BZ), shape(2, EY, BZ)],
        [receivers, receiver_wave],
        [],
        "vv",
        1.2,
    )
    early_planes, source_planes = (last - first for first, last in (EARLY_PLANES, SOURCE_PLANES))
    late, adj_late, token = call(
        merge_kernel,
        [shape(WAVE_FIX + 24, BZ), shape(ADJ_OWN[2] + EY, BZ), shape(8, BZ)],
        [from_up, from_down, corner_up, corner_down, strips, other, t, last_x, last_y, rsb],
        [],
        "vvvvvvvvva",
    )
    late = rotated(late, "gx", half)
    token = rotated(token, "gz", 1)
    ra, rsa = call(
        early_kernel,
        [shape(2, early_planes * EY, BZ), shape(2, EY, BZ)],
        [receivers, receiver_wave, adj_late],
        [],
        "vva",
        1.0,
    )
    ra, rb = ra.reshape(2, early_planes, EY, BZ), rb.reshape(2, EX, EY, BZ)
    even, odd, second = call(
        adjoint_join_kernel,
        [shape(ADJ_SIDE[2] + EY + 2 * PLANES, BZ)] * 2 + [shape(8, BZ)],
        [ql, adj_late, token, wave],
        [],
        "vvaa",
    )
    even, odd = paired(even, False), paired(odd, True)
    second = rotated(second, "gz", 1)
    src, src_strip = call(
        source_kernel,
        [shape(STEPS - 1, source_planes * EY, BZ), shape(STEPS - 1, EY, BZ)],
        [sources, source_wave, second],
        [],
        "vva",
        0.5,
    )
    src = src.reshape(STEPS - 1, source_planes, EY, BZ)
    own_s, wave_even, wave_odd = call(
        join_kernel,
        [shape(PLANES, BZ)] + [shape(WAVE_SIDE[2] + EY, BZ)] * 2,
        [wave, late, second],
        [],
        "vva",
    )
    wave_even, wave_odd = paired(wave_even, False), paired(wave_odd, True)
    adjoint_out, hist, coef, coef_strip = call(
        adjoint_kernel,
        [
            shape(4, BX, BY, BZ),
            shape(STEPS, 4, BX, BY, BZ),
            shape(3, EX, EY, BZ),
            shape(3, EY, BZ),
        ],
        [ql, adj_late, even, odd, adjoint_end, ra, rsa, rb, rsb, table],
        [pltpu.VMEM((EX, EY, BZ), F32)] * 5
        + [pltpu.VMEM((3, EX, EY, BZ), F32), pltpu.SemaphoreType.DMA],
        "vvvvhvvvvv",
        3.9,
    )
    return call(
        forward_kernel,
        [shape(2, BX, BY, BZ), shape(4, BX, BY, BZ)],
        [
            wave, own_s, late, wave_even, wave_odd, coef, coef_strip, src, src_strip, hist,
            adjoint_out,
        ],
        [pltpu.VMEM((EX, EY, BZ), F32)] * 3
        + [
            pltpu.VMEM((3, EX, EY, BZ), F32),
            pltpu.VMEM((2, BX, BY, BZ), F32),
            pltpu.SemaphoreType.DMA((2 + BX,)),
        ],
        "vvvvvvvvvvv",
        2.5,
        "a",
    )


def solution(mesh):
    return jax.shard_map(
        local,
        mesh=mesh,
        in_specs=(
            P("shot", "gx", "gy", "gz"),
            P("shot", "gx", "gy", "gz"),
            P("gx", "gy", "gz"),
            P(),
            P("shot", None),
            P(None, "shot"),
            P(),
            P(None, "shot"),
        ),
        out_specs=(P("shot", "gx", "gy", "gz"), P("shot", "gx", "gy", "gz")),
        check_vma=False,
    )
```

```python
import jax
import jax.numpy as jnp
from jax import lax
from jax.experimental import pallas as pl
from jax.experimental.pallas import tpu as pltpu
from jax.sharding import PartitionSpec as P

STEPS = 4
MARGIN = 4
BX, BY, BZ = 4, 32, 128
EX, EY = BX + 2 * MARGIN, BY + 2 * MARGIN
STRIP = 2 * MARGIN
F32 = jnp.float32
BF16 = jnp.bfloat16
VMEM_LIMIT = 16 * 1024 * 1024
PLANES = BX * BY
WAVE_OWN = (0, BY, BY + 9 * 8)
WAVE_FIX = WAVE_OWN[2] + EY
FIX_LANE = 3 * BX * STRIP
ADJ_OWN = (PLANES, PLANES + BY, PLANES + BY + 13 * 8)
WAVE_SIDE = (PLANES + 3 * BY, PLANES + 4 * BY, PLANES + 4 * BY + 6 * 8)
ADJ_SIDE = (3 * BY, 4 * BY, 4 * BY + 9 * 8)


def lanes(shape):
    return lax.broadcasted_iota(jnp.int32, shape, len(shape) - 1)


def rows(shape):
    return lax.broadcasted_iota(jnp.int32, shape, len(shape) - 2)


def run(copies):
    for copy in copies:
        copy.start()
    for copy in copies:
        copy.wait()


def coefficients(labels, table_ref):
    result = [jnp.zeros(labels.shape, F32) for _ in range(3)]
    for index in range(8):
        picked = labels == float(index + 1)
        for kind in range(3):
            row = kind * 8 + index
            result[kind] = jnp.where(picked, table_ref[row : row + 1], result[kind])
    return result


def buoyancy_of(labels, table_ref):
    result = jnp.zeros(labels.shape, F32)
    for index in range(8):
        result = jnp.where(labels == float(index + 1), table_ref[8 + index : 9 + index], result)
    return result


def half_turn(tile):
    return pltpu.roll(tile, MARGIN, 0)


def load_kernel(
    stored_hbm, adj_hbm, lab_hbm, tissue_hbm, rc_hbm, rw_hbm, sc_hbm, sw_hbm,
    wave_ref, ql_ref, q_ref, t_ref, last_x_ref, last_y_ref, strip_ref, table_ref,
    rc_ref, rw_ref, sc_ref, sw_ref, *rest,
):
    *sends, stored, adj, lab, tissue, sem = rest
    run([
        pltpu.make_async_copy(source, target, sem)
        for source, target in (
            (stored_hbm, stored), (adj_hbm, adj), (lab_hbm, lab), (tissue_hbm, tissue),
            (rc_hbm, rc_ref), (rw_hbm, rw_ref), (sc_hbm, sc_ref), (sw_hbm, sw_ref),
        )
    ])
    for index in range(tissue.shape[1]):
        speed = jnp.full((1, BZ), tissue[0, index], F32)
        density = jnp.full((1, BZ), tissue[1, index], F32)
        table_ref[index : index + 1] = density * speed
        table_ref[8 + index : 9 + index] = speed / density
        table_ref[16 + index : 17 + index] = 1.0 - jnp.full((1, BZ), tissue[2, index], F32)
    gy, gz = lax.axis_index("gy"), lax.axis_index("gz")
    lane = lanes((BY, BZ))
    row = rows((BY, BZ))
    tile_row = rows((8, BZ))
    strips = [jnp.zeros((BY, BZ), F32) for _ in range(3)]
    tiles = [None] * 39
    previous = [None, None]

    def edge_tile(block):
        return jnp.where(tile_row < MARGIN, block[0:8], block[BY - 8 : BY])

    for x in range(BX):
        labels = lab[x].astype(F32) + 1.0
        buoyancy = buoyancy_of(labels, table_ref)
        plane = slice(x * BY, x * BY + BY)
        fields = [stored[index, x] for index in range(4)] + [adj[0, x]]
        fields += [buoyancy * adj[index, x] for index in range(1, 4)] + [labels]
        wave_ref[plane] = fields[0]
        ql_ref[plane] = q_ref[plane] = fields[4]
        ql_ref[PLANES + x * BY : PLANES + x * BY + BY] = labels
        for index, block in enumerate(fields):
            tiles[index * BX + x] = edge_tile(block)
            group, slot = divmod(index, 4)
            base = slot * BX * STRIP + x * STRIP
            rolled = pltpu.roll(block, base + MARGIN, 1)
            first = base + MARGIN * gz
            strips[group] = jnp.where(
                (lane >= first) & (lane < first + MARGIN), rolled, strips[group]
            )
        for kind, (target, base) in enumerate(((wave_ref, PLANES), (t_ref, 0))):
            vx, vy, vz = fields[4 * kind + 1 : 4 * kind + 4]
            spread = vx if x == 0 else vx - previous[kind]
            spread = spread + (vy - jnp.where(row == 0, 0.0, pltpu.roll(vy, 1, 0)))
            spread = spread + (vz - jnp.where(lane == 0, 0.0, pltpu.roll(vz, 1, 1)))
            target[base + x * BY : base + x * BY + BY] = spread
            previous[kind] = vx
            index = (kind * BX + x) * 8
            last_y_ref[index : index + 8] = vy[BY - 8 : BY]
    for kind in range(2):
        last_x_ref[kind * BY : kind * BY + BY] = previous[kind]
    for group in range(3):
        strip_ref[group * BY : group * BY + BY] = strips[group]
        tiles[9 * BX + group] = edge_tile(strips[group])

    def joined(first, second):
        second = first if second is None else second
        upward = jnp.where(tile_row < MARGIN, half_turn(first), second)
        downward = jnp.where(tile_row < MARGIN, first, half_turn(second))
        if len(sends) == 2:
            return (jnp.where(gy == 0, upward, downward),)
        return upward, downward

    tiles.append(None)
    half = len(sends) // 2
    for place in range(20):
        for target, tile in zip(sends[:half], joined(tiles[2 * place], tiles[2 * place + 1])):
            target[place * 8 : place * 8 + 8] = tile
    for place in range(2):
        first = tiles[9 * BX + 2 * place]
        for target, tile in zip(sends[half:], joined(first, tiles[9 * BX + 2 * place + 1])):
            target[place * 8 : place * 8 + 8] = tile


def copy_rows(target, base, source, first, count):
    target[base : base + count] = source[pl.ds(pl.multiple_of(first, 8), count)]
    return base + count


def pair_planes():
    parity = lax.rem(lax.axis_index("gx"), 2)
    return 1 - parity, parity


def merge_kernel(
    from_up, from_down, corner_up, corner_down, strip_ref, other_ref,
    t_ref, last_x_ref, last_y_ref, _,
    wave_ref, adj_ref, token_ref,
):
    token_ref[...] = jnp.zeros((8, BZ), F32)
    gy = lax.axis_index("gy")
    tile_row = rows((8, BZ))
    row, lane = rows((BY, BZ)), lanes((BY, BZ))
    take_up = (tile_row < MARGIN) & (gy < lax.axis_size("gy") - 1)
    take_down = (tile_row >= MARGIN) & (gy > 0)
    _, cut_down = cut_flags()

    def halo(up, down, index):
        place, second = divmod(index, 2)
        sl = slice(place * 8, place * 8 + 8)
        above = half_turn(up[sl]) if second else up[sl]
        below = down[sl] if second else half_turn(down[sl])
        return jnp.where(take_up, above, jnp.where(take_down, below, 0.0))

    wide = []
    for group in range(3):
        sl = slice(group * BY, group * BY + BY)
        tile = halo(from_up, from_down, 9 * BX + group) + halo(corner_up, corner_down, group)
        wide.append(jnp.concatenate([strip_ref[sl] + other_ref[sl], tile], 0))
    strip_lane = lanes((EY, BZ))

    def strip_field(index):
        group, slot = divmod(index, 4)
        moved = pltpu.roll(wide[group], (BZ - slot * BX * STRIP) % BZ, 1) if slot else wide[group]
        return jnp.where(strip_lane < BX * STRIP, moved, 0.0)

    last_lanes = (BX - 1) * STRIP
    fix_row = jnp.zeros((8, BZ), F32)
    fix_lane = jnp.zeros((BY, BZ), F32)
    for kind, target in enumerate((wave_ref, adj_ref)):
        first = 4 * kind
        planes_end, x_end, tiles_end = (WAVE_OWN, ADJ_OWN)[kind]
        vx, vy, vz = (strip_field(first + 1 + axis) for axis in range(3))
        spread = vx - jnp.where(strip_lane < STRIP, 0.0, pltpu.roll(vx, STRIP, 1))
        spread = (spread + (vy - y_down(vy))) + (vz - pltpu.roll(vz, 1, 1))
        strip = strip_field(first)
        strip = strip + pltpu.roll(jnp.where(strip_lane < BX * STRIP, spread, 0.0), BX * STRIP, 1)
        last_slot = 2
        if kind == 1:
            strip = strip + pltpu.roll(strip_field(8), 2 * BX * STRIP, 1)
            last_slot = 3
        last = jnp.where(strip_lane >= last_lanes, vx, 0.0)
        strip = strip + pltpu.roll(last, last_slot * BX * STRIP - last_lanes, 1)
        target[planes_end:x_end] = last_x_ref[kind * BY : kind * BY + BY]

        vx_before = None
        for x in range(BX):
            vx_t, vy_t, vz_t = (
                halo(from_up, from_down, (first + 1 + axis) * BX + x) for axis in range(3)
            )
            below_z = pltpu.roll(vz, (BZ - (x * STRIP + MARGIN - 1)) % BZ, 1) * cut_down
            last_y = last_y_ref[(kind * BX + x) * 8 : (kind * BX + x) * 8 + 8]
            y_before = jnp.where(
                tile_row == 0, pltpu.roll(last_y, 1, 0), pltpu.roll(vy_t, 1, 0)
            )
            z_before = jnp.where(lane[0:8] == 0, below_z[BY:EY], pltpu.roll(vz_t, 1, 1))
            spread = vx_t if x == 0 else vx_t - vx_before
            spread = (spread + (vy_t - y_before)) + (vz_t - z_before)
            vx_before = vx_t
            if kind == 0:
                fix_row = jnp.where(tile_row == x, vy_t[7:8], fix_row)
                moved = pltpu.roll(below_z[0:BY], FIX_LANE + x, 1)
                fix_lane = jnp.where(lane == FIX_LANE + x, moved, fix_lane)
            else:
                block = t_ref[x * BY : x * BY + BY]
                block = block - jnp.where(row == 0, vy_t[7:8], 0.0)
                block = block - jnp.where(lane == 0, below_z[0:BY], 0.0)
                target[x * BY : x * BY + BY] = block
            base = x_end + x * 8
            target[base : base + 8] = halo(from_up, from_down, first * BX + x)
            target[base + 32 : base + 40] = spread
            if kind == 1:
                target[base + 64 : base + 72] = halo(from_up, from_down, 8 * BX + x)
        target[tiles_end - 8 : tiles_end] = vx_before
        if kind == 0:
            target[tiles_end : tiles_end + BY] = strip[0:BY] + fix_lane
            target[tiles_end + BY : tiles_end + EY] = strip[BY:EY]
            target[WAVE_FIX : WAVE_FIX + 8] = fix_row
            target[WAVE_FIX + 8 : WAVE_FIX + 24] = jnp.zeros((16, BZ), F32)
        else:
            target[tiles_end : tiles_end + EY] = strip


def adjoint_join_kernel(ql_ref, adj_ref, _a, _b, _c, even_ref, odd_ref, token_ref):
    token_ref[...] = jnp.zeros((8, BZ), F32)
    planes_end, x_end, tiles_end = ADJ_OWN
    for target, first in zip((even_ref, odd_ref), pair_planes()):
        base = copy_rows(target, 0, adj_ref, first * BY, 3 * BY)
        base = copy_rows(target, base, adj_ref, planes_end, BY)
        base = copy_rows(target, base, adj_ref, x_end + first * 8, 24)
        base = copy_rows(target, base, adj_ref, x_end + 32 + first * 16, 16)
        base = copy_rows(target, base, adj_ref, x_end + 64 + first * 8, 24)
        base = copy_rows(target, base, adj_ref, tiles_end - 8, 8 + EY)
        base = copy_rows(target, base, ql_ref, PLANES, PLANES)
    copy_rows(even_ref, base, ql_ref, 0, PLANES)


def join_kernel(wave_ref, late_ref, _, s_ref, even_ref, odd_ref):
    planes_end, x_end, tiles_end = WAVE_OWN
    row, lane = rows((BY, BZ)), lanes((BY, BZ))
    fix_lane = late_ref[tiles_end : tiles_end + BY]
    for x in range(BX):
        block = wave_ref[PLANES + x * BY : PLANES + x * BY + BY]
        fix_row = late_ref[WAVE_FIX + x : WAVE_FIX + x + 1]
        block = block - jnp.where(row == 0, fix_row, 0.0)
        block = block - jnp.where(lane == 0, pltpu.roll(fix_lane, BZ - FIX_LANE - x, 1), 0.0)
        s_ref[x * BY : x * BY + BY] = block
    for target, first in zip((even_ref, odd_ref), pair_planes()):
        base = copy_rows(target, 0, wave_ref, 0, PLANES)
        base = copy_rows(target, base, s_ref, first * BY, 3 * BY)
        base = copy_rows(target, base, late_ref, planes_end, BY)
        base = copy_rows(target, base, late_ref, x_end + first * 8, 24)
        base = copy_rows(target, base, late_ref, x_end + 32 + first * 16, 16)
        copy_rows(target, base, late_ref, tiles_end - 8, 8 + EY)


def split(values):
    high = values.astype(BF16)
    rest = values - high.astype(F32)
    middle = rest.astype(BF16)
    low = (rest - middle.astype(F32)).astype(BF16)
    return high, middle, low


def places(cells, sl):
    gx, gy, gz = (lax.axis_index(name) for name in ("gx", "gy", "gz"))
    cut = BZ * lax.axis_size("gz") // 2 - MARGIN
    cell_x = cells[0:1, sl] - (gx * BX - MARGIN)
    cell_y = cells[1:2, sl] - gy * BY
    cell_z = cells[2:3, sl]
    in_x = (cell_x >= 0) & (cell_x < EX)
    in_y = (cell_y >= -MARGIN) & (cell_y < BY + MARGIN)
    row = jnp.where(cell_y < 0, cell_y + EY, cell_y)
    flat = jnp.where(in_x & in_y, cell_x * EY + row, -1)
    row = jnp.where(in_y, row, -1)
    zz = cell_z - cut
    in_strip = in_x & (zz >= 0) & (zz < STRIP)
    strip_lane = jnp.where(in_strip, cell_x * STRIP + zz, -1)
    return flat, cell_z - gz * BZ, row, strip_lane


def hits(count, index):
    return rows((count, index.shape[1])) == index


def product(left, right):
    return lax.dot_general(
        left, right, (((1,), (1,)), ((), ())), preferred_element_type=F32
    )


def inject_points(cells, wave_ref, width, waves, planes, out_ref, strip_out_ref):
    count, low, total_rows = len(waves), planes[0] * EY, (planes[1] - planes[0]) * EY
    for start in range(0, cells.shape[1], width):
        sl = slice(start, start + width)
        flat, z, row, strip_lane = places(cells, sl)
        here = hits(total_rows, flat - low).astype(F32).astype(BF16)
        at_strip = hits(BZ, strip_lane).astype(F32).astype(BF16)
        at_z, at_row = hits(BZ, z), hits(EY, row)
        total = strip_total = None
        parts = [split(wave_ref[wave : wave + 1, sl]) for wave in waves]
        for part in range(3):
            amounts = [parts[wave][part].astype(F32) for wave in range(count)]
            right = jnp.concatenate([jnp.where(at_z, a, 0.0) for a in amounts], 0).astype(BF16)
            left = jnp.concatenate([jnp.where(at_row, a, 0.0) for a in amounts], 0).astype(BF16)
            term, strip_term = product(here, right), product(left, at_strip)
            total = term if part == 0 else total + term
            strip_total = strip_term if part == 0 else strip_total + strip_term
        for wave in range(count):
            value = total[:, wave * BZ : wave * BZ + BZ]
            strip_value = strip_total[wave * EY : wave * EY + EY]
            if start > 0:
                value = value + out_ref[wave]
                strip_value = strip_value + strip_out_ref[wave]
            out_ref[wave] = value
            strip_out_ref[wave] = strip_value


LATE_PLANES, EARLY_PLANES, SOURCE_PLANES = (0, EX), (2, EX - 2), (1, EX - 1)


def late_kernel(receivers, receiver_wave, r_ref, rs_ref):
    inject_points(receivers, receiver_wave, 256, (2, 3), LATE_PLANES, r_ref, rs_ref)


def early_kernel(receivers, receiver_wave, _, r_ref, rs_ref):
    inject_points(receivers, receiver_wave, 256, (0, 1), EARLY_PLANES, r_ref, rs_ref)


def source_kernel(sources, source_wave, _, s_ref, ss_ref):
    width = sources.shape[1]
    inject_points(sources, source_wave, width, (0, 1, 2), SOURCE_PLANES, s_ref, ss_ref)


def strip_of(packed, block, slot):
    lane = lanes(packed.shape)
    width = BX * STRIP
    shift = (block * width - slot * width) % BZ
    moved = pltpu.roll(packed, shift, 1) if shift else packed
    return jnp.where((lane >= block * width) & (lane < (block + 1) * width), moved, 0.0)


def y_up(v):
    return pltpu.roll(v, EY - 1, 0)


def y_down(v):
    return pltpu.roll(v, 1, 0)


def z_up(v, edge):
    return jnp.where(lanes(v.shape) == BZ - 1, edge, pltpu.roll(v, BZ - 1, 1))


def z_down(v, edge):
    return jnp.where(lanes(v.shape) == 0, edge, pltpu.roll(v, 1, 1))


def cut_edges(values, flux_z, cut_up, cut_down):
    place = lax.rem(lanes(values.shape), STRIP)
    above = jnp.where(place == MARGIN, values * cut_up, 0.0)
    below = jnp.where(place == MARGIN - 1, flux_z * cut_down, 0.0)
    return pltpu.roll(above, BZ - 2, 1) + below


def plane_edge(edges, x):
    return pltpu.roll(edges, (BZ - (x * STRIP + MARGIN - 1)) % BZ, 1)


def strip_flux(values, buoyancy):
    flux_x = buoyancy * (pltpu.roll(values, BZ - STRIP, 1) - values)
    flux_y = buoyancy * (y_up(values) - values)
    flux_z = buoyancy * (pltpu.roll(values, BZ - 1, 1) - values)
    spread = (flux_x - pltpu.roll(flux_x, STRIP, 1)) + (flux_y - y_down(flux_y))
    return flux_z, spread + (flux_z - pltpu.roll(flux_z, 1, 1))


def cut_flags():
    gz, half = lax.axis_index("gz"), lax.axis_size("gz") // 2
    return jnp.where(gz == half - 1, 1.0, 0.0), jnp.where(gz == half, 1.0, 0.0)


def sides():
    gx = lax.axis_index("gx")
    low = jnp.where(gx > 0, 1.0, 0.0)
    high = jnp.where(gx < lax.axis_size("gx") - 1, 1.0, 0.0)
    return low, high, lax.rem(gx, 2) == 0


def from_side(messages, first, count, block, side):
    even, odd = (ref[base + first : base + first + count] for ref, base in messages)
    low, high, even_above = side
    if block == 0:
        return jnp.where(even_above, odd, even) * low
    return jnp.where(even_above, even, odd) * high


def side_rows(base, wanted, step, block):
    planes = range(BX - wanted, BX) if block == 0 else range(wanted)
    return {plane: base + place * step for place, plane in enumerate(planes)}


def widened(own, own_tiles, x, layout, side):
    block, plane = divmod(x, BX)
    if block == 1:
        main = own[0][own[1] + plane * BY : own[1] + plane * BY + BY]
        tile = own_tiles[0][own_tiles[1] + plane * 8 : own_tiles[1] + plane * 8 + 8]
        return jnp.concatenate([main, tile], 0)
    parts = []
    for (messages, base, wanted), count in zip(layout, (BY, 8)):
        first = side_rows(base, wanted, count, block).get(plane)
        if first is None:
            parts.append(jnp.zeros((count, BZ), F32))
        else:
            parts.append(from_side(messages, first, count, block, side))
    return jnp.concatenate(parts, 0)


def less_plane_below(value, x, own_ref, own_rows, messages, side_rows_of, side):
    if x == BX:
        planes_end, _, tiles_end = side_rows_of
        main = from_side(messages, planes_end, BY, 0, side)
        tile = from_side(messages, tiles_end - 8, 8, 0, side)
    elif x == 2 * BX:
        planes_end, _, tiles_end = own_rows
        high = side[1]
        main = own_ref[planes_end : planes_end + BY] * high
        tile = own_ref[tiles_end - 8 : tiles_end] * high
    else:
        return value
    return value - jnp.concatenate([main, tile], 0)


def strip_below(own, messages, first, slot, side):
    lane = lanes(own.shape)
    width = BX * STRIP
    low = from_side(messages, first, EY, 0, side)
    low = pltpu.roll(low, (width - slot * width) % BZ, 1)
    own = pltpu.roll(own * side[1], (2 * width - slot * width) % BZ, 1)
    in_own = (lane >= width) & (lane < width + STRIP)
    in_high = (lane >= 2 * width) & (lane < 2 * width + STRIP)
    return jnp.where(in_own, low, jnp.where(in_high, own, 0.0))


def whole_strip(own, messages, first, slot, side):
    low = from_side(messages, first, EY, 0, side)
    high = from_side(messages, first, EY, 2, side)
    return strip_of(low, 0, slot) + strip_of(own, 1, slot) + strip_of(high, 2, slot)


def adjoint_kernel(
    ql_ref, q_odd, late_ref, even, odd, adj_hbm, ra_ref, rsa_ref, rb_ref, rsb_ref,
    table_ref,
    out_ref, hist_ref, coef_ref, coef_strip_ref,
    q_ref, t_ref, u_ref, scale_ref, edge_ref, flux_ref, w_sem,
):
    w_copy = pltpu.make_async_copy(adj_hbm.at[pl.ds(1, 3)], out_ref.at[pl.ds(1, 3)], w_sem)
    w_copy.start()
    cut_up, cut_down = cut_flags()
    side = sides()
    messages = ((even, 0), (odd, 0))
    q_messages = ((even, ADJ_SIDE[2] + EY + PLANES), (q_odd, 0))
    r_refs = ((ra_ref, 0), (ra_ref, 1), (rb_ref, 0), (rb_ref, 1))
    rs_refs = ((rsa_ref, 0), (rsa_ref, 1), (rsb_ref, 0), (rsb_ref, 1))
    tiles, own_tiles = ADJ_SIDE[1], ADJ_OWN[1]

    def initial(index, x):
        own = ((ql_ref, 0), (late_ref, 0), (ql_ref, PLANES))[index]
        layout = (
            ((q_messages, 0, 4), (messages, tiles, 3)),
            ((messages, 0, 3), (messages, tiles + 24, 2)),
            ((messages, ADJ_SIDE[2] + EY, 4), (messages, tiles + 40, 3)),
        )[index]
        value = widened(own, (late_ref, own_tiles + 32 * index), x, layout, side)
        if index == 1:
            value = less_plane_below(value, x, late_ref, ADJ_OWN, messages, ADJ_SIDE, side)
        return value

    for x in range(EX):
        stiff, buoy, damp = coefficients(initial(2, x), table_ref)
        coef_ref[0, x], coef_ref[1, x], coef_ref[2, x] = stiff, buoy, damp
        scale_ref[x] = stiff * damp
    own_strip = late_ref[ADJ_OWN[2] : ADJ_OWN[2] + EY]
    q_s, t_s, label_s = (
        whole_strip(own_strip, messages, ADJ_SIDE[2], slot, side) for slot in range(3)
    )
    t_s = t_s - strip_below(own_strip, messages, ADJ_SIDE[2], 3, side)
    stiff_s, buoy_s, damp_s = coefficients(label_s, table_ref)
    coef_strip_ref[0], coef_strip_ref[1], coef_strip_ref[2] = stiff_s, buoy_s, damp_s
    w_copy.wait()

    for step in range(1, STEPS + 1):
        k = STEPS - step
        rs_ref, place = rs_refs[k]
        q_s = q_s + rs_ref[place]
        u_s = stiff_s * damp_s * q_s
        flux_s, spread = strip_flux(u_s, buoy_s)
        t_s = t_s + spread
        q_s = damp_s * q_s + t_s
        edges = cut_edges(u_s, flux_s, cut_up, cut_down)
        r_ref, place = r_refs[k]
        r_first = (EARLY_PLANES if k < 2 else LATE_PLANES)[0]

        for x in range(step - 1, EX - step + 1):
            q = (initial(0, x) if step == 1 else q_ref[x]) + r_ref[place, x - r_first]
            q_ref[x] = q
            u_ref[x] = scale_ref[x] * q
            if step <= x < EX - step:
                edge_ref[x] = plane_edge(edges, x)

        for x in range(step - 1, EX - step):
            u, buoyancy = u_ref[x], coef_ref[1, x]
            slopes = [u_ref[x + 1] - u]
            if x >= step:
                slopes += [y_up(u) - u, z_up(u, edge_ref[x]) - u]
            for axis, slope in enumerate(slopes):
                flux_ref[axis, x] = buoyancy * slope
            if BX <= x < 2 * BX:
                for axis, slope in enumerate(slopes):
                    w = out_ref[1 + axis, x - BX] + slope[0:BY]
                    out_ref[1 + axis, x - BX] = w
                    hist_ref[k, 1 + axis, x - BX] = w

        for x in range(step, EX - step):
            flux_y, flux_z = flux_ref[1, x], flux_ref[2, x]
            spread = (flux_ref[0, x] - flux_ref[0, x - 1]) + (flux_y - y_down(flux_y))
            spread = spread + (flux_z - z_down(flux_z, edge_ref[x]))
            damped = coef_ref[2, x] * q_ref[x]
            t = (initial(1, x) if step == 1 else t_ref[x]) + spread
            if BX <= x < 2 * BX:
                hist_ref[k, 0, x - BX] = damped[0:BY]
            if step < STEPS:
                t_ref[x] = t
                q_ref[x] = damped + t
            else:
                out_ref[0, x - BX] = (damped + t)[0:BY]


def forward_kernel(
    wave_ref, own_s_ref, late_ref, even, odd, coef_ref, coef_strip_ref, s_ref, ss_ref, hist_ref,
    adjoint_ref, grad_hbm, adjoint_hbm,
    p_ref, spread_ref, edge_ref, flux_ref, grad_ref, sems,
):
    copies = [pltpu.make_async_copy(adjoint_ref, adjoint_hbm, sems.at[0])]
    copies[0].start()

    def send(index, kind, first, count):
        planes = pl.ds(first, count)
        copy = pltpu.make_async_copy(
            grad_ref.at[kind, planes], grad_hbm.at[kind, planes], sems.at[index]
        )
        copy.start()
        copies.append(copy)

    cut_up, cut_down = cut_flags()
    side = sides()
    messages = ((even, 0), (odd, 0))
    tiles, own_tiles = WAVE_SIDE[1], WAVE_OWN[1]

    def initial(index, x):
        layout = (
            ((messages, 0, 4), (messages, tiles, 3)),
            ((messages, PLANES, 3), (messages, tiles + 24, 2)),
        )[index]
        own = ((wave_ref, 0), (own_s_ref, 0))[index]
        value = widened(own, (late_ref, own_tiles + 32 * index), x, layout, side)
        if index == 1:
            value = less_plane_below(value, x, late_ref, WAVE_OWN, messages, WAVE_SIDE, side)
        return value

    own_strip = late_ref[WAVE_OWN[2] : WAVE_OWN[2] + EY]
    p_s, s_s = (
        whole_strip(own_strip, messages, WAVE_SIDE[2], slot, side) for slot in range(2)
    )
    s_s = s_s - strip_below(own_strip, messages, WAVE_SIDE[2], 2, side)
    stiff_s, buoy_s, damp_s = coef_strip_ref[0], coef_strip_ref[1], coef_strip_ref[2]

    for step in range(1, STEPS + 1):
        k = step - 1
        flux_s, spread = strip_flux(p_s, buoy_s)
        edges = cut_edges(p_s, flux_s, cut_up, cut_down)
        if step < STEPS:
            s_s = s_s - spread
            p_s = damp_s * (p_s - stiff_s * s_s) + ss_ref[k]

        for x in range(step - 1, EX - step + 1):
            if step == 1:
                p_ref[x] = initial(0, x)
            if step <= x < EX - step:
                edge_ref[x] = plane_edge(edges, x)

        for x in range(step - 1, EX - step):
            p, buoyancy = p_ref[x], coef_ref[1, x]
            slopes = [p_ref[x + 1] - p]
            if x >= step:
                slopes += [y_up(p) - p, z_up(p, edge_ref[x]) - p]
            for axis, slope in enumerate(slopes):
                flux_ref[axis, x] = buoyancy * slope
            if BX <= x < 2 * BX:
                place = x - BX
                term = hist_ref[k, 1, place] * slopes[0][0:BY]
                term = term + hist_ref[k, 2, place] * slopes[1][0:BY]
                term = term + hist_ref[k, 3, place] * slopes[2][0:BY]
                grad_ref[1, place] = -term if k == 0 else grad_ref[1, place] - term
        if step == STEPS:
            send(1, 1, 0, BX)

        for x in range(step, EX - step):
            flux_y, flux_z = flux_ref[1, x], flux_ref[2, x]
            spread = (flux_ref[0, x] - flux_ref[0, x - 1]) + (flux_y - y_down(flux_y))
            spread = spread + (flux_z - z_down(flux_z, edge_ref[x]))
            spread = (initial(1, x) if step == 1 else spread_ref[x]) - spread
            if step < STEPS:
                spread_ref[x] = spread
                p_ref[x] = (
                    coef_ref[2, x] * (p_ref[x] - coef_ref[0, x] * spread)
                    + s_ref[k, x - SOURCE_PLANES[0]]
                )
            if BX <= x < 2 * BX:
                place = x - BX
                term = hist_ref[k, 0, place] * spread[0:BY]
                grad_ref[0, place] = -term if k == 0 else grad_ref[0, place] - term
                if step == STEPS:
                    send(2 + place, 0, place, 1)
    for copy in copies:
        copy.wait()


def shape(*dims):
    return jax.ShapeDtypeStruct(dims, F32)


def call(kernel, outs, operands, scratch, places, micros=0.1, out_place="v"):
    spaces = {"h": pltpu.HBM, "a": pl.ANY, "v": pltpu.VMEM}
    operands = [
        pltpu.with_memory_space_constraint(operand, pltpu.HBM) if place == "h" else operand
        for operand, place in zip(operands, places)
    ]
    return pl.pallas_call(
        kernel,
        out_shape=outs,
        in_specs=[pl.BlockSpec(memory_space=spaces[place]) for place in places],
        out_specs=[pl.BlockSpec(memory_space=spaces[out_place])] * len(outs),
        scratch_shapes=scratch,
        compiler_params=pltpu.CompilerParams(vmem_limit_bytes=VMEM_LIMIT),
        cost_estimate=pl.CostEstimate(
            flops=0, bytes_accessed=int(3.69e6 * micros), transcendentals=0
        ),
    )(*operands)


def from_sides(sends, axes):
    count = lax.axis_size("gy")

    def route(offset):
        pairs = []
        for target in range(count):
            source = target + offset
            if 0 <= source < count:
                if "gz" in axes:
                    pairs += [(2 * source + z, 2 * target + 1 - z) for z in range(2)]
                else:
                    pairs.append((source, target))
        return pairs

    if count == 2:
        both = lax.ppermute(sends[0], axes, route(1) + route(-1))
        return both, both
    upward, downward = sends
    return lax.ppermute(downward, axes, route(1)), lax.ppermute(upward, axes, route(-1))


def rotated(array, axis, offset):
    count = lax.axis_size(axis)
    return lax.ppermute(array, axis, [((i + offset) % count, i) for i in range(count)])


def paired(array, odd):
    count = lax.axis_size("gx")
    pairs = []
    for i in range(count):
        partner = ((i - 1) ^ 1) + 1 if odd else i ^ 1
        pairs.append((partner if 0 <= partner < count else i, i))
    return lax.ppermute(array, "gx", pairs)


def local(
    stored, adjoint_end, labels, tissue, source_cells, source_wave, receiver_cells, receiver_wave
):
    assert lax.axis_size("gz") == 2 and labels.shape == (BX, BY, BZ) and tissue.shape[1] == 8
    half = lax.axis_size("gx") // 2
    arguments = [
        stored, adjoint_end, labels, tissue,
        receiver_cells.T, receiver_wave, source_cells.T, source_wave,
    ]
    ways = 1 if lax.axis_size("gy") == 2 else 2
    wave, ql, q, t, last_x, last_y, strips, table, receivers, receiver_wave, sources, source_wave, *sends = call(
        load_kernel,
        [
            shape(2 * PLANES, BZ),
            shape(2 * PLANES, BZ),
            shape(PLANES, BZ),
            shape(PLANES, BZ),
            shape(2 * BY, BZ),
            shape(2 * BX * 8, BZ),
            shape(3 * BY, BZ),
            shape(24, BZ),
        ]
        + [jax.ShapeDtypeStruct(array.shape, array.dtype) for array in arguments[4:]]
        + [shape(20 * 8, BZ)] * ways
        + [shape(2 * 8, BZ)] * ways,
        arguments,
        [
            pltpu.VMEM(stored.shape, F32),
            pltpu.VMEM(adjoint_end.shape, F32),
            pltpu.VMEM(labels.shape, jnp.int32),
            pltpu.SMEM(tissue.shape, F32),
            pltpu.SemaphoreType.DMA,
        ],
        "hhhhhhhh",
        1.4,
    )
    from_up, from_down = from_sides(sends[:ways], "gy")
    other = rotated(strips, "gz", 1)
    corner_up, corner_down = from_sides(sends[ways:], ("gy", "gz"))
    wave = rotated(wave, "gx", half)
    q_odd = paired(q, True)
    rb, rsb = call(
        late_kernel,
        [shape(2, EX * EY, BZ), shape(2, EY, BZ)],
        [receivers, receiver_wave],
        [],
        "vv",
        1.2,
    )
    early_planes, source_planes = (last - first for first, last in (EARLY_PLANES, SOURCE_PLANES))
    late, adj_late, token = call(
        merge_kernel,
        [shape(WAVE_FIX + 24, BZ), shape(ADJ_OWN[2] + EY, BZ), shape(8, BZ)],
        [from_up, from_down, corner_up, corner_down, strips, other, t, last_x, last_y, rsb],
        [],
        "vvvvvvvvva",
    )
    late = rotated(late, "gx", half)
    token = rotated(token, "gz", 1)
    ra, rsa = call(
        early_kernel,
        [shape(2, early_planes * EY, BZ), shape(2, EY, BZ)],
        [receivers, receiver_wave, adj_late],
        [],
        "vva",
        1.0,
    )
    ra, rb = ra.reshape(2, early_planes, EY, BZ), rb.reshape(2, EX, EY, BZ)
    even, odd, second = call(
        adjoint_join_kernel,
        [shape(ADJ_SIDE[2] + EY + 2 * PLANES, BZ), shape(ADJ_SIDE[2] + EY + PLANES, BZ), shape(8, BZ)],
        [ql, adj_late, token, wave, q_odd],
        [],
        "vvaaa",
    )
    even, odd = paired(even, False), paired(odd, True)
    second = rotated(second, "gz", 1)
    src, src_strip = call(
        source_kernel,
        [shape(STEPS - 1, source_planes * EY, BZ), shape(STEPS - 1, EY, BZ)],
        [sources, source_wave, adj_late],
        [],
        "vva",
        0.5,
    )
    src = src.reshape(STEPS - 1, source_planes, EY, BZ)
    own_s, wave_even, wave_odd = call(
        join_kernel,
        [shape(PLANES, BZ)] + [shape(WAVE_SIDE[2] + EY, BZ)] * 2,
        [wave, late, second],
        [],
        "vva",
    )
    wave_even, wave_odd = paired(wave_even, False), paired(wave_odd, True)
    adjoint_out, hist, coef, coef_strip = call(
        adjoint_kernel,
        [
            shape(4, BX, BY, BZ),
            shape(STEPS, 4, BX, BY, BZ),
            shape(3, EX, EY, BZ),
            shape(3, EY, BZ),
        ],
        [ql, q_odd, adj_late, even, odd, adjoint_end, ra, rsa, rb, rsb, table],
        [pltpu.VMEM((EX, EY, BZ), F32)] * 5
        + [pltpu.VMEM((3, EX, EY, BZ), F32), pltpu.SemaphoreType.DMA],
        "vvvvvhvvvvv",
        3.9,
    )
    return call(
        forward_kernel,
        [shape(2, BX, BY, BZ), shape(4, BX, BY, BZ)],
        [
            wave, own_s, late, wave_even, wave_odd, coef, coef_strip, src, src_strip, hist,
            adjoint_out,
        ],
        [pltpu.VMEM((EX, EY, BZ), F32)] * 3
        + [
            pltpu.VMEM((3, EX, EY, BZ), F32),
            pltpu.VMEM((2, BX, BY, BZ), F32),
            pltpu.SemaphoreType.DMA((2 + BX,)),
        ],
        "vvvvvvvvvvv",
        2.5,
        "a",
    )


def solution(mesh):
    return jax.shard_map(
        local,
        mesh=mesh,
        in_specs=(
            P("shot", "gx", "gy", "gz"),
            P("shot", "gx", "gy", "gz"),
            P("gx", "gy", "gz"),
            P(),
            P("shot", None),
            P(None, "shot"),
            P(),
            P(None, "shot"),
        ),
        out_specs=(P("shot", "gx", "gy", "gz"), P("shot", "gx", "gy", "gz")),
        check_vma=False,
    )
```

```python
import jax
import jax.numpy as jnp
from jax import lax
from jax.experimental import pallas as pl
from jax.experimental.pallas import tpu as pltpu
from jax.sharding import PartitionSpec as P

STEPS = 4
MARGIN = 4
BX, BY, BZ = 4, 32, 128
EX, EY = BX + 2 * MARGIN, BY + 2 * MARGIN
STRIP = 2 * MARGIN
F32 = jnp.float32
BF16 = jnp.bfloat16
VMEM_LIMIT = 16 * 1024 * 1024
PLANES = BX * BY
WAVE_OWN = (0, BY, BY + 9 * 8)
WAVE_FIX = WAVE_OWN[2] + EY
FIX_LANE = 3 * BX * STRIP
ADJ_OWN = (PLANES, PLANES + BY, PLANES + BY + 13 * 8)
WAVE_SIDE = (PLANES + 3 * BY, PLANES + 4 * BY, PLANES + 4 * BY + 6 * 8)
ADJ_SIDE = (3 * BY, 4 * BY, 4 * BY + 9 * 8)


def lanes(shape):
    return lax.broadcasted_iota(jnp.int32, shape, len(shape) - 1)


def rows(shape):
    return lax.broadcasted_iota(jnp.int32, shape, len(shape) - 2)


def run(copies):
    for copy in copies:
        copy.start()
    for copy in copies:
        copy.wait()


def coefficients(labels, table_ref):
    result = [jnp.zeros(labels.shape, F32) for _ in range(3)]
    for index in range(8):
        picked = labels == float(index + 1)
        for kind in range(3):
            row = kind * 8 + index
            result[kind] = jnp.where(picked, table_ref[row : row + 1], result[kind])
    return result


def buoyancy_of(labels, table_ref):
    result = jnp.zeros(labels.shape, F32)
    for index in range(8):
        result = jnp.where(labels == float(index + 1), table_ref[8 + index : 9 + index], result)
    return result


def half_turn(tile):
    return pltpu.roll(tile, MARGIN, 0)


def load_kernel(
    stored_hbm, adj_hbm, lab_hbm, tissue_hbm, rc_hbm, rw_hbm, sc_hbm, sw_hbm,
    wave_ref, ql_ref, t_ref, last_x_ref, last_y_ref, strip_ref, table_ref,
    rc_ref, rw_ref, sc_ref, sw_ref, *rest,
):
    *sends, stored, adj, lab, tissue, sem = rest
    run([
        pltpu.make_async_copy(source, target, sem)
        for source, target in (
            (stored_hbm, stored), (adj_hbm, adj), (lab_hbm, lab), (tissue_hbm, tissue),
            (rc_hbm, rc_ref), (rw_hbm, rw_ref), (sc_hbm, sc_ref), (sw_hbm, sw_ref),
        )
    ])
    for index in range(tissue.shape[1]):
        speed = jnp.full((1, BZ), tissue[0, index], F32)
        density = jnp.full((1, BZ), tissue[1, index], F32)
        table_ref[index : index + 1] = density * speed
        table_ref[8 + index : 9 + index] = speed / density
        table_ref[16 + index : 17 + index] = 1.0 - jnp.full((1, BZ), tissue[2, index], F32)
    gy, gz = lax.axis_index("gy"), lax.axis_index("gz")
    lane = lanes((BY, BZ))
    row = rows((BY, BZ))
    tile_row = rows((8, BZ))
    strips = [jnp.zeros((BY, BZ), F32) for _ in range(3)]
    tiles = [None] * 39
    previous = [None, None]

    def edge_tile(block):
        return jnp.where(tile_row < MARGIN, block[0:8], block[BY - 8 : BY])

    for x in range(BX):
        labels = lab[x].astype(F32) + 1.0
        buoyancy = buoyancy_of(labels, table_ref)
        plane = slice(x * BY, x * BY + BY)
        fields = [stored[index, x] for index in range(4)] + [adj[0, x]]
        fields += [buoyancy * adj[index, x] for index in range(1, 4)] + [labels]
        wave_ref[plane] = fields[0]
        ql_ref[plane] = fields[4]
        ql_ref[PLANES + x * BY : PLANES + x * BY + BY] = labels
        for index, block in enumerate(fields):
            tiles[index * BX + x] = edge_tile(block)
            group, slot = divmod(index, 4)
            base = slot * BX * STRIP + x * STRIP
            rolled = pltpu.roll(block, base + MARGIN, 1)
            first = base + MARGIN * gz
            strips[group] = jnp.where(
                (lane >= first) & (lane < first + MARGIN), rolled, strips[group]
            )
        for kind, (target, base) in enumerate(((wave_ref, PLANES), (t_ref, 0))):
            vx, vy, vz = fields[4 * kind + 1 : 4 * kind + 4]
            spread = vx if x == 0 else vx - previous[kind]
            spread = spread + (vy - jnp.where(row == 0, 0.0, pltpu.roll(vy, 1, 0)))
            spread = spread + (vz - jnp.where(lane == 0, 0.0, pltpu.roll(vz, 1, 1)))
            target[base + x * BY : base + x * BY + BY] = spread
            previous[kind] = vx
            index = (kind * BX + x) * 8
            last_y_ref[index : index + 8] = vy[BY - 8 : BY]
    for kind in range(2):
        last_x_ref[kind * BY : kind * BY + BY] = previous[kind]
    for group in range(3):
        strip_ref[group * BY : group * BY + BY] = strips[group]
        tiles[9 * BX + group] = edge_tile(strips[group])

    def joined(first, second):
        second = first if second is None else second
        upward = jnp.where(tile_row < MARGIN, half_turn(first), second)
        downward = jnp.where(tile_row < MARGIN, first, half_turn(second))
        if len(sends) == 2:
            return (jnp.where(gy == 0, upward, downward),)
        return upward, downward

    tiles.append(None)
    half = len(sends) // 2
    for place in range(20):
        for target, tile in zip(sends[:half], joined(tiles[2 * place], tiles[2 * place + 1])):
            target[place * 8 : place * 8 + 8] = tile
    for place in range(2):
        first = tiles[9 * BX + 2 * place]
        for target, tile in zip(sends[half:], joined(first, tiles[9 * BX + 2 * place + 1])):
            target[place * 8 : place * 8 + 8] = tile


def copy_rows(target, base, source, first, count):
    target[base : base + count] = source[pl.ds(pl.multiple_of(first, 8), count)]
    return base + count


def pair_planes():
    parity = lax.rem(lax.axis_index("gx"), 2)
    return 1 - parity, parity


def merge_kernel(
    from_up, from_down, corner_up, corner_down, strip_ref, other_ref,
    t_ref, last_x_ref, last_y_ref, _,
    wave_ref, adj_ref, token_ref,
):
    token_ref[...] = jnp.zeros((8, BZ), F32)
    gy = lax.axis_index("gy")
    tile_row = rows((8, BZ))
    row, lane = rows((BY, BZ)), lanes((BY, BZ))
    take_up = (tile_row < MARGIN) & (gy < lax.axis_size("gy") - 1)
    take_down = (tile_row >= MARGIN) & (gy > 0)
    _, cut_down = cut_flags()

    def halo(up, down, index):
        place, second = divmod(index, 2)
        sl = slice(place * 8, place * 8 + 8)
        above = half_turn(up[sl]) if second else up[sl]
        below = down[sl] if second else half_turn(down[sl])
        return jnp.where(take_up, above, jnp.where(take_down, below, 0.0))

    wide = []
    for group in range(3):
        sl = slice(group * BY, group * BY + BY)
        tile = halo(from_up, from_down, 9 * BX + group) + halo(corner_up, corner_down, group)
        wide.append(jnp.concatenate([strip_ref[sl] + other_ref[sl], tile], 0))
    strip_lane = lanes((EY, BZ))

    def strip_field(index):
        group, slot = divmod(index, 4)
        moved = pltpu.roll(wide[group], (BZ - slot * BX * STRIP) % BZ, 1) if slot else wide[group]
        return jnp.where(strip_lane < BX * STRIP, moved, 0.0)

    last_lanes = (BX - 1) * STRIP
    fix_row = jnp.zeros((8, BZ), F32)
    fix_lane = jnp.zeros((BY, BZ), F32)
    for kind, target in enumerate((wave_ref, adj_ref)):
        first = 4 * kind
        planes_end, x_end, tiles_end = (WAVE_OWN, ADJ_OWN)[kind]
        vx, vy, vz = (strip_field(first + 1 + axis) for axis in range(3))
        spread = vx - jnp.where(strip_lane < STRIP, 0.0, pltpu.roll(vx, STRIP, 1))
        spread = (spread + (vy - y_down(vy))) + (vz - pltpu.roll(vz, 1, 1))
        strip = strip_field(first)
        strip = strip + pltpu.roll(jnp.where(strip_lane < BX * STRIP, spread, 0.0), BX * STRIP, 1)
        last_slot = 2
        if kind == 1:
            strip = strip + pltpu.roll(strip_field(8), 2 * BX * STRIP, 1)
            last_slot = 3
        last = jnp.where(strip_lane >= last_lanes, vx, 0.0)
        strip = strip + pltpu.roll(last, last_slot * BX * STRIP - last_lanes, 1)
        target[planes_end:x_end] = last_x_ref[kind * BY : kind * BY + BY]

        vx_before = None
        for x in range(BX):
            vx_t, vy_t, vz_t = (
                halo(from_up, from_down, (first + 1 + axis) * BX + x) for axis in range(3)
            )
            below_z = pltpu.roll(vz, (BZ - (x * STRIP + MARGIN - 1)) % BZ, 1) * cut_down
            last_y = last_y_ref[(kind * BX + x) * 8 : (kind * BX + x) * 8 + 8]
            y_before = jnp.where(
                tile_row == 0, pltpu.roll(last_y, 1, 0), pltpu.roll(vy_t, 1, 0)
            )
            z_before = jnp.where(lane[0:8] == 0, below_z[BY:EY], pltpu.roll(vz_t, 1, 1))
            spread = vx_t if x == 0 else vx_t - vx_before
            spread = (spread + (vy_t - y_before)) + (vz_t - z_before)
            vx_before = vx_t
            if kind == 0:
                fix_row = jnp.where(tile_row == x, vy_t[7:8], fix_row)
                moved = pltpu.roll(below_z[0:BY], FIX_LANE + x, 1)
                fix_lane = jnp.where(lane == FIX_LANE + x, moved, fix_lane)
            else:
                block = t_ref[x * BY : x * BY + BY]
                block = block - jnp.where(row == 0, vy_t[7:8], 0.0)
                block = block - jnp.where(lane == 0, below_z[0:BY], 0.0)
                target[x * BY : x * BY + BY] = block
            base = x_end + x * 8
            target[base : base + 8] = halo(from_up, from_down, first * BX + x)
            target[base + 32 : base + 40] = spread
            if kind == 1:
                target[base + 64 : base + 72] = halo(from_up, from_down, 8 * BX + x)
        target[tiles_end - 8 : tiles_end] = vx_before
        if kind == 0:
            target[tiles_end : tiles_end + BY] = strip[0:BY] + fix_lane
            target[tiles_end + BY : tiles_end + EY] = strip[BY:EY]
            target[WAVE_FIX : WAVE_FIX + 8] = fix_row
            target[WAVE_FIX + 8 : WAVE_FIX + 24] = jnp.zeros((16, BZ), F32)
        else:
            target[tiles_end : tiles_end + EY] = strip


def adjoint_join_kernel(ql_ref, adj_ref, _a, _b, even_ref, odd_ref):
    planes_end, x_end, tiles_end = ADJ_OWN
    for target, first in zip((even_ref, odd_ref), pair_planes()):
        base = copy_rows(target, 0, adj_ref, first * BY, 3 * BY)
        base = copy_rows(target, base, adj_ref, planes_end, BY)
        base = copy_rows(target, base, adj_ref, x_end + first * 8, 24)
        base = copy_rows(target, base, adj_ref, x_end + 32 + first * 16, 16)
        base = copy_rows(target, base, adj_ref, x_end + 64 + first * 8, 24)
        base = copy_rows(target, base, adj_ref, tiles_end - 8, 8 + EY)
        copy_rows(target, base, ql_ref, 0, 2 * PLANES)


def join_kernel(wave_ref, late_ref, s_ref, even_ref, odd_ref):
    planes_end, x_end, tiles_end = WAVE_OWN
    row, lane = rows((BY, BZ)), lanes((BY, BZ))
    fix_lane = late_ref[tiles_end : tiles_end + BY]
    for x in range(BX):
        block = wave_ref[PLANES + x * BY : PLANES + x * BY + BY]
        fix_row = late_ref[WAVE_FIX + x : WAVE_FIX + x + 1]
        block = block - jnp.where(row == 0, fix_row, 0.0)
        block = block - jnp.where(lane == 0, pltpu.roll(fix_lane, BZ - FIX_LANE - x, 1), 0.0)
        s_ref[x * BY : x * BY + BY] = block
    for target, first in zip((even_ref, odd_ref), pair_planes()):
        base = copy_rows(target, 0, wave_ref, 0, PLANES)
        base = copy_rows(target, base, s_ref, first * BY, 3 * BY)
        base = copy_rows(target, base, late_ref, planes_end, BY)
        base = copy_rows(target, base, late_ref, x_end + first * 8, 24)
        base = copy_rows(target, base, late_ref, x_end + 32 + first * 16, 16)
        copy_rows(target, base, late_ref, tiles_end - 8, 8 + EY)


def split(values):
    high = values.astype(BF16)
    rest = values - high.astype(F32)
    middle = rest.astype(BF16)
    low = (rest - middle.astype(F32)).astype(BF16)
    return high, middle, low


def places(cells, sl):
    gx, gy, gz = (lax.axis_index(name) for name in ("gx", "gy", "gz"))
    cut = BZ * lax.axis_size("gz") // 2 - MARGIN
    cell_x = cells[0:1, sl] - (gx * BX - MARGIN)
    cell_y = cells[1:2, sl] - gy * BY
    cell_z = cells[2:3, sl]
    in_x = (cell_x >= 0) & (cell_x < EX)
    in_y = (cell_y >= -MARGIN) & (cell_y < BY + MARGIN)
    row = jnp.where(cell_y < 0, cell_y + EY, cell_y)
    flat = jnp.where(in_x & in_y, cell_x * EY + row, -1)
    row = jnp.where(in_y, row, -1)
    zz = cell_z - cut
    in_strip = in_x & (zz >= 0) & (zz < STRIP)
    strip_lane = jnp.where(in_strip, cell_x * STRIP + zz, -1)
    return flat, cell_z - gz * BZ, row, strip_lane


def hits(count, index):
    return rows((count, index.shape[1])) == index


def product(left, right):
    return lax.dot_general(
        left, right, (((1,), (1,)), ((), ())), preferred_element_type=F32
    )


def inject_points(cells, wave_ref, width, waves, planes, out_ref, strip_out_ref):
    count, low, total_rows = len(waves), planes[0] * EY, (planes[1] - planes[0]) * EY
    for start in range(0, cells.shape[1], width):
        sl = slice(start, start + width)
        flat, z, row, strip_lane = places(cells, sl)
        here = hits(total_rows, flat - low).astype(F32).astype(BF16)
        at_strip = hits(BZ, strip_lane).astype(F32).astype(BF16)
        at_z, at_row = hits(BZ, z), hits(EY, row)
        total = strip_total = None
        parts = [split(wave_ref[wave : wave + 1, sl]) for wave in waves]
        for part in range(3):
            amounts = [parts[wave][part].astype(F32) for wave in range(count)]
            right = jnp.concatenate([jnp.where(at_z, a, 0.0) for a in amounts], 0).astype(BF16)
            left = jnp.concatenate([jnp.where(at_row, a, 0.0) for a in amounts], 0).astype(BF16)
            term, strip_term = product(here, right), product(left, at_strip)
            total = term if part == 0 else total + term
            strip_total = strip_term if part == 0 else strip_total + strip_term
        for wave in range(count):
            value = total[:, wave * BZ : wave * BZ + BZ]
            strip_value = strip_total[wave * EY : wave * EY + EY]
            if start > 0:
                value = value + out_ref[wave]
                strip_value = strip_value + strip_out_ref[wave]
            out_ref[wave] = value
            strip_out_ref[wave] = strip_value


LATE_PLANES, EARLY_PLANES, SOURCE_PLANES = (0, EX), (2, EX - 2), (1, EX - 1)


def late_kernel(receivers, receiver_wave, r_ref, rs_ref):
    inject_points(receivers, receiver_wave, 256, (2, 3), LATE_PLANES, r_ref, rs_ref)


def early_kernel(receivers, receiver_wave, _, r_ref, rs_ref):
    inject_points(receivers, receiver_wave, 256, (0, 1), EARLY_PLANES, r_ref, rs_ref)


def source_kernel(sources, source_wave, _, s_ref, ss_ref):
    width = sources.shape[1]
    inject_points(sources, source_wave, width, (0, 1, 2), SOURCE_PLANES, s_ref, ss_ref)


def strip_of(packed, block, slot):
    lane = lanes(packed.shape)
    width = BX * STRIP
    shift = (block * width - slot * width) % BZ
    moved = pltpu.roll(packed, shift, 1) if shift else packed
    return jnp.where((lane >= block * width) & (lane < (block + 1) * width), moved, 0.0)


def y_up(v):
    return pltpu.roll(v, EY - 1, 0)


def y_down(v):
    return pltpu.roll(v, 1, 0)


def z_up(v, edge):
    return jnp.where(lanes(v.shape) == BZ - 1, edge, pltpu.roll(v, BZ - 1, 1))


def z_down(v, edge):
    return jnp.where(lanes(v.shape) == 0, edge, pltpu.roll(v, 1, 1))


def cut_edges(values, flux_z, cut_up, cut_down):
    place = lax.rem(lanes(values.shape), STRIP)
    above = jnp.where(place == MARGIN, values * cut_up, 0.0)
    below = jnp.where(place == MARGIN - 1, flux_z * cut_down, 0.0)
    return pltpu.roll(above, BZ - 2, 1) + below


def plane_edge(edges, x):
    return pltpu.roll(edges, (BZ - (x * STRIP + MARGIN - 1)) % BZ, 1)


def strip_flux(values, buoyancy):
    flux_x = buoyancy * (pltpu.roll(values, BZ - STRIP, 1) - values)
    flux_y = buoyancy * (y_up(values) - values)
    flux_z = buoyancy * (pltpu.roll(values, BZ - 1, 1) - values)
    spread = (flux_x - pltpu.roll(flux_x, STRIP, 1)) + (flux_y - y_down(flux_y))
    return flux_z, spread + (flux_z - pltpu.roll(flux_z, 1, 1))


def cut_flags():
    gz, half = lax.axis_index("gz"), lax.axis_size("gz") // 2
    return jnp.where(gz == half - 1, 1.0, 0.0), jnp.where(gz == half, 1.0, 0.0)


def sides():
    gx = lax.axis_index("gx")
    low = jnp.where(gx > 0, 1.0, 0.0)
    high = jnp.where(gx < lax.axis_size("gx") - 1, 1.0, 0.0)
    return low, high, lax.rem(gx, 2) == 0


def from_side(messages, first, count, block, side):
    even, odd = (message[first : first + count] for message in messages)
    low, high, even_above = side
    if block == 0:
        return jnp.where(even_above, odd, even) * low
    return jnp.where(even_above, even, odd) * high


def side_rows(base, wanted, step, block):
    planes = range(BX - wanted, BX) if block == 0 else range(wanted)
    return {plane: base + place * step for place, plane in enumerate(planes)}


def widened(own, own_tiles, x, layout, side):
    block, plane = divmod(x, BX)
    if block == 1:
        main = own[0][own[1] + plane * BY : own[1] + plane * BY + BY]
        tile = own_tiles[0][own_tiles[1] + plane * 8 : own_tiles[1] + plane * 8 + 8]
        return jnp.concatenate([main, tile], 0)
    parts = []
    for (messages, base, wanted), count in zip(layout, (BY, 8)):
        first = side_rows(base, wanted, count, block).get(plane)
        if first is None:
            parts.append(jnp.zeros((count, BZ), F32))
        else:
            parts.append(from_side(messages, first, count, block, side))
    return jnp.concatenate(parts, 0)


def less_plane_below(value, x, own_ref, own_rows, messages, side_rows_of, side):
    if x == BX:
        planes_end, _, tiles_end = side_rows_of
        main = from_side(messages, planes_end, BY, 0, side)
        tile = from_side(messages, tiles_end - 8, 8, 0, side)
    elif x == 2 * BX:
        planes_end, _, tiles_end = own_rows
        high = side[1]
        main = own_ref[planes_end : planes_end + BY] * high
        tile = own_ref[tiles_end - 8 : tiles_end] * high
    else:
        return value
    return value - jnp.concatenate([main, tile], 0)


def strip_below(own, messages, first, slot, side):
    lane = lanes(own.shape)
    width = BX * STRIP
    low = from_side(messages, first, EY, 0, side)
    low = pltpu.roll(low, (width - slot * width) % BZ, 1)
    own = pltpu.roll(own * side[1], (2 * width - slot * width) % BZ, 1)
    in_own = (lane >= width) & (lane < width + STRIP)
    in_high = (lane >= 2 * width) & (lane < 2 * width + STRIP)
    return jnp.where(in_own, low, jnp.where(in_high, own, 0.0))


def whole_strip(own, messages, first, slot, side):
    low = from_side(messages, first, EY, 0, side)
    high = from_side(messages, first, EY, 2, side)
    return strip_of(low, 0, slot) + strip_of(own, 1, slot) + strip_of(high, 2, slot)


def adjoint_kernel(
    ql_ref, late_ref, even, odd, adj_hbm, ra_ref, rsa_ref, rb_ref, rsb_ref,
    table_ref,
    out_ref, hist_ref, coef_ref, coef_strip_ref,
    q_ref, t_ref, u_ref, scale_ref, edge_ref, flux_ref, w_sem,
):
    w_copy = pltpu.make_async_copy(adj_hbm.at[pl.ds(1, 3)], out_ref.at[pl.ds(1, 3)], w_sem)
    w_copy.start()
    cut_up, cut_down = cut_flags()
    side = sides()
    messages = (even, odd)
    r_refs = ((ra_ref, 0), (ra_ref, 1), (rb_ref, 0), (rb_ref, 1))
    rs_refs = ((rsa_ref, 0), (rsa_ref, 1), (rsb_ref, 0), (rsb_ref, 1))
    tiles, own_tiles, raws = ADJ_SIDE[1], ADJ_OWN[1], ADJ_SIDE[2] + EY

    def initial(index, x):
        own = ((ql_ref, 0), (late_ref, 0), (ql_ref, PLANES))[index]
        layout = (
            ((messages, raws, 4), (messages, tiles, 3)),
            ((messages, 0, 3), (messages, tiles + 24, 2)),
            ((messages, raws + PLANES, 4), (messages, tiles + 40, 3)),
        )[index]
        value = widened(own, (late_ref, own_tiles + 32 * index), x, layout, side)
        if index == 1:
            value = less_plane_below(value, x, late_ref, ADJ_OWN, messages, ADJ_SIDE, side)
        return value

    for x in range(EX):
        stiff, buoy, damp = coefficients(initial(2, x), table_ref)
        coef_ref[0, x], coef_ref[1, x], coef_ref[2, x] = stiff, buoy, damp
        scale_ref[x] = stiff * damp
    own_strip = late_ref[ADJ_OWN[2] : ADJ_OWN[2] + EY]
    q_s, t_s, label_s = (
        whole_strip(own_strip, messages, ADJ_SIDE[2], slot, side) for slot in range(3)
    )
    t_s = t_s - strip_below(own_strip, messages, ADJ_SIDE[2], 3, side)
    stiff_s, buoy_s, damp_s = coefficients(label_s, table_ref)
    scale_s = stiff_s * damp_s
    coef_strip_ref[0], coef_strip_ref[1], coef_strip_ref[2] = stiff_s, buoy_s, damp_s
    w_copy.wait()

    for step in range(1, STEPS + 1):
        rs_ref, place = rs_refs[STEPS - step]
        q_s = q_s + rs_ref[place]
        u_s = scale_s * q_s
        flux_s, spread = strip_flux(u_s, buoy_s)
        t_s = t_s + spread
        q_s = damp_s * q_s + t_s
        edges = cut_edges(u_s, flux_s, cut_up, cut_down)
        for x in range(step, EX - step):
            edge_ref[step - 1, x] = plane_edge(edges, x)

    for step in range(1, STEPS + 1):
        k = STEPS - step
        r_ref, place = r_refs[k]
        r_first = (EARLY_PLANES if k < 2 else LATE_PLANES)[0]

        for x in range(step - 1, EX - step + 1):
            q = (initial(0, x) if step == 1 else q_ref[x]) + r_ref[place, x - r_first]
            q_ref[x] = q
            u_ref[x] = scale_ref[x] * q

        for x in range(step - 1, EX - step):
            u, buoyancy = u_ref[x], coef_ref[1, x]
            slopes = [u_ref[x + 1] - u]
            if x >= step:
                slopes += [y_up(u) - u, z_up(u, edge_ref[step - 1, x]) - u]
            for axis, slope in enumerate(slopes):
                flux_ref[axis, x] = buoyancy * slope
            if BX <= x < 2 * BX:
                for axis, slope in enumerate(slopes):
                    w = out_ref[1 + axis, x - BX] + slope[0:BY]
                    out_ref[1 + axis, x - BX] = w
                    hist_ref[k, 1 + axis, x - BX] = w

        for x in range(step, EX - step):
            flux_y, flux_z = flux_ref[1, x], flux_ref[2, x]
            spread = (flux_ref[0, x] - flux_ref[0, x - 1]) + (flux_y - y_down(flux_y))
            spread = spread + (flux_z - z_down(flux_z, edge_ref[step - 1, x]))
            damped = coef_ref[2, x] * q_ref[x]
            t = (initial(1, x) if step == 1 else t_ref[x]) + spread
            if BX <= x < 2 * BX:
                hist_ref[k, 0, x - BX] = damped[0:BY]
            if step < STEPS:
                t_ref[x] = t
                q_ref[x] = damped + t
            else:
                out_ref[0, x - BX] = (damped + t)[0:BY]


def forward_kernel(
    wave_ref, own_s_ref, late_ref, even, odd, coef_ref, coef_strip_ref, s_ref, ss_ref, hist_ref,
    adjoint_ref, grad_hbm, adjoint_hbm,
    p_ref, spread_ref, edge_ref, flux_ref, grad_ref, sems,
):
    copies = [pltpu.make_async_copy(adjoint_ref, adjoint_hbm, sems.at[0])]
    copies[0].start()

    def send(index, kind, first, count):
        planes = pl.ds(first, count)
        copy = pltpu.make_async_copy(
            grad_ref.at[kind, planes], grad_hbm.at[kind, planes], sems.at[index]
        )
        copy.start()
        copies.append(copy)

    cut_up, cut_down = cut_flags()
    side = sides()
    messages = (even, odd)
    tiles, own_tiles = WAVE_SIDE[1], WAVE_OWN[1]

    def initial(index, x):
        layout = (
            ((messages, 0, 4), (messages, tiles, 3)),
            ((messages, PLANES, 3), (messages, tiles + 24, 2)),
        )[index]
        own = ((wave_ref, 0), (own_s_ref, 0))[index]
        value = widened(own, (late_ref, own_tiles + 32 * index), x, layout, side)
        if index == 1:
            value = less_plane_below(value, x, late_ref, WAVE_OWN, messages, WAVE_SIDE, side)
        return value

    own_strip = late_ref[WAVE_OWN[2] : WAVE_OWN[2] + EY]
    p_s, s_s = (
        whole_strip(own_strip, messages, WAVE_SIDE[2], slot, side) for slot in range(2)
    )
    s_s = s_s - strip_below(own_strip, messages, WAVE_SIDE[2], 2, side)
    stiff_s, buoy_s, damp_s = coef_strip_ref[0], coef_strip_ref[1], coef_strip_ref[2]

    for step in range(1, STEPS + 1):
        flux_s, spread = strip_flux(p_s, buoy_s)
        edges = cut_edges(p_s, flux_s, cut_up, cut_down)
        if step < STEPS:
            s_s = s_s - spread
            p_s = damp_s * (p_s - stiff_s * s_s) + ss_ref[step - 1]
        for x in range(step, EX - step):
            edge_ref[step - 1, x] = plane_edge(edges, x)
    for x in range(EX):
        p_ref[x] = initial(0, x)

    for step in range(1, STEPS + 1):
        k = step - 1
        for x in range(step - 1, EX - step):
            p, buoyancy = p_ref[x], coef_ref[1, x]
            slopes = [p_ref[x + 1] - p]
            if x >= step:
                slopes += [y_up(p) - p, z_up(p, edge_ref[step - 1, x]) - p]
            for axis, slope in enumerate(slopes):
                flux_ref[axis, x] = buoyancy * slope
            if BX <= x < 2 * BX:
                place = x - BX
                term = hist_ref[k, 1, place] * slopes[0][0:BY]
                term = term + hist_ref[k, 2, place] * slopes[1][0:BY]
                term = term + hist_ref[k, 3, place] * slopes[2][0:BY]
                grad_ref[1, place] = -term if k == 0 else grad_ref[1, place] - term
        if step == STEPS:
            send(1, 1, 0, BX)

        for x in range(step, EX - step):
            flux_y, flux_z = flux_ref[1, x], flux_ref[2, x]
            spread = (flux_ref[0, x] - flux_ref[0, x - 1]) + (flux_y - y_down(flux_y))
            spread = spread + (flux_z - z_down(flux_z, edge_ref[step - 1, x]))
            spread = (initial(1, x) if step == 1 else spread_ref[x]) - spread
            if step < STEPS:
                spread_ref[x] = spread
                p_ref[x] = (
                    coef_ref[2, x] * (p_ref[x] - coef_ref[0, x] * spread)
                    + s_ref[k, x - SOURCE_PLANES[0]]
                )
            if BX <= x < 2 * BX:
                place = x - BX
                term = hist_ref[k, 0, place] * spread[0:BY]
                grad_ref[0, place] = -term if k == 0 else grad_ref[0, place] - term
                if step == STEPS:
                    send(2 + place, 0, place, 1)
    for copy in copies:
        copy.wait()


def shape(*dims):
    return jax.ShapeDtypeStruct(dims, F32)


def call(kernel, outs, operands, scratch, places, micros=0.1, out_place="v"):
    spaces = {"h": pltpu.HBM, "a": pl.ANY, "v": pltpu.VMEM}
    operands = [
        pltpu.with_memory_space_constraint(operand, pltpu.HBM) if place == "h" else operand
        for operand, place in zip(operands, places)
    ]
    return pl.pallas_call(
        kernel,
        out_shape=outs,
        in_specs=[pl.BlockSpec(memory_space=spaces[place]) for place in places],
        out_specs=[pl.BlockSpec(memory_space=spaces[out_place])] * len(outs),
        scratch_shapes=scratch,
        compiler_params=pltpu.CompilerParams(vmem_limit_bytes=VMEM_LIMIT),
        cost_estimate=pl.CostEstimate(
            flops=0, bytes_accessed=int(3.69e6 * micros), transcendentals=0
        ),
    )(*operands)


def from_sides(sends, axes):
    count = lax.axis_size("gy")

    def route(offset):
        pairs = []
        for target in range(count):
            source = target + offset
            if 0 <= source < count:
                if "gz" in axes:
                    pairs += [(2 * source + z, 2 * target + 1 - z) for z in range(2)]
                else:
                    pairs.append((source, target))
        return pairs

    if count == 2:
        both = lax.ppermute(sends[0], axes, route(1) + route(-1))
        return both, both
    upward, downward = sends
    return lax.ppermute(downward, axes, route(1)), lax.ppermute(upward, axes, route(-1))


def rotated(array, axis, offset):
    count = lax.axis_size(axis)
    return lax.ppermute(array, axis, [((i + offset) % count, i) for i in range(count)])


def paired(array, odd):
    count = lax.axis_size("gx")
    pairs = []
    for i in range(count):
        partner = ((i - 1) ^ 1) + 1 if odd else i ^ 1
        pairs.append((partner if 0 <= partner < count else i, i))
    return lax.ppermute(array, "gx", pairs)


def local(
    stored, adjoint_end, labels, tissue, source_cells, source_wave, receiver_cells, receiver_wave
):
    assert lax.axis_size("gz") == 2 and labels.shape == (BX, BY, BZ) and tissue.shape[1] == 8
    half = lax.axis_size("gx") // 2
    arguments = [
        stored, adjoint_end, labels, tissue,
        receiver_cells.T, receiver_wave, source_cells.T, source_wave,
    ]
    ways = 1 if lax.axis_size("gy") == 2 else 2
    wave, ql, t, last_x, last_y, strips, table, receivers, receiver_wave, sources, source_wave, *sends = call(
        load_kernel,
        [
            shape(2 * PLANES, BZ),
            shape(2 * PLANES, BZ),
            shape(PLANES, BZ),
            shape(2 * BY, BZ),
            shape(2 * BX * 8, BZ),
            shape(3 * BY, BZ),
            shape(24, BZ),
        ]
        + [jax.ShapeDtypeStruct(array.shape, array.dtype) for array in arguments[4:]]
        + [shape(20 * 8, BZ)] * ways
        + [shape(2 * 8, BZ)] * ways,
        arguments,
        [
            pltpu.VMEM(stored.shape, F32),
            pltpu.VMEM(adjoint_end.shape, F32),
            pltpu.VMEM(labels.shape, jnp.int32),
            pltpu.SMEM(tissue.shape, F32),
            pltpu.SemaphoreType.DMA,
        ],
        "hhhhhhhh",
        1.4,
    )
    from_up, from_down = from_sides(sends[:ways], "gy")
    other = rotated(strips, "gz", 1)
    corner_up, corner_down = from_sides(sends[ways:], ("gy", "gz"))
    wave = rotated(wave, "gx", half)
    rb, rsb = call(
        late_kernel,
        [shape(2, EX * EY, BZ), shape(2, EY, BZ)],
        [receivers, receiver_wave],
        [],
        "vv",
        1.2,
    )
    early_planes, source_planes = (last - first for first, last in (EARLY_PLANES, SOURCE_PLANES))
    late, adj_late, token = call(
        merge_kernel,
        [shape(WAVE_FIX + 24, BZ), shape(ADJ_OWN[2] + EY, BZ), shape(8, BZ)],
        [from_up, from_down, corner_up, corner_down, strips, other, t, last_x, last_y, rsb],
        [],
        "vvvvvvvvva",
    )
    late = rotated(late, "gx", half)
    token = rotated(token, "gz", 1)
    ra, rsa = call(
        early_kernel,
        [shape(2, early_planes * EY, BZ), shape(2, EY, BZ)],
        [receivers, receiver_wave, adj_late],
        [],
        "vva",
        1.0,
    )
    ra, rb = ra.reshape(2, early_planes, EY, BZ), rb.reshape(2, EX, EY, BZ)
    even, odd = call(
        adjoint_join_kernel,
        [shape(ADJ_SIDE[2] + EY + 2 * PLANES, BZ)] * 2,
        [ql, adj_late, token, wave],
        [],
        "vvaa",
    )
    even, odd = paired(even, False), paired(odd, True)
    src, src_strip = call(
        source_kernel,
        [shape(STEPS - 1, source_planes * EY, BZ), shape(STEPS - 1, EY, BZ)],
        [sources, source_wave, adj_late],
        [],
        "vva",
        0.5,
    )
    src = src.reshape(STEPS - 1, source_planes, EY, BZ)
    own_s, wave_even, wave_odd = call(
        join_kernel,
        [shape(PLANES, BZ)] + [shape(WAVE_SIDE[2] + EY, BZ)] * 2,
        [wave, late],
        [],
        "vv",
    )
    wave_even, wave_odd = paired(wave_even, False), paired(wave_odd, True)
    adjoint_out, hist, coef, coef_strip = call(
        adjoint_kernel,
        [
            shape(4, BX, BY, BZ),
            shape(STEPS, 4, BX, BY, BZ),
            shape(3, EX, EY, BZ),
            shape(3, EY, BZ),
        ],
        [ql, adj_late, even, odd, adjoint_end, ra, rsa, rb, rsb, table],
        [pltpu.VMEM((EX, EY, BZ), F32)] * 4
        + [
            pltpu.VMEM((STEPS, EX, EY, BZ), F32),
            pltpu.VMEM((3, EX, EY, BZ), F32),
            pltpu.SemaphoreType.DMA,
        ],
        "vvvvhvvvvv",
        3.9,
    )
    return call(
        forward_kernel,
        [shape(2, BX, BY, BZ), shape(4, BX, BY, BZ)],
        [
            wave, own_s, late, wave_even, wave_odd, coef, coef_strip, src, src_strip, hist,
            adjoint_out,
        ],
        [pltpu.VMEM((EX, EY, BZ), F32)] * 2
        + [
            pltpu.VMEM((STEPS, EX, EY, BZ), F32),
            pltpu.VMEM((3, EX, EY, BZ), F32),
            pltpu.VMEM((2, BX, BY, BZ), F32),
            pltpu.SemaphoreType.DMA((2 + BX,)),
        ],
        "vvvvvvvvvvv",
        2.5,
        "a",
    )


def solution(mesh):
    return jax.shard_map(
        local,
        mesh=mesh,
        in_specs=(
            P("shot", "gx", "gy", "gz"),
            P("shot", "gx", "gy", "gz"),
            P("gx", "gy", "gz"),
            P(),
            P("shot", None),
            P(None, "shot"),
            P(),
            P(None, "shot"),
        ),
        out_specs=(P("shot", "gx", "gy", "gz"), P("shot", "gx", "gy", "gz")),
        check_vma=False,
    )
```

```python
import jax
import jax.numpy as jnp
from jax import lax
from jax.experimental import pallas as pl
from jax.experimental.pallas import tpu as pltpu
from jax.sharding import PartitionSpec as P

STEPS = 4
MARGIN = 4
BX, BY, BZ = 4, 32, 128
EX, EY = BX + 2 * MARGIN, BY + 2 * MARGIN
STRIP = 2 * MARGIN
F32 = jnp.float32
BF16 = jnp.bfloat16
VMEM_LIMIT = 16 * 1024 * 1024
PLANES = BX * BY
WAVE_OWN = (0, BY, BY + 9 * 8)
WAVE_FIX = WAVE_OWN[2] + EY
FIX_LANE = 3 * BX * STRIP
ADJ_OWN = (PLANES, PLANES + BY, PLANES + BY + 13 * 8)
WAVE_SIDE = (PLANES + 3 * BY, PLANES + 4 * BY, PLANES + 4 * BY + 6 * 8)
ADJ_SIDE = (3 * BY, 4 * BY, 4 * BY + 9 * 8)


def lanes(shape):
    return lax.broadcasted_iota(jnp.int32, shape, len(shape) - 1)


def rows(shape):
    return lax.broadcasted_iota(jnp.int32, shape, len(shape) - 2)


def run(copies):
    for copy in copies:
        copy.start()
    for copy in copies:
        copy.wait()


def coefficients(labels, table_ref):
    result = [jnp.zeros(labels.shape, F32) for _ in range(3)]
    for index in range(8):
        picked = labels == float(index + 1)
        for kind in range(3):
            row = kind * 8 + index
            result[kind] = jnp.where(picked, table_ref[row : row + 1], result[kind])
    return result


def buoyancy_of(labels, table_ref):
    result = jnp.zeros(labels.shape, F32)
    for index in range(8):
        result = jnp.where(labels == float(index + 1), table_ref[8 + index : 9 + index], result)
    return result


def half_turn(tile):
    return pltpu.roll(tile, MARGIN, 0)


def load_kernel(
    stored_hbm, adj_hbm, lab_hbm, tissue_hbm, rc_hbm, rw_hbm, sc_hbm, sw_hbm,
    wave_ref, ql_ref, t_ref, last_x_ref, last_y_ref, strip_ref, table_ref,
    rc_ref, rw_ref, sc_ref, sw_ref, *rest,
):
    *sends, stored, adj, lab, tissue, sem = rest
    run([
        pltpu.make_async_copy(source, target, sem)
        for source, target in (
            (stored_hbm, stored), (adj_hbm, adj), (lab_hbm, lab), (tissue_hbm, tissue),
            (rc_hbm, rc_ref), (rw_hbm, rw_ref), (sc_hbm, sc_ref), (sw_hbm, sw_ref),
        )
    ])
    for index in range(tissue.shape[1]):
        speed = jnp.full((1, BZ), tissue[0, index], F32)
        density = jnp.full((1, BZ), tissue[1, index], F32)
        table_ref[index : index + 1] = density * speed
        table_ref[8 + index : 9 + index] = speed / density
        table_ref[16 + index : 17 + index] = 1.0 - jnp.full((1, BZ), tissue[2, index], F32)
    gy, gz = lax.axis_index("gy"), lax.axis_index("gz")
    lane = lanes((BY, BZ))
    row = rows((BY, BZ))
    tile_row = rows((8, BZ))
    strips = [jnp.zeros((BY, BZ), F32) for _ in range(3)]
    tiles = [None] * 39
    previous = [None, None]

    def edge_tile(block):
        return jnp.where(tile_row < MARGIN, block[0:8], block[BY - 8 : BY])

    for x in range(BX):
        labels = lab[x].astype(F32) + 1.0
        buoyancy = buoyancy_of(labels, table_ref)
        plane = slice(x * BY, x * BY + BY)
        fields = [stored[index, x] for index in range(4)] + [adj[0, x]]
        fields += [buoyancy * adj[index, x] for index in range(1, 4)] + [labels]
        wave_ref[plane] = fields[0]
        ql_ref[plane] = fields[4]
        ql_ref[PLANES + x * BY : PLANES + x * BY + BY] = labels
        for index, block in enumerate(fields):
            tiles[index * BX + x] = edge_tile(block)
            group, slot = divmod(index, 4)
            base = slot * BX * STRIP + x * STRIP
            rolled = pltpu.roll(block, base + MARGIN, 1)
            first = base + MARGIN * gz
            strips[group] = jnp.where(
                (lane >= first) & (lane < first + MARGIN), rolled, strips[group]
            )
        for kind, (target, base) in enumerate(((wave_ref, PLANES), (t_ref, 0))):
            vx, vy, vz = fields[4 * kind + 1 : 4 * kind + 4]
            spread = vx if x == 0 else vx - previous[kind]
            spread = spread + (vy - jnp.where(row == 0, 0.0, pltpu.roll(vy, 1, 0)))
            spread = spread + (vz - jnp.where(lane == 0, 0.0, pltpu.roll(vz, 1, 1)))
            target[base + x * BY : base + x * BY + BY] = spread
            previous[kind] = vx
            index = (kind * BX + x) * 8
            last_y_ref[index : index + 8] = vy[BY - 8 : BY]
    for kind in range(2):
        last_x_ref[kind * BY : kind * BY + BY] = previous[kind]
    for group in range(3):
        strip_ref[group * BY : group * BY + BY] = strips[group]
        tiles[9 * BX + group] = edge_tile(strips[group])

    def joined(first, second):
        second = first if second is None else second
        upward = jnp.where(tile_row < MARGIN, half_turn(first), second)
        downward = jnp.where(tile_row < MARGIN, first, half_turn(second))
        if len(sends) == 2:
            return (jnp.where(gy == 0, upward, downward),)
        return upward, downward

    tiles.append(None)
    half = len(sends) // 2
    for place in range(20):
        for target, tile in zip(sends[:half], joined(tiles[2 * place], tiles[2 * place + 1])):
            target[place * 8 : place * 8 + 8] = tile
    for place in range(2):
        first = tiles[9 * BX + 2 * place]
        for target, tile in zip(sends[half:], joined(first, tiles[9 * BX + 2 * place + 1])):
            target[place * 8 : place * 8 + 8] = tile


def copy_rows(target, base, source, first, count):
    target[base : base + count] = source[pl.ds(pl.multiple_of(first, 8), count)]
    return base + count


def pair_planes():
    parity = lax.rem(lax.axis_index("gx"), 2)
    return 1 - parity, parity


def merge_kernel(
    from_up, from_down, corner_up, corner_down, strip_ref, other_ref,
    t_ref, last_x_ref, last_y_ref, _,
    wave_ref, adj_ref,
):
    gy = lax.axis_index("gy")
    tile_row = rows((8, BZ))
    row, lane = rows((BY, BZ)), lanes((BY, BZ))
    take_up = (tile_row < MARGIN) & (gy < lax.axis_size("gy") - 1)
    take_down = (tile_row >= MARGIN) & (gy > 0)
    _, cut_down = cut_flags()

    def halo(up, down, index):
        place, second = divmod(index, 2)
        sl = slice(place * 8, place * 8 + 8)
        above = half_turn(up[sl]) if second else up[sl]
        below = down[sl] if second else half_turn(down[sl])
        return jnp.where(take_up, above, jnp.where(take_down, below, 0.0))

    wide = []
    for group in range(3):
        sl = slice(group * BY, group * BY + BY)
        tile = halo(from_up, from_down, 9 * BX + group) + halo(corner_up, corner_down, group)
        wide.append(jnp.concatenate([strip_ref[sl] + other_ref[sl], tile], 0))
    strip_lane = lanes((EY, BZ))

    def strip_field(index):
        group, slot = divmod(index, 4)
        moved = pltpu.roll(wide[group], (BZ - slot * BX * STRIP) % BZ, 1) if slot else wide[group]
        return jnp.where(strip_lane < BX * STRIP, moved, 0.0)

    last_lanes = (BX - 1) * STRIP
    fix_row = jnp.zeros((8, BZ), F32)
    fix_lane = jnp.zeros((BY, BZ), F32)
    for kind, target in enumerate((wave_ref, adj_ref)):
        first = 4 * kind
        planes_end, x_end, tiles_end = (WAVE_OWN, ADJ_OWN)[kind]
        vx, vy, vz = (strip_field(first + 1 + axis) for axis in range(3))
        spread = vx - jnp.where(strip_lane < STRIP, 0.0, pltpu.roll(vx, STRIP, 1))
        spread = (spread + (vy - y_down(vy))) + (vz - pltpu.roll(vz, 1, 1))
        strip = strip_field(first)
        strip = strip + pltpu.roll(jnp.where(strip_lane < BX * STRIP, spread, 0.0), BX * STRIP, 1)
        last_slot = 2
        if kind == 1:
            strip = strip + pltpu.roll(strip_field(8), 2 * BX * STRIP, 1)
            last_slot = 3
        last = jnp.where(strip_lane >= last_lanes, vx, 0.0)
        strip = strip + pltpu.roll(last, last_slot * BX * STRIP - last_lanes, 1)
        target[planes_end:x_end] = last_x_ref[kind * BY : kind * BY + BY]

        vx_before = None
        for x in range(BX):
            vx_t, vy_t, vz_t = (
                halo(from_up, from_down, (first + 1 + axis) * BX + x) for axis in range(3)
            )
            below_z = pltpu.roll(vz, (BZ - (x * STRIP + MARGIN - 1)) % BZ, 1) * cut_down
            last_y = last_y_ref[(kind * BX + x) * 8 : (kind * BX + x) * 8 + 8]
            y_before = jnp.where(
                tile_row == 0, pltpu.roll(last_y, 1, 0), pltpu.roll(vy_t, 1, 0)
            )
            z_before = jnp.where(lane[0:8] == 0, below_z[BY:EY], pltpu.roll(vz_t, 1, 1))
            spread = vx_t if x == 0 else vx_t - vx_before
            spread = (spread + (vy_t - y_before)) + (vz_t - z_before)
            vx_before = vx_t
            if kind == 0:
                fix_row = jnp.where(tile_row == x, vy_t[7:8], fix_row)
                moved = pltpu.roll(below_z[0:BY], FIX_LANE + x, 1)
                fix_lane = jnp.where(lane == FIX_LANE + x, moved, fix_lane)
            else:
                block = t_ref[x * BY : x * BY + BY]
                block = block - jnp.where(row == 0, vy_t[7:8], 0.0)
                block = block - jnp.where(lane == 0, below_z[0:BY], 0.0)
                target[x * BY : x * BY + BY] = block
            base = x_end + x * 8
            target[base : base + 8] = halo(from_up, from_down, first * BX + x)
            target[base + 32 : base + 40] = spread
            if kind == 1:
                target[base + 64 : base + 72] = halo(from_up, from_down, 8 * BX + x)
        target[tiles_end - 8 : tiles_end] = vx_before
        if kind == 0:
            target[tiles_end : tiles_end + BY] = strip[0:BY] + fix_lane
            target[tiles_end + BY : tiles_end + EY] = strip[BY:EY]
            target[WAVE_FIX : WAVE_FIX + 8] = fix_row
            target[WAVE_FIX + 8 : WAVE_FIX + 24] = jnp.zeros((16, BZ), F32)
        else:
            target[tiles_end : tiles_end + EY] = strip


def adjoint_join_kernel(ql_ref, adj_ref, _, even_ref, odd_ref):
    planes_end, x_end, tiles_end = ADJ_OWN
    for target, first in zip((even_ref, odd_ref), pair_planes()):
        base = copy_rows(target, 0, adj_ref, first * BY, 3 * BY)
        base = copy_rows(target, base, adj_ref, planes_end, BY)
        base = copy_rows(target, base, adj_ref, x_end + first * 8, 24)
        base = copy_rows(target, base, adj_ref, x_end + 32 + first * 16, 16)
        base = copy_rows(target, base, adj_ref, x_end + 64 + first * 8, 24)
        base = copy_rows(target, base, adj_ref, tiles_end - 8, 8 + EY)
        copy_rows(target, base, ql_ref, 0, 2 * PLANES)


def join_kernel(wave_ref, late_ref, s_ref, even_ref, odd_ref):
    planes_end, x_end, tiles_end = WAVE_OWN
    row, lane = rows((BY, BZ)), lanes((BY, BZ))
    fix_lane = late_ref[tiles_end : tiles_end + BY]
    for x in range(BX):
        block = wave_ref[PLANES + x * BY : PLANES + x * BY + BY]
        fix_row = late_ref[WAVE_FIX + x : WAVE_FIX + x + 1]
        block = block - jnp.where(row == 0, fix_row, 0.0)
        block = block - jnp.where(lane == 0, pltpu.roll(fix_lane, BZ - FIX_LANE - x, 1), 0.0)
        s_ref[x * BY : x * BY + BY] = block
    for target, first in zip((even_ref, odd_ref), pair_planes()):
        base = copy_rows(target, 0, wave_ref, 0, PLANES)
        base = copy_rows(target, base, s_ref, first * BY, 3 * BY)
        base = copy_rows(target, base, late_ref, planes_end, BY)
        base = copy_rows(target, base, late_ref, x_end + first * 8, 24)
        base = copy_rows(target, base, late_ref, x_end + 32 + first * 16, 16)
        copy_rows(target, base, late_ref, tiles_end - 8, 8 + EY)


def split(values):
    high = values.astype(BF16)
    rest = values - high.astype(F32)
    middle = rest.astype(BF16)
    low = (rest - middle.astype(F32)).astype(BF16)
    return high, middle, low


def places(cells, sl):
    gx, gy, gz = (lax.axis_index(name) for name in ("gx", "gy", "gz"))
    cut = BZ * lax.axis_size("gz") // 2 - MARGIN
    cell_x = cells[0:1, sl] - (gx * BX - MARGIN)
    cell_y = cells[1:2, sl] - gy * BY
    cell_z = cells[2:3, sl]
    in_x = (cell_x >= 0) & (cell_x < EX)
    in_y = (cell_y >= -MARGIN) & (cell_y < BY + MARGIN)
    row = jnp.where(cell_y < 0, cell_y + EY, cell_y)
    flat = jnp.where(in_x & in_y, cell_x * EY + row, -1)
    row = jnp.where(in_y, row, -1)
    zz = cell_z - cut
    in_strip = in_x & (zz >= 0) & (zz < STRIP)
    strip_lane = jnp.where(in_strip, cell_x * STRIP + zz, -1)
    return flat, cell_z - gz * BZ, row, strip_lane


def hits(count, index):
    return rows((count, index.shape[1])) == index


def product(left, right):
    return lax.dot_general(
        left, right, (((1,), (1,)), ((), ())), preferred_element_type=F32
    )


def inject_points(cells, wave_ref, width, waves, planes, out_ref, strip_out_ref):
    count, low, total_rows = len(waves), planes[0] * EY, (planes[1] - planes[0]) * EY
    for start in range(0, cells.shape[1], width):
        sl = slice(start, start + width)
        flat, z, row, strip_lane = places(cells, sl)
        here = hits(total_rows, flat - low).astype(F32).astype(BF16)
        at_strip = hits(BZ, strip_lane).astype(F32).astype(BF16)
        at_z, at_row = hits(BZ, z), hits(EY, row)
        total = strip_total = None
        parts = [split(wave_ref[wave : wave + 1, sl]) for wave in waves]
        for part in range(3):
            amounts = [parts[wave][part].astype(F32) for wave in range(count)]
            right = jnp.concatenate([jnp.where(at_z, a, 0.0) for a in amounts], 0).astype(BF16)
            left = jnp.concatenate([jnp.where(at_row, a, 0.0) for a in amounts], 0).astype(BF16)
            term, strip_term = product(here, right), product(left, at_strip)
            total = term if part == 0 else total + term
            strip_total = strip_term if part == 0 else strip_total + strip_term
        for wave in range(count):
            value = total[:, wave * BZ : wave * BZ + BZ]
            strip_value = strip_total[wave * EY : wave * EY + EY]
            if start > 0:
                value = value + out_ref[wave]
                strip_value = strip_value + strip_out_ref[wave]
            out_ref[wave] = value
            strip_out_ref[wave] = strip_value


LATE_PLANES, EARLY_PLANES, SOURCE_PLANES = (0, EX), (2, EX - 2), (1, EX - 1)


def late_kernel(receivers, receiver_wave, r_ref, rs_ref):
    inject_points(receivers, receiver_wave, 256, (2, 3), LATE_PLANES, r_ref, rs_ref)


def early_kernel(receivers, receiver_wave, _, r_ref, rs_ref):
    inject_points(receivers, receiver_wave, 256, (0, 1), EARLY_PLANES, r_ref, rs_ref)


def source_kernel(sources, source_wave, _, s_ref, ss_ref):
    width = sources.shape[1]
    inject_points(sources, source_wave, width, (0, 1, 2), SOURCE_PLANES, s_ref, ss_ref)


def strip_of(packed, block, slot):
    lane = lanes(packed.shape)
    width = BX * STRIP
    shift = (block * width - slot * width) % BZ
    moved = pltpu.roll(packed, shift, 1) if shift else packed
    return jnp.where((lane >= block * width) & (lane < (block + 1) * width), moved, 0.0)


def y_up(v):
    return pltpu.roll(v, EY - 1, 0)


def y_down(v):
    return pltpu.roll(v, 1, 0)


def z_up(v, edge):
    return jnp.where(lanes(v.shape) == BZ - 1, edge, pltpu.roll(v, BZ - 1, 1))


def z_down(v, edge):
    return jnp.where(lanes(v.shape) == 0, edge, pltpu.roll(v, 1, 1))


def cut_edges(values, flux_z, cut_up, cut_down):
    place = lax.rem(lanes(values.shape), STRIP)
    above = jnp.where(place == MARGIN, values * cut_up, 0.0)
    below = jnp.where(place == MARGIN - 1, flux_z * cut_down, 0.0)
    return pltpu.roll(above, BZ - 2, 1) + below


def plane_edge(edges, x):
    return pltpu.roll(edges, (BZ - (x * STRIP + MARGIN - 1)) % BZ, 1)


def strip_flux(values, buoyancy):
    flux_x = buoyancy * (pltpu.roll(values, BZ - STRIP, 1) - values)
    flux_y = buoyancy * (y_up(values) - values)
    flux_z = buoyancy * (pltpu.roll(values, BZ - 1, 1) - values)
    spread = (flux_x - pltpu.roll(flux_x, STRIP, 1)) + (flux_y - y_down(flux_y))
    return flux_z, spread + (flux_z - pltpu.roll(flux_z, 1, 1))


def cut_flags():
    gz, half = lax.axis_index("gz"), lax.axis_size("gz") // 2
    return jnp.where(gz == half - 1, 1.0, 0.0), jnp.where(gz == half, 1.0, 0.0)


def sides():
    gx = lax.axis_index("gx")
    low = jnp.where(gx > 0, 1.0, 0.0)
    high = jnp.where(gx < lax.axis_size("gx") - 1, 1.0, 0.0)
    return low, high, lax.rem(gx, 2) == 0


def from_side(messages, first, count, block, side):
    even, odd = (message[first : first + count] for message in messages)
    low, high, even_above = side
    if block == 0:
        return jnp.where(even_above, odd, even) * low
    return jnp.where(even_above, even, odd) * high


def side_rows(base, wanted, step, block):
    planes = range(BX - wanted, BX) if block == 0 else range(wanted)
    return {plane: base + place * step for place, plane in enumerate(planes)}


def widened(own, own_tiles, x, layout, side):
    block, plane = divmod(x, BX)
    if block == 1:
        main = own[0][own[1] + plane * BY : own[1] + plane * BY + BY]
        tile = own_tiles[0][own_tiles[1] + plane * 8 : own_tiles[1] + plane * 8 + 8]
        return jnp.concatenate([main, tile], 0)
    parts = []
    for (messages, base, wanted), count in zip(layout, (BY, 8)):
        first = side_rows(base, wanted, count, block).get(plane)
        if first is None:
            parts.append(jnp.zeros((count, BZ), F32))
        else:
            parts.append(from_side(messages, first, count, block, side))
    return jnp.concatenate(parts, 0)


def less_plane_below(value, x, own_ref, own_rows, messages, side_rows_of, side):
    if x == BX:
        planes_end, _, tiles_end = side_rows_of
        main = from_side(messages, planes_end, BY, 0, side)
        tile = from_side(messages, tiles_end - 8, 8, 0, side)
    elif x == 2 * BX:
        planes_end, _, tiles_end = own_rows
        high = side[1]
        main = own_ref[planes_end : planes_end + BY] * high
        tile = own_ref[tiles_end - 8 : tiles_end] * high
    else:
        return value
    return value - jnp.concatenate([main, tile], 0)


def strip_below(own, messages, first, slot, side):
    lane = lanes(own.shape)
    width = BX * STRIP
    low = from_side(messages, first, EY, 0, side)
    low = pltpu.roll(low, (width - slot * width) % BZ, 1)
    own = pltpu.roll(own * side[1], (2 * width - slot * width) % BZ, 1)
    in_own = (lane >= width) & (lane < width + STRIP)
    in_high = (lane >= 2 * width) & (lane < 2 * width + STRIP)
    return jnp.where(in_own, low, jnp.where(in_high, own, 0.0))


def whole_strip(own, messages, first, slot, side):
    low = from_side(messages, first, EY, 0, side)
    high = from_side(messages, first, EY, 2, side)
    return strip_of(low, 0, slot) + strip_of(own, 1, slot) + strip_of(high, 2, slot)


def adjoint_kernel(
    ql_ref, late_ref, even, odd, adj_hbm, ra_ref, rsa_ref, rb_ref, rsb_ref,
    table_ref,
    out_ref, hist_ref, coef_ref, coef_strip_ref,
    q_ref, t_ref, u_ref, scale_ref, edge_ref, flux_ref, w_sem,
):
    w_copy = pltpu.make_async_copy(adj_hbm.at[pl.ds(1, 3)], out_ref.at[pl.ds(1, 3)], w_sem)
    w_copy.start()
    cut_up, cut_down = cut_flags()
    side = sides()
    messages = (even, odd)
    r_refs = ((ra_ref, 0), (ra_ref, 1), (rb_ref, 0), (rb_ref, 1))
    rs_refs = ((rsa_ref, 0), (rsa_ref, 1), (rsb_ref, 0), (rsb_ref, 1))
    tiles, own_tiles, raws = ADJ_SIDE[1], ADJ_OWN[1], ADJ_SIDE[2] + EY

    def initial(index, x):
        own = ((ql_ref, 0), (late_ref, 0), (ql_ref, PLANES))[index]
        layout = (
            ((messages, raws, 4), (messages, tiles, 3)),
            ((messages, 0, 3), (messages, tiles + 24, 2)),
            ((messages, raws + PLANES, 4), (messages, tiles + 40, 3)),
        )[index]
        value = widened(own, (late_ref, own_tiles + 32 * index), x, layout, side)
        if index == 1:
            value = less_plane_below(value, x, late_ref, ADJ_OWN, messages, ADJ_SIDE, side)
        return value

    for x in range(EX):
        stiff, buoy, damp = coefficients(initial(2, x), table_ref)
        coef_ref[0, x], coef_ref[1, x], coef_ref[2, x] = stiff, buoy, damp
        scale_ref[x] = stiff * damp
    own_strip = late_ref[ADJ_OWN[2] : ADJ_OWN[2] + EY]
    q_s, t_s, label_s = (
        whole_strip(own_strip, messages, ADJ_SIDE[2], slot, side) for slot in range(3)
    )
    t_s = t_s - strip_below(own_strip, messages, ADJ_SIDE[2], 3, side)
    stiff_s, buoy_s, damp_s = coefficients(label_s, table_ref)
    scale_s = stiff_s * damp_s
    coef_strip_ref[0], coef_strip_ref[1], coef_strip_ref[2] = stiff_s, buoy_s, damp_s
    w_copy.wait()

    for step in range(1, STEPS + 1):
        rs_ref, place = rs_refs[STEPS - step]
        q_s = q_s + rs_ref[place]
        u_s = scale_s * q_s
        flux_s, spread = strip_flux(u_s, buoy_s)
        t_s = t_s + spread
        q_s = damp_s * q_s + t_s
        edges = cut_edges(u_s, flux_s, cut_up, cut_down)
        for x in range(step, EX - step):
            edge_ref[step - 1, x] = plane_edge(edges, x)

    for step in range(1, STEPS + 1):
        k = STEPS - step
        r_ref, place = r_refs[k]
        r_first = (EARLY_PLANES if k < 2 else LATE_PLANES)[0]

        for x in range(step - 1, EX - step + 1):
            q = (initial(0, x) if step == 1 else q_ref[x]) + r_ref[place, x - r_first]
            q_ref[x] = q
            u_ref[x] = scale_ref[x] * q

        for x in range(step - 1, EX - step):
            u, buoyancy = u_ref[x], coef_ref[1, x]
            slopes = [u_ref[x + 1] - u]
            if x >= step:
                slopes += [y_up(u) - u, z_up(u, edge_ref[step - 1, x]) - u]
            for axis, slope in enumerate(slopes):
                flux_ref[axis, x] = buoyancy * slope
            if BX <= x < 2 * BX:
                for axis, slope in enumerate(slopes):
                    w = out_ref[1 + axis, x - BX] + slope[0:BY]
                    out_ref[1 + axis, x - BX] = w
                    hist_ref[k, 1 + axis, x - BX] = w

        for x in range(step, EX - step):
            flux_y, flux_z = flux_ref[1, x], flux_ref[2, x]
            spread = (flux_ref[0, x] - flux_ref[0, x - 1]) + (flux_y - y_down(flux_y))
            spread = spread + (flux_z - z_down(flux_z, edge_ref[step - 1, x]))
            damped = coef_ref[2, x] * q_ref[x]
            t = (initial(1, x) if step == 1 else t_ref[x]) + spread
            if BX <= x < 2 * BX:
                hist_ref[k, 0, x - BX] = damped[0:BY]
            if step < STEPS:
                t_ref[x] = t
                q_ref[x] = damped + t
            else:
                out_ref[0, x - BX] = (damped + t)[0:BY]


def forward_kernel(
    wave_ref, own_s_ref, late_ref, even, odd, coef_ref, coef_strip_ref, s_ref, ss_ref, hist_ref,
    adjoint_ref, grad_hbm, adjoint_hbm,
    p_ref, spread_ref, edge_ref, flux_ref, grad_ref, sems,
):
    copies = [pltpu.make_async_copy(adjoint_ref, adjoint_hbm, sems.at[0])]
    copies[0].start()

    def send(index, kind, first, count):
        planes = pl.ds(first, count)
        copy = pltpu.make_async_copy(
            grad_ref.at[kind, planes], grad_hbm.at[kind, planes], sems.at[index]
        )
        copy.start()
        copies.append(copy)

    cut_up, cut_down = cut_flags()
    side = sides()
    messages = (even, odd)
    tiles, own_tiles = WAVE_SIDE[1], WAVE_OWN[1]

    def initial(index, x):
        layout = (
            ((messages, 0, 4), (messages, tiles, 3)),
            ((messages, PLANES, 3), (messages, tiles + 24, 2)),
        )[index]
        own = ((wave_ref, 0), (own_s_ref, 0))[index]
        value = widened(own, (late_ref, own_tiles + 32 * index), x, layout, side)
        if index == 1:
            value = less_plane_below(value, x, late_ref, WAVE_OWN, messages, WAVE_SIDE, side)
        return value

    own_strip = late_ref[WAVE_OWN[2] : WAVE_OWN[2] + EY]
    p_s, s_s = (
        whole_strip(own_strip, messages, WAVE_SIDE[2], slot, side) for slot in range(2)
    )
    s_s = s_s - strip_below(own_strip, messages, WAVE_SIDE[2], 2, side)
    stiff_s, buoy_s, damp_s = coef_strip_ref[0], coef_strip_ref[1], coef_strip_ref[2]

    for step in range(1, STEPS + 1):
        flux_s, spread = strip_flux(p_s, buoy_s)
        edges = cut_edges(p_s, flux_s, cut_up, cut_down)
        if step < STEPS:
            s_s = s_s - spread
            p_s = damp_s * (p_s - stiff_s * s_s) + ss_ref[step - 1]
        for x in range(step, EX - step):
            edge_ref[step - 1, x] = plane_edge(edges, x)
    for x in range(EX):
        p_ref[x] = initial(0, x)

    for step in range(1, STEPS + 1):
        k = step - 1
        for x in range(step - 1, EX - step):
            p, buoyancy = p_ref[x], coef_ref[1, x]
            slopes = [p_ref[x + 1] - p]
            if x >= step:
                slopes += [y_up(p) - p, z_up(p, edge_ref[step - 1, x]) - p]
            for axis, slope in enumerate(slopes):
                flux_ref[axis, x] = buoyancy * slope
            if BX <= x < 2 * BX:
                place = x - BX
                term = hist_ref[k, 1, place] * slopes[0][0:BY]
                term = term + hist_ref[k, 2, place] * slopes[1][0:BY]
                term = term + hist_ref[k, 3, place] * slopes[2][0:BY]
                grad_ref[1, place] = -term if k == 0 else grad_ref[1, place] - term
        if step == STEPS:
            send(1, 1, 0, BX)

        for x in range(step, EX - step):
            flux_y, flux_z = flux_ref[1, x], flux_ref[2, x]
            spread = (flux_ref[0, x] - flux_ref[0, x - 1]) + (flux_y - y_down(flux_y))
            spread = spread + (flux_z - z_down(flux_z, edge_ref[step - 1, x]))
            spread = (initial(1, x) if step == 1 else spread_ref[x]) - spread
            if step < STEPS:
                spread_ref[x] = spread
                p_ref[x] = (
                    coef_ref[2, x] * (p_ref[x] - coef_ref[0, x] * spread)
                    + s_ref[k, x - SOURCE_PLANES[0]]
                )
            if BX <= x < 2 * BX:
                place = x - BX
                term = hist_ref[k, 0, place] * spread[0:BY]
                grad_ref[0, place] = -term if k == 0 else grad_ref[0, place] - term
                if step == STEPS:
                    send(2 + place, 0, place, 1)
    for copy in copies:
        copy.wait()


def shape(*dims):
    return jax.ShapeDtypeStruct(dims, F32)


def call(kernel, outs, operands, scratch, places, micros=0.1, out_place="v"):
    spaces = {"h": pltpu.HBM, "a": pl.ANY, "v": pltpu.VMEM}
    operands = [
        pltpu.with_memory_space_constraint(operand, pltpu.HBM) if place == "h" else operand
        for operand, place in zip(operands, places)
    ]
    return pl.pallas_call(
        kernel,
        out_shape=outs,
        in_specs=[pl.BlockSpec(memory_space=spaces[place]) for place in places],
        out_specs=[pl.BlockSpec(memory_space=spaces[out_place])] * len(outs),
        scratch_shapes=scratch,
        compiler_params=pltpu.CompilerParams(vmem_limit_bytes=VMEM_LIMIT),
        cost_estimate=pl.CostEstimate(
            flops=0, bytes_accessed=int(3.69e6 * micros), transcendentals=0
        ),
    )(*operands)


def from_sides(sends, axes):
    count = lax.axis_size("gy")

    def route(offset):
        pairs = []
        for target in range(count):
            source = target + offset
            if 0 <= source < count:
                if "gz" in axes:
                    pairs += [(2 * source + z, 2 * target + 1 - z) for z in range(2)]
                else:
                    pairs.append((source, target))
        return pairs

    if count == 2:
        both = lax.ppermute(sends[0], axes, route(1) + route(-1))
        return both, both
    upward, downward = sends
    return lax.ppermute(downward, axes, route(1)), lax.ppermute(upward, axes, route(-1))


def rotated(array, axis, offset):
    count = lax.axis_size(axis)
    return lax.ppermute(array, axis, [((i + offset) % count, i) for i in range(count)])


def paired(array, odd):
    count = lax.axis_size("gx")
    pairs = []
    for i in range(count):
        partner = ((i - 1) ^ 1) + 1 if odd else i ^ 1
        pairs.append((partner if 0 <= partner < count else i, i))
    return lax.ppermute(array, "gx", pairs)


def local(
    stored, adjoint_end, labels, tissue, source_cells, source_wave, receiver_cells, receiver_wave
):
    assert lax.axis_size("gz") == 2 and labels.shape == (BX, BY, BZ) and tissue.shape[1] == 8
    half = lax.axis_size("gx") // 2
    arguments = [
        stored, adjoint_end, labels, tissue,
        receiver_cells.T, receiver_wave, source_cells.T, source_wave,
    ]
    ways = 1 if lax.axis_size("gy") == 2 else 2
    wave, ql, t, last_x, last_y, strips, table, receivers, receiver_wave, sources, source_wave, *sends = call(
        load_kernel,
        [
            shape(2 * PLANES, BZ),
            shape(2 * PLANES, BZ),
            shape(PLANES, BZ),
            shape(2 * BY, BZ),
            shape(2 * BX * 8, BZ),
            shape(3 * BY, BZ),
            shape(24, BZ),
        ]
        + [jax.ShapeDtypeStruct(array.shape, array.dtype) for array in arguments[4:]]
        + [shape(20 * 8, BZ)] * ways
        + [shape(2 * 8, BZ)] * ways,
        arguments,
        [
            pltpu.VMEM(stored.shape, F32),
            pltpu.VMEM(adjoint_end.shape, F32),
            pltpu.VMEM(labels.shape, jnp.int32),
            pltpu.SMEM(tissue.shape, F32),
            pltpu.SemaphoreType.DMA,
        ],
        "hhhhhhhh",
        1.4,
    )
    from_up, from_down = from_sides(sends[:ways], "gy")
    other = rotated(strips, "gz", 1)
    corner_up, corner_down = from_sides(sends[ways:], ("gy", "gz"))
    wave = rotated(wave, "gx", half)
    rb, rsb = call(
        late_kernel,
        [shape(2, EX * EY, BZ), shape(2, EY, BZ)],
        [receivers, receiver_wave],
        [],
        "vv",
        1.2,
    )
    early_planes, source_planes = (last - first for first, last in (EARLY_PLANES, SOURCE_PLANES))
    late, adj_late = call(
        merge_kernel,
        [shape(WAVE_FIX + 24, BZ), shape(ADJ_OWN[2] + EY, BZ)],
        [from_up, from_down, corner_up, corner_down, strips, other, t, last_x, last_y, rsb],
        [],
        "vvvvvvvvva",
    )
    late = rotated(late, "gx", half)
    ra, rsa = call(
        early_kernel,
        [shape(2, early_planes * EY, BZ), shape(2, EY, BZ)],
        [receivers, receiver_wave, adj_late],
        [],
        "vva",
        1.0,
    )
    ra, rb = ra.reshape(2, early_planes, EY, BZ), rb.reshape(2, EX, EY, BZ)
    even, odd = call(
        adjoint_join_kernel,
        [shape(ADJ_SIDE[2] + EY + 2 * PLANES, BZ)] * 2,
        [ql, adj_late, wave],
        [],
        "vva",
    )
    even, odd = paired(even, False), paired(odd, True)
    src, src_strip = call(
        source_kernel,
        [shape(STEPS - 1, source_planes * EY, BZ), shape(STEPS - 1, EY, BZ)],
        [sources, source_wave, adj_late],
        [],
        "vva",
        0.5,
    )
    src = src.reshape(STEPS - 1, source_planes, EY, BZ)
    own_s, wave_even, wave_odd = call(
        join_kernel,
        [shape(PLANES, BZ)] + [shape(WAVE_SIDE[2] + EY, BZ)] * 2,
        [wave, late],
        [],
        "vv",
    )
    wave_even, wave_odd = paired(wave_even, False), paired(wave_odd, True)
    adjoint_out, hist, coef, coef_strip = call(
        adjoint_kernel,
        [
            shape(4, BX, BY, BZ),
            shape(STEPS, 4, BX, BY, BZ),
            shape(3, EX, EY, BZ),
            shape(3, EY, BZ),
        ],
        [ql, adj_late, even, odd, adjoint_end, ra, rsa, rb, rsb, table],
        [pltpu.VMEM((EX, EY, BZ), F32)] * 4
        + [
            pltpu.VMEM((STEPS, EX, EY, BZ), F32),
            pltpu.VMEM((3, EX, EY, BZ), F32),
            pltpu.SemaphoreType.DMA,
        ],
        "vvvvhvvvvv",
        3.9,
    )
    return call(
        forward_kernel,
        [shape(2, BX, BY, BZ), shape(4, BX, BY, BZ)],
        [
            wave, own_s, late, wave_even, wave_odd, coef, coef_strip, src, src_strip, hist,
            adjoint_out,
        ],
        [pltpu.VMEM((EX, EY, BZ), F32)] * 2
        + [
            pltpu.VMEM((STEPS, EX, EY, BZ), F32),
            pltpu.VMEM((3, EX, EY, BZ), F32),
            pltpu.VMEM((2, BX, BY, BZ), F32),
            pltpu.SemaphoreType.DMA((2 + BX,)),
        ],
        "vvvvvvvvvvv",
        2.5,
        "a",
    )


def solution(mesh):
    return jax.shard_map(
        local,
        mesh=mesh,
        in_specs=(
            P("shot", "gx", "gy", "gz"),
            P("shot", "gx", "gy", "gz"),
            P("gx", "gy", "gz"),
            P(),
            P("shot", None),
            P(None, "shot"),
            P(),
            P(None, "shot"),
        ),
        out_specs=(P("shot", "gx", "gy", "gz"), P("shot", "gx", "gy", "gz")),
        check_vma=False,
    )
```

```python
import jax
import jax.numpy as jnp
from jax import lax
from jax.experimental import pallas as pl
from jax.experimental.pallas import tpu as pltpu
from jax.sharding import PartitionSpec as P

STEPS = 4
MARGIN = 4
BX, BY, BZ = 4, 32, 128
EX, EY = BX + 2 * MARGIN, BY + 2 * MARGIN
STRIP = 2 * MARGIN
F32 = jnp.float32
BF16 = jnp.bfloat16
VMEM_LIMIT = 16 * 1024 * 1024
PLANES = BX * BY
WAVE_OWN = (0, BY, BY + 9 * 8)
WAVE_FIX = WAVE_OWN[2] + EY
FIX_LANE = 3 * BX * STRIP
ADJ_OWN = (PLANES, PLANES + BY, PLANES + BY + 13 * 8)
WAVE_SIDE = (PLANES + 3 * BY, PLANES + 4 * BY, PLANES + 4 * BY + 6 * 8)
ADJ_SIDE = (3 * BY, 4 * BY, 4 * BY + 9 * 8)


def lanes(shape):
    return lax.broadcasted_iota(jnp.int32, shape, len(shape) - 1)


def rows(shape):
    return lax.broadcasted_iota(jnp.int32, shape, len(shape) - 2)


def run(copies):
    for copy in copies:
        copy.start()
    for copy in copies:
        copy.wait()


def coefficients(labels, table_ref):
    result = [jnp.zeros(labels.shape, F32) for _ in range(3)]
    for index in range(8):
        picked = labels == float(index + 1)
        for kind in range(3):
            row = kind * 8 + index
            result[kind] = jnp.where(picked, table_ref[row : row + 1], result[kind])
    return result


def buoyancy_of(labels, table_ref):
    result = jnp.zeros(labels.shape, F32)
    for index in range(8):
        result = jnp.where(labels == float(index + 1), table_ref[8 + index : 9 + index], result)
    return result


def half_turn(tile):
    return pltpu.roll(tile, MARGIN, 0)


def load_kernel(
    stored_hbm, adj_hbm, lab_hbm, tissue_hbm, rc_hbm, rw_hbm, sc_hbm, sw_hbm,
    wave_ref, ql_ref, t_ref, last_x_ref, last_y_ref, strip_ref, table_ref,
    rc_ref, rw_ref, sc_ref, sw_ref, *rest,
):
    *sends, stored, adj, lab, tissue, sem = rest
    run([
        pltpu.make_async_copy(source, target, sem)
        for source, target in (
            (stored_hbm, stored), (adj_hbm, adj), (lab_hbm, lab), (tissue_hbm, tissue),
            (rc_hbm, rc_ref), (rw_hbm, rw_ref), (sc_hbm, sc_ref), (sw_hbm, sw_ref),
        )
    ])
    for index in range(tissue.shape[1]):
        speed = jnp.full((1, BZ), tissue[0, index], F32)
        density = jnp.full((1, BZ), tissue[1, index], F32)
        table_ref[index : index + 1] = density * speed
        table_ref[8 + index : 9 + index] = speed / density
        table_ref[16 + index : 17 + index] = 1.0 - jnp.full((1, BZ), tissue[2, index], F32)
    gy, gz = lax.axis_index("gy"), lax.axis_index("gz")
    lane = lanes((BY, BZ))
    row = rows((BY, BZ))
    tile_row = rows((8, BZ))
    strips = [jnp.zeros((BY, BZ), F32) for _ in range(3)]
    tiles = [None] * 39
    previous = [None, None]

    def edge_tile(block):
        return jnp.where(tile_row < MARGIN, block[0:8], block[BY - 8 : BY])

    for x in range(BX):
        labels = lab[x].astype(F32) + 1.0
        buoyancy = buoyancy_of(labels, table_ref)
        plane = slice(x * BY, x * BY + BY)
        fields = [stored[index, x] for index in range(4)] + [adj[0, x]]
        fields += [buoyancy * adj[index, x] for index in range(1, 4)] + [labels]
        wave_ref[plane] = fields[0]
        ql_ref[plane] = fields[4]
        ql_ref[PLANES + x * BY : PLANES + x * BY + BY] = labels
        for index, block in enumerate(fields):
            tiles[index * BX + x] = edge_tile(block)
            group, slot = divmod(index, 4)
            base = slot * BX * STRIP + x * STRIP
            rolled = pltpu.roll(block, base + MARGIN, 1)
            first = base + MARGIN * gz
            strips[group] = jnp.where(
                (lane >= first) & (lane < first + MARGIN), rolled, strips[group]
            )
        for kind, (target, base) in enumerate(((wave_ref, PLANES), (t_ref, 0))):
            vx, vy, vz = fields[4 * kind + 1 : 4 * kind + 4]
            spread = vx if x == 0 else vx - previous[kind]
            spread = spread + (vy - jnp.where(row == 0, 0.0, pltpu.roll(vy, 1, 0)))
            spread = spread + (vz - jnp.where(lane == 0, 0.0, pltpu.roll(vz, 1, 1)))
            target[base + x * BY : base + x * BY + BY] = spread
            previous[kind] = vx
            index = (kind * BX + x) * 8
            last_y_ref[index : index + 8] = vy[BY - 8 : BY]
    for kind in range(2):
        last_x_ref[kind * BY : kind * BY + BY] = previous[kind]
    for group in range(3):
        strip_ref[group * BY : group * BY + BY] = strips[group]
        tiles[9 * BX + group] = edge_tile(strips[group])

    def joined(first, second):
        second = first if second is None else second
        upward = jnp.where(tile_row < MARGIN, half_turn(first), second)
        downward = jnp.where(tile_row < MARGIN, first, half_turn(second))
        if len(sends) == 2:
            return (jnp.where(gy == 0, upward, downward),)
        return upward, downward

    tiles.append(None)
    half = len(sends) // 2
    for place in range(20):
        for target, tile in zip(sends[:half], joined(tiles[2 * place], tiles[2 * place + 1])):
            target[place * 8 : place * 8 + 8] = tile
    for place in range(2):
        first = tiles[9 * BX + 2 * place]
        for target, tile in zip(sends[half:], joined(first, tiles[9 * BX + 2 * place + 1])):
            target[place * 8 : place * 8 + 8] = tile


def copy_rows(target, base, source, first, count):
    target[base : base + count] = source[pl.ds(pl.multiple_of(first, 8), count)]
    return base + count


def pair_planes():
    parity = lax.rem(lax.axis_index("gx"), 2)
    return 1 - parity, parity


def merge_kernel(
    from_up, from_down, corner_up, corner_down, strip_ref, other_ref,
    t_ref, last_x_ref, last_y_ref, _,
    wave_ref, adj_ref,
):
    gy = lax.axis_index("gy")
    tile_row = rows((8, BZ))
    row, lane = rows((BY, BZ)), lanes((BY, BZ))
    take_up = (tile_row < MARGIN) & (gy < lax.axis_size("gy") - 1)
    take_down = (tile_row >= MARGIN) & (gy > 0)
    _, cut_down = cut_flags()

    def halo(up, down, index):
        place, second = divmod(index, 2)
        sl = slice(place * 8, place * 8 + 8)
        above = half_turn(up[sl]) if second else up[sl]
        below = down[sl] if second else half_turn(down[sl])
        return jnp.where(take_up, above, jnp.where(take_down, below, 0.0))

    wide = []
    for group in range(3):
        sl = slice(group * BY, group * BY + BY)
        tile = halo(from_up, from_down, 9 * BX + group) + halo(corner_up, corner_down, group)
        wide.append(jnp.concatenate([strip_ref[sl] + other_ref[sl], tile], 0))
    strip_lane = lanes((EY, BZ))

    def strip_field(index):
        group, slot = divmod(index, 4)
        moved = pltpu.roll(wide[group], (BZ - slot * BX * STRIP) % BZ, 1) if slot else wide[group]
        return jnp.where(strip_lane < BX * STRIP, moved, 0.0)

    last_lanes = (BX - 1) * STRIP
    fix_row = jnp.zeros((8, BZ), F32)
    fix_lane = jnp.zeros((BY, BZ), F32)
    for kind, target in enumerate((wave_ref, adj_ref)):
        first = 4 * kind
        planes_end, x_end, tiles_end = (WAVE_OWN, ADJ_OWN)[kind]
        vx, vy, vz = (strip_field(first + 1 + axis) for axis in range(3))
        spread = vx - jnp.where(strip_lane < STRIP, 0.0, pltpu.roll(vx, STRIP, 1))
        spread = (spread + (vy - y_down(vy))) + (vz - pltpu.roll(vz, 1, 1))
        strip = strip_field(first)
        strip = strip + pltpu.roll(jnp.where(strip_lane < BX * STRIP, spread, 0.0), BX * STRIP, 1)
        last_slot = 2
        if kind == 1:
            strip = strip + pltpu.roll(strip_field(8), 2 * BX * STRIP, 1)
            last_slot = 3
        last = jnp.where(strip_lane >= last_lanes, vx, 0.0)
        strip = strip + pltpu.roll(last, last_slot * BX * STRIP - last_lanes, 1)
        target[planes_end:x_end] = last_x_ref[kind * BY : kind * BY + BY]

        vx_before = None
        for x in range(BX):
            vx_t, vy_t, vz_t = (
                halo(from_up, from_down, (first + 1 + axis) * BX + x) for axis in range(3)
            )
            below_z = pltpu.roll(vz, (BZ - (x * STRIP + MARGIN - 1)) % BZ, 1) * cut_down
            last_y = last_y_ref[(kind * BX + x) * 8 : (kind * BX + x) * 8 + 8]
            y_before = jnp.where(
                tile_row == 0, pltpu.roll(last_y, 1, 0), pltpu.roll(vy_t, 1, 0)
            )
            z_before = jnp.where(lane[0:8] == 0, below_z[BY:EY], pltpu.roll(vz_t, 1, 1))
            spread = vx_t if x == 0 else vx_t - vx_before
            spread = (spread + (vy_t - y_before)) + (vz_t - z_before)
            vx_before = vx_t
            if kind == 0:
                fix_row = jnp.where(tile_row == x, vy_t[7:8], fix_row)
                moved = pltpu.roll(below_z[0:BY], FIX_LANE + x, 1)
                fix_lane = jnp.where(lane == FIX_LANE + x, moved, fix_lane)
            else:
                block = t_ref[x * BY : x * BY + BY]
                block = block - jnp.where(row == 0, vy_t[7:8], 0.0)
                block = block - jnp.where(lane == 0, below_z[0:BY], 0.0)
                target[x * BY : x * BY + BY] = block
            base = x_end + x * 8
            target[base : base + 8] = halo(from_up, from_down, first * BX + x)
            target[base + 32 : base + 40] = spread
            if kind == 1:
                target[base + 64 : base + 72] = halo(from_up, from_down, 8 * BX + x)
        target[tiles_end - 8 : tiles_end] = vx_before
        if kind == 0:
            target[tiles_end : tiles_end + BY] = strip[0:BY] + fix_lane
            target[tiles_end + BY : tiles_end + EY] = strip[BY:EY]
            target[WAVE_FIX : WAVE_FIX + 8] = fix_row
            target[WAVE_FIX + 8 : WAVE_FIX + 24] = jnp.zeros((16, BZ), F32)
        else:
            target[tiles_end : tiles_end + EY] = strip


def adjoint_join_kernel(ql_ref, adj_ref, even_ref, odd_ref):
    planes_end, x_end, tiles_end = ADJ_OWN
    for target, first in zip((even_ref, odd_ref), pair_planes()):
        base = copy_rows(target, 0, adj_ref, first * BY, 3 * BY)
        base = copy_rows(target, base, adj_ref, planes_end, BY)
        base = copy_rows(target, base, adj_ref, x_end + first * 8, 24)
        base = copy_rows(target, base, adj_ref, x_end + 32 + first * 16, 16)
        base = copy_rows(target, base, adj_ref, x_end + 64 + first * 8, 24)
        base = copy_rows(target, base, adj_ref, tiles_end - 8, 8 + EY)
        copy_rows(target, base, ql_ref, 0, 2 * PLANES)


def join_kernel(wave_ref, late_ref, s_ref, even_ref, odd_ref):
    planes_end, x_end, tiles_end = WAVE_OWN
    row, lane = rows((BY, BZ)), lanes((BY, BZ))
    fix_lane = late_ref[tiles_end : tiles_end + BY]
    for x in range(BX):
        block = wave_ref[PLANES + x * BY : PLANES + x * BY + BY]
        fix_row = late_ref[WAVE_FIX + x : WAVE_FIX + x + 1]
        block = block - jnp.where(row == 0, fix_row, 0.0)
        block = block - jnp.where(lane == 0, pltpu.roll(fix_lane, BZ - FIX_LANE - x, 1), 0.0)
        s_ref[x * BY : x * BY + BY] = block
    for target, first in zip((even_ref, odd_ref), pair_planes()):
        base = copy_rows(target, 0, wave_ref, 0, PLANES)
        base = copy_rows(target, base, s_ref, first * BY, 3 * BY)
        base = copy_rows(target, base, late_ref, planes_end, BY)
        base = copy_rows(target, base, late_ref, x_end + first * 8, 24)
        base = copy_rows(target, base, late_ref, x_end + 32 + first * 16, 16)
        copy_rows(target, base, late_ref, tiles_end - 8, 8 + EY)


def split(values):
    high = values.astype(BF16)
    rest = values - high.astype(F32)
    middle = rest.astype(BF16)
    low = (rest - middle.astype(F32)).astype(BF16)
    return high, middle, low


def places(cells, sl):
    gx, gy, gz = (lax.axis_index(name) for name in ("gx", "gy", "gz"))
    cut = BZ * lax.axis_size("gz") // 2 - MARGIN
    cell_x = cells[0:1, sl] - (gx * BX - MARGIN)
    cell_y = cells[1:2, sl] - gy * BY
    cell_z = cells[2:3, sl]
    in_x = (cell_x >= 0) & (cell_x < EX)
    in_y = (cell_y >= -MARGIN) & (cell_y < BY + MARGIN)
    row = jnp.where(cell_y < 0, cell_y + EY, cell_y)
    flat = jnp.where(in_x & in_y, cell_x * EY + row, -1)
    row = jnp.where(in_y, row, -1)
    zz = cell_z - cut
    in_strip = in_x & (zz >= 0) & (zz < STRIP)
    strip_lane = jnp.where(in_strip, cell_x * STRIP + zz, -1)
    return flat, cell_z - gz * BZ, row, strip_lane


def hits(count, index):
    return rows((count, index.shape[1])) == index


def product(left, right):
    return lax.dot_general(
        left, right, (((1,), (1,)), ((), ())), preferred_element_type=F32
    )


def inject_points(cells, wave_ref, width, waves, planes, out_ref, strip_out_ref):
    count, low, total_rows = len(waves), planes[0] * EY, (planes[1] - planes[0]) * EY
    for start in range(0, cells.shape[1], width):
        sl = slice(start, start + width)
        flat, z, row, strip_lane = places(cells, sl)
        here = hits(total_rows, flat - low).astype(F32).astype(BF16)
        at_strip = hits(BZ, strip_lane).astype(F32).astype(BF16)
        at_z, at_row = hits(BZ, z), hits(EY, row)
        total = strip_total = None
        parts = [split(wave_ref[wave : wave + 1, sl]) for wave in waves]
        for part in range(3):
            amounts = [parts[wave][part].astype(F32) for wave in range(count)]
            right = jnp.concatenate([jnp.where(at_z, a, 0.0) for a in amounts], 0).astype(BF16)
            left = jnp.concatenate([jnp.where(at_row, a, 0.0) for a in amounts], 0).astype(BF16)
            term, strip_term = product(here, right), product(left, at_strip)
            total = term if part == 0 else total + term
            strip_total = strip_term if part == 0 else strip_total + strip_term
        for wave in range(count):
            value = total[:, wave * BZ : wave * BZ + BZ]
            strip_value = strip_total[wave * EY : wave * EY + EY]
            if start > 0:
                value = value + out_ref[wave]
                strip_value = strip_value + strip_out_ref[wave]
            out_ref[wave] = value
            strip_out_ref[wave] = strip_value


LATE_PLANES, EARLY_PLANES, SOURCE_PLANES = (0, EX), (2, EX - 2), (1, EX - 1)


def late_kernel(receivers, receiver_wave, r_ref, rs_ref):
    inject_points(receivers, receiver_wave, 256, (2, 3), LATE_PLANES, r_ref, rs_ref)


def early_kernel(receivers, receiver_wave, _, r_ref, rs_ref):
    inject_points(receivers, receiver_wave, 256, (0, 1), EARLY_PLANES, r_ref, rs_ref)


def source_kernel(sources, source_wave, _, s_ref, ss_ref):
    width = sources.shape[1]
    inject_points(sources, source_wave, width, (0, 1, 2), SOURCE_PLANES, s_ref, ss_ref)


def strip_of(packed, block, slot):
    lane = lanes(packed.shape)
    width = BX * STRIP
    shift = (block * width - slot * width) % BZ
    moved = pltpu.roll(packed, shift, 1) if shift else packed
    return jnp.where((lane >= block * width) & (lane < (block + 1) * width), moved, 0.0)


def y_up(v):
    return pltpu.roll(v, EY - 1, 0)


def y_down(v):
    return pltpu.roll(v, 1, 0)


def z_up(v, edge):
    return jnp.where(lanes(v.shape) == BZ - 1, edge, pltpu.roll(v, BZ - 1, 1))


def z_down(v, edge):
    return jnp.where(lanes(v.shape) == 0, edge, pltpu.roll(v, 1, 1))


def cut_edges(values, flux_z, cut_up, cut_down):
    place = lax.rem(lanes(values.shape), STRIP)
    above = jnp.where(place == MARGIN, values * cut_up, 0.0)
    below = jnp.where(place == MARGIN - 1, flux_z * cut_down, 0.0)
    return pltpu.roll(above, BZ - 2, 1) + below


def plane_edge(edges, x):
    return pltpu.roll(edges, (BZ - (x * STRIP + MARGIN - 1)) % BZ, 1)


def strip_flux(values, buoyancy):
    flux_x = buoyancy * (pltpu.roll(values, BZ - STRIP, 1) - values)
    flux_y = buoyancy * (y_up(values) - values)
    flux_z = buoyancy * (pltpu.roll(values, BZ - 1, 1) - values)
    spread = (flux_x - pltpu.roll(flux_x, STRIP, 1)) + (flux_y - y_down(flux_y))
    return flux_z, spread + (flux_z - pltpu.roll(flux_z, 1, 1))


def cut_flags():
    gz, half = lax.axis_index("gz"), lax.axis_size("gz") // 2
    return jnp.where(gz == half - 1, 1.0, 0.0), jnp.where(gz == half, 1.0, 0.0)


def sides():
    gx = lax.axis_index("gx")
    low = jnp.where(gx > 0, 1.0, 0.0)
    high = jnp.where(gx < lax.axis_size("gx") - 1, 1.0, 0.0)
    return low, high, lax.rem(gx, 2) == 0


def from_side(messages, first, count, block, side):
    even, odd = (message[first : first + count] for message in messages)
    low, high, even_above = side
    if block == 0:
        return jnp.where(even_above, odd, even) * low
    return jnp.where(even_above, even, odd) * high


def side_rows(base, wanted, step, block):
    planes = range(BX - wanted, BX) if block == 0 else range(wanted)
    return {plane: base + place * step for place, plane in enumerate(planes)}


def widened(own, own_tiles, x, layout, side):
    block, plane = divmod(x, BX)
    if block == 1:
        main = own[0][own[1] + plane * BY : own[1] + plane * BY + BY]
        tile = own_tiles[0][own_tiles[1] + plane * 8 : own_tiles[1] + plane * 8 + 8]
        return jnp.concatenate([main, tile], 0)
    parts = []
    for (messages, base, wanted), count in zip(layout, (BY, 8)):
        first = side_rows(base, wanted, count, block).get(plane)
        if first is None:
            parts.append(jnp.zeros((count, BZ), F32))
        else:
            parts.append(from_side(messages, first, count, block, side))
    return jnp.concatenate(parts, 0)


def less_plane_below(value, x, own_ref, own_rows, messages, side_rows_of, side):
    if x == BX:
        planes_end, _, tiles_end = side_rows_of
        main = from_side(messages, planes_end, BY, 0, side)
        tile = from_side(messages, tiles_end - 8, 8, 0, side)
    elif x == 2 * BX:
        planes_end, _, tiles_end = own_rows
        high = side[1]
        main = own_ref[planes_end : planes_end + BY] * high
        tile = own_ref[tiles_end - 8 : tiles_end] * high
    else:
        return value
    return value - jnp.concatenate([main, tile], 0)


def strip_below(own, messages, first, slot, side):
    lane = lanes(own.shape)
    width = BX * STRIP
    low = from_side(messages, first, EY, 0, side)
    low = pltpu.roll(low, (width - slot * width) % BZ, 1)
    own = pltpu.roll(own * side[1], (2 * width - slot * width) % BZ, 1)
    in_own = (lane >= width) & (lane < width + STRIP)
    in_high = (lane >= 2 * width) & (lane < 2 * width + STRIP)
    return jnp.where(in_own, low, jnp.where(in_high, own, 0.0))


def whole_strip(own, messages, first, slot, side):
    low = from_side(messages, first, EY, 0, side)
    high = from_side(messages, first, EY, 2, side)
    return strip_of(low, 0, slot) + strip_of(own, 1, slot) + strip_of(high, 2, slot)


def adjoint_kernel(
    ql_ref, late_ref, even, odd, adj_hbm, ra_ref, rsa_ref, rb_ref, rsb_ref,
    table_ref,
    out_ref, hist_ref, coef_ref, coef_strip_ref,
    q_ref, t_ref, u_ref, scale_ref, edge_ref, flux_ref, w_sem,
):
    w_copy = pltpu.make_async_copy(adj_hbm.at[pl.ds(1, 3)], out_ref.at[pl.ds(1, 3)], w_sem)
    w_copy.start()
    cut_up, cut_down = cut_flags()
    side = sides()
    messages = (even, odd)
    r_refs = ((ra_ref, 0), (ra_ref, 1), (rb_ref, 0), (rb_ref, 1))
    rs_refs = ((rsa_ref, 0), (rsa_ref, 1), (rsb_ref, 0), (rsb_ref, 1))
    tiles, own_tiles, raws = ADJ_SIDE[1], ADJ_OWN[1], ADJ_SIDE[2] + EY

    def initial(index, x):
        own = ((ql_ref, 0), (late_ref, 0), (ql_ref, PLANES))[index]
        layout = (
            ((messages, raws, 4), (messages, tiles, 3)),
            ((messages, 0, 3), (messages, tiles + 24, 2)),
            ((messages, raws + PLANES, 4), (messages, tiles + 40, 3)),
        )[index]
        value = widened(own, (late_ref, own_tiles + 32 * index), x, layout, side)
        if index == 1:
            value = less_plane_below(value, x, late_ref, ADJ_OWN, messages, ADJ_SIDE, side)
        return value

    for x in range(EX):
        stiff, buoy, damp = coefficients(initial(2, x), table_ref)
        coef_ref[0, x], coef_ref[1, x], coef_ref[2, x] = stiff, buoy, damp
        scale_ref[x] = stiff * damp
    own_strip = late_ref[ADJ_OWN[2] : ADJ_OWN[2] + EY]
    q_s, t_s, label_s = (
        whole_strip(own_strip, messages, ADJ_SIDE[2], slot, side) for slot in range(3)
    )
    t_s = t_s - strip_below(own_strip, messages, ADJ_SIDE[2], 3, side)
    stiff_s, buoy_s, damp_s = coefficients(label_s, table_ref)
    scale_s = stiff_s * damp_s
    coef_strip_ref[0], coef_strip_ref[1], coef_strip_ref[2] = stiff_s, buoy_s, damp_s
    w_copy.wait()

    for step in range(1, STEPS + 1):
        rs_ref, place = rs_refs[STEPS - step]
        q_s = q_s + rs_ref[place]
        u_s = scale_s * q_s
        flux_s, spread = strip_flux(u_s, buoy_s)
        t_s = t_s + spread
        q_s = damp_s * q_s + t_s
        edges = cut_edges(u_s, flux_s, cut_up, cut_down)
        for x in range(step, EX - step):
            edge_ref[step - 1, x] = plane_edge(edges, x)

    for step in range(1, STEPS + 1):
        k = STEPS - step
        r_ref, place = r_refs[k]
        r_first = (EARLY_PLANES if k < 2 else LATE_PLANES)[0]

        for x in range(step - 1, EX - step + 1):
            q = (initial(0, x) if step == 1 else q_ref[x]) + r_ref[place, x - r_first]
            q_ref[x] = q
            u_ref[x] = scale_ref[x] * q

        for x in range(step - 1, EX - step):
            u, buoyancy = u_ref[x], coef_ref[1, x]
            slopes = [u_ref[x + 1] - u]
            if x >= step:
                slopes += [y_up(u) - u, z_up(u, edge_ref[step - 1, x]) - u]
            for axis, slope in enumerate(slopes):
                flux_ref[axis, x] = buoyancy * slope
            if BX <= x < 2 * BX:
                for axis, slope in enumerate(slopes):
                    w = out_ref[1 + axis, x - BX] + slope[0:BY]
                    out_ref[1 + axis, x - BX] = w
                    hist_ref[k, 1 + axis, x - BX] = w

        for x in range(step, EX - step):
            flux_y, flux_z = flux_ref[1, x], flux_ref[2, x]
            spread = (flux_ref[0, x] - flux_ref[0, x - 1]) + (flux_y - y_down(flux_y))
            spread = spread + (flux_z - z_down(flux_z, edge_ref[step - 1, x]))
            damped = coef_ref[2, x] * q_ref[x]
            t = (initial(1, x) if step == 1 else t_ref[x]) + spread
            if BX <= x < 2 * BX:
                hist_ref[k, 0, x - BX] = damped[0:BY]
            if step < STEPS:
                t_ref[x] = t
                q_ref[x] = damped + t
            else:
                out_ref[0, x - BX] = (damped + t)[0:BY]


def forward_kernel(
    wave_ref, own_s_ref, late_ref, even, odd, coef_ref, coef_strip_ref, s_ref, ss_ref, hist_ref,
    adjoint_ref, grad_hbm, adjoint_hbm,
    p_ref, spread_ref, edge_ref, flux_ref, grad_ref, sems,
):
    copies = [pltpu.make_async_copy(adjoint_ref, adjoint_hbm, sems.at[0])]
    copies[0].start()

    def send(index, kind, first, count):
        planes = pl.ds(first, count)
        copy = pltpu.make_async_copy(
            grad_ref.at[kind, planes], grad_hbm.at[kind, planes], sems.at[index]
        )
        copy.start()
        copies.append(copy)

    cut_up, cut_down = cut_flags()
    side = sides()
    messages = (even, odd)
    tiles, own_tiles = WAVE_SIDE[1], WAVE_OWN[1]

    def initial(index, x):
        layout = (
            ((messages, 0, 4), (messages, tiles, 3)),
            ((messages, PLANES, 3), (messages, tiles + 24, 2)),
        )[index]
        own = ((wave_ref, 0), (own_s_ref, 0))[index]
        value = widened(own, (late_ref, own_tiles + 32 * index), x, layout, side)
        if index == 1:
            value = less_plane_below(value, x, late_ref, WAVE_OWN, messages, WAVE_SIDE, side)
        return value

    own_strip = late_ref[WAVE_OWN[2] : WAVE_OWN[2] + EY]
    p_s, s_s = (
        whole_strip(own_strip, messages, WAVE_SIDE[2], slot, side) for slot in range(2)
    )
    s_s = s_s - strip_below(own_strip, messages, WAVE_SIDE[2], 2, side)
    stiff_s, buoy_s, damp_s = coef_strip_ref[0], coef_strip_ref[1], coef_strip_ref[2]

    for step in range(1, STEPS + 1):
        flux_s, spread = strip_flux(p_s, buoy_s)
        edges = cut_edges(p_s, flux_s, cut_up, cut_down)
        if step < STEPS:
            s_s = s_s - spread
            p_s = damp_s * (p_s - stiff_s * s_s) + ss_ref[step - 1]
        for x in range(step, EX - step):
            edge_ref[step - 1, x] = plane_edge(edges, x)
    for x in range(EX):
        p_ref[x] = initial(0, x)

    for step in range(1, STEPS + 1):
        k = step - 1
        for x in range(step - 1, EX - step):
            p, buoyancy = p_ref[x], coef_ref[1, x]
            slopes = [p_ref[x + 1] - p]
            if x >= step:
                slopes += [y_up(p) - p, z_up(p, edge_ref[step - 1, x]) - p]
            for axis, slope in enumerate(slopes):
                flux_ref[axis, x] = buoyancy * slope
            if BX <= x < 2 * BX:
                place = x - BX
                term = hist_ref[k, 1, place] * slopes[0][0:BY]
                term = term + hist_ref[k, 2, place] * slopes[1][0:BY]
                term = term + hist_ref[k, 3, place] * slopes[2][0:BY]
                grad_ref[1, place] = -term if k == 0 else grad_ref[1, place] - term
        if step == STEPS:
            send(1, 1, 0, BX)

        for x in range(step, EX - step):
            flux_y, flux_z = flux_ref[1, x], flux_ref[2, x]
            spread = (flux_ref[0, x] - flux_ref[0, x - 1]) + (flux_y - y_down(flux_y))
            spread = spread + (flux_z - z_down(flux_z, edge_ref[step - 1, x]))
            spread = (initial(1, x) if step == 1 else spread_ref[x]) - spread
            if step < STEPS:
                spread_ref[x] = spread
                p_ref[x] = (
                    coef_ref[2, x] * (p_ref[x] - coef_ref[0, x] * spread)
                    + s_ref[k, x - SOURCE_PLANES[0]]
                )
            if BX <= x < 2 * BX:
                place = x - BX
                term = hist_ref[k, 0, place] * spread[0:BY]
                grad_ref[0, place] = -term if k == 0 else grad_ref[0, place] - term
                if step == STEPS:
                    send(2 + place, 0, place, 1)
    for copy in copies:
        copy.wait()


def shape(*dims):
    return jax.ShapeDtypeStruct(dims, F32)


def call(kernel, outs, operands, scratch, places, micros=0.1, out_place="v"):
    spaces = {"h": pltpu.HBM, "a": pl.ANY, "v": pltpu.VMEM}
    operands = [
        pltpu.with_memory_space_constraint(operand, pltpu.HBM) if place == "h" else operand
        for operand, place in zip(operands, places)
    ]
    return pl.pallas_call(
        kernel,
        out_shape=outs,
        in_specs=[pl.BlockSpec(memory_space=spaces[place]) for place in places],
        out_specs=[pl.BlockSpec(memory_space=spaces[out_place])] * len(outs),
        scratch_shapes=scratch,
        compiler_params=pltpu.CompilerParams(vmem_limit_bytes=VMEM_LIMIT),
        cost_estimate=pl.CostEstimate(
            flops=0, bytes_accessed=int(3.69e6 * micros), transcendentals=0
        ),
    )(*operands)


def from_sides(sends, axes):
    count = lax.axis_size("gy")

    def route(offset):
        pairs = []
        for target in range(count):
            source = target + offset
            if 0 <= source < count:
                if "gz" in axes:
                    pairs += [(2 * source + z, 2 * target + 1 - z) for z in range(2)]
                else:
                    pairs.append((source, target))
        return pairs

    if count == 2:
        both = lax.ppermute(sends[0], axes, route(1) + route(-1))
        return both, both
    upward, downward = sends
    return lax.ppermute(downward, axes, route(1)), lax.ppermute(upward, axes, route(-1))


def rotated(array, axis, offset):
    count = lax.axis_size(axis)
    return lax.ppermute(array, axis, [((i + offset) % count, i) for i in range(count)])


def paired(array, odd):
    count = lax.axis_size("gx")
    pairs = []
    for i in range(count):
        partner = ((i - 1) ^ 1) + 1 if odd else i ^ 1
        pairs.append((partner if 0 <= partner < count else i, i))
    return lax.ppermute(array, "gx", pairs)


def local(
    stored, adjoint_end, labels, tissue, source_cells, source_wave, receiver_cells, receiver_wave
):
    assert lax.axis_size("gz") == 2 and labels.shape == (BX, BY, BZ) and tissue.shape[1] == 8
    half = lax.axis_size("gx") // 2
    arguments = [
        stored, adjoint_end, labels, tissue,
        receiver_cells.T, receiver_wave, source_cells.T, source_wave,
    ]
    ways = 1 if lax.axis_size("gy") == 2 else 2
    wave, ql, t, last_x, last_y, strips, table, receivers, receiver_wave, sources, source_wave, *sends = call(
        load_kernel,
        [
            shape(2 * PLANES, BZ),
            shape(2 * PLANES, BZ),
            shape(PLANES, BZ),
            shape(2 * BY, BZ),
            shape(2 * BX * 8, BZ),
            shape(3 * BY, BZ),
            shape(24, BZ),
        ]
        + [jax.ShapeDtypeStruct(array.shape, array.dtype) for array in arguments[4:]]
        + [shape(20 * 8, BZ)] * ways
        + [shape(2 * 8, BZ)] * ways,
        arguments,
        [
            pltpu.VMEM(stored.shape, F32),
            pltpu.VMEM(adjoint_end.shape, F32),
            pltpu.VMEM(labels.shape, jnp.int32),
            pltpu.SMEM(tissue.shape, F32),
            pltpu.SemaphoreType.DMA,
        ],
        "hhhhhhhh",
        1.4,
    )
    from_up, from_down = from_sides(sends[:ways], "gy")
    other = rotated(strips, "gz", 1)
    corner_up, corner_down = from_sides(sends[ways:], ("gy", "gz"))
    wave = rotated(wave, "gx", half)
    rb, rsb = call(
        late_kernel,
        [shape(2, EX * EY, BZ), shape(2, EY, BZ)],
        [receivers, receiver_wave],
        [],
        "vv",
        1.2,
    )
    early_planes, source_planes = (last - first for first, last in (EARLY_PLANES, SOURCE_PLANES))
    late, adj_late = call(
        merge_kernel,
        [shape(WAVE_FIX + 24, BZ), shape(ADJ_OWN[2] + EY, BZ)],
        [from_up, from_down, corner_up, corner_down, strips, other, t, last_x, last_y, rsb],
        [],
        "vvvvvvvvva",
    )
    late = rotated(late, "gx", half)
    ra, rsa = call(
        early_kernel,
        [shape(2, early_planes * EY, BZ), shape(2, EY, BZ)],
        [receivers, receiver_wave, adj_late],
        [],
        "vva",
        1.0,
    )
    ra, rb = ra.reshape(2, early_planes, EY, BZ), rb.reshape(2, EX, EY, BZ)
    even, odd = call(
        adjoint_join_kernel,
        [shape(ADJ_SIDE[2] + EY + 2 * PLANES, BZ)] * 2,
        [ql, adj_late],
        [],
        "vv",
    )
    even, odd = paired(even, False), paired(odd, True)
    src, src_strip = call(
        source_kernel,
        [shape(STEPS - 1, source_planes * EY, BZ), shape(STEPS - 1, EY, BZ)],
        [sources, source_wave, adj_late],
        [],
        "vva",
        0.5,
    )
    src = src.reshape(STEPS - 1, source_planes, EY, BZ)
    own_s, wave_even, wave_odd = call(
        join_kernel,
        [shape(PLANES, BZ)] + [shape(WAVE_SIDE[2] + EY, BZ)] * 2,
        [wave, late],
        [],
        "vv",
    )
    wave_even, wave_odd = paired(wave_even, False), paired(wave_odd, True)
    adjoint_out, hist, coef, coef_strip = call(
        adjoint_kernel,
        [
            shape(4, BX, BY, BZ),
            shape(STEPS, 4, BX, BY, BZ),
            shape(3, EX, EY, BZ),
            shape(3, EY, BZ),
        ],
        [ql, adj_late, even, odd, adjoint_end, ra, rsa, rb, rsb, table],
        [pltpu.VMEM((EX, EY, BZ), F32)] * 4
        + [
            pltpu.VMEM((STEPS, EX, EY, BZ), F32),
            pltpu.VMEM((3, EX, EY, BZ), F32),
            pltpu.SemaphoreType.DMA,
        ],
        "vvvvhvvvvv",
        3.9,
    )
    return call(
        forward_kernel,
        [shape(2, BX, BY, BZ), shape(4, BX, BY, BZ)],
        [
            wave, own_s, late, wave_even, wave_odd, coef, coef_strip, src, src_strip, hist,
            adjoint_out,
        ],
        [pltpu.VMEM((EX, EY, BZ), F32)] * 2
        + [
            pltpu.VMEM((STEPS, EX, EY, BZ), F32),
            pltpu.VMEM((3, EX, EY, BZ), F32),
            pltpu.VMEM((2, BX, BY, BZ), F32),
            pltpu.SemaphoreType.DMA((2 + BX,)),
        ],
        "vvvvvvvvvvv",
        2.5,
        "a",
    )


def solution(mesh):
    return jax.shard_map(
        local,
        mesh=mesh,
        in_specs=(
            P("shot", "gx", "gy", "gz"),
            P("shot", "gx", "gy", "gz"),
            P("gx", "gy", "gz"),
            P(),
            P("shot", None),
            P(None, "shot"),
            P(),
            P(None, "shot"),
        ),
        out_specs=(P("shot", "gx", "gy", "gz"), P("shot", "gx", "gy", "gz")),
        check_vma=False,
    )
```

```python
import jax
import jax.numpy as jnp
from jax import lax
from jax.experimental import pallas as pl
from jax.experimental.pallas import tpu as pltpu
from jax.sharding import PartitionSpec as P

STEPS = 4
MARGIN = 4
BX, BY, BZ = 4, 32, 128
EX, EY = BX + 2 * MARGIN, BY + 2 * MARGIN
STRIP = 2 * MARGIN
F32 = jnp.float32
BF16 = jnp.bfloat16
VMEM_LIMIT = 16 * 1024 * 1024
PLANES = BX * BY
WAVE_OWN = (0, BY, BY + 9 * 8)
WAVE_FIX = WAVE_OWN[2] + EY
FIX_LANE = 3 * BX * STRIP
ADJ_OWN = (PLANES, PLANES + BY, PLANES + BY + 13 * 8)
WAVE_SIDE = (PLANES + 3 * BY, PLANES + 4 * BY, PLANES + 4 * BY + 6 * 8)
ADJ_SIDE = (3 * BY, 4 * BY, 4 * BY + 9 * 8)


def lanes(shape):
    return lax.broadcasted_iota(jnp.int32, shape, len(shape) - 1)


def rows(shape):
    return lax.broadcasted_iota(jnp.int32, shape, len(shape) - 2)


def run(copies):
    for copy in copies:
        copy.start()
    for copy in copies:
        copy.wait()


def coefficients(labels, table_ref):
    result = [jnp.zeros(labels.shape, F32) for _ in range(3)]
    for index in range(8):
        picked = labels == float(index + 1)
        for kind in range(3):
            row = kind * 8 + index
            result[kind] = jnp.where(picked, table_ref[row : row + 1], result[kind])
    return result


def buoyancy_of(labels, table_ref):
    result = jnp.zeros(labels.shape, F32)
    for index in range(8):
        result = jnp.where(labels == float(index + 1), table_ref[8 + index : 9 + index], result)
    return result


def half_turn(tile):
    return pltpu.roll(tile, MARGIN, 0)


def load_kernel(
    stored_hbm, adj_hbm, lab_hbm, tissue_hbm, rc_hbm, rw_hbm, sc_hbm, sw_hbm,
    wave_ref, ql_ref, t_ref, last_x_ref, last_y_ref, strip_ref, table_ref,
    rc_ref, rw_ref, sc_ref, sw_ref, *rest,
):
    *sends, stored, adj, lab, tissue, sem = rest
    run([
        pltpu.make_async_copy(source, target, sem)
        for source, target in (
            (stored_hbm, stored), (adj_hbm, adj), (lab_hbm, lab), (tissue_hbm, tissue),
            (rc_hbm, rc_ref), (rw_hbm, rw_ref), (sc_hbm, sc_ref), (sw_hbm, sw_ref),
        )
    ])
    for index in range(tissue.shape[1]):
        speed = jnp.full((1, BZ), tissue[0, index], F32)
        density = jnp.full((1, BZ), tissue[1, index], F32)
        table_ref[index : index + 1] = density * speed
        table_ref[8 + index : 9 + index] = speed / density
        table_ref[16 + index : 17 + index] = 1.0 - jnp.full((1, BZ), tissue[2, index], F32)
    gy, gz = lax.axis_index("gy"), lax.axis_index("gz")
    lane = lanes((BY, BZ))
    row = rows((BY, BZ))
    tile_row = rows((8, BZ))
    strips = [jnp.zeros((BY, BZ), F32) for _ in range(3)]
    tiles = [None] * 39
    previous = [None, None]

    def edge_tile(block):
        return jnp.where(tile_row < MARGIN, block[0:8], block[BY - 8 : BY])

    for x in range(BX):
        labels = lab[x].astype(F32) + 1.0
        buoyancy = buoyancy_of(labels, table_ref)
        plane = slice(x * BY, x * BY + BY)
        fields = [stored[index, x] for index in range(4)] + [adj[0, x]]
        fields += [buoyancy * adj[index, x] for index in range(1, 4)] + [labels]
        wave_ref[plane] = fields[0]
        ql_ref[plane] = fields[4]
        ql_ref[PLANES + x * BY : PLANES + x * BY + BY] = labels
        for index, block in enumerate(fields):
            tiles[index * BX + x] = edge_tile(block)
            group, slot = divmod(index, 4)
            base = slot * BX * STRIP + x * STRIP
            rolled = pltpu.roll(block, base + MARGIN, 1)
            first = base + MARGIN * gz
            strips[group] = jnp.where(
                (lane >= first) & (lane < first + MARGIN), rolled, strips[group]
            )
        for kind, (target, base) in enumerate(((wave_ref, PLANES), (t_ref, 0))):
            vx, vy, vz = fields[4 * kind + 1 : 4 * kind + 4]
            spread = vx if x == 0 else vx - previous[kind]
            spread = spread + (vy - jnp.where(row == 0, 0.0, pltpu.roll(vy, 1, 0)))
            spread = spread + (vz - jnp.where(lane == 0, 0.0, pltpu.roll(vz, 1, 1)))
            target[base + x * BY : base + x * BY + BY] = spread
            previous[kind] = vx
            index = (kind * BX + x) * 8
            last_y_ref[index : index + 8] = vy[BY - 8 : BY]
    for kind in range(2):
        last_x_ref[kind * BY : kind * BY + BY] = previous[kind]
    for group in range(3):
        strip_ref[group * BY : group * BY + BY] = strips[group]
        tiles[9 * BX + group] = edge_tile(strips[group])

    def joined(first, second):
        second = first if second is None else second
        upward = jnp.where(tile_row < MARGIN, half_turn(first), second)
        downward = jnp.where(tile_row < MARGIN, first, half_turn(second))
        if len(sends) == 2:
            return (jnp.where(gy == 0, upward, downward),)
        return upward, downward

    tiles.append(None)
    half = len(sends) // 2
    for place in range(20):
        for target, tile in zip(sends[:half], joined(tiles[2 * place], tiles[2 * place + 1])):
            target[place * 8 : place * 8 + 8] = tile
    for place in range(2):
        first = tiles[9 * BX + 2 * place]
        for target, tile in zip(sends[half:], joined(first, tiles[9 * BX + 2 * place + 1])):
            target[place * 8 : place * 8 + 8] = tile


def copy_rows(target, base, source, first, count):
    target[base : base + count] = source[pl.ds(pl.multiple_of(first, 8), count)]
    return base + count


def pair_planes():
    parity = lax.rem(lax.axis_index("gx"), 2)
    return 1 - parity, parity


def merge_kernel(
    from_up, from_down, corner_up, corner_down, strip_ref, other_ref,
    t_ref, last_x_ref, last_y_ref, _,
    wave_ref, adj_ref,
):
    gy = lax.axis_index("gy")
    tile_row = rows((8, BZ))
    row, lane = rows((BY, BZ)), lanes((BY, BZ))
    take_up = (tile_row < MARGIN) & (gy < lax.axis_size("gy") - 1)
    take_down = (tile_row >= MARGIN) & (gy > 0)
    _, cut_down = cut_flags()

    def halo(up, down, index):
        place, second = divmod(index, 2)
        sl = slice(place * 8, place * 8 + 8)
        above = half_turn(up[sl]) if second else up[sl]
        below = down[sl] if second else half_turn(down[sl])
        return jnp.where(take_up, above, jnp.where(take_down, below, 0.0))

    wide = []
    for group in range(3):
        sl = slice(group * BY, group * BY + BY)
        tile = halo(from_up, from_down, 9 * BX + group) + halo(corner_up, corner_down, group)
        wide.append(jnp.concatenate([strip_ref[sl] + other_ref[sl], tile], 0))
    strip_lane = lanes((EY, BZ))

    def strip_field(index):
        group, slot = divmod(index, 4)
        moved = pltpu.roll(wide[group], (BZ - slot * BX * STRIP) % BZ, 1) if slot else wide[group]
        return jnp.where(strip_lane < BX * STRIP, moved, 0.0)

    last_lanes = (BX - 1) * STRIP
    fix_row = jnp.zeros((8, BZ), F32)
    fix_lane = jnp.zeros((BY, BZ), F32)
    for kind, target in enumerate((wave_ref, adj_ref)):
        first = 4 * kind
        planes_end, x_end, tiles_end = (WAVE_OWN, ADJ_OWN)[kind]
        vx, vy, vz = (strip_field(first + 1 + axis) for axis in range(3))
        spread = vx - jnp.where(strip_lane < STRIP, 0.0, pltpu.roll(vx, STRIP, 1))
        spread = (spread + (vy - y_down(vy))) + (vz - pltpu.roll(vz, 1, 1))
        strip = strip_field(first)
        strip = strip + pltpu.roll(jnp.where(strip_lane < BX * STRIP, spread, 0.0), BX * STRIP, 1)
        last_slot = 2
        if kind == 1:
            strip = strip + pltpu.roll(strip_field(8), 2 * BX * STRIP, 1)
            last_slot = 3
        last = jnp.where(strip_lane >= last_lanes, vx, 0.0)
        strip = strip + pltpu.roll(last, last_slot * BX * STRIP - last_lanes, 1)
        target[planes_end:x_end] = last_x_ref[kind * BY : kind * BY + BY]

        vx_before = None
        for x in range(BX):
            vx_t, vy_t, vz_t = (
                halo(from_up, from_down, (first + 1 + axis) * BX + x) for axis in range(3)
            )
            below_z = pltpu.roll(vz, (BZ - (x * STRIP + MARGIN - 1)) % BZ, 1) * cut_down
            last_y = last_y_ref[(kind * BX + x) * 8 : (kind * BX + x) * 8 + 8]
            y_before = jnp.where(
                tile_row == 0, pltpu.roll(last_y, 1, 0), pltpu.roll(vy_t, 1, 0)
            )
            z_before = jnp.where(lane[0:8] == 0, below_z[BY:EY], pltpu.roll(vz_t, 1, 1))
            spread = vx_t if x == 0 else vx_t - vx_before
            spread = (spread + (vy_t - y_before)) + (vz_t - z_before)
            vx_before = vx_t
            if kind == 0:
                fix_row = jnp.where(tile_row == x, vy_t[7:8], fix_row)
                moved = pltpu.roll(below_z[0:BY], FIX_LANE + x, 1)
                fix_lane = jnp.where(lane == FIX_LANE + x, moved, fix_lane)
            else:
                block = t_ref[x * BY : x * BY + BY]
                block = block - jnp.where(row == 0, vy_t[7:8], 0.0)
                block = block - jnp.where(lane == 0, below_z[0:BY], 0.0)
                target[x * BY : x * BY + BY] = block
            base = x_end + x * 8
            target[base : base + 8] = halo(from_up, from_down, first * BX + x)
            target[base + 32 : base + 40] = spread
            if kind == 1:
                target[base + 64 : base + 72] = halo(from_up, from_down, 8 * BX + x)
        target[tiles_end - 8 : tiles_end] = vx_before
        if kind == 0:
            target[tiles_end : tiles_end + BY] = strip[0:BY] + fix_lane
            target[tiles_end + BY : tiles_end + EY] = strip[BY:EY]
            target[WAVE_FIX : WAVE_FIX + 8] = fix_row
            target[WAVE_FIX + 8 : WAVE_FIX + 24] = jnp.zeros((16, BZ), F32)
        else:
            target[tiles_end : tiles_end + EY] = strip


def adjoint_join_kernel(ql_ref, adj_ref, _, even_ref, odd_ref):
    planes_end, x_end, tiles_end = ADJ_OWN
    for target, first in zip((even_ref, odd_ref), pair_planes()):
        base = copy_rows(target, 0, adj_ref, first * BY, 3 * BY)
        base = copy_rows(target, base, adj_ref, planes_end, BY)
        base = copy_rows(target, base, adj_ref, x_end + first * 8, 24)
        base = copy_rows(target, base, adj_ref, x_end + 32 + first * 16, 16)
        base = copy_rows(target, base, adj_ref, x_end + 64 + first * 8, 24)
        base = copy_rows(target, base, adj_ref, tiles_end - 8, 8 + EY)
        copy_rows(target, base, ql_ref, 0, 2 * PLANES)


def join_kernel(wave_ref, late_ref, s_ref, even_ref, odd_ref):
    planes_end, x_end, tiles_end = WAVE_OWN
    row, lane = rows((BY, BZ)), lanes((BY, BZ))
    fix_lane = late_ref[tiles_end : tiles_end + BY]
    for x in range(BX):
        block = wave_ref[PLANES + x * BY : PLANES + x * BY + BY]
        fix_row = late_ref[WAVE_FIX + x : WAVE_FIX + x + 1]
        block = block - jnp.where(row == 0, fix_row, 0.0)
        block = block - jnp.where(lane == 0, pltpu.roll(fix_lane, BZ - FIX_LANE - x, 1), 0.0)
        s_ref[x * BY : x * BY + BY] = block
    for target, first in zip((even_ref, odd_ref), pair_planes()):
        base = copy_rows(target, 0, wave_ref, 0, PLANES)
        base = copy_rows(target, base, s_ref, first * BY, 3 * BY)
        base = copy_rows(target, base, late_ref, planes_end, BY)
        base = copy_rows(target, base, late_ref, x_end + first * 8, 24)
        base = copy_rows(target, base, late_ref, x_end + 32 + first * 16, 16)
        copy_rows(target, base, late_ref, tiles_end - 8, 8 + EY)


def split(values):
    high = values.astype(BF16)
    rest = values - high.astype(F32)
    middle = rest.astype(BF16)
    low = (rest - middle.astype(F32)).astype(BF16)
    return high, middle, low


def places(cells, sl):
    gx, gy, gz = (lax.axis_index(name) for name in ("gx", "gy", "gz"))
    cut = BZ * lax.axis_size("gz") // 2 - MARGIN
    cell_x = cells[0:1, sl] - (gx * BX - MARGIN)
    cell_y = cells[1:2, sl] - gy * BY
    cell_z = cells[2:3, sl]
    in_x = (cell_x >= 0) & (cell_x < EX)
    in_y = (cell_y >= -MARGIN) & (cell_y < BY + MARGIN)
    row = jnp.where(cell_y < 0, cell_y + EY, cell_y)
    flat = jnp.where(in_x & in_y, cell_x * EY + row, -1)
    row = jnp.where(in_y, row, -1)
    zz = cell_z - cut
    in_strip = in_x & (zz >= 0) & (zz < STRIP)
    strip_lane = jnp.where(in_strip, cell_x * STRIP + zz, -1)
    return flat, cell_z - gz * BZ, row, strip_lane


def hits(count, index):
    return rows((count, index.shape[1])) == index


def product(left, right):
    return lax.dot_general(
        left, right, (((1,), (1,)), ((), ())), preferred_element_type=F32
    )


def inject_points(cells, wave_ref, width, waves, planes, out_ref, strip_out_ref):
    count, low, total_rows = len(waves), planes[0] * EY, (planes[1] - planes[0]) * EY
    for start in range(0, cells.shape[1], width):
        sl = slice(start, start + width)
        flat, z, row, strip_lane = places(cells, sl)
        here = hits(total_rows, flat - low).astype(F32).astype(BF16)
        at_strip = hits(BZ, strip_lane).astype(F32).astype(BF16)
        at_z, at_row = hits(BZ, z), hits(EY, row)
        total = strip_total = None
        parts = [split(wave_ref[wave : wave + 1, sl]) for wave in waves]
        for part in range(3):
            amounts = [parts[wave][part].astype(F32) for wave in range(count)]
            right = jnp.concatenate([jnp.where(at_z, a, 0.0) for a in amounts], 0).astype(BF16)
            left = jnp.concatenate([jnp.where(at_row, a, 0.0) for a in amounts], 0).astype(BF16)
            term, strip_term = product(here, right), product(left, at_strip)
            total = term if part == 0 else total + term
            strip_total = strip_term if part == 0 else strip_total + strip_term
        for wave in range(count):
            value = total[:, wave * BZ : wave * BZ + BZ]
            strip_value = strip_total[wave * EY : wave * EY + EY]
            if start > 0:
                value = value + out_ref[wave]
                strip_value = strip_value + strip_out_ref[wave]
            out_ref[wave] = value
            strip_out_ref[wave] = strip_value


LATE_PLANES, EARLY_PLANES, SOURCE_PLANES = (0, EX), (2, EX - 2), (1, EX - 1)


def late_kernel(receivers, receiver_wave, r_ref, rs_ref):
    inject_points(receivers, receiver_wave, 256, (2, 3), LATE_PLANES, r_ref, rs_ref)


def early_kernel(receivers, receiver_wave, _, r_ref, rs_ref):
    inject_points(receivers, receiver_wave, 256, (0, 1), EARLY_PLANES, r_ref, rs_ref)


def source_kernel(sources, source_wave, _, s_ref, ss_ref):
    width = sources.shape[1]
    inject_points(sources, source_wave, width, (0, 1, 2), SOURCE_PLANES, s_ref, ss_ref)


def strip_of(packed, block, slot):
    lane = lanes(packed.shape)
    width = BX * STRIP
    shift = (block * width - slot * width) % BZ
    moved = pltpu.roll(packed, shift, 1) if shift else packed
    return jnp.where((lane >= block * width) & (lane < (block + 1) * width), moved, 0.0)


def y_up(v):
    return pltpu.roll(v, EY - 1, 0)


def y_down(v):
    return pltpu.roll(v, 1, 0)


def z_up(v, edge):
    return jnp.where(lanes(v.shape) == BZ - 1, edge, pltpu.roll(v, BZ - 1, 1))


def z_down(v, edge):
    return jnp.where(lanes(v.shape) == 0, edge, pltpu.roll(v, 1, 1))


def cut_edges(values, flux_z, cut_up, cut_down):
    place = lax.rem(lanes(values.shape), STRIP)
    above = jnp.where(place == MARGIN, values * cut_up, 0.0)
    below = jnp.where(place == MARGIN - 1, flux_z * cut_down, 0.0)
    return pltpu.roll(above, BZ - 2, 1) + below


def plane_edge(edges, x):
    return pltpu.roll(edges, (BZ - (x * STRIP + MARGIN - 1)) % BZ, 1)


def strip_flux(values, buoyancy):
    flux_x = buoyancy * (pltpu.roll(values, BZ - STRIP, 1) - values)
    flux_y = buoyancy * (y_up(values) - values)
    flux_z = buoyancy * (pltpu.roll(values, BZ - 1, 1) - values)
    spread = (flux_x - pltpu.roll(flux_x, STRIP, 1)) + (flux_y - y_down(flux_y))
    return flux_z, spread + (flux_z - pltpu.roll(flux_z, 1, 1))


def cut_flags():
    gz, half = lax.axis_index("gz"), lax.axis_size("gz") // 2
    return jnp.where(gz == half - 1, 1.0, 0.0), jnp.where(gz == half, 1.0, 0.0)


def sides():
    gx = lax.axis_index("gx")
    low = jnp.where(gx > 0, 1.0, 0.0)
    high = jnp.where(gx < lax.axis_size("gx") - 1, 1.0, 0.0)
    return low, high, lax.rem(gx, 2) == 0


def from_side(messages, first, count, block, side):
    even, odd = (message[first : first + count] for message in messages)
    low, high, even_above = side
    if block == 0:
        return jnp.where(even_above, odd, even) * low
    return jnp.where(even_above, even, odd) * high


def side_rows(base, wanted, step, block):
    planes = range(BX - wanted, BX) if block == 0 else range(wanted)
    return {plane: base + place * step for place, plane in enumerate(planes)}


def widened(own, own_tiles, x, layout, side):
    block, plane = divmod(x, BX)
    if block == 1:
        main = own[0][own[1] + plane * BY : own[1] + plane * BY + BY]
        tile = own_tiles[0][own_tiles[1] + plane * 8 : own_tiles[1] + plane * 8 + 8]
        return jnp.concatenate([main, tile], 0)
    parts = []
    for (messages, base, wanted), count in zip(layout, (BY, 8)):
        first = side_rows(base, wanted, count, block).get(plane)
        if first is None:
            parts.append(jnp.zeros((count, BZ), F32))
        else:
            parts.append(from_side(messages, first, count, block, side))
    return jnp.concatenate(parts, 0)


def less_plane_below(value, x, own_ref, own_rows, messages, side_rows_of, side):
    if x == BX:
        planes_end, _, tiles_end = side_rows_of
        main = from_side(messages, planes_end, BY, 0, side)
        tile = from_side(messages, tiles_end - 8, 8, 0, side)
    elif x == 2 * BX:
        planes_end, _, tiles_end = own_rows
        high = side[1]
        main = own_ref[planes_end : planes_end + BY] * high
        tile = own_ref[tiles_end - 8 : tiles_end] * high
    else:
        return value
    return value - jnp.concatenate([main, tile], 0)


def strip_below(own, messages, first, slot, side):
    lane = lanes(own.shape)
    width = BX * STRIP
    low = from_side(messages, first, EY, 0, side)
    low = pltpu.roll(low, (width - slot * width) % BZ, 1)
    own = pltpu.roll(own * side[1], (2 * width - slot * width) % BZ, 1)
    in_own = (lane >= width) & (lane < width + STRIP)
    in_high = (lane >= 2 * width) & (lane < 2 * width + STRIP)
    return jnp.where(in_own, low, jnp.where(in_high, own, 0.0))


def whole_strip(own, messages, first, slot, side):
    low = from_side(messages, first, EY, 0, side)
    high = from_side(messages, first, EY, 2, side)
    return strip_of(low, 0, slot) + strip_of(own, 1, slot) + strip_of(high, 2, slot)


def adjoint_kernel(
    ql_ref, late_ref, even, odd, adj_hbm, ra_ref, rsa_ref, rb_ref, rsb_ref,
    table_ref,
    out_ref, hist_ref, coef_ref, coef_strip_ref,
    q_ref, t_ref, u_ref, scale_ref, edge_ref, w_sem,
):
    w_copy = pltpu.make_async_copy(adj_hbm.at[pl.ds(1, 3)], out_ref.at[pl.ds(1, 3)], w_sem)
    w_copy.start()
    cut_up, cut_down = cut_flags()
    side = sides()
    messages = (even, odd)
    r_refs = ((ra_ref, 0), (ra_ref, 1), (rb_ref, 0), (rb_ref, 1))
    rs_refs = ((rsa_ref, 0), (rsa_ref, 1), (rsb_ref, 0), (rsb_ref, 1))
    tiles, own_tiles, raws = ADJ_SIDE[1], ADJ_OWN[1], ADJ_SIDE[2] + EY

    def initial(index, x):
        own = ((ql_ref, 0), (late_ref, 0), (ql_ref, PLANES))[index]
        layout = (
            ((messages, raws, 4), (messages, tiles, 3)),
            ((messages, 0, 3), (messages, tiles + 24, 2)),
            ((messages, raws + PLANES, 4), (messages, tiles + 40, 3)),
        )[index]
        value = widened(own, (late_ref, own_tiles + 32 * index), x, layout, side)
        if index == 1:
            value = less_plane_below(value, x, late_ref, ADJ_OWN, messages, ADJ_SIDE, side)
        return value

    for x in range(EX):
        stiff, buoy, damp = coefficients(initial(2, x), table_ref)
        coef_ref[0, x], coef_ref[1, x], coef_ref[2, x] = stiff, buoy, damp
        scale_ref[x] = stiff * damp
    own_strip = late_ref[ADJ_OWN[2] : ADJ_OWN[2] + EY]
    q_s, t_s, label_s = (
        whole_strip(own_strip, messages, ADJ_SIDE[2], slot, side) for slot in range(3)
    )
    t_s = t_s - strip_below(own_strip, messages, ADJ_SIDE[2], 3, side)
    stiff_s, buoy_s, damp_s = coefficients(label_s, table_ref)
    scale_s = stiff_s * damp_s
    coef_strip_ref[0], coef_strip_ref[1], coef_strip_ref[2] = stiff_s, buoy_s, damp_s
    w_copy.wait()

    for step in range(1, STEPS + 1):
        rs_ref, place = rs_refs[STEPS - step]
        q_s = q_s + rs_ref[place]
        u_s = scale_s * q_s
        flux_s, spread = strip_flux(u_s, buoy_s)
        t_s = t_s + spread
        q_s = damp_s * q_s + t_s
        edges = cut_edges(u_s, flux_s, cut_up, cut_down)
        for x in range(step, EX - step):
            edge_ref[step - 1, x] = plane_edge(edges, x)

    for step in range(1, STEPS + 1):
        k = STEPS - step
        r_ref, place = r_refs[k]
        r_first = (EARLY_PLANES if k < 2 else LATE_PLANES)[0]

        for x in range(step - 1, EX - step + 1):
            q = (initial(0, x) if step == 1 else q_ref[x]) + r_ref[place, x - r_first]
            q_ref[x] = q
            u_ref[x] = scale_ref[x] * q

        def close(x, flux_below, fluxes):
            flux_x, flux_y, flux_z = fluxes
            spread = (flux_x - flux_below) + (flux_y - y_down(flux_y))
            spread = spread + (flux_z - z_down(flux_z, edge_ref[step - 1, x]))
            damped = coef_ref[2, x] * q_ref[x]
            t = (initial(1, x) if step == 1 else t_ref[x]) + spread
            if BX <= x < 2 * BX:
                hist_ref[k, 0, x - BX] = damped[0:BY]
            if step < STEPS:
                t_ref[x] = t
                q_ref[x] = damped + t
            else:
                out_ref[0, x - BX] = (damped + t)[0:BY]

        waiting = flux_below = None
        for x in range(step - 1, EX - step):
            u, buoyancy = u_ref[x], coef_ref[1, x]
            slopes = [u_ref[x + 1] - u]
            if x >= step:
                slopes += [y_up(u) - u, z_up(u, edge_ref[step - 1, x]) - u]
            fluxes = [buoyancy * slope for slope in slopes]
            if BX <= x < 2 * BX:
                for axis, slope in enumerate(slopes):
                    w = out_ref[1 + axis, x - BX] + slope[0:BY]
                    out_ref[1 + axis, x - BX] = w
                    hist_ref[k, 1 + axis, x - BX] = w
            if waiting is not None:
                close(*waiting)
            waiting = (x, flux_below, fluxes) if x >= step else None
            flux_below = fluxes[0]
        close(*waiting)


def forward_kernel(
    wave_ref, own_s_ref, late_ref, even, odd, coef_ref, coef_strip_ref, s_ref, ss_ref, hist_ref,
    adjoint_ref, grad_hbm, adjoint_hbm,
    p_ref, spread_ref, edge_ref, grad_ref, sems,
):
    copies = [pltpu.make_async_copy(adjoint_ref, adjoint_hbm, sems.at[0])]
    copies[0].start()

    cut_up, cut_down = cut_flags()
    side = sides()
    messages = (even, odd)
    tiles, own_tiles = WAVE_SIDE[1], WAVE_OWN[1]

    def initial(index, x):
        layout = (
            ((messages, 0, 4), (messages, tiles, 3)),
            ((messages, PLANES, 3), (messages, tiles + 24, 2)),
        )[index]
        own = ((wave_ref, 0), (own_s_ref, 0))[index]
        value = widened(own, (late_ref, own_tiles + 32 * index), x, layout, side)
        if index == 1:
            value = less_plane_below(value, x, late_ref, WAVE_OWN, messages, WAVE_SIDE, side)
        return value

    own_strip = late_ref[WAVE_OWN[2] : WAVE_OWN[2] + EY]
    p_s, s_s = (
        whole_strip(own_strip, messages, WAVE_SIDE[2], slot, side) for slot in range(2)
    )
    s_s = s_s - strip_below(own_strip, messages, WAVE_SIDE[2], 2, side)
    stiff_s, buoy_s, damp_s = coef_strip_ref[0], coef_strip_ref[1], coef_strip_ref[2]

    for step in range(1, STEPS + 1):
        flux_s, spread = strip_flux(p_s, buoy_s)
        edges = cut_edges(p_s, flux_s, cut_up, cut_down)
        if step < STEPS:
            s_s = s_s - spread
            p_s = damp_s * (p_s - stiff_s * s_s) + ss_ref[step - 1]
        for x in range(step, EX - step):
            edge_ref[step - 1, x] = plane_edge(edges, x)
    for x in range(EX):
        p_ref[x] = initial(0, x)

    for step in range(1, STEPS + 1):
        k = step - 1
        def close(x, flux_below, fluxes):
            flux_x, flux_y, flux_z = fluxes
            spread = (flux_x - flux_below) + (flux_y - y_down(flux_y))
            spread = spread + (flux_z - z_down(flux_z, edge_ref[step - 1, x]))
            spread = (initial(1, x) if step == 1 else spread_ref[x]) - spread
            if step < STEPS:
                spread_ref[x] = spread
                p_ref[x] = (
                    coef_ref[2, x] * (p_ref[x] - coef_ref[0, x] * spread)
                    + s_ref[k, x - SOURCE_PLANES[0]]
                )
            if BX <= x < 2 * BX:
                place = x - BX
                term = hist_ref[k, 0, place] * spread[0:BY]
                grad_ref[0, place] = -term if k == 0 else grad_ref[0, place] - term

        waiting = flux_below = None
        for x in range(step - 1, EX - step):
            p, buoyancy = p_ref[x], coef_ref[1, x]
            slopes = [p_ref[x + 1] - p]
            if x >= step:
                slopes += [y_up(p) - p, z_up(p, edge_ref[step - 1, x]) - p]
            fluxes = [buoyancy * slope for slope in slopes]
            if BX <= x < 2 * BX:
                place = x - BX
                term = hist_ref[k, 1, place] * slopes[0][0:BY]
                term = term + hist_ref[k, 2, place] * slopes[1][0:BY]
                term = term + hist_ref[k, 3, place] * slopes[2][0:BY]
                grad_ref[1, place] = -term if k == 0 else grad_ref[1, place] - term
            if waiting is not None:
                close(*waiting)
            waiting = (x, flux_below, fluxes) if x >= step else None
            flux_below = fluxes[0]
        close(*waiting)

    for kind in range(2):
        copy = pltpu.make_async_copy(grad_ref.at[kind], grad_hbm.at[kind], sems.at[1 + kind])
        copy.start()
        copies.append(copy)
    for copy in copies:
        copy.wait()


def shape(*dims):
    return jax.ShapeDtypeStruct(dims, F32)


def call(kernel, outs, operands, scratch, places, micros=0.1, out_place="v"):
    spaces = {"h": pltpu.HBM, "a": pl.ANY, "v": pltpu.VMEM}
    operands = [
        pltpu.with_memory_space_constraint(operand, pltpu.HBM) if place == "h" else operand
        for operand, place in zip(operands, places)
    ]
    return pl.pallas_call(
        kernel,
        out_shape=outs,
        in_specs=[pl.BlockSpec(memory_space=spaces[place]) for place in places],
        out_specs=[pl.BlockSpec(memory_space=spaces[out_place])] * len(outs),
        scratch_shapes=scratch,
        compiler_params=pltpu.CompilerParams(vmem_limit_bytes=VMEM_LIMIT),
        cost_estimate=pl.CostEstimate(
            flops=0, bytes_accessed=int(3.69e6 * micros), transcendentals=0
        ),
    )(*operands)


def from_sides(sends, axes):
    count = lax.axis_size("gy")

    def route(offset):
        pairs = []
        for target in range(count):
            source = target + offset
            if 0 <= source < count:
                if "gz" in axes:
                    pairs += [(2 * source + z, 2 * target + 1 - z) for z in range(2)]
                else:
                    pairs.append((source, target))
        return pairs

    if count == 2:
        both = lax.ppermute(sends[0], axes, route(1) + route(-1))
        return both, both
    upward, downward = sends
    return lax.ppermute(downward, axes, route(1)), lax.ppermute(upward, axes, route(-1))


def rotated(array, axis, offset):
    count = lax.axis_size(axis)
    return lax.ppermute(array, axis, [((i + offset) % count, i) for i in range(count)])


def paired(array, odd):
    count = lax.axis_size("gx")
    pairs = []
    for i in range(count):
        partner = ((i - 1) ^ 1) + 1 if odd else i ^ 1
        pairs.append((partner if 0 <= partner < count else i, i))
    return lax.ppermute(array, "gx", pairs)


def local(
    stored, adjoint_end, labels, tissue, source_cells, source_wave, receiver_cells, receiver_wave
):
    assert lax.axis_size("gz") == 2 and labels.shape == (BX, BY, BZ) and tissue.shape[1] == 8
    half = lax.axis_size("gx") // 2
    arguments = [
        stored, adjoint_end, labels, tissue,
        receiver_cells.T, receiver_wave, source_cells.T, source_wave,
    ]
    ways = 1 if lax.axis_size("gy") == 2 else 2
    wave, ql, t, last_x, last_y, strips, table, receivers, receiver_wave, sources, source_wave, *sends = call(
        load_kernel,
        [
            shape(2 * PLANES, BZ),
            shape(2 * PLANES, BZ),
            shape(PLANES, BZ),
            shape(2 * BY, BZ),
            shape(2 * BX * 8, BZ),
            shape(3 * BY, BZ),
            shape(24, BZ),
        ]
        + [jax.ShapeDtypeStruct(array.shape, array.dtype) for array in arguments[4:]]
        + [shape(20 * 8, BZ)] * ways
        + [shape(2 * 8, BZ)] * ways,
        arguments,
        [
            pltpu.VMEM(stored.shape, F32),
            pltpu.VMEM(adjoint_end.shape, F32),
            pltpu.VMEM(labels.shape, jnp.int32),
            pltpu.SMEM(tissue.shape, F32),
            pltpu.SemaphoreType.DMA,
        ],
        "hhhhhhhh",
        1.4,
    )
    from_up, from_down = from_sides(sends[:ways], "gy")
    other = rotated(strips, "gz", 1)
    corner_up, corner_down = from_sides(sends[ways:], ("gy", "gz"))
    wave = rotated(wave, "gx", half)
    rb, rsb = call(
        late_kernel,
        [shape(2, EX * EY, BZ), shape(2, EY, BZ)],
        [receivers, receiver_wave],
        [],
        "vv",
        1.2,
    )
    early_planes, source_planes = (last - first for first, last in (EARLY_PLANES, SOURCE_PLANES))
    late, adj_late = call(
        merge_kernel,
        [shape(WAVE_FIX + 24, BZ), shape(ADJ_OWN[2] + EY, BZ)],
        [from_up, from_down, corner_up, corner_down, strips, other, t, last_x, last_y, rsb],
        [],
        "vvvvvvvvva",
    )
    late = rotated(late, "gx", half)
    ra, rsa = call(
        early_kernel,
        [shape(2, early_planes * EY, BZ), shape(2, EY, BZ)],
        [receivers, receiver_wave, adj_late],
        [],
        "vva",
        1.0,
    )
    ra, rb = ra.reshape(2, early_planes, EY, BZ), rb.reshape(2, EX, EY, BZ)
    even, odd = call(
        adjoint_join_kernel,
        [shape(ADJ_SIDE[2] + EY + 2 * PLANES, BZ)] * 2,
        [ql, adj_late, wave],
        [],
        "vva",
    )
    even, odd = paired(even, False), paired(odd, True)
    src, src_strip = call(
        source_kernel,
        [shape(STEPS - 1, source_planes * EY, BZ), shape(STEPS - 1, EY, BZ)],
        [sources, source_wave, adj_late],
        [],
        "vva",
        0.5,
    )
    src = src.reshape(STEPS - 1, source_planes, EY, BZ)
    own_s, wave_even, wave_odd = call(
        join_kernel,
        [shape(PLANES, BZ)] + [shape(WAVE_SIDE[2] + EY, BZ)] * 2,
        [wave, late],
        [],
        "vv",
    )
    wave_even, wave_odd = paired(wave_even, False), paired(wave_odd, True)
    adjoint_out, hist, coef, coef_strip = call(
        adjoint_kernel,
        [
            shape(4, BX, BY, BZ),
            shape(STEPS, 4, BX, BY, BZ),
            shape(3, EX, EY, BZ),
            shape(3, EY, BZ),
        ],
        [ql, adj_late, even, odd, adjoint_end, ra, rsa, rb, rsb, table],
        [pltpu.VMEM((EX, EY, BZ), F32)] * 4
        + [
            pltpu.VMEM((STEPS, EX, EY, BZ), F32),
            pltpu.SemaphoreType.DMA,
        ],
        "vvvvhvvvvv",
        3.9,
    )
    return call(
        forward_kernel,
        [shape(2, BX, BY, BZ), shape(4, BX, BY, BZ)],
        [
            wave, own_s, late, wave_even, wave_odd, coef, coef_strip, src, src_strip, hist,
            adjoint_out,
        ],
        [pltpu.VMEM((EX, EY, BZ), F32)] * 2
        + [
            pltpu.VMEM((STEPS, EX, EY, BZ), F32),
            pltpu.VMEM((2, BX, BY, BZ), F32),
            pltpu.SemaphoreType.DMA((3,)),
        ],
        "vvvvvvvvvvv",
        2.5,
        "a",
    )


def solution(mesh):
    return jax.shard_map(
        local,
        mesh=mesh,
        in_specs=(
            P("shot", "gx", "gy", "gz"),
            P("shot", "gx", "gy", "gz"),
            P("gx", "gy", "gz"),
            P(),
            P("shot", None),
            P(None, "shot"),
            P(),
            P(None, "shot"),
        ),
        out_specs=(P("shot", "gx", "gy", "gz"), P("shot", "gx", "gy", "gz")),
        check_vma=False,
    )
```

```python
import jax
import jax.numpy as jnp
from jax import lax
from jax.experimental import pallas as pl
from jax.experimental.pallas import tpu as pltpu
from jax.sharding import PartitionSpec as P

STEPS = 4
MARGIN = 4
BX, BY, BZ = 4, 32, 128
EX, EY = BX + 2 * MARGIN, BY + 2 * MARGIN
STRIP = 2 * MARGIN
F32 = jnp.float32
BF16 = jnp.bfloat16
VMEM_LIMIT = 16 * 1024 * 1024
PLANES = BX * BY
WAVE_OWN = (0, BY, BY + 9 * 8)
WAVE_FIX = WAVE_OWN[2] + EY
FIX_LANE = 3 * BX * STRIP
ADJ_OWN = (PLANES, PLANES + BY, PLANES + BY + 13 * 8)
WAVE_SIDE = (PLANES + 3 * BY, PLANES + 4 * BY, PLANES + 4 * BY + 6 * 8)
ADJ_SIDE = (3 * BY, 4 * BY, 4 * BY + 9 * 8)


def lanes(shape):
    return lax.broadcasted_iota(jnp.int32, shape, len(shape) - 1)


def rows(shape):
    return lax.broadcasted_iota(jnp.int32, shape, len(shape) - 2)


def run(copies):
    for copy in copies:
        copy.start()
    for copy in copies:
        copy.wait()


def coefficients(labels, table_ref):
    result = [jnp.zeros(labels.shape, F32) for _ in range(3)]
    for index in range(8):
        picked = labels == float(index + 1)
        for kind in range(3):
            row = kind * 8 + index
            result[kind] = jnp.where(picked, table_ref[row : row + 1], result[kind])
    return result


def buoyancy_of(labels, table_ref):
    result = jnp.zeros(labels.shape, F32)
    for index in range(8):
        result = jnp.where(labels == float(index + 1), table_ref[8 + index : 9 + index], result)
    return result


def half_turn(tile):
    return pltpu.roll(tile, MARGIN, 0)


def load_kernel(
    stored_hbm, adj_hbm, lab_hbm, tissue_hbm, rc_hbm, rw_hbm, sc_hbm, sw_hbm,
    wave_ref, ql_ref, t_ref, last_x_ref, last_y_ref, strip_ref, table_ref,
    rc_ref, rw_ref, sc_ref, sw_ref, *rest,
):
    *sends, stored, adj, lab, tissue, sem = rest
    run([
        pltpu.make_async_copy(source, target, sem)
        for source, target in (
            (stored_hbm, stored), (adj_hbm, adj), (lab_hbm, lab), (tissue_hbm, tissue),
            (rc_hbm, rc_ref), (rw_hbm, rw_ref), (sc_hbm, sc_ref), (sw_hbm, sw_ref),
        )
    ])
    for index in range(tissue.shape[1]):
        speed = jnp.full((1, BZ), tissue[0, index], F32)
        density = jnp.full((1, BZ), tissue[1, index], F32)
        table_ref[index : index + 1] = density * speed
        table_ref[8 + index : 9 + index] = speed / density
        table_ref[16 + index : 17 + index] = 1.0 - jnp.full((1, BZ), tissue[2, index], F32)
    gy, gz = lax.axis_index("gy"), lax.axis_index("gz")
    lane = lanes((BY, BZ))
    row = rows((BY, BZ))
    tile_row = rows((8, BZ))
    strips = [jnp.zeros((BY, BZ), F32) for _ in range(3)]
    tiles = [None] * 39
    previous = [None, None]

    def edge_tile(block):
        return jnp.where(tile_row < MARGIN, block[0:8], block[BY - 8 : BY])

    for x in range(BX):
        labels = lab[x].astype(F32) + 1.0
        buoyancy = buoyancy_of(labels, table_ref)
        plane = slice(x * BY, x * BY + BY)
        fields = [stored[index, x] for index in range(4)] + [adj[0, x]]
        fields += [buoyancy * adj[index, x] for index in range(1, 4)] + [labels]
        wave_ref[plane] = fields[0]
        ql_ref[plane] = fields[4]
        ql_ref[PLANES + x * BY : PLANES + x * BY + BY] = labels
        for index, block in enumerate(fields):
            tiles[index * BX + x] = edge_tile(block)
            group, slot = divmod(index, 4)
            base = slot * BX * STRIP + x * STRIP
            rolled = pltpu.roll(block, base + MARGIN, 1)
            first = base + MARGIN * gz
            strips[group] = jnp.where(
                (lane >= first) & (lane < first + MARGIN), rolled, strips[group]
            )
        for kind, (target, base) in enumerate(((wave_ref, PLANES), (t_ref, 0))):
            vx, vy, vz = fields[4 * kind + 1 : 4 * kind + 4]
            spread = vx if x == 0 else vx - previous[kind]
            spread = spread + (vy - jnp.where(row == 0, 0.0, pltpu.roll(vy, 1, 0)))
            spread = spread + (vz - jnp.where(lane == 0, 0.0, pltpu.roll(vz, 1, 1)))
            target[base + x * BY : base + x * BY + BY] = spread
            previous[kind] = vx
            index = (kind * BX + x) * 8
            last_y_ref[index : index + 8] = vy[BY - 8 : BY]
    for kind in range(2):
        last_x_ref[kind * BY : kind * BY + BY] = previous[kind]
    for group in range(3):
        strip_ref[group * BY : group * BY + BY] = strips[group]
        tiles[9 * BX + group] = edge_tile(strips[group])

    def joined(first, second):
        second = first if second is None else second
        upward = jnp.where(tile_row < MARGIN, half_turn(first), second)
        downward = jnp.where(tile_row < MARGIN, first, half_turn(second))
        if len(sends) == 2:
            return (jnp.where(gy == 0, upward, downward),)
        return upward, downward

    tiles.append(None)
    half = len(sends) // 2
    for place in range(20):
        for target, tile in zip(sends[:half], joined(tiles[2 * place], tiles[2 * place + 1])):
            target[place * 8 : place * 8 + 8] = tile
    for place in range(2):
        first = tiles[9 * BX + 2 * place]
        for target, tile in zip(sends[half:], joined(first, tiles[9 * BX + 2 * place + 1])):
            target[place * 8 : place * 8 + 8] = tile


def copy_rows(target, base, source, first, count):
    target[base : base + count] = source[pl.ds(pl.multiple_of(first, 8), count)]
    return base + count


def pair_planes():
    parity = lax.rem(lax.axis_index("gx"), 2)
    return 1 - parity, parity


def merge_kernel(
    from_up, from_down, corner_up, corner_down, strip_ref, other_ref,
    t_ref, last_x_ref, last_y_ref, _,
    wave_ref, adj_ref,
):
    gy = lax.axis_index("gy")
    tile_row = rows((8, BZ))
    row, lane = rows((BY, BZ)), lanes((BY, BZ))
    take_up = (tile_row < MARGIN) & (gy < lax.axis_size("gy") - 1)
    take_down = (tile_row >= MARGIN) & (gy > 0)
    _, cut_down = cut_flags()

    def halo(up, down, index):
        place, second = divmod(index, 2)
        sl = slice(place * 8, place * 8 + 8)
        above = half_turn(up[sl]) if second else up[sl]
        below = down[sl] if second else half_turn(down[sl])
        return jnp.where(take_up, above, jnp.where(take_down, below, 0.0))

    wide = []
    for group in range(3):
        sl = slice(group * BY, group * BY + BY)
        tile = halo(from_up, from_down, 9 * BX + group) + halo(corner_up, corner_down, group)
        wide.append(jnp.concatenate([strip_ref[sl] + other_ref[sl], tile], 0))
    strip_lane = lanes((EY, BZ))

    def strip_field(index):
        group, slot = divmod(index, 4)
        moved = pltpu.roll(wide[group], (BZ - slot * BX * STRIP) % BZ, 1) if slot else wide[group]
        return jnp.where(strip_lane < BX * STRIP, moved, 0.0)

    last_lanes = (BX - 1) * STRIP
    fix_row = jnp.zeros((8, BZ), F32)
    fix_lane = jnp.zeros((BY, BZ), F32)
    for kind, target in enumerate((wave_ref, adj_ref)):
        first = 4 * kind
        planes_end, x_end, tiles_end = (WAVE_OWN, ADJ_OWN)[kind]
        vx, vy, vz = (strip_field(first + 1 + axis) for axis in range(3))
        spread = vx - jnp.where(strip_lane < STRIP, 0.0, pltpu.roll(vx, STRIP, 1))
        spread = (spread + (vy - y_down(vy))) + (vz - pltpu.roll(vz, 1, 1))
        strip = strip_field(first)
        strip = strip + pltpu.roll(jnp.where(strip_lane < BX * STRIP, spread, 0.0), BX * STRIP, 1)
        last_slot = 2
        if kind == 1:
            strip = strip + pltpu.roll(strip_field(8), 2 * BX * STRIP, 1)
            last_slot = 3
        last = jnp.where(strip_lane >= last_lanes, vx, 0.0)
        strip = strip + pltpu.roll(last, last_slot * BX * STRIP - last_lanes, 1)
        target[planes_end:x_end] = last_x_ref[kind * BY : kind * BY + BY]

        vx_before = None
        for x in range(BX):
            vx_t, vy_t, vz_t = (
                halo(from_up, from_down, (first + 1 + axis) * BX + x) for axis in range(3)
            )
            below_z = pltpu.roll(vz, (BZ - (x * STRIP + MARGIN - 1)) % BZ, 1) * cut_down
            last_y = last_y_ref[(kind * BX + x) * 8 : (kind * BX + x) * 8 + 8]
            y_before = jnp.where(
                tile_row == 0, pltpu.roll(last_y, 1, 0), pltpu.roll(vy_t, 1, 0)
            )
            z_before = jnp.where(lane[0:8] == 0, below_z[BY:EY], pltpu.roll(vz_t, 1, 1))
            spread = vx_t if x == 0 else vx_t - vx_before
            spread = (spread + (vy_t - y_before)) + (vz_t - z_before)
            vx_before = vx_t
            if kind == 0:
                fix_row = jnp.where(tile_row == x, vy_t[7:8], fix_row)
                moved = pltpu.roll(below_z[0:BY], FIX_LANE + x, 1)
                fix_lane = jnp.where(lane == FIX_LANE + x, moved, fix_lane)
            else:
                block = t_ref[x * BY : x * BY + BY]
                block = block - jnp.where(row == 0, vy_t[7:8], 0.0)
                block = block - jnp.where(lane == 0, below_z[0:BY], 0.0)
                target[x * BY : x * BY + BY] = block
            base = x_end + x * 8
            target[base : base + 8] = halo(from_up, from_down, first * BX + x)
            target[base + 32 : base + 40] = spread
            if kind == 1:
                target[base + 64 : base + 72] = halo(from_up, from_down, 8 * BX + x)
        target[tiles_end - 8 : tiles_end] = vx_before
        if kind == 0:
            target[tiles_end : tiles_end + BY] = strip[0:BY] + fix_lane
            target[tiles_end + BY : tiles_end + EY] = strip[BY:EY]
            target[WAVE_FIX : WAVE_FIX + 8] = fix_row
            target[WAVE_FIX + 8 : WAVE_FIX + 24] = jnp.zeros((16, BZ), F32)
        else:
            target[tiles_end : tiles_end + EY] = strip


def adjoint_join_kernel(ql_ref, adj_ref, _, even_ref, odd_ref):
    planes_end, x_end, tiles_end = ADJ_OWN
    for target, first in zip((even_ref, odd_ref), pair_planes()):
        base = copy_rows(target, 0, adj_ref, first * BY, 3 * BY)
        base = copy_rows(target, base, adj_ref, planes_end, BY)
        base = copy_rows(target, base, adj_ref, x_end + first * 8, 24)
        base = copy_rows(target, base, adj_ref, x_end + 32 + first * 16, 16)
        base = copy_rows(target, base, adj_ref, x_end + 64 + first * 8, 24)
        base = copy_rows(target, base, adj_ref, tiles_end - 8, 8 + EY)
        copy_rows(target, base, ql_ref, 0, 2 * PLANES)


def join_kernel(wave_ref, late_ref, s_ref, even_ref, odd_ref):
    planes_end, x_end, tiles_end = WAVE_OWN
    row, lane = rows((BY, BZ)), lanes((BY, BZ))
    fix_lane = late_ref[tiles_end : tiles_end + BY]
    for x in range(BX):
        block = wave_ref[PLANES + x * BY : PLANES + x * BY + BY]
        fix_row = late_ref[WAVE_FIX + x : WAVE_FIX + x + 1]
        block = block - jnp.where(row == 0, fix_row, 0.0)
        block = block - jnp.where(lane == 0, pltpu.roll(fix_lane, BZ - FIX_LANE - x, 1), 0.0)
        s_ref[x * BY : x * BY + BY] = block
    for target, first in zip((even_ref, odd_ref), pair_planes()):
        base = copy_rows(target, 0, wave_ref, 0, PLANES)
        base = copy_rows(target, base, s_ref, first * BY, 3 * BY)
        base = copy_rows(target, base, late_ref, planes_end, BY)
        base = copy_rows(target, base, late_ref, x_end + first * 8, 24)
        base = copy_rows(target, base, late_ref, x_end + 32 + first * 16, 16)
        copy_rows(target, base, late_ref, tiles_end - 8, 8 + EY)


def split(values):
    high = values.astype(BF16)
    rest = values - high.astype(F32)
    middle = rest.astype(BF16)
    low = (rest - middle.astype(F32)).astype(BF16)
    return high, middle, low


def places(cells, sl):
    gx, gy, gz = (lax.axis_index(name) for name in ("gx", "gy", "gz"))
    cut = BZ * lax.axis_size("gz") // 2 - MARGIN
    cell_x = cells[0:1, sl] - (gx * BX - MARGIN)
    cell_y = cells[1:2, sl] - gy * BY
    cell_z = cells[2:3, sl]
    in_x = (cell_x >= 0) & (cell_x < EX)
    in_y = (cell_y >= -MARGIN) & (cell_y < BY + MARGIN)
    row = jnp.where(cell_y < 0, cell_y + EY, cell_y)
    flat = jnp.where(in_x & in_y, cell_x * EY + row, -1)
    row = jnp.where(in_y, row, -1)
    zz = cell_z - cut
    in_strip = in_x & (zz >= 0) & (zz < STRIP)
    strip_lane = jnp.where(in_strip, cell_x * STRIP + zz, -1)
    return flat, cell_z - gz * BZ, row, strip_lane


def hits(count, index):
    return rows((count, index.shape[1])) == index


def product(left, right):
    return lax.dot_general(
        left, right, (((1,), (1,)), ((), ())), preferred_element_type=F32
    )


def inject_points(cells, wave_ref, width, waves, planes, out_ref, strip_out_ref):
    count, low, total_rows = len(waves), planes[0] * EY, (planes[1] - planes[0]) * EY
    for start in range(0, cells.shape[1], width):
        sl = slice(start, start + width)
        flat, z, row, strip_lane = places(cells, sl)
        here = hits(total_rows, flat - low).astype(F32).astype(BF16)
        at_strip = hits(BZ, strip_lane).astype(F32).astype(BF16)
        at_z, at_row = hits(BZ, z), hits(EY, row)
        total = strip_total = None
        parts = [split(wave_ref[wave : wave + 1, sl]) for wave in waves]
        for part in range(3):
            amounts = [parts[wave][part].astype(F32) for wave in range(count)]
            right = jnp.concatenate([jnp.where(at_z, a, 0.0) for a in amounts], 0).astype(BF16)
            left = jnp.concatenate([jnp.where(at_row, a, 0.0) for a in amounts], 0).astype(BF16)
            term, strip_term = product(here, right), product(left, at_strip)
            total = term if part == 0 else total + term
            strip_total = strip_term if part == 0 else strip_total + strip_term
        for wave in range(count):
            value = total[:, wave * BZ : wave * BZ + BZ]
            strip_value = strip_total[wave * EY : wave * EY + EY]
            if start > 0:
                value = value + out_ref[wave]
                strip_value = strip_value + strip_out_ref[wave]
            out_ref[wave] = value
            strip_out_ref[wave] = strip_value


LATE_PLANES, EARLY_PLANES, SOURCE_PLANES = (0, EX), (2, EX - 2), (1, EX - 1)


def late_kernel(receivers, receiver_wave, r_ref, rs_ref):
    inject_points(receivers, receiver_wave, 256, (2, 3), LATE_PLANES, r_ref, rs_ref)


def early_kernel(receivers, receiver_wave, _, r_ref, rs_ref):
    inject_points(receivers, receiver_wave, 256, (0, 1), EARLY_PLANES, r_ref, rs_ref)


def source_kernel(sources, source_wave, _, s_ref, ss_ref):
    width = sources.shape[1]
    inject_points(sources, source_wave, width, (0, 1, 2), SOURCE_PLANES, s_ref, ss_ref)


def strip_of(packed, block, slot):
    lane = lanes(packed.shape)
    width = BX * STRIP
    shift = (block * width - slot * width) % BZ
    moved = pltpu.roll(packed, shift, 1) if shift else packed
    return jnp.where((lane >= block * width) & (lane < (block + 1) * width), moved, 0.0)


def y_up(v):
    return pltpu.roll(v, EY - 1, 0)


def y_down(v):
    return pltpu.roll(v, 1, 0)


def put_with_next(ref, x, value):
    ref[x, 0:EY] = value
    ref[x, EY : EY + 1] = value[0:1]


def put_with_last(ref, x, value):
    ref[x, 8 : EY + 8] = value
    ref[x, 7:8] = value[EY - 1 : EY]


def z_up(v, edge):
    return jnp.where(lanes(v.shape) == BZ - 1, edge, pltpu.roll(v, BZ - 1, 1))


def z_down(v, edge):
    return jnp.where(lanes(v.shape) == 0, edge, pltpu.roll(v, 1, 1))


def cut_edges(values, flux_z, cut_up, cut_down):
    place = lax.rem(lanes(values.shape), STRIP)
    above = jnp.where(place == MARGIN, values * cut_up, 0.0)
    below = jnp.where(place == MARGIN - 1, flux_z * cut_down, 0.0)
    return pltpu.roll(above, BZ - 2, 1) + below


def plane_edge(edges, x):
    return pltpu.roll(edges, (BZ - (x * STRIP + MARGIN - 1)) % BZ, 1)


def strip_flux(values, buoyancy):
    flux_x = buoyancy * (pltpu.roll(values, BZ - STRIP, 1) - values)
    flux_y = buoyancy * (y_up(values) - values)
    flux_z = buoyancy * (pltpu.roll(values, BZ - 1, 1) - values)
    spread = (flux_x - pltpu.roll(flux_x, STRIP, 1)) + (flux_y - y_down(flux_y))
    return flux_z, spread + (flux_z - pltpu.roll(flux_z, 1, 1))


def cut_flags():
    gz, half = lax.axis_index("gz"), lax.axis_size("gz") // 2
    return jnp.where(gz == half - 1, 1.0, 0.0), jnp.where(gz == half, 1.0, 0.0)


def sides():
    gx = lax.axis_index("gx")
    low = jnp.where(gx > 0, 1.0, 0.0)
    high = jnp.where(gx < lax.axis_size("gx") - 1, 1.0, 0.0)
    return low, high, lax.rem(gx, 2) == 0


def from_side(messages, first, count, block, side):
    even, odd = (message[first : first + count] for message in messages)
    low, high, even_above = side
    if block == 0:
        return jnp.where(even_above, odd, even) * low
    return jnp.where(even_above, even, odd) * high


def side_rows(base, wanted, step, block):
    planes = range(BX - wanted, BX) if block == 0 else range(wanted)
    return {plane: base + place * step for place, plane in enumerate(planes)}


def widened(own, own_tiles, x, layout, side):
    block, plane = divmod(x, BX)
    if block == 1:
        main = own[0][own[1] + plane * BY : own[1] + plane * BY + BY]
        tile = own_tiles[0][own_tiles[1] + plane * 8 : own_tiles[1] + plane * 8 + 8]
        return jnp.concatenate([main, tile], 0)
    parts = []
    for (messages, base, wanted), count in zip(layout, (BY, 8)):
        first = side_rows(base, wanted, count, block).get(plane)
        if first is None:
            parts.append(jnp.zeros((count, BZ), F32))
        else:
            parts.append(from_side(messages, first, count, block, side))
    return jnp.concatenate(parts, 0)


def less_plane_below(value, x, own_ref, own_rows, messages, side_rows_of, side):
    if x == BX:
        planes_end, _, tiles_end = side_rows_of
        main = from_side(messages, planes_end, BY, 0, side)
        tile = from_side(messages, tiles_end - 8, 8, 0, side)
    elif x == 2 * BX:
        planes_end, _, tiles_end = own_rows
        high = side[1]
        main = own_ref[planes_end : planes_end + BY] * high
        tile = own_ref[tiles_end - 8 : tiles_end] * high
    else:
        return value
    return value - jnp.concatenate([main, tile], 0)


def strip_below(own, messages, first, slot, side):
    lane = lanes(own.shape)
    width = BX * STRIP
    low = from_side(messages, first, EY, 0, side)
    low = pltpu.roll(low, (width - slot * width) % BZ, 1)
    own = pltpu.roll(own * side[1], (2 * width - slot * width) % BZ, 1)
    in_own = (lane >= width) & (lane < width + STRIP)
    in_high = (lane >= 2 * width) & (lane < 2 * width + STRIP)
    return jnp.where(in_own, low, jnp.where(in_high, own, 0.0))


def whole_strip(own, messages, first, slot, side):
    low = from_side(messages, first, EY, 0, side)
    high = from_side(messages, first, EY, 2, side)
    return strip_of(low, 0, slot) + strip_of(own, 1, slot) + strip_of(high, 2, slot)


def adjoint_kernel(
    ql_ref, late_ref, even, odd, adj_hbm, ra_ref, rsa_ref, rb_ref, rsb_ref,
    table_ref,
    out_ref, hist_ref, coef_ref, coef_strip_ref,
    u_ref, flux_ref, q_ref, t_ref, scale_ref, edge_ref, w_sem,
):
    w_copy = pltpu.make_async_copy(adj_hbm.at[pl.ds(1, 3)], out_ref.at[pl.ds(1, 3)], w_sem)
    w_copy.start()
    cut_up, cut_down = cut_flags()
    side = sides()
    messages = (even, odd)
    r_refs = ((ra_ref, 0), (ra_ref, 1), (rb_ref, 0), (rb_ref, 1))
    rs_refs = ((rsa_ref, 0), (rsa_ref, 1), (rsb_ref, 0), (rsb_ref, 1))
    tiles, own_tiles, raws = ADJ_SIDE[1], ADJ_OWN[1], ADJ_SIDE[2] + EY

    def initial(index, x):
        own = ((ql_ref, 0), (late_ref, 0), (ql_ref, PLANES))[index]
        layout = (
            ((messages, raws, 4), (messages, tiles, 3)),
            ((messages, 0, 3), (messages, tiles + 24, 2)),
            ((messages, raws + PLANES, 4), (messages, tiles + 40, 3)),
        )[index]
        value = widened(own, (late_ref, own_tiles + 32 * index), x, layout, side)
        if index == 1:
            value = less_plane_below(value, x, late_ref, ADJ_OWN, messages, ADJ_SIDE, side)
        return value

    for x in range(EX):
        stiff, buoy, damp = coefficients(initial(2, x), table_ref)
        coef_ref[0, x], coef_ref[1, x], coef_ref[2, x] = stiff, buoy, damp
        scale_ref[x] = stiff * damp
    own_strip = late_ref[ADJ_OWN[2] : ADJ_OWN[2] + EY]
    q_s, t_s, label_s = (
        whole_strip(own_strip, messages, ADJ_SIDE[2], slot, side) for slot in range(3)
    )
    t_s = t_s - strip_below(own_strip, messages, ADJ_SIDE[2], 3, side)
    stiff_s, buoy_s, damp_s = coefficients(label_s, table_ref)
    scale_s = stiff_s * damp_s
    coef_strip_ref[0], coef_strip_ref[1], coef_strip_ref[2] = stiff_s, buoy_s, damp_s
    w_copy.wait()

    for step in range(1, STEPS + 1):
        rs_ref, place = rs_refs[STEPS - step]
        q_s = q_s + rs_ref[place]
        u_s = scale_s * q_s
        flux_s, spread = strip_flux(u_s, buoy_s)
        t_s = t_s + spread
        q_s = damp_s * q_s + t_s
        edges = cut_edges(u_s, flux_s, cut_up, cut_down)
        for x in range(step, EX - step):
            edge_ref[step - 1, x] = plane_edge(edges, x)

    for step in range(1, STEPS + 1):
        k = STEPS - step
        r_ref, place = r_refs[k]
        r_first = (EARLY_PLANES if k < 2 else LATE_PLANES)[0]

        for x in range(step - 1, EX - step + 1):
            q = (initial(0, x) if step == 1 else q_ref[x]) + r_ref[place, x - r_first]
            q_ref[x] = q
            put_with_next(u_ref, x, scale_ref[x] * q)

        def close(x, flux_below, fluxes):
            flux_x, flux_y, flux_z = fluxes
            spread = (flux_x - flux_below) + (flux_y - flux_ref[x, 7 : EY + 7])
            spread = spread + (flux_z - z_down(flux_z, edge_ref[step - 1, x]))
            damped = coef_ref[2, x] * q_ref[x]
            t = (initial(1, x) if step == 1 else t_ref[x]) + spread
            if BX <= x < 2 * BX:
                hist_ref[k, 0, x - BX] = damped[0:BY]
            if step < STEPS:
                t_ref[x] = t
                q_ref[x] = damped + t
            else:
                out_ref[0, x - BX] = (damped + t)[0:BY]

        waiting = flux_below = None
        for x in range(step - 1, EX - step):
            u, buoyancy = u_ref[x, 0:EY], coef_ref[1, x]
            slopes = [u_ref[x + 1, 0:EY] - u]
            if x >= step:
                slopes += [u_ref[x, 1 : EY + 1] - u, z_up(u, edge_ref[step - 1, x]) - u]
            fluxes = [buoyancy * slope for slope in slopes]
            if x >= step:
                put_with_last(flux_ref, x, fluxes[1])
            if BX <= x < 2 * BX:
                for axis, slope in enumerate(slopes):
                    w = out_ref[1 + axis, x - BX] + slope[0:BY]
                    out_ref[1 + axis, x - BX] = w
                    hist_ref[k, 1 + axis, x - BX] = w
            if waiting is not None:
                close(*waiting)
            waiting = (x, flux_below, fluxes) if x >= step else None
            flux_below = fluxes[0]
        close(*waiting)


def forward_kernel(
    wave_ref, own_s_ref, late_ref, even, odd, coef_ref, coef_strip_ref, s_ref, ss_ref, hist_ref,
    adjoint_ref, grad_hbm, adjoint_hbm,
    p_ref, flux_ref, spread_ref, edge_ref, grad_ref, sems,
):
    copies = [pltpu.make_async_copy(adjoint_ref, adjoint_hbm, sems.at[0])]
    copies[0].start()

    cut_up, cut_down = cut_flags()
    side = sides()
    messages = (even, odd)
    tiles, own_tiles = WAVE_SIDE[1], WAVE_OWN[1]

    def initial(index, x):
        layout = (
            ((messages, 0, 4), (messages, tiles, 3)),
            ((messages, PLANES, 3), (messages, tiles + 24, 2)),
        )[index]
        own = ((wave_ref, 0), (own_s_ref, 0))[index]
        value = widened(own, (late_ref, own_tiles + 32 * index), x, layout, side)
        if index == 1:
            value = less_plane_below(value, x, late_ref, WAVE_OWN, messages, WAVE_SIDE, side)
        return value

    own_strip = late_ref[WAVE_OWN[2] : WAVE_OWN[2] + EY]
    p_s, s_s = (
        whole_strip(own_strip, messages, WAVE_SIDE[2], slot, side) for slot in range(2)
    )
    s_s = s_s - strip_below(own_strip, messages, WAVE_SIDE[2], 2, side)
    stiff_s, buoy_s, damp_s = coef_strip_ref[0], coef_strip_ref[1], coef_strip_ref[2]

    for step in range(1, STEPS + 1):
        flux_s, spread = strip_flux(p_s, buoy_s)
        edges = cut_edges(p_s, flux_s, cut_up, cut_down)
        if step < STEPS:
            s_s = s_s - spread
            p_s = damp_s * (p_s - stiff_s * s_s) + ss_ref[step - 1]
        for x in range(step, EX - step):
            edge_ref[step - 1, x] = plane_edge(edges, x)
    for x in range(EX):
        put_with_next(p_ref, x, initial(0, x))

    for step in range(1, STEPS + 1):
        k = step - 1
        def close(x, flux_below, fluxes):
            flux_x, flux_y, flux_z = fluxes
            spread = (flux_x - flux_below) + (flux_y - flux_ref[x, 7 : EY + 7])
            spread = spread + (flux_z - z_down(flux_z, edge_ref[step - 1, x]))
            spread = (initial(1, x) if step == 1 else spread_ref[x]) - spread
            if step < STEPS:
                spread_ref[x] = spread
                p = coef_ref[2, x] * (p_ref[x, 0:EY] - coef_ref[0, x] * spread)
                put_with_next(p_ref, x, p + s_ref[k, x - SOURCE_PLANES[0]])
            if BX <= x < 2 * BX:
                place = x - BX
                term = hist_ref[k, 0, place] * spread[0:BY]
                grad_ref[0, place] = -term if k == 0 else grad_ref[0, place] - term

        waiting = flux_below = None
        for x in range(step - 1, EX - step):
            p, buoyancy = p_ref[x, 0:EY], coef_ref[1, x]
            slopes = [p_ref[x + 1, 0:EY] - p]
            if x >= step:
                slopes += [p_ref[x, 1 : EY + 1] - p, z_up(p, edge_ref[step - 1, x]) - p]
            fluxes = [buoyancy * slope for slope in slopes]
            if x >= step:
                put_with_last(flux_ref, x, fluxes[1])
            if BX <= x < 2 * BX:
                place = x - BX
                term = hist_ref[k, 1, place] * slopes[0][0:BY]
                term = term + hist_ref[k, 2, place] * slopes[1][0:BY]
                term = term + hist_ref[k, 3, place] * slopes[2][0:BY]
                grad_ref[1, place] = -term if k == 0 else grad_ref[1, place] - term
            if waiting is not None:
                close(*waiting)
            waiting = (x, flux_below, fluxes) if x >= step else None
            flux_below = fluxes[0]
        close(*waiting)

    for kind in range(2):
        copy = pltpu.make_async_copy(grad_ref.at[kind], grad_hbm.at[kind], sems.at[1 + kind])
        copy.start()
        copies.append(copy)
    for copy in copies:
        copy.wait()


def shape(*dims):
    return jax.ShapeDtypeStruct(dims, F32)


def call(kernel, outs, operands, scratch, places, micros=0.1, out_place="v"):
    spaces = {"h": pltpu.HBM, "a": pl.ANY, "v": pltpu.VMEM}
    operands = [
        pltpu.with_memory_space_constraint(operand, pltpu.HBM) if place == "h" else operand
        for operand, place in zip(operands, places)
    ]
    return pl.pallas_call(
        kernel,
        out_shape=outs,
        in_specs=[pl.BlockSpec(memory_space=spaces[place]) for place in places],
        out_specs=[pl.BlockSpec(memory_space=spaces[out_place])] * len(outs),
        scratch_shapes=scratch,
        compiler_params=pltpu.CompilerParams(vmem_limit_bytes=VMEM_LIMIT),
        cost_estimate=pl.CostEstimate(
            flops=0, bytes_accessed=int(3.69e6 * micros), transcendentals=0
        ),
    )(*operands)


def from_sides(sends, axes):
    count = lax.axis_size("gy")

    def route(offset):
        pairs = []
        for target in range(count):
            source = target + offset
            if 0 <= source < count:
                if "gz" in axes:
                    pairs += [(2 * source + z, 2 * target + 1 - z) for z in range(2)]
                else:
                    pairs.append((source, target))
        return pairs

    if count == 2:
        both = lax.ppermute(sends[0], axes, route(1) + route(-1))
        return both, both
    upward, downward = sends
    return lax.ppermute(downward, axes, route(1)), lax.ppermute(upward, axes, route(-1))


def rotated(array, axis, offset):
    count = lax.axis_size(axis)
    return lax.ppermute(array, axis, [((i + offset) % count, i) for i in range(count)])


def paired(array, odd):
    count = lax.axis_size("gx")
    pairs = []
    for i in range(count):
        partner = ((i - 1) ^ 1) + 1 if odd else i ^ 1
        pairs.append((partner if 0 <= partner < count else i, i))
    return lax.ppermute(array, "gx", pairs)


def local(
    stored, adjoint_end, labels, tissue, source_cells, source_wave, receiver_cells, receiver_wave
):
    assert lax.axis_size("gz") == 2 and labels.shape == (BX, BY, BZ) and tissue.shape[1] == 8
    half = lax.axis_size("gx") // 2
    arguments = [
        stored, adjoint_end, labels, tissue,
        receiver_cells.T, receiver_wave, source_cells.T, source_wave,
    ]
    ways = 1 if lax.axis_size("gy") == 2 else 2
    wave, ql, t, last_x, last_y, strips, table, receivers, receiver_wave, sources, source_wave, *sends = call(
        load_kernel,
        [
            shape(2 * PLANES, BZ),
            shape(2 * PLANES, BZ),
            shape(PLANES, BZ),
            shape(2 * BY, BZ),
            shape(2 * BX * 8, BZ),
            shape(3 * BY, BZ),
            shape(24, BZ),
        ]
        + [jax.ShapeDtypeStruct(array.shape, array.dtype) for array in arguments[4:]]
        + [shape(20 * 8, BZ)] * ways
        + [shape(2 * 8, BZ)] * ways,
        arguments,
        [
            pltpu.VMEM(stored.shape, F32),
            pltpu.VMEM(adjoint_end.shape, F32),
            pltpu.VMEM(labels.shape, jnp.int32),
            pltpu.SMEM(tissue.shape, F32),
            pltpu.SemaphoreType.DMA,
        ],
        "hhhhhhhh",
        1.4,
    )
    from_up, from_down = from_sides(sends[:ways], "gy")
    other = rotated(strips, "gz", 1)
    corner_up, corner_down = from_sides(sends[ways:], ("gy", "gz"))
    wave = rotated(wave, "gx", half)
    rb, rsb = call(
        late_kernel,
        [shape(2, EX * EY, BZ), shape(2, EY, BZ)],
        [receivers, receiver_wave],
        [],
        "vv",
        1.2,
    )
    early_planes, source_planes = (last - first for first, last in (EARLY_PLANES, SOURCE_PLANES))
    late, adj_late = call(
        merge_kernel,
        [shape(WAVE_FIX + 24, BZ), shape(ADJ_OWN[2] + EY, BZ)],
        [from_up, from_down, corner_up, corner_down, strips, other, t, last_x, last_y, rsb],
        [],
        "vvvvvvvvva",
    )
    late = rotated(late, "gx", half)
    ra, rsa = call(
        early_kernel,
        [shape(2, early_planes * EY, BZ), shape(2, EY, BZ)],
        [receivers, receiver_wave, adj_late],
        [],
        "vva",
        1.0,
    )
    ra, rb = ra.reshape(2, early_planes, EY, BZ), rb.reshape(2, EX, EY, BZ)
    even, odd = call(
        adjoint_join_kernel,
        [shape(ADJ_SIDE[2] + EY + 2 * PLANES, BZ)] * 2,
        [ql, adj_late, wave],
        [],
        "vva",
    )
    even, odd = paired(even, False), paired(odd, True)
    src, src_strip = call(
        source_kernel,
        [shape(STEPS - 1, source_planes * EY, BZ), shape(STEPS - 1, EY, BZ)],
        [sources, source_wave, adj_late],
        [],
        "vva",
        0.5,
    )
    src = src.reshape(STEPS - 1, source_planes, EY, BZ)
    own_s, wave_even, wave_odd = call(
        join_kernel,
        [shape(PLANES, BZ)] + [shape(WAVE_SIDE[2] + EY, BZ)] * 2,
        [wave, late],
        [],
        "vv",
    )
    wave_even, wave_odd = paired(wave_even, False), paired(wave_odd, True)
    adjoint_out, hist, coef, coef_strip = call(
        adjoint_kernel,
        [
            shape(4, BX, BY, BZ),
            shape(STEPS, 4, BX, BY, BZ),
            shape(3, EX, EY, BZ),
            shape(3, EY, BZ),
        ],
        [ql, adj_late, even, odd, adjoint_end, ra, rsa, rb, rsb, table],
        [pltpu.VMEM((EX, EY + 8, BZ), F32)] * 2
        + [pltpu.VMEM((EX, EY, BZ), F32)] * 3
        + [
            pltpu.VMEM((STEPS, EX, EY, BZ), F32),
            pltpu.SemaphoreType.DMA,
        ],
        "vvvvhvvvvv",
        3.9,
    )
    return call(
        forward_kernel,
        [shape(2, BX, BY, BZ), shape(4, BX, BY, BZ)],
        [
            wave, own_s, late, wave_even, wave_odd, coef, coef_strip, src, src_strip, hist,
            adjoint_out,
        ],
        [pltpu.VMEM((EX, EY + 8, BZ), F32)] * 2
        + [
            pltpu.VMEM((EX, EY, BZ), F32),
            pltpu.VMEM((STEPS, EX, EY, BZ), F32),
            pltpu.VMEM((2, BX, BY, BZ), F32),
            pltpu.SemaphoreType.DMA((3,)),
        ],
        "vvvvvvvvvvv",
        2.5,
        "a",
    )


def solution(mesh):
    return jax.shard_map(
        local,
        mesh=mesh,
        in_specs=(
            P("shot", "gx", "gy", "gz"),
            P("shot", "gx", "gy", "gz"),
            P("gx", "gy", "gz"),
            P(),
            P("shot", None),
            P(None, "shot"),
            P(),
            P(None, "shot"),
        ),
        out_specs=(P("shot", "gx", "gy", "gz"), P("shot", "gx", "gy", "gz")),
        check_vma=False,
    )
```

```python
import jax
import jax.numpy as jnp
from jax import lax
from jax.experimental import pallas as pl
from jax.experimental.pallas import tpu as pltpu
from jax.sharding import PartitionSpec as P

STEPS = 4
MARGIN = 4
BX, BY, BZ = 4, 32, 128
EX, EY = BX + 2 * MARGIN, BY + 2 * MARGIN
STRIP = 2 * MARGIN
F32 = jnp.float32
BF16 = jnp.bfloat16
VMEM_LIMIT = 16 * 1024 * 1024
PLANES = BX * BY
WAVE_OWN = (0, BY, BY + 9 * 8)
WAVE_FIX = WAVE_OWN[2] + EY
FIX_LANE = 3 * BX * STRIP
ADJ_OWN = (PLANES, PLANES + BY, PLANES + BY + 13 * 8)
WAVE_SIDE = (PLANES + 3 * BY, PLANES + 4 * BY)
ADJ_SIDE = (3 * BY, 4 * BY)
WAVE_TILES, ADJ_TILES = 6, 9


def lanes(shape):
    return lax.broadcasted_iota(jnp.int32, shape, len(shape) - 1)


def rows(shape):
    return lax.broadcasted_iota(jnp.int32, shape, len(shape) - 2)


def run(copies):
    for copy in copies:
        copy.start()
    for copy in copies:
        copy.wait()


def coefficients(labels, table_ref):
    result = [jnp.zeros(labels.shape, F32) for _ in range(3)]
    for index in range(8):
        picked = labels == float(index + 1)
        for kind in range(3):
            row = kind * 8 + index
            result[kind] = jnp.where(picked, table_ref[row : row + 1], result[kind])
    return result


def buoyancy_of(labels, table_ref):
    result = jnp.zeros(labels.shape, F32)
    for index in range(8):
        result = jnp.where(labels == float(index + 1), table_ref[8 + index : 9 + index], result)
    return result


def half_turn(tile):
    return pltpu.roll(tile, MARGIN, 0)


def load_kernel(
    stored_hbm, adj_hbm, lab_hbm, tissue_hbm, rc_hbm, rw_hbm, sc_hbm, sw_hbm,
    wave_ref, ql_ref, t_ref, last_x_ref, last_y_ref, strip_ref, table_ref,
    rc_ref, rw_ref, sc_ref, sw_ref, *rest,
):
    *sends, stored, adj, lab, tissue, sem = rest
    run([
        pltpu.make_async_copy(source, target, sem)
        for source, target in (
            (stored_hbm, stored), (adj_hbm, adj), (lab_hbm, lab), (tissue_hbm, tissue),
            (rc_hbm, rc_ref), (rw_hbm, rw_ref), (sc_hbm, sc_ref), (sw_hbm, sw_ref),
        )
    ])
    for index in range(tissue.shape[1]):
        speed = jnp.full((1, BZ), tissue[0, index], F32)
        density = jnp.full((1, BZ), tissue[1, index], F32)
        table_ref[index : index + 1] = density * speed
        table_ref[8 + index : 9 + index] = speed / density
        table_ref[16 + index : 17 + index] = 1.0 - jnp.full((1, BZ), tissue[2, index], F32)
    gy, gz = lax.axis_index("gy"), lax.axis_index("gz")
    lane = lanes((BY, BZ))
    row = rows((BY, BZ))
    tile_row = rows((8, BZ))
    strips = [jnp.zeros((BY, BZ), F32) for _ in range(3)]
    tiles = [None] * 39
    previous = [None, None]

    def edge_tile(block):
        return jnp.where(tile_row < MARGIN, block[0:8], block[BY - 8 : BY])

    for x in range(BX):
        labels = lab[x].astype(F32) + 1.0
        buoyancy = buoyancy_of(labels, table_ref)
        plane = slice(x * BY, x * BY + BY)
        fields = [stored[index, x] for index in range(4)] + [adj[0, x]]
        fields += [buoyancy * adj[index, x] for index in range(1, 4)] + [labels]
        wave_ref[plane] = fields[0]
        ql_ref[plane] = fields[4]
        ql_ref[PLANES + x * BY : PLANES + x * BY + BY] = labels
        for index, block in enumerate(fields):
            tiles[index * BX + x] = edge_tile(block)
            group, slot = divmod(index, 4)
            base = slot * BX * STRIP + x * STRIP
            rolled = pltpu.roll(block, base + MARGIN, 1)
            first = base + MARGIN * gz
            strips[group] = jnp.where(
                (lane >= first) & (lane < first + MARGIN), rolled, strips[group]
            )
        for kind, (target, base) in enumerate(((wave_ref, PLANES), (t_ref, 0))):
            vx, vy, vz = fields[4 * kind + 1 : 4 * kind + 4]
            spread = vx if x == 0 else vx - previous[kind]
            spread = spread + (vy - jnp.where(row == 0, 0.0, pltpu.roll(vy, 1, 0)))
            spread = spread + (vz - jnp.where(lane == 0, 0.0, pltpu.roll(vz, 1, 1)))
            target[base + x * BY : base + x * BY + BY] = spread
            previous[kind] = vx
            index = (kind * BX + x) * 8
            last_y_ref[index : index + 8] = vy[BY - 8 : BY]
    for kind in range(2):
        last_x_ref[kind * BY : kind * BY + BY] = previous[kind]
    for group in range(3):
        strip_ref[group * BY : group * BY + BY] = strips[group]
        tiles[9 * BX + group] = edge_tile(strips[group])

    def joined(first, second):
        second = first if second is None else second
        upward = jnp.where(tile_row < MARGIN, half_turn(first), second)
        downward = jnp.where(tile_row < MARGIN, first, half_turn(second))
        if len(sends) == 2:
            return (jnp.where(gy == 0, upward, downward),)
        return upward, downward

    tiles.append(None)
    half = len(sends) // 2
    for place in range(20):
        for target, tile in zip(sends[:half], joined(tiles[2 * place], tiles[2 * place + 1])):
            target[place * 8 : place * 8 + 8] = tile
    for place in range(2):
        first = tiles[9 * BX + 2 * place]
        for target, tile in zip(sends[half:], joined(first, tiles[9 * BX + 2 * place + 1])):
            target[place * 8 : place * 8 + 8] = tile


def copy_rows(target, base, source, first, count):
    target[base : base + count] = source[pl.ds(pl.multiple_of(first, 8), count)]
    return base + count


def halved():
    return lax.axis_size("gy") == 2


def tile_rows(count):
    return (count + 1) // 2 * 8 if halved() else count * 8


def put_tiles(target, base, source, firsts):
    tiles = [source[pl.ds(pl.multiple_of(first, 8), 8)] for first in firsts]
    if halved():
        upper = lax.axis_index("gy") == 0
        row = rows((8, BZ))
        pairs = [(tiles[i], tiles[min(i + 1, len(tiles) - 1)]) for i in range(0, len(tiles), 2)]
        tiles = [
            jnp.where(
                row < MARGIN,
                jnp.where(upper, first, half_turn(first)),
                jnp.where(upper, half_turn(second), second),
            )
            for first, second in pairs
        ]
    for place, tile in enumerate(tiles):
        target[base + place * 8 : base + place * 8 + 8] = tile
    return base + 8 * len(tiles)


def pair_planes():
    parity = lax.rem(lax.axis_index("gx"), 2)
    return 1 - parity, parity


def merge_kernel(
    from_up, from_down, corner_up, corner_down, strip_ref, other_ref,
    t_ref, last_x_ref, last_y_ref, _,
    wave_ref, adj_ref,
):
    gy = lax.axis_index("gy")
    tile_row = rows((8, BZ))
    row, lane = rows((BY, BZ)), lanes((BY, BZ))
    take_up = (tile_row < MARGIN) & (gy < lax.axis_size("gy") - 1)
    take_down = (tile_row >= MARGIN) & (gy > 0)
    _, cut_down = cut_flags()

    def halo(up, down, index):
        place, second = divmod(index, 2)
        sl = slice(place * 8, place * 8 + 8)
        above = half_turn(up[sl]) if second else up[sl]
        below = down[sl] if second else half_turn(down[sl])
        return jnp.where(take_up, above, jnp.where(take_down, below, 0.0))

    wide = []
    for group in range(3):
        sl = slice(group * BY, group * BY + BY)
        tile = halo(from_up, from_down, 9 * BX + group) + halo(corner_up, corner_down, group)
        wide.append(jnp.concatenate([strip_ref[sl] + other_ref[sl], tile], 0))
    strip_lane = lanes((EY, BZ))

    def strip_field(index):
        group, slot = divmod(index, 4)
        moved = pltpu.roll(wide[group], (BZ - slot * BX * STRIP) % BZ, 1) if slot else wide[group]
        return jnp.where(strip_lane < BX * STRIP, moved, 0.0)

    last_lanes = (BX - 1) * STRIP
    fix_row = jnp.zeros((8, BZ), F32)
    fix_lane = jnp.zeros((BY, BZ), F32)
    for kind, target in enumerate((wave_ref, adj_ref)):
        first = 4 * kind
        planes_end, x_end, tiles_end = (WAVE_OWN, ADJ_OWN)[kind]
        vx, vy, vz = (strip_field(first + 1 + axis) for axis in range(3))
        spread = vx - jnp.where(strip_lane < STRIP, 0.0, pltpu.roll(vx, STRIP, 1))
        spread = (spread + (vy - y_down(vy))) + (vz - pltpu.roll(vz, 1, 1))
        strip = strip_field(first)
        strip = strip + pltpu.roll(jnp.where(strip_lane < BX * STRIP, spread, 0.0), BX * STRIP, 1)
        last_slot = 2
        if kind == 1:
            strip = strip + pltpu.roll(strip_field(8), 2 * BX * STRIP, 1)
            last_slot = 3
        last = jnp.where(strip_lane >= last_lanes, vx, 0.0)
        strip = strip + pltpu.roll(last, last_slot * BX * STRIP - last_lanes, 1)
        target[planes_end:x_end] = last_x_ref[kind * BY : kind * BY + BY]

        vx_before = None
        for x in range(BX):
            vx_t, vy_t, vz_t = (
                halo(from_up, from_down, (first + 1 + axis) * BX + x) for axis in range(3)
            )
            below_z = pltpu.roll(vz, (BZ - (x * STRIP + MARGIN - 1)) % BZ, 1) * cut_down
            last_y = last_y_ref[(kind * BX + x) * 8 : (kind * BX + x) * 8 + 8]
            y_before = jnp.where(
                tile_row == 0, pltpu.roll(last_y, 1, 0), pltpu.roll(vy_t, 1, 0)
            )
            z_before = jnp.where(lane[0:8] == 0, below_z[BY:EY], pltpu.roll(vz_t, 1, 1))
            spread = vx_t if x == 0 else vx_t - vx_before
            spread = (spread + (vy_t - y_before)) + (vz_t - z_before)
            vx_before = vx_t
            if kind == 0:
                fix_row = jnp.where(tile_row == x, vy_t[7:8], fix_row)
                moved = pltpu.roll(below_z[0:BY], FIX_LANE + x, 1)
                fix_lane = jnp.where(lane == FIX_LANE + x, moved, fix_lane)
            else:
                block = t_ref[x * BY : x * BY + BY]
                block = block - jnp.where(row == 0, vy_t[7:8], 0.0)
                block = block - jnp.where(lane == 0, below_z[0:BY], 0.0)
                target[x * BY : x * BY + BY] = block
            base = x_end + x * 8
            target[base : base + 8] = halo(from_up, from_down, first * BX + x)
            target[base + 32 : base + 40] = spread
            if kind == 1:
                target[base + 64 : base + 72] = halo(from_up, from_down, 8 * BX + x)
        target[tiles_end - 8 : tiles_end] = vx_before
        if kind == 0:
            target[tiles_end : tiles_end + BY] = strip[0:BY] + fix_lane
            target[tiles_end + BY : tiles_end + EY] = strip[BY:EY]
            target[WAVE_FIX : WAVE_FIX + 8] = fix_row
            target[WAVE_FIX + 8 : WAVE_FIX + 24] = jnp.zeros((16, BZ), F32)
        else:
            target[tiles_end : tiles_end + EY] = strip


def adjoint_join_kernel(ql_ref, adj_ref, _, even_ref, odd_ref):
    planes_end, x_end, tiles_end = ADJ_OWN
    for target, first in zip((even_ref, odd_ref), pair_planes()):
        base = copy_rows(target, 0, adj_ref, first * BY, 3 * BY)
        base = copy_rows(target, base, adj_ref, planes_end, BY)
        near = [x_end + (first + plane) * 8 for plane in range(3)]
        nearest = [x_end + 32 + first * 16 + plane * 8 for plane in range(2)]
        firsts = near + nearest + [start + 64 for start in near] + [tiles_end - 8]
        base = put_tiles(target, base, adj_ref, firsts)
        base = copy_rows(target, base, adj_ref, tiles_end, EY)
        copy_rows(target, base, ql_ref, 0, 2 * PLANES)


def join_kernel(wave_ref, late_ref, s_ref, even_ref, odd_ref):
    planes_end, x_end, tiles_end = WAVE_OWN
    row, lane = rows((BY, BZ)), lanes((BY, BZ))
    fix_lane = late_ref[tiles_end : tiles_end + BY]
    for x in range(BX):
        block = wave_ref[PLANES + x * BY : PLANES + x * BY + BY]
        fix_row = late_ref[WAVE_FIX + x : WAVE_FIX + x + 1]
        block = block - jnp.where(row == 0, fix_row, 0.0)
        block = block - jnp.where(lane == 0, pltpu.roll(fix_lane, BZ - FIX_LANE - x, 1), 0.0)
        s_ref[x * BY : x * BY + BY] = block
    for target, first in zip((even_ref, odd_ref), pair_planes()):
        base = copy_rows(target, 0, wave_ref, 0, PLANES)
        base = copy_rows(target, base, s_ref, first * BY, 3 * BY)
        base = copy_rows(target, base, late_ref, planes_end, BY)
        near = [x_end + (first + plane) * 8 for plane in range(3)]
        nearest = [x_end + 32 + first * 16 + plane * 8 for plane in range(2)]
        base = put_tiles(target, base, late_ref, near + nearest + [tiles_end - 8])
        copy_rows(target, base, late_ref, tiles_end, EY)


def split(values):
    high = values.astype(BF16)
    rest = values - high.astype(F32)
    middle = rest.astype(BF16)
    low = (rest - middle.astype(F32)).astype(BF16)
    return high, middle, low


def places(cells, sl):
    gx, gy, gz = (lax.axis_index(name) for name in ("gx", "gy", "gz"))
    cut = BZ * lax.axis_size("gz") // 2 - MARGIN
    cell_x = cells[0:1, sl] - (gx * BX - MARGIN)
    cell_y = cells[1:2, sl] - gy * BY
    cell_z = cells[2:3, sl]
    in_x = (cell_x >= 0) & (cell_x < EX)
    in_y = (cell_y >= -MARGIN) & (cell_y < BY + MARGIN)
    row = jnp.where(cell_y < 0, cell_y + EY, cell_y)
    flat = jnp.where(in_x & in_y, cell_x * EY + row, -1)
    row = jnp.where(in_y, row, -1)
    zz = cell_z - cut
    in_strip = in_x & (zz >= 0) & (zz < STRIP)
    strip_lane = jnp.where(in_strip, cell_x * STRIP + zz, -1)
    return flat, cell_z - gz * BZ, row, strip_lane


def hits(count, index):
    return rows((count, index.shape[1])) == index


def product(left, right):
    return lax.dot_general(
        left, right, (((1,), (1,)), ((), ())), preferred_element_type=F32
    )


def inject_points(cells, wave_ref, width, waves, planes, out_ref, strip_out_ref):
    count, low, total_rows = len(waves), planes[0] * EY, (planes[1] - planes[0]) * EY
    for start in range(0, cells.shape[1], width):
        sl = slice(start, start + width)
        flat, z, row, strip_lane = places(cells, sl)
        here = hits(total_rows, flat - low).astype(F32).astype(BF16)
        at_strip = hits(BZ, strip_lane).astype(F32).astype(BF16)
        at_z, at_row = hits(BZ, z), hits(EY, row)
        total = strip_total = None
        parts = [split(wave_ref[wave : wave + 1, sl]) for wave in waves]
        for part in range(3):
            amounts = [parts[wave][part].astype(F32) for wave in range(count)]
            right = jnp.concatenate([jnp.where(at_z, a, 0.0) for a in amounts], 0).astype(BF16)
            left = jnp.concatenate([jnp.where(at_row, a, 0.0) for a in amounts], 0).astype(BF16)
            term, strip_term = product(here, right), product(left, at_strip)
            total = term if part == 0 else total + term
            strip_total = strip_term if part == 0 else strip_total + strip_term
        for wave in range(count):
            value = total[:, wave * BZ : wave * BZ + BZ]
            strip_value = strip_total[wave * EY : wave * EY + EY]
            if start > 0:
                value = value + out_ref[wave]
                strip_value = strip_value + strip_out_ref[wave]
            out_ref[wave] = value
            strip_out_ref[wave] = strip_value


LATE_PLANES, EARLY_PLANES, SOURCE_PLANES = (0, EX), (2, EX - 2), (1, EX - 1)


def late_kernel(receivers, receiver_wave, r_ref, rs_ref):
    inject_points(receivers, receiver_wave, 256, (2, 3), LATE_PLANES, r_ref, rs_ref)


def early_kernel(receivers, receiver_wave, _, r_ref, rs_ref):
    inject_points(receivers, receiver_wave, 256, (0, 1), EARLY_PLANES, r_ref, rs_ref)


def source_kernel(sources, source_wave, _, s_ref, ss_ref):
    width = sources.shape[1]
    inject_points(sources, source_wave, width, (0, 1, 2), SOURCE_PLANES, s_ref, ss_ref)


def strip_of(packed, block, slot):
    lane = lanes(packed.shape)
    width = BX * STRIP
    shift = (block * width - slot * width) % BZ
    moved = pltpu.roll(packed, shift, 1) if shift else packed
    return jnp.where((lane >= block * width) & (lane < (block + 1) * width), moved, 0.0)


def y_up(v):
    return pltpu.roll(v, EY - 1, 0)


def y_down(v):
    return pltpu.roll(v, 1, 0)


def z_up(v, edge):
    return jnp.where(lanes(v.shape) == BZ - 1, edge, pltpu.roll(v, BZ - 1, 1))


def z_down(v, edge):
    return jnp.where(lanes(v.shape) == 0, edge, pltpu.roll(v, 1, 1))


def cut_edges(values, flux_z, cut_up, cut_down):
    place = lax.rem(lanes(values.shape), STRIP)
    above = jnp.where(place == MARGIN, values * cut_up, 0.0)
    below = jnp.where(place == MARGIN - 1, flux_z * cut_down, 0.0)
    return pltpu.roll(above, BZ - 2, 1) + below


def plane_edge(edges, x):
    return pltpu.roll(edges, (BZ - (x * STRIP + MARGIN - 1)) % BZ, 1)


def strip_flux(values, buoyancy):
    flux_x = buoyancy * (pltpu.roll(values, BZ - STRIP, 1) - values)
    flux_y = buoyancy * (y_up(values) - values)
    flux_z = buoyancy * (pltpu.roll(values, BZ - 1, 1) - values)
    spread = (flux_x - pltpu.roll(flux_x, STRIP, 1)) + (flux_y - y_down(flux_y))
    return flux_z, spread + (flux_z - pltpu.roll(flux_z, 1, 1))


def cut_flags():
    gz, half = lax.axis_index("gz"), lax.axis_size("gz") // 2
    return jnp.where(gz == half - 1, 1.0, 0.0), jnp.where(gz == half, 1.0, 0.0)


def sides():
    gx = lax.axis_index("gx")
    low = jnp.where(gx > 0, 1.0, 0.0)
    high = jnp.where(gx < lax.axis_size("gx") - 1, 1.0, 0.0)
    return low, high, lax.rem(gx, 2) == 0


def from_side(messages, first, count, block, side):
    even, odd = (message[first : first + count] for message in messages)
    low, high, even_above = side
    if block == 0:
        return jnp.where(even_above, odd, even) * low
    return jnp.where(even_above, even, odd) * high


def side_tile(messages, base, place, block, side):
    if not halved():
        return from_side(messages, base + place * 8, 8, block, side)
    tile = from_side(messages, base + place // 2 * 8, 8, block, side)
    upper = lax.axis_index("gy") == 0
    turned = half_turn(tile)
    tile = jnp.where(upper, turned, tile) if place % 2 else jnp.where(upper, tile, turned)
    return jnp.where((rows((8, BZ)) < MARGIN) == upper, tile, 0.0)


def side_place(wanted, plane, block):
    planes = range(BX - wanted, BX) if block == 0 else range(wanted)
    return planes.index(plane) if plane in planes else None


def widened(own, own_tiles, x, layout, side):
    block, plane = divmod(x, BX)
    if block == 1:
        main = own[0][own[1] + plane * BY : own[1] + plane * BY + BY]
        tile = own_tiles[0][own_tiles[1] + plane * 8 : own_tiles[1] + plane * 8 + 8]
        return jnp.concatenate([main, tile], 0)
    (messages, base, wanted), (tile_messages, tile_base, tile_place, tile_wanted) = layout
    main, tile = jnp.zeros((BY, BZ), F32), jnp.zeros((8, BZ), F32)
    place = side_place(wanted, plane, block)
    if place is not None:
        main = from_side(messages, base + place * BY, BY, block, side)
    place = side_place(tile_wanted, plane, block)
    if place is not None:
        tile = side_tile(tile_messages, tile_base, tile_place + place, block, side)
    return jnp.concatenate([main, tile], 0)


def less_plane_below(value, x, own_ref, own_rows, messages, side_layout, side):
    if x == BX:
        (planes_end, x_end), count = side_layout
        main = from_side(messages, planes_end, BY, 0, side)
        tile = side_tile(messages, x_end, count - 1, 0, side)
    elif x == 2 * BX:
        planes_end, _, tiles_end = own_rows
        high = side[1]
        main = own_ref[planes_end : planes_end + BY] * high
        tile = own_ref[tiles_end - 8 : tiles_end] * high
    else:
        return value
    return value - jnp.concatenate([main, tile], 0)


def strip_below(own, messages, first, slot, side):
    lane = lanes(own.shape)
    width = BX * STRIP
    low = from_side(messages, first, EY, 0, side)
    low = pltpu.roll(low, (width - slot * width) % BZ, 1)
    own = pltpu.roll(own * side[1], (2 * width - slot * width) % BZ, 1)
    in_own = (lane >= width) & (lane < width + STRIP)
    in_high = (lane >= 2 * width) & (lane < 2 * width + STRIP)
    return jnp.where(in_own, low, jnp.where(in_high, own, 0.0))


def whole_strip(own, messages, first, slot, side):
    low = from_side(messages, first, EY, 0, side)
    high = from_side(messages, first, EY, 2, side)
    return strip_of(low, 0, slot) + strip_of(own, 1, slot) + strip_of(high, 2, slot)


def adjoint_kernel(
    ql_ref, late_ref, even, odd, adj_hbm, ra_ref, rsa_ref, rb_ref, rsb_ref,
    table_ref,
    out_ref, hist_ref, coef_ref, coef_strip_ref,
    q_ref, t_ref, u_ref, scale_ref, edge_ref, flux_ref, w_sem,
):
    w_copy = pltpu.make_async_copy(adj_hbm.at[pl.ds(1, 3)], out_ref.at[pl.ds(1, 3)], w_sem)
    w_copy.start()
    cut_up, cut_down = cut_flags()
    side = sides()
    messages = (even, odd)
    r_refs = ((ra_ref, 0), (ra_ref, 1), (rb_ref, 0), (rb_ref, 1))
    rs_refs = ((rsa_ref, 0), (rsa_ref, 1), (rsb_ref, 0), (rsb_ref, 1))
    tiles, own_tiles = ADJ_SIDE[1], ADJ_OWN[1]
    side_strip = tiles + tile_rows(ADJ_TILES)
    raws = side_strip + EY

    def initial(index, x):
        own = ((ql_ref, 0), (late_ref, 0), (ql_ref, PLANES))[index]
        layout = (
            ((messages, raws, 4), (messages, tiles, 0, 3)),
            ((messages, 0, 3), (messages, tiles, 3, 2)),
            ((messages, raws + PLANES, 4), (messages, tiles, 5, 3)),
        )[index]
        value = widened(own, (late_ref, own_tiles + 32 * index), x, layout, side)
        if index == 1:
            value = less_plane_below(
                value, x, late_ref, ADJ_OWN, messages, (ADJ_SIDE, ADJ_TILES), side
            )
        return value

    for x in range(EX):
        stiff, buoy, damp = coefficients(initial(2, x), table_ref)
        coef_ref[0, x], coef_ref[1, x], coef_ref[2, x] = stiff, buoy, damp
        scale_ref[x] = stiff * damp
    own_strip = late_ref[ADJ_OWN[2] : ADJ_OWN[2] + EY]
    q_s, t_s, label_s = (
        whole_strip(own_strip, messages, side_strip, slot, side) for slot in range(3)
    )
    t_s = t_s - strip_below(own_strip, messages, side_strip, 3, side)
    stiff_s, buoy_s, damp_s = coefficients(label_s, table_ref)
    scale_s = stiff_s * damp_s
    coef_strip_ref[0], coef_strip_ref[1], coef_strip_ref[2] = stiff_s, buoy_s, damp_s
    w_copy.wait()

    for step in range(1, STEPS + 1):
        rs_ref, place = rs_refs[STEPS - step]
        q_s = q_s + rs_ref[place]
        u_s = scale_s * q_s
        flux_s, spread = strip_flux(u_s, buoy_s)
        t_s = t_s + spread
        q_s = damp_s * q_s + t_s
        edges = cut_edges(u_s, flux_s, cut_up, cut_down)
        for x in range(step, EX - step):
            edge_ref[step - 1, x] = plane_edge(edges, x)

    for step in range(1, STEPS + 1):
        k = STEPS - step
        r_ref, place = r_refs[k]
        r_first = (EARLY_PLANES if k < 2 else LATE_PLANES)[0]

        for x in range(step - 1, EX - step + 1):
            q = (initial(0, x) if step == 1 else q_ref[x]) + r_ref[place, x - r_first]
            q_ref[x] = q
            u_ref[x] = scale_ref[x] * q

        for x in range(step - 1, EX - step):
            u, buoyancy = u_ref[x], coef_ref[1, x]
            slopes = [u_ref[x + 1] - u]
            if x >= step:
                slopes += [y_up(u) - u, z_up(u, edge_ref[step - 1, x]) - u]
            for axis, slope in enumerate(slopes):
                flux_ref[axis, x] = buoyancy * slope
            if BX <= x < 2 * BX:
                for axis, slope in enumerate(slopes):
                    w = out_ref[1 + axis, x - BX] + slope[0:BY]
                    out_ref[1 + axis, x - BX] = w
                    hist_ref[k, 1 + axis, x - BX] = w

        for x in range(step, EX - step):
            flux_y, flux_z = flux_ref[1, x], flux_ref[2, x]
            spread = (flux_ref[0, x] - flux_ref[0, x - 1]) + (flux_y - y_down(flux_y))
            spread = spread + (flux_z - z_down(flux_z, edge_ref[step - 1, x]))
            damped = coef_ref[2, x] * q_ref[x]
            t = (initial(1, x) if step == 1 else t_ref[x]) + spread
            if BX <= x < 2 * BX:
                hist_ref[k, 0, x - BX] = damped[0:BY]
            if step < STEPS:
                t_ref[x] = t
                q_ref[x] = damped + t
            else:
                out_ref[0, x - BX] = (damped + t)[0:BY]


def forward_kernel(
    wave_ref, own_s_ref, late_ref, even, odd, coef_ref, coef_strip_ref, s_ref, ss_ref, hist_ref,
    adjoint_ref, grad_hbm, adjoint_hbm,
    p_ref, spread_ref, edge_ref, flux_ref, grad_ref, sems,
):
    copies = [pltpu.make_async_copy(adjoint_ref, adjoint_hbm, sems.at[0])]
    copies[0].start()

    def send(index, kind, first, count):
        planes = pl.ds(first, count)
        copy = pltpu.make_async_copy(
            grad_ref.at[kind, planes], grad_hbm.at[kind, planes], sems.at[index]
        )
        copy.start()
        copies.append(copy)

    cut_up, cut_down = cut_flags()
    side = sides()
    messages = (even, odd)
    tiles, own_tiles = WAVE_SIDE[1], WAVE_OWN[1]
    side_strip = tiles + tile_rows(WAVE_TILES)

    def initial(index, x):
        layout = (
            ((messages, 0, 4), (messages, tiles, 0, 3)),
            ((messages, PLANES, 3), (messages, tiles, 3, 2)),
        )[index]
        own = ((wave_ref, 0), (own_s_ref, 0))[index]
        value = widened(own, (late_ref, own_tiles + 32 * index), x, layout, side)
        if index == 1:
            value = less_plane_below(
                value, x, late_ref, WAVE_OWN, messages, (WAVE_SIDE, WAVE_TILES), side
            )
        return value

    own_strip = late_ref[WAVE_OWN[2] : WAVE_OWN[2] + EY]
    p_s, s_s = (
        whole_strip(own_strip, messages, side_strip, slot, side) for slot in range(2)
    )
    s_s = s_s - strip_below(own_strip, messages, side_strip, 2, side)
    stiff_s, buoy_s, damp_s = coef_strip_ref[0], coef_strip_ref[1], coef_strip_ref[2]

    for step in range(1, STEPS + 1):
        flux_s, spread = strip_flux(p_s, buoy_s)
        edges = cut_edges(p_s, flux_s, cut_up, cut_down)
        if step < STEPS:
            s_s = s_s - spread
            p_s = damp_s * (p_s - stiff_s * s_s) + ss_ref[step - 1]
        for x in range(step, EX - step):
            edge_ref[step - 1, x] = plane_edge(edges, x)
    for x in range(EX):
        p_ref[x] = initial(0, x)

    for step in range(1, STEPS + 1):
        k = step - 1
        for x in range(step - 1, EX - step):
            p, buoyancy = p_ref[x], coef_ref[1, x]
            slopes = [p_ref[x + 1] - p]
            if x >= step:
                slopes += [y_up(p) - p, z_up(p, edge_ref[step - 1, x]) - p]
            for axis, slope in enumerate(slopes):
                flux_ref[axis, x] = buoyancy * slope
            if BX <= x < 2 * BX:
                place = x - BX
                term = hist_ref[k, 1, place] * slopes[0][0:BY]
                term = term + hist_ref[k, 2, place] * slopes[1][0:BY]
                term = term + hist_ref[k, 3, place] * slopes[2][0:BY]
                grad_ref[1, place] = -term if k == 0 else grad_ref[1, place] - term
        if step == STEPS:
            send(1, 1, 0, BX)

        for x in range(step, EX - step):
            flux_y, flux_z = flux_ref[1, x], flux_ref[2, x]
            spread = (flux_ref[0, x] - flux_ref[0, x - 1]) + (flux_y - y_down(flux_y))
            spread = spread + (flux_z - z_down(flux_z, edge_ref[step - 1, x]))
            spread = (initial(1, x) if step == 1 else spread_ref[x]) - spread
            if step < STEPS:
                spread_ref[x] = spread
                p_ref[x] = (
                    coef_ref[2, x] * (p_ref[x] - coef_ref[0, x] * spread)
                    + s_ref[k, x - SOURCE_PLANES[0]]
                )
            if BX <= x < 2 * BX:
                place = x - BX
                term = hist_ref[k, 0, place] * spread[0:BY]
                grad_ref[0, place] = -term if k == 0 else grad_ref[0, place] - term
                if step == STEPS:
                    send(2 + place, 0, place, 1)
    for copy in copies:
        copy.wait()


def shape(*dims):
    return jax.ShapeDtypeStruct(dims, F32)


def call(kernel, outs, operands, scratch, places, micros=0.1, out_place="v"):
    spaces = {"h": pltpu.HBM, "a": pl.ANY, "v": pltpu.VMEM}
    operands = [
        pltpu.with_memory_space_constraint(operand, pltpu.HBM) if place == "h" else operand
        for operand, place in zip(operands, places)
    ]
    return pl.pallas_call(
        kernel,
        out_shape=outs,
        in_specs=[pl.BlockSpec(memory_space=spaces[place]) for place in places],
        out_specs=[pl.BlockSpec(memory_space=spaces[out_place])] * len(outs),
        scratch_shapes=scratch,
        compiler_params=pltpu.CompilerParams(vmem_limit_bytes=VMEM_LIMIT),
        cost_estimate=pl.CostEstimate(
            flops=0, bytes_accessed=int(3.69e6 * micros), transcendentals=0
        ),
    )(*operands)


def from_sides(sends, axes):
    count = lax.axis_size("gy")

    def route(offset):
        pairs = []
        for target in range(count):
            source = target + offset
            if 0 <= source < count:
                if "gz" in axes:
                    pairs += [(2 * source + z, 2 * target + 1 - z) for z in range(2)]
                else:
                    pairs.append((source, target))
        return pairs

    if count == 2:
        both = lax.ppermute(sends[0], axes, route(1) + route(-1))
        return both, both
    upward, downward = sends
    return lax.ppermute(downward, axes, route(1)), lax.ppermute(upward, axes, route(-1))


def rotated(array, axis, offset):
    count = lax.axis_size(axis)
    return lax.ppermute(array, axis, [((i + offset) % count, i) for i in range(count)])


def paired(array, odd):
    count = lax.axis_size("gx")
    pairs = []
    for i in range(count):
        partner = ((i - 1) ^ 1) + 1 if odd else i ^ 1
        pairs.append((partner if 0 <= partner < count else i, i))
    return lax.ppermute(array, "gx", pairs)


def local(
    stored, adjoint_end, labels, tissue, source_cells, source_wave, receiver_cells, receiver_wave
):
    assert lax.axis_size("gz") == 2 and labels.shape == (BX, BY, BZ) and tissue.shape[1] == 8
    half = lax.axis_size("gx") // 2
    arguments = [
        stored, adjoint_end, labels, tissue,
        receiver_cells.T, receiver_wave, source_cells.T, source_wave,
    ]
    ways = 1 if lax.axis_size("gy") == 2 else 2
    wave, ql, t, last_x, last_y, strips, table, receivers, receiver_wave, sources, source_wave, *sends = call(
        load_kernel,
        [
            shape(2 * PLANES, BZ),
            shape(2 * PLANES, BZ),
            shape(PLANES, BZ),
            shape(2 * BY, BZ),
            shape(2 * BX * 8, BZ),
            shape(3 * BY, BZ),
            shape(24, BZ),
        ]
        + [jax.ShapeDtypeStruct(array.shape, array.dtype) for array in arguments[4:]]
        + [shape(20 * 8, BZ)] * ways
        + [shape(2 * 8, BZ)] * ways,
        arguments,
        [
            pltpu.VMEM(stored.shape, F32),
            pltpu.VMEM(adjoint_end.shape, F32),
            pltpu.VMEM(labels.shape, jnp.int32),
            pltpu.SMEM(tissue.shape, F32),
            pltpu.SemaphoreType.DMA,
        ],
        "hhhhhhhh",
        1.4,
    )
    from_up, from_down = from_sides(sends[:ways], "gy")
    other = rotated(strips, "gz", 1)
    corner_up, corner_down = from_sides(sends[ways:], ("gy", "gz"))
    wave = rotated(wave, "gx", half)
    rb, rsb = call(
        late_kernel,
        [shape(2, EX * EY, BZ), shape(2, EY, BZ)],
        [receivers, receiver_wave],
        [],
        "vv",
        1.2,
    )
    early_planes, source_planes = (last - first for first, last in (EARLY_PLANES, SOURCE_PLANES))
    late, adj_late = call(
        merge_kernel,
        [shape(WAVE_FIX + 24, BZ), shape(ADJ_OWN[2] + EY, BZ)],
        [from_up, from_down, corner_up, corner_down, strips, other, t, last_x, last_y, rsb],
        [],
        "vvvvvvvvva",
    )
    late = rotated(late, "gx", half)
    ra, rsa = call(
        early_kernel,
        [shape(2, early_planes * EY, BZ), shape(2, EY, BZ)],
        [receivers, receiver_wave, adj_late],
        [],
        "vva",
        1.0,
    )
    ra, rb = ra.reshape(2, early_planes, EY, BZ), rb.reshape(2, EX, EY, BZ)
    even, odd = call(
        adjoint_join_kernel,
        [shape(ADJ_SIDE[1] + tile_rows(ADJ_TILES) + EY + 2 * PLANES, BZ)] * 2,
        [ql, adj_late, wave],
        [],
        "vva",
    )
    even, odd = paired(even, False), paired(odd, True)
    src, src_strip = call(
        source_kernel,
        [shape(STEPS - 1, source_planes * EY, BZ), shape(STEPS - 1, EY, BZ)],
        [sources, source_wave, adj_late],
        [],
        "vva",
        0.5,
    )
    src = src.reshape(STEPS - 1, source_planes, EY, BZ)
    own_s, wave_even, wave_odd = call(
        join_kernel,
        [shape(PLANES, BZ)] + [shape(WAVE_SIDE[1] + tile_rows(WAVE_TILES) + EY, BZ)] * 2,
        [wave, late],
        [],
        "vv",
    )
    wave_even, wave_odd = paired(wave_even, False), paired(wave_odd, True)
    adjoint_out, hist, coef, coef_strip = call(
        adjoint_kernel,
        [
            shape(4, BX, BY, BZ),
            shape(STEPS, 4, BX, BY, BZ),
            shape(3, EX, EY, BZ),
            shape(3, EY, BZ),
        ],
        [ql, adj_late, even, odd, adjoint_end, ra, rsa, rb, rsb, table],
        [pltpu.VMEM((EX, EY, BZ), F32)] * 4
        + [
            pltpu.VMEM((STEPS, EX, EY, BZ), F32),
            pltpu.VMEM((3, EX, EY, BZ), F32),
            pltpu.SemaphoreType.DMA,
        ],
        "vvvvhvvvvv",
        3.9,
    )
    return call(
        forward_kernel,
        [shape(2, BX, BY, BZ), shape(4, BX, BY, BZ)],
        [
            wave, own_s, late, wave_even, wave_odd, coef, coef_strip, src, src_strip, hist,
            adjoint_out,
        ],
        [pltpu.VMEM((EX, EY, BZ), F32)] * 2
        + [
            pltpu.VMEM((STEPS, EX, EY, BZ), F32),
            pltpu.VMEM((3, EX, EY, BZ), F32),
            pltpu.VMEM((2, BX, BY, BZ), F32),
            pltpu.SemaphoreType.DMA((2 + BX,)),
        ],
        "vvvvvvvvvvv",
        2.5,
        "a",
    )


def solution(mesh):
    return jax.shard_map(
        local,
        mesh=mesh,
        in_specs=(
            P("shot", "gx", "gy", "gz"),
            P("shot", "gx", "gy", "gz"),
            P("gx", "gy", "gz"),
            P(),
            P("shot", None),
            P(None, "shot"),
            P(),
            P(None, "shot"),
        ),
        out_specs=(P("shot", "gx", "gy", "gz"), P("shot", "gx", "gy", "gz")),
        check_vma=False,
    )
```

```python
import jax
import jax.numpy as jnp
from jax import lax
from jax.experimental import pallas as pl
from jax.experimental.pallas import tpu as pltpu
from jax.sharding import PartitionSpec as P

STEPS = 4
MARGIN = 4
BX, BY, BZ = 4, 32, 128
EX, EY = BX + 2 * MARGIN, BY + 2 * MARGIN
STRIP = 2 * MARGIN
F32 = jnp.float32
BF16 = jnp.bfloat16
VMEM_LIMIT = 16 * 1024 * 1024
PLANES = BX * BY
WAVE_OWN = (0, BY, BY + 9 * 8)
WAVE_FIX = WAVE_OWN[2] + EY
FIX_LANE = 3 * BX * STRIP
ADJ_OWN = (PLANES, PLANES + BY, PLANES + BY + 13 * 8)
WAVE_SIDE = (PLANES + 3 * BY, PLANES + 4 * BY)
ADJ_SIDE = (3 * BY, 4 * BY)
WAVE_TILES, ADJ_TILES = 6, 9


def lanes(shape):
    return lax.broadcasted_iota(jnp.int32, shape, len(shape) - 1)


def rows(shape):
    return lax.broadcasted_iota(jnp.int32, shape, len(shape) - 2)


def run(copies):
    for copy in copies:
        copy.start()
    for copy in copies:
        copy.wait()


def coefficients(labels, table_ref):
    result = [jnp.zeros(labels.shape, F32) for _ in range(3)]
    for index in range(8):
        picked = labels == float(index + 1)
        for kind in range(3):
            row = kind * 8 + index
            result[kind] = jnp.where(picked, table_ref[row : row + 1], result[kind])
    return result


def buoyancy_of(labels, table_ref):
    result = jnp.zeros(labels.shape, F32)
    for index in range(8):
        result = jnp.where(labels == float(index + 1), table_ref[8 + index : 9 + index], result)
    return result


def half_turn(tile):
    return pltpu.roll(tile, MARGIN, 0)


def load_kernel(
    stored_hbm, adj_hbm, lab_hbm, tissue_hbm, rc_hbm, rw_hbm, sc_hbm, sw_hbm,
    wave_ref, ql_ref, t_ref, last_x_ref, last_y_ref, strip_ref, table_ref,
    rc_ref, rw_ref, sc_ref, sw_ref, *rest,
):
    *sends, stored, adj, lab, tissue, sem = rest
    run([
        pltpu.make_async_copy(source, target, sem)
        for source, target in (
            (stored_hbm, stored), (adj_hbm, adj), (lab_hbm, lab), (tissue_hbm, tissue),
            (rc_hbm, rc_ref), (rw_hbm, rw_ref), (sc_hbm, sc_ref), (sw_hbm, sw_ref),
        )
    ])
    for index in range(tissue.shape[1]):
        speed = jnp.full((1, BZ), tissue[0, index], F32)
        density = jnp.full((1, BZ), tissue[1, index], F32)
        table_ref[index : index + 1] = density * speed
        table_ref[8 + index : 9 + index] = speed / density
        table_ref[16 + index : 17 + index] = 1.0 - jnp.full((1, BZ), tissue[2, index], F32)
    gy, gz = lax.axis_index("gy"), lax.axis_index("gz")
    lane = lanes((BY, BZ))
    row = rows((BY, BZ))
    tile_row = rows((8, BZ))
    strips = [jnp.zeros((BY, BZ), F32) for _ in range(3)]
    tiles = [None] * 39
    previous = [None, None]

    def edge_tile(block):
        return jnp.where(tile_row < MARGIN, block[0:8], block[BY - 8 : BY])

    for x in range(BX):
        labels = lab[x].astype(F32) + 1.0
        buoyancy = buoyancy_of(labels, table_ref)
        plane = slice(x * BY, x * BY + BY)
        fields = [stored[index, x] for index in range(4)] + [adj[0, x]]
        fields += [buoyancy * adj[index, x] for index in range(1, 4)] + [labels]
        wave_ref[plane] = fields[0]
        ql_ref[plane] = fields[4]
        ql_ref[PLANES + x * BY : PLANES + x * BY + BY] = labels
        for index, block in enumerate(fields):
            tiles[index * BX + x] = edge_tile(block)
            group, slot = divmod(index, 4)
            base = slot * BX * STRIP + x * STRIP
            rolled = pltpu.roll(block, base + MARGIN, 1)
            first = base + MARGIN * gz
            strips[group] = jnp.where(
                (lane >= first) & (lane < first + MARGIN), rolled, strips[group]
            )
        for kind, (target, base) in enumerate(((wave_ref, PLANES), (t_ref, 0))):
            vx, vy, vz = fields[4 * kind + 1 : 4 * kind + 4]
            spread = vx if x == 0 else vx - previous[kind]
            spread = spread + (vy - jnp.where(row == 0, 0.0, pltpu.roll(vy, 1, 0)))
            spread = spread + (vz - jnp.where(lane == 0, 0.0, pltpu.roll(vz, 1, 1)))
            target[base + x * BY : base + x * BY + BY] = spread
            previous[kind] = vx
            index = (kind * BX + x) * 8
            last_y_ref[index : index + 8] = vy[BY - 8 : BY]
    for kind in range(2):
        last_x_ref[kind * BY : kind * BY + BY] = previous[kind]
    wave_ref[2 * PLANES : 2 * PLANES + BY] = jnp.zeros((BY, BZ), F32)
    for group in range(3):
        strip_ref[group * BY : group * BY + BY] = strips[group]
        tiles[9 * BX + group] = edge_tile(strips[group])

    def joined(first, second):
        second = first if second is None else second
        upward = jnp.where(tile_row < MARGIN, half_turn(first), second)
        downward = jnp.where(tile_row < MARGIN, first, half_turn(second))
        if len(sends) == 2:
            return (jnp.where(gy == 0, upward, downward),)
        return upward, downward

    tiles.append(None)
    half = len(sends) // 2
    for place in range(20):
        for target, tile in zip(sends[:half], joined(tiles[2 * place], tiles[2 * place + 1])):
            target[place * 8 : place * 8 + 8] = tile
    for place in range(2):
        first = tiles[9 * BX + 2 * place]
        for target, tile in zip(sends[half:], joined(first, tiles[9 * BX + 2 * place + 1])):
            target[place * 8 : place * 8 + 8] = tile


def copy_rows(target, base, source, first, count):
    target[base : base + count] = source[pl.ds(pl.multiple_of(first, 8), count)]
    return base + count


def halved():
    return lax.axis_size("gy") == 2


def tile_rows(count):
    return (count + 1) // 2 * 8 if halved() else count * 8


def put_tiles(target, base, source, firsts):
    tiles = [source[pl.ds(pl.multiple_of(first, 8), 8)] for first in firsts]
    if halved():
        upper = lax.axis_index("gy") == 0
        row = rows((8, BZ))
        pairs = [(tiles[i], tiles[min(i + 1, len(tiles) - 1)]) for i in range(0, len(tiles), 2)]
        tiles = [
            jnp.where(
                row < MARGIN,
                jnp.where(upper, first, half_turn(first)),
                jnp.where(upper, half_turn(second), second),
            )
            for first, second in pairs
        ]
    for place, tile in enumerate(tiles):
        target[base + place * 8 : base + place * 8 + 8] = tile
    return base + 8 * len(tiles)


def pair_planes():
    parity = lax.rem(lax.axis_index("gx"), 2)
    return 1 - parity, parity


def merge_kernel(
    from_up, from_down, corner_up, corner_down, strip_ref, other_ref,
    t_ref, last_x_ref, last_y_ref, _,
    wave_ref, adj_ref,
):
    gy = lax.axis_index("gy")
    tile_row = rows((8, BZ))
    row, lane = rows((BY, BZ)), lanes((BY, BZ))
    take_up = (tile_row < MARGIN) & (gy < lax.axis_size("gy") - 1)
    take_down = (tile_row >= MARGIN) & (gy > 0)
    _, cut_down = cut_flags()

    def halo(up, down, index):
        place, second = divmod(index, 2)
        sl = slice(place * 8, place * 8 + 8)
        above = half_turn(up[sl]) if second else up[sl]
        below = down[sl] if second else half_turn(down[sl])
        return jnp.where(take_up, above, jnp.where(take_down, below, 0.0))

    wide = []
    for group in range(3):
        sl = slice(group * BY, group * BY + BY)
        tile = halo(from_up, from_down, 9 * BX + group) + halo(corner_up, corner_down, group)
        wide.append(jnp.concatenate([strip_ref[sl] + other_ref[sl], tile], 0))
    strip_lane = lanes((EY, BZ))

    def strip_field(index):
        group, slot = divmod(index, 4)
        moved = pltpu.roll(wide[group], (BZ - slot * BX * STRIP) % BZ, 1) if slot else wide[group]
        return jnp.where(strip_lane < BX * STRIP, moved, 0.0)

    last_lanes = (BX - 1) * STRIP
    fix_row = jnp.zeros((8, BZ), F32)
    fix_lane = jnp.zeros((BY, BZ), F32)
    for kind, target in enumerate((wave_ref, adj_ref)):
        first = 4 * kind
        planes_end, x_end, tiles_end = (WAVE_OWN, ADJ_OWN)[kind]
        vx, vy, vz = (strip_field(first + 1 + axis) for axis in range(3))
        spread = vx - jnp.where(strip_lane < STRIP, 0.0, pltpu.roll(vx, STRIP, 1))
        spread = (spread + (vy - y_down(vy))) + (vz - pltpu.roll(vz, 1, 1))
        strip = strip_field(first)
        strip = strip + pltpu.roll(jnp.where(strip_lane < BX * STRIP, spread, 0.0), BX * STRIP, 1)
        last_slot = 2
        if kind == 1:
            strip = strip + pltpu.roll(strip_field(8), 2 * BX * STRIP, 1)
            last_slot = 3
        last = jnp.where(strip_lane >= last_lanes, vx, 0.0)
        strip = strip + pltpu.roll(last, last_slot * BX * STRIP - last_lanes, 1)
        target[planes_end:x_end] = last_x_ref[kind * BY : kind * BY + BY]

        vx_before = None
        for x in range(BX):
            vx_t, vy_t, vz_t = (
                halo(from_up, from_down, (first + 1 + axis) * BX + x) for axis in range(3)
            )
            below_z = pltpu.roll(vz, (BZ - (x * STRIP + MARGIN - 1)) % BZ, 1) * cut_down
            last_y = last_y_ref[(kind * BX + x) * 8 : (kind * BX + x) * 8 + 8]
            y_before = jnp.where(
                tile_row == 0, pltpu.roll(last_y, 1, 0), pltpu.roll(vy_t, 1, 0)
            )
            z_before = jnp.where(lane[0:8] == 0, below_z[BY:EY], pltpu.roll(vz_t, 1, 1))
            spread = vx_t if x == 0 else vx_t - vx_before
            spread = (spread + (vy_t - y_before)) + (vz_t - z_before)
            vx_before = vx_t
            if kind == 0:
                fix_row = jnp.where(tile_row == x, vy_t[7:8], fix_row)
                moved = pltpu.roll(below_z[0:BY], FIX_LANE + x, 1)
                fix_lane = jnp.where(lane == FIX_LANE + x, moved, fix_lane)
            else:
                block = t_ref[x * BY : x * BY + BY]
                block = block - jnp.where(row == 0, vy_t[7:8], 0.0)
                block = block - jnp.where(lane == 0, below_z[0:BY], 0.0)
                target[x * BY : x * BY + BY] = block
            base = x_end + x * 8
            target[base : base + 8] = halo(from_up, from_down, first * BX + x)
            target[base + 32 : base + 40] = spread
            if kind == 1:
                target[base + 64 : base + 72] = halo(from_up, from_down, 8 * BX + x)
        target[tiles_end - 8 : tiles_end] = vx_before
        if kind == 0:
            target[tiles_end : tiles_end + BY] = strip[0:BY] + fix_lane
            target[tiles_end + BY : tiles_end + EY] = strip[BY:EY]
            target[WAVE_FIX : WAVE_FIX + 8] = fix_row
            target[WAVE_FIX + 8 : WAVE_FIX + 24] = jnp.zeros((16, BZ), F32)
        else:
            target[tiles_end : tiles_end + EY] = strip


def adjoint_join_kernel(ql_ref, adj_ref, even_ref, odd_ref):
    planes_end, x_end, tiles_end = ADJ_OWN
    for target, first in zip((even_ref, odd_ref), pair_planes()):
        base = copy_rows(target, 0, adj_ref, first * BY, 3 * BY)
        base = copy_rows(target, base, adj_ref, planes_end, BY)
        near = [x_end + (first + plane) * 8 for plane in range(3)]
        nearest = [x_end + 32 + first * 16 + plane * 8 for plane in range(2)]
        firsts = near + nearest + [start + 64 for start in near] + [tiles_end - 8]
        base = put_tiles(target, base, adj_ref, firsts)
        base = copy_rows(target, base, adj_ref, tiles_end, EY)
        copy_rows(target, base, ql_ref, 0, 2 * PLANES)


def join_kernel(wave_ref, late_ref, s_ref, even_ref, odd_ref):
    planes_end, x_end, tiles_end = WAVE_OWN
    row, lane = rows((BY, BZ)), lanes((BY, BZ))
    fix_lane = late_ref[tiles_end : tiles_end + BY]
    for x in range(BX):
        block = wave_ref[PLANES + x * BY : PLANES + x * BY + BY]
        fix_row = late_ref[WAVE_FIX + x : WAVE_FIX + x + 1]
        block = block - jnp.where(row == 0, fix_row, 0.0)
        block = block - jnp.where(lane == 0, pltpu.roll(fix_lane, BZ - FIX_LANE - x, 1), 0.0)
        s_ref[x * BY : x * BY + BY] = block
    for target, first in zip((even_ref, odd_ref), pair_planes()):
        base = copy_rows(target, 0, wave_ref, 0, PLANES)
        base = copy_rows(target, base, s_ref, first * BY, 3 * BY)
        base = copy_rows(target, base, late_ref, planes_end, BY)
        near = [x_end + (first + plane) * 8 for plane in range(3)]
        nearest = [x_end + 32 + first * 16 + plane * 8 for plane in range(2)]
        base = put_tiles(target, base, late_ref, near + nearest + [tiles_end - 8])
        copy_rows(target, base, late_ref, tiles_end, EY)


def split(values):
    high = values.astype(BF16)
    rest = values - high.astype(F32)
    middle = rest.astype(BF16)
    low = (rest - middle.astype(F32)).astype(BF16)
    return high, middle, low


def places(cells, sl):
    gx, gy, gz = (lax.axis_index(name) for name in ("gx", "gy", "gz"))
    cut = BZ * lax.axis_size("gz") // 2 - MARGIN
    cell_x = cells[0:1, sl] - (gx * BX - MARGIN)
    cell_y = cells[1:2, sl] - gy * BY
    cell_z = cells[2:3, sl]
    in_x = (cell_x >= 0) & (cell_x < EX)
    in_y = (cell_y >= -MARGIN) & (cell_y < BY + MARGIN)
    row = jnp.where(cell_y < 0, cell_y + EY, cell_y)
    flat = jnp.where(in_x & in_y, cell_x * EY + row, -1)
    row = jnp.where(in_y, row, -1)
    zz = cell_z - cut
    in_strip = in_x & (zz >= 0) & (zz < STRIP)
    strip_lane = jnp.where(in_strip, cell_x * STRIP + zz, -1)
    return flat, cell_z - gz * BZ, row, strip_lane


def hits(count, index):
    return rows((count, index.shape[1])) == index


def product(left, right):
    return lax.dot_general(
        left, right, (((1,), (1,)), ((), ())), preferred_element_type=F32
    )


def inject_points(cells, wave_ref, width, waves, planes, out_ref, strip_out_ref):
    count, low, total_rows = len(waves), planes[0] * EY, (planes[1] - planes[0]) * EY
    for start in range(0, cells.shape[1], width):
        sl = slice(start, start + width)
        flat, z, row, strip_lane = places(cells, sl)
        here = hits(total_rows, flat - low).astype(F32).astype(BF16)
        at_strip = hits(BZ, strip_lane).astype(F32).astype(BF16)
        at_z, at_row = hits(BZ, z), hits(EY, row)
        total = strip_total = None
        parts = [split(wave_ref[wave : wave + 1, sl]) for wave in waves]
        for part in range(3):
            amounts = [parts[wave][part].astype(F32) for wave in range(count)]
            right = jnp.concatenate([jnp.where(at_z, a, 0.0) for a in amounts], 0).astype(BF16)
            left = jnp.concatenate([jnp.where(at_row, a, 0.0) for a in amounts], 0).astype(BF16)
            term, strip_term = product(here, right), product(left, at_strip)
            total = term if part == 0 else total + term
            strip_total = strip_term if part == 0 else strip_total + strip_term
        for wave in range(count):
            value = total[:, wave * BZ : wave * BZ + BZ]
            strip_value = strip_total[wave * EY : wave * EY + EY]
            if start > 0:
                value = value + out_ref[wave]
                strip_value = strip_value + strip_out_ref[wave]
            out_ref[wave] = value
            strip_out_ref[wave] = strip_value


LATE_PLANES, EARLY_PLANES, SOURCE_PLANES = (0, EX), (2, EX - 2), (1, EX - 1)


def late_kernel(receivers, receiver_wave, r_ref, rs_ref):
    inject_points(receivers, receiver_wave, 256, (2, 3), LATE_PLANES, r_ref, rs_ref)


def early_kernel(receivers, receiver_wave, _, r_ref, rs_ref):
    inject_points(receivers, receiver_wave, 256, (0, 1), EARLY_PLANES, r_ref, rs_ref)


def source_kernel(sources, source_wave, _, s_ref, ss_ref):
    width = sources.shape[1]
    inject_points(sources, source_wave, width, (0, 1, 2), SOURCE_PLANES, s_ref, ss_ref)


def strip_of(packed, block, slot):
    lane = lanes(packed.shape)
    width = BX * STRIP
    shift = (block * width - slot * width) % BZ
    moved = pltpu.roll(packed, shift, 1) if shift else packed
    return jnp.where((lane >= block * width) & (lane < (block + 1) * width), moved, 0.0)


def y_up(v):
    return pltpu.roll(v, EY - 1, 0)


def y_down(v):
    return pltpu.roll(v, 1, 0)


def z_up(v, edge):
    return jnp.where(lanes(v.shape) == BZ - 1, edge, pltpu.roll(v, BZ - 1, 1))


def z_down(v, edge):
    return jnp.where(lanes(v.shape) == 0, edge, pltpu.roll(v, 1, 1))


def cut_edges(values, flux_z, cut_up, cut_down):
    place = lax.rem(lanes(values.shape), STRIP)
    above = jnp.where(place == MARGIN, values * cut_up, 0.0)
    below = jnp.where(place == MARGIN - 1, flux_z * cut_down, 0.0)
    return pltpu.roll(above, BZ - 2, 1) + below


def plane_edge(edges, x):
    return pltpu.roll(edges, (BZ - (x * STRIP + MARGIN - 1)) % BZ, 1)


def strip_flux(values, buoyancy):
    flux_x = buoyancy * (pltpu.roll(values, BZ - STRIP, 1) - values)
    flux_y = buoyancy * (y_up(values) - values)
    flux_z = buoyancy * (pltpu.roll(values, BZ - 1, 1) - values)
    spread = (flux_x - pltpu.roll(flux_x, STRIP, 1)) + (flux_y - y_down(flux_y))
    return flux_z, spread + (flux_z - pltpu.roll(flux_z, 1, 1))


def cut_flags():
    gz, half = lax.axis_index("gz"), lax.axis_size("gz") // 2
    return jnp.where(gz == half - 1, 1.0, 0.0), jnp.where(gz == half, 1.0, 0.0)


def sides():
    gx = lax.axis_index("gx")
    low = jnp.where(gx > 0, 1.0, 0.0)
    high = jnp.where(gx < lax.axis_size("gx") - 1, 1.0, 0.0)
    return low, high, lax.rem(gx, 2) == 0


def from_side(messages, first, count, block, side):
    even, odd = (message[first : first + count] for message in messages)
    low, high, even_above = side
    if block == 0:
        return jnp.where(even_above, odd, even) * low
    return jnp.where(even_above, even, odd) * high


def side_tile(messages, base, place, block, side):
    if not halved():
        return from_side(messages, base + place * 8, 8, block, side)
    tile = from_side(messages, base + place // 2 * 8, 8, block, side)
    upper = lax.axis_index("gy") == 0
    turned = half_turn(tile)
    tile = jnp.where(upper, turned, tile) if place % 2 else jnp.where(upper, tile, turned)
    return jnp.where((rows((8, BZ)) < MARGIN) == upper, tile, 0.0)


def side_place(wanted, plane, block):
    planes = range(BX - wanted, BX) if block == 0 else range(wanted)
    return planes.index(plane) if plane in planes else None


def widened(own, own_tiles, x, layout, side):
    block, plane = divmod(x, BX)
    if block == 1:
        main = own[0][own[1] + plane * BY : own[1] + plane * BY + BY]
        tile = own_tiles[0][own_tiles[1] + plane * 8 : own_tiles[1] + plane * 8 + 8]
        return jnp.concatenate([main, tile], 0)
    (messages, base, wanted), (tile_messages, tile_base, tile_place, tile_wanted) = layout
    main, tile = jnp.zeros((BY, BZ), F32), jnp.zeros((8, BZ), F32)
    place = side_place(wanted, plane, block)
    if place is not None:
        main = from_side(messages, base + place * BY, BY, block, side)
    place = side_place(tile_wanted, plane, block)
    if place is not None:
        tile = side_tile(tile_messages, tile_base, tile_place + place, block, side)
    return jnp.concatenate([main, tile], 0)


def less_plane_below(value, x, own_ref, own_rows, messages, side_layout, side):
    if x == BX:
        (planes_end, x_end), count = side_layout
        main = from_side(messages, planes_end, BY, 0, side)
        tile = side_tile(messages, x_end, count - 1, 0, side)
    elif x == 2 * BX:
        planes_end, _, tiles_end = own_rows
        high = side[1]
        main = own_ref[planes_end : planes_end + BY] * high
        tile = own_ref[tiles_end - 8 : tiles_end] * high
    else:
        return value
    return value - jnp.concatenate([main, tile], 0)


def strip_below(own, messages, first, slot, side):
    lane = lanes(own.shape)
    width = BX * STRIP
    low = from_side(messages, first, EY, 0, side)
    low = pltpu.roll(low, (width - slot * width) % BZ, 1)
    own = pltpu.roll(own * side[1], (2 * width - slot * width) % BZ, 1)
    in_own = (lane >= width) & (lane < width + STRIP)
    in_high = (lane >= 2 * width) & (lane < 2 * width + STRIP)
    return jnp.where(in_own, low, jnp.where(in_high, own, 0.0))


def whole_strip(own, messages, first, slot, side):
    low = from_side(messages, first, EY, 0, side)
    high = from_side(messages, first, EY, 2, side)
    return strip_of(low, 0, slot) + strip_of(own, 1, slot) + strip_of(high, 2, slot)


def adjoint_kernel(
    ql_ref, late_ref, even, odd, adj_hbm, ra_ref, rsa_ref, rb_ref, rsb_ref,
    table_ref,
    out_ref, hist_ref, coef_ref, coef_strip_ref,
    q_ref, t_ref, u_ref, scale_ref, edge_ref, flux_ref, w_sem,
):
    w_copy = pltpu.make_async_copy(adj_hbm.at[pl.ds(1, 3)], out_ref.at[pl.ds(1, 3)], w_sem)
    w_copy.start()
    cut_up, cut_down = cut_flags()
    side = sides()
    messages = (even, odd)
    r_refs = ((ra_ref, 0), (ra_ref, 1), (rb_ref, 0), (rb_ref, 1))
    rs_refs = ((rsa_ref, 0), (rsa_ref, 1), (rsb_ref, 0), (rsb_ref, 1))
    tiles, own_tiles = ADJ_SIDE[1], ADJ_OWN[1]
    side_strip = tiles + tile_rows(ADJ_TILES)
    raws = side_strip + EY

    def initial(index, x):
        own = ((ql_ref, 0), (late_ref, 0), (ql_ref, PLANES))[index]
        layout = (
            ((messages, raws, 4), (messages, tiles, 0, 3)),
            ((messages, 0, 3), (messages, tiles, 3, 2)),
            ((messages, raws + PLANES, 4), (messages, tiles, 5, 3)),
        )[index]
        value = widened(own, (late_ref, own_tiles + 32 * index), x, layout, side)
        if index == 1:
            value = less_plane_below(
                value, x, late_ref, ADJ_OWN, messages, (ADJ_SIDE, ADJ_TILES), side
            )
        return value

    for x in range(EX):
        stiff, buoy, damp = coefficients(initial(2, x), table_ref)
        coef_ref[0, x], coef_ref[1, x], coef_ref[2, x] = stiff, buoy, damp
        scale_ref[x] = stiff * damp
    own_strip = late_ref[ADJ_OWN[2] : ADJ_OWN[2] + EY]
    q_s, t_s, label_s = (
        whole_strip(own_strip, messages, side_strip, slot, side) for slot in range(3)
    )
    t_s = t_s - strip_below(own_strip, messages, side_strip, 3, side)
    stiff_s, buoy_s, damp_s = coefficients(label_s, table_ref)
    scale_s = stiff_s * damp_s
    coef_strip_ref[0], coef_strip_ref[1], coef_strip_ref[2] = stiff_s, buoy_s, damp_s
    w_copy.wait()

    for step in range(1, STEPS + 1):
        rs_ref, place = rs_refs[STEPS - step]
        q_s = q_s + rs_ref[place]
        u_s = scale_s * q_s
        flux_s, spread = strip_flux(u_s, buoy_s)
        t_s = t_s + spread
        q_s = damp_s * q_s + t_s
        edges = cut_edges(u_s, flux_s, cut_up, cut_down)
        for x in range(step, EX - step):
            edge_ref[step - 1, x] = plane_edge(edges, x)

    for step in range(1, STEPS + 1):
        k = STEPS - step
        r_ref, place = r_refs[k]
        r_first = (EARLY_PLANES if k < 2 else LATE_PLANES)[0]

        for x in range(step - 1, EX - step + 1):
            q = (initial(0, x) if step == 1 else q_ref[x]) + r_ref[place, x - r_first]
            q_ref[x] = q
            u_ref[x] = scale_ref[x] * q

        for x in range(step - 1, EX - step):
            u, buoyancy = u_ref[x], coef_ref[1, x]
            slopes = [u_ref[x + 1] - u]
            if x >= step:
                slopes += [y_up(u) - u, z_up(u, edge_ref[step - 1, x]) - u]
            for axis, slope in enumerate(slopes):
                flux_ref[axis, x] = buoyancy * slope
            if BX <= x < 2 * BX:
                for axis, slope in enumerate(slopes):
                    w = out_ref[1 + axis, x - BX] + slope[0:BY]
                    out_ref[1 + axis, x - BX] = w
                    hist_ref[k, 1 + axis, x - BX] = w

        for x in range(step, EX - step):
            flux_y, flux_z = flux_ref[1, x], flux_ref[2, x]
            spread = (flux_ref[0, x] - flux_ref[0, x - 1]) + (flux_y - y_down(flux_y))
            spread = spread + (flux_z - z_down(flux_z, edge_ref[step - 1, x]))
            damped = coef_ref[2, x] * q_ref[x]
            t = (initial(1, x) if step == 1 else t_ref[x]) + spread
            if BX <= x < 2 * BX:
                hist_ref[k, 0, x - BX] = damped[0:BY]
            if step < STEPS:
                t_ref[x] = t
                q_ref[x] = damped + t
            else:
                out_ref[0, x - BX] = (damped + t)[0:BY]


def forward_kernel(
    wave_ref, own_s_ref, late_ref, even, odd, coef_ref, coef_strip_ref, s_ref, ss_ref, hist_ref,
    adjoint_ref, grad_hbm, adjoint_hbm,
    p_ref, spread_ref, edge_ref, flux_ref, grad_ref, sems,
):
    copies = [pltpu.make_async_copy(adjoint_ref, adjoint_hbm, sems.at[0])]
    copies[0].start()

    def send(index, kind, first, count):
        planes = pl.ds(first, count)
        copy = pltpu.make_async_copy(
            grad_ref.at[kind, planes], grad_hbm.at[kind, planes], sems.at[index]
        )
        copy.start()
        copies.append(copy)

    cut_up, cut_down = cut_flags()
    side = sides()
    messages = (even, odd)
    tiles, own_tiles = WAVE_SIDE[1], WAVE_OWN[1]
    side_strip = tiles + tile_rows(WAVE_TILES)

    def initial(index, x):
        layout = (
            ((messages, 0, 4), (messages, tiles, 0, 3)),
            ((messages, PLANES, 3), (messages, tiles, 3, 2)),
        )[index]
        own = ((wave_ref, 0), (own_s_ref, 0))[index]
        value = widened(own, (late_ref, own_tiles + 32 * index), x, layout, side)
        if index == 1:
            value = less_plane_below(
                value, x, late_ref, WAVE_OWN, messages, (WAVE_SIDE, WAVE_TILES), side
            )
        return value

    own_strip = late_ref[WAVE_OWN[2] : WAVE_OWN[2] + EY]
    p_s, s_s = (
        whole_strip(own_strip, messages, side_strip, slot, side) for slot in range(2)
    )
    s_s = s_s - strip_below(own_strip, messages, side_strip, 2, side)
    stiff_s, buoy_s, damp_s = coef_strip_ref[0], coef_strip_ref[1], coef_strip_ref[2]

    for step in range(1, STEPS + 1):
        flux_s, spread = strip_flux(p_s, buoy_s)
        edges = cut_edges(p_s, flux_s, cut_up, cut_down)
        if step < STEPS:
            s_s = s_s - spread
            p_s = damp_s * (p_s - stiff_s * s_s) + ss_ref[step - 1]
        for x in range(step, EX - step):
            edge_ref[step - 1, x] = plane_edge(edges, x)
    for x in range(EX):
        p_ref[x] = initial(0, x)

    for step in range(1, STEPS + 1):
        k = step - 1
        for x in range(step - 1, EX - step):
            p, buoyancy = p_ref[x], coef_ref[1, x]
            slopes = [p_ref[x + 1] - p]
            if x >= step:
                slopes += [y_up(p) - p, z_up(p, edge_ref[step - 1, x]) - p]
            for axis, slope in enumerate(slopes):
                flux_ref[axis, x] = buoyancy * slope
            if BX <= x < 2 * BX:
                place = x - BX
                term = hist_ref[k, 1, place] * slopes[0][0:BY]
                term = term + hist_ref[k, 2, place] * slopes[1][0:BY]
                term = term + hist_ref[k, 3, place] * slopes[2][0:BY]
                grad_ref[1, place] = -term if k == 0 else grad_ref[1, place] - term
        if step == STEPS:
            send(1, 1, 0, BX)

        for x in range(step, EX - step):
            flux_y, flux_z = flux_ref[1, x], flux_ref[2, x]
            spread = (flux_ref[0, x] - flux_ref[0, x - 1]) + (flux_y - y_down(flux_y))
            spread = spread + (flux_z - z_down(flux_z, edge_ref[step - 1, x]))
            spread = (initial(1, x) if step == 1 else spread_ref[x]) - spread
            if step < STEPS:
                spread_ref[x] = spread
                p_ref[x] = (
                    coef_ref[2, x] * (p_ref[x] - coef_ref[0, x] * spread)
                    + s_ref[k, x - SOURCE_PLANES[0]]
                )
            if BX <= x < 2 * BX:
                place = x - BX
                term = hist_ref[k, 0, place] * spread[0:BY]
                grad_ref[0, place] = -term if k == 0 else grad_ref[0, place] - term
                if step == STEPS:
                    send(2 + place, 0, place, 1)
    for copy in copies:
        copy.wait()


def shape(*dims):
    return jax.ShapeDtypeStruct(dims, F32)


def call(kernel, outs, operands, scratch, places, micros=0.1, out_place="v"):
    spaces = {"h": pltpu.HBM, "a": pl.ANY, "v": pltpu.VMEM}
    operands = [
        pltpu.with_memory_space_constraint(operand, pltpu.HBM) if place == "h" else operand
        for operand, place in zip(operands, places)
    ]
    return pl.pallas_call(
        kernel,
        out_shape=outs,
        in_specs=[pl.BlockSpec(memory_space=spaces[place]) for place in places],
        out_specs=[pl.BlockSpec(memory_space=spaces[out_place])] * len(outs),
        scratch_shapes=scratch,
        compiler_params=pltpu.CompilerParams(vmem_limit_bytes=VMEM_LIMIT),
        cost_estimate=pl.CostEstimate(
            flops=0, bytes_accessed=int(3.69e6 * micros), transcendentals=0
        ),
    )(*operands)


def from_sides(sends, axes):
    count = lax.axis_size("gy")

    def route(offset):
        pairs = []
        for target in range(count):
            source = target + offset
            if 0 <= source < count:
                if "gz" in axes:
                    pairs += [(2 * source + z, 2 * target + 1 - z) for z in range(2)]
                else:
                    pairs.append((source, target))
        return pairs

    if count == 2:
        both = lax.ppermute(sends[0], axes, route(1) + route(-1))
        return both, both
    upward, downward = sends
    return lax.ppermute(downward, axes, route(1)), lax.ppermute(upward, axes, route(-1))


def rotated(array, axis, offset):
    count = lax.axis_size(axis)
    return lax.ppermute(array, axis, [((i + offset) % count, i) for i in range(count)])


def paired(array, odd):
    count = lax.axis_size("gx")
    pairs = []
    for i in range(count):
        partner = ((i - 1) ^ 1) + 1 if odd else i ^ 1
        pairs.append((partner if 0 <= partner < count else i, i))
    return lax.ppermute(array, "gx", pairs)


def local(
    stored, adjoint_end, labels, tissue, source_cells, source_wave, receiver_cells, receiver_wave
):
    assert lax.axis_size("gz") == 2 and labels.shape == (BX, BY, BZ) and tissue.shape[1] == 8
    half = lax.axis_size("gx") // 2
    arguments = [
        stored, adjoint_end, labels, tissue,
        receiver_cells.T, receiver_wave, source_cells.T, source_wave,
    ]
    ways = 1 if lax.axis_size("gy") == 2 else 2
    wave, ql, t, last_x, last_y, strips, table, receivers, receiver_wave, sources, source_wave, *sends = call(
        load_kernel,
        [
            shape(2 * PLANES + 32, BZ),
            shape(2 * PLANES, BZ),
            shape(PLANES, BZ),
            shape(2 * BY, BZ),
            shape(2 * BX * 8, BZ),
            shape(3 * BY, BZ),
            shape(24, BZ),
        ]
        + [jax.ShapeDtypeStruct(array.shape, array.dtype) for array in arguments[4:]]
        + [shape(20 * 8, BZ)] * ways
        + [shape(2 * 8, BZ)] * ways,
        arguments,
        [
            pltpu.VMEM(stored.shape, F32),
            pltpu.VMEM(adjoint_end.shape, F32),
            pltpu.VMEM(labels.shape, jnp.int32),
            pltpu.SMEM(tissue.shape, F32),
            pltpu.SemaphoreType.DMA,
        ],
        "hhhhhhhh",
        1.4,
    )
    from_up, from_down = from_sides(sends[:ways], "gy")
    other = rotated(strips, "gz", 1)
    corner_up, corner_down = from_sides(sends[ways:], ("gy", "gz"))
    wave = rotated(wave, "gx", half)
    rb, rsb = call(
        late_kernel,
        [shape(2, EX * EY, BZ), shape(2, EY, BZ)],
        [receivers, receiver_wave],
        [],
        "vv",
        1.2,
    )
    early_planes, source_planes = (last - first for first, last in (EARLY_PLANES, SOURCE_PLANES))
    late, adj_late = call(
        merge_kernel,
        [shape(WAVE_FIX + 24, BZ), shape(ADJ_OWN[2] + EY, BZ)],
        [from_up, from_down, corner_up, corner_down, strips, other, t, last_x, last_y, rsb],
        [],
        "vvvvvvvvva",
    )
    late = rotated(late, "gx", half)
    ra, rsa = call(
        early_kernel,
        [shape(2, early_planes * EY, BZ), shape(2, EY, BZ)],
        [receivers, receiver_wave, adj_late],
        [],
        "vva",
        1.0,
    )
    ra, rb = ra.reshape(2, early_planes, EY, BZ), rb.reshape(2, EX, EY, BZ)
    even, odd = call(
        adjoint_join_kernel,
        [shape(ADJ_SIDE[1] + tile_rows(ADJ_TILES) + EY + 2 * PLANES, BZ)] * 2,
        [ql, adj_late],
        [],
        "vv",
    )
    even, odd = paired(even, False), paired(odd, True)
    src, src_strip = call(
        source_kernel,
        [shape(STEPS - 1, source_planes * EY, BZ), shape(STEPS - 1, EY, BZ)],
        [sources, source_wave, adj_late],
        [],
        "vva",
        0.5,
    )
    src = src.reshape(STEPS - 1, source_planes, EY, BZ)
    own_s, wave_even, wave_odd = call(
        join_kernel,
        [shape(PLANES, BZ)] + [shape(WAVE_SIDE[1] + tile_rows(WAVE_TILES) + EY, BZ)] * 2,
        [wave, late],
        [],
        "vv",
    )
    wave_even, wave_odd = paired(wave_even, False), paired(wave_odd, True)
    adjoint_out, hist, coef, coef_strip = call(
        adjoint_kernel,
        [
            shape(4, BX, BY, BZ),
            shape(STEPS, 4, BX, BY, BZ),
            shape(3, EX, EY, BZ),
            shape(3, EY, BZ),
        ],
        [ql, adj_late, even, odd, adjoint_end, ra, rsa, rb, rsb, table],
        [pltpu.VMEM((EX, EY, BZ), F32)] * 4
        + [
            pltpu.VMEM((STEPS, EX, EY, BZ), F32),
            pltpu.VMEM((3, EX, EY, BZ), F32),
            pltpu.SemaphoreType.DMA,
        ],
        "vvvvhvvvvv",
        3.9,
    )
    return call(
        forward_kernel,
        [shape(2, BX, BY, BZ), shape(4, BX, BY, BZ)],
        [
            wave, own_s, late, wave_even, wave_odd, coef, coef_strip, src, src_strip, hist,
            adjoint_out,
        ],
        [pltpu.VMEM((EX, EY, BZ), F32)] * 2
        + [
            pltpu.VMEM((STEPS, EX, EY, BZ), F32),
            pltpu.VMEM((3, EX, EY, BZ), F32),
            pltpu.VMEM((2, BX, BY, BZ), F32),
            pltpu.SemaphoreType.DMA((2 + BX,)),
        ],
        "vvvvvvvvvvv",
        2.5,
        "a",
    )


def solution(mesh):
    return jax.shard_map(
        local,
        mesh=mesh,
        in_specs=(
            P("shot", "gx", "gy", "gz"),
            P("shot", "gx", "gy", "gz"),
            P("gx", "gy", "gz"),
            P(),
            P("shot", None),
            P(None, "shot"),
            P(),
            P(None, "shot"),
        ),
        out_specs=(P("shot", "gx", "gy", "gz"), P("shot", "gx", "gy", "gz")),
        check_vma=False,
    )
```

```python
import jax
import jax.numpy as jnp
from jax import lax
from jax.experimental import pallas as pl
from jax.experimental.pallas import tpu as pltpu
from jax.sharding import PartitionSpec as P

STEPS = 4
MARGIN = 4
BX, BY, BZ = 4, 32, 128
EX, EY = BX + 2 * MARGIN, BY + 2 * MARGIN
STRIP = 2 * MARGIN
F32 = jnp.float32
BF16 = jnp.bfloat16
VMEM_LIMIT = 16 * 1024 * 1024
PLANES = BX * BY
WAVE_OWN = (0, BY, BY + 9 * 8)
WAVE_FIX = WAVE_OWN[2] + EY
FIX_LANE = 3 * BX * STRIP
ADJ_OWN = (PLANES, PLANES + BY, PLANES + BY + 13 * 8)
WAVE_SIDE = (PLANES + 3 * BY, PLANES + 4 * BY)
ADJ_SIDE = (3 * BY, 4 * BY)
WAVE_TILES, ADJ_TILES = 6, 9


def lanes(shape):
    return lax.broadcasted_iota(jnp.int32, shape, len(shape) - 1)


def rows(shape):
    return lax.broadcasted_iota(jnp.int32, shape, len(shape) - 2)


def run(copies):
    for copy in copies:
        copy.start()
    for copy in copies:
        copy.wait()


def coefficients(labels, table_ref):
    result = [jnp.zeros(labels.shape, F32) for _ in range(3)]
    for index in range(8):
        picked = labels == float(index + 1)
        for kind in range(3):
            row = kind * 8 + index
            result[kind] = jnp.where(picked, table_ref[row : row + 1], result[kind])
    return result


def buoyancy_of(labels, table_ref):
    result = jnp.zeros(labels.shape, F32)
    for index in range(8):
        result = jnp.where(labels == float(index + 1), table_ref[8 + index : 9 + index], result)
    return result


def half_turn(tile):
    return pltpu.roll(tile, MARGIN, 0)


def load_kernel(
    stored_hbm, adj_hbm, lab_hbm, tissue_hbm, rc_hbm, rw_hbm, sc_hbm, sw_hbm,
    wave_ref, ql_ref, t_ref, last_x_ref, last_y_ref, strip_ref, table_ref,
    rc_ref, rw_ref, sc_ref, sw_ref, *rest,
):
    *sends, stored, adj, lab, tissue, sem = rest
    run([
        pltpu.make_async_copy(source, target, sem)
        for source, target in (
            (stored_hbm, stored), (adj_hbm, adj), (lab_hbm, lab), (tissue_hbm, tissue),
            (rc_hbm, rc_ref), (rw_hbm, rw_ref), (sc_hbm, sc_ref), (sw_hbm, sw_ref),
        )
    ])
    for index in range(tissue.shape[1]):
        speed = jnp.full((1, BZ), tissue[0, index], F32)
        density = jnp.full((1, BZ), tissue[1, index], F32)
        table_ref[index : index + 1] = density * speed
        table_ref[8 + index : 9 + index] = speed / density
        table_ref[16 + index : 17 + index] = 1.0 - jnp.full((1, BZ), tissue[2, index], F32)
    gy, gz = lax.axis_index("gy"), lax.axis_index("gz")
    lane = lanes((BY, BZ))
    row = rows((BY, BZ))
    tile_row = rows((8, BZ))
    strips = [jnp.zeros((BY, BZ), F32) for _ in range(3)]
    tiles = [None] * 39
    previous = [None, None]

    def edge_tile(block):
        return jnp.where(tile_row < MARGIN, block[0:8], block[BY - 8 : BY])

    for x in range(BX):
        labels = lab[x].astype(F32) + 1.0
        buoyancy = buoyancy_of(labels, table_ref)
        plane = slice(x * BY, x * BY + BY)
        fields = [stored[index, x] for index in range(4)] + [adj[0, x]]
        fields += [buoyancy * adj[index, x] for index in range(1, 4)] + [labels]
        wave_ref[plane] = fields[0]
        ql_ref[plane] = fields[4]
        ql_ref[PLANES + x * BY : PLANES + x * BY + BY] = labels
        for index, block in enumerate(fields):
            tiles[index * BX + x] = edge_tile(block)
            group, slot = divmod(index, 4)
            base = slot * BX * STRIP + x * STRIP
            rolled = pltpu.roll(block, base + MARGIN, 1)
            first = base + MARGIN * gz
            strips[group] = jnp.where(
                (lane >= first) & (lane < first + MARGIN), rolled, strips[group]
            )
        for kind, (target, base) in enumerate(((wave_ref, PLANES), (t_ref, 0))):
            vx, vy, vz = fields[4 * kind + 1 : 4 * kind + 4]
            spread = vx if x == 0 else vx - previous[kind]
            spread = spread + (vy - jnp.where(row == 0, 0.0, pltpu.roll(vy, 1, 0)))
            spread = spread + (vz - jnp.where(lane == 0, 0.0, pltpu.roll(vz, 1, 1)))
            target[base + x * BY : base + x * BY + BY] = spread
            previous[kind] = vx
            index = (kind * BX + x) * 8
            last_y_ref[index : index + 8] = vy[BY - 8 : BY]
    for kind in range(2):
        last_x_ref[kind * BY : kind * BY + BY] = previous[kind]
    wave_ref[2 * PLANES : 2 * PLANES + BY] = jnp.zeros((BY, BZ), F32)
    for group in range(3):
        strip_ref[group * BY : group * BY + BY] = strips[group]
        tiles[9 * BX + group] = edge_tile(strips[group])

    def joined(first, second):
        second = first if second is None else second
        upward = jnp.where(tile_row < MARGIN, half_turn(first), second)
        downward = jnp.where(tile_row < MARGIN, first, half_turn(second))
        if len(sends) == 2:
            return (jnp.where(gy == 0, upward, downward),)
        return upward, downward

    tiles.append(None)
    half = len(sends) // 2
    for place in range(20):
        for target, tile in zip(sends[:half], joined(tiles[2 * place], tiles[2 * place + 1])):
            target[place * 8 : place * 8 + 8] = tile
    for place in range(2):
        first = tiles[9 * BX + 2 * place]
        for target, tile in zip(sends[half:], joined(first, tiles[9 * BX + 2 * place + 1])):
            target[place * 8 : place * 8 + 8] = tile


def copy_rows(target, base, source, first, count):
    target[base : base + count] = source[pl.ds(pl.multiple_of(first, 8), count)]
    return base + count


def halved():
    return lax.axis_size("gy") == 2


def tile_rows(count):
    return (count + 1) // 2 * 8 if halved() else count * 8


def put_tiles(target, base, source, firsts):
    tiles = [source[pl.ds(pl.multiple_of(first, 8), 8)] for first in firsts]
    if halved():
        upper = lax.axis_index("gy") == 0
        row = rows((8, BZ))
        pairs = [(tiles[i], tiles[min(i + 1, len(tiles) - 1)]) for i in range(0, len(tiles), 2)]
        tiles = [
            jnp.where(
                row < MARGIN,
                jnp.where(upper, first, half_turn(first)),
                jnp.where(upper, half_turn(second), second),
            )
            for first, second in pairs
        ]
    for place, tile in enumerate(tiles):
        target[base + place * 8 : base + place * 8 + 8] = tile
    return base + 8 * len(tiles)


def pair_planes():
    parity = lax.rem(lax.axis_index("gx"), 2)
    return 1 - parity, parity


def merge_kernel(
    from_up, from_down, corner_up, corner_down, strip_ref, other_ref,
    t_ref, last_x_ref, last_y_ref, _,
    wave_ref, adj_ref,
):
    gy = lax.axis_index("gy")
    tile_row = rows((8, BZ))
    row, lane = rows((BY, BZ)), lanes((BY, BZ))
    take_up = (tile_row < MARGIN) & (gy < lax.axis_size("gy") - 1)
    take_down = (tile_row >= MARGIN) & (gy > 0)
    _, cut_down = cut_flags()

    def halo(up, down, index):
        place, second = divmod(index, 2)
        sl = slice(place * 8, place * 8 + 8)
        above = half_turn(up[sl]) if second else up[sl]
        below = down[sl] if second else half_turn(down[sl])
        return jnp.where(take_up, above, jnp.where(take_down, below, 0.0))

    wide = []
    for group in range(3):
        sl = slice(group * BY, group * BY + BY)
        tile = halo(from_up, from_down, 9 * BX + group) + halo(corner_up, corner_down, group)
        wide.append(jnp.concatenate([strip_ref[sl] + other_ref[sl], tile], 0))
    strip_lane = lanes((EY, BZ))

    def strip_field(index):
        group, slot = divmod(index, 4)
        moved = pltpu.roll(wide[group], (BZ - slot * BX * STRIP) % BZ, 1) if slot else wide[group]
        return jnp.where(strip_lane < BX * STRIP, moved, 0.0)

    last_lanes = (BX - 1) * STRIP
    fix_row = jnp.zeros((8, BZ), F32)
    fix_lane = jnp.zeros((BY, BZ), F32)
    for kind, target in enumerate((wave_ref, adj_ref)):
        first = 4 * kind
        planes_end, x_end, tiles_end = (WAVE_OWN, ADJ_OWN)[kind]
        vx, vy, vz = (strip_field(first + 1 + axis) for axis in range(3))
        spread = vx - jnp.where(strip_lane < STRIP, 0.0, pltpu.roll(vx, STRIP, 1))
        spread = (spread + (vy - y_down(vy))) + (vz - pltpu.roll(vz, 1, 1))
        strip = strip_field(first)
        strip = strip + pltpu.roll(jnp.where(strip_lane < BX * STRIP, spread, 0.0), BX * STRIP, 1)
        last_slot = 2
        if kind == 1:
            strip = strip + pltpu.roll(strip_field(8), 2 * BX * STRIP, 1)
            last_slot = 3
        last = jnp.where(strip_lane >= last_lanes, vx, 0.0)
        strip = strip + pltpu.roll(last, last_slot * BX * STRIP - last_lanes, 1)
        target[planes_end:x_end] = last_x_ref[kind * BY : kind * BY + BY]

        vx_before = None
        for x in range(BX):
            vx_t, vy_t, vz_t = (
                halo(from_up, from_down, (first + 1 + axis) * BX + x) for axis in range(3)
            )
            below_z = pltpu.roll(vz, (BZ - (x * STRIP + MARGIN - 1)) % BZ, 1) * cut_down
            last_y = last_y_ref[(kind * BX + x) * 8 : (kind * BX + x) * 8 + 8]
            y_before = jnp.where(
                tile_row == 0, pltpu.roll(last_y, 1, 0), pltpu.roll(vy_t, 1, 0)
            )
            z_before = jnp.where(lane[0:8] == 0, below_z[BY:EY], pltpu.roll(vz_t, 1, 1))
            spread = vx_t if x == 0 else vx_t - vx_before
            spread = (spread + (vy_t - y_before)) + (vz_t - z_before)
            vx_before = vx_t
            if kind == 0:
                fix_row = jnp.where(tile_row == x, vy_t[7:8], fix_row)
                moved = pltpu.roll(below_z[0:BY], FIX_LANE + x, 1)
                fix_lane = jnp.where(lane == FIX_LANE + x, moved, fix_lane)
            else:
                block = t_ref[x * BY : x * BY + BY]
                block = block - jnp.where(row == 0, vy_t[7:8], 0.0)
                block = block - jnp.where(lane == 0, below_z[0:BY], 0.0)
                target[x * BY : x * BY + BY] = block
            base = x_end + x * 8
            target[base : base + 8] = halo(from_up, from_down, first * BX + x)
            target[base + 32 : base + 40] = spread
            if kind == 1:
                target[base + 64 : base + 72] = halo(from_up, from_down, 8 * BX + x)
        target[tiles_end - 8 : tiles_end] = vx_before
        if kind == 0:
            target[tiles_end : tiles_end + BY] = strip[0:BY] + fix_lane
            target[tiles_end + BY : tiles_end + EY] = strip[BY:EY]
            target[WAVE_FIX : WAVE_FIX + 8] = fix_row
            target[WAVE_FIX + 8 : WAVE_FIX + 24] = jnp.zeros((16, BZ), F32)
        else:
            target[tiles_end : tiles_end + EY] = strip


def adjoint_join_kernel(ql_ref, adj_ref, even_ref, odd_ref):
    planes_end, x_end, tiles_end = ADJ_OWN
    for target, first in zip((even_ref, odd_ref), pair_planes()):
        base = copy_rows(target, 0, adj_ref, first * BY, 3 * BY)
        base = copy_rows(target, base, adj_ref, planes_end, BY)
        near = [x_end + (first + plane) * 8 for plane in range(3)]
        nearest = [x_end + 32 + first * 16 + plane * 8 for plane in range(2)]
        firsts = near + nearest + [start + 64 for start in near] + [tiles_end - 8]
        base = put_tiles(target, base, adj_ref, firsts)
        base = copy_rows(target, base, adj_ref, tiles_end, EY)
        copy_rows(target, base, ql_ref, 0, 2 * PLANES)


def join_kernel(wave_ref, late_ref, s_ref, even_ref, odd_ref):
    planes_end, x_end, tiles_end = WAVE_OWN
    row, lane = rows((BY, BZ)), lanes((BY, BZ))
    fix_lane = late_ref[tiles_end : tiles_end + BY]
    for x in range(BX):
        block = wave_ref[PLANES + x * BY : PLANES + x * BY + BY]
        fix_row = late_ref[WAVE_FIX + x : WAVE_FIX + x + 1]
        block = block - jnp.where(row == 0, fix_row, 0.0)
        block = block - jnp.where(lane == 0, pltpu.roll(fix_lane, BZ - FIX_LANE - x, 1), 0.0)
        s_ref[x * BY : x * BY + BY] = block
    for target, first in zip((even_ref, odd_ref), pair_planes()):
        base = copy_rows(target, 0, wave_ref, 0, PLANES)
        base = copy_rows(target, base, s_ref, first * BY, 3 * BY)
        base = copy_rows(target, base, late_ref, planes_end, BY)
        near = [x_end + (first + plane) * 8 for plane in range(3)]
        nearest = [x_end + 32 + first * 16 + plane * 8 for plane in range(2)]
        base = put_tiles(target, base, late_ref, near + nearest + [tiles_end - 8])
        copy_rows(target, base, late_ref, tiles_end, EY)


def split(values):
    high = values.astype(BF16)
    rest = values - high.astype(F32)
    middle = rest.astype(BF16)
    low = (rest - middle.astype(F32)).astype(BF16)
    return high, middle, low


def places(cells, sl):
    gx, gy, gz = (lax.axis_index(name) for name in ("gx", "gy", "gz"))
    cut = BZ * lax.axis_size("gz") // 2 - MARGIN
    cell_x = cells[0:1, sl] - (gx * BX - MARGIN)
    cell_y = cells[1:2, sl] - gy * BY
    cell_z = cells[2:3, sl]
    in_x = (cell_x >= 0) & (cell_x < EX)
    in_y = (cell_y >= -MARGIN) & (cell_y < BY + MARGIN)
    row = jnp.where(cell_y < 0, cell_y + EY, cell_y)
    flat = jnp.where(in_x & in_y, cell_x * EY + row, -1)
    row = jnp.where(in_y, row, -1)
    zz = cell_z - cut
    in_strip = in_x & (zz >= 0) & (zz < STRIP)
    strip_lane = jnp.where(in_strip, cell_x * STRIP + zz, -1)
    return flat, cell_z - gz * BZ, row, strip_lane


def hits(count, index):
    return rows((count, index.shape[1])) == index


def product(left, right):
    return lax.dot_general(
        left, right, (((1,), (1,)), ((), ())), preferred_element_type=F32
    )


def inject_points(cells, wave_ref, width, waves, planes, out_ref, strip_out_ref):
    count, low, total_rows = len(waves), planes[0] * EY, (planes[1] - planes[0]) * EY
    for start in range(0, cells.shape[1], width):
        sl = slice(start, start + width)
        flat, z, row, strip_lane = places(cells, sl)
        here = hits(total_rows, flat - low).astype(F32).astype(BF16)
        at_strip = hits(BZ, strip_lane).astype(F32).astype(BF16)
        at_z, at_row = hits(BZ, z), hits(EY, row)
        total = strip_total = None
        parts = [split(wave_ref[wave : wave + 1, sl]) for wave in waves]
        for part in range(3):
            amounts = [parts[wave][part].astype(F32) for wave in range(count)]
            right = jnp.concatenate([jnp.where(at_z, a, 0.0) for a in amounts], 0).astype(BF16)
            left = jnp.concatenate([jnp.where(at_row, a, 0.0) for a in amounts], 0).astype(BF16)
            term, strip_term = product(here, right), product(left, at_strip)
            total = term if part == 0 else total + term
            strip_total = strip_term if part == 0 else strip_total + strip_term
        for wave in range(count):
            value = total[:, wave * BZ : wave * BZ + BZ]
            strip_value = strip_total[wave * EY : wave * EY + EY]
            if start > 0:
                value = value + out_ref[wave]
                strip_value = strip_value + strip_out_ref[wave]
            out_ref[wave] = value
            strip_out_ref[wave] = strip_value


LATE_PLANES, EARLY_PLANES, SOURCE_PLANES = (0, EX), (2, EX - 2), (1, EX - 1)


def late_kernel(receivers, receiver_wave, r_ref, rs_ref):
    inject_points(receivers, receiver_wave, 256, (2, 3), LATE_PLANES, r_ref, rs_ref)


def early_kernel(receivers, receiver_wave, _, r_ref, rs_ref):
    inject_points(receivers, receiver_wave, 256, (0, 1), EARLY_PLANES, r_ref, rs_ref)


def source_kernel(sources, source_wave, _, s_ref, ss_ref):
    width = sources.shape[1]
    inject_points(sources, source_wave, width, (0, 1, 2), SOURCE_PLANES, s_ref, ss_ref)


def strip_of(packed, block, slot):
    lane = lanes(packed.shape)
    width = BX * STRIP
    shift = (block * width - slot * width) % BZ
    moved = pltpu.roll(packed, shift, 1) if shift else packed
    return jnp.where((lane >= block * width) & (lane < (block + 1) * width), moved, 0.0)


def y_up(v):
    return pltpu.roll(v, EY - 1, 0)


def y_down(v):
    return pltpu.roll(v, 1, 0)


def z_up(v, edge):
    return jnp.where(lanes(v.shape) == BZ - 1, edge, pltpu.roll(v, BZ - 1, 1))


def z_down(v, edge):
    return jnp.where(lanes(v.shape) == 0, edge, pltpu.roll(v, 1, 1))


def cut_edges(values, flux_z, cut_up, cut_down):
    place = lax.rem(lanes(values.shape), STRIP)
    above = jnp.where(place == MARGIN, values * cut_up, 0.0)
    below = jnp.where(place == MARGIN - 1, flux_z * cut_down, 0.0)
    return pltpu.roll(above, BZ - 2, 1) + below


def plane_edge(edges, x):
    return pltpu.roll(edges, (BZ - (x * STRIP + MARGIN - 1)) % BZ, 1)


def strip_flux(values, buoyancy):
    flux_x = buoyancy * (pltpu.roll(values, BZ - STRIP, 1) - values)
    flux_y = buoyancy * (y_up(values) - values)
    flux_z = buoyancy * (pltpu.roll(values, BZ - 1, 1) - values)
    spread = (flux_x - pltpu.roll(flux_x, STRIP, 1)) + (flux_y - y_down(flux_y))
    return flux_z, spread + (flux_z - pltpu.roll(flux_z, 1, 1))


def cut_flags():
    gz, half = lax.axis_index("gz"), lax.axis_size("gz") // 2
    return jnp.where(gz == half - 1, 1.0, 0.0), jnp.where(gz == half, 1.0, 0.0)


def sides():
    gx = lax.axis_index("gx")
    low = jnp.where(gx > 0, 1.0, 0.0)
    high = jnp.where(gx < lax.axis_size("gx") - 1, 1.0, 0.0)
    return low, high, lax.rem(gx, 2) == 0


def from_side(messages, first, count, block, side):
    even, odd = (message[first : first + count] for message in messages)
    low, high, even_above = side
    if block == 0:
        return jnp.where(even_above, odd, even) * low
    return jnp.where(even_above, even, odd) * high


def side_tile(messages, base, place, block, side):
    if not halved():
        return from_side(messages, base + place * 8, 8, block, side)
    tile = from_side(messages, base + place // 2 * 8, 8, block, side)
    upper = lax.axis_index("gy") == 0
    turned = half_turn(tile)
    tile = jnp.where(upper, turned, tile) if place % 2 else jnp.where(upper, tile, turned)
    return jnp.where((rows((8, BZ)) < MARGIN) == upper, tile, 0.0)


def side_place(wanted, plane, block):
    planes = range(BX - wanted, BX) if block == 0 else range(wanted)
    return planes.index(plane) if plane in planes else None


def widened(own, own_tiles, x, layout, side):
    block, plane = divmod(x, BX)
    if block == 1:
        main = own[0][own[1] + plane * BY : own[1] + plane * BY + BY]
        tile = own_tiles[0][own_tiles[1] + plane * 8 : own_tiles[1] + plane * 8 + 8]
        return jnp.concatenate([main, tile], 0)
    (messages, base, wanted), (tile_messages, tile_base, tile_place, tile_wanted) = layout
    main, tile = jnp.zeros((BY, BZ), F32), jnp.zeros((8, BZ), F32)
    place = side_place(wanted, plane, block)
    if place is not None:
        main = from_side(messages, base + place * BY, BY, block, side)
    place = side_place(tile_wanted, plane, block)
    if place is not None:
        tile = side_tile(tile_messages, tile_base, tile_place + place, block, side)
    return jnp.concatenate([main, tile], 0)


def less_plane_below(value, x, own_ref, own_rows, messages, side_layout, side):
    if x == BX:
        (planes_end, x_end), count = side_layout
        main = from_side(messages, planes_end, BY, 0, side)
        tile = side_tile(messages, x_end, count - 1, 0, side)
    elif x == 2 * BX:
        planes_end, _, tiles_end = own_rows
        high = side[1]
        main = own_ref[planes_end : planes_end + BY] * high
        tile = own_ref[tiles_end - 8 : tiles_end] * high
    else:
        return value
    return value - jnp.concatenate([main, tile], 0)


def strip_below(own, messages, first, slot, side):
    lane = lanes(own.shape)
    width = BX * STRIP
    low = from_side(messages, first, EY, 0, side)
    low = pltpu.roll(low, (width - slot * width) % BZ, 1)
    own = pltpu.roll(own * side[1], (2 * width - slot * width) % BZ, 1)
    in_own = (lane >= width) & (lane < width + STRIP)
    in_high = (lane >= 2 * width) & (lane < 2 * width + STRIP)
    return jnp.where(in_own, low, jnp.where(in_high, own, 0.0))


def whole_strip(own, messages, first, slot, side):
    low = from_side(messages, first, EY, 0, side)
    high = from_side(messages, first, EY, 2, side)
    return strip_of(low, 0, slot) + strip_of(own, 1, slot) + strip_of(high, 2, slot)


def adjoint_kernel(
    ql_ref, late_ref, odd, even, adj_hbm, ra_ref, rsa_ref, rb_ref, rsb_ref,
    table_ref,
    out_ref, hist_ref, coef_ref, coef_strip_ref,
    q_ref, t_ref, u_ref, scale_ref, edge_ref, flux_ref, w_sem,
):
    w_copy = pltpu.make_async_copy(adj_hbm.at[pl.ds(1, 3)], out_ref.at[pl.ds(1, 3)], w_sem)
    w_copy.start()
    cut_up, cut_down = cut_flags()
    side = sides()
    messages = (even, odd)
    r_refs = ((ra_ref, 0), (ra_ref, 1), (rb_ref, 0), (rb_ref, 1))
    rs_refs = ((rsa_ref, 0), (rsa_ref, 1), (rsb_ref, 0), (rsb_ref, 1))
    tiles, own_tiles = ADJ_SIDE[1], ADJ_OWN[1]
    side_strip = tiles + tile_rows(ADJ_TILES)
    raws = side_strip + EY

    def initial(index, x):
        own = ((ql_ref, 0), (late_ref, 0), (ql_ref, PLANES))[index]
        layout = (
            ((messages, raws, 4), (messages, tiles, 0, 3)),
            ((messages, 0, 3), (messages, tiles, 3, 2)),
            ((messages, raws + PLANES, 4), (messages, tiles, 5, 3)),
        )[index]
        value = widened(own, (late_ref, own_tiles + 32 * index), x, layout, side)
        if index == 1:
            value = less_plane_below(
                value, x, late_ref, ADJ_OWN, messages, (ADJ_SIDE, ADJ_TILES), side
            )
        return value

    for x in range(EX):
        stiff, buoy, damp = coefficients(initial(2, x), table_ref)
        coef_ref[0, x], coef_ref[1, x], coef_ref[2, x] = stiff, buoy, damp
        scale_ref[x] = stiff * damp
    own_strip = late_ref[ADJ_OWN[2] : ADJ_OWN[2] + EY]
    q_s, t_s, label_s = (
        whole_strip(own_strip, messages, side_strip, slot, side) for slot in range(3)
    )
    t_s = t_s - strip_below(own_strip, messages, side_strip, 3, side)
    stiff_s, buoy_s, damp_s = coefficients(label_s, table_ref)
    scale_s = stiff_s * damp_s
    coef_strip_ref[0], coef_strip_ref[1], coef_strip_ref[2] = stiff_s, buoy_s, damp_s
    w_copy.wait()

    for step in range(1, STEPS + 1):
        rs_ref, place = rs_refs[STEPS - step]
        q_s = q_s + rs_ref[place]
        u_s = scale_s * q_s
        flux_s, spread = strip_flux(u_s, buoy_s)
        t_s = t_s + spread
        q_s = damp_s * q_s + t_s
        edges = cut_edges(u_s, flux_s, cut_up, cut_down)
        for x in range(step, EX - step):
            edge_ref[step - 1, x] = plane_edge(edges, x)

    for step in range(1, STEPS + 1):
        k = STEPS - step
        r_ref, place = r_refs[k]
        r_first = (EARLY_PLANES if k < 2 else LATE_PLANES)[0]

        for x in range(step - 1, EX - step + 1):
            q = (initial(0, x) if step == 1 else q_ref[x]) + r_ref[place, x - r_first]
            q_ref[x] = q
            u_ref[x] = scale_ref[x] * q

        for x in range(step - 1, EX - step):
            u, buoyancy = u_ref[x], coef_ref[1, x]
            slopes = [u_ref[x + 1] - u]
            if x >= step:
                slopes += [y_up(u) - u, z_up(u, edge_ref[step - 1, x]) - u]
            for axis, slope in enumerate(slopes):
                flux_ref[axis, x] = buoyancy * slope
            if BX <= x < 2 * BX:
                for axis, slope in enumerate(slopes):
                    w = out_ref[1 + axis, x - BX] + slope[0:BY]
                    out_ref[1 + axis, x - BX] = w
                    hist_ref[k, 1 + axis, x - BX] = w

        for x in range(step, EX - step):
            flux_y, flux_z = flux_ref[1, x], flux_ref[2, x]
            spread = (flux_ref[0, x] - flux_ref[0, x - 1]) + (flux_y - y_down(flux_y))
            spread = spread + (flux_z - z_down(flux_z, edge_ref[step - 1, x]))
            damped = coef_ref[2, x] * q_ref[x]
            t = (initial(1, x) if step == 1 else t_ref[x]) + spread
            if BX <= x < 2 * BX:
                hist_ref[k, 0, x - BX] = damped[0:BY]
            if step < STEPS:
                t_ref[x] = t
                q_ref[x] = damped + t
            else:
                out_ref[0, x - BX] = (damped + t)[0:BY]


def forward_kernel(
    wave_ref, own_s_ref, late_ref, odd, even, coef_ref, coef_strip_ref, s_ref, ss_ref, hist_ref,
    adjoint_ref, grad_hbm, adjoint_hbm,
    p_ref, spread_ref, edge_ref, flux_ref, grad_ref, sems,
):
    copies = [pltpu.make_async_copy(adjoint_ref, adjoint_hbm, sems.at[0])]
    copies[0].start()

    def send(index, kind, first, count):
        planes = pl.ds(first, count)
        copy = pltpu.make_async_copy(
            grad_ref.at[kind, planes], grad_hbm.at[kind, planes], sems.at[index]
        )
        copy.start()
        copies.append(copy)

    cut_up, cut_down = cut_flags()
    side = sides()
    messages = (even, odd)
    tiles, own_tiles = WAVE_SIDE[1], WAVE_OWN[1]
    side_strip = tiles + tile_rows(WAVE_TILES)

    def initial(index, x):
        layout = (
            ((messages, 0, 4), (messages, tiles, 0, 3)),
            ((messages, PLANES, 3), (messages, tiles, 3, 2)),
        )[index]
        own = ((wave_ref, 0), (own_s_ref, 0))[index]
        value = widened(own, (late_ref, own_tiles + 32 * index), x, layout, side)
        if index == 1:
            value = less_plane_below(
                value, x, late_ref, WAVE_OWN, messages, (WAVE_SIDE, WAVE_TILES), side
            )
        return value

    own_strip = late_ref[WAVE_OWN[2] : WAVE_OWN[2] + EY]
    p_s, s_s = (
        whole_strip(own_strip, messages, side_strip, slot, side) for slot in range(2)
    )
    s_s = s_s - strip_below(own_strip, messages, side_strip, 2, side)
    stiff_s, buoy_s, damp_s = coef_strip_ref[0], coef_strip_ref[1], coef_strip_ref[2]

    for step in range(1, STEPS + 1):
        flux_s, spread = strip_flux(p_s, buoy_s)
        edges = cut_edges(p_s, flux_s, cut_up, cut_down)
        if step < STEPS:
            s_s = s_s - spread
            p_s = damp_s * (p_s - stiff_s * s_s) + ss_ref[step - 1]
        for x in range(step, EX - step):
            edge_ref[step - 1, x] = plane_edge(edges, x)
    for x in range(EX):
        p_ref[x] = initial(0, x)

    for step in range(1, STEPS + 1):
        k = step - 1
        for x in range(step - 1, EX - step):
            p, buoyancy = p_ref[x], coef_ref[1, x]
            slopes = [p_ref[x + 1] - p]
            if x >= step:
                slopes += [y_up(p) - p, z_up(p, edge_ref[step - 1, x]) - p]
            for axis, slope in enumerate(slopes):
                flux_ref[axis, x] = buoyancy * slope
            if BX <= x < 2 * BX:
                place = x - BX
                term = hist_ref[k, 1, place] * slopes[0][0:BY]
                term = term + hist_ref[k, 2, place] * slopes[1][0:BY]
                term = term + hist_ref[k, 3, place] * slopes[2][0:BY]
                grad_ref[1, place] = -term if k == 0 else grad_ref[1, place] - term
        if step == STEPS:
            send(1, 1, 0, BX)

        for x in range(step, EX - step):
            flux_y, flux_z = flux_ref[1, x], flux_ref[2, x]
            spread = (flux_ref[0, x] - flux_ref[0, x - 1]) + (flux_y - y_down(flux_y))
            spread = spread + (flux_z - z_down(flux_z, edge_ref[step - 1, x]))
            spread = (initial(1, x) if step == 1 else spread_ref[x]) - spread
            if step < STEPS:
                spread_ref[x] = spread
                p_ref[x] = (
                    coef_ref[2, x] * (p_ref[x] - coef_ref[0, x] * spread)
                    + s_ref[k, x - SOURCE_PLANES[0]]
                )
            if BX <= x < 2 * BX:
                place = x - BX
                term = hist_ref[k, 0, place] * spread[0:BY]
                grad_ref[0, place] = -term if k == 0 else grad_ref[0, place] - term
                if step == STEPS:
                    send(2 + place, 0, place, 1)
    for copy in copies:
        copy.wait()


def shape(*dims):
    return jax.ShapeDtypeStruct(dims, F32)


def call(kernel, outs, operands, scratch, places, micros=0.1, out_place="v"):
    spaces = {"h": pltpu.HBM, "a": pl.ANY, "v": pltpu.VMEM}
    operands = [
        pltpu.with_memory_space_constraint(operand, pltpu.HBM) if place == "h" else operand
        for operand, place in zip(operands, places)
    ]
    return pl.pallas_call(
        kernel,
        out_shape=outs,
        in_specs=[pl.BlockSpec(memory_space=spaces[place]) for place in places],
        out_specs=[pl.BlockSpec(memory_space=spaces[out_place])] * len(outs),
        scratch_shapes=scratch,
        compiler_params=pltpu.CompilerParams(vmem_limit_bytes=VMEM_LIMIT),
        cost_estimate=pl.CostEstimate(
            flops=0, bytes_accessed=int(3.69e6 * micros), transcendentals=0
        ),
    )(*operands)


def from_sides(sends, axes):
    count = lax.axis_size("gy")

    def route(offset):
        pairs = []
        for target in range(count):
            source = target + offset
            if 0 <= source < count:
                if "gz" in axes:
                    pairs += [(2 * source + z, 2 * target + 1 - z) for z in range(2)]
                else:
                    pairs.append((source, target))
        return pairs

    if count == 2:
        both = lax.ppermute(sends[0], axes, route(1) + route(-1))
        return both, both
    upward, downward = sends
    return lax.ppermute(downward, axes, route(1)), lax.ppermute(upward, axes, route(-1))


def rotated(array, axis, offset):
    count = lax.axis_size(axis)
    return lax.ppermute(array, axis, [((i + offset) % count, i) for i in range(count)])


def paired(array, odd):
    count = lax.axis_size("gx")
    pairs = []
    for i in range(count):
        partner = ((i - 1) ^ 1) + 1 if odd else i ^ 1
        pairs.append((partner if 0 <= partner < count else i, i))
    return lax.ppermute(array, "gx", pairs)


def local(
    stored, adjoint_end, labels, tissue, source_cells, source_wave, receiver_cells, receiver_wave
):
    assert lax.axis_size("gz") == 2 and labels.shape == (BX, BY, BZ) and tissue.shape[1] == 8
    half = lax.axis_size("gx") // 2
    arguments = [
        stored, adjoint_end, labels, tissue,
        receiver_cells.T, receiver_wave, source_cells.T, source_wave,
    ]
    ways = 1 if lax.axis_size("gy") == 2 else 2
    wave, ql, t, last_x, last_y, strips, table, receivers, receiver_wave, sources, source_wave, *sends = call(
        load_kernel,
        [
            shape(2 * PLANES + 32, BZ),
            shape(2 * PLANES, BZ),
            shape(PLANES, BZ),
            shape(2 * BY, BZ),
            shape(2 * BX * 8, BZ),
            shape(3 * BY, BZ),
            shape(24, BZ),
        ]
        + [jax.ShapeDtypeStruct(array.shape, array.dtype) for array in arguments[4:]]
        + [shape(20 * 8, BZ)] * ways
        + [shape(2 * 8, BZ)] * ways,
        arguments,
        [
            pltpu.VMEM(stored.shape, F32),
            pltpu.VMEM(adjoint_end.shape, F32),
            pltpu.VMEM(labels.shape, jnp.int32),
            pltpu.SMEM(tissue.shape, F32),
            pltpu.SemaphoreType.DMA,
        ],
        "hhhhhhhh",
        1.4,
    )
    from_up, from_down = from_sides(sends[:ways], "gy")
    other = rotated(strips, "gz", 1)
    corner_up, corner_down = from_sides(sends[ways:], ("gy", "gz"))
    wave = rotated(wave, "gx", half)
    rb, rsb = call(
        late_kernel,
        [shape(2, EX * EY, BZ), shape(2, EY, BZ)],
        [receivers, receiver_wave],
        [],
        "vv",
        1.2,
    )
    early_planes, source_planes = (last - first for first, last in (EARLY_PLANES, SOURCE_PLANES))
    late, adj_late = call(
        merge_kernel,
        [shape(WAVE_FIX + 24, BZ), shape(ADJ_OWN[2] + EY, BZ)],
        [from_up, from_down, corner_up, corner_down, strips, other, t, last_x, last_y, rsb],
        [],
        "vvvvvvvvva",
    )
    late = rotated(late, "gx", half)
    ra, rsa = call(
        early_kernel,
        [shape(2, early_planes * EY, BZ), shape(2, EY, BZ)],
        [receivers, receiver_wave, adj_late],
        [],
        "vva",
        1.0,
    )
    ra, rb = ra.reshape(2, early_planes, EY, BZ), rb.reshape(2, EX, EY, BZ)
    even, odd = call(
        adjoint_join_kernel,
        [shape(ADJ_SIDE[1] + tile_rows(ADJ_TILES) + EY + 2 * PLANES, BZ)] * 2,
        [ql, adj_late],
        [],
        "vv",
    )
    even, odd = paired(even, False), paired(odd, True)
    src, src_strip = call(
        source_kernel,
        [shape(STEPS - 1, source_planes * EY, BZ), shape(STEPS - 1, EY, BZ)],
        [sources, source_wave, adj_late],
        [],
        "vva",
        0.5,
    )
    src = src.reshape(STEPS - 1, source_planes, EY, BZ)
    own_s, wave_even, wave_odd = call(
        join_kernel,
        [shape(PLANES, BZ)] + [shape(WAVE_SIDE[1] + tile_rows(WAVE_TILES) + EY, BZ)] * 2,
        [wave, late],
        [],
        "vv",
    )
    wave_even, wave_odd = paired(wave_even, False), paired(wave_odd, True)
    adjoint_out, hist, coef, coef_strip = call(
        adjoint_kernel,
        [
            shape(4, BX, BY, BZ),
            shape(STEPS, 4, BX, BY, BZ),
            shape(3, EX, EY, BZ),
            shape(3, EY, BZ),
        ],
        [ql, adj_late, odd, even, adjoint_end, ra, rsa, rb, rsb, table],
        [pltpu.VMEM((EX, EY, BZ), F32)] * 4
        + [
            pltpu.VMEM((STEPS, EX, EY, BZ), F32),
            pltpu.VMEM((3, EX, EY, BZ), F32),
            pltpu.SemaphoreType.DMA,
        ],
        "vvvvhvvvvv",
        3.9,
    )
    return call(
        forward_kernel,
        [shape(2, BX, BY, BZ), shape(4, BX, BY, BZ)],
        [
            wave, own_s, late, wave_odd, wave_even, coef, coef_strip, src, src_strip, hist,
            adjoint_out,
        ],
        [pltpu.VMEM((EX, EY, BZ), F32)] * 2
        + [
            pltpu.VMEM((STEPS, EX, EY, BZ), F32),
            pltpu.VMEM((3, EX, EY, BZ), F32),
            pltpu.VMEM((2, BX, BY, BZ), F32),
            pltpu.SemaphoreType.DMA((2 + BX,)),
        ],
        "vvvvvvvvvvv",
        2.5,
        "a",
    )


def solution(mesh):
    return jax.shard_map(
        local,
        mesh=mesh,
        in_specs=(
            P("shot", "gx", "gy", "gz"),
            P("shot", "gx", "gy", "gz"),
            P("gx", "gy", "gz"),
            P(),
            P("shot", None),
            P(None, "shot"),
            P(),
            P(None, "shot"),
        ),
        out_specs=(P("shot", "gx", "gy", "gz"), P("shot", "gx", "gy", "gz")),
        check_vma=False,
    )
```

```python
import jax
import jax.numpy as jnp
from jax import lax
from jax.experimental import pallas as pl
from jax.experimental.pallas import tpu as pltpu
from jax.sharding import PartitionSpec as P

STEPS = 4
MARGIN = 4
BX, BY, BZ = 4, 32, 128
EX, EY = BX + 2 * MARGIN, BY + 2 * MARGIN
STRIP = 2 * MARGIN
F32 = jnp.float32
BF16 = jnp.bfloat16
VMEM_LIMIT = 16 * 1024 * 1024
PLANES = BX * BY
WAVE_OWN = (0, BY, BY + 9 * 8)
FIX_LANE = 3 * BX * STRIP
SPARE = 64
ADJ_OWN = (PLANES, PLANES + BY, PLANES + BY + 13 * 8)
WAVE_SIDE = (PLANES + 3 * BY, PLANES + 4 * BY)
ADJ_SIDE = (3 * BY, 4 * BY)
WAVE_TILES, ADJ_TILES = 6, 9


def lanes(shape):
    return lax.broadcasted_iota(jnp.int32, shape, len(shape) - 1)


def rows(shape):
    return lax.broadcasted_iota(jnp.int32, shape, len(shape) - 2)


def run(copies):
    for copy in copies:
        copy.start()
    for copy in copies:
        copy.wait()


def coefficients(labels, table_ref):
    result = [jnp.zeros(labels.shape, F32) for _ in range(3)]
    for index in range(8):
        picked = labels == float(index + 1)
        for kind in range(3):
            row = kind * 8 + index
            result[kind] = jnp.where(picked, table_ref[row : row + 1], result[kind])
    return result


def buoyancy_of(labels, table_ref):
    result = jnp.zeros(labels.shape, F32)
    for index in range(8):
        result = jnp.where(labels == float(index + 1), table_ref[8 + index : 9 + index], result)
    return result


def half_turn(tile):
    return pltpu.roll(tile, MARGIN, 0)


def load_kernel(
    stored_hbm, adj_hbm, lab_hbm, tissue_hbm, rc_hbm, rw_hbm, sc_hbm, sw_hbm,
    wave_ref, ql_ref, t_ref, last_x_ref, last_y_ref, strip_ref, table_ref,
    rc_ref, rw_ref, sc_ref, sw_ref, *rest,
):
    *sends, stored, adj, lab, tissue, sem = rest
    run([
        pltpu.make_async_copy(source, target, sem)
        for source, target in (
            (stored_hbm, stored), (adj_hbm, adj), (lab_hbm, lab), (tissue_hbm, tissue),
            (rc_hbm, rc_ref), (rw_hbm, rw_ref), (sc_hbm, sc_ref), (sw_hbm, sw_ref),
        )
    ])
    for index in range(tissue.shape[1]):
        speed = jnp.full((1, BZ), tissue[0, index], F32)
        density = jnp.full((1, BZ), tissue[1, index], F32)
        table_ref[index : index + 1] = density * speed
        table_ref[8 + index : 9 + index] = speed / density
        table_ref[16 + index : 17 + index] = 1.0 - jnp.full((1, BZ), tissue[2, index], F32)
    gy, gz = lax.axis_index("gy"), lax.axis_index("gz")
    lane = lanes((BY, BZ))
    row = rows((BY, BZ))
    tile_row = rows((8, BZ))
    strips = [jnp.zeros((BY, BZ), F32) for _ in range(3)]
    tiles = [None] * 39
    previous = [None, None]

    def edge_tile(block):
        return jnp.where(tile_row < MARGIN, block[0:8], block[BY - 8 : BY])

    for x in range(BX):
        labels = lab[x].astype(F32) + 1.0
        buoyancy = buoyancy_of(labels, table_ref)
        plane = slice(x * BY, x * BY + BY)
        fields = [stored[index, x] for index in range(4)] + [adj[0, x]]
        fields += [buoyancy * adj[index, x] for index in range(1, 4)] + [labels]
        wave_ref[plane] = fields[0]
        ql_ref[plane] = fields[4]
        ql_ref[PLANES + x * BY : PLANES + x * BY + BY] = labels
        for index, block in enumerate(fields):
            tiles[index * BX + x] = edge_tile(block)
            group, slot = divmod(index, 4)
            base = slot * BX * STRIP + x * STRIP
            rolled = pltpu.roll(block, base + MARGIN, 1)
            first = base + MARGIN * gz
            strips[group] = jnp.where(
                (lane >= first) & (lane < first + MARGIN), rolled, strips[group]
            )
        for kind, (target, base) in enumerate(((wave_ref, PLANES), (t_ref, 0))):
            vx, vy, vz = fields[4 * kind + 1 : 4 * kind + 4]
            spread = vx if x == 0 else vx - previous[kind]
            spread = spread + (vy - jnp.where(row == 0, 0.0, pltpu.roll(vy, 1, 0)))
            spread = spread + (vz - jnp.where(lane == 0, 0.0, pltpu.roll(vz, 1, 1)))
            target[base + x * BY : base + x * BY + BY] = spread
            previous[kind] = vx
            index = (kind * BX + x) * 8
            last_y_ref[index : index + 8] = vy[BY - 8 : BY]
    wave_ref[2 * PLANES : 2 * PLANES + BY] = previous[0]
    last_x_ref[...] = previous[1]
    for group in range(3):
        strip_ref[group * BY : group * BY + BY] = strips[group]
        tiles[9 * BX + group] = edge_tile(strips[group])

    def joined(first, second):
        second = first if second is None else second
        upward = jnp.where(tile_row < MARGIN, half_turn(first), second)
        downward = jnp.where(tile_row < MARGIN, first, half_turn(second))
        if len(sends) == 2:
            return (jnp.where(gy == 0, upward, downward),)
        return upward, downward

    tiles.append(None)
    half = len(sends) // 2
    for place in range(20):
        for target, tile in zip(sends[:half], joined(tiles[2 * place], tiles[2 * place + 1])):
            target[place * 8 : place * 8 + 8] = tile
    for place in range(2):
        first = tiles[9 * BX + 2 * place]
        for target, tile in zip(sends[half:], joined(first, tiles[9 * BX + 2 * place + 1])):
            target[place * 8 : place * 8 + 8] = tile


def copy_rows(target, base, source, first, count):
    target[base : base + count] = source[pl.ds(pl.multiple_of(first, 8), count)]
    return base + count


def halved():
    return lax.axis_size("gy") == 2


def tile_rows(count):
    return (count + 1) // 2 * 8 if halved() else count * 8


def put_tiles(target, base, source, firsts):
    tiles = [source[pl.ds(pl.multiple_of(first, 8), 8)] for first in firsts]
    if halved():
        upper = lax.axis_index("gy") == 0
        row = rows((8, BZ))
        pairs = [(tiles[i], tiles[min(i + 1, len(tiles) - 1)]) for i in range(0, len(tiles), 2)]
        tiles = [
            jnp.where(
                row < MARGIN,
                jnp.where(upper, first, half_turn(first)),
                jnp.where(upper, half_turn(second), second),
            )
            for first, second in pairs
        ]
    for place, tile in enumerate(tiles):
        target[base + place * 8 : base + place * 8 + 8] = tile
    return base + 8 * len(tiles)


def pair_planes():
    parity = lax.rem(lax.axis_index("gx"), 2)
    return 1 - parity, parity


def merge_kernel(
    from_up, from_down, corner_up, corner_down, strip_ref, other_ref,
    t_ref, last_x_ref, last_y_ref, _,
    late_ref, adj_ref,
    wave_ref,
):
    gy = lax.axis_index("gy")
    tile_row = rows((8, BZ))
    row, lane = rows((BY, BZ)), lanes((BY, BZ))
    take_up = (tile_row < MARGIN) & (gy < lax.axis_size("gy") - 1)
    take_down = (tile_row >= MARGIN) & (gy > 0)
    _, cut_down = cut_flags()

    def halo(up, down, index):
        place, second = divmod(index, 2)
        sl = slice(place * 8, place * 8 + 8)
        above = half_turn(up[sl]) if second else up[sl]
        below = down[sl] if second else half_turn(down[sl])
        return jnp.where(take_up, above, jnp.where(take_down, below, 0.0))

    wide = []
    for group in range(3):
        sl = slice(group * BY, group * BY + BY)
        tile = halo(from_up, from_down, 9 * BX + group) + halo(corner_up, corner_down, group)
        wide.append(jnp.concatenate([strip_ref[sl] + other_ref[sl], tile], 0))
    strip_lane = lanes((EY, BZ))

    def strip_field(index):
        group, slot = divmod(index, 4)
        moved = pltpu.roll(wide[group], (BZ - slot * BX * STRIP) % BZ, 1) if slot else wide[group]
        return jnp.where(strip_lane < BX * STRIP, moved, 0.0)

    last_lanes = (BX - 1) * STRIP
    fix_row = jnp.zeros((8, BZ), F32)
    fix_lane = jnp.zeros((BY, BZ), F32)
    for kind, target in enumerate((wave_ref, adj_ref)):
        first = 4 * kind
        planes_end, x_end, tiles_end = (WAVE_OWN, ADJ_OWN)[kind]
        vx, vy, vz = (strip_field(first + 1 + axis) for axis in range(3))
        spread = vx - jnp.where(strip_lane < STRIP, 0.0, pltpu.roll(vx, STRIP, 1))
        spread = (spread + (vy - y_down(vy))) + (vz - pltpu.roll(vz, 1, 1))
        strip = strip_field(first)
        strip = strip + pltpu.roll(jnp.where(strip_lane < BX * STRIP, spread, 0.0), BX * STRIP, 1)
        last_slot = 2
        if kind == 1:
            strip = strip + pltpu.roll(strip_field(8), 2 * BX * STRIP, 1)
            last_slot = 3
        last = jnp.where(strip_lane >= last_lanes, vx, 0.0)
        strip = strip + pltpu.roll(last, last_slot * BX * STRIP - last_lanes, 1)

        vx_before = None
        for x in range(BX):
            vx_t, vy_t, vz_t = (
                halo(from_up, from_down, (first + 1 + axis) * BX + x) for axis in range(3)
            )
            below_z = pltpu.roll(vz, (BZ - (x * STRIP + MARGIN - 1)) % BZ, 1) * cut_down
            last_y = last_y_ref[(kind * BX + x) * 8 : (kind * BX + x) * 8 + 8]
            y_before = jnp.where(
                tile_row == 0, pltpu.roll(last_y, 1, 0), pltpu.roll(vy_t, 1, 0)
            )
            z_before = jnp.where(lane[0:8] == 0, below_z[BY:EY], pltpu.roll(vz_t, 1, 1))
            spread = vx_t if x == 0 else vx_t - vx_before
            spread = (spread + (vy_t - y_before)) + (vz_t - z_before)
            vx_before = vx_t
            if kind == 0:
                fix_row = jnp.where(tile_row == x, vy_t[7:8], fix_row)
                moved = pltpu.roll(below_z[0:BY], FIX_LANE + x, 1)
                fix_lane = jnp.where(lane == FIX_LANE + x, moved, fix_lane)
            else:
                block = t_ref[x * BY : x * BY + BY]
                block = block - jnp.where(row == 0, vy_t[7:8], 0.0)
                block = block - jnp.where(lane == 0, below_z[0:BY], 0.0)
                target[x * BY : x * BY + BY] = block
            base = x_end + x * 8
            target[base : base + 8] = halo(from_up, from_down, first * BX + x)
            target[base + 32 : base + 40] = spread
            if kind == 1:
                target[base + 64 : base + 72] = halo(from_up, from_down, 8 * BX + x)
        target[tiles_end - 8 : tiles_end] = vx_before
        if kind == 0:
            base = put_tiles(late_ref, 0, wave_ref, range(x_end, tiles_end, 8))
            late_ref[base : base + BY] = strip[0:BY] + fix_lane
            late_ref[base + BY : base + EY] = strip[BY:EY]
            late_ref[base + EY : base + EY + 8] = fix_row
            late_ref[base + EY + 8 : base + EY + 8 + SPARE] = jnp.zeros((SPARE, BZ), F32)
        else:
            target[planes_end:x_end] = last_x_ref[...]
            target[tiles_end : tiles_end + EY] = strip


def adjoint_join_kernel(ql_ref, adj_ref, even_ref, odd_ref):
    planes_end, x_end, tiles_end = ADJ_OWN
    for target, first in zip((even_ref, odd_ref), pair_planes()):
        base = copy_rows(target, 0, adj_ref, first * BY, 3 * BY)
        base = copy_rows(target, base, adj_ref, planes_end, BY)
        near = [x_end + (first + plane) * 8 for plane in range(3)]
        nearest = [x_end + 32 + first * 16 + plane * 8 for plane in range(2)]
        firsts = near + nearest + [start + 64 for start in near] + [tiles_end - 8]
        base = put_tiles(target, base, adj_ref, firsts)
        base = copy_rows(target, base, adj_ref, tiles_end, EY)
        copy_rows(target, base, ql_ref, 0, 2 * PLANES)


def unpacked(tile, place):
    upper = lax.axis_index("gy") == 0
    turned = half_turn(tile)
    tile = jnp.where(upper, turned, tile) if place % 2 else jnp.where(upper, tile, turned)
    return jnp.where((rows((8, BZ)) < MARGIN) == upper, tile, 0.0)


def join_kernel(wave_ref, late_ref, s_ref, own_ref, even_ref, odd_ref):
    planes_end, x_end, tiles_end = WAVE_OWN
    own_ref[planes_end:x_end] = wave_ref[2 * PLANES : 2 * PLANES + BY]
    for place in range((tiles_end - x_end) // 8):
        if halved():
            tile = unpacked(late_ref[place // 2 * 8 : place // 2 * 8 + 8], place)
        else:
            tile = late_ref[place * 8 : place * 8 + 8]
        own_ref[x_end + place * 8 : x_end + place * 8 + 8] = tile
    strip = tile_rows((tiles_end - x_end) // 8)
    own_ref[tiles_end : tiles_end + EY] = late_ref[strip : strip + EY]
    row, lane = rows((BY, BZ)), lanes((BY, BZ))
    fix_lane = late_ref[strip : strip + BY]
    for x in range(BX):
        block = wave_ref[PLANES + x * BY : PLANES + x * BY + BY]
        fix_row = late_ref[strip + EY + x : strip + EY + x + 1]
        block = block - jnp.where(row == 0, fix_row, 0.0)
        block = block - jnp.where(lane == 0, pltpu.roll(fix_lane, BZ - FIX_LANE - x, 1), 0.0)
        s_ref[x * BY : x * BY + BY] = block
    for target, first in zip((even_ref, odd_ref), pair_planes()):
        base = copy_rows(target, 0, wave_ref, 0, PLANES)
        base = copy_rows(target, base, s_ref, first * BY, 3 * BY)
        base = copy_rows(target, base, own_ref, planes_end, BY)
        near = [x_end + (first + plane) * 8 for plane in range(3)]
        nearest = [x_end + 32 + first * 16 + plane * 8 for plane in range(2)]
        base = put_tiles(target, base, own_ref, near + nearest + [tiles_end - 8])
        copy_rows(target, base, own_ref, tiles_end, EY)


def split(values):
    high = values.astype(BF16)
    rest = values - high.astype(F32)
    middle = rest.astype(BF16)
    low = (rest - middle.astype(F32)).astype(BF16)
    return high, middle, low


def places(cells, sl):
    gx, gy, gz = (lax.axis_index(name) for name in ("gx", "gy", "gz"))
    cut = BZ * lax.axis_size("gz") // 2 - MARGIN
    cell_x = cells[0:1, sl] - (gx * BX - MARGIN)
    cell_y = cells[1:2, sl] - gy * BY
    cell_z = cells[2:3, sl]
    in_x = (cell_x >= 0) & (cell_x < EX)
    in_y = (cell_y >= -MARGIN) & (cell_y < BY + MARGIN)
    row = jnp.where(cell_y < 0, cell_y + EY, cell_y)
    flat = jnp.where(in_x & in_y, cell_x * EY + row, -1)
    row = jnp.where(in_y, row, -1)
    zz = cell_z - cut
    in_strip = in_x & (zz >= 0) & (zz < STRIP)
    strip_lane = jnp.where(in_strip, cell_x * STRIP + zz, -1)
    return flat, cell_z - gz * BZ, row, strip_lane


def hits(count, index):
    return rows((count, index.shape[1])) == index


def product(left, right):
    return lax.dot_general(
        left, right, (((1,), (1,)), ((), ())), preferred_element_type=F32
    )


def inject_points(cells, wave_ref, width, waves, planes, out_ref, strip_out_ref):
    count, low, total_rows = len(waves), planes[0] * EY, (planes[1] - planes[0]) * EY
    for start in range(0, cells.shape[1], width):
        sl = slice(start, start + width)
        flat, z, row, strip_lane = places(cells, sl)
        here = hits(total_rows, flat - low).astype(F32).astype(BF16)
        at_strip = hits(BZ, strip_lane).astype(F32).astype(BF16)
        at_z, at_row = hits(BZ, z), hits(EY, row)
        total = strip_total = None
        parts = [split(wave_ref[wave : wave + 1, sl]) for wave in waves]
        for part in range(3):
            amounts = [parts[wave][part].astype(F32) for wave in range(count)]
            right = jnp.concatenate([jnp.where(at_z, a, 0.0) for a in amounts], 0).astype(BF16)
            left = jnp.concatenate([jnp.where(at_row, a, 0.0) for a in amounts], 0).astype(BF16)
            term, strip_term = product(here, right), product(left, at_strip)
            total = term if part == 0 else total + term
            strip_total = strip_term if part == 0 else strip_total + strip_term
        for wave in range(count):
            value = total[:, wave * BZ : wave * BZ + BZ]
            strip_value = strip_total[wave * EY : wave * EY + EY]
            if start > 0:
                value = value + out_ref[wave]
                strip_value = strip_value + strip_out_ref[wave]
            out_ref[wave] = value
            strip_out_ref[wave] = strip_value


LATE_PLANES, EARLY_PLANES, SOURCE_PLANES = (0, EX), (2, EX - 2), (1, EX - 1)


def late_kernel(receivers, receiver_wave, r_ref, rs_ref):
    inject_points(receivers, receiver_wave, 256, (2, 3), LATE_PLANES, r_ref, rs_ref)


def early_kernel(receivers, receiver_wave, _, r_ref, rs_ref):
    inject_points(receivers, receiver_wave, 256, (0, 1), EARLY_PLANES, r_ref, rs_ref)


def source_kernel(sources, source_wave, _, s_ref, ss_ref):
    width = sources.shape[1]
    inject_points(sources, source_wave, width, (0, 1, 2), SOURCE_PLANES, s_ref, ss_ref)


def strip_of(packed, block, slot):
    lane = lanes(packed.shape)
    width = BX * STRIP
    shift = (block * width - slot * width) % BZ
    moved = pltpu.roll(packed, shift, 1) if shift else packed
    return jnp.where((lane >= block * width) & (lane < (block + 1) * width), moved, 0.0)


def y_up(v):
    return pltpu.roll(v, EY - 1, 0)


def y_down(v):
    return pltpu.roll(v, 1, 0)


def z_up(v, edge):
    return jnp.where(lanes(v.shape) == BZ - 1, edge, pltpu.roll(v, BZ - 1, 1))


def z_down(v, edge):
    return jnp.where(lanes(v.shape) == 0, edge, pltpu.roll(v, 1, 1))


def cut_edges(values, flux_z, cut_up, cut_down):
    place = lax.rem(lanes(values.shape), STRIP)
    above = jnp.where(place == MARGIN, values * cut_up, 0.0)
    below = jnp.where(place == MARGIN - 1, flux_z * cut_down, 0.0)
    return pltpu.roll(above, BZ - 2, 1) + below


def plane_edge(edges, x):
    return pltpu.roll(edges, (BZ - (x * STRIP + MARGIN - 1)) % BZ, 1)


def strip_flux(values, buoyancy):
    flux_x = buoyancy * (pltpu.roll(values, BZ - STRIP, 1) - values)
    flux_y = buoyancy * (y_up(values) - values)
    flux_z = buoyancy * (pltpu.roll(values, BZ - 1, 1) - values)
    spread = (flux_x - pltpu.roll(flux_x, STRIP, 1)) + (flux_y - y_down(flux_y))
    return flux_z, spread + (flux_z - pltpu.roll(flux_z, 1, 1))


def cut_flags():
    gz, half = lax.axis_index("gz"), lax.axis_size("gz") // 2
    return jnp.where(gz == half - 1, 1.0, 0.0), jnp.where(gz == half, 1.0, 0.0)


def sides():
    gx = lax.axis_index("gx")
    low = jnp.where(gx > 0, 1.0, 0.0)
    high = jnp.where(gx < lax.axis_size("gx") - 1, 1.0, 0.0)
    return low, high, lax.rem(gx, 2) == 0


def from_side(messages, first, count, block, side):
    even, odd = (message[first : first + count] for message in messages)
    low, high, even_above = side
    if block == 0:
        return jnp.where(even_above, odd, even) * low
    return jnp.where(even_above, even, odd) * high


def side_tile(messages, base, place, block, side):
    if not halved():
        return from_side(messages, base + place * 8, 8, block, side)
    tile = from_side(messages, base + place // 2 * 8, 8, block, side)
    return unpacked(tile, place)


def side_place(wanted, plane, block):
    planes = range(BX - wanted, BX) if block == 0 else range(wanted)
    return planes.index(plane) if plane in planes else None


def widened(own, own_tiles, x, layout, side):
    block, plane = divmod(x, BX)
    if block == 1:
        main = own[0][own[1] + plane * BY : own[1] + plane * BY + BY]
        tile = own_tiles[0][own_tiles[1] + plane * 8 : own_tiles[1] + plane * 8 + 8]
        return jnp.concatenate([main, tile], 0)
    (messages, base, wanted), (tile_messages, tile_base, tile_place, tile_wanted) = layout
    main, tile = jnp.zeros((BY, BZ), F32), jnp.zeros((8, BZ), F32)
    place = side_place(wanted, plane, block)
    if place is not None:
        main = from_side(messages, base + place * BY, BY, block, side)
    place = side_place(tile_wanted, plane, block)
    if place is not None:
        tile = side_tile(tile_messages, tile_base, tile_place + place, block, side)
    return jnp.concatenate([main, tile], 0)


def less_plane_below(value, x, own_ref, own_rows, messages, side_layout, side):
    if x == BX:
        (planes_end, x_end), count = side_layout
        main = from_side(messages, planes_end, BY, 0, side)
        tile = side_tile(messages, x_end, count - 1, 0, side)
    elif x == 2 * BX:
        planes_end, _, tiles_end = own_rows
        high = side[1]
        main = own_ref[planes_end : planes_end + BY] * high
        tile = own_ref[tiles_end - 8 : tiles_end] * high
    else:
        return value
    return value - jnp.concatenate([main, tile], 0)


def strip_below(own, messages, first, slot, side):
    lane = lanes(own.shape)
    width = BX * STRIP
    low = from_side(messages, first, EY, 0, side)
    low = pltpu.roll(low, (width - slot * width) % BZ, 1)
    own = pltpu.roll(own * side[1], (2 * width - slot * width) % BZ, 1)
    in_own = (lane >= width) & (lane < width + STRIP)
    in_high = (lane >= 2 * width) & (lane < 2 * width + STRIP)
    return jnp.where(in_own, low, jnp.where(in_high, own, 0.0))


def whole_strip(own, messages, first, slot, side):
    low = from_side(messages, first, EY, 0, side)
    high = from_side(messages, first, EY, 2, side)
    return strip_of(low, 0, slot) + strip_of(own, 1, slot) + strip_of(high, 2, slot)


def adjoint_kernel(
    ql_ref, late_ref, even, odd, adj_hbm, ra_ref, rsa_ref, rb_ref, rsb_ref,
    table_ref,
    out_ref, hist_ref, coef_ref, coef_strip_ref,
    q_ref, t_ref, u_ref, scale_ref, edge_ref, flux_ref, w_sem,
):
    w_copy = pltpu.make_async_copy(adj_hbm.at[pl.ds(1, 3)], out_ref.at[pl.ds(1, 3)], w_sem)
    w_copy.start()
    cut_up, cut_down = cut_flags()
    side = sides()
    messages = (even, odd)
    r_refs = ((ra_ref, 0), (ra_ref, 1), (rb_ref, 0), (rb_ref, 1))
    rs_refs = ((rsa_ref, 0), (rsa_ref, 1), (rsb_ref, 0), (rsb_ref, 1))
    tiles, own_tiles = ADJ_SIDE[1], ADJ_OWN[1]
    side_strip = tiles + tile_rows(ADJ_TILES)
    raws = side_strip + EY

    def initial(index, x):
        own = ((ql_ref, 0), (late_ref, 0), (ql_ref, PLANES))[index]
        layout = (
            ((messages, raws, 4), (messages, tiles, 0, 3)),
            ((messages, 0, 3), (messages, tiles, 3, 2)),
            ((messages, raws + PLANES, 4), (messages, tiles, 5, 3)),
        )[index]
        value = widened(own, (late_ref, own_tiles + 32 * index), x, layout, side)
        if index == 1:
            value = less_plane_below(
                value, x, late_ref, ADJ_OWN, messages, (ADJ_SIDE, ADJ_TILES), side
            )
        return value

    for x in range(EX):
        stiff, buoy, damp = coefficients(initial(2, x), table_ref)
        coef_ref[0, x], coef_ref[1, x], coef_ref[2, x] = stiff, buoy, damp
        scale_ref[x] = stiff * damp
    own_strip = late_ref[ADJ_OWN[2] : ADJ_OWN[2] + EY]
    q_s, t_s, label_s = (
        whole_strip(own_strip, messages, side_strip, slot, side) for slot in range(3)
    )
    t_s = t_s - strip_below(own_strip, messages, side_strip, 3, side)
    stiff_s, buoy_s, damp_s = coefficients(label_s, table_ref)
    scale_s = stiff_s * damp_s
    coef_strip_ref[0], coef_strip_ref[1], coef_strip_ref[2] = stiff_s, buoy_s, damp_s
    w_copy.wait()

    for step in range(1, STEPS + 1):
        rs_ref, place = rs_refs[STEPS - step]
        q_s = q_s + rs_ref[place]
        u_s = scale_s * q_s
        flux_s, spread = strip_flux(u_s, buoy_s)
        t_s = t_s + spread
        q_s = damp_s * q_s + t_s
        edges = cut_edges(u_s, flux_s, cut_up, cut_down)
        for x in range(step, EX - step):
            edge_ref[step - 1, x] = plane_edge(edges, x)

    for step in range(1, STEPS + 1):
        k = STEPS - step
        r_ref, place = r_refs[k]
        r_first = (EARLY_PLANES if k < 2 else LATE_PLANES)[0]

        for x in range(step - 1, EX - step + 1):
            q = (initial(0, x) if step == 1 else q_ref[x]) + r_ref[place, x - r_first]
            q_ref[x] = q
            u_ref[x] = scale_ref[x] * q

        for x in range(step - 1, EX - step):
            u, buoyancy = u_ref[x], coef_ref[1, x]
            slopes = [u_ref[x + 1] - u]
            if x >= step:
                slopes += [y_up(u) - u, z_up(u, edge_ref[step - 1, x]) - u]
            for axis, slope in enumerate(slopes):
                flux_ref[axis, x] = buoyancy * slope
            if BX <= x < 2 * BX:
                for axis, slope in enumerate(slopes):
                    w = out_ref[1 + axis, x - BX] + slope[0:BY]
                    out_ref[1 + axis, x - BX] = w
                    hist_ref[k, 1 + axis, x - BX] = w

        for x in range(step, EX - step):
            flux_y, flux_z = flux_ref[1, x], flux_ref[2, x]
            spread = (flux_ref[0, x] - flux_ref[0, x - 1]) + (flux_y - y_down(flux_y))
            spread = spread + (flux_z - z_down(flux_z, edge_ref[step - 1, x]))
            damped = coef_ref[2, x] * q_ref[x]
            t = (initial(1, x) if step == 1 else t_ref[x]) + spread
            if BX <= x < 2 * BX:
                hist_ref[k, 0, x - BX] = damped[0:BY]
            if step < STEPS:
                t_ref[x] = t
                q_ref[x] = damped + t
            else:
                out_ref[0, x - BX] = (damped + t)[0:BY]


def forward_kernel(
    wave_ref, own_s_ref, late_ref, even, odd, coef_ref, coef_strip_ref, s_ref, ss_ref, hist_ref,
    adjoint_ref, grad_hbm, adjoint_hbm,
    p_ref, spread_ref, edge_ref, flux_ref, grad_ref, sems,
):
    copies = [pltpu.make_async_copy(adjoint_ref, adjoint_hbm, sems.at[0])]
    copies[0].start()

    def send(index, kind, first, count):
        planes = pl.ds(first, count)
        copy = pltpu.make_async_copy(
            grad_ref.at[kind, planes], grad_hbm.at[kind, planes], sems.at[index]
        )
        copy.start()
        copies.append(copy)

    cut_up, cut_down = cut_flags()
    side = sides()
    messages = (even, odd)
    tiles, own_tiles = WAVE_SIDE[1], WAVE_OWN[1]
    side_strip = tiles + tile_rows(WAVE_TILES)

    def initial(index, x):
        layout = (
            ((messages, 0, 4), (messages, tiles, 0, 3)),
            ((messages, PLANES, 3), (messages, tiles, 3, 2)),
        )[index]
        own = ((wave_ref, 0), (own_s_ref, 0))[index]
        value = widened(own, (late_ref, own_tiles + 32 * index), x, layout, side)
        if index == 1:
            value = less_plane_below(
                value, x, late_ref, WAVE_OWN, messages, (WAVE_SIDE, WAVE_TILES), side
            )
        return value

    own_strip = late_ref[WAVE_OWN[2] : WAVE_OWN[2] + EY]
    p_s, s_s = (
        whole_strip(own_strip, messages, side_strip, slot, side) for slot in range(2)
    )
    s_s = s_s - strip_below(own_strip, messages, side_strip, 2, side)
    stiff_s, buoy_s, damp_s = coef_strip_ref[0], coef_strip_ref[1], coef_strip_ref[2]

    for step in range(1, STEPS + 1):
        flux_s, spread = strip_flux(p_s, buoy_s)
        edges = cut_edges(p_s, flux_s, cut_up, cut_down)
        if step < STEPS:
            s_s = s_s - spread
            p_s = damp_s * (p_s - stiff_s * s_s) + ss_ref[step - 1]
        for x in range(step, EX - step):
            edge_ref[step - 1, x] = plane_edge(edges, x)
    for x in range(EX):
        p_ref[x] = initial(0, x)

    for step in range(1, STEPS + 1):
        k = step - 1
        for x in range(step - 1, EX - step):
            p, buoyancy = p_ref[x], coef_ref[1, x]
            slopes = [p_ref[x + 1] - p]
            if x >= step:
                slopes += [y_up(p) - p, z_up(p, edge_ref[step - 1, x]) - p]
            for axis, slope in enumerate(slopes):
                flux_ref[axis, x] = buoyancy * slope
            if BX <= x < 2 * BX:
                place = x - BX
                term = hist_ref[k, 1, place] * slopes[0][0:BY]
                term = term + hist_ref[k, 2, place] * slopes[1][0:BY]
                term = term + hist_ref[k, 3, place] * slopes[2][0:BY]
                grad_ref[1, place] = -term if k == 0 else grad_ref[1, place] - term
        if step == STEPS:
            send(1, 1, 0, BX)

        for x in range(step, EX - step):
            flux_y, flux_z = flux_ref[1, x], flux_ref[2, x]
            spread = (flux_ref[0, x] - flux_ref[0, x - 1]) + (flux_y - y_down(flux_y))
            spread = spread + (flux_z - z_down(flux_z, edge_ref[step - 1, x]))
            spread = (initial(1, x) if step == 1 else spread_ref[x]) - spread
            if step < STEPS:
                spread_ref[x] = spread
                p_ref[x] = (
                    coef_ref[2, x] * (p_ref[x] - coef_ref[0, x] * spread)
                    + s_ref[k, x - SOURCE_PLANES[0]]
                )
            if BX <= x < 2 * BX:
                place = x - BX
                term = hist_ref[k, 0, place] * spread[0:BY]
                grad_ref[0, place] = -term if k == 0 else grad_ref[0, place] - term
                if step == STEPS:
                    send(2 + place, 0, place, 1)
    for copy in copies:
        copy.wait()


def shape(*dims):
    return jax.ShapeDtypeStruct(dims, F32)


def call(kernel, outs, operands, scratch, places, micros=0.1, out_place="v"):
    spaces = {"h": pltpu.HBM, "a": pl.ANY, "v": pltpu.VMEM}
    operands = [
        pltpu.with_memory_space_constraint(operand, pltpu.HBM) if place == "h" else operand
        for operand, place in zip(operands, places)
    ]
    return pl.pallas_call(
        kernel,
        out_shape=outs,
        in_specs=[pl.BlockSpec(memory_space=spaces[place]) for place in places],
        out_specs=[pl.BlockSpec(memory_space=spaces[out_place])] * len(outs),
        scratch_shapes=scratch,
        compiler_params=pltpu.CompilerParams(vmem_limit_bytes=VMEM_LIMIT),
        cost_estimate=pl.CostEstimate(
            flops=0, bytes_accessed=int(3.69e6 * micros), transcendentals=0
        ),
    )(*operands)


def from_sides(sends, axes):
    count = lax.axis_size("gy")

    def route(offset):
        pairs = []
        for target in range(count):
            source = target + offset
            if 0 <= source < count:
                if "gz" in axes:
                    pairs += [(2 * source + z, 2 * target + 1 - z) for z in range(2)]
                else:
                    pairs.append((source, target))
        return pairs

    if count == 2:
        both = lax.ppermute(sends[0], axes, route(1) + route(-1))
        return both, both
    upward, downward = sends
    return lax.ppermute(downward, axes, route(1)), lax.ppermute(upward, axes, route(-1))


def rotated(array, axis, offset):
    count = lax.axis_size(axis)
    return lax.ppermute(array, axis, [((i + offset) % count, i) for i in range(count)])


def paired(array, odd):
    count = lax.axis_size("gx")
    pairs = []
    for i in range(count):
        partner = ((i - 1) ^ 1) + 1 if odd else i ^ 1
        pairs.append((partner if 0 <= partner < count else i, i))
    return lax.ppermute(array, "gx", pairs)


def local(
    stored, adjoint_end, labels, tissue, source_cells, source_wave, receiver_cells, receiver_wave
):
    assert lax.axis_size("gz") == 2 and labels.shape == (BX, BY, BZ) and tissue.shape[1] == 8
    half = lax.axis_size("gx") // 2
    arguments = [
        stored, adjoint_end, labels, tissue,
        receiver_cells.T, receiver_wave, source_cells.T, source_wave,
    ]
    ways = 1 if lax.axis_size("gy") == 2 else 2
    wave, ql, t, last_x, last_y, strips, table, receivers, receiver_wave, sources, source_wave, *sends = call(
        load_kernel,
        [
            shape(2 * PLANES + BY, BZ),
            shape(2 * PLANES, BZ),
            shape(PLANES, BZ),
            shape(BY, BZ),
            shape(2 * BX * 8, BZ),
            shape(3 * BY, BZ),
            shape(24, BZ),
        ]
        + [jax.ShapeDtypeStruct(array.shape, array.dtype) for array in arguments[4:]]
        + [shape(20 * 8, BZ)] * ways
        + [shape(2 * 8, BZ)] * ways,
        arguments,
        [
            pltpu.VMEM(stored.shape, F32),
            pltpu.VMEM(adjoint_end.shape, F32),
            pltpu.VMEM(labels.shape, jnp.int32),
            pltpu.SMEM(tissue.shape, F32),
            pltpu.SemaphoreType.DMA,
        ],
        "hhhhhhhh",
        1.4,
    )
    from_up, from_down = from_sides(sends[:ways], "gy")
    other = rotated(strips, "gz", 1)
    corner_up, corner_down = from_sides(sends[ways:], ("gy", "gz"))
    wave = rotated(wave, "gx", half)
    rb, rsb = call(
        late_kernel,
        [shape(2, EX * EY, BZ), shape(2, EY, BZ)],
        [receivers, receiver_wave],
        [],
        "vv",
        1.2,
    )
    early_planes, source_planes = (last - first for first, last in (EARLY_PLANES, SOURCE_PLANES))
    late, adj_late = call(
        merge_kernel,
        [shape(tile_rows(9) + EY + 8 + SPARE, BZ), shape(ADJ_OWN[2] + EY, BZ)],
        [from_up, from_down, corner_up, corner_down, strips, other, t, last_x, last_y, rsb],
        [pltpu.VMEM((WAVE_OWN[2], BZ), F32)],
        "vvvvvvvvva",
    )
    late = rotated(late, "gx", half)
    ra, rsa = call(
        early_kernel,
        [shape(2, early_planes * EY, BZ), shape(2, EY, BZ)],
        [receivers, receiver_wave, adj_late],
        [],
        "vva",
        1.0,
    )
    ra, rb = ra.reshape(2, early_planes, EY, BZ), rb.reshape(2, EX, EY, BZ)
    even, odd = call(
        adjoint_join_kernel,
        [shape(ADJ_SIDE[1] + tile_rows(ADJ_TILES) + EY + 2 * PLANES, BZ)] * 2,
        [ql, adj_late],
        [],
        "vv",
    )
    even, odd = paired(even, False), paired(odd, True)
    src, src_strip = call(
        source_kernel,
        [shape(STEPS - 1, source_planes * EY, BZ), shape(STEPS - 1, EY, BZ)],
        [sources, source_wave, adj_late],
        [],
        "vva",
        0.5,
    )
    src = src.reshape(STEPS - 1, source_planes, EY, BZ)
    own_s, own_late, wave_even, wave_odd = call(
        join_kernel,
        [shape(PLANES, BZ), shape(WAVE_OWN[2] + EY, BZ)]
        + [shape(WAVE_SIDE[1] + tile_rows(WAVE_TILES) + EY, BZ)] * 2,
        [wave, late],
        [],
        "vv",
    )
    wave_even, wave_odd = paired(wave_even, False), paired(wave_odd, True)
    adjoint_out, hist, coef, coef_strip = call(
        adjoint_kernel,
        [
            shape(4, BX, BY, BZ),
            shape(STEPS, 4, BX, BY, BZ),
            shape(3, EX, EY, BZ),
            shape(3, EY, BZ),
        ],
        [ql, adj_late, even, odd, adjoint_end, ra, rsa, rb, rsb, table],
        [pltpu.VMEM((EX, EY, BZ), F32)] * 4
        + [
            pltpu.VMEM((STEPS, EX, EY, BZ), F32),
            pltpu.VMEM((3, EX, EY, BZ), F32),
            pltpu.SemaphoreType.DMA,
        ],
        "vvvvhvvvvv",
        3.9,
    )
    return call(
        forward_kernel,
        [shape(2, BX, BY, BZ), shape(4, BX, BY, BZ)],
        [
            wave, own_s, own_late, wave_even, wave_odd, coef, coef_strip, src, src_strip, hist,
            adjoint_out,
        ],
        [pltpu.VMEM((EX, EY, BZ), F32)] * 2
        + [
            pltpu.VMEM((STEPS, EX, EY, BZ), F32),
            pltpu.VMEM((3, EX, EY, BZ), F32),
            pltpu.VMEM((2, BX, BY, BZ), F32),
            pltpu.SemaphoreType.DMA((2 + BX,)),
        ],
        "vvvvvvvvvvv",
        2.5,
        "a",
    )


def solution(mesh):
    return jax.shard_map(
        local,
        mesh=mesh,
        in_specs=(
            P("shot", "gx", "gy", "gz"),
            P("shot", "gx", "gy", "gz"),
            P("gx", "gy", "gz"),
            P(),
            P("shot", None),
            P(None, "shot"),
            P(),
            P(None, "shot"),
        ),
        out_specs=(P("shot", "gx", "gy", "gz"), P("shot", "gx", "gy", "gz")),
        check_vma=False,
    )
```

```python
import jax
import jax.numpy as jnp
from jax import lax
from jax.experimental import pallas as pl
from jax.experimental.pallas import tpu as pltpu
from jax.sharding import PartitionSpec as P

STEPS = 4
MARGIN = 4
BX, BY, BZ = 4, 32, 128
EX, EY = BX + 2 * MARGIN, BY + 2 * MARGIN
STRIP = 2 * MARGIN
F32 = jnp.float32
BF16 = jnp.bfloat16
VMEM_LIMIT = 16 * 1024 * 1024
PLANES = BX * BY
WAVE_OWN = (0, BY, BY + 9 * 8)
FIX_LANE = 3 * BX * STRIP
SPARE = 64
ADJ_OWN = (PLANES, PLANES + BY, PLANES + BY + 13 * 8)
WAVE_SIDE = (PLANES + 3 * BY, PLANES + 4 * BY)
ADJ_SIDE = (3 * BY, 4 * BY)
WAVE_TILES, ADJ_TILES = 6, 9


def lanes(shape):
    return lax.broadcasted_iota(jnp.int32, shape, len(shape) - 1)


def rows(shape):
    return lax.broadcasted_iota(jnp.int32, shape, len(shape) - 2)


def run(copies):
    for copy in copies:
        copy.start()
    for copy in copies:
        copy.wait()


def coefficients(labels, table_ref):
    result = [jnp.zeros(labels.shape, F32) for _ in range(3)]
    for index in range(8):
        picked = labels == float(index + 1)
        for kind in range(3):
            row = kind * 8 + index
            result[kind] = jnp.where(picked, table_ref[row : row + 1], result[kind])
    return result


def buoyancy_of(labels, table_ref):
    result = jnp.zeros(labels.shape, F32)
    for index in range(8):
        result = jnp.where(labels == float(index + 1), table_ref[8 + index : 9 + index], result)
    return result


def half_turn(tile):
    return pltpu.roll(tile, MARGIN, 0)


def load_kernel(
    stored_hbm, adj_hbm, lab_hbm, tissue_hbm, rc_hbm, rw_hbm, sc_hbm, sw_hbm,
    wave_ref, ql_ref, t_ref, last_x_ref, last_y_ref, strip_ref, table_ref,
    rc_ref, rw_ref, sc_ref, sw_ref, *rest,
):
    *sends, stored, adj, lab, tissue, sem = rest
    run([
        pltpu.make_async_copy(source, target, sem)
        for source, target in (
            (stored_hbm, stored), (adj_hbm, adj), (lab_hbm, lab), (tissue_hbm, tissue),
            (rc_hbm, rc_ref), (rw_hbm, rw_ref), (sc_hbm, sc_ref), (sw_hbm, sw_ref),
        )
    ])
    for index in range(tissue.shape[1]):
        speed = jnp.full((1, BZ), tissue[0, index], F32)
        density = jnp.full((1, BZ), tissue[1, index], F32)
        table_ref[index : index + 1] = density * speed
        table_ref[8 + index : 9 + index] = speed / density
        table_ref[16 + index : 17 + index] = 1.0 - jnp.full((1, BZ), tissue[2, index], F32)
    gy, gz = lax.axis_index("gy"), lax.axis_index("gz")
    lane = lanes((BY, BZ))
    row = rows((BY, BZ))
    tile_row = rows((8, BZ))
    strips = [jnp.zeros((BY, BZ), F32) for _ in range(3)]
    tiles = [None] * 39
    previous = [None, None]

    def edge_tile(block):
        return jnp.where(tile_row < MARGIN, block[0:8], block[BY - 8 : BY])

    for x in range(BX):
        labels = lab[x].astype(F32) + 1.0
        buoyancy = buoyancy_of(labels, table_ref)
        plane = slice(x * BY, x * BY + BY)
        fields = [stored[index, x] for index in range(4)] + [adj[0, x]]
        fields += [buoyancy * adj[index, x] for index in range(1, 4)] + [labels]
        wave_ref[plane] = fields[0]
        ql_ref[plane] = fields[4]
        ql_ref[PLANES + x * BY : PLANES + x * BY + BY] = labels
        for index, block in enumerate(fields):
            tiles[index * BX + x] = edge_tile(block)
            group, slot = divmod(index, 4)
            base = slot * BX * STRIP + x * STRIP
            rolled = pltpu.roll(block, base + MARGIN, 1)
            first = base + MARGIN * gz
            strips[group] = jnp.where(
                (lane >= first) & (lane < first + MARGIN), rolled, strips[group]
            )
        for kind, (target, base) in enumerate(((wave_ref, PLANES), (t_ref, 0))):
            vx, vy, vz = fields[4 * kind + 1 : 4 * kind + 4]
            spread = vx if x == 0 else vx - previous[kind]
            spread = spread + (vy - jnp.where(row == 0, 0.0, pltpu.roll(vy, 1, 0)))
            spread = spread + (vz - jnp.where(lane == 0, 0.0, pltpu.roll(vz, 1, 1)))
            target[base + x * BY : base + x * BY + BY] = spread
            previous[kind] = vx
            index = (kind * BX + x) * 8
            last_y_ref[index : index + 8] = vy[BY - 8 : BY]
    wave_ref[2 * PLANES : 2 * PLANES + BY] = previous[0]
    wave_ref[2 * PLANES + BY :] = jnp.zeros((SPARE // 2, BZ), F32)
    last_x_ref[...] = previous[1]
    for group in range(3):
        strip_ref[group * BY : group * BY + BY] = strips[group]
        tiles[9 * BX + group] = edge_tile(strips[group])

    def joined(first, second):
        second = first if second is None else second
        upward = jnp.where(tile_row < MARGIN, half_turn(first), second)
        downward = jnp.where(tile_row < MARGIN, first, half_turn(second))
        if len(sends) == 2:
            return (jnp.where(gy == 0, upward, downward),)
        return upward, downward

    tiles.append(None)
    half = len(sends) // 2
    for place in range(20):
        for target, tile in zip(sends[:half], joined(tiles[2 * place], tiles[2 * place + 1])):
            target[place * 8 : place * 8 + 8] = tile
    for place in range(2):
        first = tiles[9 * BX + 2 * place]
        for target, tile in zip(sends[half:], joined(first, tiles[9 * BX + 2 * place + 1])):
            target[place * 8 : place * 8 + 8] = tile


def copy_rows(target, base, source, first, count):
    target[base : base + count] = source[pl.ds(pl.multiple_of(first, 8), count)]
    return base + count


def halved():
    return lax.axis_size("gy") == 2


def tile_rows(count):
    return (count + 1) // 2 * 8 if halved() else count * 8


def put_tiles(target, base, source, firsts):
    tiles = [source[pl.ds(pl.multiple_of(first, 8), 8)] for first in firsts]
    if halved():
        upper = lax.axis_index("gy") == 0
        row = rows((8, BZ))
        pairs = [(tiles[i], tiles[min(i + 1, len(tiles) - 1)]) for i in range(0, len(tiles), 2)]
        tiles = [
            jnp.where(
                row < MARGIN,
                jnp.where(upper, first, half_turn(first)),
                jnp.where(upper, half_turn(second), second),
            )
            for first, second in pairs
        ]
    for place, tile in enumerate(tiles):
        target[base + place * 8 : base + place * 8 + 8] = tile
    return base + 8 * len(tiles)


def pair_planes():
    parity = lax.rem(lax.axis_index("gx"), 2)
    return 1 - parity, parity


def merge_kernel(
    from_up, from_down, corner_up, corner_down, strip_ref, other_ref,
    t_ref, last_x_ref, last_y_ref, _,
    late_ref, adj_ref,
    wave_ref,
):
    gy = lax.axis_index("gy")
    tile_row = rows((8, BZ))
    row, lane = rows((BY, BZ)), lanes((BY, BZ))
    take_up = (tile_row < MARGIN) & (gy < lax.axis_size("gy") - 1)
    take_down = (tile_row >= MARGIN) & (gy > 0)
    _, cut_down = cut_flags()

    def halo(up, down, index):
        place, second = divmod(index, 2)
        sl = slice(place * 8, place * 8 + 8)
        above = half_turn(up[sl]) if second else up[sl]
        below = down[sl] if second else half_turn(down[sl])
        return jnp.where(take_up, above, jnp.where(take_down, below, 0.0))

    wide = []
    for group in range(3):
        sl = slice(group * BY, group * BY + BY)
        tile = halo(from_up, from_down, 9 * BX + group) + halo(corner_up, corner_down, group)
        wide.append(jnp.concatenate([strip_ref[sl] + other_ref[sl], tile], 0))
    strip_lane = lanes((EY, BZ))

    def strip_field(index):
        group, slot = divmod(index, 4)
        moved = pltpu.roll(wide[group], (BZ - slot * BX * STRIP) % BZ, 1) if slot else wide[group]
        return jnp.where(strip_lane < BX * STRIP, moved, 0.0)

    last_lanes = (BX - 1) * STRIP
    fix_row = jnp.zeros((8, BZ), F32)
    fix_lane = jnp.zeros((BY, BZ), F32)
    for kind, target in enumerate((wave_ref, adj_ref)):
        first = 4 * kind
        planes_end, x_end, tiles_end = (WAVE_OWN, ADJ_OWN)[kind]
        vx, vy, vz = (strip_field(first + 1 + axis) for axis in range(3))
        spread = vx - jnp.where(strip_lane < STRIP, 0.0, pltpu.roll(vx, STRIP, 1))
        spread = (spread + (vy - y_down(vy))) + (vz - pltpu.roll(vz, 1, 1))
        strip = strip_field(first)
        strip = strip + pltpu.roll(jnp.where(strip_lane < BX * STRIP, spread, 0.0), BX * STRIP, 1)
        last_slot = 2
        if kind == 1:
            strip = strip + pltpu.roll(strip_field(8), 2 * BX * STRIP, 1)
            last_slot = 3
        last = jnp.where(strip_lane >= last_lanes, vx, 0.0)
        strip = strip + pltpu.roll(last, last_slot * BX * STRIP - last_lanes, 1)

        vx_before = None
        for x in range(BX):
            vx_t, vy_t, vz_t = (
                halo(from_up, from_down, (first + 1 + axis) * BX + x) for axis in range(3)
            )
            below_z = pltpu.roll(vz, (BZ - (x * STRIP + MARGIN - 1)) % BZ, 1) * cut_down
            last_y = last_y_ref[(kind * BX + x) * 8 : (kind * BX + x) * 8 + 8]
            y_before = jnp.where(
                tile_row == 0, pltpu.roll(last_y, 1, 0), pltpu.roll(vy_t, 1, 0)
            )
            z_before = jnp.where(lane[0:8] == 0, below_z[BY:EY], pltpu.roll(vz_t, 1, 1))
            spread = vx_t if x == 0 else vx_t - vx_before
            spread = (spread + (vy_t - y_before)) + (vz_t - z_before)
            vx_before = vx_t
            if kind == 0:
                fix_row = jnp.where(tile_row == x, vy_t[7:8], fix_row)
                moved = pltpu.roll(below_z[0:BY], FIX_LANE + x, 1)
                fix_lane = jnp.where(lane == FIX_LANE + x, moved, fix_lane)
            else:
                block = t_ref[x * BY : x * BY + BY]
                block = block - jnp.where(row == 0, vy_t[7:8], 0.0)
                block = block - jnp.where(lane == 0, below_z[0:BY], 0.0)
                target[x * BY : x * BY + BY] = block
            base = x_end + x * 8
            target[base : base + 8] = halo(from_up, from_down, first * BX + x)
            target[base + 32 : base + 40] = spread
            if kind == 1:
                target[base + 64 : base + 72] = halo(from_up, from_down, 8 * BX + x)
        target[tiles_end - 8 : tiles_end] = vx_before
        if kind == 0:
            base = put_tiles(late_ref, 0, wave_ref, range(x_end, tiles_end, 8))
            late_ref[base : base + BY] = strip[0:BY] + fix_lane
            late_ref[base + BY : base + EY] = strip[BY:EY]
            late_ref[base + EY : base + EY + 8] = fix_row
            late_ref[base + EY + 8 : base + EY + 8 + SPARE] = jnp.zeros((SPARE, BZ), F32)
        else:
            target[planes_end:x_end] = last_x_ref[...]
            target[tiles_end : tiles_end + EY] = strip


def adjoint_join_kernel(ql_ref, adj_ref, even_ref, odd_ref):
    planes_end, x_end, tiles_end = ADJ_OWN
    for target, first in zip((even_ref, odd_ref), pair_planes()):
        base = copy_rows(target, 0, adj_ref, first * BY, 3 * BY)
        base = copy_rows(target, base, adj_ref, planes_end, BY)
        near = [x_end + (first + plane) * 8 for plane in range(3)]
        nearest = [x_end + 32 + first * 16 + plane * 8 for plane in range(2)]
        firsts = near + nearest + [start + 64 for start in near] + [tiles_end - 8]
        base = put_tiles(target, base, adj_ref, firsts)
        base = copy_rows(target, base, adj_ref, tiles_end, EY)
        copy_rows(target, base, ql_ref, 0, 2 * PLANES)


def unpacked(tile, place):
    upper = lax.axis_index("gy") == 0
    turned = half_turn(tile)
    tile = jnp.where(upper, turned, tile) if place % 2 else jnp.where(upper, tile, turned)
    return jnp.where((rows((8, BZ)) < MARGIN) == upper, tile, 0.0)


def join_kernel(wave_ref, late_ref, s_ref, own_ref, even_ref, odd_ref):
    planes_end, x_end, tiles_end = WAVE_OWN
    own_ref[planes_end:x_end] = wave_ref[2 * PLANES : 2 * PLANES + BY]
    for place in range((tiles_end - x_end) // 8):
        if halved():
            tile = unpacked(late_ref[place // 2 * 8 : place // 2 * 8 + 8], place)
        else:
            tile = late_ref[place * 8 : place * 8 + 8]
        own_ref[x_end + place * 8 : x_end + place * 8 + 8] = tile
    strip = tile_rows((tiles_end - x_end) // 8)
    own_ref[tiles_end : tiles_end + EY] = late_ref[strip : strip + EY]
    row, lane = rows((BY, BZ)), lanes((BY, BZ))
    fix_lane = late_ref[strip : strip + BY]
    for x in range(BX):
        block = wave_ref[PLANES + x * BY : PLANES + x * BY + BY]
        fix_row = late_ref[strip + EY + x : strip + EY + x + 1]
        block = block - jnp.where(row == 0, fix_row, 0.0)
        block = block - jnp.where(lane == 0, pltpu.roll(fix_lane, BZ - FIX_LANE - x, 1), 0.0)
        s_ref[x * BY : x * BY + BY] = block
    for target, first in zip((even_ref, odd_ref), pair_planes()):
        base = copy_rows(target, 0, wave_ref, 0, PLANES)
        base = copy_rows(target, base, s_ref, first * BY, 3 * BY)
        base = copy_rows(target, base, own_ref, planes_end, BY)
        near = [x_end + (first + plane) * 8 for plane in range(3)]
        nearest = [x_end + 32 + first * 16 + plane * 8 for plane in range(2)]
        base = put_tiles(target, base, own_ref, near + nearest + [tiles_end - 8])
        copy_rows(target, base, own_ref, tiles_end, EY)


def split(values):
    high = values.astype(BF16)
    rest = values - high.astype(F32)
    middle = rest.astype(BF16)
    low = (rest - middle.astype(F32)).astype(BF16)
    return high, middle, low


def places(cells, sl):
    gx, gy, gz = (lax.axis_index(name) for name in ("gx", "gy", "gz"))
    cut = BZ * lax.axis_size("gz") // 2 - MARGIN
    cell_x = cells[0:1, sl] - (gx * BX - MARGIN)
    cell_y = cells[1:2, sl] - gy * BY
    cell_z = cells[2:3, sl]
    in_x = (cell_x >= 0) & (cell_x < EX)
    in_y = (cell_y >= -MARGIN) & (cell_y < BY + MARGIN)
    row = jnp.where(cell_y < 0, cell_y + EY, cell_y)
    flat = jnp.where(in_x & in_y, cell_x * EY + row, -1)
    row = jnp.where(in_y, row, -1)
    zz = cell_z - cut
    in_strip = in_x & (zz >= 0) & (zz < STRIP)
    strip_lane = jnp.where(in_strip, cell_x * STRIP + zz, -1)
    return flat, cell_z - gz * BZ, row, strip_lane


def hits(count, index):
    return rows((count, index.shape[1])) == index


def product(left, right):
    return lax.dot_general(
        left, right, (((1,), (1,)), ((), ())), preferred_element_type=F32
    )


def inject_points(cells, wave_ref, width, waves, planes, out_ref, strip_out_ref):
    count, low, total_rows = len(waves), planes[0] * EY, (planes[1] - planes[0]) * EY
    for start in range(0, cells.shape[1], width):
        sl = slice(start, start + width)
        flat, z, row, strip_lane = places(cells, sl)
        here = hits(total_rows, flat - low).astype(F32).astype(BF16)
        at_strip = hits(BZ, strip_lane).astype(F32).astype(BF16)
        at_z, at_row = hits(BZ, z), hits(EY, row)
        total = strip_total = None
        parts = [split(wave_ref[wave : wave + 1, sl]) for wave in waves]
        for part in range(3):
            amounts = [parts[wave][part].astype(F32) for wave in range(count)]
            right = jnp.concatenate([jnp.where(at_z, a, 0.0) for a in amounts], 0).astype(BF16)
            left = jnp.concatenate([jnp.where(at_row, a, 0.0) for a in amounts], 0).astype(BF16)
            term, strip_term = product(here, right), product(left, at_strip)
            total = term if part == 0 else total + term
            strip_total = strip_term if part == 0 else strip_total + strip_term
        for wave in range(count):
            value = total[:, wave * BZ : wave * BZ + BZ]
            strip_value = strip_total[wave * EY : wave * EY + EY]
            if start > 0:
                value = value + out_ref[wave]
                strip_value = strip_value + strip_out_ref[wave]
            out_ref[wave] = value
            strip_out_ref[wave] = strip_value


LATE_PLANES, EARLY_PLANES, SOURCE_PLANES = (0, EX), (2, EX - 2), (1, EX - 1)


def late_kernel(receivers, receiver_wave, r_ref, rs_ref):
    inject_points(receivers, receiver_wave, 256, (2, 3), LATE_PLANES, r_ref, rs_ref)


def early_kernel(receivers, receiver_wave, _, r_ref, rs_ref):
    inject_points(receivers, receiver_wave, 256, (0, 1), EARLY_PLANES, r_ref, rs_ref)


def source_kernel(sources, source_wave, _, s_ref, ss_ref):
    width = sources.shape[1]
    inject_points(sources, source_wave, width, (0, 1, 2), SOURCE_PLANES, s_ref, ss_ref)


def strip_of(packed, block, slot):
    lane = lanes(packed.shape)
    width = BX * STRIP
    shift = (block * width - slot * width) % BZ
    moved = pltpu.roll(packed, shift, 1) if shift else packed
    return jnp.where((lane >= block * width) & (lane < (block + 1) * width), moved, 0.0)


def y_up(v):
    return pltpu.roll(v, EY - 1, 0)


def y_down(v):
    return pltpu.roll(v, 1, 0)


def z_up(v, edge):
    return jnp.where(lanes(v.shape) == BZ - 1, edge, pltpu.roll(v, BZ - 1, 1))


def z_down(v, edge):
    return jnp.where(lanes(v.shape) == 0, edge, pltpu.roll(v, 1, 1))


def cut_edges(values, flux_z, cut_up, cut_down):
    place = lax.rem(lanes(values.shape), STRIP)
    above = jnp.where(place == MARGIN, values * cut_up, 0.0)
    below = jnp.where(place == MARGIN - 1, flux_z * cut_down, 0.0)
    return pltpu.roll(above, BZ - 2, 1) + below


def plane_edge(edges, x):
    return pltpu.roll(edges, (BZ - (x * STRIP + MARGIN - 1)) % BZ, 1)


def strip_flux(values, buoyancy):
    flux_x = buoyancy * (pltpu.roll(values, BZ - STRIP, 1) - values)
    flux_y = buoyancy * (y_up(values) - values)
    flux_z = buoyancy * (pltpu.roll(values, BZ - 1, 1) - values)
    spread = (flux_x - pltpu.roll(flux_x, STRIP, 1)) + (flux_y - y_down(flux_y))
    return flux_z, spread + (flux_z - pltpu.roll(flux_z, 1, 1))


def cut_flags():
    gz, half = lax.axis_index("gz"), lax.axis_size("gz") // 2
    return jnp.where(gz == half - 1, 1.0, 0.0), jnp.where(gz == half, 1.0, 0.0)


def sides():
    gx = lax.axis_index("gx")
    low = jnp.where(gx > 0, 1.0, 0.0)
    high = jnp.where(gx < lax.axis_size("gx") - 1, 1.0, 0.0)
    return low, high, lax.rem(gx, 2) == 0


def from_side(messages, first, count, block, side):
    even, odd = (message[first : first + count] for message in messages)
    low, high, even_above = side
    if block == 0:
        return jnp.where(even_above, odd, even) * low
    return jnp.where(even_above, even, odd) * high


def side_tile(messages, base, place, block, side):
    if not halved():
        return from_side(messages, base + place * 8, 8, block, side)
    tile = from_side(messages, base + place // 2 * 8, 8, block, side)
    return unpacked(tile, place)


def side_place(wanted, plane, block):
    planes = range(BX - wanted, BX) if block == 0 else range(wanted)
    return planes.index(plane) if plane in planes else None


def widened(own, own_tiles, x, layout, side):
    block, plane = divmod(x, BX)
    if block == 1:
        main = own[0][own[1] + plane * BY : own[1] + plane * BY + BY]
        tile = own_tiles[0][own_tiles[1] + plane * 8 : own_tiles[1] + plane * 8 + 8]
        return jnp.concatenate([main, tile], 0)
    (messages, base, wanted), (tile_messages, tile_base, tile_place, tile_wanted) = layout
    main, tile = jnp.zeros((BY, BZ), F32), jnp.zeros((8, BZ), F32)
    place = side_place(wanted, plane, block)
    if place is not None:
        main = from_side(messages, base + place * BY, BY, block, side)
    place = side_place(tile_wanted, plane, block)
    if place is not None:
        tile = side_tile(tile_messages, tile_base, tile_place + place, block, side)
    return jnp.concatenate([main, tile], 0)


def less_plane_below(value, x, own_ref, own_rows, messages, side_layout, side):
    if x == BX:
        (planes_end, x_end), count = side_layout
        main = from_side(messages, planes_end, BY, 0, side)
        tile = side_tile(messages, x_end, count - 1, 0, side)
    elif x == 2 * BX:
        planes_end, _, tiles_end = own_rows
        high = side[1]
        main = own_ref[planes_end : planes_end + BY] * high
        tile = own_ref[tiles_end - 8 : tiles_end] * high
    else:
        return value
    return value - jnp.concatenate([main, tile], 0)


def strip_below(own, messages, first, slot, side):
    lane = lanes(own.shape)
    width = BX * STRIP
    low = from_side(messages, first, EY, 0, side)
    low = pltpu.roll(low, (width - slot * width) % BZ, 1)
    own = pltpu.roll(own * side[1], (2 * width - slot * width) % BZ, 1)
    in_own = (lane >= width) & (lane < width + STRIP)
    in_high = (lane >= 2 * width) & (lane < 2 * width + STRIP)
    return jnp.where(in_own, low, jnp.where(in_high, own, 0.0))


def whole_strip(own, messages, first, slot, side):
    low = from_side(messages, first, EY, 0, side)
    high = from_side(messages, first, EY, 2, side)
    return strip_of(low, 0, slot) + strip_of(own, 1, slot) + strip_of(high, 2, slot)


def adjoint_kernel(
    ql_ref, late_ref, even, odd, adj_hbm, ra_ref, rsa_ref, rb_ref, rsb_ref,
    table_ref,
    out_ref, hist_ref, coef_ref, coef_strip_ref,
    q_ref, t_ref, u_ref, scale_ref, edge_ref, flux_ref, w_sem,
):
    w_copy = pltpu.make_async_copy(adj_hbm.at[pl.ds(1, 3)], out_ref.at[pl.ds(1, 3)], w_sem)
    w_copy.start()
    cut_up, cut_down = cut_flags()
    side = sides()
    messages = (even, odd)
    r_refs = ((ra_ref, 0), (ra_ref, 1), (rb_ref, 0), (rb_ref, 1))
    rs_refs = ((rsa_ref, 0), (rsa_ref, 1), (rsb_ref, 0), (rsb_ref, 1))
    tiles, own_tiles = ADJ_SIDE[1], ADJ_OWN[1]
    side_strip = tiles + tile_rows(ADJ_TILES)
    raws = side_strip + EY

    def initial(index, x):
        own = ((ql_ref, 0), (late_ref, 0), (ql_ref, PLANES))[index]
        layout = (
            ((messages, raws, 4), (messages, tiles, 0, 3)),
            ((messages, 0, 3), (messages, tiles, 3, 2)),
            ((messages, raws + PLANES, 4), (messages, tiles, 5, 3)),
        )[index]
        value = widened(own, (late_ref, own_tiles + 32 * index), x, layout, side)
        if index == 1:
            value = less_plane_below(
                value, x, late_ref, ADJ_OWN, messages, (ADJ_SIDE, ADJ_TILES), side
            )
        return value

    for x in range(EX):
        stiff, buoy, damp = coefficients(initial(2, x), table_ref)
        coef_ref[0, x], coef_ref[1, x], coef_ref[2, x] = stiff, buoy, damp
        scale_ref[x] = stiff * damp
    own_strip = late_ref[ADJ_OWN[2] : ADJ_OWN[2] + EY]
    q_s, t_s, label_s = (
        whole_strip(own_strip, messages, side_strip, slot, side) for slot in range(3)
    )
    t_s = t_s - strip_below(own_strip, messages, side_strip, 3, side)
    stiff_s, buoy_s, damp_s = coefficients(label_s, table_ref)
    scale_s = stiff_s * damp_s
    coef_strip_ref[0], coef_strip_ref[1], coef_strip_ref[2] = stiff_s, buoy_s, damp_s
    w_copy.wait()

    for step in range(1, STEPS + 1):
        rs_ref, place = rs_refs[STEPS - step]
        q_s = q_s + rs_ref[place]
        u_s = scale_s * q_s
        flux_s, spread = strip_flux(u_s, buoy_s)
        t_s = t_s + spread
        q_s = damp_s * q_s + t_s
        edges = cut_edges(u_s, flux_s, cut_up, cut_down)
        for x in range(step, EX - step):
            edge_ref[step - 1, x] = plane_edge(edges, x)

    for step in range(1, STEPS + 1):
        k = STEPS - step
        r_ref, place = r_refs[k]
        r_first = (EARLY_PLANES if k < 2 else LATE_PLANES)[0]

        for x in range(step - 1, EX - step + 1):
            q = (initial(0, x) if step == 1 else q_ref[x]) + r_ref[place, x - r_first]
            q_ref[x] = q
            u_ref[x] = scale_ref[x] * q

        for x in range(step - 1, EX - step):
            u, buoyancy = u_ref[x], coef_ref[1, x]
            slopes = [u_ref[x + 1] - u]
            if x >= step:
                slopes += [y_up(u) - u, z_up(u, edge_ref[step - 1, x]) - u]
            for axis, slope in enumerate(slopes):
                flux_ref[axis, x] = buoyancy * slope
            if BX <= x < 2 * BX:
                for axis, slope in enumerate(slopes):
                    w = out_ref[1 + axis, x - BX] + slope[0:BY]
                    out_ref[1 + axis, x - BX] = w
                    hist_ref[k, 1 + axis, x - BX] = w

        for x in range(step, EX - step):
            flux_y, flux_z = flux_ref[1, x], flux_ref[2, x]
            spread = (flux_ref[0, x] - flux_ref[0, x - 1]) + (flux_y - y_down(flux_y))
            spread = spread + (flux_z - z_down(flux_z, edge_ref[step - 1, x]))
            damped = coef_ref[2, x] * q_ref[x]
            t = (initial(1, x) if step == 1 else t_ref[x]) + spread
            if BX <= x < 2 * BX:
                hist_ref[k, 0, x - BX] = damped[0:BY]
            if step < STEPS:
                t_ref[x] = t
                q_ref[x] = damped + t
            else:
                out_ref[0, x - BX] = (damped + t)[0:BY]


def forward_kernel(
    wave_ref, own_s_ref, late_ref, even, odd, coef_ref, coef_strip_ref, s_ref, ss_ref, hist_ref,
    adjoint_ref, grad_hbm, adjoint_hbm,
    p_ref, spread_ref, edge_ref, flux_ref, grad_ref, sems,
):
    copies = [pltpu.make_async_copy(adjoint_ref, adjoint_hbm, sems.at[0])]
    copies[0].start()

    def send(index, kind, first, count):
        planes = pl.ds(first, count)
        copy = pltpu.make_async_copy(
            grad_ref.at[kind, planes], grad_hbm.at[kind, planes], sems.at[index]
        )
        copy.start()
        copies.append(copy)

    cut_up, cut_down = cut_flags()
    side = sides()
    messages = (even, odd)
    tiles, own_tiles = WAVE_SIDE[1], WAVE_OWN[1]
    side_strip = tiles + tile_rows(WAVE_TILES)

    def initial(index, x):
        layout = (
            ((messages, 0, 4), (messages, tiles, 0, 3)),
            ((messages, PLANES, 3), (messages, tiles, 3, 2)),
        )[index]
        own = ((wave_ref, 0), (own_s_ref, 0))[index]
        value = widened(own, (late_ref, own_tiles + 32 * index), x, layout, side)
        if index == 1:
            value = less_plane_below(
                value, x, late_ref, WAVE_OWN, messages, (WAVE_SIDE, WAVE_TILES), side
            )
        return value

    own_strip = late_ref[WAVE_OWN[2] : WAVE_OWN[2] + EY]
    p_s, s_s = (
        whole_strip(own_strip, messages, side_strip, slot, side) for slot in range(2)
    )
    s_s = s_s - strip_below(own_strip, messages, side_strip, 2, side)
    stiff_s, buoy_s, damp_s = coef_strip_ref[0], coef_strip_ref[1], coef_strip_ref[2]

    for step in range(1, STEPS + 1):
        flux_s, spread = strip_flux(p_s, buoy_s)
        edges = cut_edges(p_s, flux_s, cut_up, cut_down)
        if step < STEPS:
            s_s = s_s - spread
            p_s = damp_s * (p_s - stiff_s * s_s) + ss_ref[step - 1]
        for x in range(step, EX - step):
            edge_ref[step - 1, x] = plane_edge(edges, x)
    for x in range(EX):
        p_ref[x] = initial(0, x)

    for step in range(1, STEPS + 1):
        k = step - 1
        for x in range(step - 1, EX - step):
            p, buoyancy = p_ref[x], coef_ref[1, x]
            slopes = [p_ref[x + 1] - p]
            if x >= step:
                slopes += [y_up(p) - p, z_up(p, edge_ref[step - 1, x]) - p]
            for axis, slope in enumerate(slopes):
                flux_ref[axis, x] = buoyancy * slope
            if BX <= x < 2 * BX:
                place = x - BX
                term = hist_ref[k, 1, place] * slopes[0][0:BY]
                term = term + hist_ref[k, 2, place] * slopes[1][0:BY]
                term = term + hist_ref[k, 3, place] * slopes[2][0:BY]
                grad_ref[1, place] = -term if k == 0 else grad_ref[1, place] - term
        if step == STEPS:
            send(1, 1, 0, BX)

        for x in range(step, EX - step):
            flux_y, flux_z = flux_ref[1, x], flux_ref[2, x]
            spread = (flux_ref[0, x] - flux_ref[0, x - 1]) + (flux_y - y_down(flux_y))
            spread = spread + (flux_z - z_down(flux_z, edge_ref[step - 1, x]))
            spread = (initial(1, x) if step == 1 else spread_ref[x]) - spread
            if step < STEPS:
                spread_ref[x] = spread
                p_ref[x] = (
                    coef_ref[2, x] * (p_ref[x] - coef_ref[0, x] * spread)
                    + s_ref[k, x - SOURCE_PLANES[0]]
                )
            if BX <= x < 2 * BX:
                place = x - BX
                term = hist_ref[k, 0, place] * spread[0:BY]
                grad_ref[0, place] = -term if k == 0 else grad_ref[0, place] - term
                if step == STEPS:
                    send(2 + place, 0, place, 1)
    for copy in copies:
        copy.wait()


def shape(*dims):
    return jax.ShapeDtypeStruct(dims, F32)


def call(kernel, outs, operands, scratch, places, micros=0.1, out_place="v"):
    spaces = {"h": pltpu.HBM, "a": pl.ANY, "v": pltpu.VMEM}
    operands = [
        pltpu.with_memory_space_constraint(operand, pltpu.HBM) if place == "h" else operand
        for operand, place in zip(operands, places)
    ]
    return pl.pallas_call(
        kernel,
        out_shape=outs,
        in_specs=[pl.BlockSpec(memory_space=spaces[place]) for place in places],
        out_specs=[pl.BlockSpec(memory_space=spaces[out_place])] * len(outs),
        scratch_shapes=scratch,
        compiler_params=pltpu.CompilerParams(vmem_limit_bytes=VMEM_LIMIT),
        cost_estimate=pl.CostEstimate(
            flops=0, bytes_accessed=int(3.69e6 * micros), transcendentals=0
        ),
    )(*operands)


def from_sides(sends, axes):
    count = lax.axis_size("gy")

    def route(offset):
        pairs = []
        for target in range(count):
            source = target + offset
            if 0 <= source < count:
                if "gz" in axes:
                    pairs += [(2 * source + z, 2 * target + 1 - z) for z in range(2)]
                else:
                    pairs.append((source, target))
        return pairs

    if count == 2:
        both = lax.ppermute(sends[0], axes, route(1) + route(-1))
        return both, both
    upward, downward = sends
    return lax.ppermute(downward, axes, route(1)), lax.ppermute(upward, axes, route(-1))


def rotated(array, axis, offset):
    count = lax.axis_size(axis)
    return lax.ppermute(array, axis, [((i + offset) % count, i) for i in range(count)])


def paired(array, odd):
    count = lax.axis_size("gx")
    pairs = []
    for i in range(count):
        partner = ((i - 1) ^ 1) + 1 if odd else i ^ 1
        pairs.append((partner if 0 <= partner < count else i, i))
    return lax.ppermute(array, "gx", pairs)


def local(
    stored, adjoint_end, labels, tissue, source_cells, source_wave, receiver_cells, receiver_wave
):
    assert lax.axis_size("gz") == 2 and labels.shape == (BX, BY, BZ) and tissue.shape[1] == 8
    half = lax.axis_size("gx") // 2
    arguments = [
        stored, adjoint_end, labels, tissue,
        receiver_cells.T, receiver_wave, source_cells.T, source_wave,
    ]
    ways = 1 if lax.axis_size("gy") == 2 else 2
    wave, ql, t, last_x, last_y, strips, table, receivers, receiver_wave, sources, source_wave, *sends = call(
        load_kernel,
        [
            shape(2 * PLANES + BY + SPARE // 2, BZ),
            shape(2 * PLANES, BZ),
            shape(PLANES, BZ),
            shape(BY, BZ),
            shape(2 * BX * 8, BZ),
            shape(3 * BY, BZ),
            shape(24, BZ),
        ]
        + [jax.ShapeDtypeStruct(array.shape, array.dtype) for array in arguments[4:]]
        + [shape(20 * 8, BZ)] * ways
        + [shape(2 * 8, BZ)] * ways,
        arguments,
        [
            pltpu.VMEM(stored.shape, F32),
            pltpu.VMEM(adjoint_end.shape, F32),
            pltpu.VMEM(labels.shape, jnp.int32),
            pltpu.SMEM(tissue.shape, F32),
            pltpu.SemaphoreType.DMA,
        ],
        "hhhhhhhh",
        1.4,
    )
    from_up, from_down = from_sides(sends[:ways], "gy")
    other = rotated(strips, "gz", 1)
    corner_up, corner_down = from_sides(sends[ways:], ("gy", "gz"))
    wave = rotated(wave, "gx", half)
    rb, rsb = call(
        late_kernel,
        [shape(2, EX * EY, BZ), shape(2, EY, BZ)],
        [receivers, receiver_wave],
        [],
        "vv",
        1.2,
    )
    early_planes, source_planes = (last - first for first, last in (EARLY_PLANES, SOURCE_PLANES))
    late, adj_late = call(
        merge_kernel,
        [shape(tile_rows(9) + EY + 8 + SPARE, BZ), shape(ADJ_OWN[2] + EY, BZ)],
        [from_up, from_down, corner_up, corner_down, strips, other, t, last_x, last_y, rsb],
        [pltpu.VMEM((WAVE_OWN[2], BZ), F32)],
        "vvvvvvvvva",
    )
    late = rotated(late, "gx", half)
    ra, rsa = call(
        early_kernel,
        [shape(2, early_planes * EY, BZ), shape(2, EY, BZ)],
        [receivers, receiver_wave, adj_late],
        [],
        "vva",
        1.0,
    )
    ra, rb = ra.reshape(2, early_planes, EY, BZ), rb.reshape(2, EX, EY, BZ)
    even, odd = call(
        adjoint_join_kernel,
        [shape(ADJ_SIDE[1] + tile_rows(ADJ_TILES) + EY + 2 * PLANES, BZ)] * 2,
        [ql, adj_late],
        [],
        "vv",
    )
    even, odd = paired(even, False), paired(odd, True)
    src, src_strip = call(
        source_kernel,
        [shape(STEPS - 1, source_planes * EY, BZ), shape(STEPS - 1, EY, BZ)],
        [sources, source_wave, adj_late],
        [],
        "vva",
        0.5,
    )
    src = src.reshape(STEPS - 1, source_planes, EY, BZ)
    own_s, own_late, wave_even, wave_odd = call(
        join_kernel,
        [shape(PLANES, BZ), shape(WAVE_OWN[2] + EY, BZ)]
        + [shape(WAVE_SIDE[1] + tile_rows(WAVE_TILES) + EY, BZ)] * 2,
        [wave, late],
        [],
        "vv",
    )
    wave_even, wave_odd = paired(wave_even, False), paired(wave_odd, True)
    adjoint_out, hist, coef, coef_strip = call(
        adjoint_kernel,
        [
            shape(4, BX, BY, BZ),
            shape(STEPS, 4, BX, BY, BZ),
            shape(3, EX, EY, BZ),
            shape(3, EY, BZ),
        ],
        [ql, adj_late, even, odd, adjoint_end, ra, rsa, rb, rsb, table],
        [pltpu.VMEM((EX, EY, BZ), F32)] * 4
        + [
            pltpu.VMEM((STEPS, EX, EY, BZ), F32),
            pltpu.VMEM((3, EX, EY, BZ), F32),
            pltpu.SemaphoreType.DMA,
        ],
        "vvvvhvvvvv",
        3.9,
    )
    return call(
        forward_kernel,
        [shape(2, BX, BY, BZ), shape(4, BX, BY, BZ)],
        [
            wave, own_s, own_late, wave_even, wave_odd, coef, coef_strip, src, src_strip, hist,
            adjoint_out,
        ],
        [pltpu.VMEM((EX, EY, BZ), F32)] * 2
        + [
            pltpu.VMEM((STEPS, EX, EY, BZ), F32),
            pltpu.VMEM((3, EX, EY, BZ), F32),
            pltpu.VMEM((2, BX, BY, BZ), F32),
            pltpu.SemaphoreType.DMA((2 + BX,)),
        ],
        "vvvvvvvvvvv",
        2.5,
        "a",
    )


def solution(mesh):
    return jax.shard_map(
        local,
        mesh=mesh,
        in_specs=(
            P("shot", "gx", "gy", "gz"),
            P("shot", "gx", "gy", "gz"),
            P("gx", "gy", "gz"),
            P(),
            P("shot", None),
            P(None, "shot"),
            P(),
            P(None, "shot"),
        ),
        out_specs=(P("shot", "gx", "gy", "gz"), P("shot", "gx", "gy", "gz")),
        check_vma=False,
    )
```

```python
import jax
import jax.numpy as jnp
from jax import lax
from jax.experimental import pallas as pl
from jax.experimental.pallas import tpu as pltpu
from jax.sharding import PartitionSpec as P

STEPS = 4
MARGIN = 4
BX, BY, BZ = 4, 32, 128
EX, EY = BX + 2 * MARGIN, BY + 2 * MARGIN
STRIP = 2 * MARGIN
F32 = jnp.float32
BF16 = jnp.bfloat16
VMEM_LIMIT = 16 * 1024 * 1024
PLANES = BX * BY
WAVE_OWN = (0, BY, BY + 9 * 8)
FIX_LANE = 3 * BX * STRIP
SPARE = 64
ADJ_OWN = (PLANES, PLANES + BY, PLANES + BY + 13 * 8)
WAVE_SIDE = (PLANES + 3 * BY, PLANES + 4 * BY)
ADJ_SIDE = (3 * BY, 4 * BY)
WAVE_TILES, ADJ_TILES = 6, 9


def lanes(shape):
    return lax.broadcasted_iota(jnp.int32, shape, len(shape) - 1)


def rows(shape):
    return lax.broadcasted_iota(jnp.int32, shape, len(shape) - 2)


def run(copies):
    for copy in copies:
        copy.start()
    for copy in copies:
        copy.wait()


def coefficients(labels, table_ref):
    result = [jnp.zeros(labels.shape, F32) for _ in range(3)]
    for index in range(8):
        picked = labels == float(index + 1)
        for kind in range(3):
            row = kind * 8 + index
            result[kind] = jnp.where(picked, table_ref[row : row + 1], result[kind])
    return result


def buoyancy_of(labels, table_ref):
    result = jnp.zeros(labels.shape, F32)
    for index in range(8):
        result = jnp.where(labels == float(index + 1), table_ref[8 + index : 9 + index], result)
    return result


def half_turn(tile):
    return pltpu.roll(tile, MARGIN, 0)


def load_kernel(
    stored_hbm, adj_hbm, lab_hbm, tissue_hbm, rc_hbm, rw_hbm, sc_hbm, sw_hbm,
    wave_ref, ql_ref, t_ref, last_x_ref, last_y_ref, strip_ref, table_ref,
    rc_ref, rw_ref, sc_ref, sw_ref, *rest,
):
    *sends, stored, adj, lab, tissue, sem = rest
    run([
        pltpu.make_async_copy(source, target, sem)
        for source, target in (
            (stored_hbm, stored), (adj_hbm, adj), (lab_hbm, lab), (tissue_hbm, tissue),
            (rc_hbm, rc_ref), (rw_hbm, rw_ref), (sc_hbm, sc_ref), (sw_hbm, sw_ref),
        )
    ])
    for index in range(tissue.shape[1]):
        speed = jnp.full((1, BZ), tissue[0, index], F32)
        density = jnp.full((1, BZ), tissue[1, index], F32)
        table_ref[index : index + 1] = density * speed
        table_ref[8 + index : 9 + index] = speed / density
        table_ref[16 + index : 17 + index] = 1.0 - jnp.full((1, BZ), tissue[2, index], F32)
    gy, gz = lax.axis_index("gy"), lax.axis_index("gz")
    lane = lanes((BY, BZ))
    row = rows((BY, BZ))
    tile_row = rows((8, BZ))
    strips = [jnp.zeros((BY, BZ), F32) for _ in range(3)]
    tiles = [None] * 39
    previous = [None, None]

    def edge_tile(block):
        return jnp.where(tile_row < MARGIN, block[0:8], block[BY - 8 : BY])

    for x in range(BX):
        labels = lab[x].astype(F32) + 1.0
        buoyancy = buoyancy_of(labels, table_ref)
        plane = slice(x * BY, x * BY + BY)
        fields = [stored[index, x] for index in range(4)] + [adj[0, x]]
        fields += [buoyancy * adj[index, x] for index in range(1, 4)] + [labels]
        wave_ref[plane] = fields[0]
        ql_ref[plane] = fields[4]
        ql_ref[PLANES + x * BY : PLANES + x * BY + BY] = labels
        for index, block in enumerate(fields):
            tiles[index * BX + x] = edge_tile(block)
            group, slot = divmod(index, 4)
            base = slot * BX * STRIP + x * STRIP
            rolled = pltpu.roll(block, base + MARGIN, 1)
            first = base + MARGIN * gz
            strips[group] = jnp.where(
                (lane >= first) & (lane < first + MARGIN), rolled, strips[group]
            )
        for kind, (target, base) in enumerate(((wave_ref, PLANES), (t_ref, 0))):
            vx, vy, vz = fields[4 * kind + 1 : 4 * kind + 4]
            spread = vx if x == 0 else vx - previous[kind]
            spread = spread + (vy - jnp.where(row == 0, 0.0, pltpu.roll(vy, 1, 0)))
            spread = spread + (vz - jnp.where(lane == 0, 0.0, pltpu.roll(vz, 1, 1)))
            target[base + x * BY : base + x * BY + BY] = spread
            previous[kind] = vx
            index = (kind * BX + x) * 8
            last_y_ref[index : index + 8] = vy[BY - 8 : BY]
    wave_ref[2 * PLANES : 2 * PLANES + BY] = previous[0]
    wave_ref[2 * PLANES + BY :] = jnp.zeros((SPARE // 2, BZ), F32)
    last_x_ref[...] = previous[1]
    for group in range(3):
        strip_ref[group * BY : group * BY + BY] = strips[group]
        tiles[9 * BX + group] = edge_tile(strips[group])

    def joined(first, second):
        second = first if second is None else second
        upward = jnp.where(tile_row < MARGIN, half_turn(first), second)
        downward = jnp.where(tile_row < MARGIN, first, half_turn(second))
        if len(sends) == 2:
            return (jnp.where(gy == 0, upward, downward),)
        return upward, downward

    tiles.append(None)
    half = len(sends) // 2
    for place in range(20):
        for target, tile in zip(sends[:half], joined(tiles[2 * place], tiles[2 * place + 1])):
            target[place * 8 : place * 8 + 8] = tile
    for place in range(2):
        first = tiles[9 * BX + 2 * place]
        for target, tile in zip(sends[half:], joined(first, tiles[9 * BX + 2 * place + 1])):
            target[place * 8 : place * 8 + 8] = tile


def copy_rows(target, base, source, first, count):
    target[base : base + count] = source[pl.ds(pl.multiple_of(first, 8), count)]
    return base + count


def halved():
    return lax.axis_size("gy") == 2


def tile_rows(count):
    return (count + 1) // 2 * 8 if halved() else count * 8


def put_tiles(target, base, source, firsts):
    tiles = [source[pl.ds(pl.multiple_of(first, 8), 8)] for first in firsts]
    if halved():
        upper = lax.axis_index("gy") == 0
        row = rows((8, BZ))
        pairs = [(tiles[i], tiles[min(i + 1, len(tiles) - 1)]) for i in range(0, len(tiles), 2)]
        tiles = [
            jnp.where(
                row < MARGIN,
                jnp.where(upper, first, half_turn(first)),
                jnp.where(upper, half_turn(second), second),
            )
            for first, second in pairs
        ]
    for place, tile in enumerate(tiles):
        target[base + place * 8 : base + place * 8 + 8] = tile
    return base + 8 * len(tiles)


def pair_planes():
    parity = lax.rem(lax.axis_index("gx"), 2)
    return 1 - parity, parity


def merge_kernel(
    from_up, from_down, corner_up, corner_down, strip_ref, other_ref,
    t_ref, last_x_ref, last_y_ref, _,
    late_ref, adj_ref,
    wave_ref,
):
    gy = lax.axis_index("gy")
    tile_row = rows((8, BZ))
    row, lane = rows((BY, BZ)), lanes((BY, BZ))
    take_up = (tile_row < MARGIN) & (gy < lax.axis_size("gy") - 1)
    take_down = (tile_row >= MARGIN) & (gy > 0)
    _, cut_down = cut_flags()

    def halo(up, down, index):
        place, second = divmod(index, 2)
        sl = slice(place * 8, place * 8 + 8)
        above = half_turn(up[sl]) if second else up[sl]
        below = down[sl] if second else half_turn(down[sl])
        return jnp.where(take_up, above, jnp.where(take_down, below, 0.0))

    wide = []
    for group in range(3):
        sl = slice(group * BY, group * BY + BY)
        tile = halo(from_up, from_down, 9 * BX + group) + halo(corner_up, corner_down, group)
        wide.append(jnp.concatenate([strip_ref[sl] + other_ref[sl], tile], 0))
    strip_lane = lanes((EY, BZ))

    def strip_field(index):
        group, slot = divmod(index, 4)
        moved = pltpu.roll(wide[group], (BZ - slot * BX * STRIP) % BZ, 1) if slot else wide[group]
        return jnp.where(strip_lane < BX * STRIP, moved, 0.0)

    last_lanes = (BX - 1) * STRIP
    fix_row = jnp.zeros((8, BZ), F32)
    fix_lane = jnp.zeros((BY, BZ), F32)
    for kind, target in enumerate((wave_ref, adj_ref)):
        first = 4 * kind
        planes_end, x_end, tiles_end = (WAVE_OWN, ADJ_OWN)[kind]
        vx, vy, vz = (strip_field(first + 1 + axis) for axis in range(3))
        spread = vx - jnp.where(strip_lane < STRIP, 0.0, pltpu.roll(vx, STRIP, 1))
        spread = (spread + (vy - y_down(vy))) + (vz - pltpu.roll(vz, 1, 1))
        strip = strip_field(first)
        strip = strip + pltpu.roll(jnp.where(strip_lane < BX * STRIP, spread, 0.0), BX * STRIP, 1)
        last_slot = 2
        if kind == 1:
            strip = strip + pltpu.roll(strip_field(8), 2 * BX * STRIP, 1)
            last_slot = 3
        last = jnp.where(strip_lane >= last_lanes, vx, 0.0)
        strip = strip + pltpu.roll(last, last_slot * BX * STRIP - last_lanes, 1)

        vx_before = None
        for x in range(BX):
            vx_t, vy_t, vz_t = (
                halo(from_up, from_down, (first + 1 + axis) * BX + x) for axis in range(3)
            )
            below_z = pltpu.roll(vz, (BZ - (x * STRIP + MARGIN - 1)) % BZ, 1) * cut_down
            last_y = last_y_ref[(kind * BX + x) * 8 : (kind * BX + x) * 8 + 8]
            y_before = jnp.where(
                tile_row == 0, pltpu.roll(last_y, 1, 0), pltpu.roll(vy_t, 1, 0)
            )
            z_before = jnp.where(lane[0:8] == 0, below_z[BY:EY], pltpu.roll(vz_t, 1, 1))
            spread = vx_t if x == 0 else vx_t - vx_before
            spread = (spread + (vy_t - y_before)) + (vz_t - z_before)
            vx_before = vx_t
            if kind == 0:
                fix_row = jnp.where(tile_row == x, vy_t[7:8], fix_row)
                moved = pltpu.roll(below_z[0:BY], FIX_LANE + x, 1)
                fix_lane = jnp.where(lane == FIX_LANE + x, moved, fix_lane)
            else:
                block = t_ref[x * BY : x * BY + BY]
                block = block - jnp.where(row == 0, vy_t[7:8], 0.0)
                block = block - jnp.where(lane == 0, below_z[0:BY], 0.0)
                target[x * BY : x * BY + BY] = block
            base = x_end + x * 8
            target[base : base + 8] = halo(from_up, from_down, first * BX + x)
            target[base + 32 : base + 40] = spread
            if kind == 1:
                target[base + 64 : base + 72] = halo(from_up, from_down, 8 * BX + x)
        target[tiles_end - 8 : tiles_end] = vx_before
        if kind == 0:
            base = put_tiles(late_ref, 0, wave_ref, range(x_end, tiles_end, 8))
            late_ref[base : base + BY] = strip[0:BY] + fix_lane
            late_ref[base + BY : base + EY] = strip[BY:EY]
            late_ref[base + EY : base + EY + 8] = fix_row
            late_ref[base + EY + 8 : base + EY + 8 + SPARE] = jnp.zeros((SPARE, BZ), F32)
        else:
            target[planes_end:x_end] = last_x_ref[...]
            target[tiles_end : tiles_end + EY] = strip


def adjoint_join_kernel(ql_ref, adj_ref, _, even_ref, odd_ref):
    planes_end, x_end, tiles_end = ADJ_OWN
    for target, first in zip((even_ref, odd_ref), pair_planes()):
        base = copy_rows(target, 0, adj_ref, first * BY, 3 * BY)
        base = copy_rows(target, base, adj_ref, planes_end, BY)
        near = [x_end + (first + plane) * 8 for plane in range(3)]
        nearest = [x_end + 32 + first * 16 + plane * 8 for plane in range(2)]
        firsts = near + nearest + [start + 64 for start in near] + [tiles_end - 8]
        base = put_tiles(target, base, adj_ref, firsts)
        base = copy_rows(target, base, adj_ref, tiles_end, EY)
        copy_rows(target, base, ql_ref, 0, 2 * PLANES)


def unpacked(tile, place):
    upper = lax.axis_index("gy") == 0
    turned = half_turn(tile)
    tile = jnp.where(upper, turned, tile) if place % 2 else jnp.where(upper, tile, turned)
    return jnp.where((rows((8, BZ)) < MARGIN) == upper, tile, 0.0)


def join_kernel(wave_ref, late_ref, s_ref, own_ref, even_ref, odd_ref):
    planes_end, x_end, tiles_end = WAVE_OWN
    own_ref[planes_end:x_end] = wave_ref[2 * PLANES : 2 * PLANES + BY]
    for place in range((tiles_end - x_end) // 8):
        if halved():
            tile = unpacked(late_ref[place // 2 * 8 : place // 2 * 8 + 8], place)
        else:
            tile = late_ref[place * 8 : place * 8 + 8]
        own_ref[x_end + place * 8 : x_end + place * 8 + 8] = tile
    strip = tile_rows((tiles_end - x_end) // 8)
    own_ref[tiles_end : tiles_end + EY] = late_ref[strip : strip + EY]
    row, lane = rows((BY, BZ)), lanes((BY, BZ))
    fix_lane = late_ref[strip : strip + BY]
    for x in range(BX):
        block = wave_ref[PLANES + x * BY : PLANES + x * BY + BY]
        fix_row = late_ref[strip + EY + x : strip + EY + x + 1]
        block = block - jnp.where(row == 0, fix_row, 0.0)
        block = block - jnp.where(lane == 0, pltpu.roll(fix_lane, BZ - FIX_LANE - x, 1), 0.0)
        s_ref[x * BY : x * BY + BY] = block
    for target, first in zip((even_ref, odd_ref), pair_planes()):
        base = copy_rows(target, 0, wave_ref, 0, PLANES)
        base = copy_rows(target, base, s_ref, first * BY, 3 * BY)
        base = copy_rows(target, base, own_ref, planes_end, BY)
        near = [x_end + (first + plane) * 8 for plane in range(3)]
        nearest = [x_end + 32 + first * 16 + plane * 8 for plane in range(2)]
        base = put_tiles(target, base, own_ref, near + nearest + [tiles_end - 8])
        copy_rows(target, base, own_ref, tiles_end, EY)


def split(values):
    high = values.astype(BF16)
    rest = values - high.astype(F32)
    middle = rest.astype(BF16)
    low = (rest - middle.astype(F32)).astype(BF16)
    return high, middle, low


def places(cells, sl):
    gx, gy, gz = (lax.axis_index(name) for name in ("gx", "gy", "gz"))
    cut = BZ * lax.axis_size("gz") // 2 - MARGIN
    cell_x = cells[0:1, sl] - (gx * BX - MARGIN)
    cell_y = cells[1:2, sl] - gy * BY
    cell_z = cells[2:3, sl]
    in_x = (cell_x >= 0) & (cell_x < EX)
    in_y = (cell_y >= -MARGIN) & (cell_y < BY + MARGIN)
    row = jnp.where(cell_y < 0, cell_y + EY, cell_y)
    flat = jnp.where(in_x & in_y, cell_x * EY + row, -1)
    row = jnp.where(in_y, row, -1)
    zz = cell_z - cut
    in_strip = in_x & (zz >= 0) & (zz < STRIP)
    strip_lane = jnp.where(in_strip, cell_x * STRIP + zz, -1)
    return flat, cell_z - gz * BZ, row, strip_lane


def hits(count, index):
    return rows((count, index.shape[1])) == index


def product(left, right):
    return lax.dot_general(
        left, right, (((1,), (1,)), ((), ())), preferred_element_type=F32
    )


def inject_points(cells, wave_ref, width, waves, planes, out_ref, strip_out_ref):
    count, low, total_rows = len(waves), planes[0] * EY, (planes[1] - planes[0]) * EY
    for start in range(0, cells.shape[1], width):
        sl = slice(start, start + width)
        flat, z, row, strip_lane = places(cells, sl)
        here = hits(total_rows, flat - low).astype(F32).astype(BF16)
        at_strip = hits(BZ, strip_lane).astype(F32).astype(BF16)
        at_z, at_row = hits(BZ, z), hits(EY, row)
        total = strip_total = None
        parts = [split(wave_ref[wave : wave + 1, sl]) for wave in waves]
        for part in range(3):
            amounts = [parts[wave][part].astype(F32) for wave in range(count)]
            right = jnp.concatenate([jnp.where(at_z, a, 0.0) for a in amounts], 0).astype(BF16)
            left = jnp.concatenate([jnp.where(at_row, a, 0.0) for a in amounts], 0).astype(BF16)
            term, strip_term = product(here, right), product(left, at_strip)
            total = term if part == 0 else total + term
            strip_total = strip_term if part == 0 else strip_total + strip_term
        for wave in range(count):
            value = total[:, wave * BZ : wave * BZ + BZ]
            strip_value = strip_total[wave * EY : wave * EY + EY]
            if start > 0:
                value = value + out_ref[wave]
                strip_value = strip_value + strip_out_ref[wave]
            out_ref[wave] = value
            strip_out_ref[wave] = strip_value


LATE_PLANES, EARLY_PLANES, SOURCE_PLANES = (0, EX), (2, EX - 2), (1, EX - 1)


def late_kernel(receivers, receiver_wave, r_ref, rs_ref):
    inject_points(receivers, receiver_wave, 256, (2, 3), LATE_PLANES, r_ref, rs_ref)


def early_kernel(receivers, receiver_wave, _, r_ref, rs_ref):
    inject_points(receivers, receiver_wave, 256, (0, 1), EARLY_PLANES, r_ref, rs_ref)


def source_kernel(sources, source_wave, _, s_ref, ss_ref):
    width = sources.shape[1]
    inject_points(sources, source_wave, width, (0, 1, 2), SOURCE_PLANES, s_ref, ss_ref)


def strip_of(packed, block, slot):
    lane = lanes(packed.shape)
    width = BX * STRIP
    shift = (block * width - slot * width) % BZ
    moved = pltpu.roll(packed, shift, 1) if shift else packed
    return jnp.where((lane >= block * width) & (lane < (block + 1) * width), moved, 0.0)


def y_up(v):
    return pltpu.roll(v, EY - 1, 0)


def y_down(v):
    return pltpu.roll(v, 1, 0)


def z_up(v, edge):
    return jnp.where(lanes(v.shape) == BZ - 1, edge, pltpu.roll(v, BZ - 1, 1))


def z_down(v, edge):
    return jnp.where(lanes(v.shape) == 0, edge, pltpu.roll(v, 1, 1))


def cut_edges(values, flux_z, cut_up, cut_down):
    place = lax.rem(lanes(values.shape), STRIP)
    above = jnp.where(place == MARGIN, values * cut_up, 0.0)
    below = jnp.where(place == MARGIN - 1, flux_z * cut_down, 0.0)
    return pltpu.roll(above, BZ - 2, 1) + below


def plane_edge(edges, x):
    return pltpu.roll(edges, (BZ - (x * STRIP + MARGIN - 1)) % BZ, 1)


def strip_flux(values, buoyancy):
    flux_x = buoyancy * (pltpu.roll(values, BZ - STRIP, 1) - values)
    flux_y = buoyancy * (y_up(values) - values)
    flux_z = buoyancy * (pltpu.roll(values, BZ - 1, 1) - values)
    spread = (flux_x - pltpu.roll(flux_x, STRIP, 1)) + (flux_y - y_down(flux_y))
    return flux_z, spread + (flux_z - pltpu.roll(flux_z, 1, 1))


def cut_flags():
    gz, half = lax.axis_index("gz"), lax.axis_size("gz") // 2
    return jnp.where(gz == half - 1, 1.0, 0.0), jnp.where(gz == half, 1.0, 0.0)


def sides():
    gx = lax.axis_index("gx")
    low = jnp.where(gx > 0, 1.0, 0.0)
    high = jnp.where(gx < lax.axis_size("gx") - 1, 1.0, 0.0)
    return low, high, lax.rem(gx, 2) == 0


def from_side(messages, first, count, block, side):
    even, odd = (message[first : first + count] for message in messages)
    low, high, even_above = side
    if block == 0:
        return jnp.where(even_above, odd, even) * low
    return jnp.where(even_above, even, odd) * high


def side_tile(messages, base, place, block, side):
    if not halved():
        return from_side(messages, base + place * 8, 8, block, side)
    tile = from_side(messages, base + place // 2 * 8, 8, block, side)
    return unpacked(tile, place)


def side_place(wanted, plane, block):
    planes = range(BX - wanted, BX) if block == 0 else range(wanted)
    return planes.index(plane) if plane in planes else None


def widened(own, own_tiles, x, layout, side):
    block, plane = divmod(x, BX)
    if block == 1:
        main = own[0][own[1] + plane * BY : own[1] + plane * BY + BY]
        tile = own_tiles[0][own_tiles[1] + plane * 8 : own_tiles[1] + plane * 8 + 8]
        return jnp.concatenate([main, tile], 0)
    (messages, base, wanted), (tile_messages, tile_base, tile_place, tile_wanted) = layout
    main, tile = jnp.zeros((BY, BZ), F32), jnp.zeros((8, BZ), F32)
    place = side_place(wanted, plane, block)
    if place is not None:
        main = from_side(messages, base + place * BY, BY, block, side)
    place = side_place(tile_wanted, plane, block)
    if place is not None:
        tile = side_tile(tile_messages, tile_base, tile_place + place, block, side)
    return jnp.concatenate([main, tile], 0)


def less_plane_below(value, x, own_ref, own_rows, messages, side_layout, side):
    if x == BX:
        (planes_end, x_end), count = side_layout
        main = from_side(messages, planes_end, BY, 0, side)
        tile = side_tile(messages, x_end, count - 1, 0, side)
    elif x == 2 * BX:
        planes_end, _, tiles_end = own_rows
        high = side[1]
        main = own_ref[planes_end : planes_end + BY] * high
        tile = own_ref[tiles_end - 8 : tiles_end] * high
    else:
        return value
    return value - jnp.concatenate([main, tile], 0)


def strip_below(own, messages, first, slot, side):
    lane = lanes(own.shape)
    width = BX * STRIP
    low = from_side(messages, first, EY, 0, side)
    low = pltpu.roll(low, (width - slot * width) % BZ, 1)
    own = pltpu.roll(own * side[1], (2 * width - slot * width) % BZ, 1)
    in_own = (lane >= width) & (lane < width + STRIP)
    in_high = (lane >= 2 * width) & (lane < 2 * width + STRIP)
    return jnp.where(in_own, low, jnp.where(in_high, own, 0.0))


def whole_strip(own, messages, first, slot, side):
    low = from_side(messages, first, EY, 0, side)
    high = from_side(messages, first, EY, 2, side)
    return strip_of(low, 0, slot) + strip_of(own, 1, slot) + strip_of(high, 2, slot)


def adjoint_kernel(
    ql_ref, late_ref, even, odd, adj_hbm, ra_ref, rsa_ref, rb_ref, rsb_ref,
    table_ref,
    out_ref, hist_ref, coef_ref, coef_strip_ref,
    q_ref, t_ref, u_ref, scale_ref, edge_ref, flux_ref, w_sem,
):
    w_copy = pltpu.make_async_copy(adj_hbm.at[pl.ds(1, 3)], out_ref.at[pl.ds(1, 3)], w_sem)
    w_copy.start()
    cut_up, cut_down = cut_flags()
    side = sides()
    messages = (even, odd)
    r_refs = ((ra_ref, 0), (ra_ref, 1), (rb_ref, 0), (rb_ref, 1))
    rs_refs = ((rsa_ref, 0), (rsa_ref, 1), (rsb_ref, 0), (rsb_ref, 1))
    tiles, own_tiles = ADJ_SIDE[1], ADJ_OWN[1]
    side_strip = tiles + tile_rows(ADJ_TILES)
    raws = side_strip + EY

    def initial(index, x):
        own = ((ql_ref, 0), (late_ref, 0), (ql_ref, PLANES))[index]
        layout = (
            ((messages, raws, 4), (messages, tiles, 0, 3)),
            ((messages, 0, 3), (messages, tiles, 3, 2)),
            ((messages, raws + PLANES, 4), (messages, tiles, 5, 3)),
        )[index]
        value = widened(own, (late_ref, own_tiles + 32 * index), x, layout, side)
        if index == 1:
            value = less_plane_below(
                value, x, late_ref, ADJ_OWN, messages, (ADJ_SIDE, ADJ_TILES), side
            )
        return value

    for x in range(EX):
        stiff, buoy, damp = coefficients(initial(2, x), table_ref)
        coef_ref[0, x], coef_ref[1, x], coef_ref[2, x] = stiff, buoy, damp
        scale_ref[x] = stiff * damp
    own_strip = late_ref[ADJ_OWN[2] : ADJ_OWN[2] + EY]
    q_s, t_s, label_s = (
        whole_strip(own_strip, messages, side_strip, slot, side) for slot in range(3)
    )
    t_s = t_s - strip_below(own_strip, messages, side_strip, 3, side)
    stiff_s, buoy_s, damp_s = coefficients(label_s, table_ref)
    scale_s = stiff_s * damp_s
    coef_strip_ref[0], coef_strip_ref[1], coef_strip_ref[2] = stiff_s, buoy_s, damp_s
    w_copy.wait()

    for step in range(1, STEPS + 1):
        rs_ref, place = rs_refs[STEPS - step]
        q_s = q_s + rs_ref[place]
        u_s = scale_s * q_s
        flux_s, spread = strip_flux(u_s, buoy_s)
        t_s = t_s + spread
        q_s = damp_s * q_s + t_s
        edges = cut_edges(u_s, flux_s, cut_up, cut_down)
        for x in range(step, EX - step):
            edge_ref[step - 1, x] = plane_edge(edges, x)

    for step in range(1, STEPS + 1):
        k = STEPS - step
        r_ref, place = r_refs[k]
        r_first = (EARLY_PLANES if k < 2 else LATE_PLANES)[0]

        for x in range(step - 1, EX - step + 1):
            q = (initial(0, x) if step == 1 else q_ref[x]) + r_ref[place, x - r_first]
            q_ref[x] = q
            u_ref[x] = scale_ref[x] * q

        for x in range(step - 1, EX - step):
            u, buoyancy = u_ref[x], coef_ref[1, x]
            slopes = [u_ref[x + 1] - u]
            if x >= step:
                slopes += [y_up(u) - u, z_up(u, edge_ref[step - 1, x]) - u]
            for axis, slope in enumerate(slopes):
                flux_ref[axis, x] = buoyancy * slope
            if BX <= x < 2 * BX:
                for axis, slope in enumerate(slopes):
                    w = out_ref[1 + axis, x - BX] + slope[0:BY]
                    out_ref[1 + axis, x - BX] = w
                    hist_ref[k, 1 + axis, x - BX] = w

        for x in range(step, EX - step):
            flux_y, flux_z = flux_ref[1, x], flux_ref[2, x]
            spread = (flux_ref[0, x] - flux_ref[0, x - 1]) + (flux_y - y_down(flux_y))
            spread = spread + (flux_z - z_down(flux_z, edge_ref[step - 1, x]))
            damped = coef_ref[2, x] * q_ref[x]
            t = (initial(1, x) if step == 1 else t_ref[x]) + spread
            if BX <= x < 2 * BX:
                hist_ref[k, 0, x - BX] = damped[0:BY]
            if step < STEPS:
                t_ref[x] = t
                q_ref[x] = damped + t
            else:
                out_ref[0, x - BX] = (damped + t)[0:BY]


def forward_kernel(
    wave_ref, own_s_ref, late_ref, even, odd, coef_ref, coef_strip_ref, s_ref, ss_ref, hist_ref,
    adjoint_ref, grad_hbm, adjoint_hbm,
    p_ref, spread_ref, edge_ref, flux_ref, grad_ref, sems,
):
    copies = [pltpu.make_async_copy(adjoint_ref, adjoint_hbm, sems.at[0])]
    copies[0].start()

    def send(index, kind, first, count):
        planes = pl.ds(first, count)
        copy = pltpu.make_async_copy(
            grad_ref.at[kind, planes], grad_hbm.at[kind, planes], sems.at[index]
        )
        copy.start()
        copies.append(copy)

    cut_up, cut_down = cut_flags()
    side = sides()
    messages = (even, odd)
    tiles, own_tiles = WAVE_SIDE[1], WAVE_OWN[1]
    side_strip = tiles + tile_rows(WAVE_TILES)

    def initial(index, x):
        layout = (
            ((messages, 0, 4), (messages, tiles, 0, 3)),
            ((messages, PLANES, 3), (messages, tiles, 3, 2)),
        )[index]
        own = ((wave_ref, 0), (own_s_ref, 0))[index]
        value = widened(own, (late_ref, own_tiles + 32 * index), x, layout, side)
        if index == 1:
            value = less_plane_below(
                value, x, late_ref, WAVE_OWN, messages, (WAVE_SIDE, WAVE_TILES), side
            )
        return value

    own_strip = late_ref[WAVE_OWN[2] : WAVE_OWN[2] + EY]
    p_s, s_s = (
        whole_strip(own_strip, messages, side_strip, slot, side) for slot in range(2)
    )
    s_s = s_s - strip_below(own_strip, messages, side_strip, 2, side)
    stiff_s, buoy_s, damp_s = coef_strip_ref[0], coef_strip_ref[1], coef_strip_ref[2]

    for step in range(1, STEPS + 1):
        flux_s, spread = strip_flux(p_s, buoy_s)
        edges = cut_edges(p_s, flux_s, cut_up, cut_down)
        if step < STEPS:
            s_s = s_s - spread
            p_s = damp_s * (p_s - stiff_s * s_s) + ss_ref[step - 1]
        for x in range(step, EX - step):
            edge_ref[step - 1, x] = plane_edge(edges, x)
    for x in range(EX):
        p_ref[x] = initial(0, x)

    for step in range(1, STEPS + 1):
        k = step - 1
        for x in range(step - 1, EX - step):
            p, buoyancy = p_ref[x], coef_ref[1, x]
            slopes = [p_ref[x + 1] - p]
            if x >= step:
                slopes += [y_up(p) - p, z_up(p, edge_ref[step - 1, x]) - p]
            for axis, slope in enumerate(slopes):
                flux_ref[axis, x] = buoyancy * slope
            if BX <= x < 2 * BX:
                place = x - BX
                term = hist_ref[k, 1, place] * slopes[0][0:BY]
                term = term + hist_ref[k, 2, place] * slopes[1][0:BY]
                term = term + hist_ref[k, 3, place] * slopes[2][0:BY]
                grad_ref[1, place] = -term if k == 0 else grad_ref[1, place] - term
        if step == STEPS:
            send(1, 1, 0, BX)

        for x in range(step, EX - step):
            flux_y, flux_z = flux_ref[1, x], flux_ref[2, x]
            spread = (flux_ref[0, x] - flux_ref[0, x - 1]) + (flux_y - y_down(flux_y))
            spread = spread + (flux_z - z_down(flux_z, edge_ref[step - 1, x]))
            spread = (initial(1, x) if step == 1 else spread_ref[x]) - spread
            if step < STEPS:
                spread_ref[x] = spread
                p_ref[x] = (
                    coef_ref[2, x] * (p_ref[x] - coef_ref[0, x] * spread)
                    + s_ref[k, x - SOURCE_PLANES[0]]
                )
            if BX <= x < 2 * BX:
                place = x - BX
                term = hist_ref[k, 0, place] * spread[0:BY]
                grad_ref[0, place] = -term if k == 0 else grad_ref[0, place] - term
                if step == STEPS:
                    send(2 + place, 0, place, 1)
    for copy in copies:
        copy.wait()


def shape(*dims):
    return jax.ShapeDtypeStruct(dims, F32)


def call(kernel, outs, operands, scratch, places, micros=0.1, out_place="v"):
    spaces = {"h": pltpu.HBM, "a": pl.ANY, "v": pltpu.VMEM}
    operands = [
        pltpu.with_memory_space_constraint(operand, pltpu.HBM) if place == "h" else operand
        for operand, place in zip(operands, places)
    ]
    return pl.pallas_call(
        kernel,
        out_shape=outs,
        in_specs=[pl.BlockSpec(memory_space=spaces[place]) for place in places],
        out_specs=[pl.BlockSpec(memory_space=spaces[out_place])] * len(outs),
        scratch_shapes=scratch,
        compiler_params=pltpu.CompilerParams(vmem_limit_bytes=VMEM_LIMIT),
        cost_estimate=pl.CostEstimate(
            flops=0, bytes_accessed=int(3.69e6 * micros), transcendentals=0
        ),
    )(*operands)


def from_sides(sends, axes):
    count = lax.axis_size("gy")

    def route(offset):
        pairs = []
        for target in range(count):
            source = target + offset
            if 0 <= source < count:
                if "gz" in axes:
                    pairs += [(2 * source + z, 2 * target + 1 - z) for z in range(2)]
                else:
                    pairs.append((source, target))
        return pairs

    if count == 2:
        both = lax.ppermute(sends[0], axes, route(1) + route(-1))
        return both, both
    upward, downward = sends
    return lax.ppermute(downward, axes, route(1)), lax.ppermute(upward, axes, route(-1))


def rotated(array, axis, offset):
    count = lax.axis_size(axis)
    return lax.ppermute(array, axis, [((i + offset) % count, i) for i in range(count)])


def paired(array, odd):
    count = lax.axis_size("gx")
    pairs = []
    for i in range(count):
        partner = ((i - 1) ^ 1) + 1 if odd else i ^ 1
        pairs.append((partner if 0 <= partner < count else i, i))
    return lax.ppermute(array, "gx", pairs)


def local(
    stored, adjoint_end, labels, tissue, source_cells, source_wave, receiver_cells, receiver_wave
):
    assert lax.axis_size("gz") == 2 and labels.shape == (BX, BY, BZ) and tissue.shape[1] == 8
    half = lax.axis_size("gx") // 2
    arguments = [
        stored, adjoint_end, labels, tissue,
        receiver_cells.T, receiver_wave, source_cells.T, source_wave,
    ]
    ways = 1 if lax.axis_size("gy") == 2 else 2
    wave, ql, t, last_x, last_y, strips, table, receivers, receiver_wave, sources, source_wave, *sends = call(
        load_kernel,
        [
            shape(2 * PLANES + BY + SPARE // 2, BZ),
            shape(2 * PLANES, BZ),
            shape(PLANES, BZ),
            shape(BY, BZ),
            shape(2 * BX * 8, BZ),
            shape(3 * BY, BZ),
            shape(24, BZ),
        ]
        + [jax.ShapeDtypeStruct(array.shape, array.dtype) for array in arguments[4:]]
        + [shape(20 * 8, BZ)] * ways
        + [shape(2 * 8, BZ)] * ways,
        arguments,
        [
            pltpu.VMEM(stored.shape, F32),
            pltpu.VMEM(adjoint_end.shape, F32),
            pltpu.VMEM(labels.shape, jnp.int32),
            pltpu.SMEM(tissue.shape, F32),
            pltpu.SemaphoreType.DMA,
        ],
        "hhhhhhhh",
        1.4,
    )
    from_up, from_down = from_sides(sends[:ways], "gy")
    other = rotated(strips, "gz", 1)
    corner_up, corner_down = from_sides(sends[ways:], ("gy", "gz"))
    wave = rotated(wave, "gx", half)
    rb, rsb = call(
        late_kernel,
        [shape(2, EX * EY, BZ), shape(2, EY, BZ)],
        [receivers, receiver_wave],
        [],
        "vv",
        1.2,
    )
    early_planes, source_planes = (last - first for first, last in (EARLY_PLANES, SOURCE_PLANES))
    late, adj_late = call(
        merge_kernel,
        [shape(tile_rows(9) + EY + 8 + SPARE, BZ), shape(ADJ_OWN[2] + EY, BZ)],
        [from_up, from_down, corner_up, corner_down, strips, other, t, last_x, last_y, rsb],
        [pltpu.VMEM((WAVE_OWN[2], BZ), F32)],
        "vvvvvvvvva",
    )
    late = rotated(late, "gx", half)
    ra, rsa = call(
        early_kernel,
        [shape(2, early_planes * EY, BZ), shape(2, EY, BZ)],
        [receivers, receiver_wave, adj_late],
        [],
        "vva",
        1.0,
    )
    ra, rb = ra.reshape(2, early_planes, EY, BZ), rb.reshape(2, EX, EY, BZ)
    src, src_strip = call(
        source_kernel,
        [shape(STEPS - 1, source_planes * EY, BZ), shape(STEPS - 1, EY, BZ)],
        [sources, source_wave, adj_late],
        [],
        "vva",
        0.5,
    )
    even, odd = call(
        adjoint_join_kernel,
        [shape(ADJ_SIDE[1] + tile_rows(ADJ_TILES) + EY + 2 * PLANES, BZ)] * 2,
        [ql, adj_late, src_strip],
        [],
        "vva",
    )
    even, odd = paired(even, False), paired(odd, True)
    src = src.reshape(STEPS - 1, source_planes, EY, BZ)
    own_s, own_late, wave_even, wave_odd = call(
        join_kernel,
        [shape(PLANES, BZ), shape(WAVE_OWN[2] + EY, BZ)]
        + [shape(WAVE_SIDE[1] + tile_rows(WAVE_TILES) + EY, BZ)] * 2,
        [wave, late],
        [],
        "vv",
    )
    wave_even, wave_odd = paired(wave_even, False), paired(wave_odd, True)
    adjoint_out, hist, coef, coef_strip = call(
        adjoint_kernel,
        [
            shape(4, BX, BY, BZ),
            shape(STEPS, 4, BX, BY, BZ),
            shape(3, EX, EY, BZ),
            shape(3, EY, BZ),
        ],
        [ql, adj_late, even, odd, adjoint_end, ra, rsa, rb, rsb, table],
        [pltpu.VMEM((EX, EY, BZ), F32)] * 4
        + [
            pltpu.VMEM((STEPS, EX, EY, BZ), F32),
            pltpu.VMEM((3, EX, EY, BZ), F32),
            pltpu.SemaphoreType.DMA,
        ],
        "vvvvhvvvvv",
        3.9,
    )
    return call(
        forward_kernel,
        [shape(2, BX, BY, BZ), shape(4, BX, BY, BZ)],
        [
            wave, own_s, own_late, wave_even, wave_odd, coef, coef_strip, src, src_strip, hist,
            adjoint_out,
        ],
        [pltpu.VMEM((EX, EY, BZ), F32)] * 2
        + [
            pltpu.VMEM((STEPS, EX, EY, BZ), F32),
            pltpu.VMEM((3, EX, EY, BZ), F32),
            pltpu.VMEM((2, BX, BY, BZ), F32),
            pltpu.SemaphoreType.DMA((2 + BX,)),
        ],
        "vvvvvvvvvvv",
        2.5,
        "a",
    )


def solution(mesh):
    return jax.shard_map(
        local,
        mesh=mesh,
        in_specs=(
            P("shot", "gx", "gy", "gz"),
            P("shot", "gx", "gy", "gz"),
            P("gx", "gy", "gz"),
            P(),
            P("shot", None),
            P(None, "shot"),
            P(),
            P(None, "shot"),
        ),
        out_specs=(P("shot", "gx", "gy", "gz"), P("shot", "gx", "gy", "gz")),
        check_vma=False,
    )
```

```python
import functools

import jax
import jax.numpy as jnp
from jax import lax
from jax.experimental import pallas as pl
from jax.experimental.pallas import tpu as pltpu
from jax.sharding import PartitionSpec as P

STEPS = 4
MARGIN = 4
BX, BY, BZ = 4, 32, 128
EX, EY = BX + 2 * MARGIN, BY + 2 * MARGIN
STRIP = 2 * MARGIN
F32 = jnp.float32
BF16 = jnp.bfloat16
VMEM_LIMIT = 16 * 1024 * 1024
PLANES = BX * BY
WAVE_OWN = (0, BY, BY + 9 * 8)
FIX_LANE = 3 * BX * STRIP
SPARE = 64
ADJ_OWN = (PLANES, PLANES + BY, PLANES + BY + 13 * 8)
WAVE_SIDE = (PLANES + 3 * BY, PLANES + 4 * BY)
ADJ_SIDE = (3 * BY, 4 * BY)
WAVE_TILES, ADJ_TILES = 6, 9


def lanes(shape):
    return lax.broadcasted_iota(jnp.int32, shape, len(shape) - 1)


def rows(shape):
    return lax.broadcasted_iota(jnp.int32, shape, len(shape) - 2)


def run(copies):
    for copy in copies:
        copy.start()
    for copy in copies:
        copy.wait()


def coefficients(labels, table_ref):
    result = [jnp.zeros(labels.shape, F32) for _ in range(3)]
    for index in range(8):
        picked = labels == float(index + 1)
        for kind in range(3):
            row = kind * 8 + index
            result[kind] = jnp.where(picked, table_ref[row : row + 1], result[kind])
    return result


def buoyancy_of(labels, table_ref):
    result = jnp.zeros(labels.shape, F32)
    for index in range(8):
        result = jnp.where(labels == float(index + 1), table_ref[8 + index : 9 + index], result)
    return result


def half_turn(tile):
    return pltpu.roll(tile, MARGIN, 0)


def load_kernel(
    stored_hbm, adj_hbm, lab_hbm, tissue_hbm, rc_hbm, rw_hbm, sc_hbm, sw_hbm,
    wave_ref, ql_ref, t_ref, last_x_ref, last_y_ref, strip_ref, table_ref,
    rc_ref, rw_ref, sc_ref, sw_ref, *rest,
):
    *sends, stored, adj, lab, tissue, sem = rest
    run([
        pltpu.make_async_copy(source, target, sem)
        for source, target in (
            (stored_hbm, stored), (adj_hbm, adj), (lab_hbm, lab), (tissue_hbm, tissue),
            (rc_hbm, rc_ref), (rw_hbm, rw_ref), (sc_hbm, sc_ref), (sw_hbm, sw_ref),
        )
    ])
    for index in range(tissue.shape[1]):
        speed = jnp.full((1, BZ), tissue[0, index], F32)
        density = jnp.full((1, BZ), tissue[1, index], F32)
        table_ref[index : index + 1] = density * speed
        table_ref[8 + index : 9 + index] = speed / density
        table_ref[16 + index : 17 + index] = 1.0 - jnp.full((1, BZ), tissue[2, index], F32)
    gy, gz = lax.axis_index("gy"), lax.axis_index("gz")
    lane = lanes((BY, BZ))
    row = rows((BY, BZ))
    tile_row = rows((8, BZ))
    strips = [jnp.zeros((BY, BZ), F32) for _ in range(3)]
    tiles = [None] * 39
    previous = [None, None]

    def edge_tile(block):
        return jnp.where(tile_row < MARGIN, block[0:8], block[BY - 8 : BY])

    for x in range(BX):
        labels = lab[x].astype(F32) + 1.0
        buoyancy = buoyancy_of(labels, table_ref)
        plane = slice(x * BY, x * BY + BY)
        fields = [stored[index, x] for index in range(4)] + [adj[0, x]]
        fields += [buoyancy * adj[index, x] for index in range(1, 4)] + [labels]
        wave_ref[plane] = fields[0]
        ql_ref[plane] = fields[4]
        ql_ref[PLANES + x * BY : PLANES + x * BY + BY] = labels
        for index, block in enumerate(fields):
            tiles[index * BX + x] = edge_tile(block)
            group, slot = divmod(index, 4)
            base = slot * BX * STRIP + x * STRIP
            rolled = pltpu.roll(block, base + MARGIN, 1)
            first = base + MARGIN * gz
            strips[group] = jnp.where(
                (lane >= first) & (lane < first + MARGIN), rolled, strips[group]
            )
        for kind, (target, base) in enumerate(((wave_ref, PLANES), (t_ref, 0))):
            vx, vy, vz = fields[4 * kind + 1 : 4 * kind + 4]
            spread = vx if x == 0 else vx - previous[kind]
            spread = spread + (vy - jnp.where(row == 0, 0.0, pltpu.roll(vy, 1, 0)))
            spread = spread + (vz - jnp.where(lane == 0, 0.0, pltpu.roll(vz, 1, 1)))
            target[base + x * BY : base + x * BY + BY] = spread
            previous[kind] = vx
            index = (kind * BX + x) * 8
            last_y_ref[index : index + 8] = vy[BY - 8 : BY]
    wave_ref[2 * PLANES : 2 * PLANES + BY] = previous[0]
    wave_ref[2 * PLANES + BY :] = jnp.zeros((SPARE // 2, BZ), F32)
    last_x_ref[...] = previous[1]
    for group in range(3):
        strip_ref[group * BY : group * BY + BY] = strips[group]
        tiles[9 * BX + group] = edge_tile(strips[group])

    def joined(first, second):
        second = first if second is None else second
        upward = jnp.where(tile_row < MARGIN, half_turn(first), second)
        downward = jnp.where(tile_row < MARGIN, first, half_turn(second))
        if len(sends) == 2:
            return (jnp.where(gy == 0, upward, downward),)
        return upward, downward

    tiles.append(None)
    half = len(sends) // 2
    for place in range(20):
        for target, tile in zip(sends[:half], joined(tiles[2 * place], tiles[2 * place + 1])):
            target[place * 8 : place * 8 + 8] = tile
    for place in range(2):
        first = tiles[9 * BX + 2 * place]
        for target, tile in zip(sends[half:], joined(first, tiles[9 * BX + 2 * place + 1])):
            target[place * 8 : place * 8 + 8] = tile


def copy_rows(target, base, source, first, count):
    target[base : base + count] = source[pl.ds(pl.multiple_of(first, 8), count)]
    return base + count


def halved():
    return lax.axis_size("gy") == 2


def tile_rows(count):
    return (count + 1) // 2 * 8 if halved() else count * 8


def put_tiles(target, base, source, firsts):
    tiles = [source[pl.ds(pl.multiple_of(first, 8), 8)] for first in firsts]
    if halved():
        upper = lax.axis_index("gy") == 0
        row = rows((8, BZ))
        pairs = [(tiles[i], tiles[min(i + 1, len(tiles) - 1)]) for i in range(0, len(tiles), 2)]
        tiles = [
            jnp.where(
                row < MARGIN,
                jnp.where(upper, first, half_turn(first)),
                jnp.where(upper, half_turn(second), second),
            )
            for first, second in pairs
        ]
    for place, tile in enumerate(tiles):
        target[base + place * 8 : base + place * 8 + 8] = tile
    return base + 8 * len(tiles)


def pair_planes():
    parity = lax.rem(lax.axis_index("gx"), 2)
    return 1 - parity, parity


def merge_kernel(
    kinds,
    from_up, from_down, corner_up, corner_down, strip_ref, other_ref,
    t_ref, last_x_ref, last_y_ref, _,
    out_ref, wave_ref,
):
    gy = lax.axis_index("gy")
    tile_row = rows((8, BZ))
    row, lane = rows((BY, BZ)), lanes((BY, BZ))
    take_up = (tile_row < MARGIN) & (gy < lax.axis_size("gy") - 1)
    take_down = (tile_row >= MARGIN) & (gy > 0)
    _, cut_down = cut_flags()

    def halo(up, down, index):
        place, second = divmod(index, 2)
        sl = slice(place * 8, place * 8 + 8)
        above = half_turn(up[sl]) if second else up[sl]
        below = down[sl] if second else half_turn(down[sl])
        return jnp.where(take_up, above, jnp.where(take_down, below, 0.0))

    wide = []
    for group in range(3):
        sl = slice(group * BY, group * BY + BY)
        tile = halo(from_up, from_down, 9 * BX + group) + halo(corner_up, corner_down, group)
        wide.append(jnp.concatenate([strip_ref[sl] + other_ref[sl], tile], 0))
    strip_lane = lanes((EY, BZ))

    def strip_field(index):
        group, slot = divmod(index, 4)
        moved = pltpu.roll(wide[group], (BZ - slot * BX * STRIP) % BZ, 1) if slot else wide[group]
        return jnp.where(strip_lane < BX * STRIP, moved, 0.0)

    last_lanes = (BX - 1) * STRIP
    fix_row = jnp.zeros((8, BZ), F32)
    fix_lane = jnp.zeros((BY, BZ), F32)
    late_ref = out_ref
    for kind in kinds:
        target = (wave_ref, out_ref)[kind]
        first = 4 * kind
        planes_end, x_end, tiles_end = (WAVE_OWN, ADJ_OWN)[kind]
        vx, vy, vz = (strip_field(first + 1 + axis) for axis in range(3))
        spread = vx - jnp.where(strip_lane < STRIP, 0.0, pltpu.roll(vx, STRIP, 1))
        spread = (spread + (vy - y_down(vy))) + (vz - pltpu.roll(vz, 1, 1))
        strip = strip_field(first)
        strip = strip + pltpu.roll(jnp.where(strip_lane < BX * STRIP, spread, 0.0), BX * STRIP, 1)
        last_slot = 2
        if kind == 1:
            strip = strip + pltpu.roll(strip_field(8), 2 * BX * STRIP, 1)
            last_slot = 3
        last = jnp.where(strip_lane >= last_lanes, vx, 0.0)
        strip = strip + pltpu.roll(last, last_slot * BX * STRIP - last_lanes, 1)

        vx_before = None
        for x in range(BX):
            vx_t, vy_t, vz_t = (
                halo(from_up, from_down, (first + 1 + axis) * BX + x) for axis in range(3)
            )
            below_z = pltpu.roll(vz, (BZ - (x * STRIP + MARGIN - 1)) % BZ, 1) * cut_down
            last_y = last_y_ref[(kind * BX + x) * 8 : (kind * BX + x) * 8 + 8]
            y_before = jnp.where(
                tile_row == 0, pltpu.roll(last_y, 1, 0), pltpu.roll(vy_t, 1, 0)
            )
            z_before = jnp.where(lane[0:8] == 0, below_z[BY:EY], pltpu.roll(vz_t, 1, 1))
            spread = vx_t if x == 0 else vx_t - vx_before
            spread = (spread + (vy_t - y_before)) + (vz_t - z_before)
            vx_before = vx_t
            if kind == 0:
                fix_row = jnp.where(tile_row == x, vy_t[7:8], fix_row)
                moved = pltpu.roll(below_z[0:BY], FIX_LANE + x, 1)
                fix_lane = jnp.where(lane == FIX_LANE + x, moved, fix_lane)
            else:
                block = t_ref[x * BY : x * BY + BY]
                block = block - jnp.where(row == 0, vy_t[7:8], 0.0)
                block = block - jnp.where(lane == 0, below_z[0:BY], 0.0)
                target[x * BY : x * BY + BY] = block
            base = x_end + x * 8
            target[base : base + 8] = halo(from_up, from_down, first * BX + x)
            target[base + 32 : base + 40] = spread
            if kind == 1:
                target[base + 64 : base + 72] = halo(from_up, from_down, 8 * BX + x)
        target[tiles_end - 8 : tiles_end] = vx_before
        if kind == 0:
            base = put_tiles(late_ref, 0, wave_ref, range(x_end, tiles_end, 8))
            late_ref[base : base + BY] = strip[0:BY] + fix_lane
            late_ref[base + BY : base + EY] = strip[BY:EY]
            late_ref[base + EY : base + EY + 8] = fix_row
            late_ref[base + EY + 8 : base + EY + 8 + SPARE] = jnp.zeros((SPARE, BZ), F32)
        else:
            target[planes_end:x_end] = last_x_ref[...]
            target[tiles_end : tiles_end + EY] = strip


def adjoint_join_kernel(ql_ref, adj_ref, even_ref, odd_ref):
    planes_end, x_end, tiles_end = ADJ_OWN
    for target, first in zip((even_ref, odd_ref), pair_planes()):
        base = copy_rows(target, 0, adj_ref, first * BY, 3 * BY)
        base = copy_rows(target, base, adj_ref, planes_end, BY)
        near = [x_end + (first + plane) * 8 for plane in range(3)]
        nearest = [x_end + 32 + first * 16 + plane * 8 for plane in range(2)]
        firsts = near + nearest + [start + 64 for start in near] + [tiles_end - 8]
        base = put_tiles(target, base, adj_ref, firsts)
        base = copy_rows(target, base, adj_ref, tiles_end, EY)
        copy_rows(target, base, ql_ref, 0, 2 * PLANES)


def unpacked(tile, place):
    upper = lax.axis_index("gy") == 0
    turned = half_turn(tile)
    tile = jnp.where(upper, turned, tile) if place % 2 else jnp.where(upper, tile, turned)
    return jnp.where((rows((8, BZ)) < MARGIN) == upper, tile, 0.0)


def join_kernel(wave_ref, late_ref, s_ref, own_ref, even_ref, odd_ref):
    planes_end, x_end, tiles_end = WAVE_OWN
    own_ref[planes_end:x_end] = wave_ref[2 * PLANES : 2 * PLANES + BY]
    for place in range((tiles_end - x_end) // 8):
        if halved():
            tile = unpacked(late_ref[place // 2 * 8 : place // 2 * 8 + 8], place)
        else:
            tile = late_ref[place * 8 : place * 8 + 8]
        own_ref[x_end + place * 8 : x_end + place * 8 + 8] = tile
    strip = tile_rows((tiles_end - x_end) // 8)
    own_ref[tiles_end : tiles_end + EY] = late_ref[strip : strip + EY]
    row, lane = rows((BY, BZ)), lanes((BY, BZ))
    fix_lane = late_ref[strip : strip + BY]
    for x in range(BX):
        block = wave_ref[PLANES + x * BY : PLANES + x * BY + BY]
        fix_row = late_ref[strip + EY + x : strip + EY + x + 1]
        block = block - jnp.where(row == 0, fix_row, 0.0)
        block = block - jnp.where(lane == 0, pltpu.roll(fix_lane, BZ - FIX_LANE - x, 1), 0.0)
        s_ref[x * BY : x * BY + BY] = block
    for target, first in zip((even_ref, odd_ref), pair_planes()):
        base = copy_rows(target, 0, wave_ref, 0, PLANES)
        base = copy_rows(target, base, s_ref, first * BY, 3 * BY)
        base = copy_rows(target, base, own_ref, planes_end, BY)
        near = [x_end + (first + plane) * 8 for plane in range(3)]
        nearest = [x_end + 32 + first * 16 + plane * 8 for plane in range(2)]
        base = put_tiles(target, base, own_ref, near + nearest + [tiles_end - 8])
        copy_rows(target, base, own_ref, tiles_end, EY)


def split(values):
    high = values.astype(BF16)
    rest = values - high.astype(F32)
    middle = rest.astype(BF16)
    low = (rest - middle.astype(F32)).astype(BF16)
    return high, middle, low


def places(cells, sl):
    gx, gy, gz = (lax.axis_index(name) for name in ("gx", "gy", "gz"))
    cut = BZ * lax.axis_size("gz") // 2 - MARGIN
    cell_x = cells[0:1, sl] - (gx * BX - MARGIN)
    cell_y = cells[1:2, sl] - gy * BY
    cell_z = cells[2:3, sl]
    in_x = (cell_x >= 0) & (cell_x < EX)
    in_y = (cell_y >= -MARGIN) & (cell_y < BY + MARGIN)
    row = jnp.where(cell_y < 0, cell_y + EY, cell_y)
    flat = jnp.where(in_x & in_y, cell_x * EY + row, -1)
    row = jnp.where(in_y, row, -1)
    zz = cell_z - cut
    in_strip = in_x & (zz >= 0) & (zz < STRIP)
    strip_lane = jnp.where(in_strip, cell_x * STRIP + zz, -1)
    return flat, cell_z - gz * BZ, row, strip_lane


def hits(count, index):
    return rows((count, index.shape[1])) == index


def product(left, right):
    return lax.dot_general(
        left, right, (((1,), (1,)), ((), ())), preferred_element_type=F32
    )


def inject_points(cells, wave_ref, width, waves, planes, out_ref, strip_out_ref):
    count, low, total_rows = len(waves), planes[0] * EY, (planes[1] - planes[0]) * EY
    for start in range(0, cells.shape[1], width):
        sl = slice(start, start + width)
        flat, z, row, strip_lane = places(cells, sl)
        here = hits(total_rows, flat - low).astype(F32).astype(BF16)
        at_strip = hits(BZ, strip_lane).astype(F32).astype(BF16)
        at_z, at_row = hits(BZ, z), hits(EY, row)
        total = strip_total = None
        parts = [split(wave_ref[wave : wave + 1, sl]) for wave in waves]
        for part in range(3):
            amounts = [parts[wave][part].astype(F32) for wave in range(count)]
            right = jnp.concatenate([jnp.where(at_z, a, 0.0) for a in amounts], 0).astype(BF16)
            left = jnp.concatenate([jnp.where(at_row, a, 0.0) for a in amounts], 0).astype(BF16)
            term, strip_term = product(here, right), product(left, at_strip)
            total = term if part == 0 else total + term
            strip_total = strip_term if part == 0 else strip_total + strip_term
        for wave in range(count):
            value = total[:, wave * BZ : wave * BZ + BZ]
            strip_value = strip_total[wave * EY : wave * EY + EY]
            if start > 0:
                value = value + out_ref[wave]
                strip_value = strip_value + strip_out_ref[wave]
            out_ref[wave] = value
            strip_out_ref[wave] = strip_value


LATE_PLANES, EARLY_PLANES, SOURCE_PLANES = (0, EX), (2, EX - 2), (1, EX - 1)


def late_kernel(receivers, receiver_wave, r_ref, rs_ref):
    inject_points(receivers, receiver_wave, 256, (2, 3), LATE_PLANES, r_ref, rs_ref)


def early_kernel(receivers, receiver_wave, _, r_ref, rs_ref):
    inject_points(receivers, receiver_wave, 256, (0, 1), EARLY_PLANES, r_ref, rs_ref)


def source_kernel(sources, source_wave, _, s_ref, ss_ref):
    width = sources.shape[1]
    inject_points(sources, source_wave, width, (0, 1, 2), SOURCE_PLANES, s_ref, ss_ref)


def strip_of(packed, block, slot):
    lane = lanes(packed.shape)
    width = BX * STRIP
    shift = (block * width - slot * width) % BZ
    moved = pltpu.roll(packed, shift, 1) if shift else packed
    return jnp.where((lane >= block * width) & (lane < (block + 1) * width), moved, 0.0)


def y_up(v):
    return pltpu.roll(v, EY - 1, 0)


def y_down(v):
    return pltpu.roll(v, 1, 0)


def z_up(v, edge):
    return jnp.where(lanes(v.shape) == BZ - 1, edge, pltpu.roll(v, BZ - 1, 1))


def z_down(v, edge):
    return jnp.where(lanes(v.shape) == 0, edge, pltpu.roll(v, 1, 1))


def cut_edges(values, flux_z, cut_up, cut_down):
    place = lax.rem(lanes(values.shape), STRIP)
    above = jnp.where(place == MARGIN, values * cut_up, 0.0)
    below = jnp.where(place == MARGIN - 1, flux_z * cut_down, 0.0)
    return pltpu.roll(above, BZ - 2, 1) + below


def plane_edge(edges, x):
    return pltpu.roll(edges, (BZ - (x * STRIP + MARGIN - 1)) % BZ, 1)


def strip_flux(values, buoyancy):
    flux_x = buoyancy * (pltpu.roll(values, BZ - STRIP, 1) - values)
    flux_y = buoyancy * (y_up(values) - values)
    flux_z = buoyancy * (pltpu.roll(values, BZ - 1, 1) - values)
    spread = (flux_x - pltpu.roll(flux_x, STRIP, 1)) + (flux_y - y_down(flux_y))
    return flux_z, spread + (flux_z - pltpu.roll(flux_z, 1, 1))


def cut_flags():
    gz, half = lax.axis_index("gz"), lax.axis_size("gz") // 2
    return jnp.where(gz == half - 1, 1.0, 0.0), jnp.where(gz == half, 1.0, 0.0)


def sides():
    gx = lax.axis_index("gx")
    low = jnp.where(gx > 0, 1.0, 0.0)
    high = jnp.where(gx < lax.axis_size("gx") - 1, 1.0, 0.0)
    return low, high, lax.rem(gx, 2) == 0


def from_side(messages, first, count, block, side):
    even, odd = (message[first : first + count] for message in messages)
    low, high, even_above = side
    if block == 0:
        return jnp.where(even_above, odd, even) * low
    return jnp.where(even_above, even, odd) * high


def side_tile(messages, base, place, block, side):
    if not halved():
        return from_side(messages, base + place * 8, 8, block, side)
    tile = from_side(messages, base + place // 2 * 8, 8, block, side)
    return unpacked(tile, place)


def side_place(wanted, plane, block):
    planes = range(BX - wanted, BX) if block == 0 else range(wanted)
    return planes.index(plane) if plane in planes else None


def widened(own, own_tiles, x, layout, side):
    block, plane = divmod(x, BX)
    if block == 1:
        main = own[0][own[1] + plane * BY : own[1] + plane * BY + BY]
        tile = own_tiles[0][own_tiles[1] + plane * 8 : own_tiles[1] + plane * 8 + 8]
        return jnp.concatenate([main, tile], 0)
    (messages, base, wanted), (tile_messages, tile_base, tile_place, tile_wanted) = layout
    main, tile = jnp.zeros((BY, BZ), F32), jnp.zeros((8, BZ), F32)
    place = side_place(wanted, plane, block)
    if place is not None:
        main = from_side(messages, base + place * BY, BY, block, side)
    place = side_place(tile_wanted, plane, block)
    if place is not None:
        tile = side_tile(tile_messages, tile_base, tile_place + place, block, side)
    return jnp.concatenate([main, tile], 0)


def less_plane_below(value, x, own_ref, own_rows, messages, side_layout, side):
    if x == BX:
        (planes_end, x_end), count = side_layout
        main = from_side(messages, planes_end, BY, 0, side)
        tile = side_tile(messages, x_end, count - 1, 0, side)
    elif x == 2 * BX:
        planes_end, _, tiles_end = own_rows
        high = side[1]
        main = own_ref[planes_end : planes_end + BY] * high
        tile = own_ref[tiles_end - 8 : tiles_end] * high
    else:
        return value
    return value - jnp.concatenate([main, tile], 0)


def strip_below(own, messages, first, slot, side):
    lane = lanes(own.shape)
    width = BX * STRIP
    low = from_side(messages, first, EY, 0, side)
    low = pltpu.roll(low, (width - slot * width) % BZ, 1)
    own = pltpu.roll(own * side[1], (2 * width - slot * width) % BZ, 1)
    in_own = (lane >= width) & (lane < width + STRIP)
    in_high = (lane >= 2 * width) & (lane < 2 * width + STRIP)
    return jnp.where(in_own, low, jnp.where(in_high, own, 0.0))


def whole_strip(own, messages, first, slot, side):
    low = from_side(messages, first, EY, 0, side)
    high = from_side(messages, first, EY, 2, side)
    return strip_of(low, 0, slot) + strip_of(own, 1, slot) + strip_of(high, 2, slot)


def adjoint_kernel(
    ql_ref, late_ref, even, odd, adj_hbm, ra_ref, rsa_ref, rb_ref, rsb_ref,
    table_ref,
    out_ref, hist_ref, coef_ref, coef_strip_ref,
    q_ref, t_ref, u_ref, scale_ref, edge_ref, flux_ref, w_sem,
):
    w_copy = pltpu.make_async_copy(adj_hbm.at[pl.ds(1, 3)], out_ref.at[pl.ds(1, 3)], w_sem)
    w_copy.start()
    cut_up, cut_down = cut_flags()
    side = sides()
    messages = (even, odd)
    r_refs = ((ra_ref, 0), (ra_ref, 1), (rb_ref, 0), (rb_ref, 1))
    rs_refs = ((rsa_ref, 0), (rsa_ref, 1), (rsb_ref, 0), (rsb_ref, 1))
    tiles, own_tiles = ADJ_SIDE[1], ADJ_OWN[1]
    side_strip = tiles + tile_rows(ADJ_TILES)
    raws = side_strip + EY

    def initial(index, x):
        own = ((ql_ref, 0), (late_ref, 0), (ql_ref, PLANES))[index]
        layout = (
            ((messages, raws, 4), (messages, tiles, 0, 3)),
            ((messages, 0, 3), (messages, tiles, 3, 2)),
            ((messages, raws + PLANES, 4), (messages, tiles, 5, 3)),
        )[index]
        value = widened(own, (late_ref, own_tiles + 32 * index), x, layout, side)
        if index == 1:
            value = less_plane_below(
                value, x, late_ref, ADJ_OWN, messages, (ADJ_SIDE, ADJ_TILES), side
            )
        return value

    for x in range(EX):
        stiff, buoy, damp = coefficients(initial(2, x), table_ref)
        coef_ref[0, x], coef_ref[1, x], coef_ref[2, x] = stiff, buoy, damp
        scale_ref[x] = stiff * damp
    own_strip = late_ref[ADJ_OWN[2] : ADJ_OWN[2] + EY]
    q_s, t_s, label_s = (
        whole_strip(own_strip, messages, side_strip, slot, side) for slot in range(3)
    )
    t_s = t_s - strip_below(own_strip, messages, side_strip, 3, side)
    stiff_s, buoy_s, damp_s = coefficients(label_s, table_ref)
    scale_s = stiff_s * damp_s
    coef_strip_ref[0], coef_strip_ref[1], coef_strip_ref[2] = stiff_s, buoy_s, damp_s
    w_copy.wait()

    for step in range(1, STEPS + 1):
        rs_ref, place = rs_refs[STEPS - step]
        q_s = q_s + rs_ref[place]
        u_s = scale_s * q_s
        flux_s, spread = strip_flux(u_s, buoy_s)
        t_s = t_s + spread
        q_s = damp_s * q_s + t_s
        edges = cut_edges(u_s, flux_s, cut_up, cut_down)
        for x in range(step, EX - step):
            edge_ref[step - 1, x] = plane_edge(edges, x)

    for step in range(1, STEPS + 1):
        k = STEPS - step
        r_ref, place = r_refs[k]
        r_first = (EARLY_PLANES if k < 2 else LATE_PLANES)[0]

        for x in range(step - 1, EX - step + 1):
            q = (initial(0, x) if step == 1 else q_ref[x]) + r_ref[place, x - r_first]
            q_ref[x] = q
            u_ref[x] = scale_ref[x] * q

        for x in range(step - 1, EX - step):
            u, buoyancy = u_ref[x], coef_ref[1, x]
            slopes = [u_ref[x + 1] - u]
            if x >= step:
                slopes += [y_up(u) - u, z_up(u, edge_ref[step - 1, x]) - u]
            for axis, slope in enumerate(slopes):
                flux_ref[axis, x] = buoyancy * slope
            if BX <= x < 2 * BX:
                for axis, slope in enumerate(slopes):
                    w = out_ref[1 + axis, x - BX] + slope[0:BY]
                    out_ref[1 + axis, x - BX] = w
                    hist_ref[k, 1 + axis, x - BX] = w

        for x in range(step, EX - step):
            flux_y, flux_z = flux_ref[1, x], flux_ref[2, x]
            spread = (flux_ref[0, x] - flux_ref[0, x - 1]) + (flux_y - y_down(flux_y))
            spread = spread + (flux_z - z_down(flux_z, edge_ref[step - 1, x]))
            damped = coef_ref[2, x] * q_ref[x]
            t = (initial(1, x) if step == 1 else t_ref[x]) + spread
            if BX <= x < 2 * BX:
                hist_ref[k, 0, x - BX] = damped[0:BY]
            if step < STEPS:
                t_ref[x] = t
                q_ref[x] = damped + t
            else:
                out_ref[0, x - BX] = (damped + t)[0:BY]


def forward_kernel(
    wave_ref, own_s_ref, late_ref, even, odd, coef_ref, coef_strip_ref, s_ref, ss_ref, hist_ref,
    adjoint_ref, grad_hbm, adjoint_hbm,
    p_ref, spread_ref, edge_ref, flux_ref, grad_ref, sems,
):
    copies = [pltpu.make_async_copy(adjoint_ref, adjoint_hbm, sems.at[0])]
    copies[0].start()

    def send(index, kind, first, count):
        planes = pl.ds(first, count)
        copy = pltpu.make_async_copy(
            grad_ref.at[kind, planes], grad_hbm.at[kind, planes], sems.at[index]
        )
        copy.start()
        copies.append(copy)

    cut_up, cut_down = cut_flags()
    side = sides()
    messages = (even, odd)
    tiles, own_tiles = WAVE_SIDE[1], WAVE_OWN[1]
    side_strip = tiles + tile_rows(WAVE_TILES)

    def initial(index, x):
        layout = (
            ((messages, 0, 4), (messages, tiles, 0, 3)),
            ((messages, PLANES, 3), (messages, tiles, 3, 2)),
        )[index]
        own = ((wave_ref, 0), (own_s_ref, 0))[index]
        value = widened(own, (late_ref, own_tiles + 32 * index), x, layout, side)
        if index == 1:
            value = less_plane_below(
                value, x, late_ref, WAVE_OWN, messages, (WAVE_SIDE, WAVE_TILES), side
            )
        return value

    own_strip = late_ref[WAVE_OWN[2] : WAVE_OWN[2] + EY]
    p_s, s_s = (
        whole_strip(own_strip, messages, side_strip, slot, side) for slot in range(2)
    )
    s_s = s_s - strip_below(own_strip, messages, side_strip, 2, side)
    stiff_s, buoy_s, damp_s = coef_strip_ref[0], coef_strip_ref[1], coef_strip_ref[2]

    for step in range(1, STEPS + 1):
        flux_s, spread = strip_flux(p_s, buoy_s)
        edges = cut_edges(p_s, flux_s, cut_up, cut_down)
        if step < STEPS:
            s_s = s_s - spread
            p_s = damp_s * (p_s - stiff_s * s_s) + ss_ref[step - 1]
        for x in range(step, EX - step):
            edge_ref[step - 1, x] = plane_edge(edges, x)
    for x in range(EX):
        p_ref[x] = initial(0, x)

    for step in range(1, STEPS + 1):
        k = step - 1
        for x in range(step - 1, EX - step):
            p, buoyancy = p_ref[x], coef_ref[1, x]
            slopes = [p_ref[x + 1] - p]
            if x >= step:
                slopes += [y_up(p) - p, z_up(p, edge_ref[step - 1, x]) - p]
            for axis, slope in enumerate(slopes):
                flux_ref[axis, x] = buoyancy * slope
            if BX <= x < 2 * BX:
                place = x - BX
                term = hist_ref[k, 1, place] * slopes[0][0:BY]
                term = term + hist_ref[k, 2, place] * slopes[1][0:BY]
                term = term + hist_ref[k, 3, place] * slopes[2][0:BY]
                grad_ref[1, place] = -term if k == 0 else grad_ref[1, place] - term
        if step == STEPS:
            send(1, 1, 0, BX)

        for x in range(step, EX - step):
            flux_y, flux_z = flux_ref[1, x], flux_ref[2, x]
            spread = (flux_ref[0, x] - flux_ref[0, x - 1]) + (flux_y - y_down(flux_y))
            spread = spread + (flux_z - z_down(flux_z, edge_ref[step - 1, x]))
            spread = (initial(1, x) if step == 1 else spread_ref[x]) - spread
            if step < STEPS:
                spread_ref[x] = spread
                p_ref[x] = (
                    coef_ref[2, x] * (p_ref[x] - coef_ref[0, x] * spread)
                    + s_ref[k, x - SOURCE_PLANES[0]]
                )
            if BX <= x < 2 * BX:
                place = x - BX
                term = hist_ref[k, 0, place] * spread[0:BY]
                grad_ref[0, place] = -term if k == 0 else grad_ref[0, place] - term
                if step == STEPS:
                    send(2 + place, 0, place, 1)
    for copy in copies:
        copy.wait()


def shape(*dims):
    return jax.ShapeDtypeStruct(dims, F32)


def call(kernel, outs, operands, scratch, places, micros=0.1, out_place="v"):
    spaces = {"h": pltpu.HBM, "a": pl.ANY, "v": pltpu.VMEM}
    operands = [
        pltpu.with_memory_space_constraint(operand, pltpu.HBM) if place == "h" else operand
        for operand, place in zip(operands, places)
    ]
    return pl.pallas_call(
        kernel,
        out_shape=outs,
        in_specs=[pl.BlockSpec(memory_space=spaces[place]) for place in places],
        out_specs=[pl.BlockSpec(memory_space=spaces[out_place])] * len(outs),
        scratch_shapes=scratch,
        compiler_params=pltpu.CompilerParams(vmem_limit_bytes=VMEM_LIMIT),
        cost_estimate=pl.CostEstimate(
            flops=0, bytes_accessed=int(3.69e6 * micros), transcendentals=0
        ),
    )(*operands)


def from_sides(sends, axes):
    count = lax.axis_size("gy")

    def route(offset):
        pairs = []
        for target in range(count):
            source = target + offset
            if 0 <= source < count:
                if "gz" in axes:
                    pairs += [(2 * source + z, 2 * target + 1 - z) for z in range(2)]
                else:
                    pairs.append((source, target))
        return pairs

    if count == 2:
        both = lax.ppermute(sends[0], axes, route(1) + route(-1))
        return both, both
    upward, downward = sends
    return lax.ppermute(downward, axes, route(1)), lax.ppermute(upward, axes, route(-1))


def rotated(array, axis, offset):
    count = lax.axis_size(axis)
    return lax.ppermute(array, axis, [((i + offset) % count, i) for i in range(count)])


def paired(array, odd):
    count = lax.axis_size("gx")
    pairs = []
    for i in range(count):
        partner = ((i - 1) ^ 1) + 1 if odd else i ^ 1
        pairs.append((partner if 0 <= partner < count else i, i))
    return lax.ppermute(array, "gx", pairs)


def local(
    stored, adjoint_end, labels, tissue, source_cells, source_wave, receiver_cells, receiver_wave
):
    assert lax.axis_size("gz") == 2 and labels.shape == (BX, BY, BZ) and tissue.shape[1] == 8
    half = lax.axis_size("gx") // 2
    arguments = [
        stored, adjoint_end, labels, tissue,
        receiver_cells.T, receiver_wave, source_cells.T, source_wave,
    ]
    ways = 1 if lax.axis_size("gy") == 2 else 2
    wave, ql, t, last_x, last_y, strips, table, receivers, receiver_wave, sources, source_wave, *sends = call(
        load_kernel,
        [
            shape(2 * PLANES + BY + SPARE // 2, BZ),
            shape(2 * PLANES, BZ),
            shape(PLANES, BZ),
            shape(BY, BZ),
            shape(2 * BX * 8, BZ),
            shape(3 * BY, BZ),
            shape(24, BZ),
        ]
        + [jax.ShapeDtypeStruct(array.shape, array.dtype) for array in arguments[4:]]
        + [shape(20 * 8, BZ)] * ways
        + [shape(2 * 8, BZ)] * ways,
        arguments,
        [
            pltpu.VMEM(stored.shape, F32),
            pltpu.VMEM(adjoint_end.shape, F32),
            pltpu.VMEM(labels.shape, jnp.int32),
            pltpu.SMEM(tissue.shape, F32),
            pltpu.SemaphoreType.DMA,
        ],
        "hhhhhhhh",
        1.4,
    )
    from_up, from_down = from_sides(sends[:ways], "gy")
    other = rotated(strips, "gz", 1)
    corner_up, corner_down = from_sides(sends[ways:], ("gy", "gz"))
    wave = rotated(wave, "gx", half)
    rb, rsb = call(
        late_kernel,
        [shape(2, EX * EY, BZ), shape(2, EY, BZ)],
        [receivers, receiver_wave],
        [],
        "vv",
        1.2,
    )
    early_planes, source_planes = (last - first for first, last in (EARLY_PLANES, SOURCE_PLANES))
    ends = [from_up, from_down, corner_up, corner_down, strips, other, t, last_x, last_y]
    (late,) = call(
        functools.partial(merge_kernel, (0,)),
        [shape(tile_rows(9) + EY + 8 + SPARE, BZ)],
        ends + [rsb],
        [pltpu.VMEM((WAVE_OWN[2], BZ), F32)],
        "vvvvvvvvva",
    )
    (adj_late,) = call(
        functools.partial(merge_kernel, (1,)),
        [shape(ADJ_OWN[2] + EY, BZ)],
        ends + [late],
        [pltpu.VMEM((WAVE_OWN[2], BZ), F32)],
        "vvvvvvvvva",
    )
    late = rotated(late, "gx", half)
    ra, rsa = call(
        early_kernel,
        [shape(2, early_planes * EY, BZ), shape(2, EY, BZ)],
        [receivers, receiver_wave, adj_late],
        [],
        "vva",
        1.0,
    )
    ra, rb = ra.reshape(2, early_planes, EY, BZ), rb.reshape(2, EX, EY, BZ)
    even, odd = call(
        adjoint_join_kernel,
        [shape(ADJ_SIDE[1] + tile_rows(ADJ_TILES) + EY + 2 * PLANES, BZ)] * 2,
        [ql, adj_late],
        [],
        "vv",
    )
    even, odd = paired(even, False), paired(odd, True)
    src, src_strip = call(
        source_kernel,
        [shape(STEPS - 1, source_planes * EY, BZ), shape(STEPS - 1, EY, BZ)],
        [sources, source_wave, adj_late],
        [],
        "vva",
        0.5,
    )
    src = src.reshape(STEPS - 1, source_planes, EY, BZ)
    own_s, own_late, wave_even, wave_odd = call(
        join_kernel,
        [shape(PLANES, BZ), shape(WAVE_OWN[2] + EY, BZ)]
        + [shape(WAVE_SIDE[1] + tile_rows(WAVE_TILES) + EY, BZ)] * 2,
        [wave, late],
        [],
        "vv",
    )
    wave_even, wave_odd = paired(wave_even, False), paired(wave_odd, True)
    adjoint_out, hist, coef, coef_strip = call(
        adjoint_kernel,
        [
            shape(4, BX, BY, BZ),
            shape(STEPS, 4, BX, BY, BZ),
            shape(3, EX, EY, BZ),
            shape(3, EY, BZ),
        ],
        [ql, adj_late, even, odd, adjoint_end, ra, rsa, rb, rsb, table],
        [pltpu.VMEM((EX, EY, BZ), F32)] * 4
        + [
            pltpu.VMEM((STEPS, EX, EY, BZ), F32),
            pltpu.VMEM((3, EX, EY, BZ), F32),
            pltpu.SemaphoreType.DMA,
        ],
        "vvvvhvvvvv",
        3.9,
    )
    return call(
        forward_kernel,
        [shape(2, BX, BY, BZ), shape(4, BX, BY, BZ)],
        [
            wave, own_s, own_late, wave_even, wave_odd, coef, coef_strip, src, src_strip, hist,
            adjoint_out,
        ],
        [pltpu.VMEM((EX, EY, BZ), F32)] * 2
        + [
            pltpu.VMEM((STEPS, EX, EY, BZ), F32),
            pltpu.VMEM((3, EX, EY, BZ), F32),
            pltpu.VMEM((2, BX, BY, BZ), F32),
            pltpu.SemaphoreType.DMA((2 + BX,)),
        ],
        "vvvvvvvvvvv",
        2.5,
        "a",
    )


def solution(mesh):
    return jax.shard_map(
        local,
        mesh=mesh,
        in_specs=(
            P("shot", "gx", "gy", "gz"),
            P("shot", "gx", "gy", "gz"),
            P("gx", "gy", "gz"),
            P(),
            P("shot", None),
            P(None, "shot"),
            P(),
            P(None, "shot"),
        ),
        out_specs=(P("shot", "gx", "gy", "gz"), P("shot", "gx", "gy", "gz")),
        check_vma=False,
    )
```

```python
import jax
import jax.numpy as jnp
from jax import lax
from jax.experimental import pallas as pl
from jax.experimental.pallas import tpu as pltpu
from jax.sharding import PartitionSpec as P

STEPS = 4
MARGIN = 4
BX, BY, BZ = 4, 32, 128
EX, EY = BX + 2 * MARGIN, BY + 2 * MARGIN
STRIP = 2 * MARGIN
F32 = jnp.float32
BF16 = jnp.bfloat16
VMEM_LIMIT = 16 * 1024 * 1024
PLANES = BX * BY
WAVE_OWN = (0, BY, BY + 9 * 8)
FIX_LANE = 3 * BX * STRIP
SPARE = 64
ADJ_OWN = (PLANES, PLANES + BY, PLANES + BY + 13 * 8)
WAVE_SIDE = (PLANES + 3 * BY, PLANES + 4 * BY)
ADJ_SIDE = (3 * BY, 4 * BY)
WAVE_TILES, ADJ_TILES = 6, 9


def lanes(shape):
    return lax.broadcasted_iota(jnp.int32, shape, len(shape) - 1)


def rows(shape):
    return lax.broadcasted_iota(jnp.int32, shape, len(shape) - 2)


def run(copies):
    for copy in copies:
        copy.start()
    for copy in copies:
        copy.wait()


def coefficients(labels, table_ref):
    result = [jnp.zeros(labels.shape, F32) for _ in range(3)]
    for index in range(8):
        picked = labels == float(index + 1)
        for kind in range(3):
            row = kind * 8 + index
            result[kind] = jnp.where(picked, table_ref[row : row + 1], result[kind])
    return result


def buoyancy_of(labels, table_ref):
    result = jnp.zeros(labels.shape, F32)
    for index in range(8):
        result = jnp.where(labels == float(index + 1), table_ref[8 + index : 9 + index], result)
    return result


def half_turn(tile):
    return pltpu.roll(tile, MARGIN, 0)


def load_kernel(
    stored_hbm, adj_hbm, lab_hbm, tissue_hbm, rc_hbm, rw_hbm, sc_hbm, sw_hbm,
    wave_ref, ql_ref, t_ref, last_x_ref, last_y_ref, strip_ref, table_ref,
    rc_ref, rw_ref, sc_ref, sw_ref, *rest,
):
    *sends, stored, adj, lab, tissue, sem = rest
    run([
        pltpu.make_async_copy(source, target, sem)
        for source, target in (
            (stored_hbm, stored), (adj_hbm, adj), (lab_hbm, lab), (tissue_hbm, tissue),
            (rc_hbm, rc_ref), (rw_hbm, rw_ref), (sc_hbm, sc_ref), (sw_hbm, sw_ref),
        )
    ])
    for index in range(tissue.shape[1]):
        speed = jnp.full((1, BZ), tissue[0, index], F32)
        density = jnp.full((1, BZ), tissue[1, index], F32)
        table_ref[index : index + 1] = density * speed
        table_ref[8 + index : 9 + index] = speed / density
        table_ref[16 + index : 17 + index] = 1.0 - jnp.full((1, BZ), tissue[2, index], F32)
    gy, gz = lax.axis_index("gy"), lax.axis_index("gz")
    lane = lanes((BY, BZ))
    row = rows((BY, BZ))
    tile_row = rows((8, BZ))
    strips = [jnp.zeros((BY, BZ), F32) for _ in range(3)]
    tiles = [None] * 39
    previous = [None, None]

    def edge_tile(block):
        return jnp.where(tile_row < MARGIN, block[0:8], block[BY - 8 : BY])

    for x in range(BX):
        labels = lab[x].astype(F32) + 1.0
        buoyancy = buoyancy_of(labels, table_ref)
        plane = slice(x * BY, x * BY + BY)
        fields = [stored[index, x] for index in range(4)] + [adj[0, x]]
        fields += [buoyancy * adj[index, x] for index in range(1, 4)] + [labels]
        wave_ref[plane] = fields[0]
        ql_ref[plane] = fields[4]
        ql_ref[PLANES + x * BY : PLANES + x * BY + BY] = labels
        for index, block in enumerate(fields):
            tiles[index * BX + x] = edge_tile(block)
            group, slot = divmod(index, 4)
            base = slot * BX * STRIP + x * STRIP
            rolled = pltpu.roll(block, base + MARGIN, 1)
            first = base + MARGIN * gz
            strips[group] = jnp.where(
                (lane >= first) & (lane < first + MARGIN), rolled, strips[group]
            )
        for kind, (target, base) in enumerate(((wave_ref, PLANES), (t_ref, 0))):
            vx, vy, vz = fields[4 * kind + 1 : 4 * kind + 4]
            spread = vx if x == 0 else vx - previous[kind]
            spread = spread + (vy - jnp.where(row == 0, 0.0, pltpu.roll(vy, 1, 0)))
            spread = spread + (vz - jnp.where(lane == 0, 0.0, pltpu.roll(vz, 1, 1)))
            target[base + x * BY : base + x * BY + BY] = spread
            previous[kind] = vx
            index = (kind * BX + x) * 8
            last_y_ref[index : index + 8] = vy[BY - 8 : BY]
    wave_ref[2 * PLANES : 2 * PLANES + BY] = previous[0]
    wave_ref[2 * PLANES + BY :] = jnp.zeros((SPARE // 2, BZ), F32)
    last_x_ref[...] = previous[1]
    for group in range(3):
        strip_ref[group * BY : group * BY + BY] = strips[group]
        tiles[9 * BX + group] = edge_tile(strips[group])

    def joined(first, second):
        second = first if second is None else second
        upward = jnp.where(tile_row < MARGIN, half_turn(first), second)
        downward = jnp.where(tile_row < MARGIN, first, half_turn(second))
        if len(sends) == 2:
            return (jnp.where(gy == 0, upward, downward),)
        return upward, downward

    tiles.append(None)
    half = len(sends) // 2
    for place in range(20):
        for target, tile in zip(sends[:half], joined(tiles[2 * place], tiles[2 * place + 1])):
            target[place * 8 : place * 8 + 8] = tile
    for place in range(2):
        first = tiles[9 * BX + 2 * place]
        for target, tile in zip(sends[half:], joined(first, tiles[9 * BX + 2 * place + 1])):
            target[place * 8 : place * 8 + 8] = tile


def copy_rows(target, base, source, first, count):
    target[base : base + count] = source[pl.ds(pl.multiple_of(first, 8), count)]
    return base + count


def halved():
    return lax.axis_size("gy") == 2


def tile_rows(count):
    return (count + 1) // 2 * 8 if halved() else count * 8


def put_tiles(target, base, source, firsts):
    tiles = [source[pl.ds(pl.multiple_of(first, 8), 8)] for first in firsts]
    if halved():
        upper = lax.axis_index("gy") == 0
        row = rows((8, BZ))
        pairs = [(tiles[i], tiles[min(i + 1, len(tiles) - 1)]) for i in range(0, len(tiles), 2)]
        tiles = [
            jnp.where(
                row < MARGIN,
                jnp.where(upper, first, half_turn(first)),
                jnp.where(upper, half_turn(second), second),
            )
            for first, second in pairs
        ]
    for place, tile in enumerate(tiles):
        target[base + place * 8 : base + place * 8 + 8] = tile
    return base + 8 * len(tiles)


def pair_planes():
    parity = lax.rem(lax.axis_index("gx"), 2)
    return 1 - parity, parity


def merge_kernel(
    from_up, from_down, corner_up, corner_down, strip_ref, other_ref,
    t_ref, last_x_ref, last_y_ref, _,
    late_ref, adj_ref,
    wave_ref,
):
    gy = lax.axis_index("gy")
    tile_row = rows((8, BZ))
    row, lane = rows((BY, BZ)), lanes((BY, BZ))
    take_up = (tile_row < MARGIN) & (gy < lax.axis_size("gy") - 1)
    take_down = (tile_row >= MARGIN) & (gy > 0)
    _, cut_down = cut_flags()

    def halo(up, down, index):
        place, second = divmod(index, 2)
        sl = slice(place * 8, place * 8 + 8)
        above = half_turn(up[sl]) if second else up[sl]
        below = down[sl] if second else half_turn(down[sl])
        return jnp.where(take_up, above, jnp.where(take_down, below, 0.0))

    wide = []
    for group in range(3):
        sl = slice(group * BY, group * BY + BY)
        tile = halo(from_up, from_down, 9 * BX + group) + halo(corner_up, corner_down, group)
        wide.append(jnp.concatenate([strip_ref[sl] + other_ref[sl], tile], 0))
    strip_lane = lanes((EY, BZ))

    def strip_field(index):
        group, slot = divmod(index, 4)
        moved = pltpu.roll(wide[group], (BZ - slot * BX * STRIP) % BZ, 1) if slot else wide[group]
        return jnp.where(strip_lane < BX * STRIP, moved, 0.0)

    last_lanes = (BX - 1) * STRIP
    fix_row = jnp.zeros((8, BZ), F32)
    fix_lane = jnp.zeros((BY, BZ), F32)
    for kind, target in enumerate((wave_ref, adj_ref)):
        first = 4 * kind
        planes_end, x_end, tiles_end = (WAVE_OWN, ADJ_OWN)[kind]
        vx, vy, vz = (strip_field(first + 1 + axis) for axis in range(3))
        spread = vx - jnp.where(strip_lane < STRIP, 0.0, pltpu.roll(vx, STRIP, 1))
        spread = (spread + (vy - y_down(vy))) + (vz - pltpu.roll(vz, 1, 1))
        strip = strip_field(first)
        strip = strip + pltpu.roll(jnp.where(strip_lane < BX * STRIP, spread, 0.0), BX * STRIP, 1)
        last_slot = 2
        if kind == 1:
            strip = strip + pltpu.roll(strip_field(8), 2 * BX * STRIP, 1)
            last_slot = 3
        last = jnp.where(strip_lane >= last_lanes, vx, 0.0)
        strip = strip + pltpu.roll(last, last_slot * BX * STRIP - last_lanes, 1)

        vx_before = None
        for x in range(BX):
            vx_t, vy_t, vz_t = (
                halo(from_up, from_down, (first + 1 + axis) * BX + x) for axis in range(3)
            )
            below_z = pltpu.roll(vz, (BZ - (x * STRIP + MARGIN - 1)) % BZ, 1) * cut_down
            last_y = last_y_ref[(kind * BX + x) * 8 : (kind * BX + x) * 8 + 8]
            y_before = jnp.where(
                tile_row == 0, pltpu.roll(last_y, 1, 0), pltpu.roll(vy_t, 1, 0)
            )
            z_before = jnp.where(lane[0:8] == 0, below_z[BY:EY], pltpu.roll(vz_t, 1, 1))
            spread = vx_t if x == 0 else vx_t - vx_before
            spread = (spread + (vy_t - y_before)) + (vz_t - z_before)
            vx_before = vx_t
            if kind == 0:
                fix_row = jnp.where(tile_row == x, vy_t[7:8], fix_row)
                moved = pltpu.roll(below_z[0:BY], FIX_LANE + x, 1)
                fix_lane = jnp.where(lane == FIX_LANE + x, moved, fix_lane)
            else:
                block = t_ref[x * BY : x * BY + BY]
                block = block - jnp.where(row == 0, vy_t[7:8], 0.0)
                block = block - jnp.where(lane == 0, below_z[0:BY], 0.0)
                target[x * BY : x * BY + BY] = block
            base = x_end + x * 8
            target[base : base + 8] = halo(from_up, from_down, first * BX + x)
            target[base + 32 : base + 40] = spread
            if kind == 1:
                target[base + 64 : base + 72] = halo(from_up, from_down, 8 * BX + x)
        target[tiles_end - 8 : tiles_end] = vx_before
        if kind == 0:
            base = put_tiles(late_ref, 0, wave_ref, range(x_end, tiles_end, 8))
            late_ref[base : base + BY] = strip[0:BY] + fix_lane
            late_ref[base + BY : base + EY] = strip[BY:EY]
            late_ref[base + EY : base + EY + 8] = fix_row
            late_ref[base + EY + 8 : base + EY + 8 + SPARE] = jnp.zeros((SPARE, BZ), F32)
        else:
            target[planes_end:x_end] = last_x_ref[...]
            target[tiles_end : tiles_end + EY] = strip


def adjoint_join_kernel(ql_ref, adj_ref, even_ref, odd_ref):
    planes_end, x_end, tiles_end = ADJ_OWN
    for target, first in zip((even_ref, odd_ref), pair_planes()):
        base = copy_rows(target, 0, adj_ref, first * BY, 3 * BY)
        base = copy_rows(target, base, adj_ref, planes_end, BY)
        near = [x_end + (first + plane) * 8 for plane in range(3)]
        nearest = [x_end + 32 + first * 16 + plane * 8 for plane in range(2)]
        firsts = near + nearest + [start + 64 for start in near] + [tiles_end - 8]
        base = put_tiles(target, base, adj_ref, firsts)
        base = copy_rows(target, base, adj_ref, tiles_end, EY)
        copy_rows(target, base, ql_ref, 0, 2 * PLANES)


def unpacked(tile, place):
    upper = lax.axis_index("gy") == 0
    turned = half_turn(tile)
    tile = jnp.where(upper, turned, tile) if place % 2 else jnp.where(upper, tile, turned)
    return jnp.where((rows((8, BZ)) < MARGIN) == upper, tile, 0.0)


def join_kernel(wave_ref, late_ref, s_ref, own_ref, even_ref, odd_ref):
    planes_end, x_end, tiles_end = WAVE_OWN
    own_ref[planes_end:x_end] = wave_ref[2 * PLANES : 2 * PLANES + BY]
    for place in range((tiles_end - x_end) // 8):
        if halved():
            tile = unpacked(late_ref[place // 2 * 8 : place // 2 * 8 + 8], place)
        else:
            tile = late_ref[place * 8 : place * 8 + 8]
        own_ref[x_end + place * 8 : x_end + place * 8 + 8] = tile
    strip = tile_rows((tiles_end - x_end) // 8)
    own_ref[tiles_end : tiles_end + EY] = late_ref[strip : strip + EY]
    row, lane = rows((BY, BZ)), lanes((BY, BZ))
    fix_lane = late_ref[strip : strip + BY]
    for x in range(BX):
        block = wave_ref[PLANES + x * BY : PLANES + x * BY + BY]
        fix_row = late_ref[strip + EY + x : strip + EY + x + 1]
        block = block - jnp.where(row == 0, fix_row, 0.0)
        block = block - jnp.where(lane == 0, pltpu.roll(fix_lane, BZ - FIX_LANE - x, 1), 0.0)
        s_ref[x * BY : x * BY + BY] = block
    for target, first in zip((even_ref, odd_ref), pair_planes()):
        base = copy_rows(target, 0, wave_ref, 0, PLANES)
        base = copy_rows(target, base, s_ref, first * BY, 3 * BY)
        base = copy_rows(target, base, own_ref, planes_end, BY)
        near = [x_end + (first + plane) * 8 for plane in range(3)]
        nearest = [x_end + 32 + first * 16 + plane * 8 for plane in range(2)]
        base = put_tiles(target, base, own_ref, near + nearest + [tiles_end - 8])
        copy_rows(target, base, own_ref, tiles_end, EY)


def split(values):
    high = values.astype(BF16)
    rest = values - high.astype(F32)
    middle = rest.astype(BF16)
    low = (rest - middle.astype(F32)).astype(BF16)
    return high, middle, low


def places(cells, sl):
    gx, gy, gz = (lax.axis_index(name) for name in ("gx", "gy", "gz"))
    cut = BZ * lax.axis_size("gz") // 2 - MARGIN
    cell_x = cells[0:1, sl] - (gx * BX - MARGIN)
    cell_y = cells[1:2, sl] - gy * BY
    cell_z = cells[2:3, sl]
    in_x = (cell_x >= 0) & (cell_x < EX)
    in_y = (cell_y >= -MARGIN) & (cell_y < BY + MARGIN)
    row = jnp.where(cell_y < 0, cell_y + EY, cell_y)
    flat = jnp.where(in_x & in_y, cell_x * EY + row, -1)
    row = jnp.where(in_y, row, -1)
    zz = cell_z - cut
    in_strip = in_x & (zz >= 0) & (zz < STRIP)
    strip_lane = jnp.where(in_strip, cell_x * STRIP + zz, -1)
    return flat, cell_z - gz * BZ, row, strip_lane


def hits(count, index):
    return rows((count, index.shape[1])) == index


def product(left, right):
    return lax.dot_general(
        left, right, (((1,), (1,)), ((), ())), preferred_element_type=F32
    )


def inject_points(cells, wave_ref, width, waves, planes, out_ref, strip_out_ref):
    count, low, total_rows = len(waves), planes[0] * EY, (planes[1] - planes[0]) * EY
    for start in range(0, cells.shape[1], width):
        sl = slice(start, start + width)
        flat, z, row, strip_lane = places(cells, sl)
        here = hits(total_rows, flat - low).astype(F32).astype(BF16)
        at_strip = hits(BZ, strip_lane).astype(F32).astype(BF16)
        at_z, at_row = hits(BZ, z), hits(EY, row)
        total = strip_total = None
        parts = [split(wave_ref[wave : wave + 1, sl]) for wave in waves]
        for part in range(3):
            amounts = [parts[wave][part].astype(F32) for wave in range(count)]
            right = jnp.concatenate([jnp.where(at_z, a, 0.0) for a in amounts], 0).astype(BF16)
            left = jnp.concatenate([jnp.where(at_row, a, 0.0) for a in amounts], 0).astype(BF16)
            term, strip_term = product(here, right), product(left, at_strip)
            total = term if part == 0 else total + term
            strip_total = strip_term if part == 0 else strip_total + strip_term
        for wave in range(count):
            value = total[:, wave * BZ : wave * BZ + BZ]
            strip_value = strip_total[wave * EY : wave * EY + EY]
            if start > 0:
                value = value + out_ref[wave]
                strip_value = strip_value + strip_out_ref[wave]
            out_ref[wave] = value
            strip_out_ref[wave] = strip_value


LATE_PLANES, EARLY_PLANES, SOURCE_PLANES = (0, EX), (2, EX - 2), (1, EX - 1)


def late_kernel(receivers, receiver_wave, r_ref, rs_ref):
    inject_points(receivers, receiver_wave, 256, (2, 3), LATE_PLANES, r_ref, rs_ref)


def early_kernel(receivers, receiver_wave, _, r_ref, rs_ref):
    inject_points(receivers, receiver_wave, 256, (0, 1), EARLY_PLANES, r_ref, rs_ref)


def source_kernel(sources, source_wave, _, s_ref, ss_ref):
    width = sources.shape[1]
    inject_points(sources, source_wave, width, (0, 1, 2), SOURCE_PLANES, s_ref, ss_ref)


def strip_of(packed, block, slot):
    lane = lanes(packed.shape)
    width = BX * STRIP
    shift = (block * width - slot * width) % BZ
    moved = pltpu.roll(packed, shift, 1) if shift else packed
    return jnp.where((lane >= block * width) & (lane < (block + 1) * width), moved, 0.0)


def y_up(v):
    return pltpu.roll(v, EY - 1, 0)


def y_down(v):
    return pltpu.roll(v, 1, 0)


def z_up(v, edge):
    return jnp.where(lanes(v.shape) == BZ - 1, edge, pltpu.roll(v, BZ - 1, 1))


def z_down(v, edge):
    return jnp.where(lanes(v.shape) == 0, edge, pltpu.roll(v, 1, 1))


def cut_edges(values, flux_z, cut_up, cut_down):
    place = lax.rem(lanes(values.shape), STRIP)
    above = jnp.where(place == MARGIN, values * cut_up, 0.0)
    below = jnp.where(place == MARGIN - 1, flux_z * cut_down, 0.0)
    return pltpu.roll(above, BZ - 2, 1) + below


def plane_edge(edges, x):
    return pltpu.roll(edges, (BZ - (x * STRIP + MARGIN - 1)) % BZ, 1)


def strip_flux(values, buoyancy):
    flux_x = buoyancy * (pltpu.roll(values, BZ - STRIP, 1) - values)
    flux_y = buoyancy * (y_up(values) - values)
    flux_z = buoyancy * (pltpu.roll(values, BZ - 1, 1) - values)
    spread = (flux_x - pltpu.roll(flux_x, STRIP, 1)) + (flux_y - y_down(flux_y))
    return flux_z, spread + (flux_z - pltpu.roll(flux_z, 1, 1))


def cut_flags():
    gz, half = lax.axis_index("gz"), lax.axis_size("gz") // 2
    return jnp.where(gz == half - 1, 1.0, 0.0), jnp.where(gz == half, 1.0, 0.0)


def sides():
    gx = lax.axis_index("gx")
    low = jnp.where(gx > 0, 1.0, 0.0)
    high = jnp.where(gx < lax.axis_size("gx") - 1, 1.0, 0.0)
    return low, high, lax.rem(gx, 2) == 0


def from_side(messages, first, count, block, side):
    even, odd = (message[first : first + count] for message in messages)
    low, high, even_above = side
    if block == 0:
        return jnp.where(even_above, odd, even) * low
    return jnp.where(even_above, even, odd) * high


def side_tile(messages, base, place, block, side):
    if not halved():
        return from_side(messages, base + place * 8, 8, block, side)
    tile = from_side(messages, base + place // 2 * 8, 8, block, side)
    return unpacked(tile, place)


def side_place(wanted, plane, block):
    planes = range(BX - wanted, BX) if block == 0 else range(wanted)
    return planes.index(plane) if plane in planes else None


def widened(own, own_tiles, x, layout, side):
    block, plane = divmod(x, BX)
    if block == 1:
        main = own[0][own[1] + plane * BY : own[1] + plane * BY + BY]
        tile = own_tiles[0][own_tiles[1] + plane * 8 : own_tiles[1] + plane * 8 + 8]
        return jnp.concatenate([main, tile], 0)
    (messages, base, wanted), (tile_messages, tile_base, tile_place, tile_wanted) = layout
    main, tile = jnp.zeros((BY, BZ), F32), jnp.zeros((8, BZ), F32)
    place = side_place(wanted, plane, block)
    if place is not None:
        main = from_side(messages, base + place * BY, BY, block, side)
    place = side_place(tile_wanted, plane, block)
    if place is not None:
        tile = side_tile(tile_messages, tile_base, tile_place + place, block, side)
    return jnp.concatenate([main, tile], 0)


def less_plane_below(value, x, own_ref, own_rows, messages, side_layout, side):
    if x == BX:
        (planes_end, x_end), count = side_layout
        main = from_side(messages, planes_end, BY, 0, side)
        tile = side_tile(messages, x_end, count - 1, 0, side)
    elif x == 2 * BX:
        planes_end, _, tiles_end = own_rows
        high = side[1]
        main = own_ref[planes_end : planes_end + BY] * high
        tile = own_ref[tiles_end - 8 : tiles_end] * high
    else:
        return value
    return value - jnp.concatenate([main, tile], 0)


def strip_below(own, messages, first, slot, side):
    lane = lanes(own.shape)
    width = BX * STRIP
    low = from_side(messages, first, EY, 0, side)
    low = pltpu.roll(low, (width - slot * width) % BZ, 1)
    own = pltpu.roll(own * side[1], (2 * width - slot * width) % BZ, 1)
    in_own = (lane >= width) & (lane < width + STRIP)
    in_high = (lane >= 2 * width) & (lane < 2 * width + STRIP)
    return jnp.where(in_own, low, jnp.where(in_high, own, 0.0))


def whole_strip(own, messages, first, slot, side):
    low = from_side(messages, first, EY, 0, side)
    high = from_side(messages, first, EY, 2, side)
    return strip_of(low, 0, slot) + strip_of(own, 1, slot) + strip_of(high, 2, slot)


def adjoint_kernel(
    ql_ref, late_ref, even, odd, adj_hbm, ra_ref, rsa_ref, rb_ref, rsb_ref,
    table_ref,
    out_ref, hist_ref, coef_ref, coef_strip_ref,
    q_ref, t_ref, u_ref, scale_ref, edge_ref, flux_ref, w_sem,
):
    w_copy = pltpu.make_async_copy(adj_hbm.at[pl.ds(1, 3)], out_ref.at[pl.ds(1, 3)], w_sem)
    w_copy.start()
    cut_up, cut_down = cut_flags()
    side = sides()
    messages = (even, odd)
    r_refs = ((ra_ref, 0), (ra_ref, 1), (rb_ref, 0), (rb_ref, 1))
    rs_refs = ((rsa_ref, 0), (rsa_ref, 1), (rsb_ref, 0), (rsb_ref, 1))
    tiles, own_tiles = ADJ_SIDE[1], ADJ_OWN[1]
    side_strip = tiles + tile_rows(ADJ_TILES)
    raws = side_strip + EY

    def initial(index, x):
        own = ((ql_ref, 0), (late_ref, 0), (ql_ref, PLANES))[index]
        layout = (
            ((messages, raws, 4), (messages, tiles, 0, 3)),
            ((messages, 0, 3), (messages, tiles, 3, 2)),
            ((messages, raws + PLANES, 4), (messages, tiles, 5, 3)),
        )[index]
        value = widened(own, (late_ref, own_tiles + 32 * index), x, layout, side)
        if index == 1:
            value = less_plane_below(
                value, x, late_ref, ADJ_OWN, messages, (ADJ_SIDE, ADJ_TILES), side
            )
        return value

    for x in range(EX):
        stiff, buoy, damp = coefficients(initial(2, x), table_ref)
        coef_ref[0, x], coef_ref[1, x], coef_ref[2, x] = stiff, buoy, damp
        scale_ref[x] = stiff * damp
    own_strip = late_ref[ADJ_OWN[2] : ADJ_OWN[2] + EY]
    q_s, t_s, label_s = (
        whole_strip(own_strip, messages, side_strip, slot, side) for slot in range(3)
    )
    t_s = t_s - strip_below(own_strip, messages, side_strip, 3, side)
    stiff_s, buoy_s, damp_s = coefficients(label_s, table_ref)
    scale_s = stiff_s * damp_s
    coef_strip_ref[0], coef_strip_ref[1], coef_strip_ref[2] = stiff_s, buoy_s, damp_s
    w_copy.wait()

    for step in range(1, STEPS + 1):
        rs_ref, place = rs_refs[STEPS - step]
        q_s = q_s + rs_ref[place]
        u_s = scale_s * q_s
        flux_s, spread = strip_flux(u_s, buoy_s)
        t_s = t_s + spread
        q_s = damp_s * q_s + t_s
        edges = cut_edges(u_s, flux_s, cut_up, cut_down)
        for x in range(step, EX - step):
            edge_ref[step - 1, x] = plane_edge(edges, x)

    for step in range(1, STEPS + 1):
        k = STEPS - step
        r_ref, place = r_refs[k]
        r_first = (EARLY_PLANES if k < 2 else LATE_PLANES)[0]

        for x in range(step - 1, EX - step + 1):
            q = (initial(0, x) if step == 1 else q_ref[x]) + r_ref[place, x - r_first]
            q_ref[x] = q
            u_ref[x] = scale_ref[x] * q

        for x in range(step - 1, EX - step):
            u, buoyancy = u_ref[x], coef_ref[1, x]
            slopes = [u_ref[x + 1] - u]
            if x >= step:
                slopes += [y_up(u) - u, z_up(u, edge_ref[step - 1, x]) - u]
            for axis, slope in enumerate(slopes):
                flux_ref[axis, x] = buoyancy * slope
            if BX <= x < 2 * BX:
                for axis, slope in enumerate(slopes):
                    w = out_ref[1 + axis, x - BX] + slope[0:BY]
                    out_ref[1 + axis, x - BX] = w
                    hist_ref[k, 1 + axis, x - BX] = w

        for x in range(step, EX - step):
            flux_y, flux_z = flux_ref[1, x], flux_ref[2, x]
            spread = (flux_ref[0, x] - flux_ref[0, x - 1]) + (flux_y - y_down(flux_y))
            spread = spread + (flux_z - z_down(flux_z, edge_ref[step - 1, x]))
            damped = coef_ref[2, x] * q_ref[x]
            t = (initial(1, x) if step == 1 else t_ref[x]) + spread
            if BX <= x < 2 * BX:
                hist_ref[k, 0, x - BX] = damped[0:BY]
            if step < STEPS:
                t_ref[x] = t
                q_ref[x] = damped + t
            else:
                out_ref[0, x - BX] = (damped + t)[0:BY]


def forward_kernel(
    wave_ref, own_s_ref, late_ref, odd, even, coef_ref, coef_strip_ref, s_ref, ss_ref, hist_ref,
    adjoint_ref, grad_hbm, adjoint_hbm,
    p_ref, spread_ref, edge_ref, flux_ref, grad_ref, sems,
):
    copies = [pltpu.make_async_copy(adjoint_ref, adjoint_hbm, sems.at[0])]
    copies[0].start()

    def send(index, kind, first, count):
        planes = pl.ds(first, count)
        copy = pltpu.make_async_copy(
            grad_ref.at[kind, planes], grad_hbm.at[kind, planes], sems.at[index]
        )
        copy.start()
        copies.append(copy)

    cut_up, cut_down = cut_flags()
    side = sides()
    messages = (even, odd)
    tiles, own_tiles = WAVE_SIDE[1], WAVE_OWN[1]
    side_strip = tiles + tile_rows(WAVE_TILES)

    def initial(index, x):
        layout = (
            ((messages, 0, 4), (messages, tiles, 0, 3)),
            ((messages, PLANES, 3), (messages, tiles, 3, 2)),
        )[index]
        own = ((wave_ref, 0), (own_s_ref, 0))[index]
        value = widened(own, (late_ref, own_tiles + 32 * index), x, layout, side)
        if index == 1:
            value = less_plane_below(
                value, x, late_ref, WAVE_OWN, messages, (WAVE_SIDE, WAVE_TILES), side
            )
        return value

    own_strip = late_ref[WAVE_OWN[2] : WAVE_OWN[2] + EY]
    p_s, s_s = (
        whole_strip(own_strip, messages, side_strip, slot, side) for slot in range(2)
    )
    s_s = s_s - strip_below(own_strip, messages, side_strip, 2, side)
    stiff_s, buoy_s, damp_s = coef_strip_ref[0], coef_strip_ref[1], coef_strip_ref[2]

    for step in range(1, STEPS + 1):
        flux_s, spread = strip_flux(p_s, buoy_s)
        edges = cut_edges(p_s, flux_s, cut_up, cut_down)
        if step < STEPS:
            s_s = s_s - spread
            p_s = damp_s * (p_s - stiff_s * s_s) + ss_ref[step - 1]
        for x in range(step, EX - step):
            edge_ref[step - 1, x] = plane_edge(edges, x)
    for x in range(EX):
        p_ref[x] = initial(0, x)

    for step in range(1, STEPS + 1):
        k = step - 1
        for x in range(step - 1, EX - step):
            p, buoyancy = p_ref[x], coef_ref[1, x]
            slopes = [p_ref[x + 1] - p]
            if x >= step:
                slopes += [y_up(p) - p, z_up(p, edge_ref[step - 1, x]) - p]
            for axis, slope in enumerate(slopes):
                flux_ref[axis, x] = buoyancy * slope
            if BX <= x < 2 * BX:
                place = x - BX
                term = hist_ref[k, 1, place] * slopes[0][0:BY]
                term = term + hist_ref[k, 2, place] * slopes[1][0:BY]
                term = term + hist_ref[k, 3, place] * slopes[2][0:BY]
                grad_ref[1, place] = -term if k == 0 else grad_ref[1, place] - term
        if step == STEPS:
            send(1, 1, 0, BX)

        for x in range(step, EX - step):
            flux_y, flux_z = flux_ref[1, x], flux_ref[2, x]
            spread = (flux_ref[0, x] - flux_ref[0, x - 1]) + (flux_y - y_down(flux_y))
            spread = spread + (flux_z - z_down(flux_z, edge_ref[step - 1, x]))
            spread = (initial(1, x) if step == 1 else spread_ref[x]) - spread
            if step < STEPS:
                spread_ref[x] = spread
                p_ref[x] = (
                    coef_ref[2, x] * (p_ref[x] - coef_ref[0, x] * spread)
                    + s_ref[k, x - SOURCE_PLANES[0]]
                )
            if BX <= x < 2 * BX:
                place = x - BX
                term = hist_ref[k, 0, place] * spread[0:BY]
                grad_ref[0, place] = -term if k == 0 else grad_ref[0, place] - term
                if step == STEPS:
                    send(2 + place, 0, place, 1)
    for copy in copies:
        copy.wait()


def shape(*dims):
    return jax.ShapeDtypeStruct(dims, F32)


def call(kernel, outs, operands, scratch, places, micros=0.1, out_place="v"):
    spaces = {"h": pltpu.HBM, "a": pl.ANY, "v": pltpu.VMEM}
    operands = [
        pltpu.with_memory_space_constraint(operand, pltpu.HBM) if place == "h" else operand
        for operand, place in zip(operands, places)
    ]
    return pl.pallas_call(
        kernel,
        out_shape=outs,
        in_specs=[pl.BlockSpec(memory_space=spaces[place]) for place in places],
        out_specs=[pl.BlockSpec(memory_space=spaces[out_place])] * len(outs),
        scratch_shapes=scratch,
        compiler_params=pltpu.CompilerParams(vmem_limit_bytes=VMEM_LIMIT),
        cost_estimate=pl.CostEstimate(
            flops=0, bytes_accessed=int(3.69e6 * micros), transcendentals=0
        ),
    )(*operands)


def from_sides(sends, axes):
    count = lax.axis_size("gy")

    def route(offset):
        pairs = []
        for target in range(count):
            source = target + offset
            if 0 <= source < count:
                if "gz" in axes:
                    pairs += [(2 * source + z, 2 * target + 1 - z) for z in range(2)]
                else:
                    pairs.append((source, target))
        return pairs

    if count == 2:
        both = lax.ppermute(sends[0], axes, route(1) + route(-1))
        return both, both
    upward, downward = sends
    return lax.ppermute(downward, axes, route(1)), lax.ppermute(upward, axes, route(-1))


def rotated(array, axis, offset):
    count = lax.axis_size(axis)
    return lax.ppermute(array, axis, [((i + offset) % count, i) for i in range(count)])


def paired(array, odd):
    count = lax.axis_size("gx")
    pairs = []
    for i in range(count):
        partner = ((i - 1) ^ 1) + 1 if odd else i ^ 1
        pairs.append((partner if 0 <= partner < count else i, i))
    return lax.ppermute(array, "gx", pairs)


def local(
    stored, adjoint_end, labels, tissue, source_cells, source_wave, receiver_cells, receiver_wave
):
    assert lax.axis_size("gz") == 2 and labels.shape == (BX, BY, BZ) and tissue.shape[1] == 8
    half = lax.axis_size("gx") // 2
    arguments = [
        stored, adjoint_end, labels, tissue,
        receiver_cells.T, receiver_wave, source_cells.T, source_wave,
    ]
    ways = 1 if lax.axis_size("gy") == 2 else 2
    wave, ql, t, last_x, last_y, strips, table, receivers, receiver_wave, sources, source_wave, *sends = call(
        load_kernel,
        [
            shape(2 * PLANES + BY + SPARE // 2, BZ),
            shape(2 * PLANES, BZ),
            shape(PLANES, BZ),
            shape(BY, BZ),
            shape(2 * BX * 8, BZ),
            shape(3 * BY, BZ),
            shape(24, BZ),
        ]
        + [jax.ShapeDtypeStruct(array.shape, array.dtype) for array in arguments[4:]]
        + [shape(20 * 8, BZ)] * ways
        + [shape(2 * 8, BZ)] * ways,
        arguments,
        [
            pltpu.VMEM(stored.shape, F32),
            pltpu.VMEM(adjoint_end.shape, F32),
            pltpu.VMEM(labels.shape, jnp.int32),
            pltpu.SMEM(tissue.shape, F32),
            pltpu.SemaphoreType.DMA,
        ],
        "hhhhhhhh",
        1.4,
    )
    from_up, from_down = from_sides(sends[:ways], "gy")
    other = rotated(strips, "gz", 1)
    corner_up, corner_down = from_sides(sends[ways:], ("gy", "gz"))
    wave = rotated(wave, "gx", half)
    rb, rsb = call(
        late_kernel,
        [shape(2, EX * EY, BZ), shape(2, EY, BZ)],
        [receivers, receiver_wave],
        [],
        "vv",
        1.2,
    )
    early_planes, source_planes = (last - first for first, last in (EARLY_PLANES, SOURCE_PLANES))
    late, adj_late = call(
        merge_kernel,
        [shape(tile_rows(9) + EY + 8 + SPARE, BZ), shape(ADJ_OWN[2] + EY, BZ)],
        [from_up, from_down, corner_up, corner_down, strips, other, t, last_x, last_y, rsb],
        [pltpu.VMEM((WAVE_OWN[2], BZ), F32)],
        "vvvvvvvvva",
    )
    late = rotated(late, "gx", half)
    ra, rsa = call(
        early_kernel,
        [shape(2, early_planes * EY, BZ), shape(2, EY, BZ)],
        [receivers, receiver_wave, adj_late],
        [],
        "vva",
        1.0,
    )
    ra, rb = ra.reshape(2, early_planes, EY, BZ), rb.reshape(2, EX, EY, BZ)
    even, odd = call(
        adjoint_join_kernel,
        [shape(ADJ_SIDE[1] + tile_rows(ADJ_TILES) + EY + 2 * PLANES, BZ)] * 2,
        [ql, adj_late],
        [],
        "vv",
    )
    even, odd = paired(even, False), paired(odd, True)
    src, src_strip = call(
        source_kernel,
        [shape(STEPS - 1, source_planes * EY, BZ), shape(STEPS - 1, EY, BZ)],
        [sources, source_wave, adj_late],
        [],
        "vva",
        0.5,
    )
    src = src.reshape(STEPS - 1, source_planes, EY, BZ)
    own_s, own_late, wave_even, wave_odd = call(
        join_kernel,
        [shape(PLANES, BZ), shape(WAVE_OWN[2] + EY, BZ)]
        + [shape(WAVE_SIDE[1] + tile_rows(WAVE_TILES) + EY, BZ)] * 2,
        [wave, late],
        [],
        "vv",
    )
    wave_even, wave_odd = paired(wave_even, False), paired(wave_odd, True)
    adjoint_out, hist, coef, coef_strip = call(
        adjoint_kernel,
        [
            shape(4, BX, BY, BZ),
            shape(STEPS, 4, BX, BY, BZ),
            shape(3, EX, EY, BZ),
            shape(3, EY, BZ),
        ],
        [ql, adj_late, even, odd, adjoint_end, ra, rsa, rb, rsb, table],
        [pltpu.VMEM((EX, EY, BZ), F32)] * 4
        + [
            pltpu.VMEM((STEPS, EX, EY, BZ), F32),
            pltpu.VMEM((3, EX, EY, BZ), F32),
            pltpu.SemaphoreType.DMA,
        ],
        "vvvvhvvvvv",
        3.9,
    )
    return call(
        forward_kernel,
        [shape(2, BX, BY, BZ), shape(4, BX, BY, BZ)],
        [
            wave, own_s, own_late, wave_odd, wave_even, coef, coef_strip, src, src_strip, hist,
            adjoint_out,
        ],
        [pltpu.VMEM((EX, EY, BZ), F32)] * 2
        + [
            pltpu.VMEM((STEPS, EX, EY, BZ), F32),
            pltpu.VMEM((3, EX, EY, BZ), F32),
            pltpu.VMEM((2, BX, BY, BZ), F32),
            pltpu.SemaphoreType.DMA((2 + BX,)),
        ],
        "vvvvvvvvvvv",
        2.5,
        "a",
    )


def solution(mesh):
    return jax.shard_map(
        local,
        mesh=mesh,
        in_specs=(
            P("shot", "gx", "gy", "gz"),
            P("shot", "gx", "gy", "gz"),
            P("gx", "gy", "gz"),
            P(),
            P("shot", None),
            P(None, "shot"),
            P(),
            P(None, "shot"),
        ),
        out_specs=(P("shot", "gx", "gy", "gz"), P("shot", "gx", "gy", "gz")),
        check_vma=False,
    )
```

```python
import jax
import jax.numpy as jnp
from jax import lax
from jax.experimental import pallas as pl
from jax.experimental.pallas import tpu as pltpu
from jax.sharding import PartitionSpec as P

STEPS = 4
MARGIN = 4
BX, BY, BZ = 4, 32, 128
EX, EY = BX + 2 * MARGIN, BY + 2 * MARGIN
STRIP = 2 * MARGIN
F32 = jnp.float32
BF16 = jnp.bfloat16
VMEM_LIMIT = 16 * 1024 * 1024
PLANES = BX * BY
WAVE_OWN = (0, BY, BY + 9 * 8)
FIX_LANE = 3 * BX * STRIP
SPARE = 64
ADJ_OWN = (PLANES, PLANES + BY, PLANES + BY + 13 * 8)
WAVE_SIDE = (PLANES + 3 * BY, PLANES + 4 * BY)
ADJ_SIDE = (3 * BY, 4 * BY)
WAVE_TILES, ADJ_TILES = 6, 9


def lanes(shape):
    return lax.broadcasted_iota(jnp.int32, shape, len(shape) - 1)


def rows(shape):
    return lax.broadcasted_iota(jnp.int32, shape, len(shape) - 2)


def run(copies):
    for copy in copies:
        copy.start()
    for copy in copies:
        copy.wait()


def coefficients(labels, table_ref):
    result = [jnp.zeros(labels.shape, F32) for _ in range(3)]
    for index in range(8):
        picked = labels == float(index + 1)
        for kind in range(3):
            row = kind * 8 + index
            result[kind] = jnp.where(picked, table_ref[row : row + 1], result[kind])
    return result


def buoyancy_of(labels, table_ref):
    result = jnp.zeros(labels.shape, F32)
    for index in range(8):
        result = jnp.where(labels == float(index + 1), table_ref[8 + index : 9 + index], result)
    return result


def half_turn(tile):
    return pltpu.roll(tile, MARGIN, 0)


def load_kernel(
    stored_hbm, adj_hbm, lab_hbm, tissue_hbm, rc_hbm, rw_hbm, sc_hbm, sw_hbm,
    wave_ref, ql_ref, t_ref, last_x_ref, last_y_ref, strip_ref, table_ref,
    rc_ref, rw_ref, sc_ref, sw_ref, *rest,
):
    *sends, stored, adj, lab, tissue, sem = rest
    run([
        pltpu.make_async_copy(source, target, sem)
        for source, target in (
            (stored_hbm, stored), (adj_hbm, adj), (lab_hbm, lab), (tissue_hbm, tissue),
            (rc_hbm, rc_ref), (rw_hbm, rw_ref), (sc_hbm, sc_ref), (sw_hbm, sw_ref),
        )
    ])
    for index in range(tissue.shape[1]):
        speed = jnp.full((1, BZ), tissue[0, index], F32)
        density = jnp.full((1, BZ), tissue[1, index], F32)
        table_ref[index : index + 1] = density * speed
        table_ref[8 + index : 9 + index] = speed / density
        table_ref[16 + index : 17 + index] = 1.0 - jnp.full((1, BZ), tissue[2, index], F32)
    gy, gz = lax.axis_index("gy"), lax.axis_index("gz")
    lane = lanes((BY, BZ))
    row = rows((BY, BZ))
    tile_row = rows((8, BZ))
    strips = [jnp.zeros((BY, BZ), F32) for _ in range(3)]
    tiles = [None] * 39
    previous = [None, None]

    def edge_tile(block):
        return jnp.where(tile_row < MARGIN, block[0:8], block[BY - 8 : BY])

    for x in range(BX):
        labels = lab[x].astype(F32) + 1.0
        buoyancy = buoyancy_of(labels, table_ref)
        plane = slice(x * BY, x * BY + BY)
        fields = [stored[index, x] for index in range(4)] + [adj[0, x]]
        fields += [buoyancy * adj[index, x] for index in range(1, 4)] + [labels]
        wave_ref[plane] = fields[0]
        ql_ref[plane] = fields[4]
        ql_ref[PLANES + x * BY : PLANES + x * BY + BY] = labels
        for index, block in enumerate(fields):
            tiles[index * BX + x] = edge_tile(block)
            group, slot = divmod(index, 4)
            base = slot * BX * STRIP + x * STRIP
            rolled = pltpu.roll(block, base + MARGIN, 1)
            first = base + MARGIN * gz
            strips[group] = jnp.where(
                (lane >= first) & (lane < first + MARGIN), rolled, strips[group]
            )
        for kind, (target, base) in enumerate(((wave_ref, PLANES), (t_ref, 0))):
            vx, vy, vz = fields[4 * kind + 1 : 4 * kind + 4]
            spread = vx if x == 0 else vx - previous[kind]
            spread = spread + (vy - jnp.where(row == 0, 0.0, pltpu.roll(vy, 1, 0)))
            spread = spread + (vz - jnp.where(lane == 0, 0.0, pltpu.roll(vz, 1, 1)))
            target[base + x * BY : base + x * BY + BY] = spread
            previous[kind] = vx
            index = (kind * BX + x) * 8
            last_y_ref[index : index + 8] = vy[BY - 8 : BY]
    wave_ref[2 * PLANES : 2 * PLANES + BY] = previous[0]
    wave_ref[2 * PLANES + BY :] = jnp.zeros((SPARE // 2, BZ), F32)
    last_x_ref[...] = previous[1]
    for group in range(3):
        strip_ref[group * BY : group * BY + BY] = strips[group]
        tiles[9 * BX + group] = edge_tile(strips[group])

    def joined(first, second):
        second = first if second is None else second
        upward = jnp.where(tile_row < MARGIN, half_turn(first), second)
        downward = jnp.where(tile_row < MARGIN, first, half_turn(second))
        if len(sends) == 2:
            return (jnp.where(gy == 0, upward, downward),)
        return upward, downward

    tiles.append(None)
    half = len(sends) // 2
    for place in range(20):
        for target, tile in zip(sends[:half], joined(tiles[2 * place], tiles[2 * place + 1])):
            target[place * 8 : place * 8 + 8] = tile
    for place in range(2):
        first = tiles[9 * BX + 2 * place]
        for target, tile in zip(sends[half:], joined(first, tiles[9 * BX + 2 * place + 1])):
            target[place * 8 : place * 8 + 8] = tile


def copy_rows(target, base, source, first, count):
    target[base : base + count] = source[pl.ds(pl.multiple_of(first, 8), count)]
    return base + count


def halved():
    return lax.axis_size("gy") == 2


def tile_rows(count):
    return (count + 1) // 2 * 8 if halved() else count * 8


def put_tiles(target, base, source, firsts):
    tiles = [source[pl.ds(pl.multiple_of(first, 8), 8)] for first in firsts]
    if halved():
        upper = lax.axis_index("gy") == 0
        row = rows((8, BZ))
        pairs = [(tiles[i], tiles[min(i + 1, len(tiles) - 1)]) for i in range(0, len(tiles), 2)]
        tiles = [
            jnp.where(
                row < MARGIN,
                jnp.where(upper, first, half_turn(first)),
                jnp.where(upper, half_turn(second), second),
            )
            for first, second in pairs
        ]
    for place, tile in enumerate(tiles):
        target[base + place * 8 : base + place * 8 + 8] = tile
    return base + 8 * len(tiles)


def pair_planes():
    parity = lax.rem(lax.axis_index("gx"), 2)
    return 1 - parity, parity


def merge_kernel(
    from_up, from_down, corner_up, corner_down, strip_ref, other_ref,
    t_ref, last_x_ref, last_y_ref, _,
    late_ref, adj_ref,
    wave_ref,
):
    gy = lax.axis_index("gy")
    tile_row = rows((8, BZ))
    row, lane = rows((BY, BZ)), lanes((BY, BZ))
    take_up = (tile_row < MARGIN) & (gy < lax.axis_size("gy") - 1)
    take_down = (tile_row >= MARGIN) & (gy > 0)
    _, cut_down = cut_flags()

    def halo(up, down, index):
        place, second = divmod(index, 2)
        sl = slice(place * 8, place * 8 + 8)
        above = half_turn(up[sl]) if second else up[sl]
        below = down[sl] if second else half_turn(down[sl])
        return jnp.where(take_up, above, jnp.where(take_down, below, 0.0))

    wide = []
    for group in range(3):
        sl = slice(group * BY, group * BY + BY)
        tile = halo(from_up, from_down, 9 * BX + group) + halo(corner_up, corner_down, group)
        wide.append(jnp.concatenate([strip_ref[sl] + other_ref[sl], tile], 0))
    strip_lane = lanes((EY, BZ))

    def strip_field(index):
        group, slot = divmod(index, 4)
        moved = pltpu.roll(wide[group], (BZ - slot * BX * STRIP) % BZ, 1) if slot else wide[group]
        return jnp.where(strip_lane < BX * STRIP, moved, 0.0)

    last_lanes = (BX - 1) * STRIP
    fix_row = jnp.zeros((8, BZ), F32)
    fix_lane = jnp.zeros((BY, BZ), F32)
    for kind, target in enumerate((wave_ref, adj_ref)):
        first = 4 * kind
        planes_end, x_end, tiles_end = (WAVE_OWN, ADJ_OWN)[kind]
        vx, vy, vz = (strip_field(first + 1 + axis) for axis in range(3))
        spread = vx - jnp.where(strip_lane < STRIP, 0.0, pltpu.roll(vx, STRIP, 1))
        spread = (spread + (vy - y_down(vy))) + (vz - pltpu.roll(vz, 1, 1))
        strip = strip_field(first)
        strip = strip + pltpu.roll(jnp.where(strip_lane < BX * STRIP, spread, 0.0), BX * STRIP, 1)
        last_slot = 2
        if kind == 1:
            strip = strip + pltpu.roll(strip_field(8), 2 * BX * STRIP, 1)
            last_slot = 3
        last = jnp.where(strip_lane >= last_lanes, vx, 0.0)
        strip = strip + pltpu.roll(last, last_slot * BX * STRIP - last_lanes, 1)

        vx_before = None
        for x in range(BX):
            vx_t, vy_t, vz_t = (
                halo(from_up, from_down, (first + 1 + axis) * BX + x) for axis in range(3)
            )
            below_z = pltpu.roll(vz, (BZ - (x * STRIP + MARGIN - 1)) % BZ, 1) * cut_down
            last_y = last_y_ref[(kind * BX + x) * 8 : (kind * BX + x) * 8 + 8]
            y_before = jnp.where(
                tile_row == 0, pltpu.roll(last_y, 1, 0), pltpu.roll(vy_t, 1, 0)
            )
            z_before = jnp.where(lane[0:8] == 0, below_z[BY:EY], pltpu.roll(vz_t, 1, 1))
            spread = vx_t if x == 0 else vx_t - vx_before
            spread = (spread + (vy_t - y_before)) + (vz_t - z_before)
            vx_before = vx_t
            if kind == 0:
                fix_row = jnp.where(tile_row == x, vy_t[7:8], fix_row)
                moved = pltpu.roll(below_z[0:BY], FIX_LANE + x, 1)
                fix_lane = jnp.where(lane == FIX_LANE + x, moved, fix_lane)
            else:
                block = t_ref[x * BY : x * BY + BY]
                block = block - jnp.where(row == 0, vy_t[7:8], 0.0)
                block = block - jnp.where(lane == 0, below_z[0:BY], 0.0)
                target[x * BY : x * BY + BY] = block
            base = x_end + x * 8
            target[base : base + 8] = halo(from_up, from_down, first * BX + x)
            target[base + 32 : base + 40] = spread
            if kind == 1:
                target[base + 64 : base + 72] = halo(from_up, from_down, 8 * BX + x)
        target[tiles_end - 8 : tiles_end] = vx_before
        if kind == 0:
            base = put_tiles(late_ref, 0, wave_ref, range(x_end, tiles_end, 8))
            late_ref[base : base + BY] = strip[0:BY] + fix_lane
            late_ref[base + BY : base + EY] = strip[BY:EY]
            late_ref[base + EY : base + EY + 8] = fix_row
            late_ref[base + EY + 8 : base + EY + 8 + SPARE] = jnp.zeros((SPARE, BZ), F32)
        else:
            target[planes_end:x_end] = last_x_ref[...]
            target[tiles_end : tiles_end + EY] = strip


def adjoint_join_kernel(ql_ref, adj_ref, even_ref, odd_ref):
    planes_end, x_end, tiles_end = ADJ_OWN
    for target, first in zip((even_ref, odd_ref), pair_planes()):
        base = copy_rows(target, 0, adj_ref, first * BY, 3 * BY)
        base = copy_rows(target, base, adj_ref, planes_end, BY)
        near = [x_end + (first + plane) * 8 for plane in range(3)]
        nearest = [x_end + 32 + first * 16 + plane * 8 for plane in range(2)]
        firsts = near + nearest + [start + 64 for start in near] + [tiles_end - 8]
        base = put_tiles(target, base, adj_ref, firsts)
        base = copy_rows(target, base, adj_ref, tiles_end, EY)
        copy_rows(target, base, ql_ref, 0, 2 * PLANES)


def unpacked(tile, place):
    upper = lax.axis_index("gy") == 0
    turned = half_turn(tile)
    tile = jnp.where(upper, turned, tile) if place % 2 else jnp.where(upper, tile, turned)
    return jnp.where((rows((8, BZ)) < MARGIN) == upper, tile, 0.0)


def join_kernel(wave_ref, late_ref, _, s_ref, own_ref, even_ref, odd_ref):
    planes_end, x_end, tiles_end = WAVE_OWN
    own_ref[planes_end:x_end] = wave_ref[2 * PLANES : 2 * PLANES + BY]
    for place in range((tiles_end - x_end) // 8):
        if halved():
            tile = unpacked(late_ref[place // 2 * 8 : place // 2 * 8 + 8], place)
        else:
            tile = late_ref[place * 8 : place * 8 + 8]
        own_ref[x_end + place * 8 : x_end + place * 8 + 8] = tile
    strip = tile_rows((tiles_end - x_end) // 8)
    own_ref[tiles_end : tiles_end + EY] = late_ref[strip : strip + EY]
    row, lane = rows((BY, BZ)), lanes((BY, BZ))
    fix_lane = late_ref[strip : strip + BY]
    for x in range(BX):
        block = wave_ref[PLANES + x * BY : PLANES + x * BY + BY]
        fix_row = late_ref[strip + EY + x : strip + EY + x + 1]
        block = block - jnp.where(row == 0, fix_row, 0.0)
        block = block - jnp.where(lane == 0, pltpu.roll(fix_lane, BZ - FIX_LANE - x, 1), 0.0)
        s_ref[x * BY : x * BY + BY] = block
    for target, first in zip((even_ref, odd_ref), pair_planes()):
        base = copy_rows(target, 0, wave_ref, 0, PLANES)
        base = copy_rows(target, base, s_ref, first * BY, 3 * BY)
        base = copy_rows(target, base, own_ref, planes_end, BY)
        near = [x_end + (first + plane) * 8 for plane in range(3)]
        nearest = [x_end + 32 + first * 16 + plane * 8 for plane in range(2)]
        base = put_tiles(target, base, own_ref, near + nearest + [tiles_end - 8])
        copy_rows(target, base, own_ref, tiles_end, EY)


def split(values):
    high = values.astype(BF16)
    rest = values - high.astype(F32)
    middle = rest.astype(BF16)
    low = (rest - middle.astype(F32)).astype(BF16)
    return high, middle, low


def places(cells, sl):
    gx, gy, gz = (lax.axis_index(name) for name in ("gx", "gy", "gz"))
    cut = BZ * lax.axis_size("gz") // 2 - MARGIN
    cell_x = cells[0:1, sl] - (gx * BX - MARGIN)
    cell_y = cells[1:2, sl] - gy * BY
    cell_z = cells[2:3, sl]
    in_x = (cell_x >= 0) & (cell_x < EX)
    in_y = (cell_y >= -MARGIN) & (cell_y < BY + MARGIN)
    row = jnp.where(cell_y < 0, cell_y + EY, cell_y)
    flat = jnp.where(in_x & in_y, cell_x * EY + row, -1)
    row = jnp.where(in_y, row, -1)
    zz = cell_z - cut
    in_strip = in_x & (zz >= 0) & (zz < STRIP)
    strip_lane = jnp.where(in_strip, cell_x * STRIP + zz, -1)
    return flat, cell_z - gz * BZ, row, strip_lane


def hits(count, index):
    return rows((count, index.shape[1])) == index


def product(left, right):
    return lax.dot_general(
        left, right, (((1,), (1,)), ((), ())), preferred_element_type=F32
    )


def inject_points(cells, wave_ref, width, waves, planes, out_ref, strip_out_ref):
    count, low, total_rows = len(waves), planes[0] * EY, (planes[1] - planes[0]) * EY
    for start in range(0, cells.shape[1], width):
        sl = slice(start, start + width)
        flat, z, row, strip_lane = places(cells, sl)
        here = hits(total_rows, flat - low).astype(F32).astype(BF16)
        at_strip = hits(BZ, strip_lane).astype(F32).astype(BF16)
        at_z, at_row = hits(BZ, z), hits(EY, row)
        total = strip_total = None
        parts = [split(wave_ref[wave : wave + 1, sl]) for wave in waves]
        for part in range(3):
            amounts = [parts[wave][part].astype(F32) for wave in range(count)]
            right = jnp.concatenate([jnp.where(at_z, a, 0.0) for a in amounts], 0).astype(BF16)
            left = jnp.concatenate([jnp.where(at_row, a, 0.0) for a in amounts], 0).astype(BF16)
            term, strip_term = product(here, right), product(left, at_strip)
            total = term if part == 0 else total + term
            strip_total = strip_term if part == 0 else strip_total + strip_term
        for wave in range(count):
            value = total[:, wave * BZ : wave * BZ + BZ]
            strip_value = strip_total[wave * EY : wave * EY + EY]
            if start > 0:
                value = value + out_ref[wave]
                strip_value = strip_value + strip_out_ref[wave]
            out_ref[wave] = value
            strip_out_ref[wave] = strip_value


LATE_PLANES, EARLY_PLANES, SOURCE_PLANES = (0, EX), (2, EX - 2), (1, EX - 1)


def late_kernel(receivers, receiver_wave, r_ref, rs_ref):
    inject_points(receivers, receiver_wave, 256, (2, 3), LATE_PLANES, r_ref, rs_ref)


def early_kernel(receivers, receiver_wave, _, r_ref, rs_ref):
    inject_points(receivers, receiver_wave, 256, (0, 1), EARLY_PLANES, r_ref, rs_ref)


def source_kernel(sources, source_wave, _, s_ref, ss_ref):
    width = sources.shape[1]
    inject_points(sources, source_wave, width, (0, 1, 2), SOURCE_PLANES, s_ref, ss_ref)


def strip_of(packed, block, slot):
    lane = lanes(packed.shape)
    width = BX * STRIP
    shift = (block * width - slot * width) % BZ
    moved = pltpu.roll(packed, shift, 1) if shift else packed
    return jnp.where((lane >= block * width) & (lane < (block + 1) * width), moved, 0.0)


def y_up(v):
    return pltpu.roll(v, EY - 1, 0)


def y_down(v):
    return pltpu.roll(v, 1, 0)


def z_up(v, edge):
    return jnp.where(lanes(v.shape) == BZ - 1, edge, pltpu.roll(v, BZ - 1, 1))


def z_down(v, edge):
    return jnp.where(lanes(v.shape) == 0, edge, pltpu.roll(v, 1, 1))


def cut_edges(values, flux_z, cut_up, cut_down):
    place = lax.rem(lanes(values.shape), STRIP)
    above = jnp.where(place == MARGIN, values * cut_up, 0.0)
    below = jnp.where(place == MARGIN - 1, flux_z * cut_down, 0.0)
    return pltpu.roll(above, BZ - 2, 1) + below


def plane_edge(edges, x):
    return pltpu.roll(edges, (BZ - (x * STRIP + MARGIN - 1)) % BZ, 1)


def strip_flux(values, buoyancy):
    flux_x = buoyancy * (pltpu.roll(values, BZ - STRIP, 1) - values)
    flux_y = buoyancy * (y_up(values) - values)
    flux_z = buoyancy * (pltpu.roll(values, BZ - 1, 1) - values)
    spread = (flux_x - pltpu.roll(flux_x, STRIP, 1)) + (flux_y - y_down(flux_y))
    return flux_z, spread + (flux_z - pltpu.roll(flux_z, 1, 1))


def cut_flags():
    gz, half = lax.axis_index("gz"), lax.axis_size("gz") // 2
    return jnp.where(gz == half - 1, 1.0, 0.0), jnp.where(gz == half, 1.0, 0.0)


def sides():
    gx = lax.axis_index("gx")
    low = jnp.where(gx > 0, 1.0, 0.0)
    high = jnp.where(gx < lax.axis_size("gx") - 1, 1.0, 0.0)
    return low, high, lax.rem(gx, 2) == 0


def from_side(messages, first, count, block, side):
    even, odd = (message[first : first + count] for message in messages)
    low, high, even_above = side
    if block == 0:
        return jnp.where(even_above, odd, even) * low
    return jnp.where(even_above, even, odd) * high


def side_tile(messages, base, place, block, side):
    if not halved():
        return from_side(messages, base + place * 8, 8, block, side)
    tile = from_side(messages, base + place // 2 * 8, 8, block, side)
    return unpacked(tile, place)


def side_place(wanted, plane, block):
    planes = range(BX - wanted, BX) if block == 0 else range(wanted)
    return planes.index(plane) if plane in planes else None


def widened(own, own_tiles, x, layout, side):
    block, plane = divmod(x, BX)
    if block == 1:
        main = own[0][own[1] + plane * BY : own[1] + plane * BY + BY]
        tile = own_tiles[0][own_tiles[1] + plane * 8 : own_tiles[1] + plane * 8 + 8]
        return jnp.concatenate([main, tile], 0)
    (messages, base, wanted), (tile_messages, tile_base, tile_place, tile_wanted) = layout
    main, tile = jnp.zeros((BY, BZ), F32), jnp.zeros((8, BZ), F32)
    place = side_place(wanted, plane, block)
    if place is not None:
        main = from_side(messages, base + place * BY, BY, block, side)
    place = side_place(tile_wanted, plane, block)
    if place is not None:
        tile = side_tile(tile_messages, tile_base, tile_place + place, block, side)
    return jnp.concatenate([main, tile], 0)


def less_plane_below(value, x, own_ref, own_rows, messages, side_layout, side):
    if x == BX:
        (planes_end, x_end), count = side_layout
        main = from_side(messages, planes_end, BY, 0, side)
        tile = side_tile(messages, x_end, count - 1, 0, side)
    elif x == 2 * BX:
        planes_end, _, tiles_end = own_rows
        high = side[1]
        main = own_ref[planes_end : planes_end + BY] * high
        tile = own_ref[tiles_end - 8 : tiles_end] * high
    else:
        return value
    return value - jnp.concatenate([main, tile], 0)


def strip_below(own, messages, first, slot, side):
    lane = lanes(own.shape)
    width = BX * STRIP
    low = from_side(messages, first, EY, 0, side)
    low = pltpu.roll(low, (width - slot * width) % BZ, 1)
    own = pltpu.roll(own * side[1], (2 * width - slot * width) % BZ, 1)
    in_own = (lane >= width) & (lane < width + STRIP)
    in_high = (lane >= 2 * width) & (lane < 2 * width + STRIP)
    return jnp.where(in_own, low, jnp.where(in_high, own, 0.0))


def whole_strip(own, messages, first, slot, side):
    low = from_side(messages, first, EY, 0, side)
    high = from_side(messages, first, EY, 2, side)
    return strip_of(low, 0, slot) + strip_of(own, 1, slot) + strip_of(high, 2, slot)


def adjoint_kernel(
    ql_ref, late_ref, even, odd, adj_hbm, ra_ref, rsa_ref, rb_ref, rsb_ref,
    table_ref,
    out_ref, hist_ref, coef_ref, coef_strip_ref,
    q_ref, t_ref, u_ref, scale_ref, edge_ref, flux_ref, w_sem,
):
    w_copy = pltpu.make_async_copy(adj_hbm.at[pl.ds(1, 3)], out_ref.at[pl.ds(1, 3)], w_sem)
    w_copy.start()
    cut_up, cut_down = cut_flags()
    side = sides()
    messages = (even, odd)
    r_refs = ((ra_ref, 0), (ra_ref, 1), (rb_ref, 0), (rb_ref, 1))
    rs_refs = ((rsa_ref, 0), (rsa_ref, 1), (rsb_ref, 0), (rsb_ref, 1))
    tiles, own_tiles = ADJ_SIDE[1], ADJ_OWN[1]
    side_strip = tiles + tile_rows(ADJ_TILES)
    raws = side_strip + EY

    def initial(index, x):
        own = ((ql_ref, 0), (late_ref, 0), (ql_ref, PLANES))[index]
        layout = (
            ((messages, raws, 4), (messages, tiles, 0, 3)),
            ((messages, 0, 3), (messages, tiles, 3, 2)),
            ((messages, raws + PLANES, 4), (messages, tiles, 5, 3)),
        )[index]
        value = widened(own, (late_ref, own_tiles + 32 * index), x, layout, side)
        if index == 1:
            value = less_plane_below(
                value, x, late_ref, ADJ_OWN, messages, (ADJ_SIDE, ADJ_TILES), side
            )
        return value

    for x in range(EX):
        stiff, buoy, damp = coefficients(initial(2, x), table_ref)
        coef_ref[0, x], coef_ref[1, x], coef_ref[2, x] = stiff, buoy, damp
        scale_ref[x] = stiff * damp
    own_strip = late_ref[ADJ_OWN[2] : ADJ_OWN[2] + EY]
    q_s, t_s, label_s = (
        whole_strip(own_strip, messages, side_strip, slot, side) for slot in range(3)
    )
    t_s = t_s - strip_below(own_strip, messages, side_strip, 3, side)
    stiff_s, buoy_s, damp_s = coefficients(label_s, table_ref)
    scale_s = stiff_s * damp_s
    coef_strip_ref[0], coef_strip_ref[1], coef_strip_ref[2] = stiff_s, buoy_s, damp_s
    w_copy.wait()

    for step in range(1, STEPS + 1):
        rs_ref, place = rs_refs[STEPS - step]
        q_s = q_s + rs_ref[place]
        u_s = scale_s * q_s
        flux_s, spread = strip_flux(u_s, buoy_s)
        t_s = t_s + spread
        q_s = damp_s * q_s + t_s
        edges = cut_edges(u_s, flux_s, cut_up, cut_down)
        for x in range(step, EX - step):
            edge_ref[step - 1, x] = plane_edge(edges, x)

    for step in range(1, STEPS + 1):
        k = STEPS - step
        r_ref, place = r_refs[k]
        r_first = (EARLY_PLANES if k < 2 else LATE_PLANES)[0]

        for x in range(step - 1, EX - step + 1):
            q = (initial(0, x) if step == 1 else q_ref[x]) + r_ref[place, x - r_first]
            q_ref[x] = q
            u_ref[x] = scale_ref[x] * q

        for x in range(step - 1, EX - step):
            u, buoyancy = u_ref[x], coef_ref[1, x]
            slopes = [u_ref[x + 1] - u]
            if x >= step:
                slopes += [y_up(u) - u, z_up(u, edge_ref[step - 1, x]) - u]
            for axis, slope in enumerate(slopes):
                flux_ref[axis, x] = buoyancy * slope
            if BX <= x < 2 * BX:
                for axis, slope in enumerate(slopes):
                    w = out_ref[1 + axis, x - BX] + slope[0:BY]
                    out_ref[1 + axis, x - BX] = w
                    hist_ref[k, 1 + axis, x - BX] = w

        for x in range(step, EX - step):
            flux_y, flux_z = flux_ref[1, x], flux_ref[2, x]
            spread = (flux_ref[0, x] - flux_ref[0, x - 1]) + (flux_y - y_down(flux_y))
            spread = spread + (flux_z - z_down(flux_z, edge_ref[step - 1, x]))
            damped = coef_ref[2, x] * q_ref[x]
            t = (initial(1, x) if step == 1 else t_ref[x]) + spread
            if BX <= x < 2 * BX:
                hist_ref[k, 0, x - BX] = damped[0:BY]
            if step < STEPS:
                t_ref[x] = t
                q_ref[x] = damped + t
            else:
                out_ref[0, x - BX] = (damped + t)[0:BY]


def forward_kernel(
    wave_ref, own_s_ref, late_ref, even, odd, coef_ref, coef_strip_ref, s_ref, ss_ref, hist_ref,
    adjoint_ref, grad_hbm, adjoint_hbm,
    p_ref, spread_ref, edge_ref, flux_ref, grad_ref, sems,
):
    copies = [pltpu.make_async_copy(adjoint_ref, adjoint_hbm, sems.at[0])]
    copies[0].start()

    def send(index, kind, first, count):
        planes = pl.ds(first, count)
        copy = pltpu.make_async_copy(
            grad_ref.at[kind, planes], grad_hbm.at[kind, planes], sems.at[index]
        )
        copy.start()
        copies.append(copy)

    cut_up, cut_down = cut_flags()
    side = sides()
    messages = (even, odd)
    tiles, own_tiles = WAVE_SIDE[1], WAVE_OWN[1]
    side_strip = tiles + tile_rows(WAVE_TILES)

    def initial(index, x):
        layout = (
            ((messages, 0, 4), (messages, tiles, 0, 3)),
            ((messages, PLANES, 3), (messages, tiles, 3, 2)),
        )[index]
        own = ((wave_ref, 0), (own_s_ref, 0))[index]
        value = widened(own, (late_ref, own_tiles + 32 * index), x, layout, side)
        if index == 1:
            value = less_plane_below(
                value, x, late_ref, WAVE_OWN, messages, (WAVE_SIDE, WAVE_TILES), side
            )
        return value

    own_strip = late_ref[WAVE_OWN[2] : WAVE_OWN[2] + EY]
    p_s, s_s = (
        whole_strip(own_strip, messages, side_strip, slot, side) for slot in range(2)
    )
    s_s = s_s - strip_below(own_strip, messages, side_strip, 2, side)
    stiff_s, buoy_s, damp_s = coef_strip_ref[0], coef_strip_ref[1], coef_strip_ref[2]

    for step in range(1, STEPS + 1):
        flux_s, spread = strip_flux(p_s, buoy_s)
        edges = cut_edges(p_s, flux_s, cut_up, cut_down)
        if step < STEPS:
            s_s = s_s - spread
            p_s = damp_s * (p_s - stiff_s * s_s) + ss_ref[step - 1]
        for x in range(step, EX - step):
            edge_ref[step - 1, x] = plane_edge(edges, x)
    for x in range(EX):
        p_ref[x] = initial(0, x)

    for step in range(1, STEPS + 1):
        k = step - 1
        for x in range(step - 1, EX - step):
            p, buoyancy = p_ref[x], coef_ref[1, x]
            slopes = [p_ref[x + 1] - p]
            if x >= step:
                slopes += [y_up(p) - p, z_up(p, edge_ref[step - 1, x]) - p]
            for axis, slope in enumerate(slopes):
                flux_ref[axis, x] = buoyancy * slope
            if BX <= x < 2 * BX:
                place = x - BX
                term = hist_ref[k, 1, place] * slopes[0][0:BY]
                term = term + hist_ref[k, 2, place] * slopes[1][0:BY]
                term = term + hist_ref[k, 3, place] * slopes[2][0:BY]
                grad_ref[1, place] = -term if k == 0 else grad_ref[1, place] - term
        if step == STEPS:
            send(1, 1, 0, BX)

        for x in range(step, EX - step):
            flux_y, flux_z = flux_ref[1, x], flux_ref[2, x]
            spread = (flux_ref[0, x] - flux_ref[0, x - 1]) + (flux_y - y_down(flux_y))
            spread = spread + (flux_z - z_down(flux_z, edge_ref[step - 1, x]))
            spread = (initial(1, x) if step == 1 else spread_ref[x]) - spread
            if step < STEPS:
                spread_ref[x] = spread
                p_ref[x] = (
                    coef_ref[2, x] * (p_ref[x] - coef_ref[0, x] * spread)
                    + s_ref[k, x - SOURCE_PLANES[0]]
                )
            if BX <= x < 2 * BX:
                place = x - BX
                term = hist_ref[k, 0, place] * spread[0:BY]
                grad_ref[0, place] = -term if k == 0 else grad_ref[0, place] - term
                if step == STEPS:
                    send(2 + place, 0, place, 1)
    for copy in copies:
        copy.wait()


def shape(*dims):
    return jax.ShapeDtypeStruct(dims, F32)


def call(kernel, outs, operands, scratch, places, micros=0.1, out_place="v"):
    spaces = {"h": pltpu.HBM, "a": pl.ANY, "v": pltpu.VMEM}
    operands = [
        pltpu.with_memory_space_constraint(operand, pltpu.HBM) if place == "h" else operand
        for operand, place in zip(operands, places)
    ]
    return pl.pallas_call(
        kernel,
        out_shape=outs,
        in_specs=[pl.BlockSpec(memory_space=spaces[place]) for place in places],
        out_specs=[pl.BlockSpec(memory_space=spaces[out_place])] * len(outs),
        scratch_shapes=scratch,
        compiler_params=pltpu.CompilerParams(vmem_limit_bytes=VMEM_LIMIT),
        cost_estimate=pl.CostEstimate(
            flops=0, bytes_accessed=int(3.69e6 * micros), transcendentals=0
        ),
    )(*operands)


def from_sides(sends, axes):
    count = lax.axis_size("gy")

    def route(offset):
        pairs = []
        for target in range(count):
            source = target + offset
            if 0 <= source < count:
                if "gz" in axes:
                    pairs += [(2 * source + z, 2 * target + 1 - z) for z in range(2)]
                else:
                    pairs.append((source, target))
        return pairs

    if count == 2:
        both = lax.ppermute(sends[0], axes, route(1) + route(-1))
        return both, both
    upward, downward = sends
    return lax.ppermute(downward, axes, route(1)), lax.ppermute(upward, axes, route(-1))


def rotated(array, axis, offset):
    count = lax.axis_size(axis)
    return lax.ppermute(array, axis, [((i + offset) % count, i) for i in range(count)])


def paired(array, odd):
    count = lax.axis_size("gx")
    pairs = []
    for i in range(count):
        partner = ((i - 1) ^ 1) + 1 if odd else i ^ 1
        pairs.append((partner if 0 <= partner < count else i, i))
    return lax.ppermute(array, "gx", pairs)


def local(
    stored, adjoint_end, labels, tissue, source_cells, source_wave, receiver_cells, receiver_wave
):
    assert lax.axis_size("gz") == 2 and labels.shape == (BX, BY, BZ) and tissue.shape[1] == 8
    half = lax.axis_size("gx") // 2
    arguments = [
        stored, adjoint_end, labels, tissue,
        receiver_cells.T, receiver_wave, source_cells.T, source_wave,
    ]
    ways = 1 if lax.axis_size("gy") == 2 else 2
    wave, ql, t, last_x, last_y, strips, table, receivers, receiver_wave, sources, source_wave, *sends = call(
        load_kernel,
        [
            shape(2 * PLANES + BY + SPARE // 2, BZ),
            shape(2 * PLANES, BZ),
            shape(PLANES, BZ),
            shape(BY, BZ),
            shape(2 * BX * 8, BZ),
            shape(3 * BY, BZ),
            shape(24, BZ),
        ]
        + [jax.ShapeDtypeStruct(array.shape, array.dtype) for array in arguments[4:]]
        + [shape(20 * 8, BZ)] * ways
        + [shape(2 * 8, BZ)] * ways,
        arguments,
        [
            pltpu.VMEM(stored.shape, F32),
            pltpu.VMEM(adjoint_end.shape, F32),
            pltpu.VMEM(labels.shape, jnp.int32),
            pltpu.SMEM(tissue.shape, F32),
            pltpu.SemaphoreType.DMA,
        ],
        "hhhhhhhh",
        1.4,
    )
    from_up, from_down = from_sides(sends[:ways], "gy")
    other = rotated(strips, "gz", 1)
    corner_up, corner_down = from_sides(sends[ways:], ("gy", "gz"))
    wave = rotated(wave, "gx", half)
    rb, rsb = call(
        late_kernel,
        [shape(2, EX * EY, BZ), shape(2, EY, BZ)],
        [receivers, receiver_wave],
        [],
        "vv",
        1.2,
    )
    early_planes, source_planes = (last - first for first, last in (EARLY_PLANES, SOURCE_PLANES))
    late, adj_late = call(
        merge_kernel,
        [shape(tile_rows(9) + EY + 8 + SPARE, BZ), shape(ADJ_OWN[2] + EY, BZ)],
        [from_up, from_down, corner_up, corner_down, strips, other, t, last_x, last_y, rsb],
        [pltpu.VMEM((WAVE_OWN[2], BZ), F32)],
        "vvvvvvvvva",
    )
    late = rotated(late, "gx", half)
    ra, rsa = call(
        early_kernel,
        [shape(2, early_planes * EY, BZ), shape(2, EY, BZ)],
        [receivers, receiver_wave, adj_late],
        [],
        "vva",
        1.0,
    )
    ra, rb = ra.reshape(2, early_planes, EY, BZ), rb.reshape(2, EX, EY, BZ)
    even, odd = call(
        adjoint_join_kernel,
        [shape(ADJ_SIDE[1] + tile_rows(ADJ_TILES) + EY + 2 * PLANES, BZ)] * 2,
        [ql, adj_late],
        [],
        "vv",
    )
    even, odd = paired(even, False), paired(odd, True)
    src, src_strip = call(
        source_kernel,
        [shape(STEPS - 1, source_planes * EY, BZ), shape(STEPS - 1, EY, BZ)],
        [sources, source_wave, adj_late],
        [],
        "vva",
        0.5,
    )
    src = src.reshape(STEPS - 1, source_planes, EY, BZ)
    own_s, own_late, wave_even, wave_odd = call(
        join_kernel,
        [shape(PLANES, BZ), shape(WAVE_OWN[2] + EY, BZ)]
        + [shape(WAVE_SIDE[1] + tile_rows(WAVE_TILES) + EY, BZ)] * 2,
        [wave, late, rsa],
        [],
        "vva",
    )
    wave_even, wave_odd = paired(wave_even, False), paired(wave_odd, True)
    adjoint_out, hist, coef, coef_strip = call(
        adjoint_kernel,
        [
            shape(4, BX, BY, BZ),
            shape(STEPS, 4, BX, BY, BZ),
            shape(3, EX, EY, BZ),
            shape(3, EY, BZ),
        ],
        [ql, adj_late, even, odd, adjoint_end, ra, rsa, rb, rsb, table],
        [pltpu.VMEM((EX, EY, BZ), F32)] * 4
        + [
            pltpu.VMEM((STEPS, EX, EY, BZ), F32),
            pltpu.VMEM((3, EX, EY, BZ), F32),
            pltpu.SemaphoreType.DMA,
        ],
        "vvvvhvvvvv",
        3.9,
    )
    return call(
        forward_kernel,
        [shape(2, BX, BY, BZ), shape(4, BX, BY, BZ)],
        [
            wave, own_s, own_late, wave_even, wave_odd, coef, coef_strip, src, src_strip, hist,
            adjoint_out,
        ],
        [pltpu.VMEM((EX, EY, BZ), F32)] * 2
        + [
            pltpu.VMEM((STEPS, EX, EY, BZ), F32),
            pltpu.VMEM((3, EX, EY, BZ), F32),
            pltpu.VMEM((2, BX, BY, BZ), F32),
            pltpu.SemaphoreType.DMA((2 + BX,)),
        ],
        "vvvvvvvvvvv",
        2.5,
        "a",
    )


def solution(mesh):
    return jax.shard_map(
        local,
        mesh=mesh,
        in_specs=(
            P("shot", "gx", "gy", "gz"),
            P("shot", "gx", "gy", "gz"),
            P("gx", "gy", "gz"),
            P(),
            P("shot", None),
            P(None, "shot"),
            P(),
            P(None, "shot"),
        ),
        out_specs=(P("shot", "gx", "gy", "gz"), P("shot", "gx", "gy", "gz")),
        check_vma=False,
    )
```
